32 devices in a mesh: fsdp: 4 (over y, x), seq: 8 (over z, core).
Axes of the slice: x: 2, y: 2, z: 4, core: 2. Of those that a mesh axis runs over, the one named last changes fastest.
Arguments:
- tokens: bfloat16 [4, 1024, 2048], P('fsdp', 'seq'), may hold values from -6 to 6
- gain_one: bfloat16 [2048], P(('fsdp', 'seq')), may hold values from 0.5 to 1.5
- shift_one: bfloat16 [2048], P(('fsdp', 'seq')), may hold values from -3 to 3
- w_qkv: bfloat16 [2048, 3, 2048], P('fsdp', None, 'seq'), may hold values from -0.125 to 0.125
- b_qkv: bfloat16 [3, 2048], P(None, ('fsdp', 'seq')), may hold values from -3 to 3
- w_out: bfloat16 [2048, 2048], P('seq', 'fsdp'), may hold values from -0.5 to 0.5
- gain_two: bfloat16 [2048], P(('fsdp', 'seq')), may hold values from 0.5 to 1.5
- shift_two: bfloat16 [2048], P(('fsdp', 'seq')), may hold values from -3 to 3
- w_gate: bfloat16 [2048, 5632], P('fsdp', 'seq'), may hold values from -0.125 to 0.125
- w_up: bfloat16 [2048, 5632], P('fsdp', 'seq'), may hold values from -0.125 to 0.125
- w_down: bfloat16 [5632, 2048], P('seq', 'fsdp'), may hold values from -0.078125 to 0.078125
- grad_output: bfloat16 [4, 1024, 2048], P('fsdp', 'seq'), may hold values from -6 to 6
Outputs:
- output: bfloat16 [4, 1024, 2048], P('fsdp', 'seq')
- grad_input: float32 [4, 1024, 2048], P('fsdp', 'seq')
- grad_gain_one: float32 [2048], P(('fsdp', 'seq'))
- grad_shift_one: float32 [2048], P(('fsdp', 'seq'))
- grad_w_qkv: float32 [2048, 3, 2048], P('fsdp', None, 'seq')
- grad_b_qkv: float32 [3, 2048], P(None, ('fsdp', 'seq'))
- grad_w_out: float32 [2048, 2048], P('seq', 'fsdp')
- grad_gain_two: float32 [2048], P(('fsdp', 'seq'))
- grad_shift_two: float32 [2048], P(('fsdp', 'seq'))
- grad_w_gate: float32 [2048, 5632], P('fsdp', 'seq')
- grad_w_up: float32 [2048, 5632], P('fsdp', 'seq')
- grad_w_down: float32 [5632, 2048], P('seq', 'fsdp')
The draws below stay inside these ranges and needn't reach their ends.
All inputs are finite; a program needn't handle non-finite values.
Results may differ from the reference program's by a relative error of at most 0.018.
Values may be sent and summed in bfloat16 or wider, within the bound.
A program may use at most 192 MiB of HBM per device.

```python
import jax
import jax.numpy as jnp
from jax import lax

D = 2048
HEADS = 32
FF = 5632
HEAD = 64
ROT = 16
LENGTH = 1024
SEQS = 4


def levels(own_key, extent, split, smallest, high):
    level, own = 1.0, jax.random.fold_in(own_key, 6)
    for axis_at, parts in split:
        draws = jnp.exp(jax.random.uniform(jax.random.fold_in(own, axis_at), (parts,), jnp.float32, smallest / len(split), high / len(split)))
        level = level * jnp.repeat(draws, extent[axis_at] // parts).reshape([-1 if axis == axis_at else 1 for axis in range(len(extent))])
    return level


def noise(rng, shape, deviation, limit, cuts=(), kind=jnp.bfloat16):
    drawn = jax.random.normal(rng, shape, jnp.float32) * deviation
    if len(cuts) > 0:
        drawn = levels(rng, shape, cuts, -0.22, 0.18) * drawn
    return jnp.clip(drawn, min=-limit, max=limit).astype(kind)


def setup_inputs(seed: int = 0) -> dict:
    streams_of = jax.random.split(jax.random.key(seed), 13)
    tokens = noise(streams_of[0], (SEQS, LENGTH, D), 1.0, 6.0, ((0, 4), (1, 8)))
    gain_one = jnp.clip(1.0 + 0.1 * jax.random.normal(streams_of[1], (D,), jnp.float32), 0.5, 1.5).astype(jnp.bfloat16)
    shift_one = noise(streams_of[2], (D,), 0.5, 3.0, ((0, 32),))
    w_qkv = noise(streams_of[3], (D, 3, D), D ** -0.5, 0.125, ((0, 4), (2, 8)))
    b_qkv = noise(streams_of[4], (3, D), 0.5, 3.0, ((1, 32),))
    w_out = noise(streams_of[5], (D, D), (D // 16) ** -0.5, 0.5, ((0, 8), (1, 4)))
    gain_two = jnp.clip(1.0 + 0.1 * jax.random.normal(streams_of[6], (D,), jnp.float32), 0.5, 1.5).astype(jnp.bfloat16)
    shift_two = noise(streams_of[7], (D,), 0.5, 3.0, ((0, 32),))
    w_gate = noise(streams_of[8], (D, FF), D ** -0.5, 0.125, ((0, 4), (1, 8)))
    w_up = noise(streams_of[9], (D, FF), D ** -0.5, 0.125, ((0, 4), (1, 8)))
    w_down = noise(streams_of[10], (FF, D), FF ** -0.5, 0.078125, ((0, 8), (1, 4)))
    grad_output = noise(streams_of[11], (SEQS, LENGTH, D), 1.0, 6.0, ((0, 4), (1, 8)))
    return {"tokens": tokens, "gain_one": gain_one, "shift_one": shift_one, "w_qkv": w_qkv, "b_qkv": b_qkv, "w_out": w_out, "gain_two": gain_two, "shift_two": shift_two, "w_gate": w_gate, "w_up": w_up, "w_down": w_down, "grad_output": grad_output}


EPSILON = 1e-05
NEG_LARGE = -1e+30

@jax.custom_vjp
def low(v):
    return lax.optimization_barrier(v.astype(jnp.bfloat16)).astype(jnp.float32)

@jax.custom_vjp
def low_back(v):
    return v

def low_keep(v):
    return (low(v), None)

def low_pass(kept, grad):
    return (grad,)

def back_keep(v):
    return (v, None)

def back_low(kept, grad):
    return (low(grad),)
low.defvjp(low_keep, low_pass)
low_back.defvjp(back_keep, back_low)

def matmul(left, right):
    return jnp.dot(left, right, precision=lax.Precision.HIGHEST, preferred_element_type=jnp.float32)

def layer_norm(values, gain, shift):
    center = values - lax.optimization_barrier(jnp.mean(values, -1, keepdims=True))
    spread = lax.optimization_barrier(jnp.mean(center * center, -1, keepdims=True))
    return center * lax.rsqrt(spread + EPSILON) * gain + shift

def rotary_tables(positions):
    half = ROT // 2
    freqs = 10000.0 ** (-jnp.arange(half, dtype=jnp.float32) * 2.0 / ROT)
    angles = positions.astype(jnp.float32)[:, None] * freqs[None, :]
    return (jnp.cos(angles)[:, None, :], jnp.sin(angles)[:, None, :])

def rotate(values, cosine, sine):
    half = ROT // 2
    first = values[..., :half]
    second = values[..., half:ROT]
    return jnp.concatenate([first * cosine - second * sine, second * cosine + first * sine, values[..., ROT:]], -1)

def attention(queries, keyset, valset):
    length = queries.shape[0]
    block_rows = min(512, length)
    scale = HEAD ** (-0.5)

    def one_block(offset):
        rows = lax.dynamic_slice_in_dim(queries, offset, block_rows, 0)
        scores = jnp.einsum('qhd,khd->hqk', rows, keyset, precision=lax.Precision.HIGHEST, preferred_element_type=jnp.float32) * scale
        scores = low_back(scores)
        visible = (offset + jnp.arange(block_rows, dtype=jnp.int32))[:, None] >= jnp.arange(length, dtype=jnp.int32)[None, :]
        scores = jnp.where(visible[None], scores, NEG_LARGE)
        weights = low(jax.nn.softmax(scores, -1))
        return jnp.einsum('hqk,khd->qhd', weights, valset, precision=lax.Precision.HIGHEST, preferred_element_type=jnp.float32)
    offsets = jnp.arange(length // block_rows, dtype=jnp.int32) * block_rows
    outputs = lax.map(jax.checkpoint(one_block), offsets)
    return outputs.reshape(length, HEADS, HEAD)

def forward(inputs, gain_one, shift_one, w_qkv, b_qkv, w_out, gain_two, shift_two, w_gate, w_up, w_down):
    length = inputs.shape[0]
    cosine, sine = rotary_tables(jnp.arange(length, dtype=jnp.int32))
    normed = low(layer_norm(inputs, gain_one, shift_one))
    projected = low_back(matmul(normed, w_qkv.reshape(D, 3 * D)) + b_qkv.reshape(3 * D))
    head_shape = (length, HEADS, HEAD)
    queries = low(low_back(rotate(projected[:, :D].reshape(head_shape), cosine, sine)))
    keyset = low(low_back(rotate(projected[:, D:2 * D].reshape(head_shape), cosine, sine)))
    valset = low(low_back(projected[:, 2 * D:].reshape(head_shape)))
    mixed = low(low_back(attention(queries, keyset, valset).reshape(length, D)))
    middle = inputs + low_back(matmul(mixed, w_out))
    normed_two = low(layer_norm(middle, gain_two, shift_two))
    gate = low_back(matmul(normed_two, w_gate))
    up_part = low_back(matmul(normed_two, w_up))
    hidden = low(jax.nn.silu(gate) * up_part)
    return middle + low_back(matmul(hidden, w_down))

def reference(tokens, gain_one, shift_one, w_qkv, b_qkv, w_out, gain_two, shift_two, w_gate, w_up, w_down, grad_output):
    params = tuple((p.astype(jnp.float32) for p in (gain_one, shift_one, w_qkv, b_qkv, w_out, gain_two, shift_two, w_gate, w_up, w_down)))

    def one_sequence(totals, item):
        inputs, cotangent = item
        result, pull = jax.vjp(forward, inputs.astype(jnp.float32), *params)
        grads = pull(cotangent.astype(jnp.float32))
        totals = tuple((a + b for a, b in zip(totals, grads[1:])))
        return (totals, (result.astype(jnp.bfloat16), grads[0]))
    zeros = tuple((jnp.zeros(p.shape, jnp.float32) for p in params))
    totals, (outputs, grad_inputs) = lax.scan(one_sequence, zeros, (tokens, grad_output))
    return (outputs, grad_inputs, totals[0], totals[1], totals[2], totals[3], totals[4], totals[5], totals[6], totals[7], totals[8], totals[9])
```

```python
import functools

import jax
import jax.numpy as jnp
import numpy as np
from jax import lax
from jax.experimental import pallas as pl
from jax.experimental.pallas import tpu as pltpu
from jax.sharding import PartitionSpec as P

HEAD = 64
ROT = 16
EPSILON = 1e-05
NEG_LARGE = -1e30
MESH = pl.DeviceIdType.MESH
ANY = pl.BlockSpec(memory_space=pl.ANY)
VMEM = pl.BlockSpec(memory_space=pltpu.VMEM)
BF = jnp.bfloat16
F32 = jnp.float32
SMALL = 8


def put(src, dst, send, recv, **device):
    return pltpu.make_async_remote_copy(
        src_ref=src, dst_ref=dst, send_sem=send, recv_sem=recv, device_id=device, device_id_type=MESH
    )


def dot(left, right):
    return jnp.dot(left, right, preferred_element_type=F32)


def dot_nt(left, right):
    return lax.dot_general(left, right, (((1,), (1,)), ((), ())), preferred_element_type=F32)


def dot_tn(left, right):
    return lax.dot_general(left, right, (((0,), (0,)), ((), ())), preferred_element_type=F32)


def aligned(start, size, unit=None):
    return pl.ds(pl.multiple_of(start, unit or size), size)


class Net:
    def __init__(self):
        self.n_f, self.n_s = lax.axis_size("fsdp"), lax.axis_size("seq")
        self.tall = 2 if self.n_f % 2 == 0 else 1
        self.wide = self.n_f // self.tall
        self.n_l = self.n_s // 2
        self.f, self.s = lax.axis_index("fsdp"), lax.axis_index("seq")
        self.a, self.b = self.f // self.wide, self.f % self.wide
        self.z, self.c = self.s // 2, self.s % 2
        self.mate = self.s + 1 - 2 * self.c

    def barrier(self):
        sem = pltpu.get_barrier_semaphore()
        for k in range(1, self.n_f):
            pl.semaphore_signal(
                sem, inc=1, device_id={"fsdp": (self.f + k) % self.n_f}, device_id_type=MESH
            )
        for k in range(1, self.n_s):
            pl.semaphore_signal(
                sem, inc=1, device_id={"seq": (self.s + k) % self.n_s}, device_id_type=MESH
            )
        pl.semaphore_wait(sem, self.n_f + self.n_s - 2)

    def sides(self, hop, act):
        for side in range(2):
            other = self.z + (2 * side - 1) * hop

            @pl.when((other >= 0) & (other < self.n_l))
            def _():
                act(other, side)


class Spread:
    def __init__(self, net, src, part, sems):
        self.net, self.src, self.part, self.sems = net, src, part, sems
        self.rows = [j for j in range(1, net.wide)]
        self.cols = [i for i in range(1, net.tall)]

    @staticmethod
    def count(n_f):
        tall = 2 if n_f % 2 == 0 else 1
        wide = n_f // tall
        return 1 + 2 * (wide - 1) + 2 * (tall - 1) + 4 * (wide - 1) * (tall - 1)

    def at(self, kind, i, j):
        w, t = len(self.rows), len(self.cols)
        base = {
            "own": 0,
            "row": 1,
            "col": 1 + 2 * w,
            "half0": 1 + 2 * w + 2 * t,
            "half1": 1 + 2 * w + 2 * t + 2 * w * t,
        }[kind]
        if kind == "own":
            return self.sems.at[0]
        k = j - 1 if kind == "row" else i - 1 if kind == "col" else (i - 1) * w + j - 1
        return self.sems.at[base + 2 * k], self.sems.at[base + 2 * k + 1]

    def rank(self, i, j):
        net = self.net
        return ((net.a + i) % net.tall) * net.wide + (net.b + j) % net.wide

    def back(self, i, j):
        net = self.net
        return ((net.a - i + net.tall) % net.tall) * net.wide + (net.b - j + net.wide) % net.wide

    def own(self):
        return pltpu.make_async_copy(self.src, self.part(self.net.f, None), self.at("own", 0, 0))

    def first(self, i, j):
        send, recv = self.at("row" if i == 0 else "col", i, j)
        return put(self.src, self.part(self.net.f, None), send, recv, fsdp=self.rank(i, j))

    def came(self, i, j):
        send, recv = self.at("row" if i == 0 else "col", i, j)
        place = self.part(self.back(i, j), None)
        return put(place, place, send, recv, fsdp=self.rank(i, j))

    def second(self, half, i, j, came=False):
        send, recv = self.at("half0" if half == 0 else "half1", i, j)
        origin = self.back(i, j) if came else self.back(0, j) if half == 0 else self.back(i, 0)
        place = self.part(origin, half)
        return put(place, place, send, recv, fsdp=self.rank(i, 0) if half == 0 else self.rank(0, j))

    def start(self):
        self.own().start()
        for i in self.cols:
            self.first(i, 0).start()
        for j in self.rows:
            self.first(0, j).start()

    def relay(self):
        for j in self.rows:
            self.came(0, j).wait_recv()
            for i in self.cols:
                self.second(0, i, j).start()
        for i in self.cols:
            self.came(i, 0).wait_recv()
            for j in self.rows:
                self.second(1, i, j).start()

    def finish(self):
        self.own().wait()
        for j in self.rows:
            self.first(0, j).wait_send()
        for i in self.cols:
            self.first(i, 0).wait_send()
        for i in self.cols:
            for j in self.rows:
                for half in range(2):
                    self.second(half, i, j, came=True).wait_recv()
                    self.second(half, i, j).wait_send()


class Line:
    def __init__(self, net, src, part, recv, send):
        self.net, self.src, self.part, self.recv, self.send = net, src, part, recv, send

    @staticmethod
    def sems(n_s):
        return [pltpu.SemaphoreType.DMA((n_s,)), pltpu.SemaphoreType.DMA((4, n_s // 2))]

    def own(self):
        net = self.net
        return pltpu.make_async_copy(self.src, self.part(net.s), self.recv.at[net.s])

    def on_line(self, src, chunk, side, hop):
        net = self.net
        return put(
            src,
            self.part(chunk),
            self.send.at[side, hop],
            self.recv.at[chunk],
            seq=net.s + 2 - 4 * side,
        )

    def to_mate(self, src, chunk, side, hop):
        return put(src, self.part(chunk), self.send.at[2 + side, hop], self.recv.at[chunk], seq=self.net.mate)

    def goes_on(self, side):
        return self.net.z < self.net.n_l - 1 if side == 0 else self.net.z > 0

    def start(self):
        net = self.net
        self.own().start()
        for side in range(2):

            @pl.when(self.goes_on(side))
            def _():
                self.on_line(self.src, net.s, side, 0).start()

        self.to_mate(self.src, net.s, 0, 0).start()

    def arrive(self, chunk):
        place = self.part(chunk)
        put(place, place, self.send.at[0, 0], self.recv.at[chunk], seq=self.net.mate).wait_recv()

    def step(self, hop):
        net = self.net

        def act(other, side):
            chunk = 2 * other + net.c
            self.arrive(chunk)

            @pl.when(self.goes_on(side))
            def _():
                self.on_line(self.part(chunk), chunk, side, hop).start()

            self.to_mate(self.part(chunk), chunk, side, hop).start()

        net.sides(hop, act)

    def pair(self, other):
        self.arrive(2 * other + 1 - self.net.c)

    def finish(self):
        net = self.net
        for side in range(2):

            @pl.when(self.goes_on(side))
            def _():
                self.on_line(self.src, net.s, side, 0).wait_send()

        self.to_mate(self.src, net.s, 0, 0).wait_send()

        @pl.loop(1, net.n_l)
        def _(hop):
            def act(other, side):
                chunk = 2 * other + net.c

                @pl.when(self.goes_on(side))
                def _():
                    self.on_line(self.part(chunk), chunk, side, hop).wait_send()

                self.to_mate(self.part(chunk), chunk, side, hop).wait_send()

            net.sides(hop, act)


class Packets:
    def __init__(self, net, src, buf, sems):
        self.net, self.src, self.buf, self.sems = net, src, buf, sems

    @staticmethod
    def count(n_f, n_s):
        return 1 + 2 * (n_f - 1) + 2 * (n_s - 1)

    def own(self):
        net = self.net
        return pltpu.make_async_copy(self.src, self.buf.at[net.s, net.f], self.sems.at[0])

    def one(self, k, came=False):
        net = self.net
        f = (net.f - k + net.n_f) % net.n_f if came else net.f
        place = self.buf.at[net.s, f]
        return put(
            place if came else self.src,
            place,
            self.sems.at[2 * k - 1],
            self.sems.at[2 * k],
            fsdp=(net.f + k) % net.n_f,
        )

    def two(self, k, came=False):
        net = self.net
        place = self.buf.at[(net.s - k + net.n_s) % net.n_s if came else net.s]
        at = 2 * (net.n_f - 1) + 2 * k - 1
        return put(place, place, self.sems.at[at], self.sems.at[at + 1], seq=(net.s + k) % net.n_s)

    def start(self):
        self.own().start()
        for k in range(1, self.net.n_f):
            self.one(k).start()

    def middle(self):
        self.own().wait()
        for k in range(1, self.net.n_f):
            self.one(k, came=True).wait_recv()
            self.one(k).wait_send()
        for k in range(1, self.net.n_s):
            self.two(k).start()

    def finish(self):
        for k in range(1, self.net.n_s):
            self.two(k, came=True).wait_recv()
            self.two(k).wait_send()

    def unpack(self, out, width):
        net = self.net
        per = 128 // width
        for tile in range(net.n_f * net.n_s // per):
            total = None
            for j in range(per):
                f, s = divmod(tile * per + j, net.n_s)
                piece = self.buf[s, f]
                if j:
                    piece = pltpu.roll(piece, j * width, axis=1)
                total = piece if total is None else total + piece
            out[:, tile * 128 : (tile + 1) * 128] = total


def rotary(values, cosine, sine_next, sine_last):
    columns = values.shape[1]
    half = ROT // 2
    times = columns // 128

    def wide(table):
        return table if times == 1 else jnp.concatenate([table] * times, axis=1)

    following = pltpu.roll(values, columns - half, axis=1)
    previous = pltpu.roll(values, half, axis=1)
    return values * wide(cosine) + following * wide(sine_next) + previous * wide(sine_last)


def rotary_tables(length):
    half = ROT // 2
    freqs = 10000.0 ** (-jnp.arange(half, dtype=F32) * 2.0 / ROT)
    angles = jnp.arange(length, dtype=jnp.int32).astype(F32)[:, None] * freqs[None, :]
    cosine, sine = jnp.cos(angles), jnp.sin(angles)
    rest = jnp.zeros((length, HEAD - ROT), F32)
    none = jnp.zeros_like(sine)
    keep = jnp.concatenate([cosine, cosine, rest + 1.0], 1)
    following = jnp.concatenate([-sine, none, rest], 1)
    previous = jnp.concatenate([none, sine, rest], 1)
    return [jnp.concatenate([t, t], 1) for t in (keep, following, previous)]


def normalize(values):
    center = values - jnp.mean(values, -1, keepdims=True)
    inverse = lax.rsqrt(jnp.mean(center * center, -1, keepdims=True) + EPSILON)
    return center * inverse, inverse


def attend_kernel(
    tok,
    packet,
    wq,
    wo,
    cosine,
    sine_next,
    sine_last,
    q_o,
    k_o,
    kt_o,
    v_o,
    att_o,
    lse_o,
    n1_o,
    gains_o,
    wq_o,
    wo_o,
    rows,
    packets,
    vt,
    ot,
    pk_sems,
    wq_sems,
    wo_sems,
    tok_recv,
    tok_send,
):
    net = Net()
    chunk, width = tok.shape
    length = chunk * net.n_s
    depth = wq.shape[1]
    columns = wq.shape[2]
    heads = columns // HEAD
    pair = 2 * chunk
    block = 256

    net.barrier()
    pk = Packets(net, packet, packets, pk_sems)

    def wq_part(f, half):
        if half is None:
            return wq_o.at[:, aligned(f * depth, depth), :]
        return wq_o.at[:, aligned(f * depth + half * (depth // 2), depth // 2), :]

    def wo_part(f, half):
        span = aligned(f * depth, depth)
        if half is None:
            return wo_o.at[:, span]
        return wo_o.at[pl.ds(half * (columns // 2), columns // 2), span]

    spread_q = Spread(net, wq, wq_part, wq_sems)
    spread_o = Spread(net, wo, wo_part, wo_sems)
    line = Line(net, tok, lambda s: rows.at[aligned(s * chunk, chunk)], tok_recv, tok_send)
    pk.start()
    line.start()
    spread_q.start()
    spread_o.start()
    pk.middle()
    pk.finish()
    pk.unpack(gains_o, width // (net.n_f * net.n_s))

    def norm_block(other):
        gain, shift = gains_o[0:1, :], gains_o[1:2, :]

        @pl.loop(0, pair // 32)
        def _(i):
            span = aligned(other * pair + i * 32, 32)
            scaled, _ = normalize(rows[span, :].astype(F32))
            n1_o[span, :] = (scaled * gain + shift).astype(BF)

    def project_block(other):
        span = aligned(other * pair, pair)
        left = n1_o[span, :]
        cols = aligned(net.s * columns, columns)
        tables = cosine[span, :], sine_next[span, :], sine_last[span, :]
        for kind in range(3):
            value = dot(left, wq_o[kind]) + gains_o[4 + kind : 5 + kind, cols]
            if kind == 0:
                q_o[span, :] = rotary(value, *tables).astype(BF)
            elif kind == 1:
                value = rotary(value, *tables)
                k_o[span, :] = value.astype(BF)
                kt_o[:, span] = value.T.astype(BF)
            else:
                v_o[span, :] = value.astype(BF)
                vt[:, span] = value.T.astype(BF)

    line.arrive(net.s)
    line.pair(net.z)
    norm_block(net.z)

    def hop_norm(hop):
        line.step(hop)

        def act(other, side):
            line.pair(other)
            norm_block(other)

        net.sides(hop, act)

    for hop in range(1, net.n_l - 1):
        hop_norm(hop)
        if hop == 1:
            spread_q.relay()
    spread_q.finish()

    @pl.loop(0, net.n_l - 1)
    def _(hop):
        def act(other, side):
            @pl.when((hop > 0) | (side == 0))
            def _():
                project_block(other)

        net.sides(hop, act)

    spread_o.relay()
    hop_norm(net.n_l - 1)
    net.sides(net.n_l - 1, lambda other, side: project_block(other))

    @pl.loop(0, heads)
    def _(head):
        lane = lax.broadcasted_iota(jnp.int32, (1, columns), 1)
        here = jnp.where(lane // HEAD == head, HEAD**-0.5, 0.0).astype(BF)
        visible = lax.broadcasted_iota(jnp.int32, (block, block), 0) <= lax.broadcasted_iota(
            jnp.int32, (block, block), 1
        )
        head_rows = aligned(head * HEAD, HEAD)
        for i in range(length // block):
            lo, hi = i * block, (i + 1) * block
            query = q_o[lo:hi, :] * here
            near = jnp.where(visible, dot_nt(k_o[lo:hi, :], query), NEG_LARGE)
            highest = jnp.max(near, 0, keepdims=True)
            if i:
                far = dot_nt(k_o[0:lo, :], query)
                highest = jnp.maximum(highest, jnp.max(far, 0, keepdims=True))
            near = jnp.exp(near - highest)
            total = jnp.sum(near, 0, keepdims=True)
            out = dot(vt[head_rows, lo:hi], near.astype(BF))
            if i:
                far = jnp.exp(far - highest)
                total = total + jnp.sum(far, 0, keepdims=True)
                out = out + dot(vt[head_rows, 0:lo], far.astype(BF))
            ot[head_rows, lo:hi] = out / total
            lse_o[pl.ds(head, 1), lo:hi] = highest + jnp.log(total)

    for i in range(length // block):
        att_o[i * block : (i + 1) * block, :] = ot[:, i * block : (i + 1) * block].T.astype(BF)

    line.finish()
    spread_o.finish()


def attend_part(tokens, packet, wq, wo, tables):
    chunk, width = tokens.shape
    n_f, n_s = lax.axis_size("fsdp"), lax.axis_size("seq")
    length = chunk * n_s
    columns = wq.shape[2]
    shape = jax.ShapeDtypeStruct
    return pl.pallas_call(
        attend_kernel,
        name="attend",
        out_shape=[
            shape((length, columns), BF),
            shape((length, columns), BF),
            shape((columns, length), BF),
            shape((length, columns), BF),
            shape((length, columns), BF),
            shape((8, length), F32),
            shape((length, width), BF),
            shape((SMALL, width), F32),
            shape((3, width, columns), BF),
            shape((columns, width), BF),
        ],
        in_specs=[ANY, VMEM, ANY, ANY, VMEM, VMEM, VMEM],
        out_specs=[VMEM] * 9 + [ANY],
        scratch_shapes=[
            pltpu.VMEM((length, width), BF),
            pltpu.VMEM((n_s, n_f, SMALL, 128), F32),
            pltpu.VMEM((columns, length), BF),
            pltpu.VMEM((columns, length), F32),
            pltpu.SemaphoreType.DMA((Packets.count(n_f, n_s),)),
            pltpu.SemaphoreType.DMA((Spread.count(n_f),)),
            pltpu.SemaphoreType.DMA((Spread.count(n_f),)),
            *Line.sems(n_s),
        ],
        compiler_params=pltpu.CompilerParams(
            collective_id=1, has_side_effects=True, vmem_limit_bytes=60 * 2**20
        ),
        cost_estimate=pl.CostEstimate(
            flops=2 * length * columns * (3 * width + 2 * length),
            bytes_accessed=4 * length * width,
            transcendentals=length * length * columns // HEAD,
        ),
    )(tokens, packet, wq, wo, *tables)


def layer_norm(values, gain, shift):
    center = values - jnp.mean(values, -1, keepdims=True)
    spread = jnp.mean(center * center, -1, keepdims=True)
    inverse = lax.rsqrt(spread + EPSILON)
    scaled = center * inverse
    return (scaled * gain + shift, scaled, inverse)


def norm_back(grad, scaled, inverse, gain):
    upstream = grad * gain
    inner = jnp.mean(upstream, -1, keepdims=True)
    cross = jnp.mean(upstream * scaled, -1, keepdims=True)
    return (
        inverse * (upstream - inner - scaled * cross),
        jnp.sum(grad * scaled, 0),
        jnp.sum(grad, 0),
    )


def angle_tables(positions):
    half = ROT // 2
    freqs = 10000.0 ** (-jnp.arange(half, dtype=jnp.float32) * 2.0 / ROT)
    angles = positions.astype(jnp.float32)[:, None] * freqs[None, :]
    return (jnp.cos(angles)[:, None, :], jnp.sin(angles)[:, None, :])


def rotate(values, cosine, sine):
    half = ROT // 2
    first = values[..., :half]
    second = values[..., half:ROT]
    return jnp.concatenate(
        [first * cosine - second * sine, second * cosine + first * sine, values[..., ROT:]], -1
    )


def score_block(rows, keyset, offset, scale):
    length = keyset.shape[0]
    block_rows = rows.shape[0]
    scores = jnp.einsum("qhd,khd->hqk", rows, keyset, preferred_element_type=jnp.float32) * scale
    visible = (offset + jnp.arange(block_rows, dtype=jnp.int32))[:, None] >= jnp.arange(
        length, dtype=jnp.int32
    )[None, :]
    return jnp.where(visible[None], scores, NEG_LARGE)


def attend_back(queries, keyset, valset, logsums, grad_out):
    length = queries.shape[0]
    block_rows = min(512, length)
    scale = HEAD ** (-0.5)

    def one_block(carry, item):
        grad_keys, grad_vals = carry
        offset, logsum = item
        rows = lax.dynamic_slice_in_dim(queries, offset, block_rows, 0)
        grad_rows = lax.dynamic_slice_in_dim(grad_out, offset, block_rows, 0)
        scores = score_block(rows, keyset, offset, scale)
        weights = jnp.exp(scores - logsum)
        grad_vals = grad_vals + jnp.einsum(
            "hqk,qhd->khd",
            weights.astype(jnp.bfloat16),
            grad_rows,
            preferred_element_type=jnp.float32,
        )
        grad_weights = jnp.einsum(
            "qhd,khd->hqk", grad_rows, valset, preferred_element_type=jnp.float32
        )
        inner = jnp.sum(weights * grad_weights, -1, keepdims=True)
        grad_scores = (weights * (grad_weights - inner)).astype(jnp.bfloat16)
        grad_query_rows = (
            jnp.einsum("hqk,khd->qhd", grad_scores, keyset, preferred_element_type=jnp.float32)
            * scale
        )
        grad_keys = grad_keys + jnp.einsum(
            "hqk,qhd->khd", grad_scores, rows, preferred_element_type=jnp.float32
        )
        return ((grad_keys, grad_vals), grad_query_rows)

    offsets = jnp.arange(length // block_rows, dtype=jnp.int32) * block_rows
    zeros = jnp.zeros(queries.shape, jnp.float32)
    (grad_keys, grad_vals), grad_queries = lax.scan(one_block, (zeros, zeros), (offsets, logsums))
    return (grad_queries.reshape(queries.shape), grad_keys * scale, grad_vals)


def per_device(
    tokens,
    gain_one,
    shift_one,
    w_qkv,
    b_qkv,
    w_out,
    gain_two,
    shift_two,
    w_gate,
    w_up,
    w_down,
    grad_output,
):
    rows_here = tokens.shape[1]
    width = tokens.shape[2]
    groups = lax.axis_size("seq")
    length = rows_here * groups
    columns = w_qkv.shape[2]
    heads_here = columns // HEAD
    column_start = lax.axis_index("seq") * columns
    inputs = tokens[0].astype(jnp.float32)
    cosine, sine = angle_tables(jnp.arange(length, dtype=jnp.int32))
    lanes = 128 - gain_one.shape[0]
    packet = jnp.concatenate(
        [
            jnp.stack([gain_one, shift_one, gain_two, shift_two]),
            b_qkv,
            jnp.zeros((1, gain_one.shape[0]), BF),
        ]
    ).astype(F32)
    packet = jnp.pad(packet, ((0, 0), (0, lanes)))
    queries, keyset, keys_t, valset, mixed_cols, lse, normed_rows, gains, full_qkv, full_out = attend_part(
        tokens[0], packet, w_qkv.transpose(1, 0, 2), w_out, rotary_tables(length)
    )
    full_gain_one, full_shift_one, full_gain_two, full_shift_two = [gains[i] for i in range(4)]
    full_qkv = full_qkv.transpose(1, 0, 2)
    head_shape = (length, heads_here, HEAD)
    queries, keyset, valset = [v.reshape(head_shape) for v in (queries, keyset, valset)]
    block_rows = min(512, length)
    logsums = lse[:heads_here].reshape(heads_here, length // block_rows, block_rows).transpose(1, 0, 2)[..., None]
    full_gate, full_up, full_down = (
        lax.all_gather(w_gate, "fsdp", axis=0, tiled=True),
        lax.all_gather(w_up, "fsdp", axis=0, tiled=True),
        lax.all_gather(w_down, "fsdp", axis=1, tiled=True),
    )
    back_qkv, back_out, back_gate, back_up, back_down = full_qkv, full_out, full_gate, full_up, full_down
    normed, scaled_one, inverse_one = layer_norm(inputs, full_gain_one, full_shift_one)
    part = mixed_cols
    middle = inputs + lax.psum_scatter(
        jnp.dot(part, full_out, preferred_element_type=jnp.float32),
        "seq",
        scatter_dimension=0,
        tiled=True,
    )
    normed_two, scaled_two, inverse_two = layer_norm(middle, full_gain_two, full_shift_two)
    normed_two_low = normed_two.astype(jnp.bfloat16)
    two_rows = lax.all_gather(normed_two_low, "seq", axis=0, tiled=True)
    gate = jnp.dot(two_rows, full_gate, preferred_element_type=jnp.float32)
    up_part = jnp.dot(two_rows, full_up, preferred_element_type=jnp.float32)
    hidden_low = (jax.nn.silu(gate) * up_part).astype(jnp.bfloat16)
    part = hidden_low
    output = middle + lax.psum_scatter(
        jnp.dot(part, full_down, preferred_element_type=jnp.float32).astype(jnp.bfloat16),
        "seq",
        scatter_dimension=0,
        tiled=True,
    ).astype(jnp.float32)
    grad_top = grad_output[0].astype(jnp.float32)
    grad_rows = lax.all_gather(grad_output[0], "seq", axis=0, tiled=True)
    back_normed_rows, back_two_rows = normed_rows, two_rows
    term_down = jnp.einsum("tf,td->fd", hidden_low, grad_rows, preferred_element_type=jnp.float32)
    grad_hidden = jnp.einsum("td,fd->tf", grad_rows, back_down, preferred_element_type=jnp.float32)
    sigma = jax.nn.sigmoid(gate)
    grad_gate = (grad_hidden * up_part * (sigma * (1.0 + gate * (1.0 - sigma)))).astype(
        jnp.bfloat16
    )
    grad_up = (grad_hidden * (gate * sigma)).astype(jnp.bfloat16)
    term_gate = jnp.einsum(
        "td,tf->df", back_two_rows, grad_gate, preferred_element_type=jnp.float32
    )
    term_up = jnp.einsum("td,tf->df", back_two_rows, grad_up, preferred_element_type=jnp.float32)
    grad_normed_two = lax.psum_scatter(
        jnp.einsum("tf,df->td", grad_gate, back_gate, preferred_element_type=jnp.float32)
        + jnp.einsum("tf,df->td", grad_up, back_up, preferred_element_type=jnp.float32),
        "seq",
        scatter_dimension=0,
        tiled=True,
    )
    grad_mid_part, term_gain_two, term_shift_two = norm_back(
        grad_normed_two, scaled_two, inverse_two, full_gain_two
    )
    grad_middle = grad_top + grad_mid_part
    middle_low = grad_middle.astype(jnp.bfloat16)
    mid_rows = lax.all_gather(middle_low, "seq", axis=0, tiled=True)
    term_out = jnp.einsum("tc,te->ce", mixed_cols, mid_rows, preferred_element_type=jnp.float32)
    grad_mixed = jnp.einsum(
        "te,ce->tc", mid_rows, back_out, preferred_element_type=jnp.float32
    ).astype(jnp.bfloat16)
    grad_queries, grad_keys, grad_vals = attend_back(
        queries, keyset, valset, logsums, grad_mixed.reshape(head_shape)
    )
    unrot_queries = rotate(grad_queries.astype(jnp.bfloat16).astype(jnp.float32), cosine, -sine)
    unrot_keys = rotate(grad_keys.astype(jnp.bfloat16).astype(jnp.float32), cosine, -sine)
    grad_projected = jnp.stack(
        [
            unrot_queries.reshape(length, columns).astype(jnp.bfloat16),
            unrot_keys.reshape(length, columns).astype(jnp.bfloat16),
            grad_vals.reshape(length, columns).astype(jnp.bfloat16),
        ],
        1,
    )
    term_qkv = jnp.einsum(
        "td,tkc->dkc", back_normed_rows, grad_projected, preferred_element_type=jnp.float32
    )
    bias_here = jnp.sum(grad_projected.astype(jnp.float32), 0)
    term_bias = lax.dynamic_update_slice(
        jnp.zeros((3, width), jnp.float32), bias_here, (jnp.int32(0), column_start)
    )
    part = grad_projected
    grad_normed = lax.psum_scatter(
        jnp.einsum("tkc,dkc->td", part, back_qkv, preferred_element_type=jnp.float32).astype(
            jnp.bfloat16
        ),
        "seq",
        scatter_dimension=0,
        tiled=True,
    ).astype(jnp.float32)
    grad_in_part, term_gain_one, term_shift_one = norm_back(
        grad_normed, scaled_one, inverse_one, full_gain_one
    )
    grad_input = grad_middle + grad_in_part
    grad_qkv, grad_out, grad_gate_w, grad_up_w, grad_down_w = (
        lax.psum_scatter(
            term_qkv.astype(jnp.bfloat16), "fsdp", scatter_dimension=0, tiled=True
        ).astype(jnp.float32),
        lax.psum_scatter(
            term_out.astype(jnp.bfloat16), "fsdp", scatter_dimension=1, tiled=True
        ).astype(jnp.float32),
        lax.psum_scatter(
            term_gate.astype(jnp.bfloat16), "fsdp", scatter_dimension=0, tiled=True
        ).astype(jnp.float32),
        lax.psum_scatter(
            term_up.astype(jnp.bfloat16), "fsdp", scatter_dimension=0, tiled=True
        ).astype(jnp.float32),
        lax.psum_scatter(
            term_down.astype(jnp.bfloat16), "fsdp", scatter_dimension=1, tiled=True
        ).astype(jnp.float32),
    )
    grad_gain_one, grad_shift_one, grad_gain_two, grad_shift_two, grad_bias = (
        lax.psum_scatter(term_gain_one, ("fsdp", "seq"), scatter_dimension=0, tiled=True),
        lax.psum_scatter(term_shift_one, ("fsdp", "seq"), scatter_dimension=0, tiled=True),
        lax.psum_scatter(term_gain_two, ("fsdp", "seq"), scatter_dimension=0, tiled=True),
        lax.psum_scatter(term_shift_two, ("fsdp", "seq"), scatter_dimension=0, tiled=True),
        lax.psum_scatter(term_bias, ("fsdp", "seq"), scatter_dimension=1, tiled=True),
    )
    return (
        output.astype(jnp.bfloat16)[None],
        grad_input[None],
        grad_gain_one,
        grad_shift_one,
        grad_qkv,
        grad_bias,
        grad_out,
        grad_gain_two,
        grad_shift_two,
        grad_gate_w,
        grad_up_w,
        grad_down_w,
    )


def solution(mesh):
    return jax.shard_map(
        per_device,
        mesh=mesh,
        in_specs=(
            P("fsdp", "seq", None),
            P(("fsdp", "seq")),
            P(("fsdp", "seq")),
            P("fsdp", None, "seq"),
            P(None, ("fsdp", "seq")),
            P("seq", "fsdp"),
            P(("fsdp", "seq")),
            P(("fsdp", "seq")),
            P("fsdp", "seq"),
            P("fsdp", "seq"),
            P("seq", "fsdp"),
            P("fsdp", "seq", None),
        ),
        out_specs=(
            P("fsdp", "seq", None),
            P("fsdp", "seq", None),
            P(("fsdp", "seq")),
            P(("fsdp", "seq")),
            P("fsdp", None, "seq"),
            P(None, ("fsdp", "seq")),
            P("seq", "fsdp"),
            P(("fsdp", "seq")),
            P(("fsdp", "seq")),
            P("fsdp", "seq"),
            P("fsdp", "seq"),
            P("seq", "fsdp"),
        ),
        check_vma=False,
    )
```

```python
import functools

import jax
import jax.numpy as jnp
import numpy as np
from jax import lax
from jax.experimental import pallas as pl
from jax.experimental.pallas import tpu as pltpu
from jax.sharding import PartitionSpec as P

HEAD = 64
ROT = 16
EPSILON = 1e-05
NEG_LARGE = -1e30
MESH = pl.DeviceIdType.MESH
ANY = pl.BlockSpec(memory_space=pl.ANY)
VMEM = pl.BlockSpec(memory_space=pltpu.VMEM)
BF = jnp.bfloat16
F32 = jnp.float32
SMALL = 8


def put(src, dst, send, recv, **device):
    return pltpu.make_async_remote_copy(
        src_ref=src, dst_ref=dst, send_sem=send, recv_sem=recv, device_id=device, device_id_type=MESH
    )


def dot(left, right):
    return jnp.dot(left, right, preferred_element_type=F32)


def dot_nt(left, right):
    return lax.dot_general(left, right, (((1,), (1,)), ((), ())), preferred_element_type=F32)


def dot_tn(left, right):
    return lax.dot_general(left, right, (((0,), (0,)), ((), ())), preferred_element_type=F32)


def aligned(start, size, unit=None):
    return pl.ds(pl.multiple_of(start, unit or size), size)


class Net:
    def __init__(self):
        self.n_f, self.n_s = lax.axis_size("fsdp"), lax.axis_size("seq")
        self.tall = 2 if self.n_f % 2 == 0 else 1
        self.wide = self.n_f // self.tall
        self.n_l = self.n_s // 2
        self.f, self.s = lax.axis_index("fsdp"), lax.axis_index("seq")
        self.a, self.b = self.f // self.wide, self.f % self.wide
        self.z, self.c = self.s // 2, self.s % 2
        self.mate = self.s + 1 - 2 * self.c

    def barrier(self):
        sem = pltpu.get_barrier_semaphore()
        for k in range(1, self.n_f):
            pl.semaphore_signal(
                sem, inc=1, device_id={"fsdp": (self.f + k) % self.n_f}, device_id_type=MESH
            )
        for k in range(1, self.n_s):
            pl.semaphore_signal(
                sem, inc=1, device_id={"seq": (self.s + k) % self.n_s}, device_id_type=MESH
            )
        pl.semaphore_wait(sem, self.n_f + self.n_s - 2)

    def sides(self, hop, act):
        @pl.loop(0, 2)
        def _(side):
            other = self.z + (2 * side - 1) * hop

            @pl.when((other >= 0) & (other < self.n_l))
            def _():
                act(other, side)


class Spread:
    def __init__(self, net, src, part, sems):
        self.net, self.src, self.part, self.sems = net, src, part, sems
        self.rows = [j for j in range(1, net.wide)]
        self.cols = [i for i in range(1, net.tall)]

    @staticmethod
    def count(n_f):
        tall = 2 if n_f % 2 == 0 else 1
        wide = n_f // tall
        return 1 + 2 * (wide - 1) + 2 * (tall - 1) + 4 * (wide - 1) * (tall - 1)

    def at(self, kind, i, j):
        w, t = len(self.rows), len(self.cols)
        base = {
            "own": 0,
            "row": 1,
            "col": 1 + 2 * w,
            "half0": 1 + 2 * w + 2 * t,
            "half1": 1 + 2 * w + 2 * t + 2 * w * t,
        }[kind]
        if kind == "own":
            return self.sems.at[0]
        k = j - 1 if kind == "row" else i - 1 if kind == "col" else (i - 1) * w + j - 1
        return self.sems.at[base + 2 * k], self.sems.at[base + 2 * k + 1]

    def rank(self, i, j):
        net = self.net
        return ((net.a + i) % net.tall) * net.wide + (net.b + j) % net.wide

    def back(self, i, j):
        net = self.net
        return ((net.a - i + net.tall) % net.tall) * net.wide + (net.b - j + net.wide) % net.wide

    def own(self):
        return pltpu.make_async_copy(self.src, self.part(self.net.f, None), self.at("own", 0, 0))

    def first(self, i, j):
        send, recv = self.at("row" if i == 0 else "col", i, j)
        return put(self.src, self.part(self.net.f, None), send, recv, fsdp=self.rank(i, j))

    def came(self, i, j):
        send, recv = self.at("row" if i == 0 else "col", i, j)
        place = self.part(self.back(i, j), None)
        return put(place, place, send, recv, fsdp=self.rank(i, j))

    def second(self, half, i, j, came=False):
        send, recv = self.at("half0" if half == 0 else "half1", i, j)
        origin = self.back(i, j) if came else self.back(0, j) if half == 0 else self.back(i, 0)
        place = self.part(origin, half)
        return put(place, place, send, recv, fsdp=self.rank(i, 0) if half == 0 else self.rank(0, j))

    def start(self):
        self.own().start()
        for i in self.cols:
            self.first(i, 0).start()
        for j in self.rows:
            self.first(0, j).start()

    def relay(self):
        for j in self.rows:
            self.came(0, j).wait_recv()
            for i in self.cols:
                self.second(0, i, j).start()
        for i in self.cols:
            self.came(i, 0).wait_recv()
            for j in self.rows:
                self.second(1, i, j).start()

    def finish(self):
        self.own().wait()
        for j in self.rows:
            self.first(0, j).wait_send()
        for i in self.cols:
            self.first(i, 0).wait_send()
        for i in self.cols:
            for j in self.rows:
                for half in range(2):
                    self.second(half, i, j, came=True).wait_recv()
                    self.second(half, i, j).wait_send()


class Line:
    def __init__(self, net, src, part, recv, send):
        self.net, self.src, self.part, self.recv, self.send = net, src, part, recv, send

    @staticmethod
    def sems(n_s):
        return [pltpu.SemaphoreType.DMA((n_s,)), pltpu.SemaphoreType.DMA((4, n_s // 2))]

    def own(self):
        net = self.net
        return pltpu.make_async_copy(self.src, self.part(net.s), self.recv.at[net.s])

    def on_line(self, src, chunk, side, hop):
        net = self.net
        return put(
            src,
            self.part(chunk),
            self.send.at[side, hop],
            self.recv.at[chunk],
            seq=net.s + 2 - 4 * side,
        )

    def to_mate(self, src, chunk, side, hop):
        return put(src, self.part(chunk), self.send.at[2 + side, hop], self.recv.at[chunk], seq=self.net.mate)

    def goes_on(self, side):
        after = self.net.z + 1 - 2 * side
        return (after >= 0) & (after < self.net.n_l)

    def start(self):
        net = self.net
        self.own().start()
        for side in range(2):

            @pl.when(self.goes_on(side))
            def _():
                self.on_line(self.src, net.s, side, 0).start()

        self.to_mate(self.src, net.s, 0, 0).start()

    def arrive(self, chunk):
        place = self.part(chunk)
        put(place, place, self.send.at[0, 0], self.recv.at[chunk], seq=self.net.mate).wait_recv()

    def step(self, hop):
        net = self.net

        def act(other, side):
            chunk = 2 * other + net.c
            self.arrive(chunk)

            @pl.when(self.goes_on(side))
            def _():
                self.on_line(self.part(chunk), chunk, side, hop).start()

            self.to_mate(self.part(chunk), chunk, side, hop).start()

        net.sides(hop, act)

    def pair(self, other):
        self.arrive(2 * other + 1 - self.net.c)

    def finish(self):
        net = self.net
        for side in range(2):

            @pl.when(self.goes_on(side))
            def _():
                self.on_line(self.src, net.s, side, 0).wait_send()

        self.to_mate(self.src, net.s, 0, 0).wait_send()

        @pl.loop(1, net.n_l)
        def _(hop):
            def act(other, side):
                chunk = 2 * other + net.c

                @pl.when(self.goes_on(side))
                def _():
                    self.on_line(self.part(chunk), chunk, side, hop).wait_send()

                self.to_mate(self.part(chunk), chunk, side, hop).wait_send()

            net.sides(hop, act)


class Packets:
    def __init__(self, net, src, buf, sems):
        self.net, self.src, self.buf, self.sems = net, src, buf, sems

    @staticmethod
    def count(n_f, n_s):
        return 1 + 2 * (n_f - 1) + 2 * (n_s - 1)

    def own(self):
        net = self.net
        return pltpu.make_async_copy(self.src, self.buf.at[net.s, net.f], self.sems.at[0])

    def one(self, k, came=False):
        net = self.net
        f = (net.f - k + net.n_f) % net.n_f if came else net.f
        place = self.buf.at[net.s, f]
        return put(
            place if came else self.src,
            place,
            self.sems.at[2 * k - 1],
            self.sems.at[2 * k],
            fsdp=(net.f + k) % net.n_f,
        )

    def two(self, k, came=False):
        net = self.net
        place = self.buf.at[(net.s - k + net.n_s) % net.n_s if came else net.s]
        at = 2 * (net.n_f - 1) + 2 * k - 1
        return put(place, place, self.sems.at[at], self.sems.at[at + 1], seq=(net.s + k) % net.n_s)

    def start(self):
        self.own().start()
        for k in range(1, self.net.n_f):
            self.one(k).start()

    def middle(self):
        self.own().wait()
        for k in range(1, self.net.n_f):
            self.one(k, came=True).wait_recv()
            self.one(k).wait_send()
        for k in range(1, self.net.n_s):
            self.two(k).start()

    def finish(self):
        for k in range(1, self.net.n_s):
            self.two(k, came=True).wait_recv()
            self.two(k).wait_send()

    def unpack(self, out, width):
        net = self.net
        per = 128 // width
        for tile in range(net.n_f * net.n_s // per):
            total = None
            for j in range(per):
                f, s = divmod(tile * per + j, net.n_s)
                piece = self.buf[s, f]
                if j:
                    piece = pltpu.roll(piece, j * width, axis=1)
                total = piece if total is None else total + piece
            out[:, tile * 128 : (tile + 1) * 128] = total


def rotary(values, cosine, sine_next, sine_last):
    columns = values.shape[1]
    half = ROT // 2
    times = columns // 128

    def wide(table):
        return table if times == 1 else jnp.concatenate([table] * times, axis=1)

    following = pltpu.roll(values, columns - half, axis=1)
    previous = pltpu.roll(values, half, axis=1)
    return values * wide(cosine) + following * wide(sine_next) + previous * wide(sine_last)


def rotary_tables(length):
    half = ROT // 2
    freqs = np.float32(10000.0) ** (-np.arange(half, dtype=np.float32) * np.float32(2.0 / ROT))
    angles = np.arange(length, dtype=np.float32)[:, None] * freqs[None, :].astype(np.float32)
    cosine, sine = np.cos(angles), np.sin(angles)
    rest = np.zeros((length, HEAD - ROT), np.float32)
    none = np.zeros_like(sine)
    keep = np.concatenate([cosine, cosine, rest + 1], 1)
    following = np.concatenate([-sine, none, rest], 1)
    previous = np.concatenate([none, sine, rest], 1)
    return [np.tile(t, (1, 128 // HEAD)).astype(np.float32) for t in (keep, following, previous)]


def normalize(values):
    center = values - jnp.mean(values, -1, keepdims=True)
    inverse = lax.rsqrt(jnp.mean(center * center, -1, keepdims=True) + EPSILON)
    return center * inverse, inverse


def attend_kernel(
    tok,
    packet,
    wq,
    wo,
    cosine,
    sine_next,
    sine_last,
    q_o,
    k_o,
    kt_o,
    v_o,
    att_o,
    lse_o,
    n1_o,
    gains_o,
    wq_o,
    wo_o,
    rows,
    packets,
    vt,
    ot,
    pk_sems,
    wq_sems,
    wo_sems,
    tok_recv,
    tok_send,
):
    net = Net()
    chunk, width = tok.shape
    length = chunk * net.n_s
    depth = wq.shape[1]
    columns = wq.shape[2]
    heads = columns // HEAD
    pair = 2 * chunk
    block = 256

    net.barrier()
    pk = Packets(net, packet, packets, pk_sems)

    def wq_part(f, half):
        if half is None:
            return wq_o.at[:, aligned(f * depth, depth), :]
        return wq_o.at[:, aligned(f * depth + half * (depth // 2), depth // 2), :]

    def wo_part(f, half):
        span = aligned(f * depth, depth)
        if half is None:
            return wo_o.at[:, span]
        return wo_o.at[pl.ds(half * (columns // 2), columns // 2), span]

    spread_q = Spread(net, wq, wq_part, wq_sems)
    spread_o = Spread(net, wo, wo_part, wo_sems)
    line = Line(net, tok, lambda s: rows.at[aligned(s * chunk, chunk)], tok_recv, tok_send)
    pk.start()
    line.start()
    spread_q.start()
    spread_o.start()
    pk.middle()
    pk.finish()
    pk.unpack(gains_o, width // (net.n_f * net.n_s))

    def norm_block(other):
        gain, shift = gains_o[0:1, :], gains_o[1:2, :]

        @pl.loop(0, pair // 32)
        def _(i):
            span = aligned(other * pair + i * 32, 32)
            scaled, _ = normalize(rows[span, :].astype(F32))
            n1_o[span, :] = (scaled * gain + shift).astype(BF)

    def project_block(other):
        span = aligned(other * pair, pair)
        left = n1_o[span, :]
        cols = aligned(net.s * columns, columns)
        tables = cosine[span, :], sine_next[span, :], sine_last[span, :]
        for kind in range(3):
            value = dot(left, wq_o[kind]) + gains_o[4 + kind : 5 + kind, cols]
            if kind == 0:
                q_o[span, :] = rotary(value, *tables).astype(BF)
            elif kind == 1:
                value = rotary(value, *tables)
                k_o[span, :] = value.astype(BF)
                kt_o[:, span] = value.T.astype(BF)
            else:
                v_o[span, :] = value.astype(BF)
                vt[:, span] = value.T.astype(BF)

    line.arrive(net.s)
    line.pair(net.z)
    norm_block(net.z)

    def hop_norm(hop):
        line.step(hop)

        def act(other, side):
            line.pair(other)
            norm_block(other)

        net.sides(hop, act)

    for hop in range(1, net.n_l - 1):
        hop_norm(hop)
        if hop == 1:
            spread_q.relay()
    spread_q.finish()

    @pl.loop(0, net.n_l - 1)
    def _(hop):
        def act(other, side):
            @pl.when((hop > 0) | (side == 0))
            def _():
                project_block(other)

        net.sides(hop, act)

    spread_o.relay()
    hop_norm(net.n_l - 1)
    net.sides(net.n_l - 1, lambda other, side: project_block(other))

    @pl.loop(0, heads)
    def _(head):
        lane = lax.broadcasted_iota(jnp.int32, (1, columns), 1)
        here = jnp.where(lane // HEAD == head, HEAD**-0.5, 0.0).astype(BF)
        visible = lax.broadcasted_iota(jnp.int32, (block, block), 0) <= lax.broadcasted_iota(
            jnp.int32, (block, block), 1
        )
        head_rows = aligned(head * HEAD, HEAD)
        for i in range(length // block):
            lo, hi = i * block, (i + 1) * block
            query = q_o[lo:hi, :] * here
            near = jnp.where(visible, dot_nt(k_o[lo:hi, :], query), NEG_LARGE)
            highest = jnp.max(near, 0, keepdims=True)
            if i:
                far = dot_nt(k_o[0:lo, :], query)
                highest = jnp.maximum(highest, jnp.max(far, 0, keepdims=True))
            near = jnp.exp(near - highest)
            total = jnp.sum(near, 0, keepdims=True)
            out = dot(vt[head_rows, lo:hi], near.astype(BF))
            if i:
                far = jnp.exp(far - highest)
                total = total + jnp.sum(far, 0, keepdims=True)
                out = out + dot(vt[head_rows, 0:lo], far.astype(BF))
            ot[head_rows, lo:hi] = out / total
            lse_o[pl.ds(head, 1), lo:hi] = highest + jnp.log(total)

    for i in range(length // block):
        att_o[i * block : (i + 1) * block, :] = ot[:, i * block : (i + 1) * block].T.astype(BF)

    line.finish()
    spread_o.finish()


def attend_part(tokens, packet, wq, wo, tables):
    chunk, width = tokens.shape
    n_f, n_s = lax.axis_size("fsdp"), lax.axis_size("seq")
    length = chunk * n_s
    columns = wq.shape[2]
    shape = jax.ShapeDtypeStruct
    return pl.pallas_call(
        attend_kernel,
        name="attend",
        out_shape=[
            shape((length, columns), BF),
            shape((length, columns), BF),
            shape((columns, length), BF),
            shape((length, columns), BF),
            shape((length, columns), BF),
            shape((8, length), F32),
            shape((length, width), BF),
            shape((SMALL, width), F32),
            shape((3, width, columns), BF),
            shape((columns, width), BF),
        ],
        in_specs=[ANY, VMEM, ANY, ANY, VMEM, VMEM, VMEM],
        out_specs=[VMEM] * 9 + [ANY],
        scratch_shapes=[
            pltpu.VMEM((length, width), BF),
            pltpu.VMEM((n_s, n_f, SMALL, 128), F32),
            pltpu.VMEM((columns, length), BF),
            pltpu.VMEM((columns, length), F32),
            pltpu.SemaphoreType.DMA((Packets.count(n_f, n_s),)),
            pltpu.SemaphoreType.DMA((Spread.count(n_f),)),
            pltpu.SemaphoreType.DMA((Spread.count(n_f),)),
            *Line.sems(n_s),
        ],
        compiler_params=pltpu.CompilerParams(
            collective_id=1, has_side_effects=True, vmem_limit_bytes=60 * 2**20
        ),
        cost_estimate=pl.CostEstimate(
            flops=2 * length * columns * (3 * width + 2 * length),
            bytes_accessed=4 * length * width,
            transcendentals=length * length * columns // HEAD,
        ),
    )(tokens, packet, wq, wo, *tables)


def wide_rows(start, count):
    return lambda i: aligned(start + i * 32, 32), count // 32


class Fold:
    def __init__(self, net, acc, mate_in, coming, mate_out, out, mate_send, mate_recv, send, recv):
        self.net, self.acc = net, acc
        self.mate_in, self.coming, self.mate_out, self.out = mate_in, coming, mate_out, out
        self.mate_send, self.mate_recv, self.send, self.recv = mate_send, mate_recv, send, recv
        self.chunk = acc.shape[0] // 2

    @staticmethod
    def buffers(n_s, chunk, width):
        n_l = n_s // 2
        return [
            pltpu.VMEM((n_l, chunk, width), BF),
            pltpu.VMEM((n_l + 1, chunk, width), BF),
            pltpu.VMEM((2, chunk, width), BF),
            pltpu.VMEM((2, 2, chunk, width), BF),
        ]

    @staticmethod
    def sems(n_s):
        n_l = n_s // 2
        return [
            pltpu.SemaphoreType.DMA((2,)),
            pltpu.SemaphoreType.DMA((n_l,)),
            pltpu.SemaphoreType.DMA((2, 2)),
            pltpu.SemaphoreType.DMA((n_l + 1,)),
        ]

    def mine(self, i):
        return aligned(self.net.c * self.chunk + i * 32, 32)

    def place(self, other):
        return (other >= 0) & (other < self.net.n_l)

    def to_mate(self, target, side):
        return put(
            self.mate_out.at[side],
            self.mate_in.at[target],
            self.mate_send.at[side],
            self.mate_recv.at[target],
            seq=self.net.mate,
        )

    def onward(self, target, side, hop):
        last = (1 - side) * (1 // hop)
        slot = target + (self.net.n_l - target) * last
        return put(
            self.out.at[side, hop % 2],
            self.coming.at[slot],
            self.send.at[side, hop % 2],
            self.recv.at[slot],
            seq=self.net.s + 4 * side - 2,
        )

    def came(self, slot):
        place = self.coming.at[slot]
        put(place, place, self.send.at[0, 0], self.recv.at[slot], seq=self.net.mate).wait_recv()

    def swap(self, target, side):
        count = self.chunk // 32

        @pl.loop(0, count)
        def _(i):
            theirs = aligned((1 - self.net.c) * self.chunk + i * 32, 32)
            self.mate_out[side, aligned(i * 32, 32), :] = self.acc[theirs, :].astype(BF)

        self.to_mate(target, side).start()

    def swapped(self, target, side):
        self.to_mate(target, side).wait_recv()

    def add(self, ref, at):
        @pl.loop(0, self.chunk // 32)
        def _(i):
            span = self.mine(i)
            self.acc[span, :] = self.acc[span, :] + ref[at, aligned(i * 32, 32), :].astype(F32)

    def step(self, hop, produce):
        net = self.net

        def act(target, side):
            produce(target, self.acc)
            further = target + 2 * side - 1

            @pl.when(self.place(further))
            def _():
                self.to_mate(further, side).wait_send()

            self.swap(target, side)
            self.swapped(target, side)
            self.add(self.mate_in, target)

            @pl.when(self.place(net.z + 1 - 2 * side))
            def _():
                self.came(target)
                self.add(self.coming, target)

            @pl.when(self.place(further + 2 * side - 1))
            def _():
                self.onward(target, side, hop + 2).wait_send()

            @pl.loop(0, self.chunk // 32)
            def _(i):
                self.out[side, hop % 2, aligned(i * 32, 32), :] = self.acc[self.mine(i), :].astype(BF)

            self.onward(target, side, hop).start()

        net.sides(hop, act)

    def last(self, produce):
        net = self.net

        @pl.when(net.z > 0)
        def _():
            self.to_mate(net.z - 1, 0).wait_send()

        produce(net.z, self.acc)
        self.swap(net.z, 0)
        self.swapped(net.z, 0)
        self.add(self.mate_in, net.z)

        @pl.when(net.z > 0)
        def _():
            self.came(net.z)
            self.add(self.coming, net.z)

        @pl.when(net.z < net.n_l - 1)
        def _():
            self.came(net.n_l)
            self.add(self.coming, net.n_l)

    def finish(self):
        net = self.net
        self.to_mate(net.z, 0).wait_send()

        @pl.when(net.z < net.n_l - 1)
        def _():
            self.to_mate(net.z + 1, 1).wait_send()

        @pl.loop(1, min(3, net.n_l))
        def _(hop):
            net.sides(hop, lambda target, side: self.onward(target, side, hop).wait_send())


class Direct:
    def __init__(self, net, stage, recv, sems):
        self.net, self.stage, self.recv, self.sems = net, stage, recv, sems

    def owner(self, k):
        return (self.net.f + k) % self.net.n_f

    def copy(self, k):
        return put(
            self.stage.at[k],
            self.recv.at[self.net.f],
            self.sems.at[0, k],
            self.sems.at[1, k],
            fsdp=self.owner(k),
        )

    def keep(self):
        return pltpu.make_async_copy(self.stage.at[0], self.recv.at[self.net.f], self.sems.at[0, 0])

    def finish(self):
        self.keep().wait()

        @pl.loop(1, self.net.n_f)
        def _(k):
            place = self.recv.at[(self.net.f - k + self.net.n_f) % self.net.n_f]
            put(place, place, self.sems.at[0, k], self.sems.at[1, k], fsdp=self.owner(k)).wait_recv()
            self.copy(k).wait_send()


class PacketSum:
    def __init__(self, net, out, seq_in, total, fsdp_in, sems):
        self.net, self.out, self.seq_in, self.total, self.fsdp_in, self.sems = net, out, seq_in, total, fsdp_in, sems

    @staticmethod
    def scratch(n_f, n_s):
        return [
            pltpu.VMEM((n_s, n_f, SMALL, 128), F32),
            pltpu.VMEM((n_s, n_f, SMALL, 128), F32),
            pltpu.VMEM((n_f, SMALL, 128), F32),
            pltpu.VMEM((n_f, SMALL, 128), F32),
            pltpu.SemaphoreType.DMA((2 * (n_f + n_s),)),
        ]

    def one(self, k):
        to = (self.net.s + k) % self.net.n_s
        return put(self.out.at[to], self.seq_in.at[k], self.sems.at[2 * k], self.sems.at[2 * k + 1], seq=to)

    def two(self, k):
        to = (self.net.f + k) % self.net.n_f
        at = 2 * (self.net.n_s + k)
        return put(self.total.at[to], self.fsdp_in.at[k], self.sems.at[at], self.sems.at[at + 1], fsdp=to)

    def run(self, terms, result, width):
        net = self.net
        per = 128 // width
        for tile in range(net.n_f * net.n_s // per):
            value = terms[:, tile * 128 : (tile + 1) * 128]
            for j in range(per):
                f, s = divmod(tile * per + j, net.n_s)
                self.out[s, f] = pltpu.roll(value, 128 - j * width, axis=1) if j else value
        for k in range(1, net.n_s):
            self.one(k).start()
        total = self.out[net.s]
        for k in range(1, net.n_s):
            self.one(k).wait()
            total = total + self.seq_in[k]
        self.total[...] = total
        for k in range(1, net.n_f):
            self.two(k).start()
        total = self.total[net.f]
        for k in range(1, net.n_f):
            self.two(k).wait()
            total = total + self.fsdp_in[k]
        result[...] = total


def norm_backward(rows, source, grad, grad_rows, gain, terms, at, write):
    terms[at : at + 2, :] = jnp.zeros((2, terms.shape[1]), F32)

    @pl.loop(0, rows // 32)
    def _(i):
        span = aligned(i * 32, 32)
        scaled, inverse = normalize(source[span, :].astype(F32))
        value = grad[grad_rows(i), :]
        upstream = value * gain
        inner = jnp.mean(upstream, -1, keepdims=True)
        cross = jnp.mean(upstream * scaled, -1, keepdims=True)
        terms[at : at + 1, :] = terms[at : at + 1, :] + jnp.sum(value * scaled, 0, keepdims=True)
        terms[at + 1 : at + 2, :] = terms[at + 1 : at + 2, :] + jnp.sum(value, 0, keepdims=True)
        write(span, inverse * (upstream - inner - scaled * cross))


def middle_kernel(
    att,
    wo,
    tok,
    gains,
    gout_own,
    gout_any,
    wg_own,
    wu_own,
    wd_own,
    dmid_o,
    top_o,
    terms_o,
    dm_rows_o,
    gate_o,
    up_o,
    down_o,
    mid,
    n2,
    n2_own,
    gout,
    hidden,
    dgate,
    dup,
    wg,
    wu,
    wd,
    stage_gate,
    stage_up,
    stage_down,
    acc,
    *rest,
):
    net = Net()
    chunk, width = tok.shape
    units = wg.shape[1]
    pair = 2 * chunk
    depth = wg_own.shape[0]
    tile = 512
    first_buffers, rest = rest[:4], rest[4:]
    second_buffers, rest = rest[:4], rest[4:]
    first_sems, rest = rest[:4], rest[4:]
    middle_sems, rest = rest[:4], rest[4:]
    last_sems, rest = rest[:4], rest[4:]
    gout_sems, rest = rest[:2], rest[2:]
    n2_sems, rest = rest[:2], rest[2:]
    dm_sems, rest = rest[:2], rest[2:]
    spread_sems, rest = rest[:3], rest[3:]
    gate_sems, up_sems, down_sems = rest

    net.barrier()

    def deep(ref):
        def part(f, half):
            if half is None:
                return ref.at[aligned(f * depth, depth), :]
            return ref.at[aligned(f * depth + half * (depth // 2), depth // 2), :]

        return part

    def wd_part(f, half):
        span = aligned(f * depth, depth)
        if half is None:
            return wd.at[:, span]
        return wd.at[pl.ds(half * (units // 2), units // 2), span]

    spreads = [
        Spread(net, wg_own, deep(wg), spread_sems[0]),
        Spread(net, wu_own, deep(wu), spread_sems[1]),
        Spread(net, wd_own, wd_part, spread_sems[2]),
    ]
    chunk_of = lambda ref: lambda s: ref.at[aligned(s * chunk, chunk)]
    gout_line = Line(net, gout_any, chunk_of(gout), *gout_sems)
    n2_line = Line(net, n2_own, chunk_of(n2), *n2_sems)
    dm_line = Line(net, n2_own, chunk_of(dm_rows_o), *dm_sems)
    first = Fold(net, acc, *first_buffers, *first_sems)
    middle = Fold(net, acc, *first_buffers, *middle_sems)
    last = Fold(net, acc, *second_buffers, *last_sems)

    for spread in spreads:
        spread.start()
    gout_line.start()

    def produce_attended(place, acc):
        left = att[aligned(place * pair, pair), :]

        @pl.loop(0, width // tile)
        def _(j):
            cols = aligned(j * tile, tile)
            acc[:, cols] = dot(left, wo[:, cols])

    @pl.loop(0, net.n_l - 1)
    def _(j):
        first.step(net.n_l - 1 - j, produce_attended)
        gout_line.step(j + 1)

    first.last(produce_attended)

    gain_two, shift_two = gains[2:3, :], gains[3:4, :]

    @pl.loop(0, chunk // 32)
    def _(i):
        span = aligned(i * 32, 32)
        value = tok[span, :].astype(F32) + acc[first.mine(i), :]
        mid[span, :] = value
        scaled, _ = normalize(value)
        n2_own[span, :] = (scaled * gain_two + shift_two).astype(BF)

    n2_line.start()
    first.finish()
    for spread in spreads:
        spread.relay()

    gout_line.arrive(net.s)
    gout_line.pair(net.z)

    @pl.loop(1, net.n_l)
    def _(hop):
        net.sides(hop, lambda other, side: gout_line.pair(other))

    def forward_block(other):
        span = aligned(other * pair, pair)
        rows = n2[span, :]
        gate = dot(rows, wg[...])
        up = dot(rows, wu[...])
        back = dot_nt(gout[span, :], wd[...])
        sigma = jax.nn.sigmoid(gate)
        active = gate * sigma
        hidden[span, :] = (active * up).astype(BF)
        dgate[span, :] = (back * up * (sigma * (1.0 + gate * (1.0 - sigma)))).astype(BF)
        dup[span, :] = (back * active).astype(BF)

    n2_line.arrive(net.s)
    n2_line.pair(net.z)

    @pl.loop(1, net.n_l - 1)
    def _(hop):
        n2_line.step(hop)
        net.sides(hop, lambda other, side: n2_line.pair(other))

    for spread in spreads:
        spread.finish()

    @pl.loop(0, net.n_l - 1)
    def _(hop):
        def act(other, side):
            @pl.when((hop > 0) | (side == 0))
            def _():
                forward_block(other)

        net.sides(hop, act)

    n2_line.step(net.n_l - 1)

    def last_block(other, side):
        n2_line.pair(other)
        forward_block(other)

    net.sides(net.n_l - 1, last_block)
    n2_line.finish()

    gate_direct = Direct(net, stage_gate, gate_o, gate_sems)
    up_direct = Direct(net, stage_up, up_o, up_sems)
    down_direct = Direct(net, stage_down, down_o, down_sems)

    def weight_terms(k):
        cols = aligned(gate_direct.owner(k) * depth, depth)
        stage_down[k] = dot_tn(hidden[...], gout[:, cols]).astype(BF)
        left = n2[:, cols].T
        stage_gate[k] = dot(left, dgate[...]).astype(BF)
        stage_up[k] = dot(left, dup[...]).astype(BF)

    def send_terms(k):
        weight_terms(k)
        down_direct.copy(k).start()
        gate_direct.copy(k).start()
        up_direct.copy(k).start()

    def produce_normed(place, acc):
        span = aligned(place * pair, pair)
        left, right = dgate[span, :], dup[span, :]

        @pl.loop(0, width // tile)
        def _(j):
            cols = aligned(j * tile, tile)
            acc[:, cols] = dot_nt(left, wg[cols, :]) + dot_nt(right, wu[cols, :])

    each = -(-(net.n_f - 1) // (net.n_l - 1))

    @pl.loop(0, net.n_l - 1)
    def _(j):
        middle.step(net.n_l - 1 - j, produce_normed)

        @pl.loop(0, each)
        def _(i):
            k = 1 + j * each + i

            @pl.when(k < net.n_f)
            def _():
                send_terms(k)

    middle.last(produce_normed)

    def write_middle(span, value):
        value = value + gout_own[span, :].astype(F32)
        dmid_o[span, :] = value
        n2_own[span, :] = value.astype(BF)

    terms_o[...] = jnp.zeros(terms_o.shape, F32)
    norm_backward(chunk, mid, acc, middle.mine, gain_two, terms_o, 2, write_middle)
    dm_line.start()
    middle.finish()

    def produce_top(place, acc):
        left = hidden[aligned(place * pair, pair), :]

        @pl.loop(0, width // tile)
        def _(j):
            cols = aligned(j * tile, tile)
            acc[:, cols] = dot(left, wd[:, cols])

    @pl.loop(0, net.n_l - 1)
    def _(j):
        last.step(net.n_l - 1 - j, produce_top)
        dm_line.step(j + 1)

    last.last(produce_top)

    @pl.loop(0, chunk // 32)
    def _(i):
        span = aligned(i * 32, 32)
        top_o[span, :] = (mid[span, :] + acc[last.mine(i), :]).astype(BF)

    weight_terms(0)
    for direct in (gate_direct, up_direct, down_direct):
        direct.keep().start()

    last.finish()
    dm_line.arrive(net.s)
    dm_line.pair(net.z)

    @pl.loop(1, net.n_l)
    def _(hop):
        net.sides(hop, lambda other, side: dm_line.pair(other))

    gout_line.finish()
    dm_line.finish()
    for direct in (gate_direct, up_direct, down_direct):
        direct.finish()


def middle_part(att, wo, tokens, gains, gout, wg, wu, wd):
    chunk, width = tokens.shape
    n_f, n_s = lax.axis_size("fsdp"), lax.axis_size("seq")
    length = chunk * n_s
    depth, units = wg.shape
    shape = jax.ShapeDtypeStruct
    buffers = Fold.buffers(n_s, chunk, width)
    direct = pltpu.SemaphoreType.DMA((2, n_f))
    return pl.pallas_call(
        middle_kernel,
        name="middle",
        out_shape=[
            shape((chunk, width), F32),
            shape((chunk, width), BF),
            shape((SMALL, width), F32),
            shape((length, width), BF),
            shape((n_f, depth, units), BF),
            shape((n_f, depth, units), BF),
            shape((n_f, units, depth), BF),
        ],
        in_specs=[VMEM] * 5 + [ANY] * 4,
        out_specs=[VMEM] * 3 + [ANY] * 4,
        scratch_shapes=[
            pltpu.VMEM((chunk, width), F32),
            pltpu.VMEM((length, width), BF),
            pltpu.VMEM((chunk, width), BF),
            pltpu.VMEM((length, width), BF),
            pltpu.VMEM((length, units), BF),
            pltpu.VMEM((length, units), BF),
            pltpu.VMEM((length, units), BF),
            pltpu.VMEM((width, units), BF),
            pltpu.VMEM((width, units), BF),
            pltpu.VMEM((units, width), BF),
            pltpu.VMEM((n_f, depth, units), BF),
            pltpu.VMEM((n_f, depth, units), BF),
            pltpu.VMEM((n_f, units, depth), BF),
            pltpu.VMEM((2 * chunk, width), F32),
            *buffers,
            *buffers,
            *Fold.sems(n_s),
            *Fold.sems(n_s),
            *Fold.sems(n_s),
            *Line.sems(n_s),
            *Line.sems(n_s),
            *Line.sems(n_s),
            *[pltpu.SemaphoreType.DMA((Spread.count(n_f),))] * 3,
            *[direct] * 3,
        ],
        compiler_params=pltpu.CompilerParams(
            collective_id=2, has_side_effects=True, vmem_limit_bytes=62 * 2**20
        ),
        cost_estimate=pl.CostEstimate(
            flops=2 * length * width * units * 9,
            bytes_accessed=4 * length * width,
            transcendentals=length * units,
        ),
    )(att, wo, tokens, gains, gout, gout, wg, wu, wd)


def back_kernel(
    dm,
    wo,
    att,
    q,
    k,
    kt,
    v,
    lse,
    n1,
    wq,
    tok,
    dmid,
    gains,
    terms_in,
    cosine,
    sine_next,
    sine_last,
    gin_o,
    small_o,
    out_o,
    qkv_o,
    datt,
    dk,
    dv,
    dqt,
    dproj,
    stage_out,
    stage_qkv,
    terms,
    acc,
    *rest,
):
    net = Net()
    chunk, width = tok.shape
    length, columns = q.shape
    heads = columns // HEAD
    pair = 2 * chunk
    depth = width // net.n_f
    block = 256
    tile = 512
    buffers, rest = rest[:4], rest[4:]
    fold_sems, rest = rest[:4], rest[4:]
    packet_scratch, rest = rest[:5], rest[5:]
    out_sems, qkv_sems = rest

    net.barrier()
    out_direct = Direct(net, stage_out, out_o, out_sems)
    qkv_direct = Direct(net, stage_qkv, qkv_o, qkv_sems)

    @pl.loop(0, length // block)
    def _(i):
        span = aligned(i * block, block)
        datt[span, :] = dot_nt(dm[span, :], wo[...]).astype(BF)
        dk[span, :] = jnp.zeros((block, columns), F32)
        dv[span, :] = jnp.zeros((block, columns), F32)

    def out_term(k):
        cols = aligned(out_direct.owner(k) * depth, depth)
        stage_out[k] = dot_tn(att[...], dm[:, cols]).astype(BF)

    @pl.loop(1, net.n_f)
    def _(k):
        out_term(k)
        out_direct.copy(k).start()

    out_term(0)
    out_direct.keep().start()

    @pl.loop(0, heads)
    def _(head):
        lane = lax.broadcasted_iota(jnp.int32, (1, columns), 1)
        here = jnp.where(lane // HEAD == head, 1.0, 0.0).astype(BF)
        scale = HEAD**-0.5
        visible = lax.broadcasted_iota(jnp.int32, (block, block), 0) <= lax.broadcasted_iota(
            jnp.int32, (block, block), 1
        )
        head_rows = aligned(head * HEAD, HEAD)
        for i in range(length // block):
            lo, hi = i * block, (i + 1) * block
            query = q[lo:hi, :] * (here * scale)
            upstream = datt[lo:hi, :] * here
            logsum = lse[pl.ds(head, 1), lo:hi]

            def part(at, end, mask):
                probs = jnp.exp(dot_nt(k[at:end, :], query) - logsum)
                if mask:
                    probs = jnp.where(visible, probs, 0.0)
                grads = dot_nt(v[at:end, :], upstream)
                dv[at:end, :] = dv[at:end, :] + dot(probs.astype(BF), upstream)
                return probs, grads, jnp.sum(probs * grads, 0, keepdims=True)

            def scored(at, end, probs, grads, inner):
                scores = (probs * (grads - inner)).astype(BF)
                dk[at:end, :] = dk[at:end, :] + dot(scores, query)
                return dot(kt[head_rows, at:end], scores)

            near, near_grads, inner = part(lo, hi, True)
            if i:
                far, far_grads, more = part(0, lo, False)
                inner = inner + more
            out = scored(lo, hi, near, near_grads, inner)
            if i:
                out = out + scored(0, lo, far, far_grads, inner)
            dqt[head_rows, lo:hi] = out * scale

    terms[...] = terms_in[...]
    bias_cols = aligned(net.s * columns, columns)

    @pl.loop(0, length // block)
    def _(i):
        span = aligned(i * block, block)
        tables = cosine[span, :], -sine_next[span, :], -sine_last[span, :]
        parts = [
            rotary(dqt[:, span].T.astype(BF).astype(F32), *tables).astype(BF),
            rotary(dk[span, :].astype(BF).astype(F32), *tables).astype(BF),
            dv[span, :].astype(BF),
        ]
        for kind in range(3):
            dproj[kind, span, :] = parts[kind]
            row = slice(4 + kind, 5 + kind)
            terms[row, bias_cols] = terms[row, bias_cols] + jnp.sum(parts[kind].astype(F32), 0, keepdims=True)

    def qkv_term(k):
        cols = aligned(qkv_direct.owner(k) * depth, depth)
        left = n1[:, cols].T
        for kind in range(3):
            stage_qkv[k, kind] = dot(left, dproj[kind]).astype(BF)

    def produce(place, acc):
        span = aligned(place * pair, pair)

        @pl.loop(0, width // tile)
        def _(j):
            cols = aligned(j * tile, tile)
            total = dot_nt(dproj[0, span, :], wq[0, cols, :])
            for kind in range(1, 3):
                total = total + dot_nt(dproj[kind, span, :], wq[kind, cols, :])
            acc[:, cols] = total

    fold = Fold(net, acc, *buffers, *fold_sems)
    each = -(-(net.n_f - 1) // (net.n_l - 1))

    @pl.loop(0, net.n_l - 1)
    def _(j):
        fold.step(net.n_l - 1 - j, produce)

        @pl.loop(0, each)
        def _(i):
            k = 1 + j * each + i

            @pl.when(k < net.n_f)
            def _():
                qkv_term(k)
                qkv_direct.copy(k).start()

    fold.last(produce)

    def write_input(span, value):
        gin_o[span, :] = value + dmid[span, :]

    norm_backward(chunk, tok, acc, fold.mine, gains[0:1, :], terms, 0, write_input)
    PacketSum(net, *packet_scratch).run(terms, small_o, width // (net.n_f * net.n_s))
    qkv_term(0)
    qkv_direct.keep().start()
    fold.finish()
    out_direct.finish()
    qkv_direct.finish()


def back_part(dm, wo, att, q, k, kt, v, lse, n1, wq, tokens, dmid, gains, terms, tables):
    chunk, width = tokens.shape
    n_f, n_s = lax.axis_size("fsdp"), lax.axis_size("seq")
    length, columns = q.shape
    depth = width // n_f
    shape = jax.ShapeDtypeStruct
    direct = pltpu.SemaphoreType.DMA((2, n_f))
    return pl.pallas_call(
        back_kernel,
        name="back",
        out_shape=[
            shape((chunk, width), F32),
            shape((SMALL, 128), F32),
            shape((n_f, columns, depth), BF),
            shape((n_f, 3, depth, columns), BF),
        ],
        in_specs=[VMEM] * 17,
        out_specs=[VMEM] * 2 + [ANY] * 2,
        scratch_shapes=[
            pltpu.VMEM((length, columns), BF),
            pltpu.VMEM((length, columns), F32),
            pltpu.VMEM((length, columns), F32),
            pltpu.VMEM((columns, length), F32),
            pltpu.VMEM((3, length, columns), BF),
            pltpu.VMEM((n_f, columns, depth), BF),
            pltpu.VMEM((n_f, 3, depth, columns), BF),
            pltpu.VMEM((SMALL, width), F32),
            pltpu.VMEM((2 * chunk, width), F32),
            *Fold.buffers(n_s, chunk, width),
            *Fold.sems(n_s),
            *PacketSum.scratch(n_f, n_s),
            direct,
            direct,
        ],
        compiler_params=pltpu.CompilerParams(
            collective_id=3, has_side_effects=True, vmem_limit_bytes=62 * 2**20
        ),
        cost_estimate=pl.CostEstimate(
            flops=2 * length * columns * (8 * width + 5 * length),
            bytes_accessed=4 * length * width,
            transcendentals=length * length * columns // HEAD,
        ),
    )(dm, wo, att, q, k, kt, v, lse, n1, wq, tokens, dmid, gains, terms, *tables)


def per_device(
    tokens,
    gain_one,
    shift_one,
    w_qkv,
    b_qkv,
    w_out,
    gain_two,
    shift_two,
    w_gate,
    w_up,
    w_down,
    grad_output,
):
    length = tokens.shape[1] * lax.axis_size("seq")
    width = gain_one.shape[0]
    packet = jnp.concatenate(
        [jnp.stack([gain_one, shift_one, gain_two, shift_two]), b_qkv, jnp.zeros((1, width), BF)]
    )
    packet = jnp.pad(packet.astype(F32), ((0, 0), (0, 128 - width)))
    tables = rotary_tables(length)
    q, k, kt, v, att, lse, n1, gains, wq, wo = attend_part(
        tokens[0], packet, w_qkv.transpose(1, 0, 2), w_out, tables
    )
    dmid, top, terms, dm_rows, gate, up, down = middle_part(
        att, wo, tokens[0], gains, grad_output[0], w_gate, w_up, w_down
    )
    grad_input, small, out, qkv = back_part(
        dm_rows, wo, att, q, k, kt, v, lse, n1, wq, tokens[0], dmid, gains, terms, tables
    )

    def total(terms):
        return jnp.sum(terms.astype(F32), 0)

    return (
        top[None],
        grad_input[None],
        small[0, :width],
        small[1, :width],
        total(qkv).transpose(1, 0, 2),
        small[4:7, :width],
        total(out),
        small[2, :width],
        small[3, :width],
        total(gate),
        total(up),
        total(down),
    )


def solution(mesh):
    whole = P(("fsdp", "seq"))
    rows = P("fsdp", "seq", None)
    inner = P("seq", "fsdp")
    outer = P("fsdp", "seq")
    heads = P("fsdp", None, "seq")
    bias = P(None, ("fsdp", "seq"))
    return jax.shard_map(
        per_device,
        mesh=mesh,
        in_specs=(rows, whole, whole, heads, bias, inner, whole, whole, outer, outer, inner, rows),
        out_specs=(rows, rows, whole, whole, heads, bias, inner, whole, whole, outer, outer, inner),
        check_vma=False,
    )
```

```python
import functools

import jax
import jax.numpy as jnp
import numpy as np
from jax import lax
from jax.experimental import pallas as pl
from jax.experimental.pallas import tpu as pltpu
from jax.sharding import PartitionSpec as P

HEAD = 64
ROT = 16
EPSILON = 1e-05
NEG_LARGE = -1e30
MESH = pl.DeviceIdType.MESH
ANY = pl.BlockSpec(memory_space=pl.ANY)
VMEM = pl.BlockSpec(memory_space=pltpu.VMEM)
BF = jnp.bfloat16
F32 = jnp.float32
VMEM_BYTES = 62 * 2**20
SMALL = 8


def put(src, dst, send, recv, **device):
    return pltpu.make_async_remote_copy(
        src_ref=src, dst_ref=dst, send_sem=send, recv_sem=recv, device_id=device, device_id_type=MESH
    )


def dot(left, right):
    return jnp.dot(left, right, preferred_element_type=F32)


def dot_nt(left, right):
    return lax.dot_general(left, right, (((1,), (1,)), ((), ())), preferred_element_type=F32)


def dot_tn(left, right):
    return lax.dot_general(left, right, (((0,), (0,)), ((), ())), preferred_element_type=F32)


def aligned(start, size, unit=None):
    return pl.ds(pl.multiple_of(start, unit or size), size)


class Net:
    def __init__(self):
        self.n_f, self.n_s = lax.axis_size("fsdp"), lax.axis_size("seq")
        self.tall = 2 if self.n_f % 2 == 0 else 1
        self.wide = self.n_f // self.tall
        self.n_l = self.n_s // 2
        self.f, self.s = lax.axis_index("fsdp"), lax.axis_index("seq")
        self.a, self.b = self.f // self.wide, self.f % self.wide
        self.z, self.c = self.s // 2, self.s % 2
        self.mate = self.s + 1 - 2 * self.c

    def barrier(self):
        sem = pltpu.get_barrier_semaphore()
        for k in range(1, self.n_f):
            pl.semaphore_signal(
                sem, inc=1, device_id={"fsdp": (self.f + k) % self.n_f}, device_id_type=MESH
            )
        for k in range(1, self.n_s):
            pl.semaphore_signal(
                sem, inc=1, device_id={"seq": (self.s + k) % self.n_s}, device_id_type=MESH
            )
        pl.semaphore_wait(sem, self.n_f + self.n_s - 2)

    def sides(self, hop, act):
        @pl.loop(0, 2)
        def _(side):
            other = self.z + (2 * side - 1) * hop

            @pl.when((other >= 0) & (other < self.n_l))
            def _():
                act(other, side)


class Spread:
    def __init__(self, net, src, part, sems):
        self.net, self.src, self.part, self.sems = net, src, part, sems
        self.rows = [j for j in range(1, net.wide)]
        self.cols = [i for i in range(1, net.tall)]

    @staticmethod
    def count(n_f):
        tall = 2 if n_f % 2 == 0 else 1
        wide = n_f // tall
        return 1 + 2 * (wide - 1) + 2 * (tall - 1) + 4 * (wide - 1) * (tall - 1)

    def at(self, kind, i, j):
        w, t = len(self.rows), len(self.cols)
        base = {
            "own": 0,
            "row": 1,
            "col": 1 + 2 * w,
            "half0": 1 + 2 * w + 2 * t,
            "half1": 1 + 2 * w + 2 * t + 2 * w * t,
        }[kind]
        if kind == "own":
            return self.sems.at[0]
        k = j - 1 if kind == "row" else i - 1 if kind == "col" else (i - 1) * w + j - 1
        return self.sems.at[base + 2 * k], self.sems.at[base + 2 * k + 1]

    def rank(self, i, j):
        net = self.net
        return ((net.a + i) % net.tall) * net.wide + (net.b + j) % net.wide

    def back(self, i, j):
        net = self.net
        return ((net.a - i + net.tall) % net.tall) * net.wide + (net.b - j + net.wide) % net.wide

    def own(self):
        return pltpu.make_async_copy(self.src, self.part(self.net.f, None), self.at("own", 0, 0))

    def first(self, i, j):
        send, recv = self.at("row" if i == 0 else "col", i, j)
        return put(self.src, self.part(self.net.f, None), send, recv, fsdp=self.rank(i, j))

    def came(self, i, j):
        send, recv = self.at("row" if i == 0 else "col", i, j)
        place = self.part(self.back(i, j), None)
        return put(place, place, send, recv, fsdp=self.rank(i, j))

    def second(self, half, i, j, came=False):
        send, recv = self.at("half0" if half == 0 else "half1", i, j)
        origin = self.back(i, j) if came else self.back(0, j) if half == 0 else self.back(i, 0)
        place = self.part(origin, half)
        return put(place, place, send, recv, fsdp=self.rank(i, 0) if half == 0 else self.rank(0, j))

    def start(self):
        self.own().start()
        for i in self.cols:
            self.first(i, 0).start()
        for j in self.rows:
            self.first(0, j).start()

    def relay(self):
        for j in self.rows:
            self.came(0, j).wait_recv()
            for i in self.cols:
                self.second(0, i, j).start()
        for i in self.cols:
            self.came(i, 0).wait_recv()
            for j in self.rows:
                self.second(1, i, j).start()

    def finish(self):
        self.own().wait()
        for j in self.rows:
            self.first(0, j).wait_send()
        for i in self.cols:
            self.first(i, 0).wait_send()
        for i in self.cols:
            for j in self.rows:
                for half in range(2):
                    self.second(half, i, j, came=True).wait_recv()
                    self.second(half, i, j).wait_send()


class Line:
    def __init__(self, net, src, part, recv, send):
        self.net, self.src, self.part, self.recv, self.send = net, src, part, recv, send

    @staticmethod
    def sems(n_s):
        return [pltpu.SemaphoreType.DMA((n_s,)), pltpu.SemaphoreType.DMA((4, n_s // 2))]

    def own(self):
        net = self.net
        return pltpu.make_async_copy(self.src, self.part(net.s), self.recv.at[net.s])

    def on_line(self, src, chunk, side, hop):
        net = self.net
        return put(
            src,
            self.part(chunk),
            self.send.at[side, hop],
            self.recv.at[chunk],
            seq=net.s + 2 - 4 * side,
        )

    def to_mate(self, src, chunk, side, hop):
        return put(src, self.part(chunk), self.send.at[2 + side, hop], self.recv.at[chunk], seq=self.net.mate)

    def goes_on(self, side):
        after = self.net.z + 1 - 2 * side
        return (after >= 0) & (after < self.net.n_l)

    def start(self):
        net = self.net
        self.own().start()
        for side in range(2):

            @pl.when(self.goes_on(side))
            def _():
                self.on_line(self.src, net.s, side, 0).start()

        self.to_mate(self.src, net.s, 0, 0).start()

    def arrive(self, chunk):
        place = self.part(chunk)
        put(place, place, self.send.at[0, 0], self.recv.at[chunk], seq=self.net.mate).wait_recv()

    def step(self, hop):
        net = self.net

        def act(other, side):
            chunk = 2 * other + net.c
            self.arrive(chunk)

            @pl.when(self.goes_on(side))
            def _():
                self.on_line(self.part(chunk), chunk, side, hop).start()

            self.to_mate(self.part(chunk), chunk, side, hop).start()

        net.sides(hop, act)

    def pair(self, other):
        self.arrive(2 * other + 1 - self.net.c)

    def finish(self):
        net = self.net
        for side in range(2):

            @pl.when(self.goes_on(side))
            def _():
                self.on_line(self.src, net.s, side, 0).wait_send()

        self.to_mate(self.src, net.s, 0, 0).wait_send()

        @pl.loop(1, net.n_l)
        def _(hop):
            def act(other, side):
                chunk = 2 * other + net.c

                @pl.when(self.goes_on(side))
                def _():
                    self.on_line(self.part(chunk), chunk, side, hop).wait_send()

                self.to_mate(self.part(chunk), chunk, side, hop).wait_send()

            net.sides(hop, act)


class Packets:
    def __init__(self, net, src, buf, sems):
        self.net, self.src, self.buf, self.sems = net, src, buf, sems

    @staticmethod
    def count(n_f, n_s):
        return 1 + 2 * (n_f - 1) + 2 * (n_s - 1)

    def own(self):
        net = self.net
        return pltpu.make_async_copy(self.src, self.buf.at[net.s, net.f], self.sems.at[0])

    def one(self, k, came=False):
        net = self.net
        f = (net.f - k + net.n_f) % net.n_f if came else net.f
        place = self.buf.at[net.s, f]
        return put(
            place if came else self.src,
            place,
            self.sems.at[2 * k - 1],
            self.sems.at[2 * k],
            fsdp=(net.f + k) % net.n_f,
        )

    def two(self, k, came=False):
        net = self.net
        place = self.buf.at[(net.s - k + net.n_s) % net.n_s if came else net.s]
        at = 2 * (net.n_f - 1) + 2 * k - 1
        return put(place, place, self.sems.at[at], self.sems.at[at + 1], seq=(net.s + k) % net.n_s)

    def start(self):
        self.own().start()
        for k in range(1, self.net.n_f):
            self.one(k).start()

    def middle(self):
        self.own().wait()
        for k in range(1, self.net.n_f):
            self.one(k, came=True).wait_recv()
            self.one(k).wait_send()
        for k in range(1, self.net.n_s):
            self.two(k).start()

    def finish(self):
        for k in range(1, self.net.n_s):
            self.two(k, came=True).wait_recv()
            self.two(k).wait_send()

    def unpack(self, out, width):
        net = self.net
        per = 128 // width
        for tile in range(net.n_f * net.n_s // per):
            total = None
            for j in range(per):
                f, s = divmod(tile * per + j, net.n_s)
                piece = self.buf[s, f]
                if j:
                    piece = pltpu.roll(piece, j * width, axis=1)
                total = piece if total is None else total + piece
            out[:, tile * 128 : (tile + 1) * 128] = total


def rotary(values, cosine, sine_next, sine_last):
    columns = values.shape[1]
    half = ROT // 2
    times = columns // 128

    def wide(table):
        return table if times == 1 else jnp.concatenate([table] * times, axis=1)

    following = pltpu.roll(values, columns - half, axis=1)
    previous = pltpu.roll(values, half, axis=1)
    return values * wide(cosine) + following * wide(sine_next) + previous * wide(sine_last)


def rotary_tables(length):
    half = ROT // 2
    freqs = np.float32(10000.0) ** (-np.arange(half, dtype=np.float32) * np.float32(2.0 / ROT))
    angles = np.arange(length, dtype=np.float32)[:, None] * freqs[None, :].astype(np.float32)
    cosine, sine = np.cos(angles), np.sin(angles)
    rest = np.zeros((length, HEAD - ROT), np.float32)
    none = np.zeros_like(sine)
    keep = np.concatenate([cosine, cosine, rest + 1], 1)
    following = np.concatenate([-sine, none, rest], 1)
    previous = np.concatenate([none, sine, rest], 1)
    return [np.tile(t, (1, 128 // HEAD)).astype(np.float32) for t in (keep, following, previous)]


def normalize(values):
    center = values - jnp.mean(values, -1, keepdims=True)
    inverse = lax.rsqrt(jnp.mean(center * center, -1, keepdims=True) + EPSILON)
    return center * inverse, inverse


class Copies:
    def __init__(self, sems):
        self.sems, self.all, self.open = sems, [], []

    def start(self, src, dst):
        copy = pltpu.make_async_copy(src, dst, self.sems.at[len(self.all)])
        copy.start()
        self.all.append(copy)
        self.open.append(copy)
        return copy

    def wait(self, *copies):
        for copy in copies or list(self.open):
            copy.wait()
            self.open.remove(copy)


def columns_of(ref, depth):
    half_rows = ref.shape[0] // 2

    def part(f, half):
        span = aligned(f * depth, depth)
        if half is None:
            return ref.at[:, span]
        return ref.at[pl.ds(half * half_rows, half_rows), span]

    return part


def rows_of(ref, chunk):
    return lambda s: ref.at[aligned(s * chunk, chunk)]


class Fold:
    def __init__(self, net, acc, mate_in, coming, mate_out, out, mate_send, mate_recv, send, recv):
        self.net, self.acc = net, acc
        self.mate_in, self.coming, self.mate_out, self.out = mate_in, coming, mate_out, out
        self.mate_send, self.mate_recv, self.send, self.recv = mate_send, mate_recv, send, recv
        self.chunk = acc.shape[0] // 2

    @staticmethod
    def buffers(n_s, chunk, width):
        n_l = n_s // 2
        return [
            pltpu.VMEM((n_l, chunk, width), BF),
            pltpu.VMEM((n_l + 1, chunk, width), BF),
            pltpu.VMEM((2, chunk, width), BF),
            pltpu.VMEM((2, 2, chunk, width), BF),
        ]

    @staticmethod
    def sems(n_s):
        n_l = n_s // 2
        return [
            pltpu.SemaphoreType.DMA((2,)),
            pltpu.SemaphoreType.DMA((n_l,)),
            pltpu.SemaphoreType.DMA((2, 2)),
            pltpu.SemaphoreType.DMA((n_l + 1,)),
        ]

    def mine(self, i):
        return aligned(self.net.c * self.chunk + i * 32, 32)

    def place(self, other):
        return (other >= 0) & (other < self.net.n_l)

    def to_mate(self, target, side):
        return put(
            self.mate_out.at[side],
            self.mate_in.at[target],
            self.mate_send.at[side],
            self.mate_recv.at[target],
            seq=self.net.mate,
        )

    def onward(self, target, side, hop):
        last = (1 - side) * (1 // hop)
        slot = target + (self.net.n_l - target) * last
        return put(
            self.out.at[side, hop % 2],
            self.coming.at[slot],
            self.send.at[side, hop % 2],
            self.recv.at[slot],
            seq=self.net.s + 4 * side - 2,
        )

    def came(self, slot):
        place = self.coming.at[slot]
        put(place, place, self.send.at[0, 0], self.recv.at[slot], seq=self.net.mate).wait_recv()

    def swap(self, target, side):
        count = self.chunk // 32

        @pl.loop(0, count)
        def _(i):
            theirs = aligned((1 - self.net.c) * self.chunk + i * 32, 32)
            self.mate_out[side, aligned(i * 32, 32), :] = self.acc[theirs, :].astype(BF)

        self.to_mate(target, side).start()

    def swapped(self, target, side):
        self.to_mate(target, side).wait_recv()

    def add(self, ref, at):
        @pl.loop(0, self.chunk // 32)
        def _(i):
            span = self.mine(i)
            self.acc[span, :] = self.acc[span, :] + ref[at, aligned(i * 32, 32), :].astype(F32)

    def step(self, hop, produce):
        net = self.net

        def act(target, side):
            produce(target, self.acc)
            further = target + 2 * side - 1

            @pl.when(self.place(further))
            def _():
                self.to_mate(further, side).wait_send()

            self.swap(target, side)
            self.swapped(target, side)
            self.add(self.mate_in, target)

            @pl.when(self.place(net.z + 1 - 2 * side))
            def _():
                self.came(target)
                self.add(self.coming, target)

            @pl.when(self.place(further + 2 * side - 1))
            def _():
                self.onward(target, side, hop + 2).wait_send()

            @pl.loop(0, self.chunk // 32)
            def _(i):
                self.out[side, hop % 2, aligned(i * 32, 32), :] = self.acc[self.mine(i), :].astype(BF)

            self.onward(target, side, hop).start()

        net.sides(hop, act)

    def last(self, produce):
        net = self.net

        @pl.when(net.z > 0)
        def _():
            self.to_mate(net.z - 1, 0).wait_send()

        produce(net.z, self.acc)
        self.swap(net.z, 0)
        self.swapped(net.z, 0)
        self.add(self.mate_in, net.z)

        @pl.when(net.z > 0)
        def _():
            self.came(net.z)
            self.add(self.coming, net.z)

        @pl.when(net.z < net.n_l - 1)
        def _():
            self.came(net.n_l)
            self.add(self.coming, net.n_l)

    def finish(self):
        net = self.net
        self.to_mate(net.z, 0).wait_send()

        @pl.when(net.z < net.n_l - 1)
        def _():
            self.to_mate(net.z + 1, 1).wait_send()

        @pl.loop(1, min(3, net.n_l))
        def _(hop):
            net.sides(hop, lambda target, side: self.onward(target, side, hop).wait_send())


class Direct:
    def __init__(self, net, stage, recv, sems):
        self.net, self.stage, self.recv, self.sems = net, stage, recv, sems

    def owner(self, k):
        return (self.net.f + k) % self.net.n_f

    def copy(self, k):
        return put(
            self.stage.at[k],
            self.recv.at[self.net.f],
            self.sems.at[0, k],
            self.sems.at[1, k],
            fsdp=self.owner(k),
        )

    def keep(self):
        return pltpu.make_async_copy(self.stage.at[0], self.recv.at[self.net.f], self.sems.at[0, 0])

    def finish(self):
        self.keep().wait()

        @pl.loop(1, self.net.n_f)
        def _(k):
            place = self.recv.at[(self.net.f - k + self.net.n_f) % self.net.n_f]
            put(place, place, self.sems.at[0, k], self.sems.at[1, k], fsdp=self.owner(k)).wait_recv()
            self.copy(k).wait_send()


class PacketSum:
    def __init__(self, net, out, seq_in, total, fsdp_in, sems):
        self.net, self.out, self.seq_in, self.total, self.fsdp_in, self.sems = net, out, seq_in, total, fsdp_in, sems

    @staticmethod
    def scratch(n_f, n_s):
        return [
            pltpu.VMEM((n_s, n_f, SMALL, 128), F32),
            pltpu.VMEM((n_s, n_f, SMALL, 128), F32),
            pltpu.VMEM((n_f, SMALL, 128), F32),
            pltpu.VMEM((n_f, SMALL, 128), F32),
            pltpu.SemaphoreType.DMA((2 * (n_f + n_s),)),
        ]

    def one(self, k):
        to = (self.net.s + k) % self.net.n_s
        return put(self.out.at[to], self.seq_in.at[k], self.sems.at[2 * k], self.sems.at[2 * k + 1], seq=to)

    def two(self, k):
        to = (self.net.f + k) % self.net.n_f
        at = 2 * (self.net.n_s + k)
        return put(self.total.at[to], self.fsdp_in.at[k], self.sems.at[at], self.sems.at[at + 1], fsdp=to)

    def run(self, terms, result, width):
        net = self.net
        per = 128 // width
        for tile in range(net.n_f * net.n_s // per):
            value = terms[:, tile * 128 : (tile + 1) * 128]
            for j in range(per):
                f, s = divmod(tile * per + j, net.n_s)
                self.out[s, f] = pltpu.roll(value, 128 - j * width, axis=1) if j else value
        for k in range(1, net.n_s):
            self.one(k).start()
        total = self.out[net.s]
        for k in range(1, net.n_s):
            self.one(k).wait()
            total = total + self.seq_in[k]
        self.total[...] = total
        for k in range(1, net.n_f):
            self.two(k).start()
        total = self.total[net.f]
        for k in range(1, net.n_f):
            self.two(k).wait()
            total = total + self.fsdp_in[k]
        result[...] = total


def norm_backward(rows, source, grad, grad_rows, gain, terms, at, write):
    terms[at : at + 2, :] = jnp.zeros((2, terms.shape[1]), F32)

    @pl.loop(0, rows // 32)
    def _(i):
        span = aligned(i * 32, 32)
        scaled, inverse = normalize(source[span, :].astype(F32))
        value = grad[grad_rows(i), :]
        upstream = value * gain
        inner = jnp.mean(upstream, -1, keepdims=True)
        cross = jnp.mean(upstream * scaled, -1, keepdims=True)
        terms[at : at + 1, :] = terms[at : at + 1, :] + jnp.sum(value * scaled, 0, keepdims=True)
        terms[at + 1 : at + 2, :] = terms[at + 1 : at + 2, :] + jnp.sum(value, 0, keepdims=True)
        write(span, inverse * (upstream - inner - scaled * cross))


def forward_kernel(
    tok,
    packet,
    wq_own,
    wo_own,
    wg_own,
    wu_own,
    wd_own,
    gout_own,
    cosine,
    sine_next,
    sine_last,
    q_o,
    k_o,
    kt_o,
    v_o,
    att_o,
    lse_o,
    n1_o,
    gains_o,
    wq_o,
    wo_o,
    wg_o,
    wu_o,
    wd_o,
    gout_o,
    n2_o,
    hidden_o,
    dgate_o,
    dup_o,
    mid_o,
    rows,
    n1,
    gout,
    wq,
    wo,
    wg,
    wu,
    wd,
    q,
    k,
    kt,
    v,
    vt,
    ot,
    att,
    hidden,
    dgate,
    dup,
    mid,
    tok_in,
    n2_own,
    packets,
    acc,
    *rest,
):
    net = Net()
    chunk, width = tok.shape
    length = chunk * net.n_s
    depth = wq_own.shape[1]
    columns = wq_own.shape[2]
    heads = columns // HEAD
    pair = 2 * chunk
    block = 256
    tile = 512
    buffers, rest = rest[:4], rest[4:]
    fold_sems, rest = rest[:4], rest[4:]
    tok_sems, rest = rest[:2], rest[2:]
    gout_sems, rest = rest[:2], rest[2:]
    n2_sems, rest = rest[:2], rest[2:]
    spread_sems, rest = rest[:5], rest[5:]
    pk_sems, copy_sems = rest
    copies = Copies(copy_sems)

    tok_copy = copies.start(tok, tok_in)
    net.barrier()

    def wq_part(f, half):
        if half is None:
            return wq.at[:, aligned(f * depth, depth), :]
        return wq.at[:, aligned(f * depth + half * (depth // 2), depth // 2), :]

    spread_q = Spread(net, wq_own, wq_part, spread_sems[0])
    spread_o, spread_g, spread_u, spread_d = [
        Spread(net, own, columns_of(full, depth), sems)
        for own, full, sems in zip((wo_own, wg_own, wu_own, wd_own), (wo, wg, wu, wd), spread_sems[1:])
    ]
    pk = Packets(net, packet, packets, pk_sems)
    line = Line(net, tok, rows_of(rows, chunk), *tok_sems)
    gout_line = Line(net, gout_own, rows_of(gout, chunk), *gout_sems)
    n2_line = Line(net, n2_own, rows_of(rows, chunk), *n2_sems)
    fold = Fold(net, acc, *buffers, *fold_sems)

    pk.start()
    line.start()
    spread_q.start()
    pk.middle()
    pk.finish()
    pk.unpack(gains_o, width // (net.n_f * net.n_s))

    def norm_block(other):
        gain, shift = gains_o[0:1, :], gains_o[1:2, :]

        @pl.loop(0, pair // 32)
        def _(i):
            span = aligned(other * pair + i * 32, 32)
            scaled, _ = normalize(rows[span, :].astype(F32))
            n1[span, :] = (scaled * gain + shift).astype(BF)

    def project_block(other):
        span = aligned(other * pair, pair)
        left = n1[span, :]
        cols = aligned(net.s * columns, columns)
        tables = cosine[span, :], sine_next[span, :], sine_last[span, :]
        for kind in range(3):
            value = dot(left, wq[kind]) + gains_o[4 + kind : 5 + kind, cols]
            if kind == 0:
                q[span, :] = rotary(value, *tables).astype(BF)
            elif kind == 1:
                value = rotary(value, *tables)
                k[span, :] = value.astype(BF)
                kt[:, span] = value.T.astype(BF)
            else:
                v[span, :] = value.astype(BF)
                vt[:, span] = value.T.astype(BF)

    line.arrive(net.s)
    line.pair(net.z)
    norm_block(net.z)

    def hop_norm(hop):
        line.step(hop)

        def act(other, side):
            line.pair(other)
            norm_block(other)

        net.sides(hop, act)

    for hop in range(1, net.n_l - 1):
        hop_norm(hop)
        if hop == 1:
            spread_o.start()
            spread_g.start()
            spread_q.relay()
    spread_q.finish()

    @pl.loop(0, net.n_l - 1)
    def _(hop):
        def act(other, side):
            @pl.when((hop > 0) | (side == 0))
            def _():
                project_block(other)

        net.sides(hop, act)

    spread_u.start()
    spread_o.relay()
    hop_norm(net.n_l - 1)
    gout_line.start()
    net.sides(net.n_l - 1, lambda other, side: project_block(other))
    for pair_of in ((n1, n1_o), (wq, wq_o), (q, q_o), (k, k_o), (kt, kt_o), (v, v_o)):
        copies.start(*pair_of)

    @pl.loop(0, heads)
    def _(head):
        lane = lax.broadcasted_iota(jnp.int32, (1, columns), 1)
        here = jnp.where(lane // HEAD == head, HEAD**-0.5, 0.0).astype(BF)
        visible = lax.broadcasted_iota(jnp.int32, (block, block), 0) <= lax.broadcasted_iota(
            jnp.int32, (block, block), 1
        )
        head_rows = aligned(head * HEAD, HEAD)
        for i in range(length // block):
            lo, hi = i * block, (i + 1) * block
            query = q[lo:hi, :] * here
            near = jnp.where(visible, dot_nt(k[lo:hi, :], query), NEG_LARGE)
            highest = jnp.max(near, 0, keepdims=True)
            if i:
                far = dot_nt(k[0:lo, :], query)
                highest = jnp.maximum(highest, jnp.max(far, 0, keepdims=True))
            near = jnp.exp(near - highest)
            total = jnp.sum(near, 0, keepdims=True)
            out = dot(vt[head_rows, lo:hi], near.astype(BF))
            if i:
                far = jnp.exp(far - highest)
                total = total + jnp.sum(far, 0, keepdims=True)
                out = out + dot(vt[head_rows, 0:lo], far.astype(BF))
            ot[head_rows, lo:hi] = out / total
            lse_o[pl.ds(head, 1), lo:hi] = highest + jnp.log(total)

    for i in range(length // block):
        att[i * block : (i + 1) * block, :] = ot[:, i * block : (i + 1) * block].T.astype(BF)

    spread_o.finish()
    spread_g.relay()
    spread_d.start()
    line.finish()
    copies.start(att, att_o)
    copies.start(wo, wo_o)

    def produce_attended(place, acc):
        left = att[aligned(place * pair, pair), :]

        @pl.loop(0, width // tile)
        def _(j):
            cols = aligned(j * tile, tile)
            acc[:, cols] = dot(left, wo[:, cols])

    for j in range(net.n_l - 1):
        fold.step(net.n_l - 1 - j, produce_attended)
        gout_line.step(j + 1)
        if j == 0:
            spread_u.relay()

    fold.last(produce_attended)
    copies.wait(tok_copy)
    gain_two, shift_two = gains_o[2:3, :], gains_o[3:4, :]

    @pl.loop(0, chunk // 32)
    def _(i):
        span = aligned(i * 32, 32)
        value = tok_in[span, :].astype(F32) + acc[fold.mine(i), :]
        mid[span, :] = value
        scaled, _ = normalize(value)
        n2_own[span, :] = (scaled * gain_two + shift_two).astype(BF)

    n2_line.start()
    spread_d.relay()
    fold.finish()
    copies.start(mid, mid_o)
    gout_line.arrive(net.s)
    gout_line.pair(net.z)

    @pl.loop(1, net.n_l)
    def _(hop):
        net.sides(hop, lambda other, side: gout_line.pair(other))

    copies.start(gout, gout_o)

    def forward_block(other):
        span = aligned(other * pair, pair)
        right = rows[span, :]
        gate = dot_nt(wg[...], right)
        up = dot_nt(wu[...], right)
        back = dot_nt(wd[...], gout[span, :])
        sigma = jax.nn.sigmoid(gate)
        active = gate * sigma
        hidden[:, span] = (active * up).astype(BF)
        dgate[:, span] = (back * up * (sigma * (1.0 + gate * (1.0 - sigma)))).astype(BF)
        dup[:, span] = (back * active).astype(BF)

    n2_line.arrive(net.s)
    n2_line.pair(net.z)

    @pl.loop(1, net.n_l - 1)
    def _(hop):
        n2_line.step(hop)
        net.sides(hop, lambda other, side: n2_line.pair(other))

    for spread in (spread_g, spread_u, spread_d):
        spread.finish()
    for pair_of in ((wg, wg_o), (wu, wu_o), (wd, wd_o)):
        copies.start(*pair_of)

    @pl.loop(0, net.n_l - 1)
    def _(hop):
        def act(other, side):
            @pl.when((hop > 0) | (side == 0))
            def _():
                forward_block(other)

        net.sides(hop, act)

    n2_line.step(net.n_l - 1)

    def last_block(other, side):
        n2_line.pair(other)
        forward_block(other)

    net.sides(net.n_l - 1, last_block)
    for pair_of in ((dgate, dgate_o), (dup, dup_o), (hidden, hidden_o), (rows, n2_o)):
        copies.start(*pair_of)
    gout_line.finish()
    n2_line.finish()
    copies.wait()


def forward_part(tokens, packet, wq, wo, wg, wu, wd, gout, tables):
    chunk, width = tokens.shape
    n_f, n_s = lax.axis_size("fsdp"), lax.axis_size("seq")
    length = chunk * n_s
    columns = wq.shape[2]
    units = wg.shape[0]
    shape = jax.ShapeDtypeStruct
    wide, head, turned = (length, width), (length, columns), (units, length)
    return pl.pallas_call(
        forward_kernel,
        name="forward",
        out_shape=[
            shape(head, BF),
            shape(head, BF),
            shape((columns, length), BF),
            shape(head, BF),
            shape(head, BF),
            shape((8, length), F32),
            shape(wide, BF),
            shape((SMALL, width), F32),
            shape((3, width, columns), BF),
            shape((columns, width), BF),
            *[shape((units, width), BF)] * 3,
            shape(wide, BF),
            shape(wide, BF),
            *[shape(turned, BF)] * 3,
            shape((chunk, width), F32),
        ],
        in_specs=[ANY, VMEM, *[ANY] * 6, VMEM, VMEM, VMEM],
        out_specs=[*[ANY] * 5, VMEM, ANY, VMEM, *[ANY] * 11],
        scratch_shapes=[
            pltpu.VMEM(wide, BF),
            pltpu.VMEM(wide, BF),
            pltpu.VMEM(wide, BF),
            pltpu.VMEM((3, width, columns), BF),
            pltpu.VMEM((columns, width), BF),
            *[pltpu.VMEM((units, width), BF)] * 3,
            pltpu.VMEM(head, BF),
            pltpu.VMEM(head, BF),
            pltpu.VMEM((columns, length), BF),
            pltpu.VMEM(head, BF),
            pltpu.VMEM((columns, length), BF),
            pltpu.VMEM((columns, length), F32),
            pltpu.VMEM(head, BF),
            *[pltpu.VMEM(turned, BF)] * 3,
            pltpu.VMEM((chunk, width), F32),
            pltpu.VMEM((chunk, width), BF),
            pltpu.VMEM((chunk, width), BF),
            pltpu.VMEM((n_s, n_f, SMALL, 128), F32),
            pltpu.VMEM((2 * chunk, width), F32),
            *Fold.buffers(n_s, chunk, width),
            *Fold.sems(n_s),
            *Line.sems(n_s),
            *Line.sems(n_s),
            *Line.sems(n_s),
            *[pltpu.SemaphoreType.DMA((Spread.count(n_f),))] * 5,
            pltpu.SemaphoreType.DMA((Packets.count(n_f, n_s),)),
            pltpu.SemaphoreType.DMA((20,)),
        ],
        compiler_params=pltpu.CompilerParams(
            collective_id=1, has_side_effects=True, vmem_limit_bytes=VMEM_BYTES
        ),
        cost_estimate=pl.CostEstimate(
            flops=2 * length * width * (4 * columns + 3 * units),
            bytes_accessed=8 * length * width,
            transcendentals=length * (length * columns // HEAD + units),
        ),
    )(tokens, packet, wq, wo, wg, wu, wd, gout, *tables)


def middle_kernel(
    dgate_in,
    dup_in,
    wg_in,
    wu_in,
    n2_in,
    hidden_in,
    gout_in,
    wd_in,
    mid,
    gains,
    gout_own,
    dmid_o,
    top_o,
    terms_o,
    dm_o,
    gate_o,
    up_o,
    down_o,
    dgate,
    dup,
    wg,
    wu,
    n2,
    hidden,
    gout,
    wd,
    dmid_low,
    stage_gate,
    stage_up,
    stage_down,
    acc,
    *rest,
):
    net = Net()
    chunk, width = mid.shape
    pair = 2 * chunk
    depth = width // net.n_f
    tile = 512
    first_buffers, rest = rest[:4], rest[4:]
    last_buffers, rest = rest[:4], rest[4:]
    first_sems, rest = rest[:4], rest[4:]
    last_sems, rest = rest[:4], rest[4:]
    dm_sems, rest = rest[:2], rest[2:]
    gate_sems, up_sems, down_sems, copy_sems = rest

    copies = Copies(copy_sems)
    loads = [
        copies.start(src, dst)
        for src, dst in (
            (dgate_in, dgate),
            (dup_in, dup),
            (wg_in, wg),
            (wu_in, wu),
            (n2_in, n2),
            (hidden_in, hidden),
            (gout_in, gout),
            (wd_in, wd),
        )
    ]
    net.barrier()
    dm_line = Line(net, dmid_low, rows_of(dm_o, chunk), *dm_sems)
    fold = Fold(net, acc, *first_buffers, *first_sems)
    last = Fold(net, acc, *last_buffers, *last_sems)
    gate_direct = Direct(net, stage_gate, gate_o, gate_sems)
    up_direct = Direct(net, stage_up, up_o, up_sems)
    down_direct = Direct(net, stage_down, down_o, down_sems)
    directs = (down_direct, gate_direct, up_direct)

    def weight_terms(k):
        cols = aligned(gate_direct.owner(k) * depth, depth)
        stage_down[k] = dot(hidden[...], gout[:, cols]).astype(BF)
        right = n2[:, cols]
        stage_gate[k] = dot(dgate[...], right).astype(BF)
        stage_up[k] = dot(dup[...], right).astype(BF)

    def produce_normed(place, acc):
        span = aligned(place * pair, pair)
        left, right = dgate[:, span].T, dup[:, span].T

        @pl.loop(0, width // tile)
        def _(j):
            cols = aligned(j * tile, tile)
            acc[:, cols] = dot(left, wg[:, cols]) + dot(right, wu[:, cols])

    copies.wait(*loads[:4])
    each = -(-(net.n_f - 1) // (net.n_l - 1))
    for j in range(net.n_l - 1):
        fold.step(net.n_l - 1 - j, produce_normed)
        if j == 0:
            copies.wait(*loads[4:])

        @pl.loop(1 + j * each, min(1 + (j + 1) * each, net.n_f))
        def _(k):
            weight_terms(k)
            for direct in directs:
                direct.copy(k).start()

    fold.last(produce_normed)

    def write_middle(span, value):
        value = value + gout_own[span, :].astype(F32)
        dmid_o[span, :] = value
        dmid_low[span, :] = value.astype(BF)

    terms_o[...] = jnp.zeros(terms_o.shape, F32)
    norm_backward(chunk, mid, acc, fold.mine, gains[2:3, :], terms_o, 2, write_middle)
    dm_line.start()
    fold.finish()

    def produce_top(place, acc):
        left = hidden[:, aligned(place * pair, pair)].T

        @pl.loop(0, width // tile)
        def _(j):
            cols = aligned(j * tile, tile)
            acc[:, cols] = dot(left, wd[:, cols])

    @pl.loop(0, net.n_l - 1)
    def _(j):
        last.step(net.n_l - 1 - j, produce_top)
        dm_line.step(j + 1)

    last.last(produce_top)

    @pl.loop(0, chunk // 32)
    def _(i):
        span = aligned(i * 32, 32)
        top_o[span, :] = (mid[span, :] + acc[last.mine(i), :]).astype(BF)

    weight_terms(0)
    for direct in directs:
        direct.keep().start()

    last.finish()
    dm_line.arrive(net.s)
    dm_line.pair(net.z)

    @pl.loop(1, net.n_l)
    def _(hop):
        net.sides(hop, lambda other, side: dm_line.pair(other))

    dm_line.finish()
    for direct in directs:
        direct.finish()


def middle_part(dgate, dup, wg, wu, n2, hidden, gout_rows, wd, mid, gains, gout):
    chunk, width = mid.shape
    n_f, n_s = lax.axis_size("fsdp"), lax.axis_size("seq")
    length = chunk * n_s
    units = wg.shape[0]
    depth = width // n_f
    shape = jax.ShapeDtypeStruct
    buffers = Fold.buffers(n_s, chunk, width)
    direct = pltpu.SemaphoreType.DMA((2, n_f))
    wide, turned, weight, terms = (length, width), (units, length), (units, width), (n_f, units, depth)
    return pl.pallas_call(
        middle_kernel,
        name="middle",
        out_shape=[
            shape((chunk, width), F32),
            shape((chunk, width), BF),
            shape((SMALL, width), F32),
            shape(wide, BF),
            *[shape(terms, BF)] * 3,
        ],
        in_specs=[ANY] * 8 + [VMEM] * 3,
        out_specs=[VMEM] * 3 + [ANY] * 4,
        scratch_shapes=[
            pltpu.VMEM(turned, BF),
            pltpu.VMEM(turned, BF),
            pltpu.VMEM(weight, BF),
            pltpu.VMEM(weight, BF),
            pltpu.VMEM(wide, BF),
            pltpu.VMEM(turned, BF),
            pltpu.VMEM(wide, BF),
            pltpu.VMEM(weight, BF),
            pltpu.VMEM((chunk, width), BF),
            *[pltpu.VMEM(terms, BF)] * 3,
            pltpu.VMEM((2 * chunk, width), F32),
            *buffers,
            *buffers,
            *Fold.sems(n_s),
            *Fold.sems(n_s),
            *Line.sems(n_s),
            *[direct] * 3,
            pltpu.SemaphoreType.DMA((8,)),
        ],
        compiler_params=pltpu.CompilerParams(
            collective_id=2, has_side_effects=True, vmem_limit_bytes=VMEM_BYTES
        ),
        cost_estimate=pl.CostEstimate(
            flops=2 * length * width * units * 6, bytes_accessed=8 * length * width, transcendentals=0
        ),
    )(dgate, dup, wg, wu, n2, hidden, gout_rows, wd, mid, gains, gout)


def back_kernel(
    dm_in,
    wo_in,
    att_in,
    q_in,
    k_in,
    kt_in,
    v_in,
    n1_in,
    wq_in,
    lse,
    tok,
    dmid,
    gains,
    terms_in,
    cosine,
    sine_next,
    sine_last,
    gin_o,
    small_o,
    out_o,
    qkv_o,
    dm,
    wo,
    att,
    q,
    k,
    kt,
    v,
    n1,
    wq,
    datt,
    dk,
    dv,
    dqt,
    dproj,
    stage_out,
    stage_qkv,
    terms,
    acc,
    *rest,
):
    net = Net()
    chunk, width = tok.shape
    length, columns = q_in.shape
    heads = columns // HEAD
    pair = 2 * chunk
    depth = width // net.n_f
    block = 256
    tile = 512
    buffers, rest = rest[:4], rest[4:]
    fold_sems, rest = rest[:4], rest[4:]
    packet_scratch, rest = rest[:5], rest[5:]
    out_sems, qkv_sems, copy_sems = rest

    copies = Copies(copy_sems)
    loads = [
        copies.start(src, dst)
        for src, dst in (
            (dm_in, dm),
            (wo_in, wo),
            (att_in, att),
            (q_in, q),
            (k_in, k),
            (kt_in, kt),
            (v_in, v),
            (n1_in, n1),
            (wq_in, wq),
        )
    ]
    net.barrier()
    copies.wait(*loads[:3])
    out_direct = Direct(net, stage_out, out_o, out_sems)
    qkv_direct = Direct(net, stage_qkv, qkv_o, qkv_sems)

    @pl.loop(0, length // block)
    def _(i):
        span = aligned(i * block, block)
        datt[span, :] = dot_nt(dm[span, :], wo[...]).astype(BF)
        dk[span, :] = jnp.zeros((block, columns), F32)
        dv[span, :] = jnp.zeros((block, columns), F32)

    def out_term(k):
        cols = aligned(out_direct.owner(k) * depth, depth)
        stage_out[k] = dot_tn(att[...], dm[:, cols]).astype(BF)

    @pl.loop(1, net.n_f)
    def _(k):
        out_term(k)
        out_direct.copy(k).start()

    out_term(0)
    out_direct.keep().start()
    copies.wait()

    @pl.loop(0, heads)
    def _(head):
        lane = lax.broadcasted_iota(jnp.int32, (1, columns), 1)
        here = jnp.where(lane // HEAD == head, 1.0, 0.0).astype(BF)
        scale = HEAD**-0.5
        visible = lax.broadcasted_iota(jnp.int32, (block, block), 0) <= lax.broadcasted_iota(
            jnp.int32, (block, block), 1
        )
        head_rows = aligned(head * HEAD, HEAD)
        for i in range(length // block):
            lo, hi = i * block, (i + 1) * block
            query = q[lo:hi, :] * (here * scale)
            upstream = datt[lo:hi, :] * here
            logsum = lse[pl.ds(head, 1), lo:hi]

            def part(at, end, mask):
                probs = jnp.exp(dot_nt(k[at:end, :], query) - logsum)
                if mask:
                    probs = jnp.where(visible, probs, 0.0)
                grads = dot_nt(v[at:end, :], upstream)
                dv[at:end, :] = dv[at:end, :] + dot(probs.astype(BF), upstream)
                return probs, grads, jnp.sum(probs * grads, 0, keepdims=True)

            def scored(at, end, probs, grads, inner):
                scores = (probs * (grads - inner)).astype(BF)
                dk[at:end, :] = dk[at:end, :] + dot(scores, query)
                return dot(kt[head_rows, at:end], scores)

            near, near_grads, inner = part(lo, hi, True)
            if i:
                far, far_grads, more = part(0, lo, False)
                inner = inner + more
            out = scored(lo, hi, near, near_grads, inner)
            if i:
                out = out + scored(0, lo, far, far_grads, inner)
            dqt[head_rows, lo:hi] = out * scale

    terms[...] = terms_in[...]
    bias_cols = aligned(net.s * columns, columns)

    @pl.loop(0, length // block)
    def _(i):
        span = aligned(i * block, block)
        tables = cosine[span, :], -sine_next[span, :], -sine_last[span, :]
        parts = [
            rotary(dqt[:, span].T.astype(BF).astype(F32), *tables).astype(BF),
            rotary(dk[span, :].astype(BF).astype(F32), *tables).astype(BF),
            dv[span, :].astype(BF),
        ]
        for kind in range(3):
            dproj[kind, span, :] = parts[kind]
            row = slice(4 + kind, 5 + kind)
            terms[row, bias_cols] = terms[row, bias_cols] + jnp.sum(parts[kind].astype(F32), 0, keepdims=True)

    def qkv_term(k):
        cols = aligned(qkv_direct.owner(k) * depth, depth)
        left = n1[:, cols].T
        for kind in range(3):
            stage_qkv[k, kind] = dot(left, dproj[kind]).astype(BF)

    def produce(place, acc):
        span = aligned(place * pair, pair)

        @pl.loop(0, width // tile)
        def _(j):
            cols = aligned(j * tile, tile)
            total = dot_nt(dproj[0, span, :], wq[0, cols, :])
            for kind in range(1, 3):
                total = total + dot_nt(dproj[kind, span, :], wq[kind, cols, :])
            acc[:, cols] = total

    fold = Fold(net, acc, *buffers, *fold_sems)
    each = -(-(net.n_f - 1) // (net.n_l - 1))

    @pl.loop(0, net.n_l - 1)
    def _(j):
        fold.step(net.n_l - 1 - j, produce)

        @pl.loop(0, each)
        def _(i):
            k = 1 + j * each + i

            @pl.when(k < net.n_f)
            def _():
                qkv_term(k)
                qkv_direct.copy(k).start()

    fold.last(produce)

    def write_input(span, value):
        gin_o[span, :] = value + dmid[span, :]

    norm_backward(chunk, tok, acc, fold.mine, gains[0:1, :], terms, 0, write_input)
    PacketSum(net, *packet_scratch).run(terms, small_o, width // (net.n_f * net.n_s))
    qkv_term(0)
    qkv_direct.keep().start()
    fold.finish()
    out_direct.finish()
    qkv_direct.finish()


def back_part(dm, wo, att, q, k, kt, v, n1, wq, lse, tokens, dmid, gains, terms, tables):
    chunk, width = tokens.shape
    n_f, n_s = lax.axis_size("fsdp"), lax.axis_size("seq")
    length, columns = q.shape
    depth = width // n_f
    shape = jax.ShapeDtypeStruct
    direct = pltpu.SemaphoreType.DMA((2, n_f))
    return pl.pallas_call(
        back_kernel,
        name="back",
        out_shape=[
            shape((chunk, width), F32),
            shape((SMALL, 128), F32),
            shape((n_f, columns, depth), BF),
            shape((n_f, 3, depth, columns), BF),
        ],
        in_specs=[ANY] * 9 + [VMEM] * 8,
        out_specs=[VMEM] * 2 + [ANY] * 2,
        scratch_shapes=[
            pltpu.VMEM((length, width), BF),
            pltpu.VMEM((columns, width), BF),
            pltpu.VMEM((length, columns), BF),
            pltpu.VMEM((length, columns), BF),
            pltpu.VMEM((length, columns), BF),
            pltpu.VMEM((columns, length), BF),
            pltpu.VMEM((length, columns), BF),
            pltpu.VMEM((length, width), BF),
            pltpu.VMEM((3, width, columns), BF),
            pltpu.VMEM((length, columns), BF),
            pltpu.VMEM((length, columns), F32),
            pltpu.VMEM((length, columns), F32),
            pltpu.VMEM((columns, length), F32),
            pltpu.VMEM((3, length, columns), BF),
            pltpu.VMEM((n_f, columns, depth), BF),
            pltpu.VMEM((n_f, 3, depth, columns), BF),
            pltpu.VMEM((SMALL, width), F32),
            pltpu.VMEM((2 * chunk, width), F32),
            *Fold.buffers(n_s, chunk, width),
            *Fold.sems(n_s),
            *PacketSum.scratch(n_f, n_s),
            direct,
            direct,
            pltpu.SemaphoreType.DMA((9,)),
        ],
        compiler_params=pltpu.CompilerParams(
            collective_id=3, has_side_effects=True, vmem_limit_bytes=VMEM_BYTES
        ),
        cost_estimate=pl.CostEstimate(
            flops=2 * length * columns * (8 * width + 5 * length),
            bytes_accessed=4 * length * width,
            transcendentals=length * length * columns // HEAD,
        ),
    )(dm, wo, att, q, k, kt, v, n1, wq, lse, tokens, dmid, gains, terms, *tables)


def per_device(
    tokens,
    gain_one,
    shift_one,
    w_qkv,
    b_qkv,
    w_out,
    gain_two,
    shift_two,
    w_gate,
    w_up,
    w_down,
    grad_output,
):
    length = tokens.shape[1] * lax.axis_size("seq")
    width = gain_one.shape[0]
    packet = jnp.concatenate(
        [jnp.stack([gain_one, shift_one, gain_two, shift_two]), b_qkv, jnp.zeros((1, width), BF)]
    )
    packet = jnp.pad(packet.astype(F32), ((0, 0), (0, 128 - width)))
    tables = rotary_tables(length)
    (q, k, kt, v, att, lse, n1, gains, wq, wo, wg, wu, wd, gout, n2, hidden, dgate, dup, mid) = forward_part(
        tokens[0], packet, w_qkv.transpose(1, 0, 2), w_out, w_gate.T, w_up.T, w_down, grad_output[0], tables
    )
    dmid, top, terms, dm, gate, up, down = middle_part(
        dgate, dup, wg, wu, n2, hidden, gout, wd, mid, gains, grad_output[0]
    )
    grad_input, small, out, qkv = back_part(
        dm, wo, att, q, k, kt, v, n1, wq, lse, tokens[0], dmid, gains, terms, tables
    )

    def total(terms):
        return jnp.sum(terms.astype(F32), 0)

    return (
        top[None],
        grad_input[None],
        small[0, :width],
        small[1, :width],
        total(qkv).transpose(1, 0, 2),
        small[4:7, :width],
        total(out),
        small[2, :width],
        small[3, :width],
        total(gate).T,
        total(up).T,
        total(down),
    )


def solution(mesh):
    whole = P(("fsdp", "seq"))
    rows = P("fsdp", "seq", None)
    inner = P("seq", "fsdp")
    outer = P("fsdp", "seq")
    heads = P("fsdp", None, "seq")
    bias = P(None, ("fsdp", "seq"))
    return jax.shard_map(
        per_device,
        mesh=mesh,
        in_specs=(rows, whole, whole, heads, bias, inner, whole, whole, outer, outer, inner, rows),
        out_specs=(rows, rows, whole, whole, heads, bias, inner, whole, whole, outer, outer, inner),
        check_vma=False,
    )
```

```python
import functools

import jax
import jax.numpy as jnp
import numpy as np
from jax import lax
from jax.experimental import pallas as pl
from jax.experimental.pallas import tpu as pltpu
from jax.sharding import PartitionSpec as P

HEAD = 64
ROT = 16
EPSILON = 1e-05
NEG_LARGE = -1e30
MESH = pl.DeviceIdType.MESH
ANY = pl.BlockSpec(memory_space=pl.ANY)
VMEM = pl.BlockSpec(memory_space=pltpu.VMEM)
BF = jnp.bfloat16
F32 = jnp.float32
VMEM_BYTES = 62 * 2**20
SMALL = 8


def put(src, dst, send, recv, **device):
    return pltpu.make_async_remote_copy(
        src_ref=src, dst_ref=dst, send_sem=send, recv_sem=recv, device_id=device, device_id_type=MESH
    )


def dot(left, right):
    return jnp.dot(left, right, preferred_element_type=F32)


def dot_nt(left, right):
    return lax.dot_general(left, right, (((1,), (1,)), ((), ())), preferred_element_type=F32)


def dot_tn(left, right):
    return lax.dot_general(left, right, (((0,), (0,)), ((), ())), preferred_element_type=F32)


def aligned(start, size, unit=None):
    return pl.ds(pl.multiple_of(start, unit or size), size)


class Net:
    def __init__(self):
        self.n_f, self.n_s = lax.axis_size("fsdp"), lax.axis_size("seq")
        self.tall = 2 if self.n_f % 2 == 0 else 1
        self.wide = self.n_f // self.tall
        self.n_l = self.n_s // 2
        self.f, self.s = lax.axis_index("fsdp"), lax.axis_index("seq")
        self.a, self.b = self.f // self.wide, self.f % self.wide
        self.z, self.c = self.s // 2, self.s % 2
        self.mate = self.s + 1 - 2 * self.c

    def barrier(self):
        sem = pltpu.get_barrier_semaphore()
        for k in range(1, self.n_f):
            pl.semaphore_signal(
                sem, inc=1, device_id={"fsdp": (self.f + k) % self.n_f}, device_id_type=MESH
            )
        for k in range(1, self.n_s):
            pl.semaphore_signal(
                sem, inc=1, device_id={"seq": (self.s + k) % self.n_s}, device_id_type=MESH
            )
        pl.semaphore_wait(sem, self.n_f + self.n_s - 2)

    def sides(self, hop, act):
        @pl.loop(0, 2)
        def _(side):
            other = self.z + (2 * side - 1) * hop

            @pl.when((other >= 0) & (other < self.n_l))
            def _():
                act(other, side)


class Spread:
    def __init__(self, net, src, part, sems):
        self.net, self.src, self.part, self.sems = net, src, part, sems
        self.rows = [j for j in range(1, net.wide)]
        self.cols = [i for i in range(1, net.tall)]

    @staticmethod
    def count(n_f):
        tall = 2 if n_f % 2 == 0 else 1
        wide = n_f // tall
        return 1 + 2 * (wide - 1) + 2 * (tall - 1) + 4 * (wide - 1) * (tall - 1)

    def at(self, kind, i, j):
        w, t = len(self.rows), len(self.cols)
        base = {
            "own": 0,
            "row": 1,
            "col": 1 + 2 * w,
            "half0": 1 + 2 * w + 2 * t,
            "half1": 1 + 2 * w + 2 * t + 2 * w * t,
        }[kind]
        if kind == "own":
            return self.sems.at[0]
        k = j - 1 if kind == "row" else i - 1 if kind == "col" else (i - 1) * w + j - 1
        return self.sems.at[base + 2 * k], self.sems.at[base + 2 * k + 1]

    def rank(self, i, j):
        net = self.net
        return ((net.a + i) % net.tall) * net.wide + (net.b + j) % net.wide

    def back(self, i, j):
        net = self.net
        return ((net.a - i + net.tall) % net.tall) * net.wide + (net.b - j + net.wide) % net.wide

    def own(self):
        return pltpu.make_async_copy(self.src, self.part(self.net.f, None), self.at("own", 0, 0))

    def first(self, i, j):
        send, recv = self.at("row" if i == 0 else "col", i, j)
        return put(self.src, self.part(self.net.f, None), send, recv, fsdp=self.rank(i, j))

    def came(self, i, j):
        send, recv = self.at("row" if i == 0 else "col", i, j)
        place = self.part(self.back(i, j), None)
        return put(place, place, send, recv, fsdp=self.rank(i, j))

    def second(self, half, i, j, came=False):
        send, recv = self.at("half0" if half == 0 else "half1", i, j)
        origin = self.back(i, j) if came else self.back(0, j) if half == 0 else self.back(i, 0)
        place = self.part(origin, half)
        return put(place, place, send, recv, fsdp=self.rank(i, 0) if half == 0 else self.rank(0, j))

    def start(self):
        self.own().start()
        for i in self.cols:
            self.first(i, 0).start()
        for j in self.rows:
            self.first(0, j).start()

    def relay(self):
        for j in self.rows:
            self.came(0, j).wait_recv()
            for i in self.cols:
                self.second(0, i, j).start()
        for i in self.cols:
            self.came(i, 0).wait_recv()
            for j in self.rows:
                self.second(1, i, j).start()

    def finish(self):
        self.own().wait()
        for j in self.rows:
            self.first(0, j).wait_send()
        for i in self.cols:
            self.first(i, 0).wait_send()
        for i in self.cols:
            for j in self.rows:
                for half in range(2):
                    self.second(half, i, j, came=True).wait_recv()
                    self.second(half, i, j).wait_send()


class Line:
    def __init__(self, net, src, part, recv, send):
        self.net, self.src, self.part, self.recv, self.send = net, src, part, recv, send

    @staticmethod
    def sems(n_s):
        return [pltpu.SemaphoreType.DMA((n_s,)), pltpu.SemaphoreType.DMA((4, n_s // 2))]

    def own(self):
        net = self.net
        return pltpu.make_async_copy(self.src, self.part(net.s), self.recv.at[net.s])

    def on_line(self, src, chunk, side, hop):
        net = self.net
        return put(
            src,
            self.part(chunk),
            self.send.at[side, hop],
            self.recv.at[chunk],
            seq=net.s + 2 - 4 * side,
        )

    def to_mate(self, src, chunk, side, hop):
        return put(src, self.part(chunk), self.send.at[2 + side, hop], self.recv.at[chunk], seq=self.net.mate)

    def goes_on(self, side):
        after = self.net.z + 1 - 2 * side
        return (after >= 0) & (after < self.net.n_l)

    def start(self):
        net = self.net
        self.own().start()
        for side in range(2):

            @pl.when(self.goes_on(side))
            def _():
                self.on_line(self.src, net.s, side, 0).start()

        self.to_mate(self.src, net.s, 0, 0).start()

    def arrive(self, chunk):
        place = self.part(chunk)
        put(place, place, self.send.at[0, 0], self.recv.at[chunk], seq=self.net.mate).wait_recv()

    def step(self, hop):
        net = self.net

        def act(other, side):
            chunk = 2 * other + net.c
            self.arrive(chunk)

            @pl.when(self.goes_on(side))
            def _():
                self.on_line(self.part(chunk), chunk, side, hop).start()

            self.to_mate(self.part(chunk), chunk, side, hop).start()

        net.sides(hop, act)

    def pair(self, other):
        self.arrive(2 * other + 1 - self.net.c)

    def finish(self):
        net = self.net
        for side in range(2):

            @pl.when(self.goes_on(side))
            def _():
                self.on_line(self.src, net.s, side, 0).wait_send()

        self.to_mate(self.src, net.s, 0, 0).wait_send()

        @pl.loop(1, net.n_l)
        def _(hop):
            def act(other, side):
                chunk = 2 * other + net.c

                @pl.when(self.goes_on(side))
                def _():
                    self.on_line(self.part(chunk), chunk, side, hop).wait_send()

                self.to_mate(self.part(chunk), chunk, side, hop).wait_send()

            net.sides(hop, act)


class Packets:
    def __init__(self, net, src, buf, sems):
        self.net, self.src, self.buf, self.sems = net, src, buf, sems

    @staticmethod
    def count(n_f, n_s):
        return 1 + 2 * (n_f - 1) + 2 * (n_s - 1)

    def own(self):
        net = self.net
        return pltpu.make_async_copy(self.src, self.buf.at[net.s, net.f], self.sems.at[0])

    def one(self, k, came=False):
        net = self.net
        f = (net.f - k + net.n_f) % net.n_f if came else net.f
        place = self.buf.at[net.s, f]
        return put(
            place if came else self.src,
            place,
            self.sems.at[2 * k - 1],
            self.sems.at[2 * k],
            fsdp=(net.f + k) % net.n_f,
        )

    def two(self, k, came=False):
        net = self.net
        place = self.buf.at[(net.s - k + net.n_s) % net.n_s if came else net.s]
        at = 2 * (net.n_f - 1) + 2 * k - 1
        return put(place, place, self.sems.at[at], self.sems.at[at + 1], seq=(net.s + k) % net.n_s)

    def start(self):
        self.own().start()
        for k in range(1, self.net.n_f):
            self.one(k).start()

    def middle(self):
        self.own().wait()
        for k in range(1, self.net.n_f):
            self.one(k, came=True).wait_recv()
            self.one(k).wait_send()
        for k in range(1, self.net.n_s):
            self.two(k).start()

    def finish(self):
        for k in range(1, self.net.n_s):
            self.two(k, came=True).wait_recv()
            self.two(k).wait_send()

    def unpack(self, out, width):
        net = self.net
        per = 128 // width
        for tile in range(net.n_f * net.n_s // per):
            total = None
            for j in range(per):
                f, s = divmod(tile * per + j, net.n_s)
                piece = self.buf[s, f]
                if j:
                    piece = pltpu.roll(piece, j * width, axis=1)
                total = piece if total is None else total + piece
            out[:, tile * 128 : (tile + 1) * 128] = total


def rotary(values, cosine, sine_next, sine_last):
    columns = values.shape[1]
    half = ROT // 2
    times = columns // 128

    def wide(table):
        return table if times == 1 else jnp.concatenate([table] * times, axis=1)

    following = pltpu.roll(values, columns - half, axis=1)
    previous = pltpu.roll(values, half, axis=1)
    return values * wide(cosine) + following * wide(sine_next) + previous * wide(sine_last)


def rotary_tables(length):
    half = ROT // 2
    freqs = np.float32(10000.0) ** (-np.arange(half, dtype=np.float32) * np.float32(2.0 / ROT))
    angles = np.arange(length, dtype=np.float32)[:, None] * freqs[None, :].astype(np.float32)
    cosine, sine = np.cos(angles), np.sin(angles)
    rest = np.zeros((length, HEAD - ROT), np.float32)
    none = np.zeros_like(sine)
    keep = np.concatenate([cosine, cosine, rest + 1], 1)
    following = np.concatenate([-sine, none, rest], 1)
    previous = np.concatenate([none, sine, rest], 1)
    return [np.tile(t, (1, 128 // HEAD)).astype(np.float32) for t in (keep, following, previous)]


def normalize(values):
    center = values - jnp.mean(values, -1, keepdims=True)
    inverse = lax.rsqrt(jnp.mean(center * center, -1, keepdims=True) + EPSILON)
    return center * inverse, inverse


class Copies:
    def __init__(self, sems):
        self.sems, self.all, self.open = sems, [], []

    def start(self, src, dst):
        copy = pltpu.make_async_copy(src, dst, self.sems.at[len(self.all)])
        copy.start()
        self.all.append(copy)
        self.open.append(copy)
        return copy

    def wait(self, *copies):
        for copy in copies or list(self.open):
            copy.wait()
            self.open.remove(copy)


def columns_of(ref, depth):
    half_rows = ref.shape[0] // 2

    def part(f, half):
        span = aligned(f * depth, depth)
        if half is None:
            return ref.at[:, span]
        return ref.at[pl.ds(half * half_rows, half_rows), span]

    return part


def rows_of(ref, chunk):
    return lambda s: ref.at[aligned(s * chunk, chunk)]


class Fold:
    def __init__(self, net, acc, mate_in, coming, mate_out, out, mate_send, mate_recv, send, recv):
        self.net, self.acc = net, acc
        self.mate_in, self.coming, self.mate_out, self.out = mate_in, coming, mate_out, out
        self.mate_send, self.mate_recv, self.send, self.recv = mate_send, mate_recv, send, recv
        self.chunk = acc.shape[0] // 2

    @staticmethod
    def buffers(n_s, chunk, width):
        n_l = n_s // 2
        return [
            pltpu.VMEM((n_l, chunk, width), BF),
            pltpu.VMEM((n_l + 1, chunk, width), BF),
            pltpu.VMEM((2, chunk, width), BF),
            pltpu.VMEM((2, 2, chunk, width), BF),
        ]

    @staticmethod
    def sems(n_s):
        n_l = n_s // 2
        return [
            pltpu.SemaphoreType.DMA((2,)),
            pltpu.SemaphoreType.DMA((n_l,)),
            pltpu.SemaphoreType.DMA((2, 2)),
            pltpu.SemaphoreType.DMA((n_l + 1,)),
        ]

    def mine(self, i):
        return aligned(self.net.c * self.chunk + i * 32, 32)

    def place(self, other):
        return (other >= 0) & (other < self.net.n_l)

    def to_mate(self, target, side):
        return put(
            self.mate_out.at[side],
            self.mate_in.at[target],
            self.mate_send.at[side],
            self.mate_recv.at[target],
            seq=self.net.mate,
        )

    def onward(self, target, side, hop):
        last = (1 - side) * (1 // hop)
        slot = target + (self.net.n_l - target) * last
        return put(
            self.out.at[side, hop % 2],
            self.coming.at[slot],
            self.send.at[side, hop % 2],
            self.recv.at[slot],
            seq=self.net.s + 4 * side - 2,
        )

    def came(self, slot):
        place = self.coming.at[slot]
        put(place, place, self.send.at[0, 0], self.recv.at[slot], seq=self.net.mate).wait_recv()

    def swap(self, target, side):
        count = self.chunk // 32

        @pl.loop(0, count)
        def _(i):
            theirs = aligned((1 - self.net.c) * self.chunk + i * 32, 32)
            self.mate_out[side, aligned(i * 32, 32), :] = self.acc[theirs, :].astype(BF)

        self.to_mate(target, side).start()

    def swapped(self, target, side):
        self.to_mate(target, side).wait_recv()

    def add(self, ref, at):
        @pl.loop(0, self.chunk // 32)
        def _(i):
            span = self.mine(i)
            self.acc[span, :] = self.acc[span, :] + ref[at, aligned(i * 32, 32), :].astype(F32)

    def step(self, hop, produce):
        net = self.net

        def act(target, side):
            produce(target, self.acc)
            further = target + 2 * side - 1

            @pl.when(self.place(further))
            def _():
                self.to_mate(further, side).wait_send()

            self.swap(target, side)
            self.swapped(target, side)
            self.add(self.mate_in, target)

            @pl.when(self.place(net.z + 1 - 2 * side))
            def _():
                self.came(target)
                self.add(self.coming, target)

            @pl.when(self.place(further + 2 * side - 1))
            def _():
                self.onward(target, side, hop + 2).wait_send()

            @pl.loop(0, self.chunk // 32)
            def _(i):
                self.out[side, hop % 2, aligned(i * 32, 32), :] = self.acc[self.mine(i), :].astype(BF)

            self.onward(target, side, hop).start()

        net.sides(hop, act)

    def last(self, produce):
        net = self.net

        @pl.when(net.z > 0)
        def _():
            self.to_mate(net.z - 1, 0).wait_send()

        produce(net.z, self.acc)
        self.swap(net.z, 0)
        self.swapped(net.z, 0)
        self.add(self.mate_in, net.z)

        @pl.when(net.z > 0)
        def _():
            self.came(net.z)
            self.add(self.coming, net.z)

        @pl.when(net.z < net.n_l - 1)
        def _():
            self.came(net.n_l)
            self.add(self.coming, net.n_l)

    def finish(self):
        net = self.net
        self.to_mate(net.z, 0).wait_send()

        @pl.when(net.z < net.n_l - 1)
        def _():
            self.to_mate(net.z + 1, 1).wait_send()

        @pl.loop(1, min(3, net.n_l))
        def _(hop):
            net.sides(hop, lambda target, side: self.onward(target, side, hop).wait_send())


class Direct:
    def __init__(self, net, stage, recv, sems):
        self.net, self.stage, self.recv, self.sems = net, stage, recv, sems

    def owner(self, k):
        return (self.net.f + k) % self.net.n_f

    def copy(self, k):
        return put(
            self.stage.at[k],
            self.recv.at[self.net.f],
            self.sems.at[0, k],
            self.sems.at[1, k],
            fsdp=self.owner(k),
        )

    def keep(self):
        return pltpu.make_async_copy(self.stage.at[0], self.recv.at[self.net.f], self.sems.at[0, 0])

    def finish(self):
        self.keep().wait()

        @pl.loop(1, self.net.n_f)
        def _(k):
            place = self.recv.at[(self.net.f - k + self.net.n_f) % self.net.n_f]
            put(place, place, self.sems.at[0, k], self.sems.at[1, k], fsdp=self.owner(k)).wait_recv()
            self.copy(k).wait_send()


class PacketSum:
    def __init__(self, net, out, seq_in, total, fsdp_in, sems):
        self.net, self.out, self.seq_in, self.total, self.fsdp_in, self.sems = net, out, seq_in, total, fsdp_in, sems

    @staticmethod
    def scratch(n_f, n_s):
        return [
            pltpu.VMEM((n_s, n_f, SMALL, 128), F32),
            pltpu.VMEM((n_s, n_f, SMALL, 128), F32),
            pltpu.VMEM((n_f, SMALL, 128), F32),
            pltpu.VMEM((n_f, SMALL, 128), F32),
            pltpu.SemaphoreType.DMA((2 * (n_f + n_s),)),
        ]

    def one(self, k):
        to = (self.net.s + k) % self.net.n_s
        return put(self.out.at[to], self.seq_in.at[k], self.sems.at[2 * k], self.sems.at[2 * k + 1], seq=to)

    def two(self, k):
        to = (self.net.f + k) % self.net.n_f
        at = 2 * (self.net.n_s + k)
        return put(self.total.at[to], self.fsdp_in.at[k], self.sems.at[at], self.sems.at[at + 1], fsdp=to)

    def run(self, terms, result, width):
        net = self.net
        per = 128 // width
        for tile in range(net.n_f * net.n_s // per):
            value = terms[:, tile * 128 : (tile + 1) * 128]
            for j in range(per):
                f, s = divmod(tile * per + j, net.n_s)
                self.out[s, f] = pltpu.roll(value, 128 - j * width, axis=1) if j else value
        for k in range(1, net.n_s):
            self.one(k).start()
        total = self.out[net.s]
        for k in range(1, net.n_s):
            self.one(k).wait()
            total = total + self.seq_in[k]
        self.total[...] = total
        for k in range(1, net.n_f):
            self.two(k).start()
        total = self.total[net.f]
        for k in range(1, net.n_f):
            self.two(k).wait()
            total = total + self.fsdp_in[k]
        result[...] = total


def norm_backward(rows, source, grad, grad_rows, gain, terms, at, write):
    terms[at : at + 2, :] = jnp.zeros((2, terms.shape[1]), F32)

    @pl.loop(0, rows // 32)
    def _(i):
        span = aligned(i * 32, 32)
        scaled, inverse = normalize(source[span, :].astype(F32))
        value = grad[grad_rows(i), :]
        upstream = value * gain
        inner = jnp.mean(upstream, -1, keepdims=True)
        cross = jnp.mean(upstream * scaled, -1, keepdims=True)
        terms[at : at + 1, :] = terms[at : at + 1, :] + jnp.sum(value * scaled, 0, keepdims=True)
        terms[at + 1 : at + 2, :] = terms[at + 1 : at + 2, :] + jnp.sum(value, 0, keepdims=True)
        write(span, inverse * (upstream - inner - scaled * cross))


def forward_kernel(
    tok,
    packet,
    wq_own,
    wo_own,
    wg_own,
    wu_own,
    wd_own,
    gout_own,
    cosine,
    sine_next,
    sine_last,
    q_o,
    k_o,
    kt_o,
    v_o,
    att_o,
    lse_o,
    n1_o,
    gains_o,
    wq_o,
    wo_o,
    wg_o,
    wu_o,
    wd_o,
    gout_o,
    n2_o,
    mid_o,
    rows,
    n1,
    gout,
    wq,
    wo,
    wg,
    wu,
    wd,
    q,
    k,
    kt,
    v,
    vt,
    ot,
    att,
    mid,
    tok_in,
    n2_own,
    packets,
    acc,
    *rest,
):
    net = Net()
    chunk, width = tok.shape
    length = chunk * net.n_s
    depth = wq_own.shape[1]
    columns = wq_own.shape[2]
    heads = columns // HEAD
    pair = 2 * chunk
    block = 256
    tile = 512
    buffers, rest = rest[:4], rest[4:]
    fold_sems, rest = rest[:4], rest[4:]
    tok_sems, rest = rest[:2], rest[2:]
    gout_sems, rest = rest[:2], rest[2:]
    n2_sems, rest = rest[:2], rest[2:]
    spread_sems, rest = rest[:5], rest[5:]
    pk_sems, copy_sems = rest
    copies = Copies(copy_sems)

    tok_copy = copies.start(tok, tok_in)
    net.barrier()

    def wq_part(f, half):
        if half is None:
            return wq.at[:, aligned(f * depth, depth), :]
        return wq.at[:, aligned(f * depth + half * (depth // 2), depth // 2), :]

    spread_q = Spread(net, wq_own, wq_part, spread_sems[0])
    spread_o, spread_g, spread_u, spread_d = [
        Spread(net, own, columns_of(full, depth), sems)
        for own, full, sems in zip((wo_own, wg_own, wu_own, wd_own), (wo, wg, wu, wd), spread_sems[1:])
    ]
    pk = Packets(net, packet, packets, pk_sems)
    line = Line(net, tok, rows_of(rows, chunk), *tok_sems)
    gout_line = Line(net, gout_own, rows_of(gout, chunk), *gout_sems)
    n2_line = Line(net, n2_own, rows_of(rows, chunk), *n2_sems)
    fold = Fold(net, acc, *buffers, *fold_sems)

    pk.start()
    line.start()
    spread_q.start()
    pk.middle()
    pk.finish()
    pk.unpack(gains_o, width // (net.n_f * net.n_s))

    def norm_block(other):
        gain, shift = gains_o[0:1, :], gains_o[1:2, :]

        @pl.loop(0, pair // 32)
        def _(i):
            span = aligned(other * pair + i * 32, 32)
            scaled, _ = normalize(rows[span, :].astype(F32))
            n1[span, :] = (scaled * gain + shift).astype(BF)

    def project_block(other):
        span = aligned(other * pair, pair)
        left = n1[span, :]
        cols = aligned(net.s * columns, columns)
        tables = cosine[span, :], sine_next[span, :], sine_last[span, :]
        for kind in range(3):
            value = dot(left, wq[kind]) + gains_o[4 + kind : 5 + kind, cols]
            if kind == 0:
                q[span, :] = rotary(value, *tables).astype(BF)
            elif kind == 1:
                value = rotary(value, *tables)
                k[span, :] = value.astype(BF)
                kt[:, span] = value.T.astype(BF)
            else:
                v[span, :] = value.astype(BF)
                vt[:, span] = value.T.astype(BF)

    line.arrive(net.s)
    line.pair(net.z)
    norm_block(net.z)

    def hop_norm(hop):
        line.step(hop)

        def act(other, side):
            line.pair(other)
            norm_block(other)

        net.sides(hop, act)

    for hop in range(1, net.n_l - 1):
        hop_norm(hop)
        if hop == 1:
            spread_o.start()
            spread_g.start()
            spread_q.relay()
    spread_q.finish()

    @pl.loop(0, net.n_l - 1)
    def _(hop):
        def act(other, side):
            @pl.when((hop > 0) | (side == 0))
            def _():
                project_block(other)

        net.sides(hop, act)

    spread_u.start()
    spread_o.relay()
    hop_norm(net.n_l - 1)
    gout_line.start()
    net.sides(net.n_l - 1, lambda other, side: project_block(other))
    for pair_of in ((n1, n1_o), (wq, wq_o), (q, q_o), (k, k_o), (kt, kt_o), (v, v_o)):
        copies.start(*pair_of)

    @pl.loop(0, heads)
    def _(head):
        lane = lax.broadcasted_iota(jnp.int32, (1, columns), 1)
        here = jnp.where(lane // HEAD == head, HEAD**-0.5, 0.0).astype(BF)
        visible = lax.broadcasted_iota(jnp.int32, (block, block), 0) <= lax.broadcasted_iota(
            jnp.int32, (block, block), 1
        )
        head_rows = aligned(head * HEAD, HEAD)
        for i in range(length // block):
            lo, hi = i * block, (i + 1) * block
            query = q[lo:hi, :] * here
            near = jnp.where(visible, dot_nt(k[lo:hi, :], query), NEG_LARGE)
            highest = jnp.max(near, 0, keepdims=True)
            if i:
                far = dot_nt(k[0:lo, :], query)
                highest = jnp.maximum(highest, jnp.max(far, 0, keepdims=True))
            near = jnp.exp(near - highest)
            total = jnp.sum(near, 0, keepdims=True)
            out = dot(vt[head_rows, lo:hi], near.astype(BF))
            if i:
                far = jnp.exp(far - highest)
                total = total + jnp.sum(far, 0, keepdims=True)
                out = out + dot(vt[head_rows, 0:lo], far.astype(BF))
            ot[head_rows, lo:hi] = out / total
            lse_o[pl.ds(head, 1), lo:hi] = highest + jnp.log(total)

    for i in range(length // block):
        att[i * block : (i + 1) * block, :] = ot[:, i * block : (i + 1) * block].T.astype(BF)

    spread_o.finish()
    spread_g.relay()
    spread_d.start()
    line.finish()
    copies.start(att, att_o)
    copies.start(wo, wo_o)

    def produce_attended(place, acc):
        left = att[aligned(place * pair, pair), :]

        @pl.loop(0, width // tile)
        def _(j):
            cols = aligned(j * tile, tile)
            acc[:, cols] = dot(left, wo[:, cols])

    for j in range(net.n_l - 1):
        fold.step(net.n_l - 1 - j, produce_attended)
        gout_line.step(j + 1)
        if j == 0:
            spread_u.relay()

    fold.last(produce_attended)
    copies.wait(tok_copy)
    gain_two, shift_two = gains_o[2:3, :], gains_o[3:4, :]

    @pl.loop(0, chunk // 32)
    def _(i):
        span = aligned(i * 32, 32)
        value = tok_in[span, :].astype(F32) + acc[fold.mine(i), :]
        mid[span, :] = value
        scaled, _ = normalize(value)
        n2_own[span, :] = (scaled * gain_two + shift_two).astype(BF)

    n2_line.start()
    spread_d.relay()
    fold.finish()
    copies.start(mid, mid_o)
    gout_line.arrive(net.s)
    gout_line.pair(net.z)

    @pl.loop(1, net.n_l)
    def _(hop):
        net.sides(hop, lambda other, side: gout_line.pair(other))

    copies.start(gout, gout_o)

    n2_line.arrive(net.s)
    n2_line.pair(net.z)

    @pl.loop(1, net.n_l)
    def _(hop):
        n2_line.step(hop)
        net.sides(hop, lambda other, side: n2_line.pair(other))

    for spread in (spread_g, spread_u, spread_d):
        spread.finish()
    for pair_of in ((wg, wg_o), (wu, wu_o), (wd, wd_o), (rows, n2_o)):
        copies.start(*pair_of)
    gout_line.finish()
    n2_line.finish()
    copies.wait()


def forward_part(tokens, packet, wq, wo, wg, wu, wd, gout, tables):
    chunk, width = tokens.shape
    n_f, n_s = lax.axis_size("fsdp"), lax.axis_size("seq")
    length = chunk * n_s
    columns = wq.shape[2]
    units = wg.shape[0]
    shape = jax.ShapeDtypeStruct
    wide, head = (length, width), (length, columns)
    return pl.pallas_call(
        forward_kernel,
        name="forward",
        out_shape=[
            shape(head, BF),
            shape(head, BF),
            shape((columns, length), BF),
            shape(head, BF),
            shape(head, BF),
            shape((8, length), F32),
            shape(wide, BF),
            shape((SMALL, width), F32),
            shape((3, width, columns), BF),
            shape((columns, width), BF),
            *[shape((units, width), BF)] * 3,
            shape(wide, BF),
            shape(wide, BF),
            shape((chunk, width), F32),
        ],
        in_specs=[ANY, VMEM, *[ANY] * 6, VMEM, VMEM, VMEM],
        out_specs=[*[ANY] * 5, VMEM, ANY, VMEM, *[ANY] * 8],
        scratch_shapes=[
            pltpu.VMEM(wide, BF),
            pltpu.VMEM(wide, BF),
            pltpu.VMEM(wide, BF),
            pltpu.VMEM((3, width, columns), BF),
            pltpu.VMEM((columns, width), BF),
            *[pltpu.VMEM((units, width), BF)] * 3,
            pltpu.VMEM(head, BF),
            pltpu.VMEM(head, BF),
            pltpu.VMEM((columns, length), BF),
            pltpu.VMEM(head, BF),
            pltpu.VMEM((columns, length), BF),
            pltpu.VMEM((columns, length), F32),
            pltpu.VMEM(head, BF),
            pltpu.VMEM((chunk, width), F32),
            pltpu.VMEM((chunk, width), BF),
            pltpu.VMEM((chunk, width), BF),
            pltpu.VMEM((n_s, n_f, SMALL, 128), F32),
            pltpu.VMEM((2 * chunk, width), F32),
            *Fold.buffers(n_s, chunk, width),
            *Fold.sems(n_s),
            *Line.sems(n_s),
            *Line.sems(n_s),
            *Line.sems(n_s),
            *[pltpu.SemaphoreType.DMA((Spread.count(n_f),))] * 5,
            pltpu.SemaphoreType.DMA((Packets.count(n_f, n_s),)),
            pltpu.SemaphoreType.DMA((20,)),
        ],
        compiler_params=pltpu.CompilerParams(
            collective_id=1, has_side_effects=True, vmem_limit_bytes=VMEM_BYTES
        ),
        cost_estimate=pl.CostEstimate(
            flops=2 * length * width * 4 * columns,
            bytes_accessed=8 * length * width,
            transcendentals=length * length * columns // HEAD,
        ),
    )(tokens, packet, wq, wo, wg, wu, wd, gout, *tables)


def middle_kernel(
    dgate_in,
    dup_in,
    wg_in,
    wu_in,
    n2_in,
    hidden_in,
    gout_in,
    wd_in,
    mid,
    gains,
    gout_own,
    dmid_o,
    top_o,
    terms_o,
    dm_o,
    gate_o,
    up_o,
    down_o,
    dgate,
    dup,
    wg,
    wu,
    n2,
    hidden,
    gout,
    wd,
    dmid_low,
    stage_gate,
    stage_up,
    stage_down,
    acc,
    *rest,
):
    net = Net()
    chunk, width = mid.shape
    pair = 2 * chunk
    depth = width // net.n_f
    tile = 512
    first_buffers, rest = rest[:4], rest[4:]
    last_buffers, rest = rest[:4], rest[4:]
    first_sems, rest = rest[:4], rest[4:]
    last_sems, rest = rest[:4], rest[4:]
    dm_sems, rest = rest[:2], rest[2:]
    gate_sems, up_sems, down_sems, copy_sems = rest

    copies = Copies(copy_sems)
    loads = [
        copies.start(src, dst)
        for src, dst in (
            (dgate_in, dgate),
            (dup_in, dup),
            (wg_in, wg),
            (wu_in, wu),
            (n2_in, n2),
            (hidden_in, hidden),
            (gout_in, gout),
            (wd_in, wd),
        )
    ]
    net.barrier()
    dm_line = Line(net, dmid_low, rows_of(dm_o, chunk), *dm_sems)
    fold = Fold(net, acc, *first_buffers, *first_sems)
    last = Fold(net, acc, *last_buffers, *last_sems)
    gate_direct = Direct(net, stage_gate, gate_o, gate_sems)
    up_direct = Direct(net, stage_up, up_o, up_sems)
    down_direct = Direct(net, stage_down, down_o, down_sems)
    directs = (down_direct, gate_direct, up_direct)

    def weight_terms(k):
        cols = aligned(gate_direct.owner(k) * depth, depth)
        stage_down[k] = dot(hidden[...], gout[:, cols]).astype(BF)
        right = n2[:, cols]
        stage_gate[k] = dot(dgate[...], right).astype(BF)
        stage_up[k] = dot(dup[...], right).astype(BF)

    def produce_normed(place, acc):
        span = aligned(place * pair, pair)
        left, right = dgate[:, span].T, dup[:, span].T

        @pl.loop(0, width // tile)
        def _(j):
            cols = aligned(j * tile, tile)
            acc[:, cols] = dot(left, wg[:, cols]) + dot(right, wu[:, cols])

    copies.wait(*loads[:4])
    each = -(-(net.n_f - 1) // (net.n_l - 1))
    for j in range(net.n_l - 1):
        fold.step(net.n_l - 1 - j, produce_normed)
        if j == 0:
            copies.wait(*loads[4:])

        @pl.loop(1 + j * each, min(1 + (j + 1) * each, net.n_f))
        def _(k):
            weight_terms(k)
            for direct in directs:
                direct.copy(k).start()

    fold.last(produce_normed)

    def write_middle(span, value):
        value = value + gout_own[span, :].astype(F32)
        dmid_o[span, :] = value
        dmid_low[span, :] = value.astype(BF)

    terms_o[...] = jnp.zeros(terms_o.shape, F32)
    norm_backward(chunk, mid, acc, fold.mine, gains[2:3, :], terms_o, 2, write_middle)
    dm_line.start()
    fold.finish()

    def produce_top(place, acc):
        left = hidden[:, aligned(place * pair, pair)].T

        @pl.loop(0, width // tile)
        def _(j):
            cols = aligned(j * tile, tile)
            acc[:, cols] = dot(left, wd[:, cols])

    @pl.loop(0, net.n_l - 1)
    def _(j):
        last.step(net.n_l - 1 - j, produce_top)
        dm_line.step(j + 1)

    last.last(produce_top)

    @pl.loop(0, chunk // 32)
    def _(i):
        span = aligned(i * 32, 32)
        top_o[span, :] = (mid[span, :] + acc[last.mine(i), :]).astype(BF)

    weight_terms(0)
    for direct in directs:
        direct.keep().start()

    last.finish()
    dm_line.arrive(net.s)
    dm_line.pair(net.z)

    @pl.loop(1, net.n_l)
    def _(hop):
        net.sides(hop, lambda other, side: dm_line.pair(other))

    dm_line.finish()
    for direct in directs:
        direct.finish()


def middle_part(dgate, dup, wg, wu, n2, hidden, gout_rows, wd, mid, gains, gout):
    chunk, width = mid.shape
    n_f, n_s = lax.axis_size("fsdp"), lax.axis_size("seq")
    length = chunk * n_s
    units = wg.shape[0]
    depth = width // n_f
    shape = jax.ShapeDtypeStruct
    buffers = Fold.buffers(n_s, chunk, width)
    direct = pltpu.SemaphoreType.DMA((2, n_f))
    wide, turned, weight, terms = (length, width), (units, length), (units, width), (n_f, units, depth)
    return pl.pallas_call(
        middle_kernel,
        name="middle",
        out_shape=[
            shape((chunk, width), F32),
            shape((chunk, width), BF),
            shape((SMALL, width), F32),
            shape(wide, BF),
            *[shape(terms, BF)] * 3,
        ],
        in_specs=[ANY] * 8 + [VMEM] * 3,
        out_specs=[VMEM] * 3 + [ANY] * 4,
        scratch_shapes=[
            pltpu.VMEM(turned, BF),
            pltpu.VMEM(turned, BF),
            pltpu.VMEM(weight, BF),
            pltpu.VMEM(weight, BF),
            pltpu.VMEM(wide, BF),
            pltpu.VMEM(turned, BF),
            pltpu.VMEM(wide, BF),
            pltpu.VMEM(weight, BF),
            pltpu.VMEM((chunk, width), BF),
            *[pltpu.VMEM(terms, BF)] * 3,
            pltpu.VMEM((2 * chunk, width), F32),
            *buffers,
            *buffers,
            *Fold.sems(n_s),
            *Fold.sems(n_s),
            *Line.sems(n_s),
            *[direct] * 3,
            pltpu.SemaphoreType.DMA((8,)),
        ],
        compiler_params=pltpu.CompilerParams(
            collective_id=2, has_side_effects=True, vmem_limit_bytes=VMEM_BYTES
        ),
        cost_estimate=pl.CostEstimate(
            flops=2 * length * width * units * 6, bytes_accessed=8 * length * width, transcendentals=0
        ),
    )(dgate, dup, wg, wu, n2, hidden, gout_rows, wd, mid, gains, gout)


def back_kernel(
    dm_in,
    wo_in,
    att_in,
    q_in,
    k_in,
    kt_in,
    v_in,
    n1_in,
    wq_in,
    lse,
    tok,
    dmid,
    gains,
    terms_in,
    cosine,
    sine_next,
    sine_last,
    gin_o,
    small_o,
    out_o,
    qkv_o,
    dm,
    wo,
    att,
    q,
    k,
    kt,
    v,
    n1,
    wq,
    datt,
    dk,
    dv,
    dqt,
    dproj,
    stage_out,
    stage_qkv,
    terms,
    acc,
    *rest,
):
    net = Net()
    chunk, width = tok.shape
    length, columns = q_in.shape
    heads = columns // HEAD
    pair = 2 * chunk
    depth = width // net.n_f
    block = 256
    tile = 512
    buffers, rest = rest[:4], rest[4:]
    fold_sems, rest = rest[:4], rest[4:]
    packet_scratch, rest = rest[:5], rest[5:]
    out_sems, qkv_sems, copy_sems = rest

    copies = Copies(copy_sems)
    loads = [
        copies.start(src, dst)
        for src, dst in (
            (dm_in, dm),
            (wo_in, wo),
            (att_in, att),
            (q_in, q),
            (k_in, k),
            (kt_in, kt),
            (v_in, v),
            (n1_in, n1),
            (wq_in, wq),
        )
    ]
    net.barrier()
    copies.wait(*loads[:3])
    out_direct = Direct(net, stage_out, out_o, out_sems)
    qkv_direct = Direct(net, stage_qkv, qkv_o, qkv_sems)

    @pl.loop(0, length // block)
    def _(i):
        span = aligned(i * block, block)
        datt[span, :] = dot_nt(dm[span, :], wo[...]).astype(BF)
        dk[span, :] = jnp.zeros((block, columns), F32)
        dv[span, :] = jnp.zeros((block, columns), F32)

    def out_term(k):
        cols = aligned(out_direct.owner(k) * depth, depth)
        stage_out[k] = dot_tn(att[...], dm[:, cols]).astype(BF)

    @pl.loop(1, net.n_f)
    def _(k):
        out_term(k)
        out_direct.copy(k).start()

    out_term(0)
    out_direct.keep().start()
    copies.wait()

    @pl.loop(0, heads)
    def _(head):
        lane = lax.broadcasted_iota(jnp.int32, (1, columns), 1)
        here = jnp.where(lane // HEAD == head, 1.0, 0.0).astype(BF)
        scale = HEAD**-0.5
        visible = lax.broadcasted_iota(jnp.int32, (block, block), 0) <= lax.broadcasted_iota(
            jnp.int32, (block, block), 1
        )
        head_rows = aligned(head * HEAD, HEAD)
        for i in range(length // block):
            lo, hi = i * block, (i + 1) * block
            query = q[lo:hi, :] * (here * scale)
            upstream = datt[lo:hi, :] * here
            logsum = lse[pl.ds(head, 1), lo:hi]

            def part(at, end, mask):
                probs = jnp.exp(dot_nt(k[at:end, :], query) - logsum)
                if mask:
                    probs = jnp.where(visible, probs, 0.0)
                grads = dot_nt(v[at:end, :], upstream)
                dv[at:end, :] = dv[at:end, :] + dot(probs.astype(BF), upstream)
                return probs, grads, jnp.sum(probs * grads, 0, keepdims=True)

            def scored(at, end, probs, grads, inner):
                scores = (probs * (grads - inner)).astype(BF)
                dk[at:end, :] = dk[at:end, :] + dot(scores, query)
                return dot(kt[head_rows, at:end], scores)

            near, near_grads, inner = part(lo, hi, True)
            if i:
                far, far_grads, more = part(0, lo, False)
                inner = inner + more
            out = scored(lo, hi, near, near_grads, inner)
            if i:
                out = out + scored(0, lo, far, far_grads, inner)
            dqt[head_rows, lo:hi] = out * scale

    terms[...] = terms_in[...]
    bias_cols = aligned(net.s * columns, columns)

    @pl.loop(0, length // block)
    def _(i):
        span = aligned(i * block, block)
        tables = cosine[span, :], -sine_next[span, :], -sine_last[span, :]
        parts = [
            rotary(dqt[:, span].T.astype(BF).astype(F32), *tables).astype(BF),
            rotary(dk[span, :].astype(BF).astype(F32), *tables).astype(BF),
            dv[span, :].astype(BF),
        ]
        for kind in range(3):
            dproj[kind, span, :] = parts[kind]
            row = slice(4 + kind, 5 + kind)
            terms[row, bias_cols] = terms[row, bias_cols] + jnp.sum(parts[kind].astype(F32), 0, keepdims=True)

    def qkv_term(k):
        cols = aligned(qkv_direct.owner(k) * depth, depth)
        left = n1[:, cols].T
        for kind in range(3):
            stage_qkv[k, kind] = dot(left, dproj[kind]).astype(BF)

    def produce(place, acc):
        span = aligned(place * pair, pair)

        @pl.loop(0, width // tile)
        def _(j):
            cols = aligned(j * tile, tile)
            total = dot_nt(dproj[0, span, :], wq[0, cols, :])
            for kind in range(1, 3):
                total = total + dot_nt(dproj[kind, span, :], wq[kind, cols, :])
            acc[:, cols] = total

    fold = Fold(net, acc, *buffers, *fold_sems)
    each = -(-(net.n_f - 1) // (net.n_l - 1))

    @pl.loop(0, net.n_l - 1)
    def _(j):
        fold.step(net.n_l - 1 - j, produce)

        @pl.loop(0, each)
        def _(i):
            k = 1 + j * each + i

            @pl.when(k < net.n_f)
            def _():
                qkv_term(k)
                qkv_direct.copy(k).start()

    fold.last(produce)

    def write_input(span, value):
        gin_o[span, :] = value + dmid[span, :]

    norm_backward(chunk, tok, acc, fold.mine, gains[0:1, :], terms, 0, write_input)
    PacketSum(net, *packet_scratch).run(terms, small_o, width // (net.n_f * net.n_s))
    qkv_term(0)
    qkv_direct.keep().start()
    fold.finish()
    out_direct.finish()
    qkv_direct.finish()


def back_part(dm, wo, att, q, k, kt, v, n1, wq, lse, tokens, dmid, gains, terms, tables):
    chunk, width = tokens.shape
    n_f, n_s = lax.axis_size("fsdp"), lax.axis_size("seq")
    length, columns = q.shape
    depth = width // n_f
    shape = jax.ShapeDtypeStruct
    direct = pltpu.SemaphoreType.DMA((2, n_f))
    return pl.pallas_call(
        back_kernel,
        name="back",
        out_shape=[
            shape((chunk, width), F32),
            shape((SMALL, 128), F32),
            shape((n_f, columns, depth), BF),
            shape((n_f, 3, depth, columns), BF),
        ],
        in_specs=[ANY] * 9 + [VMEM] * 8,
        out_specs=[VMEM] * 2 + [ANY] * 2,
        scratch_shapes=[
            pltpu.VMEM((length, width), BF),
            pltpu.VMEM((columns, width), BF),
            pltpu.VMEM((length, columns), BF),
            pltpu.VMEM((length, columns), BF),
            pltpu.VMEM((length, columns), BF),
            pltpu.VMEM((columns, length), BF),
            pltpu.VMEM((length, columns), BF),
            pltpu.VMEM((length, width), BF),
            pltpu.VMEM((3, width, columns), BF),
            pltpu.VMEM((length, columns), BF),
            pltpu.VMEM((length, columns), F32),
            pltpu.VMEM((length, columns), F32),
            pltpu.VMEM((columns, length), F32),
            pltpu.VMEM((3, length, columns), BF),
            pltpu.VMEM((n_f, columns, depth), BF),
            pltpu.VMEM((n_f, 3, depth, columns), BF),
            pltpu.VMEM((SMALL, width), F32),
            pltpu.VMEM((2 * chunk, width), F32),
            *Fold.buffers(n_s, chunk, width),
            *Fold.sems(n_s),
            *PacketSum.scratch(n_f, n_s),
            direct,
            direct,
            pltpu.SemaphoreType.DMA((9,)),
        ],
        compiler_params=pltpu.CompilerParams(
            collective_id=3, has_side_effects=True, vmem_limit_bytes=VMEM_BYTES
        ),
        cost_estimate=pl.CostEstimate(
            flops=2 * length * columns * (8 * width + 5 * length),
            bytes_accessed=4 * length * width,
            transcendentals=length * length * columns // HEAD,
        ),
    )(dm, wo, att, q, k, kt, v, n1, wq, lse, tokens, dmid, gains, terms, *tables)


def per_device(
    tokens,
    gain_one,
    shift_one,
    w_qkv,
    b_qkv,
    w_out,
    gain_two,
    shift_two,
    w_gate,
    w_up,
    w_down,
    grad_output,
):
    length = tokens.shape[1] * lax.axis_size("seq")
    width = gain_one.shape[0]
    packet = jnp.concatenate(
        [jnp.stack([gain_one, shift_one, gain_two, shift_two]), b_qkv, jnp.zeros((1, width), BF)]
    )
    packet = jnp.pad(packet.astype(F32), ((0, 0), (0, 128 - width)))
    tables = rotary_tables(length)
    (q, k, kt, v, att, lse, n1, gains, wq, wo, wg, wu, wd, gout, n2, mid) = forward_part(
        tokens[0], packet, w_qkv.transpose(1, 0, 2), w_out, w_gate.T, w_up.T, w_down, grad_output[0], tables
    )

    def product(weight, rows):
        return jnp.einsum("fd,td->ft", weight, rows, preferred_element_type=F32)

    gate, up, back = product(wg, n2), product(wu, n2), product(wd, gout)
    sigma = jax.nn.sigmoid(gate)
    active = gate * sigma
    hidden = (active * up).astype(BF)
    dgate = (back * up * (sigma * (1.0 + gate * (1.0 - sigma)))).astype(BF)
    dup = (back * active).astype(BF)
    dmid, top, terms, dm, gate, up, down = middle_part(
        dgate, dup, wg, wu, n2, hidden, gout, wd, mid, gains, grad_output[0]
    )
    grad_input, small, out, qkv = back_part(
        dm, wo, att, q, k, kt, v, n1, wq, lse, tokens[0], dmid, gains, terms, tables
    )

    def total(terms):
        return jnp.sum(terms.astype(F32), 0)

    return (
        top[None],
        grad_input[None],
        small[0, :width],
        small[1, :width],
        total(qkv).transpose(1, 0, 2),
        small[4:7, :width],
        total(out),
        small[2, :width],
        small[3, :width],
        total(gate).T,
        total(up).T,
        total(down),
    )


def solution(mesh):
    whole = P(("fsdp", "seq"))
    rows = P("fsdp", "seq", None)
    inner = P("seq", "fsdp")
    outer = P("fsdp", "seq")
    heads = P("fsdp", None, "seq")
    bias = P(None, ("fsdp", "seq"))
    return jax.shard_map(
        per_device,
        mesh=mesh,
        in_specs=(rows, whole, whole, heads, bias, inner, whole, whole, outer, outer, inner, rows),
        out_specs=(rows, rows, whole, whole, heads, bias, inner, whole, whole, outer, outer, inner),
        check_vma=False,
    )
```

```python
import functools

import jax
import jax.numpy as jnp
import numpy as np
from jax import lax
from jax.experimental import pallas as pl
from jax.experimental.pallas import tpu as pltpu
from jax.sharding import PartitionSpec as P

HEAD = 64
ROT = 16
EPSILON = 1e-05
NEG_LARGE = -1e30
MESH = pl.DeviceIdType.MESH
ANY = pl.BlockSpec(memory_space=pl.ANY)
VMEM = pl.BlockSpec(memory_space=pltpu.VMEM)
BF = jnp.bfloat16
F32 = jnp.float32
VMEM_BYTES = 62 * 2**20
TILE = 512
SMALL = 8


def put(src, dst, send, recv, **device):
    return pltpu.make_async_remote_copy(
        src_ref=src, dst_ref=dst, send_sem=send, recv_sem=recv, device_id=device, device_id_type=MESH
    )


def dot(left, right):
    return jnp.dot(left, right, preferred_element_type=F32)


def dot_nt(left, right):
    return lax.dot_general(left, right, (((1,), (1,)), ((), ())), preferred_element_type=F32)


def dot_tn(left, right):
    return lax.dot_general(left, right, (((0,), (0,)), ((), ())), preferred_element_type=F32)


def aligned(start, size, unit=None):
    return pl.ds(pl.multiple_of(start, unit or size), size)


class Net:
    def __init__(self):
        self.n_f, self.n_s = lax.axis_size("fsdp"), lax.axis_size("seq")
        self.tall = 2 if self.n_f % 2 == 0 else 1
        self.wide = self.n_f // self.tall
        self.n_l = self.n_s // 2
        self.f, self.s = lax.axis_index("fsdp"), lax.axis_index("seq")
        self.a, self.b = self.f // self.wide, self.f % self.wide
        self.z, self.c = self.s // 2, self.s % 2
        self.mate = self.s + 1 - 2 * self.c

    def barrier(self):
        sem = pltpu.get_barrier_semaphore()
        for k in range(1, self.n_f):
            pl.semaphore_signal(
                sem, inc=1, device_id={"fsdp": (self.f + k) % self.n_f}, device_id_type=MESH
            )
        for k in range(1, self.n_s):
            pl.semaphore_signal(
                sem, inc=1, device_id={"seq": (self.s + k) % self.n_s}, device_id_type=MESH
            )
        pl.semaphore_wait(sem, self.n_f + self.n_s - 2)

    def sides(self, hop, act):
        @pl.loop(0, 2)
        def _(side):
            other = self.z + (2 * side - 1) * hop

            @pl.when((other >= 0) & (other < self.n_l))
            def _():
                act(other, side)


class Spread:
    def __init__(self, net, src, part, sems):
        self.net, self.src, self.part, self.sems = net, src, part, sems
        self.rows = [j for j in range(1, net.wide)]
        self.cols = [i for i in range(1, net.tall)]

    @staticmethod
    def count(n_f):
        tall = 2 if n_f % 2 == 0 else 1
        wide = n_f // tall
        return 1 + 2 * (wide - 1) + 2 * (tall - 1) + 4 * (wide - 1) * (tall - 1)

    def at(self, kind, i, j):
        w, t = len(self.rows), len(self.cols)
        base = {
            "own": 0,
            "row": 1,
            "col": 1 + 2 * w,
            "half0": 1 + 2 * w + 2 * t,
            "half1": 1 + 2 * w + 2 * t + 2 * w * t,
        }[kind]
        if kind == "own":
            return self.sems.at[0]
        k = j - 1 if kind == "row" else i - 1 if kind == "col" else (i - 1) * w + j - 1
        return self.sems.at[base + 2 * k], self.sems.at[base + 2 * k + 1]

    def rank(self, i, j):
        net = self.net
        return ((net.a + i) % net.tall) * net.wide + (net.b + j) % net.wide

    def back(self, i, j):
        net = self.net
        return ((net.a - i + net.tall) % net.tall) * net.wide + (net.b - j + net.wide) % net.wide

    def own(self):
        return pltpu.make_async_copy(self.src, self.part(self.net.f, None), self.at("own", 0, 0))

    def first(self, i, j):
        send, recv = self.at("row" if i == 0 else "col", i, j)
        return put(self.src, self.part(self.net.f, None), send, recv, fsdp=self.rank(i, j))

    def came(self, i, j):
        send, recv = self.at("row" if i == 0 else "col", i, j)
        place = self.part(self.back(i, j), None)
        return put(place, place, send, recv, fsdp=self.rank(i, j))

    def second(self, half, i, j, came=False):
        send, recv = self.at("half0" if half == 0 else "half1", i, j)
        origin = self.back(i, j) if came else self.back(0, j) if half == 0 else self.back(i, 0)
        place = self.part(origin, half)
        return put(place, place, send, recv, fsdp=self.rank(i, 0) if half == 0 else self.rank(0, j))

    def start(self):
        self.own().start()
        for i in self.cols:
            self.first(i, 0).start()
        for j in self.rows:
            self.first(0, j).start()

    def relay(self):
        for j in self.rows:
            self.came(0, j).wait_recv()
            for i in self.cols:
                self.second(0, i, j).start()
        for i in self.cols:
            self.came(i, 0).wait_recv()
            for j in self.rows:
                self.second(1, i, j).start()

    def finish(self):
        self.own().wait()
        for j in self.rows:
            self.first(0, j).wait_send()
        for i in self.cols:
            self.first(i, 0).wait_send()
        for i in self.cols:
            for j in self.rows:
                for half in range(2):
                    self.second(half, i, j, came=True).wait_recv()
                    self.second(half, i, j).wait_send()


class Line:
    def __init__(self, net, src, part, recv, send, local):
        self.net, self.src, self.part, self.recv, self.send, self.local = net, src, part, recv, send, local
        self.pieces = recv.shape[1]
        self.rows = src.shape[0] // self.pieces

    @staticmethod
    def sems(n_s, pieces=2):
        return [
            pltpu.SemaphoreType.DMA((n_s, pieces)),
            pltpu.SemaphoreType.DMA((4, n_s // 2, pieces)),
            pltpu.SemaphoreType.DMA((1,)),
        ]

    def cut(self, ref, piece):
        return ref.at[aligned(piece * self.rows, self.rows)]

    def own(self):
        return pltpu.make_async_copy(self.src, self.part(self.net.s), self.local.at[0])

    def on_line(self, src, chunk, side, hop, piece):
        return put(
            self.cut(src, piece),
            self.cut(self.part(chunk), piece),
            self.send.at[side, hop, piece],
            self.recv.at[chunk, piece],
            seq=self.net.s + 2 - 4 * side,
        )

    def to_mate(self, src, chunk, side, hop, piece):
        return put(
            self.cut(src, piece),
            self.cut(self.part(chunk), piece),
            self.send.at[2 + side, hop, piece],
            self.recv.at[chunk, piece],
            seq=self.net.mate,
        )

    def goes_on(self, side):
        after = self.net.z + 1 - 2 * side
        return (after >= 0) & (after < self.net.n_l)

    def each_piece(self, act):
        pl.loop(0, self.pieces)(act)

    def start(self):
        net = self.net

        @self.each_piece
        def _(piece):
            for side in range(2):

                @pl.when(self.goes_on(side))
                def _():
                    self.on_line(self.src, net.s, side, 0, piece).start()

            self.to_mate(self.src, net.s, 0, 0, piece).start()

        self.own().start()

    def came(self, chunk, piece):
        place = self.cut(self.part(chunk), piece)
        put(place, place, self.send.at[0, 0, 0], self.recv.at[chunk, piece], seq=self.net.mate).wait_recv()

    def step(self, hop):
        net = self.net

        @self.each_piece
        def _(piece):
            def act(other, side):
                chunk = 2 * other + net.c
                self.came(chunk, piece)

                @pl.when(self.goes_on(side))
                def _():
                    self.on_line(self.part(chunk), chunk, side, hop, piece).start()

                self.to_mate(self.part(chunk), chunk, side, hop, piece).start()

            net.sides(hop, act)

    def pair(self, other):
        @self.each_piece
        def _(piece):
            self.came(2 * other + 1 - self.net.c, piece)

    def here(self):
        self.own().wait()
        self.pair(self.net.z)

    def finish(self):
        net = self.net

        @self.each_piece
        def _(piece):
            for side in range(2):

                @pl.when(self.goes_on(side))
                def _():
                    self.on_line(self.src, net.s, side, 0, piece).wait_send()

            self.to_mate(self.src, net.s, 0, 0, piece).wait_send()

            @pl.loop(1, net.n_l)
            def _(hop):
                def act(other, side):
                    chunk = 2 * other + net.c

                    @pl.when(self.goes_on(side))
                    def _():
                        self.on_line(self.part(chunk), chunk, side, hop, piece).wait_send()

                    self.to_mate(self.part(chunk), chunk, side, hop, piece).wait_send()

                net.sides(hop, act)


class Packets:
    def __init__(self, net, src, buf, sems):
        self.net, self.src, self.buf, self.sems = net, src, buf, sems

    @staticmethod
    def count(n_f, n_s):
        return 1 + 2 * (n_f - 1) + 2 * (n_s - 1)

    def own(self):
        net = self.net
        return pltpu.make_async_copy(self.src, self.buf.at[net.s, net.f], self.sems.at[0])

    def one(self, k, came=False):
        net = self.net
        f = (net.f - k + net.n_f) % net.n_f if came else net.f
        place = self.buf.at[net.s, f]
        return put(
            place if came else self.src,
            place,
            self.sems.at[2 * k - 1],
            self.sems.at[2 * k],
            fsdp=(net.f + k) % net.n_f,
        )

    def two(self, k, came=False):
        net = self.net
        place = self.buf.at[(net.s - k + net.n_s) % net.n_s if came else net.s]
        at = 2 * (net.n_f - 1) + 2 * k - 1
        return put(place, place, self.sems.at[at], self.sems.at[at + 1], seq=(net.s + k) % net.n_s)

    def start(self):
        self.own().start()
        for k in range(1, self.net.n_f):
            self.one(k).start()

    def middle(self):
        self.own().wait()
        for k in range(1, self.net.n_f):
            self.one(k, came=True).wait_recv()
            self.one(k).wait_send()
        for k in range(1, self.net.n_s):
            self.two(k).start()

    def finish(self):
        for k in range(1, self.net.n_s):
            self.two(k, came=True).wait_recv()
            self.two(k).wait_send()

    def unpack(self, out, width):
        net = self.net
        per = 128 // width
        for tile in range(net.n_f * net.n_s // per):
            total = None
            for j in range(per):
                f, s = divmod(tile * per + j, net.n_s)
                piece = self.buf[s, f]
                if j:
                    piece = pltpu.roll(piece, j * width, axis=1)
                total = piece if total is None else total + piece
            out[:, tile * 128 : (tile + 1) * 128] = total


def rotary(values, cosine, sine_next, sine_last):
    columns = values.shape[1]
    half = ROT // 2
    times = columns // 128

    def wide(table):
        return table if times == 1 else jnp.concatenate([table] * times, axis=1)

    following = pltpu.roll(values, columns - half, axis=1)
    previous = pltpu.roll(values, half, axis=1)
    return values * wide(cosine) + following * wide(sine_next) + previous * wide(sine_last)


def rotary_tables(length):
    half = ROT // 2
    freqs = np.float32(10000.0) ** (-np.arange(half, dtype=np.float32) * np.float32(2.0 / ROT))
    angles = np.arange(length, dtype=np.float32)[:, None] * freqs[None, :].astype(np.float32)
    cosine, sine = np.cos(angles), np.sin(angles)
    rest = np.zeros((length, HEAD - ROT), np.float32)
    none = np.zeros_like(sine)
    keep = np.concatenate([cosine, cosine, rest + 1], 1)
    following = np.concatenate([-sine, none, rest], 1)
    previous = np.concatenate([none, sine, rest], 1)
    return [np.tile(t, (1, 128 // HEAD)).astype(np.float32) for t in (keep, following, previous)]


def normalize(values):
    center = values - jnp.mean(values, -1, keepdims=True)
    inverse = lax.rsqrt(jnp.mean(center * center, -1, keepdims=True) + EPSILON)
    return center * inverse, inverse


class Copies:
    def __init__(self, sems):
        self.sems, self.all, self.open = sems, [], []

    def start(self, src, dst):
        copy = pltpu.make_async_copy(src, dst, self.sems.at[len(self.all)])
        copy.start()
        self.all.append(copy)
        self.open.append(copy)
        return copy

    def wait(self, *copies):
        for copy in copies or list(self.open):
            copy.wait()
            self.open.remove(copy)


def columns_of(ref, depth):
    half_rows = ref.shape[0] // 2

    def part(f, half):
        span = aligned(f * depth, depth)
        if half is None:
            return ref.at[:, span]
        return ref.at[pl.ds(half * half_rows, half_rows), span]

    return part


def rows_of(ref, chunk):
    return lambda s: ref.at[aligned(s * chunk, chunk)]


class Fold:
    def __init__(self, net, tile, total, mate_in, coming, mate_out, out, mate_send, mate_recv, send, recv):
        self.net, self.tile, self.total = net, tile, total
        self.mate_in, self.coming, self.mate_out, self.out = mate_in, coming, mate_out, out
        self.mate_send, self.mate_recv, self.send, self.recv = mate_send, mate_recv, send, recv
        self.chunk = total.shape[0]
        self.pieces = recv.shape[1]
        self.rows = self.chunk // self.pieces

    @staticmethod
    def shared(chunk, width):
        return [pltpu.VMEM((2 * chunk, TILE), F32), pltpu.VMEM((chunk, width), F32)]

    @staticmethod
    def buffers(n_s, chunk, width):
        n_l = n_s // 2
        return [
            pltpu.VMEM((n_l, chunk, width), BF),
            pltpu.VMEM((n_l + 1, chunk, width), BF),
            pltpu.VMEM((2, 2, chunk, width), BF),
            pltpu.VMEM((n_l, chunk, width), BF),
        ]

    @staticmethod
    def sems(n_s, pieces=4):
        n_l = n_s // 2
        return [
            pltpu.SemaphoreType.DMA((2, 2, pieces)),
            pltpu.SemaphoreType.DMA((n_l, pieces)),
            pltpu.SemaphoreType.DMA((n_l, pieces)),
            pltpu.SemaphoreType.DMA((n_l + 1, pieces)),
        ]

    def place(self, other):
        return (other >= 0) & (other < self.net.n_l)

    def fed(self, side):
        return self.place(self.net.z + 1 - 2 * side)

    def span(self, piece):
        return aligned(piece * self.rows, self.rows)

    def each_piece(self, act):
        pl.loop(0, self.pieces)(act)

    def to_mate(self, target, side, hop, piece):
        span = self.span(piece)
        return put(
            self.mate_out.at[side, hop % 2, span],
            self.mate_in.at[target, span],
            self.mate_send.at[side, hop % 2, piece],
            self.mate_recv.at[target, piece],
            seq=self.net.mate,
        )

    def onward(self, target, side, hop, piece):
        span = self.span(piece)
        slot = target + (self.net.n_l - target) * (1 - side) * (1 // hop)
        return put(
            self.out.at[target, span],
            self.coming.at[slot, span],
            self.send.at[target, piece],
            self.recv.at[slot, piece],
            seq=self.net.s + 4 * side - 2,
        )

    def came(self, slot, piece):
        place = self.coming.at[slot, self.span(piece)]
        put(place, place, self.send.at[0, 0], self.recv.at[slot, piece], seq=self.net.mate).wait_recv()

    def mate_sent(self, target, side, hop):
        @pl.when(self.place(target))
        def _():
            self.each_piece(lambda piece: self.to_mate(target, side, hop, piece).wait_send())

    def begin_one(self, target, side, hop, produce):
        self.mate_sent(target + 4 * side - 2, side, hop)
        mine = aligned(self.net.c * self.chunk, self.chunk)
        theirs = aligned((1 - self.net.c) * self.chunk, self.chunk)

        def write(cols, value):
            self.tile[...] = value
            self.out[target, :, cols] = self.tile[mine, :].astype(BF)
            self.mate_out[side, hop % 2, :, cols] = self.tile[theirs, :].astype(BF)

        produce(target, write)
        self.each_piece(lambda piece: self.to_mate(target, side, hop, piece).start())

    def begin(self, produce):
        net = self.net

        @pl.loop(0, net.n_l - 1)
        def _(j):
            hop = net.n_l - 1 - j

            def act(target, side):
                self.begin_one(target, side, hop, produce)

                @pl.when(jnp.logical_not(self.fed(side)))
                def _():
                    self.pass_on(target, side, hop, False)

            net.sides(hop, act)

        self.begin_one(net.z, 0, 0, produce)

    def pass_on(self, target, side, hop, fed):
        @self.each_piece
        def _(piece):
            self.to_mate(target, 0, 0, piece).wait_recv()
            span = self.span(piece)
            value = self.out[target, span, :].astype(F32) + self.mate_in[target, span, :].astype(F32)
            if fed:
                self.came(target, piece)
                value = value + self.coming[target, span, :].astype(F32)
            self.out[target, span, :] = value.astype(BF)
            self.onward(target, side, hop, piece).start()

    def step(self, hop):
        def act(target, side):
            @pl.when(self.fed(side))
            def _():
                self.pass_on(target, side, hop, True)

        self.net.sides(hop, act)

    def last(self):
        net = self.net

        @self.each_piece
        def _(piece):
            self.to_mate(net.z, 0, 0, piece).wait_recv()
            span = self.span(piece)
            self.total[span, :] = self.out[net.z, span, :].astype(F32) + self.mate_in[net.z, span, :].astype(F32)
            for fed, slot in ((net.z > 0, net.z), (net.z < net.n_l - 1, net.n_l)):

                @pl.when(fed)
                def _():
                    self.came(slot, piece)
                    self.total[span, :] = self.total[span, :] + self.coming[slot, span, :].astype(F32)

    def finish(self):
        net = self.net
        self.mate_sent(net.z, 0, 0)
        self.mate_sent(net.z - 1, 0, 1)
        self.mate_sent(net.z + 1, 1, 1)
        self.mate_sent(net.z + 2, 1, 2)

        @pl.loop(1, net.n_l)
        def _(hop):
            net.sides(
                hop,
                lambda target, side: self.each_piece(
                    lambda piece: self.onward(target, side, hop, piece).wait_send()
                ),
            )


class Direct:
    def __init__(self, net, stage, recv, sems):
        self.net, self.stage, self.recv, self.sems = net, stage, recv, sems

    def owner(self, k):
        return (self.net.f + k) % self.net.n_f

    def copy(self, k):
        return put(
            self.stage.at[k],
            self.recv.at[self.net.f],
            self.sems.at[0, k],
            self.sems.at[1, k],
            fsdp=self.owner(k),
        )

    def keep(self):
        return pltpu.make_async_copy(self.stage.at[0], self.recv.at[self.net.f], self.sems.at[0, 0])

    def finish(self):
        self.keep().wait()

        @pl.loop(1, self.net.n_f)
        def _(k):
            place = self.recv.at[(self.net.f - k + self.net.n_f) % self.net.n_f]
            put(place, place, self.sems.at[0, k], self.sems.at[1, k], fsdp=self.owner(k)).wait_recv()
            self.copy(k).wait_send()


class PacketSum:
    def __init__(self, net, out, seq_in, total, fsdp_in, sems):
        self.net, self.out, self.seq_in, self.total, self.fsdp_in, self.sems = net, out, seq_in, total, fsdp_in, sems

    @staticmethod
    def scratch(n_f, n_s):
        return [
            pltpu.VMEM((n_s, n_f, SMALL, 128), F32),
            pltpu.VMEM((n_s, n_f, SMALL, 128), F32),
            pltpu.VMEM((n_f, SMALL, 128), F32),
            pltpu.VMEM((n_f, SMALL, 128), F32),
            pltpu.SemaphoreType.DMA((2 * (n_f + n_s),)),
        ]

    def one(self, k):
        to = (self.net.s + k) % self.net.n_s
        return put(self.out.at[to], self.seq_in.at[k], self.sems.at[2 * k], self.sems.at[2 * k + 1], seq=to)

    def two(self, k):
        to = (self.net.f + k) % self.net.n_f
        at = 2 * (self.net.n_s + k)
        return put(self.total.at[to], self.fsdp_in.at[k], self.sems.at[at], self.sems.at[at + 1], fsdp=to)

    def run(self, terms, result, width):
        net = self.net
        per = 128 // width
        for tile in range(net.n_f * net.n_s // per):
            value = terms[:, tile * 128 : (tile + 1) * 128]
            for j in range(per):
                f, s = divmod(tile * per + j, net.n_s)
                self.out[s, f] = pltpu.roll(value, 128 - j * width, axis=1) if j else value
        for k in range(1, net.n_s):
            self.one(k).start()
        total = self.out[net.s]
        for k in range(1, net.n_s):
            self.one(k).wait()
            total = total + self.seq_in[k]
        self.total[...] = total
        for k in range(1, net.n_f):
            self.two(k).start()
        total = self.total[net.f]
        for k in range(1, net.n_f):
            self.two(k).wait()
            total = total + self.fsdp_in[k]
        result[...] = total


def norm_backward(rows, source, grad, gain, terms, at, write):
    terms[at : at + 2, :] = jnp.zeros((2, terms.shape[1]), F32)

    @pl.loop(0, rows // 32)
    def _(i):
        span = aligned(i * 32, 32)
        scaled, inverse = normalize(source[span, :].astype(F32))
        value = grad[span, :]
        upstream = value * gain
        inner = jnp.mean(upstream, -1, keepdims=True)
        cross = jnp.mean(upstream * scaled, -1, keepdims=True)
        terms[at : at + 1, :] = terms[at : at + 1, :] + jnp.sum(value * scaled, 0, keepdims=True)
        terms[at + 1 : at + 2, :] = terms[at + 1 : at + 2, :] + jnp.sum(value, 0, keepdims=True)
        write(span, inverse * (upstream - inner - scaled * cross))


def forward_kernel(
    tok,
    packet,
    wq_own,
    wo_own,
    wg_own,
    wu_own,
    wd_own,
    gout_own,
    cosine,
    sine_next,
    sine_last,
    q_o,
    k_o,
    kt_o,
    v_o,
    att_o,
    lse_o,
    n1_o,
    gains_o,
    wq_o,
    wo_o,
    wg_o,
    wu_o,
    wd_o,
    gout_o,
    n2_o,
    hidden_o,
    dgate_o,
    dup_o,
    mid_o,
    rows,
    n1,
    gout,
    wq,
    wo,
    wg,
    wu,
    wd,
    q,
    k,
    kt,
    v,
    vt,
    ot,
    att,
    hidden,
    dgate,
    dup,
    mid,
    tok_in,
    n2_own,
    packets,
    tiles,
    total,
    *rest,
):
    net = Net()
    chunk, width = tok.shape
    length = chunk * net.n_s
    depth = wq_own.shape[1]
    columns = wq_own.shape[2]
    heads = columns // HEAD
    pair = 2 * chunk
    block = 256
    buffers, rest = rest[:4], rest[4:]
    fold_sems, rest = rest[:4], rest[4:]
    tok_sems, rest = rest[:3], rest[3:]
    gout_sems, rest = rest[:3], rest[3:]
    n2_sems, rest = rest[:3], rest[3:]
    spread_sems, rest = rest[:5], rest[5:]
    pk_sems, copy_sems = rest
    copies = Copies(copy_sems)

    tok_copy = copies.start(tok, tok_in)
    net.barrier()

    def wq_part(f, half):
        if half is None:
            return wq.at[:, aligned(f * depth, depth), :]
        return wq.at[:, aligned(f * depth + half * (depth // 2), depth // 2), :]

    spread_q = Spread(net, wq_own, wq_part, spread_sems[0])
    spread_o, spread_g, spread_u, spread_d = [
        Spread(net, own, columns_of(full, depth), sems)
        for own, full, sems in zip((wo_own, wg_own, wu_own, wd_own), (wo, wg, wu, wd), spread_sems[1:])
    ]
    pk = Packets(net, packet, packets, pk_sems)
    line = Line(net, tok, rows_of(rows, chunk), *tok_sems)
    gout_line = Line(net, gout_own, rows_of(gout, chunk), *gout_sems)
    n2_line = Line(net, n2_own, rows_of(rows, chunk), *n2_sems)
    fold = Fold(net, tiles, total, *buffers, *fold_sems)

    pk.start()
    line.start()
    spread_q.start()
    pk.middle()
    pk.finish()
    pk.unpack(gains_o, width // (net.n_f * net.n_s))

    def norm_block(other):
        gain, shift = gains_o[0:1, :], gains_o[1:2, :]

        @pl.loop(0, pair // 32)
        def _(i):
            span = aligned(other * pair + i * 32, 32)
            scaled, _ = normalize(rows[span, :].astype(F32))
            n1[span, :] = (scaled * gain + shift).astype(BF)

    def project_block(other):
        span = aligned(other * pair, pair)
        left = n1[span, :]
        cols = aligned(net.s * columns, columns)
        tables = cosine[span, :], sine_next[span, :], sine_last[span, :]
        for kind in range(3):
            value = dot(left, wq[kind]) + gains_o[4 + kind : 5 + kind, cols]
            if kind == 0:
                q[span, :] = rotary(value, *tables).astype(BF)
            elif kind == 1:
                value = rotary(value, *tables)
                k[span, :] = value.astype(BF)
                kt[:, span] = value.T.astype(BF)
            else:
                v[span, :] = value.astype(BF)
                vt[:, span] = value.T.astype(BF)

    line.here()
    norm_block(net.z)

    def hop_norm(hop):
        line.step(hop)

        def act(other, side):
            line.pair(other)
            norm_block(other)

        net.sides(hop, act)

    for hop in range(1, net.n_l - 1):
        hop_norm(hop)
        if hop == 1:
            spread_o.start()
            spread_g.start()
            spread_q.relay()
    spread_q.finish()

    @pl.loop(0, net.n_l - 1)
    def _(hop):
        def act(other, side):
            @pl.when((hop > 0) | (side == 0))
            def _():
                project_block(other)

        net.sides(hop, act)

    spread_u.start()
    spread_o.relay()
    hop_norm(net.n_l - 1)
    gout_line.start()
    net.sides(net.n_l - 1, lambda other, side: project_block(other))
    for pair_of in ((n1, n1_o), (wq, wq_o), (q, q_o), (k, k_o), (kt, kt_o), (v, v_o)):
        copies.start(*pair_of)

    @pl.loop(0, heads)
    def _(head):
        lane = lax.broadcasted_iota(jnp.int32, (1, columns), 1)
        here = jnp.where(lane // HEAD == head, HEAD**-0.5, 0.0).astype(BF)
        visible = lax.broadcasted_iota(jnp.int32, (block, block), 0) <= lax.broadcasted_iota(
            jnp.int32, (block, block), 1
        )
        head_rows = aligned(head * HEAD, HEAD)
        for i in range(length // block):
            lo, hi = i * block, (i + 1) * block
            query = q[lo:hi, :] * here
            near = jnp.where(visible, dot_nt(k[lo:hi, :], query), NEG_LARGE)
            highest = jnp.max(near, 0, keepdims=True)
            if i:
                far = dot_nt(k[0:lo, :], query)
                highest = jnp.maximum(highest, jnp.max(far, 0, keepdims=True))
            near = jnp.exp(near - highest)
            total = jnp.sum(near, 0, keepdims=True)
            out = dot(vt[head_rows, lo:hi], near.astype(BF))
            if i:
                far = jnp.exp(far - highest)
                total = total + jnp.sum(far, 0, keepdims=True)
                out = out + dot(vt[head_rows, 0:lo], far.astype(BF))
            ot[head_rows, lo:hi] = out / total
            lse_o[pl.ds(head, 1), lo:hi] = highest + jnp.log(total)

    for i in range(length // block):
        att[i * block : (i + 1) * block, :] = ot[:, i * block : (i + 1) * block].T.astype(BF)

    spread_o.finish()
    spread_g.relay()
    spread_d.start()
    line.finish()
    copies.start(att, att_o)
    copies.start(wo, wo_o)

    def produce_attended(place, write):
        left = att[aligned(place * pair, pair), :]

        @pl.loop(0, width // TILE)
        def _(j):
            cols = aligned(j * TILE, TILE)
            write(cols, dot(left, wo[:, cols]))

    gout_line.step(1)
    fold.begin(produce_attended)
    spread_u.relay()
    for hop in range(net.n_l - 2, 0, -1):
        fold.step(hop)
        gout_line.step(net.n_l - hop)
    fold.last()
    copies.wait(tok_copy)
    gain_two, shift_two = gains_o[2:3, :], gains_o[3:4, :]

    @pl.loop(0, chunk // 32)
    def _(i):
        span = aligned(i * 32, 32)
        value = tok_in[span, :].astype(F32) + total[span, :]
        mid[span, :] = value
        scaled, _ = normalize(value)
        n2_own[span, :] = (scaled * gain_two + shift_two).astype(BF)

    n2_line.start()
    spread_d.relay()
    fold.finish()
    copies.start(mid, mid_o)
    gout_line.here()

    @pl.loop(1, net.n_l)
    def _(hop):
        net.sides(hop, lambda other, side: gout_line.pair(other))

    copies.start(gout, gout_o)

    def forward_block(other):
        span = aligned(other * pair, pair)
        right = rows[span, :]
        gate = dot_nt(wg[...], right)
        up = dot_nt(wu[...], right)
        back = dot_nt(wd[...], gout[span, :])
        sigma = jax.nn.sigmoid(gate)
        active = gate * sigma
        hidden[:, span] = (active * up).astype(BF)
        dgate[:, span] = (back * up * (sigma * (1.0 + gate * (1.0 - sigma)))).astype(BF)
        dup[:, span] = (back * active).astype(BF)

    n2_line.here()

    @pl.loop(1, net.n_l - 1)
    def _(hop):
        n2_line.step(hop)
        net.sides(hop, lambda other, side: n2_line.pair(other))

    for spread in (spread_g, spread_u, spread_d):
        spread.finish()
    for pair_of in ((wg, wg_o), (wu, wu_o), (wd, wd_o)):
        copies.start(*pair_of)

    @pl.loop(0, net.n_l - 1)
    def _(hop):
        def act(other, side):
            @pl.when((hop > 0) | (side == 0))
            def _():
                forward_block(other)

        net.sides(hop, act)

    n2_line.step(net.n_l - 1)

    def last_block(other, side):
        n2_line.pair(other)
        forward_block(other)

    net.sides(net.n_l - 1, last_block)
    for pair_of in ((dgate, dgate_o), (dup, dup_o), (hidden, hidden_o), (rows, n2_o)):
        copies.start(*pair_of)
    gout_line.finish()
    n2_line.finish()
    copies.wait()


def forward_part(tokens, packet, wq, wo, wg, wu, wd, gout, tables):
    chunk, width = tokens.shape
    n_f, n_s = lax.axis_size("fsdp"), lax.axis_size("seq")
    length = chunk * n_s
    columns = wq.shape[2]
    units = wg.shape[0]
    shape = jax.ShapeDtypeStruct
    wide, head, turned = (length, width), (length, columns), (units, length)
    return pl.pallas_call(
        forward_kernel,
        name="forward",
        out_shape=[
            shape(head, BF),
            shape(head, BF),
            shape((columns, length), BF),
            shape(head, BF),
            shape(head, BF),
            shape((8, length), F32),
            shape(wide, BF),
            shape((SMALL, width), F32),
            shape((3, width, columns), BF),
            shape((columns, width), BF),
            *[shape((units, width), BF)] * 3,
            shape(wide, BF),
            shape(wide, BF),
            *[shape(turned, BF)] * 3,
            shape((chunk, width), F32),
        ],
        in_specs=[ANY, VMEM, *[ANY] * 6, VMEM, VMEM, VMEM],
        out_specs=[*[ANY] * 5, VMEM, ANY, VMEM, *[ANY] * 11],
        scratch_shapes=[
            pltpu.VMEM(wide, BF),
            pltpu.VMEM(wide, BF),
            pltpu.VMEM(wide, BF),
            pltpu.VMEM((3, width, columns), BF),
            pltpu.VMEM((columns, width), BF),
            *[pltpu.VMEM((units, width), BF)] * 3,
            pltpu.VMEM(head, BF),
            pltpu.VMEM(head, BF),
            pltpu.VMEM((columns, length), BF),
            pltpu.VMEM(head, BF),
            pltpu.VMEM((columns, length), BF),
            pltpu.VMEM((columns, length), F32),
            pltpu.VMEM(head, BF),
            *[pltpu.VMEM(turned, BF)] * 3,
            pltpu.VMEM((chunk, width), F32),
            pltpu.VMEM((chunk, width), BF),
            pltpu.VMEM((chunk, width), BF),
            pltpu.VMEM((n_s, n_f, SMALL, 128), F32),
            *Fold.shared(chunk, width),
            *Fold.buffers(n_s, chunk, width),
            *Fold.sems(n_s),
            *Line.sems(n_s),
            *Line.sems(n_s),
            *Line.sems(n_s),
            *[pltpu.SemaphoreType.DMA((Spread.count(n_f),))] * 5,
            pltpu.SemaphoreType.DMA((Packets.count(n_f, n_s),)),
            pltpu.SemaphoreType.DMA((20,)),
        ],
        compiler_params=pltpu.CompilerParams(
            collective_id=1, has_side_effects=True, vmem_limit_bytes=VMEM_BYTES
        ),
        cost_estimate=pl.CostEstimate(
            flops=2 * length * width * (4 * columns + 3 * units),
            bytes_accessed=8 * length * width,
            transcendentals=length * (length * columns // HEAD + units),
        ),
    )(tokens, packet, wq, wo, wg, wu, wd, gout, *tables)


def middle_kernel(
    dgate_in,
    dup_in,
    wg_in,
    wu_in,
    n2_in,
    hidden_in,
    gout_in,
    wd_in,
    mid,
    gains,
    gout_own,
    dmid_o,
    top_o,
    terms_o,
    dm_o,
    gate_o,
    up_o,
    down_o,
    dgate,
    dup,
    wg,
    wu,
    n2,
    hidden,
    gout,
    wd,
    dmid_low,
    stage_gate,
    stage_up,
    stage_down,
    tiles,
    total,
    *rest,
):
    net = Net()
    chunk, width = mid.shape
    pair = 2 * chunk
    depth = width // net.n_f
    first_buffers, rest = rest[:4], rest[4:]
    last_buffers, rest = rest[:4], rest[4:]
    first_sems, rest = rest[:4], rest[4:]
    last_sems, rest = rest[:4], rest[4:]
    dm_sems, rest = rest[:3], rest[3:]
    gate_sems, up_sems, down_sems, copy_sems, column_sems = rest

    copies = Copies(copy_sems)
    loads = [
        copies.start(src, dst)
        for src, dst in (
            (dgate_in, dgate),
            (dup_in, dup),
            (wg_in, wg),
            (wu_in, wu),
            (hidden_in, hidden),
            (wd_in, wd),
        )
    ]
    net.barrier()
    dm_line = Line(net, dmid_low, rows_of(dm_o, chunk), *dm_sems)
    fold = Fold(net, tiles, total, *first_buffers, *first_sems)
    last = Fold(net, tiles, total, *last_buffers, *last_sems)
    gate_direct = Direct(net, stage_gate, gate_o, gate_sems)
    up_direct = Direct(net, stage_up, up_o, up_sems)
    down_direct = Direct(net, stage_down, down_o, down_sems)
    directs = (down_direct, gate_direct, up_direct)

    def columns(i):
        cols = aligned(gate_direct.owner(i + 1) * depth, depth)
        return [
            pltpu.make_async_copy(src.at[:, cols], dst.at[i % 2], column_sems.at[at, i % 2])
            for at, (src, dst) in enumerate(((n2_in, n2), (gout_in, gout)))
        ]

    def weight_terms(i):
        k = (i + 1) % net.n_f
        for copy in columns(i):
            copy.wait()
        stage_down[k] = dot(hidden[...], gout[i % 2]).astype(BF)
        right = n2[i % 2]
        stage_gate[k] = dot(dgate[...], right).astype(BF)
        stage_up[k] = dot(dup[...], right).astype(BF)

        @pl.when(i + 2 < net.n_f)
        def _():
            for copy in columns(i + 2):
                copy.start()

    def produce_normed(place, write):
        span = aligned(place * pair, pair)
        left, right = dgate[:, span].T, dup[:, span].T

        @pl.loop(0, width // TILE)
        def _(j):
            cols = aligned(j * TILE, TILE)
            write(cols, dot(left, wg[:, cols]) + dot(right, wu[:, cols]))

    for i in range(min(2, net.n_f)):
        for copy in columns(i):
            copy.start()
    copies.wait(*loads[:4])
    fold.begin(produce_normed)
    copies.wait(*loads[4:])
    steps = max(net.n_l - 2, 1)
    each = -(-(net.n_f - 1) // steps)
    for j in range(steps):

        @pl.loop(j * each, min((j + 1) * each, net.n_f - 1))
        def _(i):
            weight_terms(i)
            for direct in directs:
                direct.copy(i + 1).start()

        if j < net.n_l - 2:
            fold.step(net.n_l - 2 - j)

    fold.last()

    def write_middle(span, value):
        value = value + gout_own[span, :].astype(F32)
        dmid_o[span, :] = value
        dmid_low[span, :] = value.astype(BF)

    terms_o[...] = jnp.zeros(terms_o.shape, F32)
    norm_backward(chunk, mid, total, gains[2:3, :], terms_o, 2, write_middle)
    dm_line.start()
    fold.finish()

    def produce_top(place, write):
        left = hidden[:, aligned(place * pair, pair)].T

        @pl.loop(0, width // TILE)
        def _(j):
            cols = aligned(j * TILE, TILE)
            write(cols, dot(left, wd[:, cols]))

    last.begin(produce_top)
    dm_line.step(1)
    for hop in range(net.n_l - 2, 0, -1):
        last.step(hop)
        dm_line.step(net.n_l - hop)
    last.last()

    @pl.loop(0, chunk // 32)
    def _(i):
        span = aligned(i * 32, 32)
        top_o[span, :] = (mid[span, :] + total[span, :]).astype(BF)

    weight_terms(net.n_f - 1)
    for direct in directs:
        direct.keep().start()

    last.finish()
    dm_line.here()

    @pl.loop(1, net.n_l)
    def _(hop):
        net.sides(hop, lambda other, side: dm_line.pair(other))

    dm_line.finish()
    for direct in directs:
        direct.finish()


def middle_part(dgate, dup, wg, wu, n2, hidden, gout_rows, wd, mid, gains, gout):
    chunk, width = mid.shape
    n_f, n_s = lax.axis_size("fsdp"), lax.axis_size("seq")
    length = chunk * n_s
    units = wg.shape[0]
    depth = width // n_f
    shape = jax.ShapeDtypeStruct
    buffers = Fold.buffers(n_s, chunk, width)
    direct = pltpu.SemaphoreType.DMA((2, n_f))
    wide, turned, weight, terms = (length, width), (units, length), (units, width), (n_f, units, depth)
    return pl.pallas_call(
        middle_kernel,
        name="middle",
        out_shape=[
            shape((chunk, width), F32),
            shape((chunk, width), BF),
            shape((SMALL, width), F32),
            shape(wide, BF),
            *[shape(terms, BF)] * 3,
        ],
        in_specs=[ANY] * 8 + [VMEM] * 3,
        out_specs=[VMEM] * 3 + [ANY] * 4,
        scratch_shapes=[
            pltpu.VMEM(turned, BF),
            pltpu.VMEM(turned, BF),
            pltpu.VMEM(weight, BF),
            pltpu.VMEM(weight, BF),
            pltpu.VMEM((2, length, depth), BF),
            pltpu.VMEM(turned, BF),
            pltpu.VMEM((2, length, depth), BF),
            pltpu.VMEM(weight, BF),
            pltpu.VMEM((chunk, width), BF),
            *[pltpu.VMEM(terms, BF)] * 3,
            *Fold.shared(chunk, width),
            *buffers,
            *buffers,
            *Fold.sems(n_s),
            *Fold.sems(n_s),
            *Line.sems(n_s),
            *[direct] * 3,
            pltpu.SemaphoreType.DMA((6,)),
            pltpu.SemaphoreType.DMA((2, 2)),
        ],
        compiler_params=pltpu.CompilerParams(
            collective_id=2, has_side_effects=True, vmem_limit_bytes=VMEM_BYTES
        ),
        cost_estimate=pl.CostEstimate(
            flops=2 * length * width * units * 6, bytes_accessed=8 * length * width, transcendentals=0
        ),
    )(dgate, dup, wg, wu, n2, hidden, gout_rows, wd, mid, gains, gout)


def back_kernel(
    dm_in,
    wo_in,
    att_in,
    q_in,
    k_in,
    kt_in,
    v_in,
    n1_in,
    wq_in,
    lse,
    tok,
    dmid,
    gains,
    terms_in,
    cosine,
    sine_next,
    sine_last,
    gin_o,
    small_o,
    out_o,
    qkv_o,
    dm,
    wo,
    att,
    q,
    k,
    kt,
    v,
    n1,
    wq,
    datt,
    dk,
    dv,
    dqt,
    dproj,
    stage_out,
    stage_qkv,
    terms,
    tiles,
    total,
    *rest,
):
    net = Net()
    chunk, width = tok.shape
    length, columns = q_in.shape
    heads = columns // HEAD
    pair = 2 * chunk
    depth = width // net.n_f
    block = 256
    buffers, rest = rest[:4], rest[4:]
    fold_sems, rest = rest[:4], rest[4:]
    packet_scratch, rest = rest[:5], rest[5:]
    out_sems, qkv_sems, copy_sems = rest

    copies = Copies(copy_sems)
    loads = [
        copies.start(src, dst)
        for src, dst in (
            (dm_in, dm),
            (wo_in, wo),
            (att_in, att),
            (q_in, q),
            (k_in, k),
            (kt_in, kt),
            (v_in, v),
            (n1_in, n1),
            (wq_in, wq),
        )
    ]
    net.barrier()
    copies.wait(*loads[:3])
    out_direct = Direct(net, stage_out, out_o, out_sems)
    qkv_direct = Direct(net, stage_qkv, qkv_o, qkv_sems)

    @pl.loop(0, length // block)
    def _(i):
        span = aligned(i * block, block)
        datt[span, :] = dot_nt(dm[span, :], wo[...]).astype(BF)
        dk[span, :] = jnp.zeros((block, columns), F32)
        dv[span, :] = jnp.zeros((block, columns), F32)

    def out_term(k):
        cols = aligned(out_direct.owner(k) * depth, depth)
        stage_out[k] = dot_tn(att[...], dm[:, cols]).astype(BF)

    @pl.loop(1, net.n_f)
    def _(k):
        out_term(k)
        out_direct.copy(k).start()

    out_term(0)
    out_direct.keep().start()
    copies.wait()

    @pl.loop(0, heads)
    def _(head):
        lane = lax.broadcasted_iota(jnp.int32, (1, columns), 1)
        here = jnp.where(lane // HEAD == head, 1.0, 0.0).astype(BF)
        scale = HEAD**-0.5
        visible = lax.broadcasted_iota(jnp.int32, (block, block), 0) <= lax.broadcasted_iota(
            jnp.int32, (block, block), 1
        )
        head_rows = aligned(head * HEAD, HEAD)
        for i in range(length // block):
            lo, hi = i * block, (i + 1) * block
            query = q[lo:hi, :] * (here * scale)
            upstream = datt[lo:hi, :] * here
            logsum = lse[pl.ds(head, 1), lo:hi]

            def part(at, end, mask):
                probs = jnp.exp(dot_nt(k[at:end, :], query) - logsum)
                if mask:
                    probs = jnp.where(visible, probs, 0.0)
                grads = dot_nt(v[at:end, :], upstream)
                dv[at:end, :] = dv[at:end, :] + dot(probs.astype(BF), upstream)
                return probs, grads, jnp.sum(probs * grads, 0, keepdims=True)

            def scored(at, end, probs, grads, inner):
                scores = (probs * (grads - inner)).astype(BF)
                dk[at:end, :] = dk[at:end, :] + dot(scores, query)
                return dot(kt[head_rows, at:end], scores)

            near, near_grads, inner = part(lo, hi, True)
            if i:
                far, far_grads, more = part(0, lo, False)
                inner = inner + more
            out = scored(lo, hi, near, near_grads, inner)
            if i:
                out = out + scored(0, lo, far, far_grads, inner)
            dqt[head_rows, lo:hi] = out * scale

    terms[...] = terms_in[...]
    bias_cols = aligned(net.s * columns, columns)

    @pl.loop(0, length // block)
    def _(i):
        span = aligned(i * block, block)
        tables = cosine[span, :], -sine_next[span, :], -sine_last[span, :]
        parts = [
            rotary(dqt[:, span].T.astype(BF).astype(F32), *tables).astype(BF),
            rotary(dk[span, :].astype(BF).astype(F32), *tables).astype(BF),
            dv[span, :].astype(BF),
        ]
        for kind in range(3):
            dproj[kind, span, :] = parts[kind]
            row = slice(4 + kind, 5 + kind)
            terms[row, bias_cols] = terms[row, bias_cols] + jnp.sum(parts[kind].astype(F32), 0, keepdims=True)

    def qkv_term(k):
        cols = aligned(qkv_direct.owner(k) * depth, depth)
        left = n1[:, cols].T
        for kind in range(3):
            stage_qkv[k, kind] = dot(left, dproj[kind]).astype(BF)

    def produce(place, write):
        span = aligned(place * pair, pair)

        @pl.loop(0, width // TILE)
        def _(j):
            cols = aligned(j * TILE, TILE)
            value = dot_nt(dproj[0, span, :], wq[0, cols, :])
            for kind in range(1, 3):
                value = value + dot_nt(dproj[kind, span, :], wq[kind, cols, :])
            write(cols, value)

    fold = Fold(net, tiles, total, *buffers, *fold_sems)
    fold.begin(produce)
    steps = max(net.n_l - 2, 1)
    each = -(-(net.n_f - 1) // steps)
    for j in range(steps):

        @pl.loop(1 + j * each, min(1 + (j + 1) * each, net.n_f))
        def _(k):
            qkv_term(k)
            qkv_direct.copy(k).start()

        if j < net.n_l - 2:
            fold.step(net.n_l - 2 - j)

    fold.last()

    def write_input(span, value):
        gin_o[span, :] = value + dmid[span, :]

    norm_backward(chunk, tok, total, gains[0:1, :], terms, 0, write_input)
    PacketSum(net, *packet_scratch).run(terms, small_o, width // (net.n_f * net.n_s))
    qkv_term(0)
    qkv_direct.keep().start()
    fold.finish()
    out_direct.finish()
    qkv_direct.finish()


def back_part(dm, wo, att, q, k, kt, v, n1, wq, lse, tokens, dmid, gains, terms, tables):
    chunk, width = tokens.shape
    n_f, n_s = lax.axis_size("fsdp"), lax.axis_size("seq")
    length, columns = q.shape
    depth = width // n_f
    shape = jax.ShapeDtypeStruct
    direct = pltpu.SemaphoreType.DMA((2, n_f))
    return pl.pallas_call(
        back_kernel,
        name="back",
        out_shape=[
            shape((chunk, width), F32),
            shape((SMALL, 128), F32),
            shape((n_f, columns, depth), BF),
            shape((n_f, 3, depth, columns), BF),
        ],
        in_specs=[ANY] * 9 + [VMEM] * 8,
        out_specs=[VMEM] * 2 + [ANY] * 2,
        scratch_shapes=[
            pltpu.VMEM((length, width), BF),
            pltpu.VMEM((columns, width), BF),
            pltpu.VMEM((length, columns), BF),
            pltpu.VMEM((length, columns), BF),
            pltpu.VMEM((length, columns), BF),
            pltpu.VMEM((columns, length), BF),
            pltpu.VMEM((length, columns), BF),
            pltpu.VMEM((length, width), BF),
            pltpu.VMEM((3, width, columns), BF),
            pltpu.VMEM((length, columns), BF),
            pltpu.VMEM((length, columns), F32),
            pltpu.VMEM((length, columns), F32),
            pltpu.VMEM((columns, length), F32),
            pltpu.VMEM((3, length, columns), BF),
            pltpu.VMEM((n_f, columns, depth), BF),
            pltpu.VMEM((n_f, 3, depth, columns), BF),
            pltpu.VMEM((SMALL, width), F32),
            *Fold.shared(chunk, width),
            *Fold.buffers(n_s, chunk, width),
            *Fold.sems(n_s),
            *PacketSum.scratch(n_f, n_s),
            direct,
            direct,
            pltpu.SemaphoreType.DMA((9,)),
        ],
        compiler_params=pltpu.CompilerParams(
            collective_id=3, has_side_effects=True, vmem_limit_bytes=VMEM_BYTES
        ),
        cost_estimate=pl.CostEstimate(
            flops=2 * length * columns * (8 * width + 5 * length),
            bytes_accessed=4 * length * width,
            transcendentals=length * length * columns // HEAD,
        ),
    )(dm, wo, att, q, k, kt, v, n1, wq, lse, tokens, dmid, gains, terms, *tables)


def per_device(
    tokens,
    gain_one,
    shift_one,
    w_qkv,
    b_qkv,
    w_out,
    gain_two,
    shift_two,
    w_gate,
    w_up,
    w_down,
    grad_output,
):
    length = tokens.shape[1] * lax.axis_size("seq")
    width = gain_one.shape[0]
    packet = jnp.concatenate(
        [jnp.stack([gain_one, shift_one, gain_two, shift_two]), b_qkv, jnp.zeros((1, width), BF)]
    )
    packet = jnp.pad(packet.astype(F32), ((0, 0), (0, 128 - width)))
    tables = rotary_tables(length)
    (q, k, kt, v, att, lse, n1, gains, wq, wo, wg, wu, wd, gout, n2, hidden, dgate, dup, mid) = forward_part(
        tokens[0], packet, w_qkv.transpose(1, 0, 2), w_out, w_gate.T, w_up.T, w_down, grad_output[0], tables
    )
    dmid, top, terms, dm, gate, up, down = middle_part(
        dgate, dup, wg, wu, n2, hidden, gout, wd, mid, gains, grad_output[0]
    )
    grad_input, small, out, qkv = back_part(
        dm, wo, att, q, k, kt, v, n1, wq, lse, tokens[0], dmid, gains, terms, tables
    )

    def total(terms):
        return jnp.sum(terms.astype(F32), 0)

    return (
        top[None],
        grad_input[None],
        small[0, :width],
        small[1, :width],
        total(qkv).transpose(1, 0, 2),
        small[4:7, :width],
        total(out),
        small[2, :width],
        small[3, :width],
        total(gate).T,
        total(up).T,
        total(down),
    )


def solution(mesh):
    whole = P(("fsdp", "seq"))
    rows = P("fsdp", "seq", None)
    inner = P("seq", "fsdp")
    outer = P("fsdp", "seq")
    heads = P("fsdp", None, "seq")
    bias = P(None, ("fsdp", "seq"))
    return jax.shard_map(
        per_device,
        mesh=mesh,
        in_specs=(rows, whole, whole, heads, bias, inner, whole, whole, outer, outer, inner, rows),
        out_specs=(rows, rows, whole, whole, heads, bias, inner, whole, whole, outer, outer, inner),
        check_vma=False,
    )
```

```python
import functools

import jax
import jax.numpy as jnp
import numpy as np
from jax import lax
from jax.experimental import pallas as pl
from jax.experimental.pallas import tpu as pltpu
from jax.sharding import PartitionSpec as P

HEAD = 64
ROT = 16
EPSILON = 1e-05
NEG_LARGE = -1e30
MESH = pl.DeviceIdType.MESH
ANY = pl.BlockSpec(memory_space=pl.ANY)
VMEM = pl.BlockSpec(memory_space=pltpu.VMEM)
BF = jnp.bfloat16
F32 = jnp.float32
VMEM_BYTES = 62 * 2**20
TILE = 512
SMALL = 8


def put(src, dst, send, recv, **device):
    return pltpu.make_async_remote_copy(
        src_ref=src, dst_ref=dst, send_sem=send, recv_sem=recv, device_id=device, device_id_type=MESH
    )


def dot(left, right):
    return jnp.dot(left, right, preferred_element_type=F32)


def dot_nt(left, right):
    return lax.dot_general(left, right, (((1,), (1,)), ((), ())), preferred_element_type=F32)


def dot_tn(left, right):
    return lax.dot_general(left, right, (((0,), (0,)), ((), ())), preferred_element_type=F32)


def aligned(start, size, unit=None):
    return pl.ds(pl.multiple_of(start, unit or size), size)


class Net:
    def __init__(self):
        self.n_f, self.n_s = lax.axis_size("fsdp"), lax.axis_size("seq")
        self.tall = 2 if self.n_f % 2 == 0 else 1
        self.wide = self.n_f // self.tall
        self.n_l = self.n_s // 2
        self.f, self.s = lax.axis_index("fsdp"), lax.axis_index("seq")
        self.a, self.b = self.f // self.wide, self.f % self.wide
        self.z, self.c = self.s // 2, self.s % 2
        self.mate = self.s + 1 - 2 * self.c

    def barrier(self):
        sem = pltpu.get_barrier_semaphore()
        for k in range(1, self.n_f):
            pl.semaphore_signal(
                sem, inc=1, device_id={"fsdp": (self.f + k) % self.n_f}, device_id_type=MESH
            )
        for k in range(1, self.n_s):
            pl.semaphore_signal(
                sem, inc=1, device_id={"seq": (self.s + k) % self.n_s}, device_id_type=MESH
            )
        pl.semaphore_wait(sem, self.n_f + self.n_s - 2)

    def sides(self, hop, act):
        @pl.loop(0, 2)
        def _(side):
            other = self.z + (2 * side - 1) * hop

            @pl.when((other >= 0) & (other < self.n_l))
            def _():
                act(other, side)


class Spread:
    def __init__(self, net, src, part, sems):
        self.net, self.src, self.part, self.sems = net, src, part, sems
        self.rows = [j for j in range(1, net.wide)]
        self.cols = [i for i in range(1, net.tall)]

    @staticmethod
    def count(n_f):
        tall = 2 if n_f % 2 == 0 else 1
        wide = n_f // tall
        return 1 + 2 * (wide - 1) + 2 * (tall - 1) + 4 * (wide - 1) * (tall - 1)

    def at(self, kind, i, j):
        w, t = len(self.rows), len(self.cols)
        base = {
            "own": 0,
            "row": 1,
            "col": 1 + 2 * w,
            "half0": 1 + 2 * w + 2 * t,
            "half1": 1 + 2 * w + 2 * t + 2 * w * t,
        }[kind]
        if kind == "own":
            return self.sems.at[0]
        k = j - 1 if kind == "row" else i - 1 if kind == "col" else (i - 1) * w + j - 1
        return self.sems.at[base + 2 * k], self.sems.at[base + 2 * k + 1]

    def rank(self, i, j):
        net = self.net
        return ((net.a + i) % net.tall) * net.wide + (net.b + j) % net.wide

    def back(self, i, j):
        net = self.net
        return ((net.a - i + net.tall) % net.tall) * net.wide + (net.b - j + net.wide) % net.wide

    def own(self):
        return pltpu.make_async_copy(self.src, self.part(self.net.f, None), self.at("own", 0, 0))

    def first(self, i, j):
        send, recv = self.at("row" if i == 0 else "col", i, j)
        return put(self.src, self.part(self.net.f, None), send, recv, fsdp=self.rank(i, j))

    def came(self, i, j):
        send, recv = self.at("row" if i == 0 else "col", i, j)
        place = self.part(self.back(i, j), None)
        return put(place, place, send, recv, fsdp=self.rank(i, j))

    def second(self, half, i, j, came=False):
        send, recv = self.at("half0" if half == 0 else "half1", i, j)
        origin = self.back(i, j) if came else self.back(0, j) if half == 0 else self.back(i, 0)
        place = self.part(origin, half)
        return put(place, place, send, recv, fsdp=self.rank(i, 0) if half == 0 else self.rank(0, j))

    def start(self):
        self.own().start()
        for i in self.cols:
            self.first(i, 0).start()
        for j in self.rows:
            self.first(0, j).start()

    def relay(self):
        for j in self.rows:
            self.came(0, j).wait_recv()
            for i in self.cols:
                self.second(0, i, j).start()
        for i in self.cols:
            self.came(i, 0).wait_recv()
            for j in self.rows:
                self.second(1, i, j).start()

    def finish(self):
        self.own().wait()
        for j in self.rows:
            self.first(0, j).wait_send()
        for i in self.cols:
            self.first(i, 0).wait_send()
        for i in self.cols:
            for j in self.rows:
                for half in range(2):
                    self.second(half, i, j, came=True).wait_recv()
                    self.second(half, i, j).wait_send()


class Line:
    def __init__(self, net, src, part, recv, send, local):
        self.net, self.src, self.part, self.recv, self.send, self.local = net, src, part, recv, send, local
        self.pieces = recv.shape[1]
        self.rows = src.shape[0] // self.pieces

    @staticmethod
    def sems(n_s, pieces=2):
        return [
            pltpu.SemaphoreType.DMA((n_s, pieces)),
            pltpu.SemaphoreType.DMA((4, n_s // 2, pieces)),
            pltpu.SemaphoreType.DMA((1,)),
        ]

    def cut(self, ref, piece):
        return ref.at[aligned(piece * self.rows, self.rows)]

    def own(self):
        return pltpu.make_async_copy(self.src, self.part(self.net.s), self.local.at[0])

    def on_line(self, src, chunk, side, hop, piece):
        return put(
            self.cut(src, piece),
            self.cut(self.part(chunk), piece),
            self.send.at[side, hop, piece],
            self.recv.at[chunk, piece],
            seq=self.net.s + 2 - 4 * side,
        )

    def to_mate(self, src, chunk, side, hop, piece):
        return put(
            self.cut(src, piece),
            self.cut(self.part(chunk), piece),
            self.send.at[2 + side, hop, piece],
            self.recv.at[chunk, piece],
            seq=self.net.mate,
        )

    def goes_on(self, side):
        after = self.net.z + 1 - 2 * side
        return (after >= 0) & (after < self.net.n_l)

    def each_piece(self, act):
        pl.loop(0, self.pieces)(act)

    def start(self):
        net = self.net

        @self.each_piece
        def _(piece):
            for side in range(2):

                @pl.when(self.goes_on(side))
                def _():
                    self.on_line(self.src, net.s, side, 0, piece).start()

            self.to_mate(self.src, net.s, 0, 0, piece).start()

        self.own().start()

    def came(self, chunk, piece):
        place = self.cut(self.part(chunk), piece)
        put(place, place, self.send.at[0, 0, 0], self.recv.at[chunk, piece], seq=self.net.mate).wait_recv()

    def step(self, hop):
        net = self.net

        @self.each_piece
        def _(piece):
            def act(other, side):
                chunk = 2 * other + net.c
                self.came(chunk, piece)

                @pl.when(self.goes_on(side))
                def _():
                    self.on_line(self.part(chunk), chunk, side, hop, piece).start()

                self.to_mate(self.part(chunk), chunk, side, hop, piece).start()

            net.sides(hop, act)

    def pair(self, other):
        @self.each_piece
        def _(piece):
            self.came(2 * other + 1 - self.net.c, piece)

    def here(self):
        self.own().wait()
        self.pair(self.net.z)

    def finish(self):
        net = self.net

        @self.each_piece
        def _(piece):
            for side in range(2):

                @pl.when(self.goes_on(side))
                def _():
                    self.on_line(self.src, net.s, side, 0, piece).wait_send()

            self.to_mate(self.src, net.s, 0, 0, piece).wait_send()

            @pl.loop(1, net.n_l)
            def _(hop):
                def act(other, side):
                    chunk = 2 * other + net.c

                    @pl.when(self.goes_on(side))
                    def _():
                        self.on_line(self.part(chunk), chunk, side, hop, piece).wait_send()

                    self.to_mate(self.part(chunk), chunk, side, hop, piece).wait_send()

                net.sides(hop, act)


class Packets:
    def __init__(self, net, src, buf, sems):
        self.net, self.src, self.buf, self.sems = net, src, buf, sems

    @staticmethod
    def count(n_f, n_s):
        return 1 + 2 * (n_f - 1) + 2 * (n_s - 1)

    def own(self):
        net = self.net
        return pltpu.make_async_copy(self.src, self.buf.at[net.s, net.f], self.sems.at[0])

    def one(self, k, came=False):
        net = self.net
        f = (net.f - k + net.n_f) % net.n_f if came else net.f
        place = self.buf.at[net.s, f]
        return put(
            place if came else self.src,
            place,
            self.sems.at[2 * k - 1],
            self.sems.at[2 * k],
            fsdp=(net.f + k) % net.n_f,
        )

    def two(self, k, came=False):
        net = self.net
        place = self.buf.at[(net.s - k + net.n_s) % net.n_s if came else net.s]
        at = 2 * (net.n_f - 1) + 2 * k - 1
        return put(place, place, self.sems.at[at], self.sems.at[at + 1], seq=(net.s + k) % net.n_s)

    def start(self):
        self.own().start()
        for k in range(1, self.net.n_f):
            self.one(k).start()

    def middle(self):
        self.own().wait()
        for k in range(1, self.net.n_f):
            self.one(k, came=True).wait_recv()
            self.one(k).wait_send()
        for k in range(1, self.net.n_s):
            self.two(k).start()

    def finish(self):
        for k in range(1, self.net.n_s):
            self.two(k, came=True).wait_recv()
            self.two(k).wait_send()

    def unpack(self, out, width):
        net = self.net
        per = 128 // width
        for tile in range(net.n_f * net.n_s // per):
            total = None
            for j in range(per):
                f, s = divmod(tile * per + j, net.n_s)
                piece = self.buf[s, f]
                if j:
                    piece = pltpu.roll(piece, j * width, axis=1)
                total = piece if total is None else total + piece
            out[:, tile * 128 : (tile + 1) * 128] = total


def rotary(values, cosine, sine_next, sine_last):
    columns = values.shape[1]
    half = ROT // 2
    times = columns // 128

    def wide(table):
        return table if times == 1 else jnp.concatenate([table] * times, axis=1)

    following = pltpu.roll(values, columns - half, axis=1)
    previous = pltpu.roll(values, half, axis=1)
    return values * wide(cosine) + following * wide(sine_next) + previous * wide(sine_last)


def rotary_tables(length):
    half = ROT // 2
    freqs = np.float32(10000.0) ** (-np.arange(half, dtype=np.float32) * np.float32(2.0 / ROT))
    angles = np.arange(length, dtype=np.float32)[:, None] * freqs[None, :].astype(np.float32)
    cosine, sine = np.cos(angles), np.sin(angles)
    rest = np.zeros((length, HEAD - ROT), np.float32)
    none = np.zeros_like(sine)
    keep = np.concatenate([cosine, cosine, rest + 1], 1)
    following = np.concatenate([-sine, none, rest], 1)
    previous = np.concatenate([none, sine, rest], 1)
    return [np.tile(t, (1, 128 // HEAD)).astype(np.float32) for t in (keep, following, previous)]


def normalize(values):
    center = values - jnp.mean(values, -1, keepdims=True)
    inverse = lax.rsqrt(jnp.mean(center * center, -1, keepdims=True) + EPSILON)
    return center * inverse, inverse


class Copies:
    def __init__(self, sems):
        self.sems, self.all, self.open = sems, [], []

    def start(self, src, dst):
        copy = pltpu.make_async_copy(src, dst, self.sems.at[len(self.all)])
        copy.start()
        self.all.append(copy)
        self.open.append(copy)
        return copy

    def wait(self, *copies):
        for copy in copies or list(self.open):
            copy.wait()
            self.open.remove(copy)


def columns_of(ref, depth):
    half_rows = ref.shape[0] // 2

    def part(f, half):
        span = aligned(f * depth, depth)
        if half is None:
            return ref.at[:, span]
        return ref.at[pl.ds(half * half_rows, half_rows), span]

    return part


def rows_of(ref, chunk):
    return lambda s: ref.at[aligned(s * chunk, chunk)]


class Fold:
    def __init__(self, net, tile, total, mate_in, coming, mate_out, out, mate_send, mate_recv, send, recv):
        self.net, self.tile, self.total = net, tile, total
        self.mate_in, self.coming, self.mate_out, self.out = mate_in, coming, mate_out, out
        self.mate_send, self.mate_recv, self.send, self.recv = mate_send, mate_recv, send, recv
        self.chunk = total.shape[0]
        self.pieces = recv.shape[1]
        self.rows = self.chunk // self.pieces

    @staticmethod
    def shared(chunk, width):
        return [pltpu.VMEM((2 * chunk, TILE), F32), pltpu.VMEM((chunk, width), F32)]

    @staticmethod
    def buffers(n_s, chunk, width):
        n_l = n_s // 2
        return [
            pltpu.VMEM((n_l, chunk, width), BF),
            pltpu.VMEM((n_l + 1, chunk, width), BF),
            pltpu.VMEM((2, 2, chunk, width), BF),
            pltpu.VMEM((n_l, chunk, width), BF),
        ]

    @staticmethod
    def sems(n_s, pieces=4):
        n_l = n_s // 2
        return [
            pltpu.SemaphoreType.DMA((2, 2, pieces)),
            pltpu.SemaphoreType.DMA((n_l, pieces)),
            pltpu.SemaphoreType.DMA((n_l, pieces)),
            pltpu.SemaphoreType.DMA((n_l + 1, pieces)),
        ]

    def place(self, other):
        return (other >= 0) & (other < self.net.n_l)

    def fed(self, side):
        return self.place(self.net.z + 1 - 2 * side)

    def span(self, piece):
        return aligned(piece * self.rows, self.rows)

    def each_piece(self, act):
        pl.loop(0, self.pieces)(act)

    def to_mate(self, target, side, hop, piece):
        span = self.span(piece)
        return put(
            self.mate_out.at[side, hop % 2, span],
            self.mate_in.at[target, span],
            self.mate_send.at[side, hop % 2, piece],
            self.mate_recv.at[target, piece],
            seq=self.net.mate,
        )

    def onward(self, target, side, hop, piece):
        span = self.span(piece)
        slot = target + (self.net.n_l - target) * (1 - side) * (1 // hop)
        return put(
            self.out.at[target, span],
            self.coming.at[slot, span],
            self.send.at[target, piece],
            self.recv.at[slot, piece],
            seq=self.net.s + 4 * side - 2,
        )

    def came(self, slot, piece):
        place = self.coming.at[slot, self.span(piece)]
        put(place, place, self.send.at[0, 0], self.recv.at[slot, piece], seq=self.net.mate).wait_recv()

    def mate_sent(self, target, side, hop):
        @pl.when(self.place(target))
        def _():
            self.each_piece(lambda piece: self.to_mate(target, side, hop, piece).wait_send())

    def begin_one(self, target, side, hop, produce):
        self.mate_sent(target + 4 * side - 2, side, hop)
        mine = aligned(self.net.c * self.chunk, self.chunk)
        theirs = aligned((1 - self.net.c) * self.chunk, self.chunk)

        def write(cols, value):
            self.tile[...] = value
            self.out[target, :, cols] = self.tile[mine, :].astype(BF)
            self.mate_out[side, hop % 2, :, cols] = self.tile[theirs, :].astype(BF)

        produce(target, write)
        self.each_piece(lambda piece: self.to_mate(target, side, hop, piece).start())

    def begin(self, produce):
        net = self.net

        @pl.loop(0, net.n_l - 1)
        def _(j):
            hop = net.n_l - 1 - j

            def act(target, side):
                self.begin_one(target, side, hop, produce)

                @pl.when(jnp.logical_not(self.fed(side)))
                def _():
                    self.pass_on(target, side, hop, False)

            net.sides(hop, act)

        self.begin_one(net.z, 0, 0, produce)

    def pass_on(self, target, side, hop, fed):
        @self.each_piece
        def _(piece):
            self.to_mate(target, 0, 0, piece).wait_recv()
            span = self.span(piece)
            value = self.out[target, span, :].astype(F32) + self.mate_in[target, span, :].astype(F32)
            if fed:
                self.came(target, piece)
                value = value + self.coming[target, span, :].astype(F32)
            self.out[target, span, :] = value.astype(BF)
            self.onward(target, side, hop, piece).start()

    def step(self, hop):
        def act(target, side):
            @pl.when(self.fed(side))
            def _():
                self.pass_on(target, side, hop, True)

        self.net.sides(hop, act)

    def last(self):
        net = self.net

        @self.each_piece
        def _(piece):
            self.to_mate(net.z, 0, 0, piece).wait_recv()
            span = self.span(piece)
            self.total[span, :] = self.out[net.z, span, :].astype(F32) + self.mate_in[net.z, span, :].astype(F32)
            for fed, slot in ((net.z > 0, net.z), (net.z < net.n_l - 1, net.n_l)):

                @pl.when(fed)
                def _():
                    self.came(slot, piece)
                    self.total[span, :] = self.total[span, :] + self.coming[slot, span, :].astype(F32)

    def finish(self):
        net = self.net
        self.mate_sent(net.z, 0, 0)
        self.mate_sent(net.z - 1, 0, 1)
        self.mate_sent(net.z + 1, 1, 1)
        self.mate_sent(net.z + 2, 1, 2)

        @pl.loop(1, net.n_l)
        def _(hop):
            net.sides(
                hop,
                lambda target, side: self.each_piece(
                    lambda piece: self.onward(target, side, hop, piece).wait_send()
                ),
            )


class GridSum:
    def __init__(self, net, stage, came, sems):
        self.net, self.stage, self.came, self.sems = net, stage, came, sems
        self.half = stage.shape[1] // 2
        self.rows = next(r for r in (176, 128, 96, 64, 32, 16) if self.half % r == 0)
        self.cols = range(1, net.tall)
        self.along = range(1, net.wide)
        self.bases = self.layout(net.n_f)

    @staticmethod
    def layout(n_f):
        tall = 2 if n_f % 2 == 0 else 1
        wide = n_f // tall
        sizes = [(wide - 1) * tall, (tall - 1) * wide, tall - 1, wide - 1]
        return [sum(sizes[:at]) for at in range(5)]

    @staticmethod
    def scratch(n_f, rows, columns):
        count = GridSum.layout(n_f)[4]
        return [
            pltpu.VMEM((n_f, rows, columns), BF),
            pltpu.VMEM((count, rows // 2, columns), BF),
            pltpu.SemaphoreType.DMA((2, count)),
        ]

    def slot(self, kind, i, j):
        base = self.bases[kind]
        return base + [(j - 1) * self.net.tall + i, (i - 1) * self.net.wide + j, i - 1, j - 1][kind]

    def rank(self, i, j):
        net = self.net
        return ((net.a + i) % net.tall) * net.wide + (net.b + j) % net.wide

    def owner(self, at):
        return self.rank(at // self.net.wide, at % self.net.wide)

    def copy(self, kind, i, j):
        half = kind % 2
        along = kind in (0, 3)
        slot = self.slot(kind, i, j)
        at = i * self.net.wide + j
        return put(
            self.stage.at[at, pl.ds(half * self.half, self.half)],
            self.came.at[slot],
            self.sems.at[0, slot],
            self.sems.at[1, slot],
            fsdp=self.rank(0, j) if along else self.rank(i, 0),
        )

    def first(self, at):
        i, j = at // self.net.wide, at % self.net.wide

        @pl.when(j > 0)
        def _():
            self.copy(0, i, j).start()

        @pl.when(i > 0)
        def _():
            self.copy(1, i, j).start()

    def gather(self, half, at, slots, write):
        @pl.loop(0, self.half // self.rows)
        def _(step):
            span = aligned(half * self.half + step * self.rows, self.rows, 16)
            value = self.stage[at, span, :].astype(F32)
            for slot in slots:
                value = value + self.came[slot, aligned(step * self.rows, self.rows, 16), :].astype(F32)
            write(span, value)

    def wait(self, *copies):
        for kind, i, j in copies:
            self.copy(kind, i, j).wait_recv()
        return [self.slot(*copy) for copy in copies]

    def second(self):
        def keep(at):
            def write(span, value):
                self.stage[at, span, :] = value.astype(BF)

            return write

        for i in self.cols:
            at = i * self.net.wide
            self.gather(0, at, self.wait(*[(0, i, j) for j in self.along]), keep(at))
            self.copy(2, i, 0).start()
        for j in self.along:
            self.gather(1, j, self.wait(*[(1, i, j) for i in self.cols]), keep(j))
            self.copy(3, 0, j).start()

    def last(self, out):
        def write(span, value):
            out[span, :] = value

        self.gather(
            0, 0, self.wait(*[(0, 0, j) for j in self.along], *[(2, i, 0) for i in self.cols]), write
        )
        self.gather(
            1, 0, self.wait(*[(1, i, 0) for i in self.cols], *[(3, 0, j) for j in self.along]), write
        )

    def finish(self):
        net = self.net
        for i in range(net.tall):
            for j in range(net.wide):
                if j:
                    self.copy(0, i, j).wait_send()
                if i:
                    self.copy(1, i, j).wait_send()
        for i in self.cols:
            self.copy(2, i, 0).wait_send()
        for j in self.along:
            self.copy(3, 0, j).wait_send()


class PacketSum:
    def __init__(self, net, out, seq_in, total, fsdp_in, sems):
        self.net, self.out, self.seq_in, self.total, self.fsdp_in, self.sems = net, out, seq_in, total, fsdp_in, sems

    @staticmethod
    def scratch(n_f, n_s):
        return [
            pltpu.VMEM((n_s, n_f, SMALL, 128), F32),
            pltpu.VMEM((n_s, n_f, SMALL, 128), F32),
            pltpu.VMEM((n_f, SMALL, 128), F32),
            pltpu.VMEM((n_f, SMALL, 128), F32),
            pltpu.SemaphoreType.DMA((2 * (n_f + n_s),)),
        ]

    def one(self, k):
        to = (self.net.s + k) % self.net.n_s
        return put(self.out.at[to], self.seq_in.at[k], self.sems.at[2 * k], self.sems.at[2 * k + 1], seq=to)

    def two(self, k):
        to = (self.net.f + k) % self.net.n_f
        at = 2 * (self.net.n_s + k)
        return put(self.total.at[to], self.fsdp_in.at[k], self.sems.at[at], self.sems.at[at + 1], fsdp=to)

    def run(self, terms, result, width):
        net = self.net
        per = 128 // width
        for tile in range(net.n_f * net.n_s // per):
            value = terms[:, tile * 128 : (tile + 1) * 128]
            for j in range(per):
                f, s = divmod(tile * per + j, net.n_s)
                self.out[s, f] = pltpu.roll(value, 128 - j * width, axis=1) if j else value
        for k in range(1, net.n_s):
            self.one(k).start()
        total = self.out[net.s]
        for k in range(1, net.n_s):
            self.one(k).wait()
            total = total + self.seq_in[k]
        self.total[...] = total
        for k in range(1, net.n_f):
            self.two(k).start()
        total = self.total[net.f]
        for k in range(1, net.n_f):
            self.two(k).wait()
            total = total + self.fsdp_in[k]
        result[...] = total


def norm_backward(rows, source, grad, gain, terms, at, write):
    terms[at : at + 2, :] = jnp.zeros((2, terms.shape[1]), F32)

    @pl.loop(0, rows // 32)
    def _(i):
        span = aligned(i * 32, 32)
        scaled, inverse = normalize(source[span, :].astype(F32))
        value = grad[span, :]
        upstream = value * gain
        inner = jnp.mean(upstream, -1, keepdims=True)
        cross = jnp.mean(upstream * scaled, -1, keepdims=True)
        terms[at : at + 1, :] = terms[at : at + 1, :] + jnp.sum(value * scaled, 0, keepdims=True)
        terms[at + 1 : at + 2, :] = terms[at + 1 : at + 2, :] + jnp.sum(value, 0, keepdims=True)
        write(span, inverse * (upstream - inner - scaled * cross))


def forward_kernel(
    tok,
    packet,
    wq_own,
    wo_own,
    wg_own,
    wu_own,
    wd_own,
    gout_own,
    cosine,
    sine_next,
    sine_last,
    q_o,
    k_o,
    kt_o,
    v_o,
    att_o,
    lse_o,
    n1_o,
    gains_o,
    wq_o,
    wo_o,
    wg_o,
    wu_o,
    wd_o,
    gout_o,
    n2_o,
    hidden_o,
    dgate_o,
    dup_o,
    mid_o,
    rows,
    n1,
    gout,
    wq,
    wo,
    wg,
    wu,
    wd,
    q,
    k,
    kt,
    v,
    vt,
    ot,
    att,
    hidden,
    dgate,
    dup,
    mid,
    tok_in,
    n2_own,
    packets,
    tiles,
    total,
    *rest,
):
    net = Net()
    chunk, width = tok.shape
    length = chunk * net.n_s
    depth = wq_own.shape[1]
    columns = wq_own.shape[2]
    heads = columns // HEAD
    pair = 2 * chunk
    block = 256
    buffers, rest = rest[:4], rest[4:]
    fold_sems, rest = rest[:4], rest[4:]
    tok_sems, rest = rest[:3], rest[3:]
    gout_sems, rest = rest[:3], rest[3:]
    n2_sems, rest = rest[:3], rest[3:]
    spread_sems, rest = rest[:5], rest[5:]
    pk_sems, copy_sems = rest
    copies = Copies(copy_sems)

    tok_copy = copies.start(tok, tok_in)
    net.barrier()

    def wq_part(f, half):
        if half is None:
            return wq.at[:, aligned(f * depth, depth), :]
        return wq.at[:, aligned(f * depth + half * (depth // 2), depth // 2), :]

    spread_q = Spread(net, wq_own, wq_part, spread_sems[0])
    spread_o, spread_g, spread_u, spread_d = [
        Spread(net, own, columns_of(full, depth), sems)
        for own, full, sems in zip((wo_own, wg_own, wu_own, wd_own), (wo, wg, wu, wd), spread_sems[1:])
    ]
    pk = Packets(net, packet, packets, pk_sems)
    line = Line(net, tok, rows_of(rows, chunk), *tok_sems)
    gout_line = Line(net, gout_own, rows_of(gout, chunk), *gout_sems)
    n2_line = Line(net, n2_own, rows_of(rows, chunk), *n2_sems)
    fold = Fold(net, tiles, total, *buffers, *fold_sems)

    pk.start()
    line.start()
    spread_q.start()
    pk.middle()
    pk.finish()
    pk.unpack(gains_o, width // (net.n_f * net.n_s))

    def norm_block(other):
        gain, shift = gains_o[0:1, :], gains_o[1:2, :]

        @pl.loop(0, pair // 32)
        def _(i):
            span = aligned(other * pair + i * 32, 32)
            scaled, _ = normalize(rows[span, :].astype(F32))
            n1[span, :] = (scaled * gain + shift).astype(BF)

    def project_block(other):
        span = aligned(other * pair, pair)
        left = n1[span, :]
        cols = aligned(net.s * columns, columns)
        tables = cosine[span, :], sine_next[span, :], sine_last[span, :]
        for kind in range(3):
            value = dot(left, wq[kind]) + gains_o[4 + kind : 5 + kind, cols]
            if kind == 0:
                q[span, :] = rotary(value, *tables).astype(BF)
            elif kind == 1:
                value = rotary(value, *tables)
                k[span, :] = value.astype(BF)
                kt[:, span] = value.T.astype(BF)
            else:
                v[span, :] = value.astype(BF)
                vt[:, span] = value.T.astype(BF)

    line.here()
    norm_block(net.z)

    def hop_norm(hop):
        line.step(hop)

        def act(other, side):
            line.pair(other)
            norm_block(other)

        net.sides(hop, act)

    for hop in range(1, net.n_l - 1):
        hop_norm(hop)
        if hop == 1:
            spread_o.start()
            spread_g.start()
            spread_q.relay()
    spread_q.finish()

    @pl.loop(0, net.n_l - 1)
    def _(hop):
        def act(other, side):
            @pl.when((hop > 0) | (side == 0))
            def _():
                project_block(other)

        net.sides(hop, act)

    spread_u.start()
    spread_o.relay()
    hop_norm(net.n_l - 1)
    gout_line.start()
    net.sides(net.n_l - 1, lambda other, side: project_block(other))
    for pair_of in ((n1, n1_o), (wq, wq_o), (q, q_o), (k, k_o), (kt, kt_o), (v, v_o)):
        copies.start(*pair_of)

    @pl.loop(0, heads)
    def _(head):
        lane = lax.broadcasted_iota(jnp.int32, (1, columns), 1)
        here = jnp.where(lane // HEAD == head, HEAD**-0.5, 0.0).astype(BF)
        visible = lax.broadcasted_iota(jnp.int32, (block, block), 0) <= lax.broadcasted_iota(
            jnp.int32, (block, block), 1
        )
        head_rows = aligned(head * HEAD, HEAD)
        for i in range(length // block):
            lo, hi = i * block, (i + 1) * block
            query = q[lo:hi, :] * here
            near = jnp.where(visible, dot_nt(k[lo:hi, :], query), NEG_LARGE)
            highest = jnp.max(near, 0, keepdims=True)
            if i:
                far = dot_nt(k[0:lo, :], query)
                highest = jnp.maximum(highest, jnp.max(far, 0, keepdims=True))
            near = jnp.exp(near - highest)
            total = jnp.sum(near, 0, keepdims=True)
            out = dot(vt[head_rows, lo:hi], near.astype(BF))
            if i:
                far = jnp.exp(far - highest)
                total = total + jnp.sum(far, 0, keepdims=True)
                out = out + dot(vt[head_rows, 0:lo], far.astype(BF))
            ot[head_rows, lo:hi] = out / total
            lse_o[pl.ds(head, 1), lo:hi] = highest + jnp.log(total)

    for i in range(length // block):
        att[i * block : (i + 1) * block, :] = ot[:, i * block : (i + 1) * block].T.astype(BF)

    spread_o.finish()
    spread_g.relay()
    spread_d.start()
    line.finish()
    copies.start(att, att_o)
    copies.start(wo, wo_o)

    def produce_attended(place, write):
        left = att[aligned(place * pair, pair), :]

        @pl.loop(0, width // TILE)
        def _(j):
            cols = aligned(j * TILE, TILE)
            write(cols, dot(left, wo[:, cols]))

    gout_line.step(1)
    fold.begin(produce_attended)
    spread_u.relay()
    for hop in range(net.n_l - 2, 0, -1):
        fold.step(hop)
        gout_line.step(net.n_l - hop)
    fold.last()
    copies.wait(tok_copy)
    gain_two, shift_two = gains_o[2:3, :], gains_o[3:4, :]

    @pl.loop(0, chunk // 32)
    def _(i):
        span = aligned(i * 32, 32)
        value = tok_in[span, :].astype(F32) + total[span, :]
        mid[span, :] = value
        scaled, _ = normalize(value)
        n2_own[span, :] = (scaled * gain_two + shift_two).astype(BF)

    n2_line.start()
    spread_d.relay()
    fold.finish()
    copies.start(mid, mid_o)
    gout_line.here()

    @pl.loop(1, net.n_l)
    def _(hop):
        net.sides(hop, lambda other, side: gout_line.pair(other))

    copies.start(gout, gout_o)

    def forward_block(other):
        span = aligned(other * pair, pair)
        right = rows[span, :]
        gate = dot_nt(wg[...], right)
        up = dot_nt(wu[...], right)
        back = dot_nt(wd[...], gout[span, :])
        sigma = jax.nn.sigmoid(gate)
        active = gate * sigma
        hidden[:, span] = (active * up).astype(BF)
        dgate[:, span] = (back * up * (sigma * (1.0 + gate * (1.0 - sigma)))).astype(BF)
        dup[:, span] = (back * active).astype(BF)

    n2_line.here()

    @pl.loop(1, net.n_l - 1)
    def _(hop):
        n2_line.step(hop)
        net.sides(hop, lambda other, side: n2_line.pair(other))

    for spread in (spread_g, spread_u, spread_d):
        spread.finish()
    for pair_of in ((wg, wg_o), (wu, wu_o), (wd, wd_o)):
        copies.start(*pair_of)

    @pl.loop(0, net.n_l - 1)
    def _(hop):
        def act(other, side):
            @pl.when((hop > 0) | (side == 0))
            def _():
                forward_block(other)

        net.sides(hop, act)

    n2_line.step(net.n_l - 1)

    def last_block(other, side):
        n2_line.pair(other)
        forward_block(other)

    net.sides(net.n_l - 1, last_block)
    for pair_of in ((dgate, dgate_o), (dup, dup_o), (hidden, hidden_o), (rows, n2_o)):
        copies.start(*pair_of)
    gout_line.finish()
    n2_line.finish()
    copies.wait()


def forward_part(tokens, packet, wq, wo, wg, wu, wd, gout, tables):
    chunk, width = tokens.shape
    n_f, n_s = lax.axis_size("fsdp"), lax.axis_size("seq")
    length = chunk * n_s
    columns = wq.shape[2]
    units = wg.shape[0]
    shape = jax.ShapeDtypeStruct
    wide, head, turned = (length, width), (length, columns), (units, length)
    return pl.pallas_call(
        forward_kernel,
        name="forward",
        out_shape=[
            shape(head, BF),
            shape(head, BF),
            shape((columns, length), BF),
            shape(head, BF),
            shape(head, BF),
            shape((8, length), F32),
            shape(wide, BF),
            shape((SMALL, width), F32),
            shape((3, width, columns), BF),
            shape((columns, width), BF),
            *[shape((units, width), BF)] * 3,
            shape(wide, BF),
            shape(wide, BF),
            *[shape(turned, BF)] * 3,
            shape((chunk, width), F32),
        ],
        in_specs=[ANY, VMEM, *[ANY] * 6, VMEM, VMEM, VMEM],
        out_specs=[*[ANY] * 5, VMEM, ANY, VMEM, *[ANY] * 11],
        scratch_shapes=[
            pltpu.VMEM(wide, BF),
            pltpu.VMEM(wide, BF),
            pltpu.VMEM(wide, BF),
            pltpu.VMEM((3, width, columns), BF),
            pltpu.VMEM((columns, width), BF),
            *[pltpu.VMEM((units, width), BF)] * 3,
            pltpu.VMEM(head, BF),
            pltpu.VMEM(head, BF),
            pltpu.VMEM((columns, length), BF),
            pltpu.VMEM(head, BF),
            pltpu.VMEM((columns, length), BF),
            pltpu.VMEM((columns, length), F32),
            pltpu.VMEM(head, BF),
            *[pltpu.VMEM(turned, BF)] * 3,
            pltpu.VMEM((chunk, width), F32),
            pltpu.VMEM((chunk, width), BF),
            pltpu.VMEM((chunk, width), BF),
            pltpu.VMEM((n_s, n_f, SMALL, 128), F32),
            *Fold.shared(chunk, width),
            *Fold.buffers(n_s, chunk, width),
            *Fold.sems(n_s),
            *Line.sems(n_s),
            *Line.sems(n_s),
            *Line.sems(n_s),
            *[pltpu.SemaphoreType.DMA((Spread.count(n_f),))] * 5,
            pltpu.SemaphoreType.DMA((Packets.count(n_f, n_s),)),
            pltpu.SemaphoreType.DMA((20,)),
        ],
        compiler_params=pltpu.CompilerParams(
            collective_id=1, has_side_effects=True, vmem_limit_bytes=VMEM_BYTES
        ),
        cost_estimate=pl.CostEstimate(
            flops=2 * length * width * (4 * columns + 3 * units),
            bytes_accessed=8 * length * width,
            transcendentals=length * (length * columns // HEAD + units),
        ),
    )(tokens, packet, wq, wo, wg, wu, wd, gout, *tables)


def middle_kernel(
    dgate_in,
    dup_in,
    wg_in,
    wu_in,
    n2_in,
    hidden_in,
    gout_in,
    wd_in,
    mid,
    gains,
    gout_own,
    dmid_o,
    top_o,
    terms_o,
    dm_o,
    gate_o,
    up_o,
    down_o,
    dgate,
    dup,
    wg,
    wu,
    n2,
    hidden,
    gout,
    wd,
    dmid_low,
    tiles,
    total,
    *rest,
):
    net = Net()
    chunk, width = mid.shape
    pair = 2 * chunk
    depth = width // net.n_f
    first_buffers, rest = rest[:4], rest[4:]
    last_buffers, rest = rest[:4], rest[4:]
    first_sems, rest = rest[:4], rest[4:]
    last_sems, rest = rest[:4], rest[4:]
    dm_sems, rest = rest[:3], rest[3:]
    gate_sum, up_sum, down_sum = [GridSum(net, *rest[at : at + 3]) for at in (0, 3, 6)]
    sums = (down_sum, gate_sum, up_sum)
    copy_sems, column_sems = rest[9:]

    copies = Copies(copy_sems)
    loads = [
        copies.start(src, dst)
        for src, dst in (
            (dgate_in, dgate),
            (dup_in, dup),
            (wg_in, wg),
            (wu_in, wu),
            (hidden_in, hidden),
            (wd_in, wd),
        )
    ]
    net.barrier()
    dm_line = Line(net, dmid_low, rows_of(dm_o, chunk), *dm_sems)
    fold = Fold(net, tiles, total, *first_buffers, *first_sems)
    last = Fold(net, tiles, total, *last_buffers, *last_sems)

    def columns(at):
        cols = aligned(gate_sum.owner(at) * depth, depth)
        return [
            pltpu.make_async_copy(src.at[:, cols], dst.at[at % 2], column_sems.at[way, at % 2])
            for way, (src, dst) in enumerate(((n2_in, n2), (gout_in, gout)))
        ]

    def weight_terms(at):
        for copy in columns(at):
            copy.wait()
        down_sum.stage[at] = dot(hidden[...], gout[at % 2]).astype(BF)
        right = n2[at % 2]
        gate_sum.stage[at] = dot(dgate[...], right).astype(BF)
        up_sum.stage[at] = dot(dup[...], right).astype(BF)

        @pl.when(at >= 2)
        def _():
            for copy in columns(at - 2):
                copy.start()

        for grid_sum in sums:
            grid_sum.first(at)

    def produce_normed(place, write):
        span = aligned(place * pair, pair)
        left, right = dgate[:, span].T, dup[:, span].T

        @pl.loop(0, width // TILE)
        def _(j):
            cols = aligned(j * TILE, TILE)
            write(cols, dot(left, wg[:, cols]) + dot(right, wu[:, cols]))

    for at in range(net.n_f - 1, max(net.n_f - 3, -1), -1):
        for copy in columns(at):
            copy.start()
    copies.wait(*loads[:4])
    fold.begin(produce_normed)
    copies.wait(*loads[4:])
    steps = max(net.n_l - 2, 1)
    each = -(-(net.n_f - 1) // steps)
    for j in range(steps):

        @pl.loop(j * each, min((j + 1) * each, net.n_f - 1))
        def _(i):
            weight_terms(net.n_f - 1 - i)

        if j < net.n_l - 2:
            fold.step(net.n_l - 2 - j)

    fold.last()

    def write_middle(span, value):
        value = value + gout_own[span, :].astype(F32)
        dmid_o[span, :] = value
        dmid_low[span, :] = value.astype(BF)

    terms_o[...] = jnp.zeros(terms_o.shape, F32)
    norm_backward(chunk, mid, total, gains[2:3, :], terms_o, 2, write_middle)
    dm_line.start()
    fold.finish()

    def produce_top(place, write):
        left = hidden[:, aligned(place * pair, pair)].T

        @pl.loop(0, width // TILE)
        def _(j):
            cols = aligned(j * TILE, TILE)
            write(cols, dot(left, wd[:, cols]))

    last.begin(produce_top)
    weight_terms(0)
    dm_line.step(1)
    for hop in range(net.n_l - 2, 0, -1):
        last.step(hop)
        dm_line.step(net.n_l - hop)
        if hop == net.n_l - 2:
            for grid_sum in sums:
                grid_sum.second()
    last.last()

    @pl.loop(0, chunk // 32)
    def _(i):
        span = aligned(i * 32, 32)
        top_o[span, :] = (mid[span, :] + total[span, :]).astype(BF)

    last.finish()
    dm_line.here()

    @pl.loop(1, net.n_l)
    def _(hop):
        net.sides(hop, lambda other, side: dm_line.pair(other))

    dm_line.finish()
    for grid_sum, out in zip(sums, (down_o, gate_o, up_o)):
        grid_sum.last(out)
    for grid_sum in sums:
        grid_sum.finish()


def middle_part(dgate, dup, wg, wu, n2, hidden, gout_rows, wd, mid, gains, gout):
    chunk, width = mid.shape
    n_f, n_s = lax.axis_size("fsdp"), lax.axis_size("seq")
    length = chunk * n_s
    units = wg.shape[0]
    depth = width // n_f
    shape = jax.ShapeDtypeStruct
    buffers = Fold.buffers(n_s, chunk, width)
    wide, turned, weight = (length, width), (units, length), (units, width)
    return pl.pallas_call(
        middle_kernel,
        name="middle",
        out_shape=[
            shape((chunk, width), F32),
            shape((chunk, width), BF),
            shape((SMALL, width), F32),
            shape(wide, BF),
            *[shape((units, depth), F32)] * 3,
        ],
        in_specs=[ANY] * 8 + [VMEM] * 3,
        out_specs=[VMEM] * 3 + [ANY] + [VMEM] * 3,
        scratch_shapes=[
            pltpu.VMEM(turned, BF),
            pltpu.VMEM(turned, BF),
            pltpu.VMEM(weight, BF),
            pltpu.VMEM(weight, BF),
            pltpu.VMEM((2, length, depth), BF),
            pltpu.VMEM(turned, BF),
            pltpu.VMEM((2, length, depth), BF),
            pltpu.VMEM(weight, BF),
            pltpu.VMEM((chunk, width), BF),
            *Fold.shared(chunk, width),
            *buffers,
            *buffers,
            *Fold.sems(n_s),
            *Fold.sems(n_s),
            *Line.sems(n_s),
            *GridSum.scratch(n_f, units, depth) * 3,
            pltpu.SemaphoreType.DMA((6,)),
            pltpu.SemaphoreType.DMA((2, 2)),
        ],
        compiler_params=pltpu.CompilerParams(
            collective_id=2, has_side_effects=True, vmem_limit_bytes=VMEM_BYTES
        ),
        cost_estimate=pl.CostEstimate(
            flops=2 * length * width * units * 6, bytes_accessed=8 * length * width, transcendentals=0
        ),
    )(dgate, dup, wg, wu, n2, hidden, gout_rows, wd, mid, gains, gout)


def back_kernel(
    dm_in,
    wo_in,
    att_in,
    q_in,
    k_in,
    kt_in,
    v_in,
    n1_in,
    wq_in,
    lse,
    tok,
    dmid,
    gains,
    terms_in,
    cosine,
    sine_next,
    sine_last,
    gin_o,
    small_o,
    out_o,
    qkv_o,
    dm,
    wo,
    att,
    q,
    k,
    kt,
    v,
    n1,
    wq,
    datt,
    dk,
    dv,
    dqt,
    dproj,
    terms,
    tiles,
    total,
    *rest,
):
    net = Net()
    chunk, width = tok.shape
    length, columns = q_in.shape
    heads = columns // HEAD
    pair = 2 * chunk
    depth = width // net.n_f
    block = 256
    buffers, rest = rest[:4], rest[4:]
    fold_sems, rest = rest[:4], rest[4:]
    packet_scratch, rest = rest[:5], rest[5:]
    out_sum, qkv_sum = GridSum(net, *rest[:3]), GridSum(net, *rest[3:6])
    copy_sems = rest[6]

    copies = Copies(copy_sems)
    loads = [
        copies.start(src, dst)
        for src, dst in (
            (dm_in, dm),
            (wo_in, wo),
            (att_in, att),
            (q_in, q),
            (k_in, k),
            (kt_in, kt),
            (v_in, v),
            (n1_in, n1),
            (wq_in, wq),
        )
    ]
    net.barrier()
    copies.wait(*loads[:3])

    @pl.loop(0, length // block)
    def _(i):
        span = aligned(i * block, block)
        datt[span, :] = dot_nt(dm[span, :], wo[...]).astype(BF)
        dk[span, :] = jnp.zeros((block, columns), F32)
        dv[span, :] = jnp.zeros((block, columns), F32)

    copies.wait()

    @pl.loop(0, heads)
    def _(head):
        lane = lax.broadcasted_iota(jnp.int32, (1, columns), 1)
        here = jnp.where(lane // HEAD == head, 1.0, 0.0).astype(BF)
        scale = HEAD**-0.5
        visible = lax.broadcasted_iota(jnp.int32, (block, block), 0) <= lax.broadcasted_iota(
            jnp.int32, (block, block), 1
        )
        head_rows = aligned(head * HEAD, HEAD)
        for i in range(length // block):
            lo, hi = i * block, (i + 1) * block
            query = q[lo:hi, :] * (here * scale)
            upstream = datt[lo:hi, :] * here
            logsum = lse[pl.ds(head, 1), lo:hi]

            def part(at, end, mask):
                probs = jnp.exp(dot_nt(k[at:end, :], query) - logsum)
                if mask:
                    probs = jnp.where(visible, probs, 0.0)
                grads = dot_nt(v[at:end, :], upstream)
                dv[at:end, :] = dv[at:end, :] + dot(probs.astype(BF), upstream)
                return probs, grads, jnp.sum(probs * grads, 0, keepdims=True)

            def scored(at, end, probs, grads, inner):
                scores = (probs * (grads - inner)).astype(BF)
                dk[at:end, :] = dk[at:end, :] + dot(scores, query)
                return dot(kt[head_rows, at:end], scores)

            near, near_grads, inner = part(lo, hi, True)
            if i:
                far, far_grads, more = part(0, lo, False)
                inner = inner + more
            out = scored(lo, hi, near, near_grads, inner)
            if i:
                out = out + scored(0, lo, far, far_grads, inner)
            dqt[head_rows, lo:hi] = out * scale

    terms[...] = terms_in[...]
    bias_cols = aligned(net.s * columns, columns)

    @pl.loop(0, length // block)
    def _(i):
        span = aligned(i * block, block)
        tables = cosine[span, :], -sine_next[span, :], -sine_last[span, :]
        parts = [
            rotary(dqt[:, span].T.astype(BF).astype(F32), *tables).astype(BF),
            rotary(dk[span, :].astype(BF).astype(F32), *tables).astype(BF),
            dv[span, :].astype(BF),
        ]
        for kind in range(3):
            dproj[kind, span, :] = parts[kind]
            row = slice(4 + kind, 5 + kind)
            terms[row, bias_cols] = terms[row, bias_cols] + jnp.sum(parts[kind].astype(F32), 0, keepdims=True)

    def weight_terms(at):
        cols = aligned(qkv_sum.owner(at) * depth, depth)
        left = n1[:, cols].T
        for kind in range(3):
            qkv_sum.stage[at, kind * depth : (kind + 1) * depth, :] = dot(left, dproj[kind]).astype(BF)
        qkv_sum.first(at)
        out_sum.stage[at] = dot_tn(att[...], dm[:, cols]).astype(BF)
        out_sum.first(at)

    def produce(place, write):
        span = aligned(place * pair, pair)

        @pl.loop(0, width // TILE)
        def _(j):
            cols = aligned(j * TILE, TILE)
            value = dot_nt(dproj[0, span, :], wq[0, cols, :])
            for kind in range(1, 3):
                value = value + dot_nt(dproj[kind, span, :], wq[kind, cols, :])
            write(cols, value)

    fold = Fold(net, tiles, total, *buffers, *fold_sems)
    fold.begin(produce)
    steps = max(net.n_l - 2, 1)
    each = -(-(net.n_f - 1) // steps)
    for j in range(steps):

        @pl.loop(j * each, min((j + 1) * each, net.n_f - 1))
        def _(i):
            weight_terms(net.n_f - 1 - i)

        if j < net.n_l - 2:
            fold.step(net.n_l - 2 - j)

    weight_terms(0)
    for grid_sum in (qkv_sum, out_sum):
        grid_sum.second()
    fold.last()

    def write_input(span, value):
        gin_o[span, :] = value + dmid[span, :]

    norm_backward(chunk, tok, total, gains[0:1, :], terms, 0, write_input)
    PacketSum(net, *packet_scratch).run(terms, small_o, width // (net.n_f * net.n_s))
    fold.finish()
    for grid_sum, out in ((qkv_sum, qkv_o), (out_sum, out_o)):
        grid_sum.last(out)
        grid_sum.finish()


def back_part(dm, wo, att, q, k, kt, v, n1, wq, lse, tokens, dmid, gains, terms, tables):
    chunk, width = tokens.shape
    n_f, n_s = lax.axis_size("fsdp"), lax.axis_size("seq")
    length, columns = q.shape
    depth = width // n_f
    shape = jax.ShapeDtypeStruct
    return pl.pallas_call(
        back_kernel,
        name="back",
        out_shape=[
            shape((chunk, width), F32),
            shape((SMALL, 128), F32),
            shape((columns, depth), F32),
            shape((3 * depth, columns), F32),
        ],
        in_specs=[ANY] * 9 + [VMEM] * 8,
        out_specs=[VMEM] * 4,
        scratch_shapes=[
            pltpu.VMEM((length, width), BF),
            pltpu.VMEM((columns, width), BF),
            pltpu.VMEM((length, columns), BF),
            pltpu.VMEM((length, columns), BF),
            pltpu.VMEM((length, columns), BF),
            pltpu.VMEM((columns, length), BF),
            pltpu.VMEM((length, columns), BF),
            pltpu.VMEM((length, width), BF),
            pltpu.VMEM((3, width, columns), BF),
            pltpu.VMEM((length, columns), BF),
            pltpu.VMEM((length, columns), F32),
            pltpu.VMEM((length, columns), F32),
            pltpu.VMEM((columns, length), F32),
            pltpu.VMEM((3, length, columns), BF),
            pltpu.VMEM((SMALL, width), F32),
            *Fold.shared(chunk, width),
            *Fold.buffers(n_s, chunk, width),
            *Fold.sems(n_s),
            *PacketSum.scratch(n_f, n_s),
            *GridSum.scratch(n_f, columns, depth),
            *GridSum.scratch(n_f, 3 * depth, columns),
            pltpu.SemaphoreType.DMA((9,)),
        ],
        compiler_params=pltpu.CompilerParams(
            collective_id=3, has_side_effects=True, vmem_limit_bytes=VMEM_BYTES
        ),
        cost_estimate=pl.CostEstimate(
            flops=2 * length * columns * (8 * width + 5 * length),
            bytes_accessed=4 * length * width,
            transcendentals=length * length * columns // HEAD,
        ),
    )(dm, wo, att, q, k, kt, v, n1, wq, lse, tokens, dmid, gains, terms, *tables)


def per_device(
    tokens,
    gain_one,
    shift_one,
    w_qkv,
    b_qkv,
    w_out,
    gain_two,
    shift_two,
    w_gate,
    w_up,
    w_down,
    grad_output,
):
    length = tokens.shape[1] * lax.axis_size("seq")
    width = gain_one.shape[0]
    packet = jnp.concatenate(
        [jnp.stack([gain_one, shift_one, gain_two, shift_two]), b_qkv, jnp.zeros((1, width), BF)]
    )
    packet = jnp.pad(packet.astype(F32), ((0, 0), (0, 128 - width)))
    tables = rotary_tables(length)
    (q, k, kt, v, att, lse, n1, gains, wq, wo, wg, wu, wd, gout, n2, hidden, dgate, dup, mid) = forward_part(
        tokens[0], packet, w_qkv.transpose(1, 0, 2), w_out, w_gate.T, w_up.T, w_down, grad_output[0], tables
    )
    dmid, top, terms, dm, gate, up, down = middle_part(
        dgate, dup, wg, wu, n2, hidden, gout, wd, mid, gains, grad_output[0]
    )
    grad_input, small, out, qkv = back_part(
        dm, wo, att, q, k, kt, v, n1, wq, lse, tokens[0], dmid, gains, terms, tables
    )

    return (
        top[None],
        grad_input[None],
        small[0, :width],
        small[1, :width],
        qkv.reshape(3, -1, qkv.shape[1]).transpose(1, 0, 2),
        small[4:7, :width],
        out,
        small[2, :width],
        small[3, :width],
        gate.T,
        up.T,
        down,
    )


def solution(mesh):
    whole = P(("fsdp", "seq"))
    rows = P("fsdp", "seq", None)
    inner = P("seq", "fsdp")
    outer = P("fsdp", "seq")
    heads = P("fsdp", None, "seq")
    bias = P(None, ("fsdp", "seq"))
    return jax.shard_map(
        per_device,
        mesh=mesh,
        in_specs=(rows, whole, whole, heads, bias, inner, whole, whole, outer, outer, inner, rows),
        out_specs=(rows, rows, whole, whole, heads, bias, inner, whole, whole, outer, outer, inner),
        check_vma=False,
    )
```

```python
import functools

import jax
import jax.numpy as jnp
import numpy as np
from jax import lax
from jax.experimental import pallas as pl
from jax.experimental.pallas import tpu as pltpu
from jax.sharding import PartitionSpec as P

HEAD = 64
ROT = 16
EPSILON = 1e-05
NEG_LARGE = -1e30
MESH = pl.DeviceIdType.MESH
ANY = pl.BlockSpec(memory_space=pl.ANY)
VMEM = pl.BlockSpec(memory_space=pltpu.VMEM)
BF = jnp.bfloat16
F32 = jnp.float32
VMEM_BYTES = 60 * 2**20
TILE = 512
SMALL = 8


def put(src, dst, send, recv, **device):
    return pltpu.make_async_remote_copy(
        src_ref=src, dst_ref=dst, send_sem=send, recv_sem=recv, device_id=device, device_id_type=MESH
    )


def dot(left, right):
    return jnp.dot(left, right, preferred_element_type=F32)


def dot_nt(left, right):
    return lax.dot_general(left, right, (((1,), (1,)), ((), ())), preferred_element_type=F32)


def dot_tn(left, right):
    return lax.dot_general(left, right, (((0,), (0,)), ((), ())), preferred_element_type=F32)


def aligned(start, size, unit=None):
    return pl.ds(pl.multiple_of(start, unit or size), size)


class Net:
    def __init__(self):
        self.n_f, self.n_s = lax.axis_size("fsdp"), lax.axis_size("seq")
        self.tall = 2 if self.n_f % 2 == 0 else 1
        self.wide = self.n_f // self.tall
        self.n_l = self.n_s // 2
        self.f, self.s = lax.axis_index("fsdp"), lax.axis_index("seq")
        self.a, self.b = self.f // self.wide, self.f % self.wide
        self.z, self.c = self.s // 2, self.s % 2
        self.mate = self.s + 1 - 2 * self.c

    def barrier(self):
        sem = pltpu.get_barrier_semaphore()
        for k in range(1, self.n_f):
            pl.semaphore_signal(
                sem, inc=1, device_id={"fsdp": (self.f + k) % self.n_f}, device_id_type=MESH
            )
        for k in range(1, self.n_s):
            pl.semaphore_signal(
                sem, inc=1, device_id={"seq": (self.s + k) % self.n_s}, device_id_type=MESH
            )
        pl.semaphore_wait(sem, self.n_f + self.n_s - 2)

    def sides(self, hop, act):
        @pl.loop(0, 2)
        def _(side):
            other = self.z + (2 * side - 1) * hop

            @pl.when((other >= 0) & (other < self.n_l))
            def _():
                act(other, side)


class Spread:
    def __init__(self, net, src, part, sems):
        self.net, self.src, self.part, self.sems = net, src, part, sems
        self.rows = [j for j in range(1, net.wide)]
        self.cols = [i for i in range(1, net.tall)]

    @staticmethod
    def count(n_f):
        tall = 2 if n_f % 2 == 0 else 1
        wide = n_f // tall
        return 1 + 2 * (wide - 1) + 2 * (tall - 1) + 4 * (wide - 1) * (tall - 1)

    def at(self, kind, i, j):
        w, t = len(self.rows), len(self.cols)
        base = {
            "own": 0,
            "row": 1,
            "col": 1 + 2 * w,
            "half0": 1 + 2 * w + 2 * t,
            "half1": 1 + 2 * w + 2 * t + 2 * w * t,
        }[kind]
        if kind == "own":
            return self.sems.at[0]
        k = j - 1 if kind == "row" else i - 1 if kind == "col" else (i - 1) * w + j - 1
        return self.sems.at[base + 2 * k], self.sems.at[base + 2 * k + 1]

    def rank(self, i, j):
        net = self.net
        return ((net.a + i) % net.tall) * net.wide + (net.b + j) % net.wide

    def back(self, i, j):
        net = self.net
        return ((net.a - i + net.tall) % net.tall) * net.wide + (net.b - j + net.wide) % net.wide

    def own(self):
        return pltpu.make_async_copy(self.src, self.part(self.net.f, None), self.at("own", 0, 0))

    def first(self, i, j):
        send, recv = self.at("row" if i == 0 else "col", i, j)
        return put(self.src, self.part(self.net.f, None), send, recv, fsdp=self.rank(i, j))

    def came(self, i, j):
        send, recv = self.at("row" if i == 0 else "col", i, j)
        place = self.part(self.back(i, j), None)
        return put(place, place, send, recv, fsdp=self.rank(i, j))

    def second(self, half, i, j, came=False):
        send, recv = self.at("half0" if half == 0 else "half1", i, j)
        origin = self.back(i, j) if came else self.back(0, j) if half == 0 else self.back(i, 0)
        place = self.part(origin, half)
        return put(place, place, send, recv, fsdp=self.rank(i, 0) if half == 0 else self.rank(0, j))

    def start(self):
        self.own().start()
        for i in self.cols:
            self.first(i, 0).start()
        for j in self.rows:
            self.first(0, j).start()

    def relay(self):
        for j in self.rows:
            self.came(0, j).wait_recv()
            for i in self.cols:
                self.second(0, i, j).start()
        for i in self.cols:
            self.came(i, 0).wait_recv()
            for j in self.rows:
                self.second(1, i, j).start()

    def finish(self):
        self.own().wait()
        for j in self.rows:
            self.first(0, j).wait_send()
        for i in self.cols:
            self.first(i, 0).wait_send()
        for i in self.cols:
            for j in self.rows:
                for half in range(2):
                    self.second(half, i, j, came=True).wait_recv()
                    self.second(half, i, j).wait_send()


class Line:
    def __init__(self, net, src, part, recv, send, local):
        self.net, self.src, self.part, self.recv, self.send, self.local = net, src, part, recv, send, local
        self.pieces = recv.shape[1]
        self.rows = src.shape[0] // self.pieces

    @staticmethod
    def sems(n_s, pieces=2):
        return [
            pltpu.SemaphoreType.DMA((n_s, pieces)),
            pltpu.SemaphoreType.DMA((4, n_s // 2, pieces)),
            pltpu.SemaphoreType.DMA((1,)),
        ]

    def cut(self, ref, piece):
        return ref.at[aligned(piece * self.rows, self.rows)]

    def own(self):
        return pltpu.make_async_copy(self.src, self.part(self.net.s), self.local.at[0])

    def on_line(self, src, chunk, side, hop, piece):
        return put(
            self.cut(src, piece),
            self.cut(self.part(chunk), piece),
            self.send.at[side, hop, piece],
            self.recv.at[chunk, piece],
            seq=self.net.s + 2 - 4 * side,
        )

    def to_mate(self, src, chunk, side, hop, piece):
        return put(
            self.cut(src, piece),
            self.cut(self.part(chunk), piece),
            self.send.at[2 + side, hop, piece],
            self.recv.at[chunk, piece],
            seq=self.net.mate,
        )

    def goes_on(self, side):
        after = self.net.z + 1 - 2 * side
        return (after >= 0) & (after < self.net.n_l)

    def each_piece(self, act):
        pl.loop(0, self.pieces)(act)

    def start(self):
        net = self.net

        @self.each_piece
        def _(piece):
            for side in range(2):

                @pl.when(self.goes_on(side))
                def _():
                    self.on_line(self.src, net.s, side, 0, piece).start()

            self.to_mate(self.src, net.s, 0, 0, piece).start()

        self.own().start()

    def came(self, chunk, piece):
        place = self.cut(self.part(chunk), piece)
        put(place, place, self.send.at[0, 0, 0], self.recv.at[chunk, piece], seq=self.net.mate).wait_recv()

    def step(self, hop):
        net = self.net

        @self.each_piece
        def _(piece):
            def act(other, side):
                chunk = 2 * other + net.c
                self.came(chunk, piece)

                @pl.when(self.goes_on(side))
                def _():
                    self.on_line(self.part(chunk), chunk, side, hop, piece).start()

                self.to_mate(self.part(chunk), chunk, side, hop, piece).start()

            net.sides(hop, act)

    def pair(self, other):
        @self.each_piece
        def _(piece):
            self.came(2 * other + 1 - self.net.c, piece)

    def here(self):
        self.own().wait()
        self.pair(self.net.z)

    def finish(self):
        net = self.net

        @self.each_piece
        def _(piece):
            for side in range(2):

                @pl.when(self.goes_on(side))
                def _():
                    self.on_line(self.src, net.s, side, 0, piece).wait_send()

            self.to_mate(self.src, net.s, 0, 0, piece).wait_send()

            @pl.loop(1, net.n_l)
            def _(hop):
                def act(other, side):
                    chunk = 2 * other + net.c

                    @pl.when(self.goes_on(side))
                    def _():
                        self.on_line(self.part(chunk), chunk, side, hop, piece).wait_send()

                    self.to_mate(self.part(chunk), chunk, side, hop, piece).wait_send()

                net.sides(hop, act)


class Packets:
    def __init__(self, net, src, buf, sems):
        self.net, self.src, self.buf, self.sems = net, src, buf, sems

    @staticmethod
    def count(n_f, n_s):
        return 1 + 2 * (n_f - 1) + 2 * (n_s - 1)

    def own(self):
        net = self.net
        return pltpu.make_async_copy(self.src, self.buf.at[net.s, net.f], self.sems.at[0])

    def one(self, k, came=False):
        net = self.net
        f = (net.f - k + net.n_f) % net.n_f if came else net.f
        place = self.buf.at[net.s, f]
        return put(
            place if came else self.src,
            place,
            self.sems.at[2 * k - 1],
            self.sems.at[2 * k],
            fsdp=(net.f + k) % net.n_f,
        )

    def two(self, k, came=False):
        net = self.net
        place = self.buf.at[(net.s - k + net.n_s) % net.n_s if came else net.s]
        at = 2 * (net.n_f - 1) + 2 * k - 1
        return put(place, place, self.sems.at[at], self.sems.at[at + 1], seq=(net.s + k) % net.n_s)

    def start(self):
        self.own().start()
        for k in range(1, self.net.n_f):
            self.one(k).start()

    def middle(self):
        self.own().wait()
        for k in range(1, self.net.n_f):
            self.one(k, came=True).wait_recv()
            self.one(k).wait_send()
        for k in range(1, self.net.n_s):
            self.two(k).start()

    def finish(self):
        for k in range(1, self.net.n_s):
            self.two(k, came=True).wait_recv()
            self.two(k).wait_send()

    def unpack(self, out, width):
        net = self.net
        per = 128 // width
        for tile in range(net.n_f * net.n_s // per):
            total = None
            for j in range(per):
                f, s = divmod(tile * per + j, net.n_s)
                piece = self.buf[s, f]
                if j:
                    piece = pltpu.roll(piece, j * width, axis=1)
                total = piece if total is None else total + piece
            out[:, tile * 128 : (tile + 1) * 128] = total


def rotary(values, cosine, sine):
    columns = values.shape[1]
    half = ROT // 2
    times = columns // 128

    def wide(table):
        return table if times == 1 else jnp.concatenate([table] * times, axis=1)

    lane = lax.broadcasted_iota(jnp.int32, values.shape, 1)
    other = jnp.where(
        lane % HEAD < half, pltpu.roll(values, columns - half, axis=1), pltpu.roll(values, half, axis=1)
    )
    return values * wide(cosine) + other * wide(sine)


def rotary_tables(length):
    half = ROT // 2
    freqs = np.float32(10000.0) ** (-np.arange(half, dtype=np.float32) * np.float32(2.0 / ROT))
    angles = np.arange(length, dtype=np.float32)[:, None] * freqs[None, :].astype(np.float32)
    cosine, sine = np.cos(angles), np.sin(angles)
    rest = np.zeros((length, HEAD - ROT), np.float32)
    keep = np.concatenate([cosine, cosine, rest + 1], 1)
    swap = np.concatenate([-sine, sine, rest], 1)
    return [np.tile(t, (1, 128 // HEAD)).astype(np.float32) for t in (keep, swap)]


def normalize(values):
    center = values - jnp.mean(values, -1, keepdims=True)
    inverse = lax.rsqrt(jnp.mean(center * center, -1, keepdims=True) + EPSILON)
    return center * inverse, inverse


class Copies:
    def __init__(self, sems):
        self.sems, self.all, self.open = sems, [], []

    def start(self, src, dst):
        copy = pltpu.make_async_copy(src, dst, self.sems.at[len(self.all)])
        copy.start()
        self.all.append(copy)
        self.open.append(copy)
        return copy

    def wait(self, *copies):
        for copy in copies or list(self.open):
            copy.wait()
            self.open.remove(copy)


def columns_of(ref, depth):
    half_rows = ref.shape[0] // 2

    def part(f, half):
        span = aligned(f * depth, depth)
        if half is None:
            return ref.at[:, span]
        return ref.at[pl.ds(half * half_rows, half_rows), span]

    return part


def rows_of(ref, chunk):
    return lambda s: ref.at[aligned(s * chunk, chunk)]


class Fold:
    def __init__(self, net, tile, total, mate_in, coming, mate_out, out, mate_send, mate_recv, send, recv):
        self.net, self.tile, self.total = net, tile, total
        self.mate_in, self.coming, self.mate_out, self.out = mate_in, coming, mate_out, out
        self.mate_send, self.mate_recv, self.send, self.recv = mate_send, mate_recv, send, recv
        self.chunk = total.shape[0]
        self.pieces = recv.shape[1]
        self.rows = self.chunk // self.pieces

    @staticmethod
    def shared(chunk, width):
        return [pltpu.VMEM((2 * chunk, TILE), F32), pltpu.VMEM((chunk, width), F32)]

    @staticmethod
    def buffers(n_s, chunk, width):
        n_l = n_s // 2
        return [
            pltpu.VMEM((n_l, chunk, width), BF),
            pltpu.VMEM((n_l + 1, chunk, width), BF),
            pltpu.VMEM((3, chunk, width), BF),
            pltpu.VMEM((n_l, chunk, width), BF),
        ]

    @staticmethod
    def sems(n_s, pieces=4):
        n_l = n_s // 2
        return [
            pltpu.SemaphoreType.DMA((3, pieces)),
            pltpu.SemaphoreType.DMA((n_l, pieces)),
            pltpu.SemaphoreType.DMA((n_l, pieces)),
            pltpu.SemaphoreType.DMA((n_l + 1, pieces)),
        ]

    def place(self, other):
        return (other >= 0) & (other < self.net.n_l)

    def fed(self, side):
        return self.place(self.net.z + 1 - 2 * side)

    def span(self, piece):
        return aligned(piece * self.rows, self.rows)

    def each_piece(self, act):
        pl.loop(0, self.pieces)(act)

    def to_mate(self, target, slot, piece):
        span = self.span(piece)
        return put(
            self.mate_out.at[slot, span],
            self.mate_in.at[target, span],
            self.mate_send.at[slot, piece],
            self.mate_recv.at[target, piece],
            seq=self.net.mate,
        )

    def onward(self, target, side, hop, piece):
        span = self.span(piece)
        slot = target + (self.net.n_l - target) * (1 - side) * (1 // hop)
        return put(
            self.out.at[target, span],
            self.coming.at[slot, span],
            self.send.at[target, piece],
            self.recv.at[slot, piece],
            seq=self.net.s + 4 * side - 2,
        )

    def came(self, slot, piece):
        place = self.coming.at[slot, self.span(piece)]
        put(place, place, self.send.at[0, 0], self.recv.at[slot, piece], seq=self.net.mate).wait_recv()

    def mate_sent(self, slot):
        self.each_piece(lambda piece: self.to_mate(self.net.z, slot, piece).wait_send())

    def begin_one(self, target, slot, produce):
        mine = aligned(self.net.c * self.chunk, self.chunk)
        theirs = aligned((1 - self.net.c) * self.chunk, self.chunk)

        def write(cols, value):
            self.tile[...] = value
            self.out[target, :, cols] = self.tile[mine, :].astype(BF)
            self.mate_out[slot, :, cols] = self.tile[theirs, :].astype(BF)

        produce(target, write)
        self.each_piece(lambda piece: self.to_mate(target, slot, piece).start())

    def leave(self, target, side, hop):
        @pl.when((hop > 0) & jnp.logical_not(self.fed(side)))
        def _():
            self.each_piece(lambda piece: self.pass_piece(target, side, hop, piece, False))

    def begin(self, produce):
        net = self.net

        @pl.loop(0, net.n_l)
        def _(j):
            hop = net.n_l - 1 - j

            def act(target, side):
                @pl.when((hop > 0) | (side == 0))
                def _():
                    @pl.when((hop > 0) & self.place(target + 2 * side - 1))
                    def _():
                        self.mate_sent(side)

                    self.begin_one(target, side + (2 - side) * (1 // (hop + 1)), produce)
                    self.leave(target, side, hop)

            net.sides(hop, act)

    def pass_piece(self, target, side, hop, piece, fed):
        self.to_mate(target, 0, piece).wait_recv()
        span = self.span(piece)
        value = self.out[target, span, :].astype(F32) + self.mate_in[target, span, :].astype(F32)
        if fed:
            self.came(target, piece)
            value = value + self.coming[target, span, :].astype(F32)
        self.out[target, span, :] = value.astype(BF)
        self.onward(target, side, hop, piece).start()

    def open_total(self):
        net = self.net

        @self.each_piece
        def _(piece):
            self.to_mate(net.z, 0, piece).wait_recv()
            span = self.span(piece)
            self.total[span, :] = self.out[net.z, span, :].astype(F32) + self.mate_in[net.z, span, :].astype(F32)

    def wave(self, at, near=False, between=None):
        net = self.net
        above = at if near else net.n_l - at

        @self.each_piece
        def _(piece):
            span = self.span(piece)

            @pl.loop(0, 2)
            def _(side):
                target = net.n_l - 1 - above + (2 * above - net.n_l + 1) * side
                hop = (target - net.z) * (2 * side - 1)

                @pl.when(self.fed(side) & (hop > 0))
                def _():
                    self.pass_piece(target, side, hop, piece, True)

                @pl.when(self.fed(side) & (hop == 0))
                def _():
                    slot = net.z + (net.n_l - net.z) * (1 - side)
                    self.came(slot, piece)
                    self.total[span, :] = self.total[span, :] + self.coming[slot, span, :].astype(F32)

            if between is not None:
                between((at - 1) * self.pieces + piece)

    def finish(self):
        net = self.net
        self.mate_sent(2)
        for side in range(2):
            pl.when(self.place(net.z + 2 * side - 1))(functools.partial(self.mate_sent, side))

        @pl.loop(1, net.n_l)
        def _(hop):
            net.sides(
                hop,
                lambda target, side: self.each_piece(
                    lambda piece: self.onward(target, side, hop, piece).wait_send()
                ),
            )


class GridSum:
    def __init__(self, net, stage, came, sems):
        self.net, self.stage, self.came, self.sems = net, stage, came, sems
        self.half = stage.shape[1] // 2
        self.rows = next(r for r in (176, 128, 96, 64, 32, 16) if self.half % r == 0)
        self.cols = range(1, net.tall)
        self.along = range(1, net.wide)
        self.bases = self.layout(net.n_f)

    @staticmethod
    def layout(n_f):
        tall = 2 if n_f % 2 == 0 else 1
        wide = n_f // tall
        sizes = [(wide - 1) * tall, (tall - 1) * wide, tall - 1, wide - 1]
        return [sum(sizes[:at]) for at in range(5)]

    @staticmethod
    def scratch(n_f, rows, columns):
        count = GridSum.layout(n_f)[4]
        return [
            pltpu.VMEM((n_f, rows, columns), BF),
            pltpu.VMEM((count, rows // 2, columns), BF),
            pltpu.SemaphoreType.DMA((2, count + 1)),
        ]

    def slot(self, kind, i, j):
        base = self.bases[kind]
        return base + [(j - 1) * self.net.tall + i, (i - 1) * self.net.wide + j, i - 1, j - 1][kind]

    def rank(self, i, j):
        net = self.net
        return ((net.a + i) % net.tall) * net.wide + (net.b + j) % net.wide

    def owner(self, at):
        return self.rank(at // self.net.wide, at % self.net.wide)

    def copy(self, kind, i, j):
        half = kind % 2
        along = kind in (0, 3)
        slot = self.slot(kind, i, j)
        at = i * self.net.wide + j
        return put(
            self.stage.at[at, pl.ds(half * self.half, self.half)],
            self.came.at[slot],
            self.sems.at[0, slot],
            self.sems.at[1, slot],
            fsdp=self.rank(0, j) if along else self.rank(i, 0),
        )

    def first(self, at):
        i, j = at // self.net.wide, at % self.net.wide

        @pl.when(j > 0)
        def _():
            self.copy(0, i, j).start()

        @pl.when(i > 0)
        def _():
            self.copy(1, i, j).start()

    def gather(self, half, at, slots, write):
        @pl.loop(0, self.half // self.rows)
        def _(step):
            span = aligned(half * self.half + step * self.rows, self.rows, 16)
            value = self.stage[at, span, :].astype(F32)
            for slot in slots:
                value = value + self.came[slot, aligned(step * self.rows, self.rows, 16), :].astype(F32)
            write(span, value)

    def wait(self, *copies):
        for kind, i, j in copies:
            self.copy(kind, i, j).wait_recv()
        return [self.slot(*copy) for copy in copies]

    def second(self):
        def keep(at):
            def write(span, value):
                self.stage[at, span, :] = value.astype(BF)

            return write

        for i in self.cols:
            at = i * self.net.wide
            self.gather(0, at, self.wait(*[(0, i, j) for j in self.along]), keep(at))
            self.copy(2, i, 0).start()
        for j in self.along:
            self.gather(1, j, self.wait(*[(1, i, j) for i in self.cols]), keep(j))
            self.copy(3, 0, j).start()

    def last(self, write, done=None):
        self.gather(
            0, 0, self.wait(*[(0, 0, j) for j in self.along], *[(2, i, 0) for i in self.cols]), write
        )
        if done is not None:
            done(0)
        self.gather(
            1, 0, self.wait(*[(1, i, 0) for i in self.cols], *[(3, 0, j) for j in self.along]), write
        )
        if done is not None:
            done(1)

    def result(self, out, half):
        span = pl.ds(half * self.half, self.half)
        return pltpu.make_async_copy(self.stage.at[0, span], out.at[span], self.sems.at[half, self.bases[4]])

    def last_to(self, out):
        def write(span, value):
            out[span, :] = value

        self.last(write)

    def last_in_place(self, out):
        def write(span, value):
            self.stage[0, span, :] = value.astype(BF)

        self.last(write, lambda half: self.result(out, half).start())

    def finish(self):
        net = self.net
        for i in range(net.tall):
            for j in range(net.wide):
                if j:
                    self.copy(0, i, j).wait_send()
                if i:
                    self.copy(1, i, j).wait_send()
        for i in self.cols:
            self.copy(2, i, 0).wait_send()
        for j in self.along:
            self.copy(3, 0, j).wait_send()


class PacketSum:
    def __init__(self, net, out, seq_in, total, fsdp_in, sems):
        self.net, self.out, self.seq_in, self.total, self.fsdp_in, self.sems = net, out, seq_in, total, fsdp_in, sems

    @staticmethod
    def scratch(n_f, n_s):
        return [
            pltpu.VMEM((n_s, n_f, SMALL, 128), F32),
            pltpu.VMEM((n_s, n_f, SMALL, 128), F32),
            pltpu.VMEM((n_f, SMALL, 128), F32),
            pltpu.VMEM((n_f, SMALL, 128), F32),
            pltpu.SemaphoreType.DMA((2 * (n_f + n_s),)),
        ]

    def one(self, k):
        to = (self.net.s + k) % self.net.n_s
        return put(self.out.at[to], self.seq_in.at[k], self.sems.at[2 * k], self.sems.at[2 * k + 1], seq=to)

    def two(self, k):
        to = (self.net.f + k) % self.net.n_f
        at = 2 * (self.net.n_s + k)
        return put(self.total.at[to], self.fsdp_in.at[k], self.sems.at[at], self.sems.at[at + 1], fsdp=to)

    def run(self, terms, result, width):
        net = self.net
        per = 128 // width
        for tile in range(net.n_f * net.n_s // per):
            value = terms[:, tile * 128 : (tile + 1) * 128]
            for j in range(per):
                f, s = divmod(tile * per + j, net.n_s)
                self.out[s, f] = pltpu.roll(value, 128 - j * width, axis=1) if j else value
        for k in range(1, net.n_s):
            self.one(k).start()
        total = self.out[net.s]
        for k in range(1, net.n_s):
            self.one(k).wait()
            total = total + self.seq_in[k]
        self.total[...] = total
        for k in range(1, net.n_f):
            self.two(k).start()
        total = self.total[net.f]
        for k in range(1, net.n_f):
            self.two(k).wait()
            total = total + self.fsdp_in[k]
        result[...] = total


def norm_backward(rows, source, grad, gain, terms, at, write):
    terms[at : at + 2, :] = jnp.zeros((2, terms.shape[1]), F32)

    @pl.loop(0, rows // 32)
    def _(i):
        span = aligned(i * 32, 32)
        scaled, inverse = normalize(source[span, :].astype(F32))
        value = grad[span, :]
        upstream = value * gain
        inner = jnp.mean(upstream, -1, keepdims=True)
        cross = jnp.mean(upstream * scaled, -1, keepdims=True)
        terms[at : at + 1, :] = terms[at : at + 1, :] + jnp.sum(value * scaled, 0, keepdims=True)
        terms[at + 1 : at + 2, :] = terms[at + 1 : at + 2, :] + jnp.sum(value, 0, keepdims=True)
        write(i, span, inverse * (upstream - inner - scaled * cross))


def layer_kernel(
    tok,
    packet,
    wq_own,
    wo_own,
    wg_own,
    wu_own,
    wd_own,
    gout_own,
    cosine,
    sine,
    q_o,
    k_o,
    kt_o,
    v_o,
    att_o,
    lse_o,
    n1_o,
    gains_o,
    wq_o,
    wo_o,
    dm_o,
    dmid_o,
    top_o,
    terms_o,
    gate_o,
    up_o,
    down_o,
    rows,
    gout,
    wq,
    wo,
    wg,
    wu,
    wd,
    q,
    k,
    kt,
    v,
    vt,
    ot,
    att,
    hidden,
    dgate,
    dup,
    mid,
    low,
    packets,
    tiles,
    total,
    *rest,
):
    net = Net()
    chunk, width = tok.shape
    length = chunk * net.n_s
    depth = wq_own.shape[1]
    columns = wq_own.shape[2]
    heads = columns // HEAD
    pair = 2 * chunk
    buffers, rest = rest[:4], rest[4:]
    folds = []
    for _ in range(3):
        folds.append(Fold(net, tiles, total, *buffers, *rest[:4]))
        rest = rest[4:]
    att_fold, normed_fold, top_fold = folds
    line_sems = [rest[at : at + 3] for at in (0, 3, 6, 9)]
    rest = rest[12:]
    spread_sems, rest = rest[:5], rest[5:]
    gate_sum, up_sum, down_sum = [GridSum(net, *rest[at : at + 3]) for at in (0, 3, 6)]
    sums = (down_sum, gate_sum, up_sum)
    pk_sems, copy_sems, n1_sems = rest[9:]
    copies = Copies(copy_sems)
    n1 = att_fold.mate_out

    net.barrier()

    def wq_part(f, half):
        if half is None:
            return wq.at[:, aligned(f * depth, depth), :]
        return wq.at[:, aligned(f * depth + half * (depth // 2), depth // 2), :]

    spread_q = Spread(net, wq_own, wq_part, spread_sems[0])
    spread_o, spread_g, spread_u, spread_d = [
        Spread(net, own, columns_of(full, depth), sems)
        for own, full, sems in zip((wo_own, wg_own, wu_own, wd_own), (wo, wg, wu, wd), spread_sems[1:])
    ]
    pk = Packets(net, packet, packets, pk_sems)
    line = Line(net, tok, rows_of(rows, chunk), *line_sems[0])
    gout_line = Line(net, gout_own, rows_of(gout, chunk), *line_sems[1])
    n2_line = Line(net, low, rows_of(rows, chunk), *line_sems[2])
    dm_line = Line(net, low, rows_of(dm_o, chunk), *line_sems[3])

    def pairs(which, hop):
        net.sides(hop, lambda other, side: which.pair(other))

    def blocks(hop, act):
        def once(other, side):
            @pl.when((hop > 0) | (side == 0))
            def _():
                act(other, side)

        net.sides(hop, once)

    pk.start()
    line.start()
    spread_q.start()
    pk.middle()
    pk.finish()
    pk.unpack(gains_o, width // (net.n_f * net.n_s))

    def project_block(other, side):
        span = aligned(other * pair, pair)
        gain, shift = gains_o[0:1, :], gains_o[1:2, :]

        for part in range(2):

            @pl.loop(0, chunk // 32)
            def _(i):
                at = aligned((2 * other + part) * chunk + i * 32, 32)
                scaled, _ = normalize(rows[at, :].astype(F32))
                n1[part, aligned(i * 32, 32), :] = (scaled * gain + shift).astype(BF)

        keeps = [
            pltpu.make_async_copy(
                n1.at[part], n1_o.at[aligned((2 * other + part) * chunk, chunk)], n1_sems.at[part]
            )
            for part in range(2)
        ]
        for copy in keeps:
            copy.start()
        left = n1[0:2].reshape(pair, width)
        cols = aligned(net.s * columns, columns)
        tables = cosine[span, :], sine[span, :]
        for kind in range(3):
            value = dot(left, wq[kind]) + gains_o[4 + kind : 5 + kind, cols]
            if kind == 0:
                q[span, :] = rotary(value, *tables).astype(BF)
            elif kind == 1:
                value = rotary(value, *tables)
                k[span, :] = value.astype(BF)
                kt[...] = value.T.astype(BF)
            else:
                v[...] = value.astype(BF)
                vt[:, span] = value.T.astype(BF)
        for copy in (
            pltpu.make_async_copy(kt, kt_o.at[:, span], n1_sems.at[2]),
            pltpu.make_async_copy(v, v_o.at[span], n1_sems.at[3]),
        ):
            copy.start()
            keeps.append(copy)
        for copy in keeps:
            copy.wait()

    line.here()
    for hop in range(1, net.n_l - 1):
        line.step(hop)
        if hop == 1:
            spread_q.relay()
        pairs(line, hop)
    spread_o.start()
    spread_q.finish()
    pl.loop(0, net.n_l - 1)(lambda hop: blocks(hop, project_block))
    spread_o.relay()
    spread_g.start()
    line.step(net.n_l - 1)
    gout_line.start()
    pairs(line, net.n_l - 1)
    blocks(net.n_l - 1, project_block)
    spread_u.start()
    for pair_of in ((wq, wq_o), (q, q_o), (k, k_o)):
        copies.start(*pair_of)
    spread_o.finish()
    line.finish()

    def attend(i):
        lo, hi = i * pair, (i + 1) * pair

        @pl.loop(0, heads)
        def _(head):
            lane = lax.broadcasted_iota(jnp.int32, (1, columns), 1)
            here = jnp.where(lane // HEAD == head, HEAD**-0.5, 0.0).astype(BF)
            visible = lax.broadcasted_iota(jnp.int32, (pair, pair), 0) <= lax.broadcasted_iota(
                jnp.int32, (pair, pair), 1
            )
            head_rows = aligned(head * HEAD, HEAD)
            query = q[lo:hi, :] * here
            near = jnp.where(visible, dot_nt(k[lo:hi, :], query), NEG_LARGE)
            highest = jnp.max(near, 0, keepdims=True)
            if i:
                far = dot_nt(k[0:lo, :], query)
                highest = jnp.maximum(highest, jnp.max(far, 0, keepdims=True))
            near = jnp.exp(near - highest)
            sum_of = jnp.sum(near, 0, keepdims=True)
            out = dot(vt[head_rows, lo:hi], near.astype(BF))
            if i:
                far = jnp.exp(far - highest)
                sum_of = sum_of + jnp.sum(far, 0, keepdims=True)
                out = out + dot(vt[head_rows, 0:lo], far.astype(BF))
            ot[head_rows, :] = out / sum_of
            lse_o[pl.ds(head, 1), lo:hi] = highest + jnp.log(sum_of)

        att[lo:hi, :] = ot[...].T.astype(BF)

    def produce_attended(place, write):
        for i in range(net.n_l):
            pl.when(place == i)(functools.partial(attend, i))
        left = att[aligned(place * pair, pair), :]

        @pl.loop(0, width // TILE)
        def _(j):
            cols = aligned(j * TILE, TILE)
            write(cols, dot(left, wo[:, cols]))

    att_fold.begin(produce_attended)
    copies.start(att, att_o)
    copies.start(wo, wo_o)
    gout_line.step(1)
    spread_g.relay()
    spread_d.start()
    att_fold.open_total()
    for at in range(1, net.n_l):
        att_fold.wave(at)
        if at + 1 < net.n_l:
            gout_line.step(at + 1)
        if at == 1:
            spread_u.relay()
    spread_d.relay()
    gain_two, shift_two = gains_o[2:3, :], gains_o[3:4, :]

    @pl.loop(0, chunk // 32)
    def _(i):
        span = aligned(i * 32, 32)
        value = rows[aligned(net.s * chunk + i * 32, 32), :].astype(F32) + total[span, :]
        mid[span, :] = value
        scaled, _ = normalize(value)
        low[span, :] = (scaled * gain_two + shift_two).astype(BF)

    n2_line.start()
    att_fold.finish()
    gout_line.here()
    pl.loop(1, net.n_l)(lambda hop: pairs(gout_line, hop))

    def forward_block(other):
        span = aligned(other * pair, pair)
        right = rows[span, :]
        half = hidden.shape[0] // 2

        @pl.loop(0, 2)
        def _(part):
            units = aligned(part * half, half, 16)
            gate = dot_nt(wg[units, :], right)
            up = dot_nt(wu[units, :], right)
            back = dot_nt(wd[units, :], gout[span, :])
            sigma = jax.nn.sigmoid(gate)
            active = gate * sigma
            hidden[units, span] = (active * up).astype(BF)
            dgate[units, span] = (back * up * (sigma * (1.0 + gate * (1.0 - sigma)))).astype(BF)
            dup[units, span] = (back * active).astype(BF)

    def produce_normed(place, write):
        span = aligned(place * pair, pair)
        left, right = dgate[:, span].T, dup[:, span].T

        @pl.loop(0, width // TILE)
        def _(j):
            cols = aligned(j * TILE, TILE)
            write(cols, dot(left, wg[:, cols]) + dot(right, wu[:, cols]))

    def begin_normed(other, side, hop):
        @pl.when(hop > 1)
        def _():
            normed_fold.mate_sent(side)

        normed_fold.begin_one(other, side + (2 - side) * (1 // (hop + 1)), produce_normed)

    def forward_blocks(hop):
        def act(other, side):
            forward_block(other)

            @pl.when(jnp.logical_not(normed_fold.fed(side)))
            def _():
                begin_normed(other, side, hop)
                normed_fold.leave(other, side, hop)

        net.sides(hop, act)

    def begin_fed(hop):
        def act(other, side):
            @pl.when((hop == 0) | normed_fold.fed(side))
            def _():
                begin_normed(other, side, hop)

        blocks(hop, act)

    n2_line.here()
    for spread in (spread_g, spread_u, spread_d):
        spread.finish()
    forward_block(net.z)

    @pl.loop(1, net.n_l)
    def _(hop):
        n2_line.step(hop)
        pairs(n2_line, hop)
        forward_blocks(hop)
        begin_fed(hop - 1)

    begin_fed(net.n_l - 1)
    normed_fold.open_total()

    def weight_terms(task):
        at, kind = net.n_f - 1 - task // 3, task % 3
        cols = aligned(gate_sum.owner(at) * depth, depth)
        for way, (grid_sum, left, right) in enumerate(
            ((down_sum, hidden, gout), (gate_sum, dgate, rows), (up_sum, dup, rows))
        ):

            @pl.when(kind == way)
            def _():
                half = left.shape[0] // 2

                @pl.loop(0, 2)
                def _(part):
                    units = aligned(part * half, half, 16)
                    grid_sum.stage[at, units, :] = dot(left[units, :], right[:, cols]).astype(BF)

                grid_sum.first(at)

    tasks = 3 * net.n_f
    slots = normed_fold.pieces * (net.n_l - 1)
    each = -(-tasks // slots)

    def between(slot):
        @pl.loop(0, each)
        def _(i):
            pl.when(slot * each + i < tasks)(lambda: weight_terms(slot * each + i))

    for at in range(1, net.n_l):
        normed_fold.wave(at, near=True, between=between)
    n2_line.finish()

    def write_middle(i, span, value):
        value = value + gout[aligned(net.s * chunk + i * 32, 32), :].astype(F32)
        dmid_o[span, :] = value
        low[span, :] = value.astype(BF)

    terms_o[...] = jnp.zeros(terms_o.shape, F32)
    norm_backward(chunk, mid, total, gain_two, terms_o, 2, write_middle)
    dm_line.start()
    normed_fold.finish()

    def produce_top(place, write):
        left = hidden[:, aligned(place * pair, pair)].T

        @pl.loop(0, width // TILE)
        def _(j):
            cols = aligned(j * TILE, TILE)
            write(cols, dot(left, wd[:, cols]))

    dm_line.here()
    dm_line.step(1)
    top_fold.begin(produce_top)
    top_fold.open_total()
    for at in range(1, net.n_l):
        if at + 1 < net.n_l:
            dm_line.step(at + 1)
        if at == 1:
            for grid_sum in sums:
                grid_sum.second()
        top_fold.wave(at)

    @pl.loop(0, chunk // 32)
    def _(i):
        span = aligned(i * 32, 32)
        top_fold.out[net.z, span, :] = (mid[span, :] + total[span, :]).astype(BF)

    copies.start(top_fold.out.at[net.z], top_o)
    top_fold.finish()
    pl.loop(1, net.n_l)(lambda hop: pairs(dm_line, hop))
    gout_line.finish()
    dm_line.finish()
    for grid_sum, out in zip(sums, (down_o, gate_o, up_o)):
        grid_sum.last_in_place(out)
    for grid_sum, out in zip(sums, (down_o, gate_o, up_o)):
        grid_sum.finish()
        for half in range(2):
            grid_sum.result(out, half).wait()
    copies.wait()


def layer_part(tokens, packet, wq, wo, wg, wu, wd, gout, tables):
    chunk, width = tokens.shape
    n_f, n_s = lax.axis_size("fsdp"), lax.axis_size("seq")
    length = chunk * n_s
    depth, columns = wq.shape[1:]
    units = wg.shape[0]
    shape = jax.ShapeDtypeStruct
    wide, head, turned, weight = (length, width), (length, columns), (units, length), (units, width)
    return pl.pallas_call(
        layer_kernel,
        name="layer",
        out_shape=[
            shape(head, BF),
            shape(head, BF),
            shape((columns, length), BF),
            shape(head, BF),
            shape(head, BF),
            shape((8, length), F32),
            shape(wide, BF),
            shape((SMALL, width), F32),
            shape((3, width, columns), BF),
            shape((columns, width), BF),
            shape(wide, BF),
            shape((chunk, width), F32),
            shape((chunk, width), BF),
            shape((SMALL, width), F32),
            *[shape((units, depth), BF)] * 3,
        ],
        in_specs=[ANY, VMEM, *[ANY] * 6, VMEM, VMEM],
        out_specs=[*[ANY] * 5, VMEM, ANY, VMEM, *[ANY] * 3, VMEM, ANY, VMEM, *[ANY] * 3],
        scratch_shapes=[
            pltpu.VMEM(wide, BF),
            pltpu.VMEM(wide, BF),
            pltpu.VMEM((3, width, columns), BF),
            pltpu.VMEM((columns, width), BF),
            *[pltpu.VMEM(weight, BF)] * 3,
            pltpu.VMEM(head, BF),
            pltpu.VMEM(head, BF),
            pltpu.VMEM((columns, 2 * chunk), BF),
            pltpu.VMEM((2 * chunk, columns), BF),
            pltpu.VMEM((columns, length), BF),
            pltpu.VMEM((columns, 2 * chunk), F32),
            pltpu.VMEM(head, BF),
            *[pltpu.VMEM(turned, BF)] * 3,
            pltpu.VMEM((chunk, width), F32),
            pltpu.VMEM((chunk, width), BF),
            pltpu.VMEM((n_s, n_f, SMALL, 128), F32),
            *Fold.shared(chunk, width),
            *Fold.buffers(n_s, chunk, width),
            *Fold.sems(n_s) * 3,
            *Line.sems(n_s) * 4,
            *[pltpu.SemaphoreType.DMA((Spread.count(n_f),))] * 5,
            *GridSum.scratch(n_f, units, depth) * 3,
            pltpu.SemaphoreType.DMA((Packets.count(n_f, n_s),)),
            pltpu.SemaphoreType.DMA((8,)),
            pltpu.SemaphoreType.DMA((4,)),
        ],
        compiler_params=pltpu.CompilerParams(
            collective_id=1, has_side_effects=True, vmem_limit_bytes=VMEM_BYTES
        ),
        cost_estimate=pl.CostEstimate(
            flops=2 * length * width * (4 * columns + 9 * units),
            bytes_accessed=8 * length * width,
            transcendentals=length * (length * columns // HEAD + units),
        ),
    )(tokens, packet, wq, wo, wg, wu, wd, gout, *tables)


def back_kernel(
    dm_in,
    wo_in,
    att_in,
    q_in,
    k_in,
    kt_in,
    v_in,
    n1_in,
    wq_in,
    lse,
    tok,
    dmid,
    gains,
    terms_in,
    cosine,
    sine,
    gin_o,
    small_o,
    out_o,
    qkv_o,
    dm,
    wo,
    att,
    q,
    k,
    kt,
    v,
    n1,
    wq,
    datt,
    dk,
    dv,
    dqt,
    dproj,
    terms,
    tiles,
    total,
    *rest,
):
    net = Net()
    chunk, width = tok.shape
    length, columns = q_in.shape
    heads = columns // HEAD
    pair = 2 * chunk
    depth = width // net.n_f
    block = 256
    buffers, rest = rest[:4], rest[4:]
    fold_sems, rest = rest[:4], rest[4:]
    packet_scratch, rest = rest[:5], rest[5:]
    out_sum, qkv_sum = GridSum(net, *rest[:3]), GridSum(net, *rest[3:6])
    copy_sems = rest[6]

    copies = Copies(copy_sems)
    loads = [
        copies.start(src, dst)
        for src, dst in (
            (dm_in, dm),
            (wo_in, wo),
            (att_in, att),
            (q_in, q),
            (k_in, k),
            (kt_in, kt),
            (v_in, v),
            (n1_in, n1),
            (wq_in, wq),
        )
    ]
    net.barrier()
    copies.wait(*loads[:3])

    @pl.loop(0, length // block)
    def _(i):
        span = aligned(i * block, block)
        datt[span, :] = dot_nt(dm[span, :], wo[...]).astype(BF)
        dk[span, :] = jnp.zeros((block, columns), F32)
        dv[span, :] = jnp.zeros((block, columns), F32)

    copies.wait()

    @pl.loop(0, heads)
    def _(head):
        lane = lax.broadcasted_iota(jnp.int32, (1, columns), 1)
        here = jnp.where(lane // HEAD == head, 1.0, 0.0).astype(BF)
        scale = HEAD**-0.5
        visible = lax.broadcasted_iota(jnp.int32, (block, block), 0) <= lax.broadcasted_iota(
            jnp.int32, (block, block), 1
        )
        head_rows = aligned(head * HEAD, HEAD)
        for i in range(length // block):
            lo, hi = i * block, (i + 1) * block
            query = q[lo:hi, :] * (here * scale)
            upstream = datt[lo:hi, :] * here
            logsum = lse[pl.ds(head, 1), lo:hi]

            def part(at, end, mask):
                probs = jnp.exp(dot_nt(k[at:end, :], query) - logsum)
                if mask:
                    probs = jnp.where(visible, probs, 0.0)
                grads = dot_nt(v[at:end, :], upstream)
                dv[at:end, :] = dv[at:end, :] + dot(probs.astype(BF), upstream)
                return probs, grads, jnp.sum(probs * grads, 0, keepdims=True)

            def scored(at, end, probs, grads, inner):
                scores = (probs * (grads - inner)).astype(BF)
                dk[at:end, :] = dk[at:end, :] + dot(scores, query)
                return dot(kt[head_rows, at:end], scores)

            near, near_grads, inner = part(lo, hi, True)
            if i:
                far, far_grads, more = part(0, lo, False)
                inner = inner + more
            out = scored(lo, hi, near, near_grads, inner)
            if i:
                out = out + scored(0, lo, far, far_grads, inner)
            dqt[head_rows, lo:hi] = out * scale

    terms[...] = terms_in[...]
    bias_cols = aligned(net.s * columns, columns)

    @pl.loop(0, length // block)
    def _(i):
        span = aligned(i * block, block)
        tables = cosine[span, :], -sine[span, :]
        parts = [
            rotary(dqt[:, span].T.astype(BF).astype(F32), *tables).astype(BF),
            rotary(dk[span, :].astype(BF).astype(F32), *tables).astype(BF),
            dv[span, :].astype(BF),
        ]
        for kind in range(3):
            dproj[kind, span, :] = parts[kind]
            row = slice(4 + kind, 5 + kind)
            terms[row, bias_cols] = terms[row, bias_cols] + jnp.sum(parts[kind].astype(F32), 0, keepdims=True)

    def weight_terms(task):
        at = net.n_f - 1 - task // 2
        cols = aligned(qkv_sum.owner(at) * depth, depth)

        @pl.when(task % 2 == 0)
        def _():
            left = n1[:, cols].T
            for kind in range(3):
                qkv_sum.stage[at, kind * depth : (kind + 1) * depth, :] = dot(left, dproj[kind]).astype(BF)
            qkv_sum.first(at)

        @pl.when(task % 2 == 1)
        def _():
            out_sum.stage[at] = dot_tn(att[...], dm[:, cols]).astype(BF)
            out_sum.first(at)

    def produce(place, write):
        span = aligned(place * pair, pair)

        @pl.loop(0, width // TILE)
        def _(j):
            cols = aligned(j * TILE, TILE)
            value = dot_nt(dproj[0, span, :], wq[0, cols, :])
            for kind in range(1, 3):
                value = value + dot_nt(dproj[kind, span, :], wq[kind, cols, :])
            write(cols, value)

    fold = Fold(net, tiles, total, *buffers, *fold_sems)
    fold.begin(produce)
    fold.open_total()
    tasks = 2 * net.n_f
    waves = max(net.n_l - 2, 1)
    each = -(-tasks // (fold.pieces * waves))

    def between(slot):
        @pl.loop(0, each)
        def _(i):
            pl.when(slot * each + i < tasks)(lambda: weight_terms(slot * each + i))

    for at in range(1, waves + 1):
        fold.wave(at, between=between)
    for grid_sum in (qkv_sum, out_sum):
        grid_sum.second()
    for at in range(waves + 1, net.n_l):
        fold.wave(at)

    def write_input(i, span, value):
        gin_o[span, :] = value + dmid[span, :]

    norm_backward(chunk, tok, total, gains[0:1, :], terms, 0, write_input)
    PacketSum(net, *packet_scratch).run(terms, small_o, width // (net.n_f * net.n_s))
    fold.finish()
    for grid_sum, out in ((qkv_sum, qkv_o), (out_sum, out_o)):
        grid_sum.last_to(out)
        grid_sum.finish()


def back_part(dm, wo, att, q, k, kt, v, n1, wq, lse, tokens, dmid, gains, terms, tables):
    chunk, width = tokens.shape
    n_f, n_s = lax.axis_size("fsdp"), lax.axis_size("seq")
    length, columns = q.shape
    depth = width // n_f
    shape = jax.ShapeDtypeStruct
    return pl.pallas_call(
        back_kernel,
        name="back",
        out_shape=[
            shape((chunk, width), F32),
            shape((SMALL, 128), F32),
            shape((columns, depth), F32),
            shape((3 * depth, columns), F32),
        ],
        in_specs=[ANY] * 9 + [VMEM] * 7,
        out_specs=[VMEM] * 4,
        scratch_shapes=[
            pltpu.VMEM((length, width), BF),
            pltpu.VMEM((columns, width), BF),
            pltpu.VMEM((length, columns), BF),
            pltpu.VMEM((length, columns), BF),
            pltpu.VMEM((length, columns), BF),
            pltpu.VMEM((columns, length), BF),
            pltpu.VMEM((length, columns), BF),
            pltpu.VMEM((length, width), BF),
            pltpu.VMEM((3, width, columns), BF),
            pltpu.VMEM((length, columns), BF),
            pltpu.VMEM((length, columns), F32),
            pltpu.VMEM((length, columns), F32),
            pltpu.VMEM((columns, length), F32),
            pltpu.VMEM((3, length, columns), BF),
            pltpu.VMEM((SMALL, width), F32),
            *Fold.shared(chunk, width),
            *Fold.buffers(n_s, chunk, width),
            *Fold.sems(n_s),
            *PacketSum.scratch(n_f, n_s),
            *GridSum.scratch(n_f, columns, depth),
            *GridSum.scratch(n_f, 3 * depth, columns),
            pltpu.SemaphoreType.DMA((9,)),
        ],
        compiler_params=pltpu.CompilerParams(
            collective_id=3, has_side_effects=True, vmem_limit_bytes=VMEM_BYTES
        ),
        cost_estimate=pl.CostEstimate(
            flops=2 * length * columns * (8 * width + 5 * length),
            bytes_accessed=4 * length * width,
            transcendentals=length * length * columns // HEAD,
        ),
    )(dm, wo, att, q, k, kt, v, n1, wq, lse, tokens, dmid, gains, terms, *tables)


def per_device(
    tokens,
    gain_one,
    shift_one,
    w_qkv,
    b_qkv,
    w_out,
    gain_two,
    shift_two,
    w_gate,
    w_up,
    w_down,
    grad_output,
):
    length = tokens.shape[1] * lax.axis_size("seq")
    width = gain_one.shape[0]
    packet = jnp.concatenate(
        [jnp.stack([gain_one, shift_one, gain_two, shift_two]), b_qkv, jnp.zeros((1, width), BF)]
    )
    packet = jnp.pad(packet.astype(F32), ((0, 0), (0, 128 - width)))
    tables = rotary_tables(length)
    q, k, kt, v, att, lse, n1, gains, wq, wo, dm, dmid, top, terms, gate, up, down = layer_part(
        tokens[0], packet, w_qkv.transpose(1, 0, 2), w_out, w_gate.T, w_up.T, w_down, grad_output[0], tables
    )
    grad_input, small, out, qkv = back_part(
        dm, wo, att, q, k, kt, v, n1, wq, lse, tokens[0], dmid, gains, terms, tables
    )

    return (
        top[None],
        grad_input[None],
        small[0, :width],
        small[1, :width],
        qkv.reshape(3, -1, qkv.shape[1]).transpose(1, 0, 2),
        small[4:7, :width],
        out,
        small[2, :width],
        small[3, :width],
        gate.T.astype(F32),
        up.T.astype(F32),
        down.astype(F32),
    )


def solution(mesh):
    whole = P(("fsdp", "seq"))
    rows = P("fsdp", "seq", None)
    inner = P("seq", "fsdp")
    outer = P("fsdp", "seq")
    heads = P("fsdp", None, "seq")
    bias = P(None, ("fsdp", "seq"))
    return jax.shard_map(
        per_device,
        mesh=mesh,
        in_specs=(rows, whole, whole, heads, bias, inner, whole, whole, outer, outer, inner, rows),
        out_specs=(rows, rows, whole, whole, heads, bias, inner, whole, whole, outer, outer, inner),
        check_vma=False,
    )
```

```python
import functools

import jax
import jax.numpy as jnp
import numpy as np
from jax import lax
from jax.experimental import pallas as pl
from jax.experimental.pallas import tpu as pltpu
from jax.sharding import PartitionSpec as P

HEAD = 64
ROT = 16
EPSILON = 1e-05
NEG_LARGE = -1e30
MESH = pl.DeviceIdType.MESH
ANY = pl.BlockSpec(memory_space=pl.ANY)
VMEM = pl.BlockSpec(memory_space=pltpu.VMEM)
BF = jnp.bfloat16
F32 = jnp.float32
VMEM_BYTES = 60 * 2**20
TILE = 512
SMALL = 8


def put(src, dst, send, recv, **device):
    return pltpu.make_async_remote_copy(
        src_ref=src, dst_ref=dst, send_sem=send, recv_sem=recv, device_id=device, device_id_type=MESH
    )


def dot(left, right):
    return jnp.dot(left, right, preferred_element_type=F32)


def dot_nt(left, right):
    return lax.dot_general(left, right, (((1,), (1,)), ((), ())), preferred_element_type=F32)


def dot_tn(left, right):
    return lax.dot_general(left, right, (((0,), (0,)), ((), ())), preferred_element_type=F32)


def aligned(start, size, unit=None):
    return pl.ds(pl.multiple_of(start, unit or size), size)


class Net:
    def __init__(self):
        self.n_f, self.n_s = lax.axis_size("fsdp"), lax.axis_size("seq")
        self.tall = 2 if self.n_f % 2 == 0 else 1
        self.wide = self.n_f // self.tall
        self.n_l = self.n_s // 2
        self.f, self.s = lax.axis_index("fsdp"), lax.axis_index("seq")
        self.a, self.b = self.f // self.wide, self.f % self.wide
        self.z, self.c = self.s // 2, self.s % 2
        self.mate = self.s + 1 - 2 * self.c

    def barrier(self):
        sem = pltpu.get_barrier_semaphore()
        for k in range(1, self.n_f):
            pl.semaphore_signal(
                sem, inc=1, device_id={"fsdp": (self.f + k) % self.n_f}, device_id_type=MESH
            )
        for k in range(1, self.n_s):
            pl.semaphore_signal(
                sem, inc=1, device_id={"seq": (self.s + k) % self.n_s}, device_id_type=MESH
            )
        pl.semaphore_wait(sem, self.n_f + self.n_s - 2)

    def sides(self, hop, act):
        @pl.loop(0, 2)
        def _(side):
            other = self.z + (2 * side - 1) * hop

            @pl.when((other >= 0) & (other < self.n_l))
            def _():
                act(other, side)


class Spread:
    def __init__(self, net, src, part, sems):
        self.net, self.src, self.part, self.sems = net, src, part, sems
        self.rows = [j for j in range(1, net.wide)]
        self.cols = [i for i in range(1, net.tall)]

    @staticmethod
    def count(n_f):
        tall = 2 if n_f % 2 == 0 else 1
        wide = n_f // tall
        return 1 + 2 * (wide - 1) + 2 * (tall - 1) + 4 * (wide - 1) * (tall - 1)

    def at(self, kind, i, j):
        w, t = len(self.rows), len(self.cols)
        base = {
            "own": 0,
            "row": 1,
            "col": 1 + 2 * w,
            "half0": 1 + 2 * w + 2 * t,
            "half1": 1 + 2 * w + 2 * t + 2 * w * t,
        }[kind]
        if kind == "own":
            return self.sems.at[0]
        k = j - 1 if kind == "row" else i - 1 if kind == "col" else (i - 1) * w + j - 1
        return self.sems.at[base + 2 * k], self.sems.at[base + 2 * k + 1]

    def rank(self, i, j):
        net = self.net
        return ((net.a + i) % net.tall) * net.wide + (net.b + j) % net.wide

    def back(self, i, j):
        net = self.net
        return ((net.a - i + net.tall) % net.tall) * net.wide + (net.b - j + net.wide) % net.wide

    def own(self):
        return pltpu.make_async_copy(self.src, self.part(self.net.f, None), self.at("own", 0, 0))

    def first(self, i, j):
        send, recv = self.at("row" if i == 0 else "col", i, j)
        return put(self.src, self.part(self.net.f, None), send, recv, fsdp=self.rank(i, j))

    def came(self, i, j):
        send, recv = self.at("row" if i == 0 else "col", i, j)
        place = self.part(self.back(i, j), None)
        return put(place, place, send, recv, fsdp=self.rank(i, j))

    def second(self, half, i, j, came=False):
        send, recv = self.at("half0" if half == 0 else "half1", i, j)
        origin = self.back(i, j) if came else self.back(0, j) if half == 0 else self.back(i, 0)
        place = self.part(origin, half)
        return put(place, place, send, recv, fsdp=self.rank(i, 0) if half == 0 else self.rank(0, j))

    def start(self):
        self.own().start()
        for i in self.cols:
            self.first(i, 0).start()
        for j in self.rows:
            self.first(0, j).start()

    def relay(self):
        for j in self.rows:
            self.came(0, j).wait_recv()
            for i in self.cols:
                self.second(0, i, j).start()
        for i in self.cols:
            self.came(i, 0).wait_recv()
            for j in self.rows:
                self.second(1, i, j).start()

    def finish(self):
        self.own().wait()
        for j in self.rows:
            self.first(0, j).wait_send()
        for i in self.cols:
            self.first(i, 0).wait_send()
        for i in self.cols:
            for j in self.rows:
                for half in range(2):
                    self.second(half, i, j, came=True).wait_recv()
                    self.second(half, i, j).wait_send()


class Line:
    def __init__(self, net, src, part, recv, send, local):
        self.net, self.src, self.part, self.recv, self.send, self.local = net, src, part, recv, send, local
        self.pieces = recv.shape[1]
        self.rows = src.shape[0] // self.pieces

    @staticmethod
    def sems(n_s, pieces=2):
        return [
            pltpu.SemaphoreType.DMA((n_s, pieces)),
            pltpu.SemaphoreType.DMA((4, n_s // 2, pieces)),
            pltpu.SemaphoreType.DMA((1,)),
        ]

    def cut(self, ref, piece):
        return ref.at[aligned(piece * self.rows, self.rows)]

    def own(self):
        return pltpu.make_async_copy(self.src, self.part(self.net.s), self.local.at[0])

    def on_line(self, src, chunk, side, hop, piece):
        return put(
            self.cut(src, piece),
            self.cut(self.part(chunk), piece),
            self.send.at[side, hop, piece],
            self.recv.at[chunk, piece],
            seq=self.net.s + 2 - 4 * side,
        )

    def to_mate(self, src, chunk, side, hop, piece):
        return put(
            self.cut(src, piece),
            self.cut(self.part(chunk), piece),
            self.send.at[2 + side, hop, piece],
            self.recv.at[chunk, piece],
            seq=self.net.mate,
        )

    def goes_on(self, side):
        after = self.net.z + 1 - 2 * side
        return (after >= 0) & (after < self.net.n_l)

    def each_piece(self, act):
        pl.loop(0, self.pieces)(act)

    def start(self):
        net = self.net

        @self.each_piece
        def _(piece):
            for side in range(2):

                @pl.when(self.goes_on(side))
                def _():
                    self.on_line(self.src, net.s, side, 0, piece).start()

            self.to_mate(self.src, net.s, 0, 0, piece).start()

        self.own().start()

    def came(self, chunk, piece):
        place = self.cut(self.part(chunk), piece)
        put(place, place, self.send.at[0, 0, 0], self.recv.at[chunk, piece], seq=self.net.mate).wait_recv()

    def step(self, hop):
        net = self.net

        @self.each_piece
        def _(piece):
            def act(other, side):
                chunk = 2 * other + net.c
                self.came(chunk, piece)

                @pl.when(self.goes_on(side))
                def _():
                    self.on_line(self.part(chunk), chunk, side, hop, piece).start()

                self.to_mate(self.part(chunk), chunk, side, hop, piece).start()

            net.sides(hop, act)

    def pair(self, other):
        @self.each_piece
        def _(piece):
            self.came(2 * other + 1 - self.net.c, piece)

    def here(self):
        self.own().wait()
        self.pair(self.net.z)

    def finish(self):
        net = self.net

        @self.each_piece
        def _(piece):
            for side in range(2):

                @pl.when(self.goes_on(side))
                def _():
                    self.on_line(self.src, net.s, side, 0, piece).wait_send()

            self.to_mate(self.src, net.s, 0, 0, piece).wait_send()

            @pl.loop(1, net.n_l)
            def _(hop):
                def act(other, side):
                    chunk = 2 * other + net.c

                    @pl.when(self.goes_on(side))
                    def _():
                        self.on_line(self.part(chunk), chunk, side, hop, piece).wait_send()

                    self.to_mate(self.part(chunk), chunk, side, hop, piece).wait_send()

                net.sides(hop, act)


class Packets:
    def __init__(self, net, src, buf, sems):
        self.net, self.src, self.buf, self.sems = net, src, buf, sems

    @staticmethod
    def count(n_f, n_s):
        return 1 + 2 * (n_f - 1) + 2 * (n_s - 1)

    def own(self):
        net = self.net
        return pltpu.make_async_copy(self.src, self.buf.at[net.s, net.f], self.sems.at[0])

    def one(self, k, came=False):
        net = self.net
        f = (net.f - k + net.n_f) % net.n_f if came else net.f
        place = self.buf.at[net.s, f]
        return put(
            place if came else self.src,
            place,
            self.sems.at[2 * k - 1],
            self.sems.at[2 * k],
            fsdp=(net.f + k) % net.n_f,
        )

    def two(self, k, came=False):
        net = self.net
        place = self.buf.at[(net.s - k + net.n_s) % net.n_s if came else net.s]
        at = 2 * (net.n_f - 1) + 2 * k - 1
        return put(place, place, self.sems.at[at], self.sems.at[at + 1], seq=(net.s + k) % net.n_s)

    def start(self):
        self.own().start()
        for k in range(1, self.net.n_f):
            self.one(k).start()

    def middle(self):
        self.own().wait()
        for k in range(1, self.net.n_f):
            self.one(k, came=True).wait_recv()
            self.one(k).wait_send()
        for k in range(1, self.net.n_s):
            self.two(k).start()

    def finish(self):
        for k in range(1, self.net.n_s):
            self.two(k, came=True).wait_recv()
            self.two(k).wait_send()

    def unpack(self, out, width):
        net = self.net
        per = 128 // width
        for tile in range(net.n_f * net.n_s // per):
            total = None
            for j in range(per):
                f, s = divmod(tile * per + j, net.n_s)
                piece = self.buf[s, f]
                if j:
                    piece = pltpu.roll(piece, j * width, axis=1)
                total = piece if total is None else total + piece
            out[:, tile * 128 : (tile + 1) * 128] = total


def rotary(values, cosine, sine):
    columns = values.shape[1]
    half = ROT // 2
    times = columns // 128

    def wide(table):
        return table if times == 1 else jnp.concatenate([table] * times, axis=1)

    lane = lax.broadcasted_iota(jnp.int32, values.shape, 1)
    other = jnp.where(
        lane % HEAD < half, pltpu.roll(values, columns - half, axis=1), pltpu.roll(values, half, axis=1)
    )
    return values * wide(cosine) + other * wide(sine)


def rotary_tables(length):
    half = ROT // 2
    freqs = np.float32(10000.0) ** (-np.arange(half, dtype=np.float32) * np.float32(2.0 / ROT))
    angles = np.arange(length, dtype=np.float32)[:, None] * freqs[None, :].astype(np.float32)
    cosine, sine = np.cos(angles), np.sin(angles)
    rest = np.zeros((length, HEAD - ROT), np.float32)
    keep = np.concatenate([cosine, cosine, rest + 1], 1)
    swap = np.concatenate([-sine, sine, rest], 1)
    return [np.tile(t, (1, 128 // HEAD)).astype(np.float32) for t in (keep, swap)]


def normalize(values):
    center = values - jnp.mean(values, -1, keepdims=True)
    inverse = lax.rsqrt(jnp.mean(center * center, -1, keepdims=True) + EPSILON)
    return center * inverse, inverse


class Copies:
    def __init__(self, sems):
        self.sems, self.all, self.open = sems, [], []

    def start(self, src, dst):
        copy = pltpu.make_async_copy(src, dst, self.sems.at[len(self.all)])
        copy.start()
        self.all.append(copy)
        self.open.append(copy)
        return copy

    def wait(self, *copies):
        for copy in copies or list(self.open):
            copy.wait()
            self.open.remove(copy)


def columns_of(ref, depth):
    half_rows = ref.shape[0] // 2

    def part(f, half):
        span = aligned(f * depth, depth)
        if half is None:
            return ref.at[:, span]
        return ref.at[pl.ds(half * half_rows, half_rows), span]

    return part


def rows_of(ref, chunk):
    return lambda s: ref.at[aligned(s * chunk, chunk)]


class Fold:
    def __init__(self, net, tile, total, mate_in, coming, mate_out, out, mate_send, mate_recv, send, recv):
        self.net, self.tile, self.total = net, tile, total
        self.mate_in, self.coming, self.mate_out, self.out = mate_in, coming, mate_out, out
        self.mate_send, self.mate_recv, self.send, self.recv = mate_send, mate_recv, send, recv
        self.chunk = total.shape[0]
        self.pieces = recv.shape[1]
        self.rows = self.chunk // self.pieces

    @staticmethod
    def shared(chunk, width):
        return [pltpu.VMEM((2 * chunk, TILE), F32), pltpu.VMEM((chunk, width), F32)]

    @staticmethod
    def buffers(n_s, chunk, width):
        n_l = n_s // 2
        return [
            pltpu.VMEM((n_l, chunk, width), BF),
            pltpu.VMEM((n_l + 1, chunk, width), BF),
            pltpu.VMEM((3, chunk, width), BF),
            pltpu.VMEM((n_l, chunk, width), BF),
        ]

    @staticmethod
    def sems(n_s, pieces=4):
        n_l = n_s // 2
        return [
            pltpu.SemaphoreType.DMA((3, pieces)),
            pltpu.SemaphoreType.DMA((n_l, pieces)),
            pltpu.SemaphoreType.DMA((n_l, pieces)),
            pltpu.SemaphoreType.DMA((n_l + 1, pieces)),
        ]

    def place(self, other):
        return (other >= 0) & (other < self.net.n_l)

    def fed(self, side):
        return self.place(self.net.z + 1 - 2 * side)

    def span(self, piece):
        return aligned(piece * self.rows, self.rows)

    def each_piece(self, act):
        pl.loop(0, self.pieces)(act)

    def to_mate(self, target, slot, piece):
        span = self.span(piece)
        return put(
            self.mate_out.at[slot, span],
            self.mate_in.at[target, span],
            self.mate_send.at[slot, piece],
            self.mate_recv.at[target, piece],
            seq=self.net.mate,
        )

    def onward(self, target, side, hop, piece):
        span = self.span(piece)
        slot = target + (self.net.n_l - target) * (1 - side) * (1 // hop)
        return put(
            self.out.at[target, span],
            self.coming.at[slot, span],
            self.send.at[target, piece],
            self.recv.at[slot, piece],
            seq=self.net.s + 4 * side - 2,
        )

    def came(self, slot, piece):
        place = self.coming.at[slot, self.span(piece)]
        put(place, place, self.send.at[0, 0], self.recv.at[slot, piece], seq=self.net.mate).wait_recv()

    def mate_sent(self, slot):
        self.each_piece(lambda piece: self.to_mate(self.net.z, slot, piece).wait_send())

    def begin_one(self, target, slot, produce):
        mine = aligned(self.net.c * self.chunk, self.chunk)
        theirs = aligned((1 - self.net.c) * self.chunk, self.chunk)

        def write(cols, value):
            self.tile[...] = value
            self.out[target, :, cols] = self.tile[mine, :].astype(BF)
            self.mate_out[slot, :, cols] = self.tile[theirs, :].astype(BF)

        produce(target, write)
        self.each_piece(lambda piece: self.to_mate(target, slot, piece).start())

    def leave(self, target, side, hop):
        @pl.when((hop > 0) & jnp.logical_not(self.fed(side)))
        def _():
            self.each_piece(lambda piece: self.pass_piece(target, side, hop, piece, False))

    def begin(self, produce):
        net = self.net

        @pl.loop(0, net.n_l)
        def _(j):
            hop = net.n_l - 1 - j

            def act(target, side):
                @pl.when((hop > 0) | (side == 0))
                def _():
                    @pl.when((hop > 0) & self.place(target + 2 * side - 1))
                    def _():
                        self.mate_sent(side)

                    self.begin_one(target, side + (2 - side) * (1 // (hop + 1)), produce)
                    self.leave(target, side, hop)

            net.sides(hop, act)

    def pass_piece(self, target, side, hop, piece, fed):
        self.to_mate(target, 0, piece).wait_recv()
        span = self.span(piece)
        value = self.out[target, span, :].astype(F32) + self.mate_in[target, span, :].astype(F32)
        if fed:
            self.came(target, piece)
            value = value + self.coming[target, span, :].astype(F32)
        self.out[target, span, :] = value.astype(BF)
        self.onward(target, side, hop, piece).start()

    def open_total(self):
        net = self.net

        @self.each_piece
        def _(piece):
            self.to_mate(net.z, 0, piece).wait_recv()
            span = self.span(piece)
            self.total[span, :] = self.out[net.z, span, :].astype(F32) + self.mate_in[net.z, span, :].astype(F32)

    def wave(self, at, near=False, between=None):
        net = self.net
        above = at if near else net.n_l - at

        @pl.loop(0, 2)
        def _(turn):
            side = (1 - (2 * net.z) // net.n_l + turn) % 2
            target = net.n_l - 1 - above + (2 * above - net.n_l + 1) * side
            hop = (target - net.z) * (2 * side - 1)

            @self.each_piece
            def _(piece):
                span = self.span(piece)

                @pl.when(self.fed(side) & (hop > 0))
                def _():
                    self.pass_piece(target, side, hop, piece, True)

                @pl.when(self.fed(side) & (hop == 0))
                def _():
                    slot = net.z + (net.n_l - net.z) * (1 - side)
                    self.came(slot, piece)
                    self.total[span, :] = self.total[span, :] + self.coming[slot, span, :].astype(F32)

                if between is not None:
                    between(((at - 1) * 2 + turn) * self.pieces + piece)

    def finish(self):
        net = self.net
        self.mate_sent(2)
        for side in range(2):
            pl.when(self.place(net.z + 2 * side - 1))(functools.partial(self.mate_sent, side))

        @pl.loop(1, net.n_l)
        def _(hop):
            net.sides(
                hop,
                lambda target, side: self.each_piece(
                    lambda piece: self.onward(target, side, hop, piece).wait_send()
                ),
            )


class GridSum:
    def __init__(self, net, stage, came, sems):
        self.net, self.stage, self.came, self.sems = net, stage, came, sems
        self.half = stage.shape[1] // 2
        self.rows = next(r for r in (176, 128, 96, 64, 32, 16) if self.half % r == 0)
        self.cols = range(1, net.tall)
        self.along = range(1, net.wide)
        self.bases = self.layout(net.n_f)

    @staticmethod
    def layout(n_f):
        tall = 2 if n_f % 2 == 0 else 1
        wide = n_f // tall
        sizes = [(wide - 1) * tall, (tall - 1) * wide, tall - 1, wide - 1]
        return [sum(sizes[:at]) for at in range(5)]

    @staticmethod
    def scratch(n_f, rows, columns):
        count = GridSum.layout(n_f)[4]
        return [
            pltpu.VMEM((n_f, rows, columns), BF),
            pltpu.VMEM((count, rows // 2, columns), BF),
            pltpu.SemaphoreType.DMA((2, count + 1)),
        ]

    def slot(self, kind, i, j):
        base = self.bases[kind]
        return base + [(j - 1) * self.net.tall + i, (i - 1) * self.net.wide + j, i - 1, j - 1][kind]

    def rank(self, i, j):
        net = self.net
        return ((net.a + i) % net.tall) * net.wide + (net.b + j) % net.wide

    def owner(self, at):
        return self.rank(at // self.net.wide, at % self.net.wide)

    def copy(self, kind, i, j):
        half = kind % 2
        along = kind in (0, 3)
        slot = self.slot(kind, i, j)
        at = i * self.net.wide + j
        return put(
            self.stage.at[at, pl.ds(half * self.half, self.half)],
            self.came.at[slot],
            self.sems.at[0, slot],
            self.sems.at[1, slot],
            fsdp=self.rank(0, j) if along else self.rank(i, 0),
        )

    def first(self, at):
        i, j = at // self.net.wide, at % self.net.wide

        @pl.when(j > 0)
        def _():
            self.copy(0, i, j).start()

        @pl.when(i > 0)
        def _():
            self.copy(1, i, j).start()

    def gather(self, half, at, slots, write):
        @pl.loop(0, self.half // self.rows)
        def _(step):
            span = aligned(half * self.half + step * self.rows, self.rows, 16)
            value = self.stage[at, span, :].astype(F32)
            for slot in slots:
                value = value + self.came[slot, aligned(step * self.rows, self.rows, 16), :].astype(F32)
            write(span, value)

    def wait(self, *copies):
        for kind, i, j in copies:
            self.copy(kind, i, j).wait_recv()
        return [self.slot(*copy) for copy in copies]

    def second(self):
        def keep(at):
            def write(span, value):
                self.stage[at, span, :] = value.astype(BF)

            return write

        for i in self.cols:
            at = i * self.net.wide
            self.gather(0, at, self.wait(*[(0, i, j) for j in self.along]), keep(at))
            self.copy(2, i, 0).start()
        for j in self.along:
            self.gather(1, j, self.wait(*[(1, i, j) for i in self.cols]), keep(j))
            self.copy(3, 0, j).start()

    def last(self, write, done=None):
        self.gather(
            0, 0, self.wait(*[(0, 0, j) for j in self.along], *[(2, i, 0) for i in self.cols]), write
        )
        if done is not None:
            done(0)
        self.gather(
            1, 0, self.wait(*[(1, i, 0) for i in self.cols], *[(3, 0, j) for j in self.along]), write
        )
        if done is not None:
            done(1)

    def result(self, out, half):
        span = pl.ds(half * self.half, self.half)
        return pltpu.make_async_copy(self.stage.at[0, span], out.at[span], self.sems.at[half, self.bases[4]])

    def last_to(self, out):
        def write(span, value):
            out[span, :] = value

        self.last(write)

    def last_in_place(self, out):
        def write(span, value):
            self.stage[0, span, :] = value.astype(BF)

        self.last(write, lambda half: self.result(out, half).start())

    def finish(self):
        net = self.net
        for i in range(net.tall):
            for j in range(net.wide):
                if j:
                    self.copy(0, i, j).wait_send()
                if i:
                    self.copy(1, i, j).wait_send()
        for i in self.cols:
            self.copy(2, i, 0).wait_send()
        for j in self.along:
            self.copy(3, 0, j).wait_send()


class PacketSum:
    def __init__(self, net, out, seq_in, total, fsdp_in, sems):
        self.net, self.out, self.seq_in, self.total, self.fsdp_in, self.sems = net, out, seq_in, total, fsdp_in, sems

    @staticmethod
    def scratch(n_f, n_s):
        return [
            pltpu.VMEM((n_s, n_f, SMALL, 128), F32),
            pltpu.VMEM((n_s, n_f, SMALL, 128), F32),
            pltpu.VMEM((n_f, SMALL, 128), F32),
            pltpu.VMEM((n_f, SMALL, 128), F32),
            pltpu.SemaphoreType.DMA((2 * (n_f + n_s),)),
        ]

    def one(self, k):
        to = (self.net.s + k) % self.net.n_s
        return put(self.out.at[to], self.seq_in.at[k], self.sems.at[2 * k], self.sems.at[2 * k + 1], seq=to)

    def two(self, k):
        to = (self.net.f + k) % self.net.n_f
        at = 2 * (self.net.n_s + k)
        return put(self.total.at[to], self.fsdp_in.at[k], self.sems.at[at], self.sems.at[at + 1], fsdp=to)

    def run(self, terms, result, width):
        net = self.net
        per = 128 // width
        for tile in range(net.n_f * net.n_s // per):
            value = terms[:, tile * 128 : (tile + 1) * 128]
            for j in range(per):
                f, s = divmod(tile * per + j, net.n_s)
                self.out[s, f] = pltpu.roll(value, 128 - j * width, axis=1) if j else value
        for k in range(1, net.n_s):
            self.one(k).start()
        total = self.out[net.s]
        for k in range(1, net.n_s):
            self.one(k).wait()
            total = total + self.seq_in[k]
        self.total[...] = total
        for k in range(1, net.n_f):
            self.two(k).start()
        total = self.total[net.f]
        for k in range(1, net.n_f):
            self.two(k).wait()
            total = total + self.fsdp_in[k]
        result[...] = total


def norm_backward(rows, source, grad, gain, terms, at, write):
    terms[at : at + 2, :] = jnp.zeros((2, terms.shape[1]), F32)

    @pl.loop(0, rows // 32)
    def _(i):
        span = aligned(i * 32, 32)
        scaled, inverse = normalize(source[span, :].astype(F32))
        value = grad[span, :]
        upstream = value * gain
        inner = jnp.mean(upstream, -1, keepdims=True)
        cross = jnp.mean(upstream * scaled, -1, keepdims=True)
        terms[at : at + 1, :] = terms[at : at + 1, :] + jnp.sum(value * scaled, 0, keepdims=True)
        terms[at + 1 : at + 2, :] = terms[at + 1 : at + 2, :] + jnp.sum(value, 0, keepdims=True)
        write(i, span, inverse * (upstream - inner - scaled * cross))


def layer_kernel(
    tok,
    packet,
    wq_own,
    wo_own,
    wg_own,
    wu_own,
    wd_own,
    gout_own,
    cosine,
    sine,
    q_o,
    k_o,
    kt_o,
    v_o,
    att_o,
    lse_o,
    n1_o,
    gains_o,
    wq_o,
    wo_o,
    dm_o,
    dmid_o,
    top_o,
    terms_o,
    gate_o,
    up_o,
    down_o,
    rows,
    gout,
    wq,
    wo,
    wg,
    wu,
    wd,
    q,
    k,
    kt,
    v,
    vt,
    ot,
    att,
    hidden,
    dgate,
    dup,
    mid,
    low,
    packets,
    tiles,
    total,
    *rest,
):
    net = Net()
    chunk, width = tok.shape
    length = chunk * net.n_s
    depth = wq_own.shape[1]
    columns = wq_own.shape[2]
    heads = columns // HEAD
    pair = 2 * chunk
    buffers, rest = rest[:4], rest[4:]
    folds = []
    for _ in range(3):
        folds.append(Fold(net, tiles, total, *buffers, *rest[:4]))
        rest = rest[4:]
    att_fold, normed_fold, top_fold = folds
    line_sems = [rest[at : at + 3] for at in (0, 3, 6, 9)]
    rest = rest[12:]
    spread_sems, rest = rest[:5], rest[5:]
    gate_sum, up_sum, down_sum = [GridSum(net, *rest[at : at + 3]) for at in (0, 3, 6)]
    sums = (down_sum, gate_sum, up_sum)
    pk_sems, copy_sems, n1_sems = rest[9:]
    copies = Copies(copy_sems)
    n1 = att_fold.mate_out

    net.barrier()

    def wq_part(f, half):
        if half is None:
            return wq.at[:, aligned(f * depth, depth), :]
        return wq.at[:, aligned(f * depth + half * (depth // 2), depth // 2), :]

    spread_q = Spread(net, wq_own, wq_part, spread_sems[0])
    spread_o, spread_g, spread_u, spread_d = [
        Spread(net, own, columns_of(full, depth), sems)
        for own, full, sems in zip((wo_own, wg_own, wu_own, wd_own), (wo, wg, wu, wd), spread_sems[1:])
    ]
    pk = Packets(net, packet, packets, pk_sems)
    line = Line(net, tok, rows_of(rows, chunk), *line_sems[0])
    gout_line = Line(net, gout_own, rows_of(gout, chunk), *line_sems[1])
    n2_line = Line(net, low, rows_of(rows, chunk), *line_sems[2])
    dm_line = Line(net, low, rows_of(dm_o, chunk), *line_sems[3])

    def pairs(which, hop):
        net.sides(hop, lambda other, side: which.pair(other))

    def blocks(hop, act):
        def once(other, side):
            @pl.when((hop > 0) | (side == 0))
            def _():
                act(other, side)

        net.sides(hop, once)

    pk.start()
    line.start()
    spread_q.start()
    pk.middle()
    pk.finish()
    pk.unpack(gains_o, width // (net.n_f * net.n_s))

    def project_block(other, side):
        span = aligned(other * pair, pair)
        gain, shift = gains_o[0:1, :], gains_o[1:2, :]

        for part in range(2):

            @pl.loop(0, chunk // 32)
            def _(i):
                at = aligned((2 * other + part) * chunk + i * 32, 32)
                scaled, _ = normalize(rows[at, :].astype(F32))
                n1[part, aligned(i * 32, 32), :] = (scaled * gain + shift).astype(BF)

        keeps = [
            pltpu.make_async_copy(
                n1.at[part], n1_o.at[aligned((2 * other + part) * chunk, chunk)], n1_sems.at[part]
            )
            for part in range(2)
        ]
        for copy in keeps:
            copy.start()
        left = n1[0:2].reshape(pair, width)
        cols = aligned(net.s * columns, columns)
        tables = cosine[span, :], sine[span, :]
        for kind in range(3):
            value = dot(left, wq[kind]) + gains_o[4 + kind : 5 + kind, cols]
            if kind == 0:
                q[span, :] = rotary(value, *tables).astype(BF)
            elif kind == 1:
                value = rotary(value, *tables)
                k[span, :] = value.astype(BF)
                kt[...] = value.T.astype(BF)
            else:
                v[...] = value.astype(BF)
                vt[:, span] = value.T.astype(BF)
        for copy in (
            pltpu.make_async_copy(kt, kt_o.at[:, span], n1_sems.at[2]),
            pltpu.make_async_copy(v, v_o.at[span], n1_sems.at[3]),
        ):
            copy.start()
            keeps.append(copy)
        for copy in keeps:
            copy.wait()

    line.here()
    for hop in range(1, net.n_l - 1):
        line.step(hop)
        if hop == 1:
            spread_q.relay()
        pairs(line, hop)
    spread_o.start()
    spread_q.finish()
    pl.loop(0, net.n_l - 1)(lambda hop: blocks(hop, project_block))
    spread_o.relay()
    spread_g.start()
    line.step(net.n_l - 1)
    gout_line.start()
    pairs(line, net.n_l - 1)
    blocks(net.n_l - 1, project_block)
    spread_u.start()
    for pair_of in ((wq, wq_o), (q, q_o), (k, k_o)):
        copies.start(*pair_of)
    spread_o.finish()
    line.finish()

    def attend(i):
        lo, hi = i * pair, (i + 1) * pair

        @pl.loop(0, heads)
        def _(head):
            lane = lax.broadcasted_iota(jnp.int32, (1, columns), 1)
            here = jnp.where(lane // HEAD == head, HEAD**-0.5, 0.0).astype(BF)
            visible = lax.broadcasted_iota(jnp.int32, (pair, pair), 0) <= lax.broadcasted_iota(
                jnp.int32, (pair, pair), 1
            )
            head_rows = aligned(head * HEAD, HEAD)
            query = q[lo:hi, :] * here
            near = jnp.where(visible, dot_nt(k[lo:hi, :], query), NEG_LARGE)
            highest = jnp.max(near, 0, keepdims=True)
            if i:
                far = dot_nt(k[0:lo, :], query)
                highest = jnp.maximum(highest, jnp.max(far, 0, keepdims=True))
            near = jnp.exp(near - highest)
            sum_of = jnp.sum(near, 0, keepdims=True)
            out = dot(vt[head_rows, lo:hi], near.astype(BF))
            if i:
                far = jnp.exp(far - highest)
                sum_of = sum_of + jnp.sum(far, 0, keepdims=True)
                out = out + dot(vt[head_rows, 0:lo], far.astype(BF))
            ot[head_rows, :] = out / sum_of
            lse_o[pl.ds(head, 1), lo:hi] = highest + jnp.log(sum_of)

        att[lo:hi, :] = ot[...].T.astype(BF)

    def produce_attended(place, write):
        for i in range(net.n_l):
            pl.when(place == i)(functools.partial(attend, i))
        left = att[aligned(place * pair, pair), :]

        @pl.loop(0, width // TILE)
        def _(j):
            cols = aligned(j * TILE, TILE)
            write(cols, dot(left, wo[:, cols]))

    att_fold.begin(produce_attended)
    copies.start(att, att_o)
    copies.start(wo, wo_o)
    gout_line.step(1)
    spread_g.relay()
    spread_d.start()
    att_fold.open_total()
    for at in range(1, net.n_l):
        att_fold.wave(at)
        if at + 1 < net.n_l:
            gout_line.step(at + 1)
        if at == 1:
            spread_u.relay()
    spread_d.relay()
    gain_two, shift_two = gains_o[2:3, :], gains_o[3:4, :]

    @pl.loop(0, chunk // 32)
    def _(i):
        span = aligned(i * 32, 32)
        value = rows[aligned(net.s * chunk + i * 32, 32), :].astype(F32) + total[span, :]
        mid[span, :] = value
        scaled, _ = normalize(value)
        low[span, :] = (scaled * gain_two + shift_two).astype(BF)

    n2_line.start()
    att_fold.finish()
    gout_line.here()
    pl.loop(1, net.n_l)(lambda hop: pairs(gout_line, hop))

    def forward_block(other):
        span = aligned(other * pair, pair)
        right = rows[span, :]
        half = hidden.shape[0] // 2

        @pl.loop(0, 2)
        def _(part):
            units = aligned(part * half, half, 16)
            gate = dot_nt(wg[units, :], right)
            up = dot_nt(wu[units, :], right)
            back = dot_nt(wd[units, :], gout[span, :])
            sigma = jax.nn.sigmoid(gate)
            active = gate * sigma
            hidden[units, span] = (active * up).astype(BF)
            dgate[units, span] = (back * up * (sigma * (1.0 + gate * (1.0 - sigma)))).astype(BF)
            dup[units, span] = (back * active).astype(BF)

    def produce_normed(place, write):
        span = aligned(place * pair, pair)
        left, right = dgate[:, span].T, dup[:, span].T

        @pl.loop(0, width // TILE)
        def _(j):
            cols = aligned(j * TILE, TILE)
            write(cols, dot(left, wg[:, cols]) + dot(right, wu[:, cols]))

    def begin_normed(other, side, hop):
        @pl.when(hop > 1)
        def _():
            normed_fold.mate_sent(side)

        normed_fold.begin_one(other, side + (2 - side) * (1 // (hop + 1)), produce_normed)

    def forward_blocks(hop):
        def act(other, side):
            forward_block(other)

            @pl.when(jnp.logical_not(normed_fold.fed(side)))
            def _():
                begin_normed(other, side, hop)
                normed_fold.leave(other, side, hop)

        net.sides(hop, act)

    def begin_fed(hop):
        def act(other, side):
            @pl.when((hop == 0) | normed_fold.fed(side))
            def _():
                begin_normed(other, side, hop)

        blocks(hop, act)

    n2_line.here()
    for spread in (spread_g, spread_u, spread_d):
        spread.finish()
    forward_block(net.z)

    @pl.loop(1, net.n_l)
    def _(hop):
        n2_line.step(hop)
        pairs(n2_line, hop)
        forward_blocks(hop)
        begin_fed(hop - 1)

    begin_fed(net.n_l - 1)
    normed_fold.open_total()

    def weight_terms(task):
        at, kind = net.n_f - 1 - task // 3, task % 3
        cols = aligned(gate_sum.owner(at) * depth, depth)
        for way, (grid_sum, left, right) in enumerate(
            ((down_sum, hidden, gout), (gate_sum, dgate, rows), (up_sum, dup, rows))
        ):

            @pl.when(kind == way)
            def _():
                half = left.shape[0] // 2

                @pl.loop(0, 2)
                def _(part):
                    units = aligned(part * half, half, 16)
                    grid_sum.stage[at, units, :] = dot(left[units, :], right[:, cols]).astype(BF)

                grid_sum.first(at)

    tasks = 3 * net.n_f
    slots = 2 * normed_fold.pieces * (net.n_l - 1)
    each = -(-tasks // slots)

    def between(slot):
        @pl.loop(0, each)
        def _(i):
            pl.when(slot * each + i < tasks)(lambda: weight_terms(slot * each + i))

    for at in range(1, net.n_l):
        normed_fold.wave(at, near=True, between=between)
    n2_line.finish()

    def write_middle(i, span, value):
        value = value + gout[aligned(net.s * chunk + i * 32, 32), :].astype(F32)
        dmid_o[span, :] = value
        low[span, :] = value.astype(BF)

    terms_o[...] = jnp.zeros(terms_o.shape, F32)
    norm_backward(chunk, mid, total, gain_two, terms_o, 2, write_middle)
    dm_line.start()
    normed_fold.finish()

    def produce_top(place, write):
        left = hidden[:, aligned(place * pair, pair)].T

        @pl.loop(0, width // TILE)
        def _(j):
            cols = aligned(j * TILE, TILE)
            write(cols, dot(left, wd[:, cols]))

    dm_line.here()
    dm_line.step(1)
    top_fold.begin(produce_top)
    top_fold.open_total()
    for at in range(1, net.n_l):
        if at + 1 < net.n_l:
            dm_line.step(at + 1)
        if at == 1:
            for grid_sum in sums:
                grid_sum.second()
        top_fold.wave(at)

    @pl.loop(0, chunk // 32)
    def _(i):
        span = aligned(i * 32, 32)
        top_fold.out[net.z, span, :] = (mid[span, :] + total[span, :]).astype(BF)

    copies.start(top_fold.out.at[net.z], top_o)
    top_fold.finish()
    pl.loop(1, net.n_l)(lambda hop: pairs(dm_line, hop))
    gout_line.finish()
    dm_line.finish()
    for grid_sum, out in zip(sums, (down_o, gate_o, up_o)):
        grid_sum.last_in_place(out)
    for grid_sum, out in zip(sums, (down_o, gate_o, up_o)):
        grid_sum.finish()
        for half in range(2):
            grid_sum.result(out, half).wait()
    copies.wait()


def layer_part(tokens, packet, wq, wo, wg, wu, wd, gout, tables):
    chunk, width = tokens.shape
    n_f, n_s = lax.axis_size("fsdp"), lax.axis_size("seq")
    length = chunk * n_s
    depth, columns = wq.shape[1:]
    units = wg.shape[0]
    shape = jax.ShapeDtypeStruct
    wide, head, turned, weight = (length, width), (length, columns), (units, length), (units, width)
    return pl.pallas_call(
        layer_kernel,
        name="layer",
        out_shape=[
            shape(head, BF),
            shape(head, BF),
            shape((columns, length), BF),
            shape(head, BF),
            shape(head, BF),
            shape((8, length), F32),
            shape(wide, BF),
            shape((SMALL, width), F32),
            shape((3, width, columns), BF),
            shape((columns, width), BF),
            shape(wide, BF),
            shape((chunk, width), F32),
            shape((chunk, width), BF),
            shape((SMALL, width), F32),
            *[shape((units, depth), BF)] * 3,
        ],
        in_specs=[ANY, VMEM, *[ANY] * 6, VMEM, VMEM],
        out_specs=[*[ANY] * 5, VMEM, ANY, VMEM, *[ANY] * 3, VMEM, ANY, VMEM, *[ANY] * 3],
        scratch_shapes=[
            pltpu.VMEM(wide, BF),
            pltpu.VMEM(wide, BF),
            pltpu.VMEM((3, width, columns), BF),
            pltpu.VMEM((columns, width), BF),
            *[pltpu.VMEM(weight, BF)] * 3,
            pltpu.VMEM(head, BF),
            pltpu.VMEM(head, BF),
            pltpu.VMEM((columns, 2 * chunk), BF),
            pltpu.VMEM((2 * chunk, columns), BF),
            pltpu.VMEM((columns, length), BF),
            pltpu.VMEM((columns, 2 * chunk), F32),
            pltpu.VMEM(head, BF),
            *[pltpu.VMEM(turned, BF)] * 3,
            pltpu.VMEM((chunk, width), F32),
            pltpu.VMEM((chunk, width), BF),
            pltpu.VMEM((n_s, n_f, SMALL, 128), F32),
            *Fold.shared(chunk, width),
            *Fold.buffers(n_s, chunk, width),
            *Fold.sems(n_s) * 3,
            *Line.sems(n_s) * 4,
            *[pltpu.SemaphoreType.DMA((Spread.count(n_f),))] * 5,
            *GridSum.scratch(n_f, units, depth) * 3,
            pltpu.SemaphoreType.DMA((Packets.count(n_f, n_s),)),
            pltpu.SemaphoreType.DMA((8,)),
            pltpu.SemaphoreType.DMA((4,)),
        ],
        compiler_params=pltpu.CompilerParams(
            collective_id=1, has_side_effects=True, vmem_limit_bytes=VMEM_BYTES
        ),
        cost_estimate=pl.CostEstimate(
            flops=2 * length * width * (4 * columns + 9 * units),
            bytes_accessed=8 * length * width,
            transcendentals=length * (length * columns // HEAD + units),
        ),
    )(tokens, packet, wq, wo, wg, wu, wd, gout, *tables)


def back_kernel(
    dm_in,
    wo_in,
    att_in,
    q_in,
    k_in,
    kt_in,
    v_in,
    n1_in,
    wq_in,
    lse,
    tok,
    dmid,
    gains,
    terms_in,
    cosine,
    sine,
    gin_o,
    small_o,
    out_o,
    qkv_o,
    dm,
    wo,
    att,
    q,
    k,
    kt,
    v,
    n1,
    wq,
    datt,
    dk,
    dv,
    dqt,
    dproj,
    terms,
    tiles,
    total,
    *rest,
):
    net = Net()
    chunk, width = tok.shape
    length, columns = q_in.shape
    heads = columns // HEAD
    pair = 2 * chunk
    depth = width // net.n_f
    block = 256
    buffers, rest = rest[:4], rest[4:]
    fold_sems, rest = rest[:4], rest[4:]
    packet_scratch, rest = rest[:5], rest[5:]
    out_sum, qkv_sum = GridSum(net, *rest[:3]), GridSum(net, *rest[3:6])
    copy_sems = rest[6]

    copies = Copies(copy_sems)
    loads = [
        copies.start(src, dst)
        for src, dst in (
            (dm_in, dm),
            (wo_in, wo),
            (att_in, att),
            (q_in, q),
            (k_in, k),
            (kt_in, kt),
            (v_in, v),
            (n1_in, n1),
            (wq_in, wq),
        )
    ]
    net.barrier()
    copies.wait(*loads[:3])

    @pl.loop(0, length // block)
    def _(i):
        span = aligned(i * block, block)
        datt[span, :] = dot_nt(dm[span, :], wo[...]).astype(BF)
        dk[span, :] = jnp.zeros((block, columns), F32)
        dv[span, :] = jnp.zeros((block, columns), F32)

    copies.wait()

    @pl.loop(0, heads)
    def _(head):
        lane = lax.broadcasted_iota(jnp.int32, (1, columns), 1)
        here = jnp.where(lane // HEAD == head, 1.0, 0.0).astype(BF)
        scale = HEAD**-0.5
        visible = lax.broadcasted_iota(jnp.int32, (block, block), 0) <= lax.broadcasted_iota(
            jnp.int32, (block, block), 1
        )
        head_rows = aligned(head * HEAD, HEAD)
        for i in range(length // block):
            lo, hi = i * block, (i + 1) * block
            query = q[lo:hi, :] * (here * scale)
            upstream = datt[lo:hi, :] * here
            logsum = lse[pl.ds(head, 1), lo:hi]

            def part(at, end, mask):
                probs = jnp.exp(dot_nt(k[at:end, :], query) - logsum)
                if mask:
                    probs = jnp.where(visible, probs, 0.0)
                grads = dot_nt(v[at:end, :], upstream)
                dv[at:end, :] = dv[at:end, :] + dot(probs.astype(BF), upstream)
                return probs, grads, jnp.sum(probs * grads, 0, keepdims=True)

            def scored(at, end, probs, grads, inner):
                scores = (probs * (grads - inner)).astype(BF)
                dk[at:end, :] = dk[at:end, :] + dot(scores, query)
                return dot(kt[head_rows, at:end], scores)

            near, near_grads, inner = part(lo, hi, True)
            if i:
                far, far_grads, more = part(0, lo, False)
                inner = inner + more
            out = scored(lo, hi, near, near_grads, inner)
            if i:
                out = out + scored(0, lo, far, far_grads, inner)
            dqt[head_rows, lo:hi] = out * scale

    terms[...] = terms_in[...]
    bias_cols = aligned(net.s * columns, columns)

    @pl.loop(0, length // block)
    def _(i):
        span = aligned(i * block, block)
        tables = cosine[span, :], -sine[span, :]
        parts = [
            rotary(dqt[:, span].T.astype(BF).astype(F32), *tables).astype(BF),
            rotary(dk[span, :].astype(BF).astype(F32), *tables).astype(BF),
            dv[span, :].astype(BF),
        ]
        for kind in range(3):
            dproj[kind, span, :] = parts[kind]
            row = slice(4 + kind, 5 + kind)
            terms[row, bias_cols] = terms[row, bias_cols] + jnp.sum(parts[kind].astype(F32), 0, keepdims=True)

    def weight_terms(task):
        at = net.n_f - 1 - task // 2
        cols = aligned(qkv_sum.owner(at) * depth, depth)

        @pl.when(task % 2 == 0)
        def _():
            left = n1[:, cols].T
            for kind in range(3):
                qkv_sum.stage[at, kind * depth : (kind + 1) * depth, :] = dot(left, dproj[kind]).astype(BF)
            qkv_sum.first(at)

        @pl.when(task % 2 == 1)
        def _():
            out_sum.stage[at] = dot_tn(att[...], dm[:, cols]).astype(BF)
            out_sum.first(at)

    def produce(place, write):
        span = aligned(place * pair, pair)

        @pl.loop(0, width // TILE)
        def _(j):
            cols = aligned(j * TILE, TILE)
            value = dot_nt(dproj[0, span, :], wq[0, cols, :])
            for kind in range(1, 3):
                value = value + dot_nt(dproj[kind, span, :], wq[kind, cols, :])
            write(cols, value)

    fold = Fold(net, tiles, total, *buffers, *fold_sems)
    fold.begin(produce)
    fold.open_total()
    tasks = 2 * net.n_f
    waves = max(net.n_l - 2, 1)
    each = -(-tasks // (2 * fold.pieces * waves))

    def between(slot):
        @pl.loop(0, each)
        def _(i):
            pl.when(slot * each + i < tasks)(lambda: weight_terms(slot * each + i))

    for at in range(1, waves + 1):
        fold.wave(at, between=between)
    for grid_sum in (qkv_sum, out_sum):
        grid_sum.second()
    for at in range(waves + 1, net.n_l):
        fold.wave(at)

    def write_input(i, span, value):
        gin_o[span, :] = value + dmid[span, :]

    norm_backward(chunk, tok, total, gains[0:1, :], terms, 0, write_input)
    PacketSum(net, *packet_scratch).run(terms, small_o, width // (net.n_f * net.n_s))
    fold.finish()
    for grid_sum, out in ((qkv_sum, qkv_o), (out_sum, out_o)):
        grid_sum.last_to(out)
        grid_sum.finish()


def back_part(dm, wo, att, q, k, kt, v, n1, wq, lse, tokens, dmid, gains, terms, tables):
    chunk, width = tokens.shape
    n_f, n_s = lax.axis_size("fsdp"), lax.axis_size("seq")
    length, columns = q.shape
    depth = width // n_f
    shape = jax.ShapeDtypeStruct
    return pl.pallas_call(
        back_kernel,
        name="back",
        out_shape=[
            shape((chunk, width), F32),
            shape((SMALL, 128), F32),
            shape((columns, depth), F32),
            shape((3 * depth, columns), F32),
        ],
        in_specs=[ANY] * 9 + [VMEM] * 7,
        out_specs=[VMEM] * 4,
        scratch_shapes=[
            pltpu.VMEM((length, width), BF),
            pltpu.VMEM((columns, width), BF),
            pltpu.VMEM((length, columns), BF),
            pltpu.VMEM((length, columns), BF),
            pltpu.VMEM((length, columns), BF),
            pltpu.VMEM((columns, length), BF),
            pltpu.VMEM((length, columns), BF),
            pltpu.VMEM((length, width), BF),
            pltpu.VMEM((3, width, columns), BF),
            pltpu.VMEM((length, columns), BF),
            pltpu.VMEM((length, columns), F32),
            pltpu.VMEM((length, columns), F32),
            pltpu.VMEM((columns, length), F32),
            pltpu.VMEM((3, length, columns), BF),
            pltpu.VMEM((SMALL, width), F32),
            *Fold.shared(chunk, width),
            *Fold.buffers(n_s, chunk, width),
            *Fold.sems(n_s),
            *PacketSum.scratch(n_f, n_s),
            *GridSum.scratch(n_f, columns, depth),
            *GridSum.scratch(n_f, 3 * depth, columns),
            pltpu.SemaphoreType.DMA((9,)),
        ],
        compiler_params=pltpu.CompilerParams(
            collective_id=3, has_side_effects=True, vmem_limit_bytes=VMEM_BYTES
        ),
        cost_estimate=pl.CostEstimate(
            flops=2 * length * columns * (8 * width + 5 * length),
            bytes_accessed=4 * length * width,
            transcendentals=length * length * columns // HEAD,
        ),
    )(dm, wo, att, q, k, kt, v, n1, wq, lse, tokens, dmid, gains, terms, *tables)


def per_device(
    tokens,
    gain_one,
    shift_one,
    w_qkv,
    b_qkv,
    w_out,
    gain_two,
    shift_two,
    w_gate,
    w_up,
    w_down,
    grad_output,
):
    length = tokens.shape[1] * lax.axis_size("seq")
    width = gain_one.shape[0]
    packet = jnp.concatenate(
        [jnp.stack([gain_one, shift_one, gain_two, shift_two]), b_qkv, jnp.zeros((1, width), BF)]
    )
    packet = jnp.pad(packet.astype(F32), ((0, 0), (0, 128 - width)))
    tables = rotary_tables(length)
    q, k, kt, v, att, lse, n1, gains, wq, wo, dm, dmid, top, terms, gate, up, down = layer_part(
        tokens[0], packet, w_qkv.transpose(1, 0, 2), w_out, w_gate.T, w_up.T, w_down, grad_output[0], tables
    )
    grad_input, small, out, qkv = back_part(
        dm, wo, att, q, k, kt, v, n1, wq, lse, tokens[0], dmid, gains, terms, tables
    )

    return (
        top[None],
        grad_input[None],
        small[0, :width],
        small[1, :width],
        qkv.reshape(3, -1, qkv.shape[1]).transpose(1, 0, 2),
        small[4:7, :width],
        out,
        small[2, :width],
        small[3, :width],
        gate.T.astype(F32),
        up.T.astype(F32),
        down.astype(F32),
    )


def solution(mesh):
    whole = P(("fsdp", "seq"))
    rows = P("fsdp", "seq", None)
    inner = P("seq", "fsdp")
    outer = P("fsdp", "seq")
    heads = P("fsdp", None, "seq")
    bias = P(None, ("fsdp", "seq"))
    return jax.shard_map(
        per_device,
        mesh=mesh,
        in_specs=(rows, whole, whole, heads, bias, inner, whole, whole, outer, outer, inner, rows),
        out_specs=(rows, rows, whole, whole, heads, bias, inner, whole, whole, outer, outer, inner),
        check_vma=False,
    )
```

```python
import functools

import jax
import jax.numpy as jnp
import numpy as np
from jax import lax
from jax.experimental import pallas as pl
from jax.experimental.pallas import tpu as pltpu
from jax.sharding import PartitionSpec as P

HEAD = 64
ROT = 16
EPSILON = 1e-05
NEG_LARGE = -1e30
MESH = pl.DeviceIdType.MESH
ANY = pl.BlockSpec(memory_space=pl.ANY)
VMEM = pl.BlockSpec(memory_space=pltpu.VMEM)
BF = jnp.bfloat16
F32 = jnp.float32
VMEM_BYTES = 60 * 2**20
TILE = 512
SMALL = 8


def put(src, dst, send, recv, **device):
    return pltpu.make_async_remote_copy(
        src_ref=src, dst_ref=dst, send_sem=send, recv_sem=recv, device_id=device, device_id_type=MESH
    )


def dot(left, right):
    return jnp.dot(left, right, preferred_element_type=F32)


def dot_nt(left, right):
    return lax.dot_general(left, right, (((1,), (1,)), ((), ())), preferred_element_type=F32)


def dot_tn(left, right):
    return lax.dot_general(left, right, (((0,), (0,)), ((), ())), preferred_element_type=F32)


def aligned(start, size, unit=None):
    return pl.ds(pl.multiple_of(start, unit or size), size)


class Net:
    def __init__(self):
        self.n_f, self.n_s = lax.axis_size("fsdp"), lax.axis_size("seq")
        self.tall = 2 if self.n_f % 2 == 0 else 1
        self.wide = self.n_f // self.tall
        self.n_l = self.n_s // 2
        self.f, self.s = lax.axis_index("fsdp"), lax.axis_index("seq")
        self.a, self.b = self.f // self.wide, self.f % self.wide
        self.z, self.c = self.s // 2, self.s % 2
        self.mate = self.s + 1 - 2 * self.c

    def barrier(self):
        sem = pltpu.get_barrier_semaphore()
        for k in range(1, self.n_f):
            pl.semaphore_signal(
                sem, inc=1, device_id={"fsdp": (self.f + k) % self.n_f}, device_id_type=MESH
            )
        for k in range(1, self.n_s):
            pl.semaphore_signal(
                sem, inc=1, device_id={"seq": (self.s + k) % self.n_s}, device_id_type=MESH
            )
        pl.semaphore_wait(sem, self.n_f + self.n_s - 2)

    def sides(self, hop, act):
        @pl.loop(0, 2)
        def _(side):
            other = self.z + (2 * side - 1) * hop

            @pl.when((other >= 0) & (other < self.n_l))
            def _():
                act(other, side)


class Spread:
    def __init__(self, net, src, part, sems):
        self.net, self.src, self.part, self.sems = net, src, part, sems
        self.rows = [j for j in range(1, net.wide)]
        self.cols = [i for i in range(1, net.tall)]

    @staticmethod
    def count(n_f):
        tall = 2 if n_f % 2 == 0 else 1
        wide = n_f // tall
        return 1 + 2 * (wide - 1) + 2 * (tall - 1) + 4 * (wide - 1) * (tall - 1)

    def at(self, kind, i, j):
        w, t = len(self.rows), len(self.cols)
        base = {
            "own": 0,
            "row": 1,
            "col": 1 + 2 * w,
            "half0": 1 + 2 * w + 2 * t,
            "half1": 1 + 2 * w + 2 * t + 2 * w * t,
        }[kind]
        if kind == "own":
            return self.sems.at[0]
        k = j - 1 if kind == "row" else i - 1 if kind == "col" else (i - 1) * w + j - 1
        return self.sems.at[base + 2 * k], self.sems.at[base + 2 * k + 1]

    def rank(self, i, j):
        net = self.net
        return ((net.a + i) % net.tall) * net.wide + (net.b + j) % net.wide

    def back(self, i, j):
        net = self.net
        return ((net.a - i + net.tall) % net.tall) * net.wide + (net.b - j + net.wide) % net.wide

    def own(self):
        return pltpu.make_async_copy(self.src, self.part(self.net.f, None), self.at("own", 0, 0))

    def first(self, i, j):
        send, recv = self.at("row" if i == 0 else "col", i, j)
        return put(self.src, self.part(self.net.f, None), send, recv, fsdp=self.rank(i, j))

    def came(self, i, j):
        send, recv = self.at("row" if i == 0 else "col", i, j)
        place = self.part(self.back(i, j), None)
        return put(place, place, send, recv, fsdp=self.rank(i, j))

    def second(self, half, i, j, came=False):
        send, recv = self.at("half0" if half == 0 else "half1", i, j)
        origin = self.back(i, j) if came else self.back(0, j) if half == 0 else self.back(i, 0)
        place = self.part(origin, half)
        return put(place, place, send, recv, fsdp=self.rank(i, 0) if half == 0 else self.rank(0, j))

    def start(self):
        self.own().start()
        for i in self.cols:
            self.first(i, 0).start()
        for j in self.rows:
            self.first(0, j).start()

    def relay(self):
        for j in self.rows:
            self.came(0, j).wait_recv()
            for i in self.cols:
                self.second(0, i, j).start()
        for i in self.cols:
            self.came(i, 0).wait_recv()
            for j in self.rows:
                self.second(1, i, j).start()

    def finish(self):
        self.own().wait()
        for j in self.rows:
            self.first(0, j).wait_send()
        for i in self.cols:
            self.first(i, 0).wait_send()
        for i in self.cols:
            for j in self.rows:
                for half in range(2):
                    self.second(half, i, j, came=True).wait_recv()
                    self.second(half, i, j).wait_send()


class Line:
    def __init__(self, net, src, part, recv, send, local):
        self.net, self.src, self.part, self.recv, self.send, self.local = net, src, part, recv, send, local
        self.pieces = recv.shape[1]
        self.rows = src.shape[0] // self.pieces

    @staticmethod
    def sems(n_s, pieces=2):
        return [
            pltpu.SemaphoreType.DMA((n_s, pieces)),
            pltpu.SemaphoreType.DMA((4, n_s // 2, pieces)),
            pltpu.SemaphoreType.DMA((1,)),
        ]

    def cut(self, ref, piece):
        return ref.at[aligned(piece * self.rows, self.rows)]

    def own(self):
        return pltpu.make_async_copy(self.src, self.part(self.net.s), self.local.at[0])

    def on_line(self, src, chunk, side, hop, piece):
        return put(
            self.cut(src, piece),
            self.cut(self.part(chunk), piece),
            self.send.at[side, hop, piece],
            self.recv.at[chunk, piece],
            seq=self.net.s + 2 - 4 * side,
        )

    def to_mate(self, src, chunk, side, hop, piece):
        return put(
            self.cut(src, piece),
            self.cut(self.part(chunk), piece),
            self.send.at[2 + side, hop, piece],
            self.recv.at[chunk, piece],
            seq=self.net.mate,
        )

    def goes_on(self, side):
        after = self.net.z + 1 - 2 * side
        return (after >= 0) & (after < self.net.n_l)

    def each_piece(self, act):
        pl.loop(0, self.pieces)(act)

    def start(self):
        net = self.net

        @self.each_piece
        def _(piece):
            for side in range(2):

                @pl.when(self.goes_on(side))
                def _():
                    self.on_line(self.src, net.s, side, 0, piece).start()

            self.to_mate(self.src, net.s, 0, 0, piece).start()

        self.own().start()

    def came(self, chunk, piece):
        place = self.cut(self.part(chunk), piece)
        put(place, place, self.send.at[0, 0, 0], self.recv.at[chunk, piece], seq=self.net.mate).wait_recv()

    def step(self, hop):
        net = self.net

        @self.each_piece
        def _(piece):
            def act(other, side):
                chunk = 2 * other + net.c
                self.came(chunk, piece)

                @pl.when(self.goes_on(side))
                def _():
                    self.on_line(self.part(chunk), chunk, side, hop, piece).start()

                self.to_mate(self.part(chunk), chunk, side, hop, piece).start()

            net.sides(hop, act)

    def pair(self, other):
        @self.each_piece
        def _(piece):
            self.came(2 * other + 1 - self.net.c, piece)

    def here(self):
        self.own().wait()
        self.pair(self.net.z)

    def finish(self):
        net = self.net

        @self.each_piece
        def _(piece):
            for side in range(2):

                @pl.when(self.goes_on(side))
                def _():
                    self.on_line(self.src, net.s, side, 0, piece).wait_send()

            self.to_mate(self.src, net.s, 0, 0, piece).wait_send()

            @pl.loop(1, net.n_l)
            def _(hop):
                def act(other, side):
                    chunk = 2 * other + net.c

                    @pl.when(self.goes_on(side))
                    def _():
                        self.on_line(self.part(chunk), chunk, side, hop, piece).wait_send()

                    self.to_mate(self.part(chunk), chunk, side, hop, piece).wait_send()

                net.sides(hop, act)


class Packets:
    def __init__(self, net, src, buf, sems):
        self.net, self.src, self.buf, self.sems = net, src, buf, sems

    @staticmethod
    def count(n_f, n_s):
        return 1 + 2 * (n_f - 1) + 2 * (n_s - 1)

    def own(self):
        net = self.net
        return pltpu.make_async_copy(self.src, self.buf.at[net.s, net.f], self.sems.at[0])

    def one(self, k, came=False):
        net = self.net
        f = (net.f - k + net.n_f) % net.n_f if came else net.f
        place = self.buf.at[net.s, f]
        return put(
            place if came else self.src,
            place,
            self.sems.at[2 * k - 1],
            self.sems.at[2 * k],
            fsdp=(net.f + k) % net.n_f,
        )

    def two(self, k, came=False):
        net = self.net
        place = self.buf.at[(net.s - k + net.n_s) % net.n_s if came else net.s]
        at = 2 * (net.n_f - 1) + 2 * k - 1
        return put(place, place, self.sems.at[at], self.sems.at[at + 1], seq=(net.s + k) % net.n_s)

    def start(self):
        self.own().start()
        for k in range(1, self.net.n_f):
            self.one(k).start()

    def middle(self):
        self.own().wait()
        for k in range(1, self.net.n_f):
            self.one(k, came=True).wait_recv()
            self.one(k).wait_send()
        for k in range(1, self.net.n_s):
            self.two(k).start()

    def finish(self):
        for k in range(1, self.net.n_s):
            self.two(k, came=True).wait_recv()
            self.two(k).wait_send()

    def unpack(self, out, width):
        net = self.net
        per = 128 // width
        for tile in range(net.n_f * net.n_s // per):
            total = None
            for j in range(per):
                f, s = divmod(tile * per + j, net.n_s)
                piece = self.buf[s, f]
                if j:
                    piece = pltpu.roll(piece, j * width, axis=1)
                total = piece if total is None else total + piece
            out[:, tile * 128 : (tile + 1) * 128] = total


def rotary(values, cosine, sine):
    columns = values.shape[1]
    half = ROT // 2
    times = columns // 128

    def wide(table):
        return table if times == 1 else jnp.concatenate([table] * times, axis=1)

    lane = lax.broadcasted_iota(jnp.int32, values.shape, 1)
    other = jnp.where(
        lane % HEAD < half, pltpu.roll(values, columns - half, axis=1), pltpu.roll(values, half, axis=1)
    )
    return values * wide(cosine) + other * wide(sine)


def rotary_tables(length):
    half = ROT // 2
    freqs = np.float32(10000.0) ** (-np.arange(half, dtype=np.float32) * np.float32(2.0 / ROT))
    angles = np.arange(length, dtype=np.float32)[:, None] * freqs[None, :].astype(np.float32)
    cosine, sine = np.cos(angles), np.sin(angles)
    rest = np.zeros((length, HEAD - ROT), np.float32)
    keep = np.concatenate([cosine, cosine, rest + 1], 1)
    swap = np.concatenate([-sine, sine, rest], 1)
    return [np.tile(t, (1, 128 // HEAD)).astype(np.float32) for t in (keep, swap)]


def normalize(values):
    center = values - jnp.mean(values, -1, keepdims=True)
    inverse = lax.rsqrt(jnp.mean(center * center, -1, keepdims=True) + EPSILON)
    return center * inverse, inverse


class Copies:
    def __init__(self, sems):
        self.sems, self.all, self.open = sems, [], []

    def start(self, src, dst):
        copy = pltpu.make_async_copy(src, dst, self.sems.at[len(self.all)])
        copy.start()
        self.all.append(copy)
        self.open.append(copy)
        return copy

    def wait(self, *copies):
        for copy in copies or list(self.open):
            copy.wait()
            self.open.remove(copy)


def columns_of(ref, depth):
    half_rows = ref.shape[0] // 2

    def part(f, half):
        span = aligned(f * depth, depth)
        if half is None:
            return ref.at[:, span]
        return ref.at[pl.ds(half * half_rows, half_rows), span]

    return part


def rows_of(ref, chunk):
    return lambda s: ref.at[aligned(s * chunk, chunk)]


class Fold:
    def __init__(self, net, tile, total, mate_in, coming, mate_out, out, mate_send, mate_recv, send, recv):
        self.net, self.tile, self.total = net, tile, total
        self.mate_in, self.coming, self.mate_out, self.out = mate_in, coming, mate_out, out
        self.mate_send, self.mate_recv, self.send, self.recv = mate_send, mate_recv, send, recv
        self.chunk = total.shape[0]
        self.pieces = recv.shape[1]
        self.rows = self.chunk // self.pieces

    @staticmethod
    def shared(chunk, width):
        return [pltpu.VMEM((2 * chunk, TILE), F32), pltpu.VMEM((chunk, width), F32)]

    @staticmethod
    def buffers(n_s, chunk, width):
        n_l = n_s // 2
        return [
            pltpu.VMEM((n_l, chunk, width), BF),
            pltpu.VMEM((n_l + 1, chunk, width), BF),
            pltpu.VMEM((3, chunk, width), BF),
            pltpu.VMEM((n_l, chunk, width), BF),
        ]

    @staticmethod
    def sems(n_s, pieces=4):
        n_l = n_s // 2
        return [
            pltpu.SemaphoreType.DMA((3, pieces)),
            pltpu.SemaphoreType.DMA((n_l, pieces)),
            pltpu.SemaphoreType.DMA((n_l, pieces)),
            pltpu.SemaphoreType.DMA((n_l + 1, pieces)),
        ]

    def place(self, other):
        return (other >= 0) & (other < self.net.n_l)

    def fed(self, side):
        return self.place(self.net.z + 1 - 2 * side)

    def span(self, piece):
        return aligned(piece * self.rows, self.rows)

    def each_piece(self, act):
        pl.loop(0, self.pieces)(act)

    def to_mate(self, target, slot, piece):
        span = self.span(piece)
        return put(
            self.mate_out.at[slot, span],
            self.mate_in.at[target, span],
            self.mate_send.at[slot, piece],
            self.mate_recv.at[target, piece],
            seq=self.net.mate,
        )

    def onward(self, target, side, hop, piece):
        span = self.span(piece)
        slot = target + (self.net.n_l - target) * (1 - side) * (1 // hop)
        return put(
            self.out.at[target, span],
            self.coming.at[slot, span],
            self.send.at[target, piece],
            self.recv.at[slot, piece],
            seq=self.net.s + 4 * side - 2,
        )

    def came(self, slot, piece):
        place = self.coming.at[slot, self.span(piece)]
        put(place, place, self.send.at[0, 0], self.recv.at[slot, piece], seq=self.net.mate).wait_recv()

    def mate_sent(self, slot):
        self.each_piece(lambda piece: self.to_mate(self.net.z, slot, piece).wait_send())

    def begin_one(self, target, slot, produce):
        mine = aligned(self.net.c * self.chunk, self.chunk)
        theirs = aligned((1 - self.net.c) * self.chunk, self.chunk)

        def write(cols, value):
            self.tile[...] = value
            self.out[target, :, cols] = self.tile[mine, :].astype(BF)
            self.mate_out[slot, :, cols] = self.tile[theirs, :].astype(BF)

        produce(target, write)
        self.each_piece(lambda piece: self.to_mate(target, slot, piece).start())

    def leave(self, target, side, hop):
        @pl.when((hop > 0) & jnp.logical_not(self.fed(side)))
        def _():
            self.each_piece(lambda piece: self.pass_piece(target, side, hop, piece, False))

    def begin(self, produce, between=None):
        net = self.net

        @pl.loop(0, net.n_l)
        def _(j):
            hop = net.n_l - 1 - j

            def act(target, side):
                @pl.when((hop > 0) | (side == 0))
                def _():
                    @pl.when((hop > 0) & self.place(target + 2 * side - 1))
                    def _():
                        self.mate_sent(side)

                    self.begin_one(target, side + (2 - side) * (1 // (hop + 1)), produce)
                    self.leave(target, side, hop)

            net.sides(hop, act)
            if between is not None:
                pl.when(j == 1)(between)

    def pass_piece(self, target, side, hop, piece, fed):
        self.to_mate(target, 0, piece).wait_recv()
        span = self.span(piece)
        value = self.out[target, span, :].astype(F32) + self.mate_in[target, span, :].astype(F32)
        if fed:
            self.came(target, piece)
            value = value + self.coming[target, span, :].astype(F32)
        self.out[target, span, :] = value.astype(BF)
        self.onward(target, side, hop, piece).start()

    def open_total(self):
        net = self.net

        @self.each_piece
        def _(piece):
            self.to_mate(net.z, 0, piece).wait_recv()
            span = self.span(piece)
            self.total[span, :] = self.out[net.z, span, :].astype(F32) + self.mate_in[net.z, span, :].astype(F32)

    def wave(self, at, near=False, between=None):
        net = self.net
        above = at if near else net.n_l - at

        @pl.loop(0, 2)
        def _(turn):
            side = (1 - (2 * net.z) // net.n_l + turn) % 2
            target = net.n_l - 1 - above + (2 * above - net.n_l + 1) * side
            hop = (target - net.z) * (2 * side - 1)

            @self.each_piece
            def _(piece):
                span = self.span(piece)

                @pl.when(self.fed(side) & (hop > 0))
                def _():
                    self.pass_piece(target, side, hop, piece, True)

                @pl.when(self.fed(side) & (hop == 0))
                def _():
                    slot = net.z + (net.n_l - net.z) * (1 - side)
                    self.came(slot, piece)
                    self.total[span, :] = self.total[span, :] + self.coming[slot, span, :].astype(F32)

                if between is not None:
                    between(((at - 1) * 2 + turn) * self.pieces + piece)

    def finish(self):
        net = self.net
        self.mate_sent(2)
        for side in range(2):
            pl.when(self.place(net.z + 2 * side - 1))(functools.partial(self.mate_sent, side))

        @pl.loop(1, net.n_l)
        def _(hop):
            net.sides(
                hop,
                lambda target, side: self.each_piece(
                    lambda piece: self.onward(target, side, hop, piece).wait_send()
                ),
            )


class GridSum:
    def __init__(self, net, stage, came, sems):
        self.net, self.stage, self.came, self.sems = net, stage, came, sems
        self.half = stage.shape[1] // 2
        self.rows = next(r for r in (176, 128, 96, 64, 32, 16) if self.half % r == 0)
        self.cols = range(1, net.tall)
        self.along = range(1, net.wide)
        self.bases = self.layout(net.n_f)

    @staticmethod
    def layout(n_f):
        tall = 2 if n_f % 2 == 0 else 1
        wide = n_f // tall
        sizes = [(wide - 1) * tall, (tall - 1) * wide, tall - 1, wide - 1]
        return [sum(sizes[:at]) for at in range(5)]

    @staticmethod
    def scratch(n_f, rows, columns):
        count = GridSum.layout(n_f)[4]
        return [
            pltpu.VMEM((n_f, rows, columns), BF),
            pltpu.VMEM((count, rows // 2, columns), BF),
            pltpu.SemaphoreType.DMA((2, count + GridEnd.count(n_f))),
        ]

    def slot(self, kind, i, j):
        base = self.bases[kind]
        return base + [(j - 1) * self.net.tall + i, (i - 1) * self.net.wide + j, i - 1, j - 1][kind]

    def rank(self, i, j):
        net = self.net
        return ((net.a + i) % net.tall) * net.wide + (net.b + j) % net.wide

    def owner(self, at):
        return self.rank(at // self.net.wide, at % self.net.wide)

    def copy(self, kind, i, j):
        half = kind % 2
        along = kind in (0, 3)
        slot = self.slot(kind, i, j)
        at = i * self.net.wide + j
        return put(
            self.stage.at[at, pl.ds(half * self.half, self.half)],
            self.came.at[slot],
            self.sems.at[0, slot],
            self.sems.at[1, slot],
            fsdp=self.rank(0, j) if along else self.rank(i, 0),
        )

    def first(self, at):
        i, j = at // self.net.wide, at % self.net.wide

        @pl.when(j > 0)
        def _():
            self.copy(0, i, j).start()

        @pl.when(i > 0)
        def _():
            self.copy(1, i, j).start()

    def gather(self, half, at, slots, write):
        @pl.loop(0, self.half // self.rows)
        def _(step):
            span = aligned(half * self.half + step * self.rows, self.rows, 16)
            value = self.stage[at, span, :].astype(F32)
            for slot in slots:
                value = value + self.came[slot, aligned(step * self.rows, self.rows, 16), :].astype(F32)
            write(span, value)

    def wait(self, *copies):
        for kind, i, j in copies:
            self.copy(kind, i, j).wait_recv()
        return [self.slot(*copy) for copy in copies]

    def second(self):
        def keep(at):
            def write(span, value):
                self.stage[at, span, :] = value.astype(BF)

            return write

        for i in self.cols:
            at = i * self.net.wide
            self.gather(0, at, self.wait(*[(0, i, j) for j in self.along]), keep(at))
            self.copy(2, i, 0).start()
        for j in self.along:
            self.gather(1, j, self.wait(*[(1, i, j) for i in self.cols]), keep(j))
            self.copy(3, 0, j).start()

    def sum_first(self):
        def keep(at):
            def write(span, value):
                self.stage[at, span, :] = value.astype(BF)

            return write

        for i in range(self.net.tall):
            at = i * self.net.wide
            self.gather(0, at, self.wait(*[(0, i, j) for j in self.along]), keep(at))
        for j in range(self.net.wide):
            self.gather(1, j, self.wait(*[(1, i, j) for i in self.cols]), keep(j))

    def hand_on(self, out):
        net = self.net
        shards = [(0, 0), (0, 1), *[(i * net.wide, 0) for i in self.cols], *[(j, 1) for j in self.along]]
        return [
            pltpu.make_async_copy(
                self.stage.at[at, pl.ds(half * self.half, self.half)], out.at[k], self.sems.at[0, self.bases[4] + k]
            )
            for k, (at, half) in enumerate(shards)
        ]

    def last(self, out):
        def write(span, value):
            out[span, :] = value

        self.gather(
            0, 0, self.wait(*[(0, 0, j) for j in self.along], *[(2, i, 0) for i in self.cols]), write
        )
        self.gather(
            1, 0, self.wait(*[(1, i, 0) for i in self.cols], *[(3, 0, j) for j in self.along]), write
        )

    def finish_first(self):
        for i in range(self.net.tall):
            for j in range(self.net.wide):
                if j:
                    self.copy(0, i, j).wait_send()
                if i:
                    self.copy(1, i, j).wait_send()

    def finish(self):
        self.finish_first()
        for i in self.cols:
            self.copy(2, i, 0).wait_send()
        for j in self.along:
            self.copy(3, 0, j).wait_send()


class GridEnd:
    def __init__(self, net, sums, came, sems):
        self.net, self.sums, self.came, self.sems = net, sums, came, sems

    @staticmethod
    def count(n_f):
        tall = 2 if n_f % 2 == 0 else 1
        return tall + n_f // tall

    @staticmethod
    def scratch(n_f, rows, columns):
        count = GridEnd.count(n_f)
        return [
            pltpu.VMEM((count, rows // 2, columns), BF),
            pltpu.VMEM((count - 2, rows // 2, columns), BF),
            pltpu.SemaphoreType.DMA((2, count - 2)),
        ]

    def copies(self):
        net = self.net
        f = [((net.a + i) % net.tall) * net.wide + net.b for i in range(1, net.tall)]
        f += [net.a * net.wide + (net.b + j) % net.wide for j in range(1, net.wide)]
        return [
            put(self.sums.at[2 + k], self.came.at[k], self.sems.at[0, k], self.sems.at[1, k], fsdp=to)
            for k, to in enumerate(f)
        ]

    def start(self):
        for copy in self.copies():
            copy.start()

    def last(self, out):
        for copy in self.copies():
            copy.wait()
        half = self.sums.shape[1]
        rows = next(r for r in (176, 128, 96, 64, 32, 16) if half % r == 0)
        down = range(self.net.tall - 1)
        along = range(self.net.tall - 1, self.net.tall + self.net.wide - 2)
        for at, slots in enumerate((down, along)):

            @pl.loop(0, half // rows)
            def _(step):
                span = aligned(step * rows, rows, 16)
                value = self.sums[at, span, :].astype(F32)
                for slot in slots:
                    value = value + self.came[slot, span, :].astype(F32)
                out[aligned(at * half + step * rows, rows, 16), :] = value


class PacketSum:
    def __init__(self, net, out, seq_in, total, fsdp_in, sems):
        self.net, self.out, self.seq_in, self.total, self.fsdp_in, self.sems = net, out, seq_in, total, fsdp_in, sems

    @staticmethod
    def scratch(n_f, n_s):
        return [
            pltpu.VMEM((n_s, n_f, SMALL, 128), F32),
            pltpu.VMEM((n_s, n_f, SMALL, 128), F32),
            pltpu.VMEM((n_f, SMALL, 128), F32),
            pltpu.VMEM((n_f, SMALL, 128), F32),
            pltpu.SemaphoreType.DMA((2 * (n_f + n_s),)),
        ]

    def one(self, k):
        to = (self.net.s + k) % self.net.n_s
        return put(self.out.at[to], self.seq_in.at[k], self.sems.at[2 * k], self.sems.at[2 * k + 1], seq=to)

    def two(self, k):
        to = (self.net.f + k) % self.net.n_f
        at = 2 * (self.net.n_s + k)
        return put(self.total.at[to], self.fsdp_in.at[k], self.sems.at[at], self.sems.at[at + 1], fsdp=to)

    def run(self, terms, result, width):
        net = self.net
        per = 128 // width
        for tile in range(net.n_f * net.n_s // per):
            value = terms[:, tile * 128 : (tile + 1) * 128]
            for j in range(per):
                f, s = divmod(tile * per + j, net.n_s)
                self.out[s, f] = pltpu.roll(value, 128 - j * width, axis=1) if j else value
        for k in range(1, net.n_s):
            self.one(k).start()
        total = self.out[net.s]
        for k in range(1, net.n_s):
            self.one(k).wait()
            total = total + self.seq_in[k]
        self.total[...] = total
        for k in range(1, net.n_f):
            self.two(k).start()
        total = self.total[net.f]
        for k in range(1, net.n_f):
            self.two(k).wait()
            total = total + self.fsdp_in[k]
        result[...] = total


def norm_backward(rows, source, grad, gain, terms, at, write):
    terms[at : at + 2, :] = jnp.zeros((2, terms.shape[1]), F32)

    @pl.loop(0, rows // 32)
    def _(i):
        span = aligned(i * 32, 32)
        scaled, inverse = normalize(source[span, :].astype(F32))
        value = grad[span, :]
        upstream = value * gain
        inner = jnp.mean(upstream, -1, keepdims=True)
        cross = jnp.mean(upstream * scaled, -1, keepdims=True)
        terms[at : at + 1, :] = terms[at : at + 1, :] + jnp.sum(value * scaled, 0, keepdims=True)
        terms[at + 1 : at + 2, :] = terms[at + 1 : at + 2, :] + jnp.sum(value, 0, keepdims=True)
        write(i, span, inverse * (upstream - inner - scaled * cross))


def layer_kernel(
    tok,
    packet,
    wq_own,
    wo_own,
    wg_own,
    wu_own,
    wd_own,
    gout_own,
    cosine,
    sine,
    q_o,
    k_o,
    kt_o,
    v_o,
    att_o,
    lse_o,
    n1_o,
    gains_o,
    wq_o,
    wo_o,
    dm_o,
    dmid_o,
    top_o,
    terms_o,
    gate_o,
    up_o,
    down_o,
    rows,
    gout,
    wq,
    wo,
    wg,
    wu,
    wd,
    q,
    k,
    kt,
    v,
    vt,
    ot,
    att,
    hidden,
    dgate,
    dup,
    mid,
    low,
    packets,
    tiles,
    total,
    *rest,
):
    net = Net()
    chunk, width = tok.shape
    length = chunk * net.n_s
    depth = wq_own.shape[1]
    columns = wq_own.shape[2]
    heads = columns // HEAD
    pair = 2 * chunk
    buffers, rest = rest[:4], rest[4:]
    folds = []
    for _ in range(3):
        folds.append(Fold(net, tiles, total, *buffers, *rest[:4]))
        rest = rest[4:]
    att_fold, normed_fold, top_fold = folds
    line_sems = [rest[at : at + 3] for at in (0, 3, 6, 9)]
    rest = rest[12:]
    spread_sems, rest = rest[:5], rest[5:]
    gate_sum, up_sum, down_sum = [GridSum(net, *rest[at : at + 3]) for at in (0, 3, 6)]
    sums = (down_sum, gate_sum, up_sum)
    pk_sems, copy_sems, n1_sems = rest[9:]
    copies = Copies(copy_sems)
    n1 = att_fold.mate_out

    net.barrier()

    def wq_part(f, half):
        if half is None:
            return wq.at[:, aligned(f * depth, depth), :]
        return wq.at[:, aligned(f * depth + half * (depth // 2), depth // 2), :]

    spread_q = Spread(net, wq_own, wq_part, spread_sems[0])
    spread_o, spread_g, spread_u, spread_d = [
        Spread(net, own, columns_of(full, depth), sems)
        for own, full, sems in zip((wo_own, wg_own, wu_own, wd_own), (wo, wg, wu, wd), spread_sems[1:])
    ]
    pk = Packets(net, packet, packets, pk_sems)
    line = Line(net, tok, rows_of(rows, chunk), *line_sems[0])
    gout_line = Line(net, gout_own, rows_of(gout, chunk), *line_sems[1])
    n2_line = Line(net, low, rows_of(rows, chunk), *line_sems[2])
    dm_line = Line(net, low, rows_of(dm_o, chunk), *line_sems[3])

    def pairs(which, hop):
        net.sides(hop, lambda other, side: which.pair(other))

    def blocks(hop, act):
        def once(other, side):
            @pl.when((hop > 0) | (side == 0))
            def _():
                act(other, side)

        net.sides(hop, once)

    pk.start()
    line.start()
    spread_q.start()
    pk.middle()
    pk.finish()
    pk.unpack(gains_o, width // (net.n_f * net.n_s))

    def project_block(other, side):
        span = aligned(other * pair, pair)
        gain, shift = gains_o[0:1, :], gains_o[1:2, :]

        for part in range(2):

            @pl.loop(0, chunk // 32)
            def _(i):
                at = aligned((2 * other + part) * chunk + i * 32, 32)
                scaled, _ = normalize(rows[at, :].astype(F32))
                n1[part, aligned(i * 32, 32), :] = (scaled * gain + shift).astype(BF)

        keeps = [
            pltpu.make_async_copy(
                n1.at[part], n1_o.at[aligned((2 * other + part) * chunk, chunk)], n1_sems.at[part]
            )
            for part in range(2)
        ]
        for copy in keeps:
            copy.start()
        left = n1[0:2].reshape(pair, width)
        cols = aligned(net.s * columns, columns)
        tables = cosine[span, :], sine[span, :]
        for kind in range(3):
            value = dot(left, wq[kind]) + gains_o[4 + kind : 5 + kind, cols]
            if kind == 0:
                q[span, :] = rotary(value, *tables).astype(BF)
            elif kind == 1:
                value = rotary(value, *tables)
                k[span, :] = value.astype(BF)
                kt[...] = value.T.astype(BF)
            else:
                v[...] = value.astype(BF)
                vt[:, span] = value.T.astype(BF)
        for copy in (
            pltpu.make_async_copy(kt, kt_o.at[:, span], n1_sems.at[2]),
            pltpu.make_async_copy(v, v_o.at[span], n1_sems.at[3]),
        ):
            copy.start()
            keeps.append(copy)
        for copy in keeps:
            copy.wait()

    line.here()
    for hop in range(1, net.n_l - 1):
        line.step(hop)
        if hop == 1:
            spread_q.relay()
        pairs(line, hop)
    spread_o.start()
    spread_q.finish()
    spread_g.start()
    pl.loop(0, net.n_l - 1)(lambda hop: blocks(hop, project_block))
    spread_o.relay()
    spread_u.start()
    line.step(net.n_l - 1)
    gout_line.start()
    pairs(line, net.n_l - 1)
    blocks(net.n_l - 1, project_block)
    spread_d.start()
    for pair_of in ((wq, wq_o), (q, q_o), (k, k_o)):
        copies.start(*pair_of)
    spread_o.finish()
    line.finish()

    def attend(i):
        lo, hi = i * pair, (i + 1) * pair

        @pl.loop(0, heads)
        def _(head):
            lane = lax.broadcasted_iota(jnp.int32, (1, columns), 1)
            here = jnp.where(lane // HEAD == head, HEAD**-0.5, 0.0).astype(BF)
            visible = lax.broadcasted_iota(jnp.int32, (pair, pair), 0) <= lax.broadcasted_iota(
                jnp.int32, (pair, pair), 1
            )
            head_rows = aligned(head * HEAD, HEAD)
            query = q[lo:hi, :] * here
            near = jnp.where(visible, dot_nt(k[lo:hi, :], query), NEG_LARGE)
            highest = jnp.max(near, 0, keepdims=True)
            if i:
                far = dot_nt(k[0:lo, :], query)
                highest = jnp.maximum(highest, jnp.max(far, 0, keepdims=True))
            near = jnp.exp(near - highest)
            sum_of = jnp.sum(near, 0, keepdims=True)
            out = dot(vt[head_rows, lo:hi], near.astype(BF))
            if i:
                far = jnp.exp(far - highest)
                sum_of = sum_of + jnp.sum(far, 0, keepdims=True)
                out = out + dot(vt[head_rows, 0:lo], far.astype(BF))
            ot[head_rows, :] = out / sum_of
            lse_o[pl.ds(head, 1), lo:hi] = highest + jnp.log(sum_of)

        att[lo:hi, :] = ot[...].T.astype(BF)

    def produce_attended(place, write):
        for i in range(net.n_l):
            pl.when(place == i)(functools.partial(attend, i))
        left = att[aligned(place * pair, pair), :]

        @pl.loop(0, width // TILE)
        def _(j):
            cols = aligned(j * TILE, TILE)
            write(cols, dot(left, wo[:, cols]))

    def relays():
        gout_line.step(1)
        spread_g.relay()

    att_fold.begin(produce_attended, relays)
    copies.start(att, att_o)
    copies.start(wo, wo_o)
    att_fold.open_total()
    for at in range(1, net.n_l):
        att_fold.wave(at)
        if at + 1 < net.n_l:
            gout_line.step(at + 1)
        if at == 1:
            spread_u.relay()
        if at == min(2, net.n_l - 1):
            spread_d.relay()
    gain_two, shift_two = gains_o[2:3, :], gains_o[3:4, :]

    @pl.loop(0, chunk // 32)
    def _(i):
        span = aligned(i * 32, 32)
        value = rows[aligned(net.s * chunk + i * 32, 32), :].astype(F32) + total[span, :]
        mid[span, :] = value
        scaled, _ = normalize(value)
        low[span, :] = (scaled * gain_two + shift_two).astype(BF)

    n2_line.start()
    att_fold.finish()
    gout_line.here()
    pl.loop(1, net.n_l)(lambda hop: pairs(gout_line, hop))

    def forward_block(other):
        span = aligned(other * pair, pair)
        right = rows[span, :]
        half = hidden.shape[0] // 2

        @pl.loop(0, 2)
        def _(part):
            units = aligned(part * half, half, 16)
            gate = dot_nt(wg[units, :], right)
            up = dot_nt(wu[units, :], right)
            back = dot_nt(wd[units, :], gout[span, :])
            sigma = jax.nn.sigmoid(gate)
            active = gate * sigma
            hidden[units, span] = (active * up).astype(BF)
            dgate[units, span] = (back * up * (sigma * (1.0 + gate * (1.0 - sigma)))).astype(BF)
            dup[units, span] = (back * active).astype(BF)

    def produce_normed(place, write):
        span = aligned(place * pair, pair)
        left, right = dgate[:, span].T, dup[:, span].T

        @pl.loop(0, width // TILE)
        def _(j):
            cols = aligned(j * TILE, TILE)
            write(cols, dot(left, wg[:, cols]) + dot(right, wu[:, cols]))

    def begin_normed(other, side, hop):
        @pl.when(hop > 1)
        def _():
            normed_fold.mate_sent(side)

        normed_fold.begin_one(other, side + (2 - side) * (1 // (hop + 1)), produce_normed)

    def forward_blocks(hop):
        def act(other, side):
            forward_block(other)

            @pl.when(jnp.logical_not(normed_fold.fed(side)))
            def _():
                begin_normed(other, side, hop)
                normed_fold.leave(other, side, hop)

        net.sides(hop, act)

    def begin_fed(hop):
        def act(other, side):
            @pl.when((hop == 0) | normed_fold.fed(side))
            def _():
                begin_normed(other, side, hop)

        blocks(hop, act)

    n2_line.here()
    for spread in (spread_g, spread_u, spread_d):
        spread.finish()
    forward_block(net.z)

    @pl.loop(1, net.n_l)
    def _(hop):
        n2_line.step(hop)
        pairs(n2_line, hop)
        forward_blocks(hop)
        begin_fed(hop - 1)

    begin_fed(net.n_l - 1)
    normed_fold.open_total()

    def weight_terms(task):
        at, kind = net.n_f - 1 - task // 3, task % 3
        cols = aligned(gate_sum.owner(at) * depth, depth)
        for way, (grid_sum, left, right) in enumerate(
            ((down_sum, hidden, gout), (gate_sum, dgate, rows), (up_sum, dup, rows))
        ):

            @pl.when(kind == way)
            def _():
                half = left.shape[0] // 2

                @pl.loop(0, 2)
                def _(part):
                    units = aligned(part * half, half, 16)
                    grid_sum.stage[at, units, :] = dot(left[units, :], right[:, cols]).astype(BF)

                grid_sum.first(at)

    tasks = 3 * net.n_f
    slots = 2 * normed_fold.pieces * (net.n_l - 1)
    each = -(-tasks // slots)

    def between(slot):
        @pl.loop(0, each)
        def _(i):
            pl.when(slot * each + i < tasks)(lambda: weight_terms(slot * each + i))

    for at in range(1, net.n_l):
        normed_fold.wave(at, near=True, between=between)
    n2_line.finish()

    def write_middle(i, span, value):
        value = value + gout[aligned(net.s * chunk + i * 32, 32), :].astype(F32)
        dmid_o[span, :] = value
        low[span, :] = value.astype(BF)

    terms_o[...] = jnp.zeros(terms_o.shape, F32)
    norm_backward(chunk, mid, total, gain_two, terms_o, 2, write_middle)
    dm_line.start()
    normed_fold.finish()

    def produce_top(place, write):
        left = hidden[:, aligned(place * pair, pair)].T

        @pl.loop(0, width // TILE)
        def _(j):
            cols = aligned(j * TILE, TILE)
            write(cols, dot(left, wd[:, cols]))

    dm_line.here()
    dm_line.step(1)
    top_fold.begin(produce_top)
    top_fold.open_total()
    for at in range(1, net.n_l):
        if at + 1 < net.n_l:
            dm_line.step(at + 1)
        top_fold.wave(at)

    @pl.loop(0, chunk // 32)
    def _(i):
        span = aligned(i * 32, 32)
        top_fold.out[net.z, span, :] = (mid[span, :] + total[span, :]).astype(BF)

    copies.start(top_fold.out.at[net.z], top_o)
    top_fold.finish()
    pl.loop(1, net.n_l)(lambda hop: pairs(dm_line, hop))
    gout_line.finish()
    dm_line.finish()
    hands = []
    for grid_sum, out in zip(sums, (down_o, gate_o, up_o)):
        grid_sum.sum_first()
        hands.extend(grid_sum.hand_on(out))
        for copy in grid_sum.hand_on(out):
            copy.start()
    for grid_sum in sums:
        grid_sum.finish_first()
    for copy in hands:
        copy.wait()
    copies.wait()


def layer_part(tokens, packet, wq, wo, wg, wu, wd, gout, tables):
    chunk, width = tokens.shape
    n_f, n_s = lax.axis_size("fsdp"), lax.axis_size("seq")
    length = chunk * n_s
    depth, columns = wq.shape[1:]
    units = wg.shape[0]
    shape = jax.ShapeDtypeStruct
    wide, head, turned, weight = (length, width), (length, columns), (units, length), (units, width)
    return pl.pallas_call(
        layer_kernel,
        name="layer",
        out_shape=[
            shape(head, BF),
            shape(head, BF),
            shape((columns, length), BF),
            shape(head, BF),
            shape(head, BF),
            shape((8, length), F32),
            shape(wide, BF),
            shape((SMALL, width), F32),
            shape((3, width, columns), BF),
            shape((columns, width), BF),
            shape(wide, BF),
            shape((chunk, width), F32),
            shape((chunk, width), BF),
            shape((SMALL, width), F32),
            *[shape((GridEnd.count(n_f), units // 2, depth), BF)] * 3,
        ],
        in_specs=[ANY, VMEM, *[ANY] * 6, VMEM, VMEM],
        out_specs=[*[ANY] * 5, VMEM, ANY, VMEM, *[ANY] * 3, VMEM, ANY, VMEM, *[ANY] * 3],
        scratch_shapes=[
            pltpu.VMEM(wide, BF),
            pltpu.VMEM(wide, BF),
            pltpu.VMEM((3, width, columns), BF),
            pltpu.VMEM((columns, width), BF),
            *[pltpu.VMEM(weight, BF)] * 3,
            pltpu.VMEM(head, BF),
            pltpu.VMEM(head, BF),
            pltpu.VMEM((columns, 2 * chunk), BF),
            pltpu.VMEM((2 * chunk, columns), BF),
            pltpu.VMEM((columns, length), BF),
            pltpu.VMEM((columns, 2 * chunk), F32),
            pltpu.VMEM(head, BF),
            *[pltpu.VMEM(turned, BF)] * 3,
            pltpu.VMEM((chunk, width), F32),
            pltpu.VMEM((chunk, width), BF),
            pltpu.VMEM((n_s, n_f, SMALL, 128), F32),
            *Fold.shared(chunk, width),
            *Fold.buffers(n_s, chunk, width),
            *Fold.sems(n_s) * 3,
            *Line.sems(n_s) * 4,
            *[pltpu.SemaphoreType.DMA((Spread.count(n_f),))] * 5,
            *GridSum.scratch(n_f, units, depth) * 3,
            pltpu.SemaphoreType.DMA((Packets.count(n_f, n_s),)),
            pltpu.SemaphoreType.DMA((8,)),
            pltpu.SemaphoreType.DMA((4,)),
        ],
        compiler_params=pltpu.CompilerParams(
            collective_id=1, has_side_effects=True, vmem_limit_bytes=VMEM_BYTES
        ),
        cost_estimate=pl.CostEstimate(
            flops=2 * length * width * (4 * columns + 9 * units),
            bytes_accessed=8 * length * width,
            transcendentals=length * (length * columns // HEAD + units),
        ),
    )(tokens, packet, wq, wo, wg, wu, wd, gout, *tables)


def back_kernel(
    dm_in,
    wo_in,
    att_in,
    q_in,
    k_in,
    kt_in,
    v_in,
    n1_in,
    wq_in,
    down_in,
    gate_in,
    up_in,
    lse,
    tok,
    dmid,
    gains,
    terms_in,
    cosine,
    sine,
    gin_o,
    small_o,
    out_o,
    qkv_o,
    down_o,
    gate_o,
    up_o,
    dm,
    wo,
    att,
    q,
    k,
    kt,
    v,
    n1,
    wq,
    datt,
    dk,
    dv,
    dqt,
    dproj,
    terms,
    tiles,
    total,
    *rest,
):
    net = Net()
    chunk, width = tok.shape
    length, columns = q_in.shape
    heads = columns // HEAD
    pair = 2 * chunk
    depth = width // net.n_f
    block = 256
    buffers, rest = rest[:4], rest[4:]
    fold_sems, rest = rest[:4], rest[4:]
    packet_scratch, rest = rest[:5], rest[5:]
    out_sum, qkv_sum = GridSum(net, *rest[:3]), GridSum(net, *rest[3:6])
    ends = [GridEnd(net, *rest[at : at + 3]) for at in (6, 9, 12)]
    copy_sems = rest[15]

    copies = Copies(copy_sems)
    loads = [
        copies.start(src, dst)
        for src, dst in (
            (dm_in, dm),
            (wo_in, wo),
            (att_in, att),
            (q_in, q),
            (k_in, k),
            (kt_in, kt),
            (v_in, v),
            (n1_in, n1),
            (wq_in, wq),
            (down_in, ends[0].sums),
            (gate_in, ends[1].sums),
            (up_in, ends[2].sums),
        )
    ]
    net.barrier()
    copies.wait(*loads[:2])

    @pl.loop(0, length // block)
    def _(i):
        span = aligned(i * block, block)
        datt[span, :] = dot_nt(dm[span, :], wo[...]).astype(BF)
        dk[span, :] = jnp.zeros((block, columns), F32)
        dv[span, :] = jnp.zeros((block, columns), F32)

    copies.wait()
    for end in ends:
        end.start()

    @pl.loop(0, heads)
    def _(head):
        lane = lax.broadcasted_iota(jnp.int32, (1, columns), 1)
        here = jnp.where(lane // HEAD == head, 1.0, 0.0).astype(BF)
        scale = HEAD**-0.5
        visible = lax.broadcasted_iota(jnp.int32, (block, block), 0) <= lax.broadcasted_iota(
            jnp.int32, (block, block), 1
        )
        head_rows = aligned(head * HEAD, HEAD)
        for i in range(length // block):
            lo, hi = i * block, (i + 1) * block
            query = q[lo:hi, :] * (here * scale)
            upstream = datt[lo:hi, :] * here
            logsum = lse[pl.ds(head, 1), lo:hi]

            def part(at, end, mask):
                probs = jnp.exp(dot_nt(k[at:end, :], query) - logsum)
                if mask:
                    probs = jnp.where(visible, probs, 0.0)
                grads = dot_nt(v[at:end, :], upstream)
                dv[at:end, :] = dv[at:end, :] + dot(probs.astype(BF), upstream)
                return probs, grads, jnp.sum(probs * grads, 0, keepdims=True)

            def scored(at, end, probs, grads, inner):
                scores = (probs * (grads - inner)).astype(BF)
                dk[at:end, :] = dk[at:end, :] + dot(scores, query)
                return dot(kt[head_rows, at:end], scores)

            near, near_grads, inner = part(lo, hi, True)
            if i:
                far, far_grads, more = part(0, lo, False)
                inner = inner + more
            out = scored(lo, hi, near, near_grads, inner)
            if i:
                out = out + scored(0, lo, far, far_grads, inner)
            dqt[head_rows, lo:hi] = out * scale

    terms[...] = terms_in[...]
    bias_cols = aligned(net.s * columns, columns)

    @pl.loop(0, length // block)
    def _(i):
        span = aligned(i * block, block)
        tables = cosine[span, :], -sine[span, :]
        parts = [
            rotary(dqt[:, span].T.astype(BF).astype(F32), *tables).astype(BF),
            rotary(dk[span, :].astype(BF).astype(F32), *tables).astype(BF),
            dv[span, :].astype(BF),
        ]
        for kind in range(3):
            dproj[kind, span, :] = parts[kind]
            row = slice(4 + kind, 5 + kind)
            terms[row, bias_cols] = terms[row, bias_cols] + jnp.sum(parts[kind].astype(F32), 0, keepdims=True)

    def weight_terms(task):
        at = net.n_f - 1 - task // 2
        cols = aligned(qkv_sum.owner(at) * depth, depth)

        @pl.when(task % 2 == 0)
        def _():
            left = n1[:, cols].T
            for kind in range(3):
                qkv_sum.stage[at, kind * depth : (kind + 1) * depth, :] = dot(left, dproj[kind]).astype(BF)
            qkv_sum.first(at)

        @pl.when(task % 2 == 1)
        def _():
            out_sum.stage[at] = dot_tn(att[...], dm[:, cols]).astype(BF)
            out_sum.first(at)

    def produce(place, write):
        span = aligned(place * pair, pair)

        @pl.loop(0, width // TILE)
        def _(j):
            cols = aligned(j * TILE, TILE)
            value = dot_nt(dproj[0, span, :], wq[0, cols, :])
            for kind in range(1, 3):
                value = value + dot_nt(dproj[kind, span, :], wq[kind, cols, :])
            write(cols, value)

    fold = Fold(net, tiles, total, *buffers, *fold_sems)
    fold.begin(produce)
    fold.open_total()
    tasks = 2 * net.n_f
    waves = max(net.n_l - 2, 1)
    each = -(-tasks // (2 * fold.pieces * waves))

    def between(slot):
        @pl.loop(0, each)
        def _(i):
            pl.when(slot * each + i < tasks)(lambda: weight_terms(slot * each + i))

    for at in range(1, waves + 1):
        fold.wave(at, between=between)
    for grid_sum in (qkv_sum, out_sum):
        grid_sum.second()
    for at in range(waves + 1, net.n_l):
        fold.wave(at)

    def write_input(i, span, value):
        gin_o[span, :] = value + dmid[span, :]

    norm_backward(chunk, tok, total, gains[0:1, :], terms, 0, write_input)
    for end, out in zip(ends, (down_o, gate_o, up_o)):
        end.last(out)
    PacketSum(net, *packet_scratch).run(terms, small_o, width // (net.n_f * net.n_s))
    fold.finish()
    for grid_sum, out in ((qkv_sum, qkv_o), (out_sum, out_o)):
        grid_sum.last(out)
        grid_sum.finish()


def back_part(dm, wo, att, q, k, kt, v, n1, wq, down, gate, up, lse, tokens, dmid, gains, terms, tables):
    chunk, width = tokens.shape
    n_f, n_s = lax.axis_size("fsdp"), lax.axis_size("seq")
    length, columns = q.shape
    depth = width // n_f
    units = 2 * gate.shape[1]
    shape = jax.ShapeDtypeStruct
    return pl.pallas_call(
        back_kernel,
        name="back",
        out_shape=[
            shape((chunk, width), F32),
            shape((SMALL, 128), F32),
            shape((columns, depth), F32),
            shape((3 * depth, columns), F32),
            *[shape((units, depth), F32)] * 3,
        ],
        in_specs=[ANY] * 12 + [VMEM] * 7,
        out_specs=[VMEM] * 7,
        scratch_shapes=[
            pltpu.VMEM((length, width), BF),
            pltpu.VMEM((columns, width), BF),
            pltpu.VMEM((length, columns), BF),
            pltpu.VMEM((length, columns), BF),
            pltpu.VMEM((length, columns), BF),
            pltpu.VMEM((columns, length), BF),
            pltpu.VMEM((length, columns), BF),
            pltpu.VMEM((length, width), BF),
            pltpu.VMEM((3, width, columns), BF),
            pltpu.VMEM((length, columns), BF),
            pltpu.VMEM((length, columns), F32),
            pltpu.VMEM((length, columns), F32),
            pltpu.VMEM((columns, length), F32),
            pltpu.VMEM((3, length, columns), BF),
            pltpu.VMEM((SMALL, width), F32),
            *Fold.shared(chunk, width),
            *Fold.buffers(n_s, chunk, width),
            *Fold.sems(n_s),
            *PacketSum.scratch(n_f, n_s),
            *GridSum.scratch(n_f, columns, depth),
            *GridSum.scratch(n_f, 3 * depth, columns),
            *GridEnd.scratch(n_f, units, depth) * 3,
            pltpu.SemaphoreType.DMA((12,)),
        ],
        compiler_params=pltpu.CompilerParams(
            collective_id=3, has_side_effects=True, vmem_limit_bytes=VMEM_BYTES
        ),
        cost_estimate=pl.CostEstimate(
            flops=2 * length * columns * (8 * width + 5 * length),
            bytes_accessed=4 * length * width,
            transcendentals=length * length * columns // HEAD,
        ),
    )(dm, wo, att, q, k, kt, v, n1, wq, down, gate, up, lse, tokens, dmid, gains, terms, *tables)


def per_device(
    tokens,
    gain_one,
    shift_one,
    w_qkv,
    b_qkv,
    w_out,
    gain_two,
    shift_two,
    w_gate,
    w_up,
    w_down,
    grad_output,
):
    length = tokens.shape[1] * lax.axis_size("seq")
    width = gain_one.shape[0]
    packet = jnp.concatenate(
        [jnp.stack([gain_one, shift_one, gain_two, shift_two]), b_qkv, jnp.zeros((1, width), BF)]
    )
    packet = jnp.pad(packet.astype(F32), ((0, 0), (0, 128 - width)))
    tables = rotary_tables(length)
    q, k, kt, v, att, lse, n1, gains, wq, wo, dm, dmid, top, terms, gate, up, down = layer_part(
        tokens[0], packet, w_qkv.transpose(1, 0, 2), w_out, w_gate.T, w_up.T, w_down, grad_output[0], tables
    )
    grad_input, small, out, qkv, down, gate, up = back_part(
        dm, wo, att, q, k, kt, v, n1, wq, down, gate, up, lse, tokens[0], dmid, gains, terms, tables
    )

    return (
        top[None],
        grad_input[None],
        small[0, :width],
        small[1, :width],
        qkv.reshape(3, -1, qkv.shape[1]).transpose(1, 0, 2),
        small[4:7, :width],
        out,
        small[2, :width],
        small[3, :width],
        gate.T,
        up.T,
        down,
    )


def solution(mesh):
    whole = P(("fsdp", "seq"))
    rows = P("fsdp", "seq", None)
    inner = P("seq", "fsdp")
    outer = P("fsdp", "seq")
    heads = P("fsdp", None, "seq")
    bias = P(None, ("fsdp", "seq"))
    return jax.shard_map(
        per_device,
        mesh=mesh,
        in_specs=(rows, whole, whole, heads, bias, inner, whole, whole, outer, outer, inner, rows),
        out_specs=(rows, rows, whole, whole, heads, bias, inner, whole, whole, outer, outer, inner),
        check_vma=False,
    )
```

```python
import functools

import jax
import jax.numpy as jnp
import numpy as np
from jax import lax
from jax.experimental import pallas as pl
from jax.experimental.pallas import tpu as pltpu
from jax.sharding import PartitionSpec as P

HEAD = 64
ROT = 16
EPSILON = 1e-05
NEG_LARGE = -1e30
MESH = pl.DeviceIdType.MESH
ANY = pl.BlockSpec(memory_space=pl.ANY)
VMEM = pl.BlockSpec(memory_space=pltpu.VMEM)
BF = jnp.bfloat16
F32 = jnp.float32
VMEM_BYTES = 60 * 2**20
TILE = 512
SMALL = 8


def put(src, dst, send, recv, **device):
    return pltpu.make_async_remote_copy(
        src_ref=src, dst_ref=dst, send_sem=send, recv_sem=recv, device_id=device, device_id_type=MESH
    )


def dot(left, right):
    return jnp.dot(left, right, preferred_element_type=F32)


def dot_nt(left, right):
    return lax.dot_general(left, right, (((1,), (1,)), ((), ())), preferred_element_type=F32)


def dot_tn(left, right):
    return lax.dot_general(left, right, (((0,), (0,)), ((), ())), preferred_element_type=F32)


def aligned(start, size, unit=None):
    return pl.ds(pl.multiple_of(start, unit or size), size)


class Net:
    def __init__(self):
        self.n_f, self.n_s = lax.axis_size("fsdp"), lax.axis_size("seq")
        self.tall = 2 if self.n_f % 2 == 0 else 1
        self.wide = self.n_f // self.tall
        self.n_l = self.n_s // 2
        self.f, self.s = lax.axis_index("fsdp"), lax.axis_index("seq")
        self.a, self.b = self.f // self.wide, self.f % self.wide
        self.z, self.c = self.s // 2, self.s % 2
        self.mate = self.s + 1 - 2 * self.c

    def barrier(self):
        sem = pltpu.get_barrier_semaphore()
        for k in range(1, self.n_f):
            pl.semaphore_signal(
                sem, inc=1, device_id={"fsdp": (self.f + k) % self.n_f}, device_id_type=MESH
            )
        for k in range(1, self.n_s):
            pl.semaphore_signal(
                sem, inc=1, device_id={"seq": (self.s + k) % self.n_s}, device_id_type=MESH
            )
        pl.semaphore_wait(sem, self.n_f + self.n_s - 2)

    def sides(self, hop, act):
        @pl.loop(0, 2)
        def _(side):
            other = self.z + (2 * side - 1) * hop

            @pl.when((other >= 0) & (other < self.n_l))
            def _():
                act(other, side)


class Spread:
    def __init__(self, net, src, part, sems):
        self.net, self.src, self.part, self.sems = net, src, part, sems
        self.rows = [j for j in range(1, net.wide)]
        self.cols = [i for i in range(1, net.tall)]

    @staticmethod
    def count(n_f):
        tall = 2 if n_f % 2 == 0 else 1
        wide = n_f // tall
        return 1 + 2 * (wide - 1) + 2 * (tall - 1) + 4 * (wide - 1) * (tall - 1)

    def at(self, kind, i, j):
        w, t = len(self.rows), len(self.cols)
        base = {
            "own": 0,
            "row": 1,
            "col": 1 + 2 * w,
            "half0": 1 + 2 * w + 2 * t,
            "half1": 1 + 2 * w + 2 * t + 2 * w * t,
        }[kind]
        if kind == "own":
            return self.sems.at[0]
        k = j - 1 if kind == "row" else i - 1 if kind == "col" else (i - 1) * w + j - 1
        return self.sems.at[base + 2 * k], self.sems.at[base + 2 * k + 1]

    def rank(self, i, j):
        net = self.net
        return ((net.a + i) % net.tall) * net.wide + (net.b + j) % net.wide

    def back(self, i, j):
        net = self.net
        return ((net.a - i + net.tall) % net.tall) * net.wide + (net.b - j + net.wide) % net.wide

    def own(self):
        return pltpu.make_async_copy(self.src, self.part(self.net.f, None), self.at("own", 0, 0))

    def first(self, i, j):
        send, recv = self.at("row" if i == 0 else "col", i, j)
        return put(self.src, self.part(self.net.f, None), send, recv, fsdp=self.rank(i, j))

    def came(self, i, j):
        send, recv = self.at("row" if i == 0 else "col", i, j)
        place = self.part(self.back(i, j), None)
        return put(place, place, send, recv, fsdp=self.rank(i, j))

    def second(self, half, i, j, came=False):
        send, recv = self.at("half0" if half == 0 else "half1", i, j)
        origin = self.back(i, j) if came else self.back(0, j) if half == 0 else self.back(i, 0)
        place = self.part(origin, half)
        return put(place, place, send, recv, fsdp=self.rank(i, 0) if half == 0 else self.rank(0, j))

    def start(self):
        self.own().start()
        for i in self.cols:
            self.first(i, 0).start()
        for j in self.rows:
            self.first(0, j).start()

    def relay(self):
        for j in self.rows:
            self.came(0, j).wait_recv()
            for i in self.cols:
                self.second(0, i, j).start()
        for i in self.cols:
            self.came(i, 0).wait_recv()
            for j in self.rows:
                self.second(1, i, j).start()

    def finish(self):
        self.own().wait()
        for j in self.rows:
            self.first(0, j).wait_send()
        for i in self.cols:
            self.first(i, 0).wait_send()
        for i in self.cols:
            for j in self.rows:
                for half in range(2):
                    self.second(half, i, j, came=True).wait_recv()
                    self.second(half, i, j).wait_send()


class Cast:
    def __init__(self, net, src, part, sems):
        self.net, self.src, self.part, self.sems = net, src, part, sems

    def own(self):
        return pltpu.make_async_copy(self.src, self.part(self.net.f, None), self.sems.at[0])

    def copy(self, k):
        net = self.net
        return put(
            self.src,
            self.part(net.f, None),
            self.sems.at[2 * k - 1],
            self.sems.at[2 * k],
            fsdp=(net.f + k) % net.n_f,
        )

    def start(self):
        self.own().start()
        for k in range(1, self.net.n_f):
            self.copy(k).start()

    def finish(self):
        net = self.net
        self.own().wait()
        for k in range(1, net.n_f):
            place = self.part((net.f - k + net.n_f) % net.n_f, None)
            put(place, place, self.sems.at[2 * k - 1], self.sems.at[2 * k], fsdp=(net.f + k) % net.n_f).wait_recv()
            self.copy(k).wait_send()


class Line:
    def __init__(self, net, src, part, recv, send, local):
        self.net, self.src, self.part, self.recv, self.send, self.local = net, src, part, recv, send, local
        self.pieces = recv.shape[1]
        self.rows = src.shape[0] // self.pieces

    @staticmethod
    def sems(n_s, pieces=2):
        return [
            pltpu.SemaphoreType.DMA((n_s, pieces)),
            pltpu.SemaphoreType.DMA((4, n_s // 2, pieces)),
            pltpu.SemaphoreType.DMA((1,)),
        ]

    def cut(self, ref, piece):
        return ref.at[aligned(piece * self.rows, self.rows)]

    def own(self):
        return pltpu.make_async_copy(self.src, self.part(self.net.s), self.local.at[0])

    def on_line(self, src, chunk, side, hop, piece):
        return put(
            self.cut(src, piece),
            self.cut(self.part(chunk), piece),
            self.send.at[side, hop, piece],
            self.recv.at[chunk, piece],
            seq=self.net.s + 2 - 4 * side,
        )

    def to_mate(self, src, chunk, side, hop, piece):
        return put(
            self.cut(src, piece),
            self.cut(self.part(chunk), piece),
            self.send.at[2 + side, hop, piece],
            self.recv.at[chunk, piece],
            seq=self.net.mate,
        )

    def goes_on(self, side):
        after = self.net.z + 1 - 2 * side
        return (after >= 0) & (after < self.net.n_l)

    def each_piece(self, act):
        pl.loop(0, self.pieces)(act)

    def start(self):
        net = self.net

        @self.each_piece
        def _(piece):
            for side in range(2):

                @pl.when(self.goes_on(side))
                def _():
                    self.on_line(self.src, net.s, side, 0, piece).start()

            self.to_mate(self.src, net.s, 0, 0, piece).start()

        self.own().start()

    def came(self, chunk, piece):
        place = self.cut(self.part(chunk), piece)
        put(place, place, self.send.at[0, 0, 0], self.recv.at[chunk, piece], seq=self.net.mate).wait_recv()

    def step(self, hop):
        net = self.net

        @self.each_piece
        def _(piece):
            def act(other, side):
                chunk = 2 * other + net.c
                self.came(chunk, piece)

                @pl.when(self.goes_on(side))
                def _():
                    self.on_line(self.part(chunk), chunk, side, hop, piece).start()

                self.to_mate(self.part(chunk), chunk, side, hop, piece).start()

            net.sides(hop, act)

    def pair(self, other):
        @self.each_piece
        def _(piece):
            self.came(2 * other + 1 - self.net.c, piece)

    def here(self):
        self.own().wait()
        self.pair(self.net.z)

    def finish(self):
        net = self.net

        @self.each_piece
        def _(piece):
            for side in range(2):

                @pl.when(self.goes_on(side))
                def _():
                    self.on_line(self.src, net.s, side, 0, piece).wait_send()

            self.to_mate(self.src, net.s, 0, 0, piece).wait_send()

            @pl.loop(1, net.n_l)
            def _(hop):
                def act(other, side):
                    chunk = 2 * other + net.c

                    @pl.when(self.goes_on(side))
                    def _():
                        self.on_line(self.part(chunk), chunk, side, hop, piece).wait_send()

                    self.to_mate(self.part(chunk), chunk, side, hop, piece).wait_send()

                net.sides(hop, act)


class Packets:
    def __init__(self, net, src, buf, sems):
        self.net, self.src, self.buf, self.sems = net, src, buf, sems

    @staticmethod
    def count(n_f, n_s):
        return 1 + 2 * (n_f - 1) + 2 * (n_s - 1)

    def own(self):
        net = self.net
        return pltpu.make_async_copy(self.src, self.buf.at[net.s, net.f], self.sems.at[0])

    def one(self, k, came=False):
        net = self.net
        f = (net.f - k + net.n_f) % net.n_f if came else net.f
        place = self.buf.at[net.s, f]
        return put(
            place if came else self.src,
            place,
            self.sems.at[2 * k - 1],
            self.sems.at[2 * k],
            fsdp=(net.f + k) % net.n_f,
        )

    def two(self, k, came=False):
        net = self.net
        place = self.buf.at[(net.s - k + net.n_s) % net.n_s if came else net.s]
        at = 2 * (net.n_f - 1) + 2 * k - 1
        return put(place, place, self.sems.at[at], self.sems.at[at + 1], seq=(net.s + k) % net.n_s)

    def start(self):
        self.own().start()
        for k in range(1, self.net.n_f):
            self.one(k).start()

    def middle(self):
        self.own().wait()
        for k in range(1, self.net.n_f):
            self.one(k, came=True).wait_recv()
            self.one(k).wait_send()
        for k in range(1, self.net.n_s):
            self.two(k).start()

    def finish(self):
        for k in range(1, self.net.n_s):
            self.two(k, came=True).wait_recv()
            self.two(k).wait_send()

    def unpack(self, out, width):
        net = self.net
        per = 128 // width
        for tile in range(net.n_f * net.n_s // per):
            total = None
            for j in range(per):
                f, s = divmod(tile * per + j, net.n_s)
                piece = self.buf[s, f]
                if j:
                    piece = pltpu.roll(piece, j * width, axis=1)
                total = piece if total is None else total + piece
            out[:, tile * 128 : (tile + 1) * 128] = total


def rotary(values, cosine, sine):
    columns = values.shape[1]
    half = ROT // 2
    times = columns // 128

    def wide(table):
        return table if times == 1 else jnp.concatenate([table] * times, axis=1)

    lane = lax.broadcasted_iota(jnp.int32, values.shape, 1)
    other = jnp.where(
        lane % HEAD < half, pltpu.roll(values, columns - half, axis=1), pltpu.roll(values, half, axis=1)
    )
    return values * wide(cosine) + other * wide(sine)


def rotary_tables(length):
    half = ROT // 2
    freqs = np.float32(10000.0) ** (-np.arange(half, dtype=np.float32) * np.float32(2.0 / ROT))
    angles = np.arange(length, dtype=np.float32)[:, None] * freqs[None, :].astype(np.float32)
    cosine, sine = np.cos(angles), np.sin(angles)
    rest = np.zeros((length, HEAD - ROT), np.float32)
    keep = np.concatenate([cosine, cosine, rest + 1], 1)
    swap = np.concatenate([-sine, sine, rest], 1)
    return [np.tile(t, (1, 128 // HEAD)).astype(np.float32) for t in (keep, swap)]


def normalize(values):
    center = values - jnp.mean(values, -1, keepdims=True)
    inverse = lax.rsqrt(jnp.mean(center * center, -1, keepdims=True) + EPSILON)
    return center * inverse, inverse


class Copies:
    def __init__(self, sems):
        self.sems, self.all, self.open = sems, [], []

    def start(self, src, dst):
        copy = pltpu.make_async_copy(src, dst, self.sems.at[len(self.all)])
        copy.start()
        self.all.append(copy)
        self.open.append(copy)
        return copy

    def wait(self, *copies):
        for copy in copies or list(self.open):
            copy.wait()
            self.open.remove(copy)


def columns_of(ref, depth):
    half_rows = ref.shape[0] // 2

    def part(f, half):
        span = aligned(f * depth, depth)
        if half is None:
            return ref.at[:, span]
        return ref.at[pl.ds(half * half_rows, half_rows), span]

    return part


def rows_of(ref, chunk):
    return lambda s: ref.at[aligned(s * chunk, chunk)]


class Fold:
    def __init__(self, net, tile, total, mate_in, coming, mate_out, out, mate_send, mate_recv, send, recv):
        self.net, self.tile, self.total = net, tile, total
        self.mate_in, self.coming, self.mate_out, self.out = mate_in, coming, mate_out, out
        self.mate_send, self.mate_recv, self.send, self.recv = mate_send, mate_recv, send, recv
        self.chunk = total.shape[0]
        self.pieces = recv.shape[1]
        self.rows = self.chunk // self.pieces

    @staticmethod
    def shared(chunk, width):
        return [pltpu.VMEM((2 * chunk, TILE), F32), pltpu.VMEM((chunk, width), F32)]

    @staticmethod
    def buffers(n_s, chunk, width):
        n_l = n_s // 2
        return [
            pltpu.VMEM((n_l, chunk, width), BF),
            pltpu.VMEM((n_l + 1, chunk, width), BF),
            pltpu.VMEM((3, chunk, width), BF),
            pltpu.VMEM((n_l, chunk, width), BF),
        ]

    @staticmethod
    def sems(n_s, pieces=4):
        n_l = n_s // 2
        return [
            pltpu.SemaphoreType.DMA((3, pieces)),
            pltpu.SemaphoreType.DMA((n_l, pieces)),
            pltpu.SemaphoreType.DMA((n_l, pieces)),
            pltpu.SemaphoreType.DMA((n_l + 1, pieces)),
        ]

    def place(self, other):
        return (other >= 0) & (other < self.net.n_l)

    def fed(self, side):
        return self.place(self.net.z + 1 - 2 * side)

    def span(self, piece):
        return aligned(piece * self.rows, self.rows)

    def each_piece(self, act):
        pl.loop(0, self.pieces)(act)

    def to_mate(self, target, slot, piece):
        span = self.span(piece)
        return put(
            self.mate_out.at[slot, span],
            self.mate_in.at[target, span],
            self.mate_send.at[slot, piece],
            self.mate_recv.at[target, piece],
            seq=self.net.mate,
        )

    def onward(self, target, side, hop, piece):
        span = self.span(piece)
        slot = target + (self.net.n_l - target) * (1 - side) * (1 // hop)
        return put(
            self.out.at[target, span],
            self.coming.at[slot, span],
            self.send.at[target, piece],
            self.recv.at[slot, piece],
            seq=self.net.s + 4 * side - 2,
        )

    def came(self, slot, piece):
        place = self.coming.at[slot, self.span(piece)]
        put(place, place, self.send.at[0, 0], self.recv.at[slot, piece], seq=self.net.mate).wait_recv()

    def mate_sent(self, slot):
        self.each_piece(lambda piece: self.to_mate(self.net.z, slot, piece).wait_send())

    def begin_one(self, target, slot, produce):
        mine = aligned(self.net.c * self.chunk, self.chunk)
        theirs = aligned((1 - self.net.c) * self.chunk, self.chunk)

        def write(cols, value):
            self.tile[...] = value
            self.out[target, :, cols] = self.tile[mine, :].astype(BF)
            self.mate_out[slot, :, cols] = self.tile[theirs, :].astype(BF)

        produce(target, write)
        self.each_piece(lambda piece: self.to_mate(target, slot, piece).start())

    def targets(self, wave, near, act):
        net = self.net
        above = wave if near else net.n_l - wave

        @pl.loop(0, 2)
        def _(turn):
            side = (1 - (2 * net.z) // net.n_l + turn) % 2
            target = net.n_l - 1 - above + (2 * above - net.n_l + 1) * side
            hop = (target - net.z) * (2 * side - 1)
            pl.when(hop > 0)(lambda: act(target, side, hop, turn))

    def begins(self, wave, produce):
        net = self.net
        above = net.n_l - wave

        @pl.loop(0, 3)
        def _(turn):
            here = turn // 2
            side = (1 - (2 * net.z) // net.n_l + turn) % 2
            target = net.n_l - 1 - above + (2 * above - net.n_l + 1) * side
            hop = (target - net.z) * (2 * side - 1)

            @pl.when(((here == 0) & (hop > 0)) | ((here == 1) & (wave == min(2, net.n_l - 1))))
            def _():
                @pl.when((here == 0) & self.place(target + 2 * side - 1))
                def _():
                    self.mate_sent(side)

                self.begin_one(
                    target + (net.z - target) * here, side + (2 - side) * here, produce
                )

    def leave(self, wave, near=False):
        def act(target, side, hop, turn):
            @pl.when(jnp.logical_not(self.fed(side)))
            def _():
                self.each_piece(lambda piece: self.pass_piece(target, side, hop, piece, False))

        self.targets(wave, near, act)

    def passes(self, wave, near=False):
        def act(target, side, hop, turn):
            @pl.when(self.fed(side))
            def _():
                self.each_piece(lambda piece: self.pass_piece(target, side, hop, piece, True))

        self.targets(wave, near, act)

    def passes_between(self, wave, near, between):
        net = self.net
        above = wave if near else net.n_l - wave

        @pl.loop(0, 2)
        def _(turn):
            side = (1 - (2 * net.z) // net.n_l + turn) % 2
            target = net.n_l - 1 - above + (2 * above - net.n_l + 1) * side
            hop = (target - net.z) * (2 * side - 1)

            @self.each_piece
            def _(piece):
                @pl.when((hop > 0) & self.fed(side))
                def _():
                    self.pass_piece(target, side, hop, piece, True)

                between(turn, piece)

    def far(self, produce, begun=None, passing=True):
        net = self.net

        @pl.loop(1, net.n_l)
        def _(wave):
            self.begins(wave, produce)
            pl.when(wave > 1)(lambda: self.leave(wave - 1))
            if begun is not None:
                begun(wave)
            if passing:
                self.passes(wave)

        self.leave(net.n_l - 1)

    def pass_piece(self, target, side, hop, piece, fed):
        self.to_mate(target, 0, piece).wait_recv()
        span = self.span(piece)
        value = self.out[target, span, :].astype(F32) + self.mate_in[target, span, :].astype(F32)
        if fed:
            self.came(target, piece)
            value = value + self.coming[target, span, :].astype(F32)
        self.out[target, span, :] = value.astype(BF)
        self.onward(target, side, hop, piece).start()

    def finals(self):
        net = self.net

        @self.each_piece
        def _(piece):
            self.to_mate(net.z, 0, piece).wait_recv()
            span = self.span(piece)
            self.total[span, :] = self.out[net.z, span, :].astype(F32) + self.mate_in[net.z, span, :].astype(F32)

        @pl.loop(0, 2)
        def _(turn):
            side = (1 - (2 * net.z) // net.n_l + turn) % 2

            @pl.when(self.fed(side))
            def _():
                slot = net.z + (net.n_l - net.z) * (1 - side)

                @self.each_piece
                def _(piece):
                    span = self.span(piece)
                    self.came(slot, piece)
                    self.total[span, :] = self.total[span, :] + self.coming[slot, span, :].astype(F32)

    def finish(self):
        net = self.net
        self.mate_sent(2)
        for side in range(2):
            pl.when(self.place(net.z + 2 * side - 1))(functools.partial(self.mate_sent, side))

        @pl.loop(1, net.n_l)
        def _(hop):
            net.sides(
                hop,
                lambda target, side: self.each_piece(
                    lambda piece: self.onward(target, side, hop, piece).wait_send()
                ),
            )


class GridSum:
    def __init__(self, net, stage, came, sems):
        self.net, self.stage, self.came, self.sems = net, stage, came, sems
        self.half = stage.shape[1] // 2
        self.rows = next(r for r in (176, 128, 96, 64, 32, 16) if self.half % r == 0)
        self.cols = range(1, net.tall)
        self.along = range(1, net.wide)
        self.bases = self.layout(net.n_f)

    @staticmethod
    def layout(n_f):
        tall = 2 if n_f % 2 == 0 else 1
        wide = n_f // tall
        sizes = [(wide - 1) * tall, (tall - 1) * wide, tall - 1, wide - 1]
        return [sum(sizes[:at]) for at in range(5)]

    @staticmethod
    def scratch(n_f, rows, columns):
        count = GridSum.layout(n_f)[4]
        return [
            pltpu.VMEM((n_f, rows, columns), BF),
            pltpu.VMEM((count, rows // 2, columns), BF),
            pltpu.SemaphoreType.DMA((2, count + GridEnd.count(n_f))),
        ]

    def slot(self, kind, i, j):
        base = self.bases[kind]
        return base + [(j - 1) * self.net.tall + i, (i - 1) * self.net.wide + j, i - 1, j - 1][kind]

    def rank(self, i, j):
        net = self.net
        return ((net.a + i) % net.tall) * net.wide + (net.b + j) % net.wide

    def owner(self, at):
        return self.rank(at // self.net.wide, at % self.net.wide)

    def copy(self, kind, i, j):
        half = kind % 2
        along = kind in (0, 3)
        slot = self.slot(kind, i, j)
        at = i * self.net.wide + j
        return put(
            self.stage.at[at, pl.ds(half * self.half, self.half)],
            self.came.at[slot],
            self.sems.at[0, slot],
            self.sems.at[1, slot],
            fsdp=self.rank(0, j) if along else self.rank(i, 0),
        )

    def first(self, at):
        i, j = at // self.net.wide, at % self.net.wide

        @pl.when(j > 0)
        def _():
            self.copy(0, i, j).start()

        @pl.when(i > 0)
        def _():
            self.copy(1, i, j).start()

    def gather(self, half, at, slots, write):
        @pl.loop(0, self.half // self.rows)
        def _(step):
            span = aligned(half * self.half + step * self.rows, self.rows, 16)
            value = self.stage[at, span, :].astype(F32)
            for slot in slots:
                value = value + self.came[slot, aligned(step * self.rows, self.rows, 16), :].astype(F32)
            write(span, value)

    def wait(self, *copies):
        for kind, i, j in copies:
            self.copy(kind, i, j).wait_recv()
        return [self.slot(*copy) for copy in copies]

    def second(self):
        def keep(at):
            def write(span, value):
                self.stage[at, span, :] = value.astype(BF)

            return write

        for i in self.cols:
            at = i * self.net.wide
            self.gather(0, at, self.wait(*[(0, i, j) for j in self.along]), keep(at))
            self.copy(2, i, 0).start()
        for j in self.along:
            self.gather(1, j, self.wait(*[(1, i, j) for i in self.cols]), keep(j))
            self.copy(3, 0, j).start()

    def sum_first(self):
        def keep(at):
            def write(span, value):
                self.stage[at, span, :] = value.astype(BF)

            return write

        for i in range(self.net.tall):
            at = i * self.net.wide
            self.gather(0, at, self.wait(*[(0, i, j) for j in self.along]), keep(at))
        for j in range(self.net.wide):
            self.gather(1, j, self.wait(*[(1, i, j) for i in self.cols]), keep(j))

    def hand_on(self, out):
        net = self.net
        shards = [(0, 0), (0, 1), *[(i * net.wide, 0) for i in self.cols], *[(j, 1) for j in self.along]]
        return [
            pltpu.make_async_copy(
                self.stage.at[at, pl.ds(half * self.half, self.half)], out.at[k], self.sems.at[0, self.bases[4] + k]
            )
            for k, (at, half) in enumerate(shards)
        ]

    def last(self, out):
        def write(span, value):
            out[span, :] = value

        self.gather(
            0, 0, self.wait(*[(0, 0, j) for j in self.along], *[(2, i, 0) for i in self.cols]), write
        )
        self.gather(
            1, 0, self.wait(*[(1, i, 0) for i in self.cols], *[(3, 0, j) for j in self.along]), write
        )

    def finish_first(self):
        for i in range(self.net.tall):
            for j in range(self.net.wide):
                if j:
                    self.copy(0, i, j).wait_send()
                if i:
                    self.copy(1, i, j).wait_send()

    def finish(self):
        self.finish_first()
        for i in self.cols:
            self.copy(2, i, 0).wait_send()
        for j in self.along:
            self.copy(3, 0, j).wait_send()


class GridEnd:
    def __init__(self, net, sums, came, sems):
        self.net, self.sums, self.came, self.sems = net, sums, came, sems

    @staticmethod
    def count(n_f):
        tall = 2 if n_f % 2 == 0 else 1
        return tall + n_f // tall

    @staticmethod
    def scratch(n_f, rows, columns):
        count = GridEnd.count(n_f)
        return [
            pltpu.VMEM((count, rows // 2, columns), BF),
            pltpu.VMEM((count - 2, rows // 2, columns), BF),
            pltpu.SemaphoreType.DMA((2, count - 2)),
        ]

    def copies(self):
        net = self.net
        f = [((net.a + i) % net.tall) * net.wide + net.b for i in range(1, net.tall)]
        f += [net.a * net.wide + (net.b + j) % net.wide for j in range(1, net.wide)]
        return [
            put(self.sums.at[2 + k], self.came.at[k], self.sems.at[0, k], self.sems.at[1, k], fsdp=to)
            for k, to in enumerate(f)
        ]

    def start(self):
        for copy in self.copies():
            copy.start()

    def last(self, out):
        for copy in self.copies():
            copy.wait()
        half = self.sums.shape[1]
        rows = next(r for r in (176, 128, 96, 64, 32, 16) if half % r == 0)
        down = range(self.net.tall - 1)
        along = range(self.net.tall - 1, self.net.tall + self.net.wide - 2)
        for at, slots in enumerate((down, along)):

            @pl.loop(0, half // rows)
            def _(step):
                span = aligned(step * rows, rows, 16)
                value = self.sums[at, span, :].astype(F32)
                for slot in slots:
                    value = value + self.came[slot, span, :].astype(F32)
                out[aligned(at * half + step * rows, rows, 16), :] = value


class PacketSum:
    def __init__(self, net, out, seq_in, total, fsdp_in, sems):
        self.net, self.out, self.seq_in, self.total, self.fsdp_in, self.sems = net, out, seq_in, total, fsdp_in, sems

    @staticmethod
    def scratch(n_f, n_s):
        return [
            pltpu.VMEM((n_s, n_f, SMALL, 128), F32),
            pltpu.VMEM((n_s, n_f, SMALL, 128), F32),
            pltpu.VMEM((n_f, SMALL, 128), F32),
            pltpu.VMEM((n_f, SMALL, 128), F32),
            pltpu.SemaphoreType.DMA((2 * (n_f + n_s),)),
        ]

    def one(self, k):
        to = (self.net.s + k) % self.net.n_s
        return put(self.out.at[to], self.seq_in.at[k], self.sems.at[2 * k], self.sems.at[2 * k + 1], seq=to)

    def two(self, k):
        to = (self.net.f + k) % self.net.n_f
        at = 2 * (self.net.n_s + k)
        return put(self.total.at[to], self.fsdp_in.at[k], self.sems.at[at], self.sems.at[at + 1], fsdp=to)

    def run(self, terms, result, width):
        net = self.net
        per = 128 // width
        for tile in range(net.n_f * net.n_s // per):
            value = terms[:, tile * 128 : (tile + 1) * 128]
            for j in range(per):
                f, s = divmod(tile * per + j, net.n_s)
                self.out[s, f] = pltpu.roll(value, 128 - j * width, axis=1) if j else value
        for k in range(1, net.n_s):
            self.one(k).start()
        total = self.out[net.s]
        for k in range(1, net.n_s):
            self.one(k).wait()
            total = total + self.seq_in[k]
        self.total[...] = total
        for k in range(1, net.n_f):
            self.two(k).start()
        total = self.total[net.f]
        for k in range(1, net.n_f):
            self.two(k).wait()
            total = total + self.fsdp_in[k]
        result[...] = total


def norm_backward(rows, source, grad, gain, terms, at, write):
    terms[at : at + 2, :] = jnp.zeros((2, terms.shape[1]), F32)

    @pl.loop(0, rows // 32)
    def _(i):
        span = aligned(i * 32, 32)
        scaled, inverse = normalize(source[span, :].astype(F32))
        value = grad[span, :]
        upstream = value * gain
        inner = jnp.mean(upstream, -1, keepdims=True)
        cross = jnp.mean(upstream * scaled, -1, keepdims=True)
        terms[at : at + 1, :] = terms[at : at + 1, :] + jnp.sum(value * scaled, 0, keepdims=True)
        terms[at + 1 : at + 2, :] = terms[at + 1 : at + 2, :] + jnp.sum(value, 0, keepdims=True)
        write(i, span, inverse * (upstream - inner - scaled * cross))


def layer_kernel(
    tok,
    packet,
    wq_own,
    wo_own,
    wg_own,
    wu_own,
    wd_own,
    gout_own,
    cosine,
    sine,
    q_o,
    k_o,
    kt_o,
    v_o,
    att_o,
    lse_o,
    n1_o,
    gains_o,
    wq_o,
    wo_o,
    dm_o,
    dmid_o,
    top_o,
    terms_o,
    gate_o,
    up_o,
    down_o,
    rows,
    gout,
    wq,
    wo,
    wg,
    wu,
    wd,
    q,
    k,
    kt,
    v,
    vt,
    ot,
    att,
    hidden,
    dgate,
    dup,
    mid,
    low,
    packets,
    tiles,
    total,
    *rest,
):
    net = Net()
    chunk, width = tok.shape
    length = chunk * net.n_s
    depth = wq_own.shape[1]
    columns = wq_own.shape[2]
    heads = columns // HEAD
    pair = 2 * chunk
    buffers, rest = rest[:4], rest[4:]
    folds = []
    for _ in range(3):
        folds.append(Fold(net, tiles, total, *buffers, *rest[:4]))
        rest = rest[4:]
    att_fold, normed_fold, top_fold = folds
    line_sems = [rest[at : at + 3] for at in (0, 3, 6, 9)]
    rest = rest[12:]
    spread_sems, rest = rest[:5], rest[5:]
    gate_sum, up_sum, down_sum = [GridSum(net, *rest[at : at + 3]) for at in (0, 3, 6)]
    sums = (down_sum, gate_sum, up_sum)
    pk_sems, copy_sems, n1_sems = rest[9:]
    copies = Copies(copy_sems)
    n1 = att_fold.mate_out

    net.barrier()

    def wq_part(f, half):
        if half is None:
            return wq.at[:, aligned(f * depth, depth), :]
        return wq.at[:, aligned(f * depth + half * (depth // 2), depth // 2), :]

    spread_q = Spread(net, wq_own, wq_part, spread_sems[0])
    spread_o, spread_g, cast_u, cast_d = [
        kind(net, own, columns_of(full, depth), sems)
        for kind, own, full, sems in zip(
            (Spread, Spread, Cast, Cast), (wo_own, wg_own, wu_own, wd_own), (wo, wg, wu, wd), spread_sems[1:]
        )
    ]
    pk = Packets(net, packet, packets, pk_sems)
    line = Line(net, tok, rows_of(rows, chunk), *line_sems[0])
    gout_line = Line(net, gout_own, rows_of(gout, chunk), *line_sems[1])
    n2_line = Line(net, low, rows_of(rows, chunk), *line_sems[2])
    dm_line = Line(net, low, rows_of(dm_o, chunk), *line_sems[3])

    def pairs(which, hop):
        net.sides(hop, lambda other, side: which.pair(other))

    def blocks(hop, act):
        def once(other, side):
            @pl.when((hop > 0) | (side == 0))
            def _():
                act(other, side)

        net.sides(hop, once)

    pk.start()
    line.start()
    spread_q.start()
    pk.middle()
    pk.finish()
    pk.unpack(gains_o, width // (net.n_f * net.n_s))

    def project_block(other, side):
        span = aligned(other * pair, pair)
        gain, shift = gains_o[0:1, :], gains_o[1:2, :]

        for part in range(2):

            @pl.loop(0, chunk // 32)
            def _(i):
                at = aligned((2 * other + part) * chunk + i * 32, 32)
                scaled, _ = normalize(rows[at, :].astype(F32))
                n1[part, aligned(i * 32, 32), :] = (scaled * gain + shift).astype(BF)

        keeps = [
            pltpu.make_async_copy(
                n1.at[part], n1_o.at[aligned((2 * other + part) * chunk, chunk)], n1_sems.at[part]
            )
            for part in range(2)
        ]
        for copy in keeps:
            copy.start()
        left = n1[0:2].reshape(pair, width)
        cols = aligned(net.s * columns, columns)
        tables = cosine[span, :], sine[span, :]
        for kind in range(3):
            value = dot(left, wq[kind]) + gains_o[4 + kind : 5 + kind, cols]
            if kind == 0:
                q[span, :] = rotary(value, *tables).astype(BF)
            elif kind == 1:
                value = rotary(value, *tables)
                k[span, :] = value.astype(BF)
                kt[...] = value.T.astype(BF)
            else:
                v[...] = value.astype(BF)
                vt[:, span] = value.T.astype(BF)
        for copy in (
            pltpu.make_async_copy(kt, kt_o.at[:, span], n1_sems.at[2]),
            pltpu.make_async_copy(v, v_o.at[span], n1_sems.at[3]),
        ):
            copy.start()
            keeps.append(copy)
        for copy in keeps:
            copy.wait()

    line.here()
    for hop in range(1, net.n_l - 1):
        line.step(hop)
        if hop == 1:
            spread_q.relay()
        pairs(line, hop)
    spread_o.start()
    spread_q.finish()
    spread_g.start()
    pl.loop(0, net.n_l - 1)(lambda hop: blocks(hop, project_block))
    spread_o.relay()
    line.step(net.n_l - 1)
    gout_line.start()
    pairs(line, net.n_l - 1)
    blocks(net.n_l - 1, project_block)
    spread_g.relay()
    cast_u.start()
    cast_d.start()
    for pair_of in ((wq, wq_o), (q, q_o), (k, k_o)):
        copies.start(*pair_of)
    spread_o.finish()
    line.finish()

    def attend(i):
        lo, hi = i * pair, (i + 1) * pair

        @pl.loop(0, heads)
        def _(head):
            lane = lax.broadcasted_iota(jnp.int32, (1, columns), 1)
            here = jnp.where(lane // HEAD == head, HEAD**-0.5, 0.0).astype(BF)
            visible = lax.broadcasted_iota(jnp.int32, (pair, pair), 0) <= lax.broadcasted_iota(
                jnp.int32, (pair, pair), 1
            )
            head_rows = aligned(head * HEAD, HEAD)
            query = q[lo:hi, :] * here
            near = jnp.where(visible, dot_nt(k[lo:hi, :], query), NEG_LARGE)
            highest = jnp.max(near, 0, keepdims=True)
            if i:
                far = dot_nt(k[0:lo, :], query)
                highest = jnp.maximum(highest, jnp.max(far, 0, keepdims=True))
            near = jnp.exp(near - highest)
            sum_of = jnp.sum(near, 0, keepdims=True)
            out = dot(vt[head_rows, lo:hi], near.astype(BF))
            if i:
                far = jnp.exp(far - highest)
                sum_of = sum_of + jnp.sum(far, 0, keepdims=True)
                out = out + dot(vt[head_rows, 0:lo], far.astype(BF))
            ot[head_rows, :] = out / sum_of
            lse_o[pl.ds(head, 1), lo:hi] = highest + jnp.log(sum_of)

        att[lo:hi, :] = ot[...].T.astype(BF)

    def produce_attended(place, write):
        for i in range(net.n_l):
            pl.when(place == i)(functools.partial(attend, i))
        left = att[aligned(place * pair, pair), :]

        @pl.loop(0, width // TILE)
        def _(j):
            cols = aligned(j * TILE, TILE)
            write(cols, dot(left, wo[:, cols]))

    def begun(wave):
        pl.when(wave < net.n_l - 1)(lambda: gout_line.step(wave))

    att_fold.far(produce_attended, begun)
    gout_line.step(net.n_l - 1)
    copies.start(att, att_o)
    copies.start(wo, wo_o)
    att_fold.finals()
    gain_two, shift_two = gains_o[2:3, :], gains_o[3:4, :]

    @pl.loop(0, chunk // 32)
    def _(i):
        span = aligned(i * 32, 32)
        value = rows[aligned(net.s * chunk + i * 32, 32), :].astype(F32) + total[span, :]
        mid[span, :] = value
        scaled, _ = normalize(value)
        low[span, :] = (scaled * gain_two + shift_two).astype(BF)

    n2_line.start()
    att_fold.finish()
    gout_line.here()
    pl.loop(1, net.n_l)(lambda hop: pairs(gout_line, hop))

    def forward_block(other):
        span = aligned(other * pair, pair)
        right = rows[span, :]
        half = hidden.shape[0] // 2

        @pl.loop(0, 2)
        def _(part):
            units = aligned(part * half, half, 16)
            gate = dot_nt(wg[units, :], right)
            up = dot_nt(wu[units, :], right)
            back = dot_nt(wd[units, :], gout[span, :])
            sigma = jax.nn.sigmoid(gate)
            active = gate * sigma
            hidden[units, span] = (active * up).astype(BF)
            dgate[units, span] = (back * up * (sigma * (1.0 + gate * (1.0 - sigma)))).astype(BF)
            dup[units, span] = (back * active).astype(BF)

    def produce_normed(place, write):
        span = aligned(place * pair, pair)
        left, right = dgate[:, span].T, dup[:, span].T

        @pl.loop(0, width // TILE)
        def _(j):
            cols = aligned(j * TILE, TILE)
            write(cols, dot(left, wg[:, cols]) + dot(right, wu[:, cols]))

    def settle(hop):
        def act(other, side):
            begins = (hop == 0) | normed_fold.fed(side)

            @pl.when(begins)
            def _():
                pl.when(hop > 1)(lambda: normed_fold.mate_sent(side))
                normed_fold.begin_one(other, side + (2 - side) * (1 // (hop + 1)), produce_normed)

            @pl.when(jnp.logical_not(begins))
            def _():
                normed_fold.each_piece(lambda piece: normed_fold.pass_piece(other, side, hop, piece, False))

        blocks(hop, act)

    def forward_blocks(hop):
        def act(other, side):
            forward_block(other)

            @pl.when(jnp.logical_not(normed_fold.fed(side)))
            def _():
                pl.when(hop > 1)(lambda: normed_fold.mate_sent(side))
                normed_fold.begin_one(other, side, produce_normed)

        net.sides(hop, act)

    n2_line.here()
    spread_g.finish()
    cast_u.finish()
    cast_d.finish()
    forward_block(net.z)

    @pl.loop(1, net.n_l)
    def _(hop):
        n2_line.step(hop)
        settle(hop - 1)
        pairs(n2_line, hop)
        forward_blocks(hop)

    settle(net.n_l - 1)

    def weight_terms(task):
        at, kind = net.n_f - 1 - task // 3, task % 3
        cols = aligned(gate_sum.owner(at) * depth, depth)
        for way, (grid_sum, left, right) in enumerate(
            ((down_sum, hidden, gout), (gate_sum, dgate, rows), (up_sum, dup, rows))
        ):

            @pl.when(kind == way)
            def _():
                half = left.shape[0] // 2

                @pl.loop(0, 2)
                def _(part):
                    units = aligned(part * half, half, 16)
                    grid_sum.stage[at, units, :] = dot(left[units, :], right[:, cols]).astype(BF)

                grid_sum.first(at)

    tasks = 3 * net.n_f
    waves = max(net.n_l - 2, 1)
    each = -(-tasks // (2 * normed_fold.pieces * waves))
    for wave in range(net.n_l - waves, net.n_l):

        def between(turn, piece):
            slot = ((wave - net.n_l + waves) * 2 + turn) * normed_fold.pieces + piece

            @pl.loop(0, each)
            def _(i):
                pl.when(slot * each + i < tasks)(lambda: weight_terms(slot * each + i))

        normed_fold.passes_between(wave, True, between)
    normed_fold.finals()
    n2_line.finish()

    def write_middle(i, span, value):
        value = value + gout[aligned(net.s * chunk + i * 32, 32), :].astype(F32)
        dmid_o[span, :] = value
        low[span, :] = value.astype(BF)

    terms_o[...] = jnp.zeros(terms_o.shape, F32)
    norm_backward(chunk, mid, total, gain_two, terms_o, 2, write_middle)
    dm_line.start()
    normed_fold.finish()

    def produce_top(place, write):
        left = hidden[:, aligned(place * pair, pair)].T

        @pl.loop(0, width // TILE)
        def _(j):
            cols = aligned(j * TILE, TILE)
            write(cols, dot(left, wd[:, cols]))

    dm_line.here()
    dm_line.step(1)
    top_fold.far(produce_top, passing=False)
    pl.loop(2, net.n_l)(dm_line.step)
    for wave in range(1, net.n_l - 1):
        top_fold.passes(wave)
    top_fold.finals()

    @pl.loop(0, chunk // 32)
    def _(i):
        span = aligned(i * 32, 32)
        top_fold.out[net.z, span, :] = (mid[span, :] + total[span, :]).astype(BF)

    copies.start(top_fold.out.at[net.z], top_o)
    top_fold.finish()
    pl.loop(1, net.n_l)(lambda hop: pairs(dm_line, hop))
    gout_line.finish()
    dm_line.finish()
    hands = []
    for grid_sum, out in zip(sums, (down_o, gate_o, up_o)):
        grid_sum.sum_first()
        hands.extend(grid_sum.hand_on(out))
        for copy in grid_sum.hand_on(out):
            copy.start()
    for grid_sum in sums:
        grid_sum.finish_first()
    for copy in hands:
        copy.wait()
    copies.wait()


def layer_part(tokens, packet, wq, wo, wg, wu, wd, gout, tables):
    chunk, width = tokens.shape
    n_f, n_s = lax.axis_size("fsdp"), lax.axis_size("seq")
    length = chunk * n_s
    depth, columns = wq.shape[1:]
    units = wg.shape[0]
    shape = jax.ShapeDtypeStruct
    wide, head, turned, weight = (length, width), (length, columns), (units, length), (units, width)
    return pl.pallas_call(
        layer_kernel,
        name="layer",
        out_shape=[
            shape(head, BF),
            shape(head, BF),
            shape((columns, length), BF),
            shape(head, BF),
            shape(head, BF),
            shape((8, length), F32),
            shape(wide, BF),
            shape((SMALL, width), F32),
            shape((3, width, columns), BF),
            shape((columns, width), BF),
            shape(wide, BF),
            shape((chunk, width), F32),
            shape((chunk, width), BF),
            shape((SMALL, width), F32),
            *[shape((GridEnd.count(n_f), units // 2, depth), BF)] * 3,
        ],
        in_specs=[ANY, VMEM, *[ANY] * 6, VMEM, VMEM],
        out_specs=[*[ANY] * 5, VMEM, ANY, VMEM, *[ANY] * 3, VMEM, ANY, VMEM, *[ANY] * 3],
        scratch_shapes=[
            pltpu.VMEM(wide, BF),
            pltpu.VMEM(wide, BF),
            pltpu.VMEM((3, width, columns), BF),
            pltpu.VMEM((columns, width), BF),
            *[pltpu.VMEM(weight, BF)] * 3,
            pltpu.VMEM(head, BF),
            pltpu.VMEM(head, BF),
            pltpu.VMEM((columns, 2 * chunk), BF),
            pltpu.VMEM((2 * chunk, columns), BF),
            pltpu.VMEM((columns, length), BF),
            pltpu.VMEM((columns, 2 * chunk), F32),
            pltpu.VMEM(head, BF),
            *[pltpu.VMEM(turned, BF)] * 3,
            pltpu.VMEM((chunk, width), F32),
            pltpu.VMEM((chunk, width), BF),
            pltpu.VMEM((n_s, n_f, SMALL, 128), F32),
            *Fold.shared(chunk, width),
            *Fold.buffers(n_s, chunk, width),
            *Fold.sems(n_s) * 3,
            *Line.sems(n_s) * 4,
            *[pltpu.SemaphoreType.DMA((Spread.count(n_f),))] * 5,
            *GridSum.scratch(n_f, units, depth) * 3,
            pltpu.SemaphoreType.DMA((Packets.count(n_f, n_s),)),
            pltpu.SemaphoreType.DMA((8,)),
            pltpu.SemaphoreType.DMA((4,)),
        ],
        compiler_params=pltpu.CompilerParams(
            collective_id=1, has_side_effects=True, vmem_limit_bytes=VMEM_BYTES
        ),
        cost_estimate=pl.CostEstimate(
            flops=2 * length * width * (4 * columns + 9 * units),
            bytes_accessed=8 * length * width,
            transcendentals=length * (length * columns // HEAD + units),
        ),
    )(tokens, packet, wq, wo, wg, wu, wd, gout, *tables)


def back_kernel(
    dm_in,
    wo_in,
    att_in,
    q_in,
    k_in,
    kt_in,
    v_in,
    n1_in,
    wq_in,
    down_in,
    gate_in,
    up_in,
    lse,
    tok,
    dmid,
    gains,
    terms_in,
    cosine,
    sine,
    gin_o,
    small_o,
    out_o,
    qkv_o,
    down_o,
    gate_o,
    up_o,
    dm,
    wo,
    att,
    q,
    k,
    kt,
    v,
    n1,
    wq,
    datt,
    dk,
    dv,
    dqt,
    dproj,
    terms,
    tiles,
    total,
    *rest,
):
    net = Net()
    chunk, width = tok.shape
    length, columns = q_in.shape
    heads = columns // HEAD
    pair = 2 * chunk
    depth = width // net.n_f
    block = 256
    buffers, rest = rest[:4], rest[4:]
    fold_sems, rest = rest[:4], rest[4:]
    packet_scratch, rest = rest[:5], rest[5:]
    out_sum, qkv_sum = GridSum(net, *rest[:3]), GridSum(net, *rest[3:6])
    ends = [GridEnd(net, *rest[at : at + 3]) for at in (6, 9, 12)]
    copy_sems = rest[15]

    copies = Copies(copy_sems)
    loads = [
        copies.start(src, dst)
        for src, dst in (
            (dm_in, dm),
            (wo_in, wo),
            (att_in, att),
            (q_in, q),
            (k_in, k),
            (kt_in, kt),
            (v_in, v),
            (n1_in, n1),
            (wq_in, wq),
            (down_in, ends[0].sums),
            (gate_in, ends[1].sums),
            (up_in, ends[2].sums),
        )
    ]
    net.barrier()
    copies.wait(*loads[:2])

    @pl.loop(0, length // block)
    def _(i):
        span = aligned(i * block, block)
        datt[span, :] = dot_nt(dm[span, :], wo[...]).astype(BF)
        dk[span, :] = jnp.zeros((block, columns), F32)
        dv[span, :] = jnp.zeros((block, columns), F32)

    copies.wait()
    for end in ends:
        end.start()

    @pl.loop(0, heads)
    def _(head):
        lane = lax.broadcasted_iota(jnp.int32, (1, columns), 1)
        here = jnp.where(lane // HEAD == head, 1.0, 0.0).astype(BF)
        scale = HEAD**-0.5
        visible = lax.broadcasted_iota(jnp.int32, (block, block), 0) <= lax.broadcasted_iota(
            jnp.int32, (block, block), 1
        )
        head_rows = aligned(head * HEAD, HEAD)
        for i in range(length // block):
            lo, hi = i * block, (i + 1) * block
            query = q[lo:hi, :] * (here * scale)
            upstream = datt[lo:hi, :] * here
            logsum = lse[pl.ds(head, 1), lo:hi]

            def part(at, end, mask):
                probs = jnp.exp(dot_nt(k[at:end, :], query) - logsum)
                if mask:
                    probs = jnp.where(visible, probs, 0.0)
                grads = dot_nt(v[at:end, :], upstream)
                dv[at:end, :] = dv[at:end, :] + dot(probs.astype(BF), upstream)
                return probs, grads, jnp.sum(probs * grads, 0, keepdims=True)

            def scored(at, end, probs, grads, inner):
                scores = (probs * (grads - inner)).astype(BF)
                dk[at:end, :] = dk[at:end, :] + dot(scores, query)
                return dot(kt[head_rows, at:end], scores)

            near, near_grads, inner = part(lo, hi, True)
            if i:
                far, far_grads, more = part(0, lo, False)
                inner = inner + more
            out = scored(lo, hi, near, near_grads, inner)
            if i:
                out = out + scored(0, lo, far, far_grads, inner)
            dqt[head_rows, lo:hi] = out * scale

    terms[...] = terms_in[...]
    bias_cols = aligned(net.s * columns, columns)

    @pl.loop(0, length // block)
    def _(i):
        span = aligned(i * block, block)
        tables = cosine[span, :], -sine[span, :]
        parts = [
            rotary(dqt[:, span].T.astype(BF).astype(F32), *tables).astype(BF),
            rotary(dk[span, :].astype(BF).astype(F32), *tables).astype(BF),
            dv[span, :].astype(BF),
        ]
        for kind in range(3):
            dproj[kind, span, :] = parts[kind]
            row = slice(4 + kind, 5 + kind)
            terms[row, bias_cols] = terms[row, bias_cols] + jnp.sum(parts[kind].astype(F32), 0, keepdims=True)

    def weight_terms(task):
        at = net.n_f - 1 - task // 2
        cols = aligned(qkv_sum.owner(at) * depth, depth)

        @pl.when(task % 2 == 0)
        def _():
            left = n1[:, cols].T
            for kind in range(3):
                qkv_sum.stage[at, kind * depth : (kind + 1) * depth, :] = dot(left, dproj[kind]).astype(BF)
            qkv_sum.first(at)

        @pl.when(task % 2 == 1)
        def _():
            out_sum.stage[at] = dot_tn(att[...], dm[:, cols]).astype(BF)
            out_sum.first(at)

    def produce(place, write):
        span = aligned(place * pair, pair)

        @pl.loop(0, width // TILE)
        def _(j):
            cols = aligned(j * TILE, TILE)
            value = dot_nt(dproj[0, span, :], wq[0, cols, :])
            for kind in range(1, 3):
                value = value + dot_nt(dproj[kind, span, :], wq[kind, cols, :])
            write(cols, value)

    fold = Fold(net, tiles, total, *buffers, *fold_sems)
    fold.far(produce, passing=False)
    tasks = 2 * net.n_f
    waves = max(net.n_l - 2, 1)
    each = -(-tasks // (2 * fold.pieces * waves))
    for wave in range(1, waves + 1):

        def between(turn, piece):
            slot = ((wave - 1) * 2 + turn) * fold.pieces + piece

            @pl.loop(0, each)
            def _(i):
                pl.when(slot * each + i < tasks)(lambda: weight_terms(slot * each + i))

        fold.passes_between(wave, False, between)
    for grid_sum in (qkv_sum, out_sum):
        grid_sum.second()
    fold.finals()

    def write_input(i, span, value):
        gin_o[span, :] = value + dmid[span, :]

    norm_backward(chunk, tok, total, gains[0:1, :], terms, 0, write_input)
    for end, out in zip(ends, (down_o, gate_o, up_o)):
        end.last(out)
    PacketSum(net, *packet_scratch).run(terms, small_o, width // (net.n_f * net.n_s))
    fold.finish()
    for grid_sum, out in ((qkv_sum, qkv_o), (out_sum, out_o)):
        grid_sum.last(out)
        grid_sum.finish()


def back_part(dm, wo, att, q, k, kt, v, n1, wq, down, gate, up, lse, tokens, dmid, gains, terms, tables):
    chunk, width = tokens.shape
    n_f, n_s = lax.axis_size("fsdp"), lax.axis_size("seq")
    length, columns = q.shape
    depth = width // n_f
    units = 2 * gate.shape[1]
    shape = jax.ShapeDtypeStruct
    return pl.pallas_call(
        back_kernel,
        name="back",
        out_shape=[
            shape((chunk, width), F32),
            shape((SMALL, 128), F32),
            shape((columns, depth), F32),
            shape((3 * depth, columns), F32),
            *[shape((units, depth), F32)] * 3,
        ],
        in_specs=[ANY] * 12 + [VMEM] * 7,
        out_specs=[VMEM] * 7,
        scratch_shapes=[
            pltpu.VMEM((length, width), BF),
            pltpu.VMEM((columns, width), BF),
            pltpu.VMEM((length, columns), BF),
            pltpu.VMEM((length, columns), BF),
            pltpu.VMEM((length, columns), BF),
            pltpu.VMEM((columns, length), BF),
            pltpu.VMEM((length, columns), BF),
            pltpu.VMEM((length, width), BF),
            pltpu.VMEM((3, width, columns), BF),
            pltpu.VMEM((length, columns), BF),
            pltpu.VMEM((length, columns), F32),
            pltpu.VMEM((length, columns), F32),
            pltpu.VMEM((columns, length), F32),
            pltpu.VMEM((3, length, columns), BF),
            pltpu.VMEM((SMALL, width), F32),
            *Fold.shared(chunk, width),
            *Fold.buffers(n_s, chunk, width),
            *Fold.sems(n_s),
            *PacketSum.scratch(n_f, n_s),
            *GridSum.scratch(n_f, columns, depth),
            *GridSum.scratch(n_f, 3 * depth, columns),
            *GridEnd.scratch(n_f, units, depth) * 3,
            pltpu.SemaphoreType.DMA((12,)),
        ],
        compiler_params=pltpu.CompilerParams(
            collective_id=3, has_side_effects=True, vmem_limit_bytes=VMEM_BYTES
        ),
        cost_estimate=pl.CostEstimate(
            flops=2 * length * columns * (8 * width + 5 * length),
            bytes_accessed=4 * length * width,
            transcendentals=length * length * columns // HEAD,
        ),
    )(dm, wo, att, q, k, kt, v, n1, wq, down, gate, up, lse, tokens, dmid, gains, terms, *tables)


def per_device(
    tokens,
    gain_one,
    shift_one,
    w_qkv,
    b_qkv,
    w_out,
    gain_two,
    shift_two,
    w_gate,
    w_up,
    w_down,
    grad_output,
):
    length = tokens.shape[1] * lax.axis_size("seq")
    width = gain_one.shape[0]
    packet = jnp.concatenate(
        [jnp.stack([gain_one, shift_one, gain_two, shift_two]), b_qkv, jnp.zeros((1, width), BF)]
    )
    packet = jnp.pad(packet.astype(F32), ((0, 0), (0, 128 - width)))
    tables = rotary_tables(length)
    q, k, kt, v, att, lse, n1, gains, wq, wo, dm, dmid, top, terms, gate, up, down = layer_part(
        tokens[0], packet, w_qkv.transpose(1, 0, 2), w_out, w_gate.T, w_up.T, w_down, grad_output[0], tables
    )
    grad_input, small, out, qkv, down, gate, up = back_part(
        dm, wo, att, q, k, kt, v, n1, wq, down, gate, up, lse, tokens[0], dmid, gains, terms, tables
    )

    return (
        top[None],
        grad_input[None],
        small[0, :width],
        small[1, :width],
        qkv.reshape(3, -1, qkv.shape[1]).transpose(1, 0, 2),
        small[4:7, :width],
        out,
        small[2, :width],
        small[3, :width],
        gate.T,
        up.T,
        down,
    )


def solution(mesh):
    whole = P(("fsdp", "seq"))
    rows = P("fsdp", "seq", None)
    inner = P("seq", "fsdp")
    outer = P("fsdp", "seq")
    heads = P("fsdp", None, "seq")
    bias = P(None, ("fsdp", "seq"))
    return jax.shard_map(
        per_device,
        mesh=mesh,
        in_specs=(rows, whole, whole, heads, bias, inner, whole, whole, outer, outer, inner, rows),
        out_specs=(rows, rows, whole, whole, heads, bias, inner, whole, whole, outer, outer, inner),
        check_vma=False,
    )
```

```python
import functools

import jax
import jax.numpy as jnp
import numpy as np
from jax import lax
from jax.experimental import pallas as pl
from jax.experimental.pallas import tpu as pltpu
from jax.sharding import PartitionSpec as P

HEAD = 64
ROT = 16
EPSILON = 1e-05
NEG_LARGE = -1e30
MESH = pl.DeviceIdType.MESH
ANY = pl.BlockSpec(memory_space=pl.ANY)
VMEM = pl.BlockSpec(memory_space=pltpu.VMEM)
BF = jnp.bfloat16
F32 = jnp.float32
VMEM_BYTES = 60 * 2**20
TILE = 512
SMALL = 8


def put(src, dst, send, recv, **device):
    return pltpu.make_async_remote_copy(
        src_ref=src, dst_ref=dst, send_sem=send, recv_sem=recv, device_id=device, device_id_type=MESH
    )


def dot(left, right):
    return jnp.dot(left, right, preferred_element_type=F32)


def dot_nt(left, right):
    return lax.dot_general(left, right, (((1,), (1,)), ((), ())), preferred_element_type=F32)


def dot_tn(left, right):
    return lax.dot_general(left, right, (((0,), (0,)), ((), ())), preferred_element_type=F32)


def aligned(start, size, unit=None):
    return pl.ds(pl.multiple_of(start, unit or size), size)


class Net:
    def __init__(self):
        self.n_f, self.n_s = lax.axis_size("fsdp"), lax.axis_size("seq")
        self.tall = 2 if self.n_f % 2 == 0 else 1
        self.wide = self.n_f // self.tall
        self.n_l = self.n_s // 2
        self.f, self.s = lax.axis_index("fsdp"), lax.axis_index("seq")
        self.a, self.b = self.f // self.wide, self.f % self.wide
        self.z, self.c = self.s // 2, self.s % 2
        self.mate = self.s + 1 - 2 * self.c

    def barrier(self):
        sem = pltpu.get_barrier_semaphore()
        for k in range(1, self.n_f):
            pl.semaphore_signal(
                sem, inc=1, device_id={"fsdp": (self.f + k) % self.n_f}, device_id_type=MESH
            )
        for k in range(1, self.n_s):
            pl.semaphore_signal(
                sem, inc=1, device_id={"seq": (self.s + k) % self.n_s}, device_id_type=MESH
            )
        pl.semaphore_wait(sem, self.n_f + self.n_s - 2)

    def sides(self, hop, act):
        @pl.loop(0, 2)
        def _(side):
            other = self.z + (2 * side - 1) * hop

            @pl.when((other >= 0) & (other < self.n_l))
            def _():
                act(other, side)


class Spread:
    def __init__(self, net, src, part, sems):
        self.net, self.src, self.part, self.sems = net, src, part, sems
        self.rows = [j for j in range(1, net.wide)]
        self.cols = [i for i in range(1, net.tall)]

    @staticmethod
    def count(n_f):
        tall = 2 if n_f % 2 == 0 else 1
        wide = n_f // tall
        return 1 + 2 * (wide - 1) + 2 * (tall - 1) + 4 * (wide - 1) * (tall - 1)

    def at(self, kind, i, j):
        w, t = len(self.rows), len(self.cols)
        base = {
            "own": 0,
            "row": 1,
            "col": 1 + 2 * w,
            "half0": 1 + 2 * w + 2 * t,
            "half1": 1 + 2 * w + 2 * t + 2 * w * t,
        }[kind]
        if kind == "own":
            return self.sems.at[0]
        k = j - 1 if kind == "row" else i - 1 if kind == "col" else (i - 1) * w + j - 1
        return self.sems.at[base + 2 * k], self.sems.at[base + 2 * k + 1]

    def rank(self, i, j):
        net = self.net
        return ((net.a + i) % net.tall) * net.wide + (net.b + j) % net.wide

    def back(self, i, j):
        net = self.net
        return ((net.a - i + net.tall) % net.tall) * net.wide + (net.b - j + net.wide) % net.wide

    def own(self):
        return pltpu.make_async_copy(self.src, self.part(self.net.f, None), self.at("own", 0, 0))

    def first(self, i, j):
        send, recv = self.at("row" if i == 0 else "col", i, j)
        return put(self.src, self.part(self.net.f, None), send, recv, fsdp=self.rank(i, j))

    def came(self, i, j):
        send, recv = self.at("row" if i == 0 else "col", i, j)
        place = self.part(self.back(i, j), None)
        return put(place, place, send, recv, fsdp=self.rank(i, j))

    def second(self, half, i, j, came=False):
        send, recv = self.at("half0" if half == 0 else "half1", i, j)
        origin = self.back(i, j) if came else self.back(0, j) if half == 0 else self.back(i, 0)
        place = self.part(origin, half)
        return put(place, place, send, recv, fsdp=self.rank(i, 0) if half == 0 else self.rank(0, j))

    def start(self):
        self.own().start()
        for i in self.cols:
            self.first(i, 0).start()
        for j in self.rows:
            self.first(0, j).start()

    def relay(self):
        for j in self.rows:
            self.came(0, j).wait_recv()
            for i in self.cols:
                self.second(0, i, j).start()
        for i in self.cols:
            self.came(i, 0).wait_recv()
            for j in self.rows:
                self.second(1, i, j).start()

    def finish(self):
        self.own().wait()
        for j in self.rows:
            self.first(0, j).wait_send()
        for i in self.cols:
            self.first(i, 0).wait_send()
        for i in self.cols:
            for j in self.rows:
                for half in range(2):
                    self.second(half, i, j, came=True).wait_recv()
                    self.second(half, i, j).wait_send()


class Line:
    def __init__(self, net, src, part, recv, send, local):
        self.net, self.src, self.part, self.recv, self.send, self.local = net, src, part, recv, send, local
        self.pieces = recv.shape[1]
        self.rows = src.shape[0] // self.pieces

    @staticmethod
    def sems(n_s, pieces=2):
        return [
            pltpu.SemaphoreType.DMA((n_s, pieces)),
            pltpu.SemaphoreType.DMA((4, n_s // 2, pieces)),
            pltpu.SemaphoreType.DMA((1,)),
        ]

    def cut(self, ref, piece):
        return ref.at[aligned(piece * self.rows, self.rows)]

    def own(self):
        return pltpu.make_async_copy(self.src, self.part(self.net.s), self.local.at[0])

    def on_line(self, src, chunk, side, hop, piece):
        return put(
            self.cut(src, piece),
            self.cut(self.part(chunk), piece),
            self.send.at[side, hop, piece],
            self.recv.at[chunk, piece],
            seq=self.net.s + 2 - 4 * side,
        )

    def to_mate(self, src, chunk, side, hop, piece):
        return put(
            self.cut(src, piece),
            self.cut(self.part(chunk), piece),
            self.send.at[2 + side, hop, piece],
            self.recv.at[chunk, piece],
            seq=self.net.mate,
        )

    def goes_on(self, side):
        after = self.net.z + 1 - 2 * side
        return (after >= 0) & (after < self.net.n_l)

    def each_piece(self, act):
        pl.loop(0, self.pieces)(act)

    def start(self):
        net = self.net

        @self.each_piece
        def _(piece):
            for side in range(2):

                @pl.when(self.goes_on(side))
                def _():
                    self.on_line(self.src, net.s, side, 0, piece).start()

            self.to_mate(self.src, net.s, 0, 0, piece).start()

        self.own().start()

    def came(self, chunk, piece):
        place = self.cut(self.part(chunk), piece)
        put(place, place, self.send.at[0, 0, 0], self.recv.at[chunk, piece], seq=self.net.mate).wait_recv()

    def step(self, hop):
        net = self.net

        @self.each_piece
        def _(piece):
            def act(other, side):
                chunk = 2 * other + net.c
                self.came(chunk, piece)

                @pl.when(self.goes_on(side))
                def _():
                    self.on_line(self.part(chunk), chunk, side, hop, piece).start()

                self.to_mate(self.part(chunk), chunk, side, hop, piece).start()

            net.sides(hop, act)

    def pair(self, other):
        @self.each_piece
        def _(piece):
            self.came(2 * other + 1 - self.net.c, piece)

    def here(self):
        self.own().wait()
        self.pair(self.net.z)

    def finish(self):
        net = self.net

        @self.each_piece
        def _(piece):
            for side in range(2):

                @pl.when(self.goes_on(side))
                def _():
                    self.on_line(self.src, net.s, side, 0, piece).wait_send()

            self.to_mate(self.src, net.s, 0, 0, piece).wait_send()

            @pl.loop(1, net.n_l)
            def _(hop):
                def act(other, side):
                    chunk = 2 * other + net.c

                    @pl.when(self.goes_on(side))
                    def _():
                        self.on_line(self.part(chunk), chunk, side, hop, piece).wait_send()

                    self.to_mate(self.part(chunk), chunk, side, hop, piece).wait_send()

                net.sides(hop, act)


class Packets:
    def __init__(self, net, src, buf, sems):
        self.net, self.src, self.buf, self.sems = net, src, buf, sems

    @staticmethod
    def count(n_f, n_s):
        return 1 + 2 * (n_f - 1) + 2 * (n_s - 1)

    def own(self):
        net = self.net
        return pltpu.make_async_copy(self.src, self.buf.at[net.s, net.f], self.sems.at[0])

    def one(self, k, came=False):
        net = self.net
        f = (net.f - k + net.n_f) % net.n_f if came else net.f
        place = self.buf.at[net.s, f]
        return put(
            place if came else self.src,
            place,
            self.sems.at[2 * k - 1],
            self.sems.at[2 * k],
            fsdp=(net.f + k) % net.n_f,
        )

    def two(self, k, came=False):
        net = self.net
        place = self.buf.at[(net.s - k + net.n_s) % net.n_s if came else net.s]
        at = 2 * (net.n_f - 1) + 2 * k - 1
        return put(place, place, self.sems.at[at], self.sems.at[at + 1], seq=(net.s + k) % net.n_s)

    def start(self):
        self.own().start()
        for k in range(1, self.net.n_f):
            self.one(k).start()

    def middle(self):
        self.own().wait()
        for k in range(1, self.net.n_f):
            self.one(k, came=True).wait_recv()
            self.one(k).wait_send()
        for k in range(1, self.net.n_s):
            self.two(k).start()

    def finish(self):
        for k in range(1, self.net.n_s):
            self.two(k, came=True).wait_recv()
            self.two(k).wait_send()

    def unpack(self, out, width):
        net = self.net
        per = 128 // width
        for tile in range(net.n_f * net.n_s // per):
            total = None
            for j in range(per):
                f, s = divmod(tile * per + j, net.n_s)
                piece = self.buf[s, f]
                if j:
                    piece = pltpu.roll(piece, j * width, axis=1)
                total = piece if total is None else total + piece
            out[:, tile * 128 : (tile + 1) * 128] = total


def rotary(values, cosine, sine):
    columns = values.shape[1]
    half = ROT // 2
    times = columns // 128

    def wide(table):
        return table if times == 1 else jnp.concatenate([table] * times, axis=1)

    lane = lax.broadcasted_iota(jnp.int32, values.shape, 1)
    other = jnp.where(
        lane % HEAD < half, pltpu.roll(values, columns - half, axis=1), pltpu.roll(values, half, axis=1)
    )
    return values * wide(cosine) + other * wide(sine)


def rotary_tables(length):
    half = ROT // 2
    freqs = np.float32(10000.0) ** (-np.arange(half, dtype=np.float32) * np.float32(2.0 / ROT))
    angles = np.arange(length, dtype=np.float32)[:, None] * freqs[None, :].astype(np.float32)
    cosine, sine = np.cos(angles), np.sin(angles)
    rest = np.zeros((length, HEAD - ROT), np.float32)
    keep = np.concatenate([cosine, cosine, rest + 1], 1)
    swap = np.concatenate([-sine, sine, rest], 1)
    return [np.tile(t, (1, 128 // HEAD)).astype(np.float32) for t in (keep, swap)]


def normalize(values):
    center = values - jnp.mean(values, -1, keepdims=True)
    inverse = lax.rsqrt(jnp.mean(center * center, -1, keepdims=True) + EPSILON)
    return center * inverse, inverse


class Copies:
    def __init__(self, sems):
        self.sems, self.all, self.open = sems, [], []

    def start(self, src, dst):
        copy = pltpu.make_async_copy(src, dst, self.sems.at[len(self.all)])
        copy.start()
        self.all.append(copy)
        self.open.append(copy)
        return copy

    def wait(self, *copies):
        for copy in copies or list(self.open):
            copy.wait()
            self.open.remove(copy)


def columns_of(ref, depth):
    half_rows = ref.shape[0] // 2

    def part(f, half):
        span = aligned(f * depth, depth)
        if half is None:
            return ref.at[:, span]
        return ref.at[pl.ds(half * half_rows, half_rows), span]

    return part


def rows_of(ref, chunk):
    return lambda s: ref.at[aligned(s * chunk, chunk)]


class Fold:
    def __init__(self, net, tile, total, mate_in, coming, mate_out, out, mate_send, mate_recv, send, recv):
        self.net, self.tile, self.total = net, tile, total
        self.mate_in, self.coming, self.mate_out, self.out = mate_in, coming, mate_out, out
        self.mate_send, self.mate_recv, self.send, self.recv = mate_send, mate_recv, send, recv
        self.chunk = total.shape[0]
        self.pieces = recv.shape[1]
        self.rows = self.chunk // self.pieces

    @staticmethod
    def shared(chunk, width):
        return [pltpu.VMEM((2 * chunk, TILE), F32), pltpu.VMEM((chunk, width), F32)]

    @staticmethod
    def buffers(n_s, chunk, width):
        n_l = n_s // 2
        return [
            pltpu.VMEM((n_l, chunk, width), BF),
            pltpu.VMEM((n_l + 1, chunk, width), BF),
            pltpu.VMEM((3, chunk, width), BF),
            pltpu.VMEM((n_l, chunk, width), BF),
        ]

    @staticmethod
    def sems(n_s, pieces=4):
        n_l = n_s // 2
        return [
            pltpu.SemaphoreType.DMA((3, pieces)),
            pltpu.SemaphoreType.DMA((n_l, pieces)),
            pltpu.SemaphoreType.DMA((n_l, pieces)),
            pltpu.SemaphoreType.DMA((n_l + 1, pieces)),
        ]

    def place(self, other):
        return (other >= 0) & (other < self.net.n_l)

    def fed(self, side):
        return self.place(self.net.z + 1 - 2 * side)

    def span(self, piece):
        return aligned(piece * self.rows, self.rows)

    def each_piece(self, act):
        pl.loop(0, self.pieces)(act)

    def to_mate(self, target, slot, piece):
        span = self.span(piece)
        return put(
            self.mate_out.at[slot, span],
            self.mate_in.at[target, span],
            self.mate_send.at[slot, piece],
            self.mate_recv.at[target, piece],
            seq=self.net.mate,
        )

    def onward(self, target, side, hop, piece):
        span = self.span(piece)
        slot = target + (self.net.n_l - target) * (1 - side) * (1 // hop)
        return put(
            self.out.at[target, span],
            self.coming.at[slot, span],
            self.send.at[target, piece],
            self.recv.at[slot, piece],
            seq=self.net.s + 4 * side - 2,
        )

    def came(self, slot, piece):
        place = self.coming.at[slot, self.span(piece)]
        put(place, place, self.send.at[0, 0], self.recv.at[slot, piece], seq=self.net.mate).wait_recv()

    def mate_sent(self, slot):
        self.each_piece(lambda piece: self.to_mate(self.net.z, slot, piece).wait_send())

    def begin_one(self, target, slot, produce):
        mine = aligned(self.net.c * self.chunk, self.chunk)
        theirs = aligned((1 - self.net.c) * self.chunk, self.chunk)

        def write(cols, value):
            self.tile[...] = value
            self.out[target, :, cols] = self.tile[mine, :].astype(BF)
            self.mate_out[slot, :, cols] = self.tile[theirs, :].astype(BF)

        produce(target, write)
        self.each_piece(lambda piece: self.to_mate(target, slot, piece).start())

    def targets(self, wave, near, act):
        net = self.net
        above = wave if near else net.n_l - wave

        @pl.loop(0, 2)
        def _(turn):
            side = (1 - (2 * net.z) // net.n_l + turn) % 2
            target = net.n_l - 1 - above + (2 * above - net.n_l + 1) * side
            hop = (target - net.z) * (2 * side - 1)
            pl.when(hop > 0)(lambda: act(target, side, hop, turn))

    def begins(self, wave, produce):
        net = self.net
        above = net.n_l - wave

        @pl.loop(0, 3)
        def _(turn):
            here = turn // 2
            side = (1 - (2 * net.z) // net.n_l + turn) % 2
            target = net.n_l - 1 - above + (2 * above - net.n_l + 1) * side
            hop = (target - net.z) * (2 * side - 1)

            @pl.when(((here == 0) & (hop > 0)) | ((here == 1) & (wave == min(2, net.n_l - 1))))
            def _():
                @pl.when((here == 0) & self.place(target + 2 * side - 1))
                def _():
                    self.mate_sent(side)

                self.begin_one(
                    target + (net.z - target) * here, side + (2 - side) * here, produce
                )

    def leave(self, wave, near=False):
        def act(target, side, hop, turn):
            @pl.when(jnp.logical_not(self.fed(side)))
            def _():
                self.each_piece(lambda piece: self.pass_piece(target, side, hop, piece, False))

        self.targets(wave, near, act)

    def passes(self, wave, near=False):
        def act(target, side, hop, turn):
            @pl.when(self.fed(side))
            def _():
                self.each_piece(lambda piece: self.pass_piece(target, side, hop, piece, True))

        self.targets(wave, near, act)

    def passes_between(self, wave, near, between):
        net = self.net
        above = wave if near else net.n_l - wave

        @pl.loop(0, 2)
        def _(turn):
            side = (1 - (2 * net.z) // net.n_l + turn) % 2
            target = net.n_l - 1 - above + (2 * above - net.n_l + 1) * side
            hop = (target - net.z) * (2 * side - 1)

            @self.each_piece
            def _(piece):
                @pl.when((hop > 0) & self.fed(side))
                def _():
                    self.pass_piece(target, side, hop, piece, True)

                between(turn, piece)

    def far(self, produce, begun=None, passing=True):
        net = self.net

        @pl.loop(1, net.n_l)
        def _(wave):
            self.begins(wave, produce)
            pl.when(wave > 1)(lambda: self.leave(wave - 1))
            if begun is not None:
                begun(wave)
            if passing:
                self.passes(wave)

        self.leave(net.n_l - 1)

    def pass_piece(self, target, side, hop, piece, fed):
        self.to_mate(target, 0, piece).wait_recv()
        span = self.span(piece)
        value = self.out[target, span, :].astype(F32) + self.mate_in[target, span, :].astype(F32)
        if fed:
            self.came(target, piece)
            value = value + self.coming[target, span, :].astype(F32)
        self.out[target, span, :] = value.astype(BF)
        self.onward(target, side, hop, piece).start()

    def finals(self):
        net = self.net

        @self.each_piece
        def _(piece):
            self.to_mate(net.z, 0, piece).wait_recv()
            span = self.span(piece)
            self.total[span, :] = self.out[net.z, span, :].astype(F32) + self.mate_in[net.z, span, :].astype(F32)

        @pl.loop(0, 2)
        def _(turn):
            side = (1 - (2 * net.z) // net.n_l + turn) % 2

            @pl.when(self.fed(side))
            def _():
                slot = net.z + (net.n_l - net.z) * (1 - side)

                @self.each_piece
                def _(piece):
                    span = self.span(piece)
                    self.came(slot, piece)
                    self.total[span, :] = self.total[span, :] + self.coming[slot, span, :].astype(F32)

    def finish(self):
        net = self.net
        self.mate_sent(2)
        for side in range(2):
            pl.when(self.place(net.z + 2 * side - 1))(functools.partial(self.mate_sent, side))

        @pl.loop(1, net.n_l)
        def _(hop):
            net.sides(
                hop,
                lambda target, side: self.each_piece(
                    lambda piece: self.onward(target, side, hop, piece).wait_send()
                ),
            )


class GridSum:
    def __init__(self, net, stage, came, sems):
        self.net, self.stage, self.came, self.sems = net, stage, came, sems
        self.half = stage.shape[1] // 2
        self.rows = next(r for r in (176, 128, 96, 64, 32, 16) if self.half % r == 0)
        self.cols = range(1, net.tall)
        self.along = range(1, net.wide)
        self.bases = self.layout(net.n_f)

    @staticmethod
    def layout(n_f):
        tall = 2 if n_f % 2 == 0 else 1
        wide = n_f // tall
        sizes = [(wide - 1) * tall, (tall - 1) * wide, tall - 1, wide - 1]
        return [sum(sizes[:at]) for at in range(5)]

    @staticmethod
    def scratch(n_f, rows, columns):
        count = GridSum.layout(n_f)[4]
        return [
            pltpu.VMEM((n_f, rows, columns), BF),
            pltpu.VMEM((count, rows // 2, columns), BF),
            pltpu.SemaphoreType.DMA((2, count + GridEnd.count(n_f))),
        ]

    def slot(self, kind, i, j):
        base = self.bases[kind]
        return base + [(j - 1) * self.net.tall + i, (i - 1) * self.net.wide + j, i - 1, j - 1][kind]

    def rank(self, i, j):
        net = self.net
        return ((net.a + i) % net.tall) * net.wide + (net.b + j) % net.wide

    def owner(self, at):
        return self.rank(at // self.net.wide, at % self.net.wide)

    def copy(self, kind, i, j):
        half = kind % 2
        along = kind in (0, 3)
        slot = self.slot(kind, i, j)
        at = i * self.net.wide + j
        return put(
            self.stage.at[at, pl.ds(half * self.half, self.half)],
            self.came.at[slot],
            self.sems.at[0, slot],
            self.sems.at[1, slot],
            fsdp=self.rank(0, j) if along else self.rank(i, 0),
        )

    def first(self, at):
        i, j = at // self.net.wide, at % self.net.wide

        @pl.when(j > 0)
        def _():
            self.copy(0, i, j).start()

        @pl.when(i > 0)
        def _():
            self.copy(1, i, j).start()

    def gather(self, half, at, slots, write):
        @pl.loop(0, self.half // self.rows)
        def _(step):
            span = aligned(half * self.half + step * self.rows, self.rows, 16)
            value = self.stage[at, span, :].astype(F32)
            for slot in slots:
                value = value + self.came[slot, aligned(step * self.rows, self.rows, 16), :].astype(F32)
            write(span, value)

    def wait(self, *copies):
        for kind, i, j in copies:
            self.copy(kind, i, j).wait_recv()
        return [self.slot(*copy) for copy in copies]

    def second(self):
        for i in self.cols:
            at = i * self.net.wide
            self.gather(0, at, self.wait(*[(0, i, j) for j in self.along]), self.keep(at))
            self.copy(2, i, 0).start()
        for j in self.along:
            self.gather(1, j, self.wait(*[(1, i, j) for i in self.cols]), self.keep(j))
            self.copy(3, 0, j).start()

    def keep(self, at):
        def write(span, value):
            self.stage[at, span, :] = value.astype(BF)

        return write

    def sum_first(self, own_only=False):
        for i in range(1 if own_only else self.net.tall):
            at = i * self.net.wide
            self.gather(0, at, self.wait(*[(0, i, j) for j in self.along]), self.keep(at))
        for j in range(1 if own_only else self.net.wide):
            self.gather(1, j, self.wait(*[(1, i, j) for i in self.cols]), self.keep(j))

    def hand_on(self, out, done=False):
        net = self.net
        shards = [(0, 0), (0, 1), *[(i * net.wide, 0) for i in self.cols], *[(j, 1) for j in self.along]]
        sources = [self.stage.at[at, pl.ds(half * self.half, self.half)] for at, half in shards]
        if done:
            came = self.wait(*[(2, i, 0) for i in self.cols], *[(3, 0, j) for j in self.along])
            sources[2:] = [self.came.at[slot] for slot in came]
        return [
            pltpu.make_async_copy(source, out.at[k], self.sems.at[0, self.bases[4] + k])
            for k, source in enumerate(sources)
        ]

    def last(self, out):
        def write(span, value):
            out[span, :] = value

        self.gather(
            0, 0, self.wait(*[(0, 0, j) for j in self.along], *[(2, i, 0) for i in self.cols]), write
        )
        self.gather(
            1, 0, self.wait(*[(1, i, 0) for i in self.cols], *[(3, 0, j) for j in self.along]), write
        )

    def finish_first(self):
        for i in range(self.net.tall):
            for j in range(self.net.wide):
                if j:
                    self.copy(0, i, j).wait_send()
                if i:
                    self.copy(1, i, j).wait_send()

    def finish(self):
        self.finish_first()
        for i in self.cols:
            self.copy(2, i, 0).wait_send()
        for j in self.along:
            self.copy(3, 0, j).wait_send()


class GridEnd:
    def __init__(self, net, sums, came=None, sems=None):
        self.net, self.sums, self.came, self.sems = net, sums, came, sems

    @staticmethod
    def count(n_f):
        tall = 2 if n_f % 2 == 0 else 1
        return tall + n_f // tall

    @staticmethod
    def scratch(n_f, rows, columns):
        count = GridEnd.count(n_f)
        sums = pltpu.VMEM((count, rows // 2, columns), BF)
        return [
            sums,
            sums,
            sums,
            pltpu.VMEM((count - 2, rows // 2, columns), BF),
            pltpu.SemaphoreType.DMA((2, count - 2)),
        ]

    def copies(self):
        net = self.net
        f = [((net.a + i) % net.tall) * net.wide + net.b for i in range(1, net.tall)]
        f += [net.a * net.wide + (net.b + j) % net.wide for j in range(1, net.wide)]
        return [
            put(self.sums.at[2 + k], self.came.at[k], self.sems.at[0, k], self.sems.at[1, k], fsdp=to)
            for k, to in enumerate(f)
        ]

    def start(self):
        for copy in self.copies():
            copy.start()

    def last(self, out):
        came, base = self.sums, 2
        if self.came is not None:
            came, base = self.came, 0
            for copy in self.copies():
                copy.wait()
        half = self.sums.shape[1]
        rows = next(r for r in (176, 128, 96, 64, 32, 16) if half % r == 0)
        down = range(self.net.tall - 1)
        along = range(self.net.tall - 1, self.net.tall + self.net.wide - 2)
        for at, slots in enumerate((down, along)):

            @pl.loop(0, half // rows)
            def _(step):
                span = aligned(step * rows, rows, 16)
                value = self.sums[at, span, :].astype(F32)
                for slot in slots:
                    value = value + came[base + slot, span, :].astype(F32)
                out[aligned(at * half + step * rows, rows, 16), :] = value


class PacketSum:
    def __init__(self, net, out, seq_in, total, fsdp_in, sems):
        self.net, self.out, self.seq_in, self.total, self.fsdp_in, self.sems = net, out, seq_in, total, fsdp_in, sems

    @staticmethod
    def scratch(n_f, n_s):
        return [
            pltpu.VMEM((n_s, n_f, SMALL, 128), F32),
            pltpu.VMEM((n_s, n_f, SMALL, 128), F32),
            pltpu.VMEM((n_f, SMALL, 128), F32),
            pltpu.VMEM((n_f, SMALL, 128), F32),
            pltpu.SemaphoreType.DMA((2 * (n_f + n_s),)),
        ]

    def one(self, k):
        to = (self.net.s + k) % self.net.n_s
        return put(self.out.at[to], self.seq_in.at[k], self.sems.at[2 * k], self.sems.at[2 * k + 1], seq=to)

    def two(self, k):
        to = (self.net.f + k) % self.net.n_f
        at = 2 * (self.net.n_s + k)
        return put(self.total.at[to], self.fsdp_in.at[k], self.sems.at[at], self.sems.at[at + 1], fsdp=to)

    def start(self, terms, width):
        net = self.net
        per = 128 // width
        for tile in range(net.n_f * net.n_s // per):
            value = terms[:, tile * 128 : (tile + 1) * 128]
            for j in range(per):
                f, s = divmod(tile * per + j, net.n_s)
                self.out[s, f] = pltpu.roll(value, 128 - j * width, axis=1) if j else value
        for k in range(1, net.n_s):
            self.one(k).start()

    def middle(self):
        net = self.net
        total = self.out[net.s]
        for k in range(1, net.n_s):
            self.one(k).wait()
            total = total + self.seq_in[k]
        self.total[...] = total
        for k in range(1, net.n_f):
            self.two(k).start()

    def finish(self, result):
        net = self.net
        total = self.total[net.f]
        for k in range(1, net.n_f):
            self.two(k).wait()
            total = total + self.fsdp_in[k]
        result[...] = total


def norm_backward(rows, source, grad, gain, terms, at, write):
    terms[at : at + 2, :] = jnp.zeros((2, terms.shape[1]), F32)

    @pl.loop(0, rows // 32)
    def _(i):
        span = aligned(i * 32, 32)
        scaled, inverse = normalize(source[span, :].astype(F32))
        value = grad[span, :]
        upstream = value * gain
        inner = jnp.mean(upstream, -1, keepdims=True)
        cross = jnp.mean(upstream * scaled, -1, keepdims=True)
        terms[at : at + 1, :] = terms[at : at + 1, :] + jnp.sum(value * scaled, 0, keepdims=True)
        terms[at + 1 : at + 2, :] = terms[at + 1 : at + 2, :] + jnp.sum(value, 0, keepdims=True)
        write(i, span, inverse * (upstream - inner - scaled * cross))


def layer_kernel(
    tok,
    packet,
    wq_own,
    wo_own,
    wg_own,
    wu_own,
    wd_own,
    gout_own,
    cosine,
    sine,
    q_o,
    k_o,
    kt_o,
    v_o,
    att_o,
    lse_o,
    n1_o,
    gains_o,
    wq_o,
    wo_o,
    dm_o,
    dmid_o,
    top_o,
    terms_o,
    gate_o,
    up_o,
    down_o,
    rows,
    gout,
    wq,
    wo,
    wg,
    wu,
    wd,
    q,
    k,
    kt,
    v,
    vt,
    ot,
    att,
    hidden,
    dgate,
    dup,
    mid,
    low,
    packets,
    tiles,
    total,
    *rest,
):
    net = Net()
    chunk, width = tok.shape
    length = chunk * net.n_s
    depth = wq_own.shape[1]
    columns = wq_own.shape[2]
    heads = columns // HEAD
    pair = 2 * chunk
    buffers, rest = rest[:4], rest[4:]
    folds = []
    for _ in range(3):
        folds.append(Fold(net, tiles, total, *buffers, *rest[:4]))
        rest = rest[4:]
    att_fold, normed_fold, top_fold = folds
    line_sems = [rest[at : at + 3] for at in (0, 3, 6, 9)]
    rest = rest[12:]
    spread_sems, rest = rest[:5], rest[5:]
    gate_sum, up_sum, down_sum = [GridSum(net, *rest[at : at + 3]) for at in (0, 3, 6)]
    sums = (down_sum, gate_sum, up_sum)
    pk_sems, copy_sems, n1_sems = rest[9:]
    copies = Copies(copy_sems)
    n1 = att_fold.mate_out

    net.barrier()

    def wq_part(f, half):
        if half is None:
            return wq.at[:, aligned(f * depth, depth), :]
        return wq.at[:, aligned(f * depth + half * (depth // 2), depth // 2), :]

    spread_q = Spread(net, wq_own, wq_part, spread_sems[0])
    spread_o, spread_g, spread_u, spread_d = [
        Spread(net, own, columns_of(full, depth), sems)
        for own, full, sems in zip((wo_own, wg_own, wu_own, wd_own), (wo, wg, wu, wd), spread_sems[1:])
    ]
    pk = Packets(net, packet, packets, pk_sems)
    line = Line(net, tok, rows_of(rows, chunk), *line_sems[0])
    gout_line = Line(net, gout_own, rows_of(gout, chunk), *line_sems[1])
    n2_line = Line(net, low, rows_of(rows, chunk), *line_sems[2])
    dm_line = Line(net, low, rows_of(dm_o, chunk), *line_sems[3])

    def pairs(which, hop):
        net.sides(hop, lambda other, side: which.pair(other))

    def blocks(hop, act):
        def once(other, side):
            @pl.when((hop > 0) | (side == 0))
            def _():
                act(other, side)

        net.sides(hop, once)

    pk.start()
    line.start()
    spread_q.start()
    pk.middle()
    pk.finish()
    pk.unpack(gains_o, width // (net.n_f * net.n_s))

    def project_block(other, side):
        span = aligned(other * pair, pair)
        gain, shift = gains_o[0:1, :], gains_o[1:2, :]

        for part in range(2):

            @pl.loop(0, chunk // 32)
            def _(i):
                at = aligned((2 * other + part) * chunk + i * 32, 32)
                scaled, _ = normalize(rows[at, :].astype(F32))
                n1[part, aligned(i * 32, 32), :] = (scaled * gain + shift).astype(BF)

        keeps = [
            pltpu.make_async_copy(
                n1.at[part], n1_o.at[aligned((2 * other + part) * chunk, chunk)], n1_sems.at[part]
            )
            for part in range(2)
        ]
        for copy in keeps:
            copy.start()
        left = n1[0:2].reshape(pair, width)
        cols = aligned(net.s * columns, columns)
        tables = cosine[span, :], sine[span, :]
        for kind in range(3):
            value = dot(left, wq[kind]) + gains_o[4 + kind : 5 + kind, cols]
            if kind == 0:
                q[span, :] = rotary(value, *tables).astype(BF)
            elif kind == 1:
                value = rotary(value, *tables)
                k[span, :] = value.astype(BF)
                kt[...] = value.T.astype(BF)
            else:
                v[...] = value.astype(BF)
                vt[:, span] = value.T.astype(BF)
        for copy in (
            pltpu.make_async_copy(kt, kt_o.at[:, span], n1_sems.at[2]),
            pltpu.make_async_copy(v, v_o.at[span], n1_sems.at[3]),
        ):
            copy.start()
            keeps.append(copy)
        for copy in keeps:
            copy.wait()

    line.here()
    for hop in range(1, net.n_l - 1):
        line.step(hop)
        if hop == 1:
            spread_q.relay()
        pairs(line, hop)
    spread_q.finish()
    spread_o.start()
    spread_g.start()
    pl.loop(0, net.n_l - 1)(lambda hop: blocks(hop, project_block))
    line.step(net.n_l - 1)
    gout_line.start()
    pairs(line, net.n_l - 1)
    spread_o.relay()
    spread_u.start()
    blocks(net.n_l - 1, project_block)
    for pair_of in ((wq, wq_o), (q, q_o), (k, k_o)):
        copies.start(*pair_of)
    spread_o.finish()
    line.finish()

    def attend(i):
        lo, hi = i * pair, (i + 1) * pair

        @pl.loop(0, heads)
        def _(head):
            lane = lax.broadcasted_iota(jnp.int32, (1, columns), 1)
            here = jnp.where(lane // HEAD == head, HEAD**-0.5, 0.0).astype(BF)
            visible = lax.broadcasted_iota(jnp.int32, (pair, pair), 0) <= lax.broadcasted_iota(
                jnp.int32, (pair, pair), 1
            )
            head_rows = aligned(head * HEAD, HEAD)
            query = q[lo:hi, :] * here
            near = jnp.where(visible, dot_nt(k[lo:hi, :], query), NEG_LARGE)
            highest = jnp.max(near, 0, keepdims=True)
            if i:
                far = dot_nt(k[0:lo, :], query)
                highest = jnp.maximum(highest, jnp.max(far, 0, keepdims=True))
            near = jnp.exp(near - highest)
            sum_of = jnp.sum(near, 0, keepdims=True)
            out = dot(vt[head_rows, lo:hi], near.astype(BF))
            if i:
                far = jnp.exp(far - highest)
                sum_of = sum_of + jnp.sum(far, 0, keepdims=True)
                out = out + dot(vt[head_rows, 0:lo], far.astype(BF))
            ot[head_rows, :] = out / sum_of
            lse_o[pl.ds(head, 1), lo:hi] = highest + jnp.log(sum_of)

        att[lo:hi, :] = ot[...].T.astype(BF)

    def produce_attended(place, write):
        for i in range(net.n_l):
            pl.when(place == i)(functools.partial(attend, i))
        left = att[aligned(place * pair, pair), :]

        @pl.loop(0, width // TILE)
        def _(j):
            cols = aligned(j * TILE, TILE)
            write(cols, dot(left, wo[:, cols]))

    def begun(wave):
        pl.when(wave < net.n_l - 1)(lambda: gout_line.step(wave))
        pl.when(wave == 1)(spread_d.start)

    att_fold.far(produce_attended, begun)
    spread_g.relay()
    spread_u.relay()
    gout_line.step(net.n_l - 1)
    copies.start(att, att_o)
    copies.start(wo, wo_o)
    att_fold.finals()
    gain_two, shift_two = gains_o[2:3, :], gains_o[3:4, :]

    @pl.loop(0, chunk // 32)
    def _(i):
        span = aligned(i * 32, 32)
        value = rows[aligned(net.s * chunk + i * 32, 32), :].astype(F32) + total[span, :]
        mid[span, :] = value
        scaled, _ = normalize(value)
        low[span, :] = (scaled * gain_two + shift_two).astype(BF)

    n2_line.start()
    spread_d.relay()
    att_fold.finish()
    gout_line.here()
    pl.loop(1, net.n_l)(lambda hop: pairs(gout_line, hop))

    def forward_block(other):
        span = aligned(other * pair, pair)
        right = rows[span, :]
        half = hidden.shape[0] // 2

        @pl.loop(0, 2)
        def _(part):
            units = aligned(part * half, half, 16)
            gate = dot_nt(wg[units, :], right)
            up = dot_nt(wu[units, :], right)
            back = dot_nt(wd[units, :], gout[span, :])
            sigma = jax.nn.sigmoid(gate)
            active = gate * sigma
            hidden[units, span] = (active * up).astype(BF)
            dgate[units, span] = (back * up * (sigma * (1.0 + gate * (1.0 - sigma)))).astype(BF)
            dup[units, span] = (back * active).astype(BF)

    def produce_normed(place, write):
        span = aligned(place * pair, pair)
        left, right = dgate[:, span].T, dup[:, span].T

        @pl.loop(0, width // TILE)
        def _(j):
            cols = aligned(j * TILE, TILE)
            write(cols, dot(left, wg[:, cols]) + dot(right, wu[:, cols]))

    def settle(hop):
        def act(other, side):
            begins = (hop == 0) | normed_fold.fed(side)

            @pl.when(begins)
            def _():
                pl.when(hop > 1)(lambda: normed_fold.mate_sent(side))
                normed_fold.begin_one(other, side + (2 - side) * (1 // (hop + 1)), produce_normed)

            @pl.when(jnp.logical_not(begins))
            def _():
                normed_fold.each_piece(lambda piece: normed_fold.pass_piece(other, side, hop, piece, False))

        blocks(hop, act)

    def forward_blocks(hop):
        def act(other, side):
            forward_block(other)

            @pl.when(jnp.logical_not(normed_fold.fed(side)))
            def _():
                pl.when(hop > 1)(lambda: normed_fold.mate_sent(side))
                normed_fold.begin_one(other, side, produce_normed)

        net.sides(hop, act)

    n2_line.here()
    n2_line.step(1)
    for spread in (spread_g, spread_u, spread_d):
        spread.finish()
    forward_block(net.z)

    @pl.loop(1, net.n_l)
    def _(hop):
        pl.when(hop > 1)(lambda: n2_line.step(hop))
        settle(hop - 1)
        pairs(n2_line, hop)
        forward_blocks(hop)

    settle(net.n_l - 1)

    def weight_terms(task):
        at, kind = net.n_f - 1 - task // 3, task % 3
        cols = aligned(gate_sum.owner(at) * depth, depth)
        for way, (grid_sum, left, right) in enumerate(
            ((down_sum, hidden, gout), (gate_sum, dgate, rows), (up_sum, dup, rows))
        ):

            @pl.when(kind == way)
            def _():
                half = left.shape[0] // 2

                @pl.loop(0, 2)
                def _(part):
                    units = aligned(part * half, half, 16)
                    grid_sum.stage[at, units, :] = dot(left[units, :], right[:, cols]).astype(BF)

                grid_sum.first(at)

    tasks = 3 * net.n_f
    waves = max(net.n_l - 2, 1)
    each = -(-tasks // (2 * normed_fold.pieces * waves))
    for wave in range(net.n_l - waves, net.n_l):

        def between(turn, piece):
            slot = ((wave - net.n_l + waves) * 2 + turn) * normed_fold.pieces + piece

            @pl.loop(0, each)
            def _(i):
                pl.when(slot * each + i < tasks)(lambda: weight_terms(slot * each + i))

        normed_fold.passes_between(wave, True, between)
    normed_fold.finals()
    n2_line.finish()

    def write_middle(i, span, value):
        value = value + gout[aligned(net.s * chunk + i * 32, 32), :].astype(F32)
        dmid_o[span, :] = value
        low[span, :] = value.astype(BF)

    terms_o[...] = jnp.zeros(terms_o.shape, F32)
    norm_backward(chunk, mid, total, gain_two, terms_o, 2, write_middle)
    dm_line.start()
    normed_fold.finish()

    def produce_top(place, write):
        left = hidden[:, aligned(place * pair, pair)].T

        @pl.loop(0, width // TILE)
        def _(j):
            cols = aligned(j * TILE, TILE)
            write(cols, dot(left, wd[:, cols]))

    dm_line.here()
    dm_line.step(1)
    top_fold.far(produce_top, passing=False)
    pl.loop(2, net.n_l)(dm_line.step)
    for grid_sum in sums[:2]:
        grid_sum.second()
    for wave in range(1, net.n_l - 1):
        top_fold.passes(wave)
    top_fold.finals()

    @pl.loop(0, chunk // 32)
    def _(i):
        span = aligned(i * 32, 32)
        top_fold.out[net.z, span, :] = (mid[span, :] + total[span, :]).astype(BF)

    copies.start(top_fold.out.at[net.z], top_o)
    top_fold.finish()
    pl.loop(1, net.n_l)(lambda hop: pairs(dm_line, hop))
    gout_line.finish()
    dm_line.finish()
    hands = []
    for grid_sum, out in zip(sums, (down_o, gate_o, up_o)):
        grid_sum.sum_first(grid_sum in sums[:2])
        hands.extend(grid_sum.hand_on(out, grid_sum in sums[:2]))
        for copy in hands[-GridEnd.count(net.n_f) :]:
            copy.start()
    for grid_sum in sums[:2]:
        grid_sum.finish()
    sums[2].finish_first()
    for copy in hands:
        copy.wait()
    copies.wait()


def layer_part(tokens, packet, wq, wo, wg, wu, wd, gout, tables):
    chunk, width = tokens.shape
    n_f, n_s = lax.axis_size("fsdp"), lax.axis_size("seq")
    length = chunk * n_s
    depth, columns = wq.shape[1:]
    units = wg.shape[0]
    shape = jax.ShapeDtypeStruct
    wide, head, turned, weight = (length, width), (length, columns), (units, length), (units, width)
    return pl.pallas_call(
        layer_kernel,
        name="layer",
        out_shape=[
            shape(head, BF),
            shape(head, BF),
            shape((columns, length), BF),
            shape(head, BF),
            shape(head, BF),
            shape((8, length), F32),
            shape(wide, BF),
            shape((SMALL, width), F32),
            shape((3, width, columns), BF),
            shape((columns, width), BF),
            shape(wide, BF),
            shape((chunk, width), F32),
            shape((chunk, width), BF),
            shape((SMALL, width), F32),
            *[shape((GridEnd.count(n_f), units // 2, depth), BF)] * 3,
        ],
        in_specs=[ANY, VMEM, *[ANY] * 6, VMEM, VMEM],
        out_specs=[*[ANY] * 5, VMEM, ANY, VMEM, *[ANY] * 3, VMEM, ANY, VMEM, *[ANY] * 3],
        scratch_shapes=[
            pltpu.VMEM(wide, BF),
            pltpu.VMEM(wide, BF),
            pltpu.VMEM((3, width, columns), BF),
            pltpu.VMEM((columns, width), BF),
            *[pltpu.VMEM(weight, BF)] * 3,
            pltpu.VMEM(head, BF),
            pltpu.VMEM(head, BF),
            pltpu.VMEM((columns, 2 * chunk), BF),
            pltpu.VMEM((2 * chunk, columns), BF),
            pltpu.VMEM((columns, length), BF),
            pltpu.VMEM((columns, 2 * chunk), F32),
            pltpu.VMEM(head, BF),
            *[pltpu.VMEM(turned, BF)] * 3,
            pltpu.VMEM((chunk, width), F32),
            pltpu.VMEM((chunk, width), BF),
            pltpu.VMEM((n_s, n_f, SMALL, 128), F32),
            *Fold.shared(chunk, width),
            *Fold.buffers(n_s, chunk, width),
            *Fold.sems(n_s) * 3,
            *Line.sems(n_s) * 4,
            *[pltpu.SemaphoreType.DMA((Spread.count(n_f),))] * 5,
            *GridSum.scratch(n_f, units, depth) * 3,
            pltpu.SemaphoreType.DMA((Packets.count(n_f, n_s),)),
            pltpu.SemaphoreType.DMA((8,)),
            pltpu.SemaphoreType.DMA((4,)),
        ],
        compiler_params=pltpu.CompilerParams(
            collective_id=1, has_side_effects=True, vmem_limit_bytes=VMEM_BYTES
        ),
        cost_estimate=pl.CostEstimate(
            flops=2 * length * width * (4 * columns + 9 * units),
            bytes_accessed=8 * length * width,
            transcendentals=length * (length * columns // HEAD + units),
        ),
    )(tokens, packet, wq, wo, wg, wu, wd, gout, *tables)


def back_kernel(
    dm_in,
    wo_in,
    att_in,
    q_in,
    k_in,
    kt_in,
    v_in,
    n1_in,
    wq_in,
    down_in,
    gate_in,
    up_in,
    lse,
    tok,
    dmid,
    gains,
    terms_in,
    cosine,
    sine,
    gin_o,
    small_o,
    out_o,
    qkv_o,
    down_o,
    gate_o,
    up_o,
    dm,
    wo,
    att,
    q,
    k,
    kt,
    v,
    n1,
    wq,
    datt,
    dk,
    dv,
    dqt,
    dproj,
    terms,
    tiles,
    total,
    *rest,
):
    net = Net()
    chunk, width = tok.shape
    length, columns = q_in.shape
    heads = columns // HEAD
    pair = 2 * chunk
    depth = width // net.n_f
    block = 256
    buffers, rest = rest[:4], rest[4:]
    fold_sems, rest = rest[:4], rest[4:]
    packet_scratch, rest = rest[:5], rest[5:]
    out_sum, qkv_sum = GridSum(net, *rest[:3]), GridSum(net, *rest[3:6])
    ends = [GridEnd(net, rest[6]), GridEnd(net, rest[7]), GridEnd(net, *rest[8:11])]
    copy_sems = rest[11]

    copies = Copies(copy_sems)
    loads = [
        copies.start(src, dst)
        for src, dst in (
            (dm_in, dm),
            (wo_in, wo),
            (att_in, att),
            (q_in, q),
            (k_in, k),
            (kt_in, kt),
            (v_in, v),
            (n1_in, n1),
            (wq_in, wq),
            (down_in, ends[0].sums),
            (gate_in, ends[1].sums),
            (up_in, ends[2].sums),
        )
    ]
    net.barrier()
    copies.wait(*loads[:2])

    @pl.loop(0, length // block)
    def _(i):
        span = aligned(i * block, block)
        datt[span, :] = dot_nt(dm[span, :], wo[...]).astype(BF)
        dk[span, :] = jnp.zeros((block, columns), F32)
        dv[span, :] = jnp.zeros((block, columns), F32)

    copies.wait()
    ends[2].start()

    @pl.loop(0, heads)
    def _(head):
        lane = lax.broadcasted_iota(jnp.int32, (1, columns), 1)
        here = jnp.where(lane // HEAD == head, 1.0, 0.0).astype(BF)
        scale = HEAD**-0.5
        visible = lax.broadcasted_iota(jnp.int32, (block, block), 0) <= lax.broadcasted_iota(
            jnp.int32, (block, block), 1
        )
        head_rows = aligned(head * HEAD, HEAD)
        for i in range(length // block):
            lo, hi = i * block, (i + 1) * block
            query = q[lo:hi, :] * (here * scale)
            upstream = datt[lo:hi, :] * here
            logsum = lse[pl.ds(head, 1), lo:hi]

            def part(at, end, mask):
                probs = jnp.exp(dot_nt(k[at:end, :], query) - logsum)
                if mask:
                    probs = jnp.where(visible, probs, 0.0)
                grads = dot_nt(v[at:end, :], upstream)
                dv[at:end, :] = dv[at:end, :] + dot(probs.astype(BF), upstream)
                return probs, grads, jnp.sum(probs * grads, 0, keepdims=True)

            def scored(at, end, probs, grads, inner):
                scores = (probs * (grads - inner)).astype(BF)
                dk[at:end, :] = dk[at:end, :] + dot(scores, query)
                return dot(kt[head_rows, at:end], scores)

            near, near_grads, inner = part(lo, hi, True)
            if i:
                far, far_grads, more = part(0, lo, False)
                inner = inner + more
            out = scored(lo, hi, near, near_grads, inner)
            if i:
                out = out + scored(0, lo, far, far_grads, inner)
            dqt[head_rows, lo:hi] = out * scale

    terms[...] = terms_in[...]
    bias_cols = aligned(net.s * columns, columns)

    @pl.loop(0, length // block)
    def _(i):
        span = aligned(i * block, block)
        tables = cosine[span, :], -sine[span, :]
        parts = [
            rotary(dqt[:, span].T.astype(BF).astype(F32), *tables).astype(BF),
            rotary(dk[span, :].astype(BF).astype(F32), *tables).astype(BF),
            dv[span, :].astype(BF),
        ]
        for kind in range(3):
            dproj[kind, span, :] = parts[kind]
            row = slice(4 + kind, 5 + kind)
            terms[row, bias_cols] = terms[row, bias_cols] + jnp.sum(parts[kind].astype(F32), 0, keepdims=True)

    def weight_terms(task):
        at = net.n_f - 1 - task // 2
        cols = aligned(qkv_sum.owner(at) * depth, depth)

        @pl.when(task % 2 == 0)
        def _():
            left = n1[:, cols].T
            for kind in range(3):
                qkv_sum.stage[at, kind * depth : (kind + 1) * depth, :] = dot(left, dproj[kind]).astype(BF)
            qkv_sum.first(at)

        @pl.when(task % 2 == 1)
        def _():
            out_sum.stage[at] = dot_tn(att[...], dm[:, cols]).astype(BF)
            out_sum.first(at)

    def produce(place, write):
        span = aligned(place * pair, pair)

        @pl.loop(0, width // TILE)
        def _(j):
            cols = aligned(j * TILE, TILE)
            value = dot_nt(dproj[0, span, :], wq[0, cols, :])
            for kind in range(1, 3):
                value = value + dot_nt(dproj[kind, span, :], wq[kind, cols, :])
            write(cols, value)

    fold = Fold(net, tiles, total, *buffers, *fold_sems)
    fold.far(produce, passing=False)
    tasks = 2 * net.n_f
    ahead = min(4, tasks)
    pl.loop(0, ahead)(weight_terms)
    waves = max(net.n_l - 2, 1)
    each = -(-(tasks - ahead) // (2 * fold.pieces * waves))
    for wave in range(1, waves + 1):

        def between(turn, piece):
            slot = ((wave - 1) * 2 + turn) * fold.pieces + piece

            @pl.loop(0, each)
            def _(i):
                task = ahead + slot * each + i
                pl.when(task < tasks)(lambda: weight_terms(task))

        fold.passes_between(wave, False, between)
    fold.finals()

    def write_input(i, span, value):
        gin_o[span, :] = value + dmid[span, :]

    norm_backward(chunk, tok, total, gains[0:1, :], terms, 0, write_input)
    packet_sum = PacketSum(net, *packet_scratch)
    packet_sum.start(terms, width // (net.n_f * net.n_s))
    for grid_sum in (qkv_sum, out_sum):
        grid_sum.second()
    packet_sum.middle()
    for end, out in zip(ends, (down_o, gate_o, up_o)):
        end.last(out)
    packet_sum.finish(small_o)
    fold.finish()
    for grid_sum, out in ((qkv_sum, qkv_o), (out_sum, out_o)):
        grid_sum.last(out)
        grid_sum.finish()


def back_part(dm, wo, att, q, k, kt, v, n1, wq, down, gate, up, lse, tokens, dmid, gains, terms, tables):
    chunk, width = tokens.shape
    n_f, n_s = lax.axis_size("fsdp"), lax.axis_size("seq")
    length, columns = q.shape
    depth = width // n_f
    units = 2 * gate.shape[1]
    shape = jax.ShapeDtypeStruct
    return pl.pallas_call(
        back_kernel,
        name="back",
        out_shape=[
            shape((chunk, width), F32),
            shape((SMALL, 128), F32),
            shape((columns, depth), F32),
            shape((3 * depth, columns), F32),
            *[shape((units, depth), F32)] * 3,
        ],
        in_specs=[ANY] * 12 + [VMEM] * 7,
        out_specs=[VMEM] * 7,
        scratch_shapes=[
            pltpu.VMEM((length, width), BF),
            pltpu.VMEM((columns, width), BF),
            pltpu.VMEM((length, columns), BF),
            pltpu.VMEM((length, columns), BF),
            pltpu.VMEM((length, columns), BF),
            pltpu.VMEM((columns, length), BF),
            pltpu.VMEM((length, columns), BF),
            pltpu.VMEM((length, width), BF),
            pltpu.VMEM((3, width, columns), BF),
            pltpu.VMEM((length, columns), BF),
            pltpu.VMEM((length, columns), F32),
            pltpu.VMEM((length, columns), F32),
            pltpu.VMEM((columns, length), F32),
            pltpu.VMEM((3, length, columns), BF),
            pltpu.VMEM((SMALL, width), F32),
            *Fold.shared(chunk, width),
            *Fold.buffers(n_s, chunk, width),
            *Fold.sems(n_s),
            *PacketSum.scratch(n_f, n_s),
            *GridSum.scratch(n_f, columns, depth),
            *GridSum.scratch(n_f, 3 * depth, columns),
            *GridEnd.scratch(n_f, units, depth),
            pltpu.SemaphoreType.DMA((12,)),
        ],
        compiler_params=pltpu.CompilerParams(
            collective_id=3, has_side_effects=True, vmem_limit_bytes=VMEM_BYTES
        ),
        cost_estimate=pl.CostEstimate(
            flops=2 * length * columns * (8 * width + 5 * length),
            bytes_accessed=4 * length * width,
            transcendentals=length * length * columns // HEAD,
        ),
    )(dm, wo, att, q, k, kt, v, n1, wq, down, gate, up, lse, tokens, dmid, gains, terms, *tables)


def per_device(
    tokens,
    gain_one,
    shift_one,
    w_qkv,
    b_qkv,
    w_out,
    gain_two,
    shift_two,
    w_gate,
    w_up,
    w_down,
    grad_output,
):
    length = tokens.shape[1] * lax.axis_size("seq")
    width = gain_one.shape[0]
    packet = jnp.concatenate(
        [jnp.stack([gain_one, shift_one, gain_two, shift_two]), b_qkv, jnp.zeros((1, width), BF)]
    )
    packet = jnp.pad(packet.astype(F32), ((0, 0), (0, 128 - width)))
    tables = rotary_tables(length)
    q, k, kt, v, att, lse, n1, gains, wq, wo, dm, dmid, top, terms, gate, up, down = layer_part(
        tokens[0], packet, w_qkv.transpose(1, 0, 2), w_out, w_gate.T, w_up.T, w_down, grad_output[0], tables
    )
    grad_input, small, out, qkv, down, gate, up = back_part(
        dm, wo, att, q, k, kt, v, n1, wq, down, gate, up, lse, tokens[0], dmid, gains, terms, tables
    )

    return (
        top[None],
        grad_input[None],
        small[0, :width],
        small[1, :width],
        qkv.reshape(3, -1, qkv.shape[1]).transpose(1, 0, 2),
        small[4:7, :width],
        out,
        small[2, :width],
        small[3, :width],
        gate.T,
        up.T,
        down,
    )


def solution(mesh):
    whole = P(("fsdp", "seq"))
    rows = P("fsdp", "seq", None)
    inner = P("seq", "fsdp")
    outer = P("fsdp", "seq")
    heads = P("fsdp", None, "seq")
    bias = P(None, ("fsdp", "seq"))
    return jax.shard_map(
        per_device,
        mesh=mesh,
        in_specs=(rows, whole, whole, heads, bias, inner, whole, whole, outer, outer, inner, rows),
        out_specs=(rows, rows, whole, whole, heads, bias, inner, whole, whole, outer, outer, inner),
        check_vma=False,
    )
```

```python
import functools

import jax
import jax.numpy as jnp
import numpy as np
from jax import lax
from jax.experimental import pallas as pl
from jax.experimental.pallas import tpu as pltpu
from jax.sharding import PartitionSpec as P

HEAD = 64
ROT = 16
EPSILON = 1e-05
NEG_LARGE = -1e30
MESH = pl.DeviceIdType.MESH
ANY = pl.BlockSpec(memory_space=pl.ANY)
VMEM = pl.BlockSpec(memory_space=pltpu.VMEM)
BF = jnp.bfloat16
F32 = jnp.float32
VMEM_BYTES = 60 * 2**20
TILE = 512
SMALL = 8


def put(src, dst, send, recv, **device):
    return pltpu.make_async_remote_copy(
        src_ref=src, dst_ref=dst, send_sem=send, recv_sem=recv, device_id=device, device_id_type=MESH
    )


def dot(left, right):
    return jnp.dot(left, right, preferred_element_type=F32)


def dot_nt(left, right):
    return lax.dot_general(left, right, (((1,), (1,)), ((), ())), preferred_element_type=F32)


def dot_tn(left, right):
    return lax.dot_general(left, right, (((0,), (0,)), ((), ())), preferred_element_type=F32)


def aligned(start, size, unit=None):
    return pl.ds(pl.multiple_of(start, unit or size), size)


class Net:
    def __init__(self):
        self.n_f, self.n_s = lax.axis_size("fsdp"), lax.axis_size("seq")
        self.tall = 2 if self.n_f % 2 == 0 else 1
        self.wide = self.n_f // self.tall
        self.n_l = self.n_s // 2
        self.f, self.s = lax.axis_index("fsdp"), lax.axis_index("seq")
        self.a, self.b = self.f // self.wide, self.f % self.wide
        self.z, self.c = self.s // 2, self.s % 2
        self.mate = self.s + 1 - 2 * self.c

    def barrier(self):
        sem = pltpu.get_barrier_semaphore()
        for k in range(1, self.n_f):
            pl.semaphore_signal(
                sem, inc=1, device_id={"fsdp": (self.f + k) % self.n_f}, device_id_type=MESH
            )
        for k in range(1, self.n_s):
            pl.semaphore_signal(
                sem, inc=1, device_id={"seq": (self.s + k) % self.n_s}, device_id_type=MESH
            )
        pl.semaphore_wait(sem, self.n_f + self.n_s - 2)

    def sides(self, hop, act):
        @pl.loop(0, 2)
        def _(side):
            other = self.z + (2 * side - 1) * hop

            @pl.when((other >= 0) & (other < self.n_l))
            def _():
                act(other, side)


class Spread:
    def __init__(self, net, src, part, sems):
        self.net, self.src, self.part, self.sems = net, src, part, sems
        self.rows = [j for j in range(1, net.wide)]
        self.cols = [i for i in range(1, net.tall)]

    @staticmethod
    def count(n_f):
        tall = 2 if n_f % 2 == 0 else 1
        wide = n_f // tall
        return 1 + 2 * (wide - 1) + 2 * (tall - 1) + 4 * (wide - 1) * (tall - 1)

    def at(self, kind, i, j):
        w, t = len(self.rows), len(self.cols)
        base = {
            "own": 0,
            "row": 1,
            "col": 1 + 2 * w,
            "half0": 1 + 2 * w + 2 * t,
            "half1": 1 + 2 * w + 2 * t + 2 * w * t,
        }[kind]
        if kind == "own":
            return self.sems.at[0]
        k = j - 1 if kind == "row" else i - 1 if kind == "col" else (i - 1) * w + j - 1
        return self.sems.at[base + 2 * k], self.sems.at[base + 2 * k + 1]

    def rank(self, i, j):
        net = self.net
        return ((net.a + i) % net.tall) * net.wide + (net.b + j) % net.wide

    def back(self, i, j):
        net = self.net
        return ((net.a - i + net.tall) % net.tall) * net.wide + (net.b - j + net.wide) % net.wide

    def own(self):
        return pltpu.make_async_copy(self.src, self.part(self.net.f, None), self.at("own", 0, 0))

    def first(self, i, j):
        send, recv = self.at("row" if i == 0 else "col", i, j)
        return put(self.src, self.part(self.net.f, None), send, recv, fsdp=self.rank(i, j))

    def came(self, i, j):
        send, recv = self.at("row" if i == 0 else "col", i, j)
        place = self.part(self.back(i, j), None)
        return put(place, place, send, recv, fsdp=self.rank(i, j))

    def second(self, half, i, j, came=False):
        send, recv = self.at("half0" if half == 0 else "half1", i, j)
        origin = self.back(i, j) if came else self.back(0, j) if half == 0 else self.back(i, 0)
        place = self.part(origin, half)
        return put(place, place, send, recv, fsdp=self.rank(i, 0) if half == 0 else self.rank(0, j))

    def start(self):
        self.own().start()
        for i in self.cols:
            self.first(i, 0).start()
        for j in self.rows:
            self.first(0, j).start()

    def relay(self):
        for j in self.rows:
            self.came(0, j).wait_recv()
            for i in self.cols:
                self.second(0, i, j).start()
        for i in self.cols:
            self.came(i, 0).wait_recv()
            for j in self.rows:
                self.second(1, i, j).start()

    def finish(self):
        self.own().wait()
        for j in self.rows:
            self.first(0, j).wait_send()
        for i in self.cols:
            self.first(i, 0).wait_send()
        for i in self.cols:
            for j in self.rows:
                for half in range(2):
                    self.second(half, i, j, came=True).wait_recv()
                    self.second(half, i, j).wait_send()


class Line:
    def __init__(self, net, src, part, recv, send, local):
        self.net, self.src, self.part, self.recv, self.send, self.local = net, src, part, recv, send, local
        self.pieces = recv.shape[1]
        self.rows = src.shape[0] // self.pieces

    @staticmethod
    def sems(n_s, pieces=2):
        return [
            pltpu.SemaphoreType.DMA((n_s, pieces)),
            pltpu.SemaphoreType.DMA((4, n_s // 2, pieces)),
            pltpu.SemaphoreType.DMA((1,)),
        ]

    def cut(self, ref, piece):
        return ref.at[aligned(piece * self.rows, self.rows)]

    def own(self):
        return pltpu.make_async_copy(self.src, self.part(self.net.s), self.local.at[0])

    def on_line(self, src, chunk, side, hop, piece):
        return put(
            self.cut(src, piece),
            self.cut(self.part(chunk), piece),
            self.send.at[side, hop, piece],
            self.recv.at[chunk, piece],
            seq=self.net.s + 2 - 4 * side,
        )

    def to_mate(self, src, chunk, side, hop, piece):
        return put(
            self.cut(src, piece),
            self.cut(self.part(chunk), piece),
            self.send.at[2 + side, hop, piece],
            self.recv.at[chunk, piece],
            seq=self.net.mate,
        )

    def goes_on(self, side):
        after = self.net.z + 1 - 2 * side
        return (after >= 0) & (after < self.net.n_l)

    def each_piece(self, act):
        pl.loop(0, self.pieces)(act)

    def start(self):
        net = self.net

        @self.each_piece
        def _(piece):
            for side in range(2):

                @pl.when(self.goes_on(side))
                def _():
                    self.on_line(self.src, net.s, side, 0, piece).start()

            self.to_mate(self.src, net.s, 0, 0, piece).start()

        self.own().start()

    def came(self, chunk, piece):
        place = self.cut(self.part(chunk), piece)
        put(place, place, self.send.at[0, 0, 0], self.recv.at[chunk, piece], seq=self.net.mate).wait_recv()

    def step(self, hop):
        net = self.net

        @self.each_piece
        def _(piece):
            def act(other, side):
                chunk = 2 * other + net.c
                self.came(chunk, piece)

                @pl.when(self.goes_on(side))
                def _():
                    self.on_line(self.part(chunk), chunk, side, hop, piece).start()

                self.to_mate(self.part(chunk), chunk, side, hop, piece).start()

            net.sides(hop, act)

    def pair(self, other):
        @self.each_piece
        def _(piece):
            self.came(2 * other + 1 - self.net.c, piece)

    def here(self):
        self.own().wait()
        self.pair(self.net.z)

    def finish(self):
        net = self.net

        @self.each_piece
        def _(piece):
            for side in range(2):

                @pl.when(self.goes_on(side))
                def _():
                    self.on_line(self.src, net.s, side, 0, piece).wait_send()

            self.to_mate(self.src, net.s, 0, 0, piece).wait_send()

            @pl.loop(1, net.n_l)
            def _(hop):
                def act(other, side):
                    chunk = 2 * other + net.c

                    @pl.when(self.goes_on(side))
                    def _():
                        self.on_line(self.part(chunk), chunk, side, hop, piece).wait_send()

                    self.to_mate(self.part(chunk), chunk, side, hop, piece).wait_send()

                net.sides(hop, act)


class Packets:
    def __init__(self, net, src, buf, sems):
        self.net, self.src, self.buf, self.sems = net, src, buf, sems

    @staticmethod
    def count(n_f, n_s):
        return 1 + 2 * (n_f - 1) + 2 * (n_s - 1)

    def own(self):
        net = self.net
        return pltpu.make_async_copy(self.src, self.buf.at[net.s, net.f], self.sems.at[0])

    def one(self, k, came=False):
        net = self.net
        f = (net.f - k + net.n_f) % net.n_f if came else net.f
        place = self.buf.at[net.s, f]
        return put(
            place if came else self.src,
            place,
            self.sems.at[2 * k - 1],
            self.sems.at[2 * k],
            fsdp=(net.f + k) % net.n_f,
        )

    def two(self, k, came=False):
        net = self.net
        place = self.buf.at[(net.s - k + net.n_s) % net.n_s if came else net.s]
        at = 2 * (net.n_f - 1) + 2 * k - 1
        return put(place, place, self.sems.at[at], self.sems.at[at + 1], seq=(net.s + k) % net.n_s)

    def start(self):
        self.own().start()
        for k in range(1, self.net.n_f):
            self.one(k).start()

    def middle(self):
        self.own().wait()
        for k in range(1, self.net.n_f):
            self.one(k, came=True).wait_recv()
            self.one(k).wait_send()
        for k in range(1, self.net.n_s):
            self.two(k).start()

    def finish(self):
        for k in range(1, self.net.n_s):
            self.two(k, came=True).wait_recv()
            self.two(k).wait_send()

    def unpack(self, out, width):
        net = self.net
        per = 128 // width
        for tile in range(net.n_f * net.n_s // per):
            total = None
            for j in range(per):
                f, s = divmod(tile * per + j, net.n_s)
                piece = self.buf[s, f]
                if j:
                    piece = pltpu.roll(piece, j * width, axis=1)
                total = piece if total is None else total + piece
            out[:, tile * 128 : (tile + 1) * 128] = total


def rotary(values, cosine, sine):
    columns = values.shape[1]
    half = ROT // 2
    times = columns // 128

    def wide(table):
        return table if times == 1 else jnp.concatenate([table] * times, axis=1)

    lane = lax.broadcasted_iota(jnp.int32, values.shape, 1)
    other = jnp.where(
        lane % HEAD < half, pltpu.roll(values, columns - half, axis=1), pltpu.roll(values, half, axis=1)
    )
    return values * wide(cosine) + other * wide(sine)


def rotary_tables(length):
    half = ROT // 2
    freqs = np.float32(10000.0) ** (-np.arange(half, dtype=np.float32) * np.float32(2.0 / ROT))
    angles = np.arange(length, dtype=np.float32)[:, None] * freqs[None, :].astype(np.float32)
    cosine, sine = np.cos(angles), np.sin(angles)
    rest = np.zeros((length, HEAD - ROT), np.float32)
    keep = np.concatenate([cosine, cosine, rest + 1], 1)
    swap = np.concatenate([-sine, sine, rest], 1)
    return [np.tile(t, (1, 128 // HEAD)).astype(np.float32) for t in (keep, swap)]


def normalize(values):
    center = values - jnp.mean(values, -1, keepdims=True)
    inverse = lax.rsqrt(jnp.mean(center * center, -1, keepdims=True) + EPSILON)
    return center * inverse, inverse


class Copies:
    def __init__(self, sems):
        self.sems, self.all, self.open = sems, [], []

    def start(self, src, dst):
        copy = pltpu.make_async_copy(src, dst, self.sems.at[len(self.all)])
        copy.start()
        self.all.append(copy)
        self.open.append(copy)
        return copy

    def wait(self, *copies):
        for copy in copies or list(self.open):
            copy.wait()
            self.open = [c for c in self.open if c is not copy]


def columns_of(ref, depth):
    half_rows = ref.shape[0] // 2

    def part(f, half):
        span = aligned(f * depth, depth)
        if half is None:
            return ref.at[:, span]
        return ref.at[pl.ds(half * half_rows, half_rows), span]

    return part


def rows_of(ref, chunk):
    return lambda s: ref.at[aligned(s * chunk, chunk)]


class Fold:
    def __init__(self, net, tile, total, mate_in, coming, mate_out, out, mate_send, mate_recv, send, recv):
        self.net, self.tile, self.total = net, tile, total
        self.mate_in, self.coming, self.mate_out, self.out = mate_in, coming, mate_out, out
        self.mate_send, self.mate_recv, self.send, self.recv = mate_send, mate_recv, send, recv
        self.chunk = total.shape[0]
        self.pieces = recv.shape[1]
        self.rows = self.chunk // self.pieces

    @staticmethod
    def shared(chunk, width):
        return [pltpu.VMEM((2 * chunk, TILE), F32), pltpu.VMEM((chunk, width), F32)]

    @staticmethod
    def buffers(n_s, chunk, width):
        n_l = n_s // 2
        return [
            pltpu.VMEM((n_l, chunk, width), BF),
            pltpu.VMEM((n_l + 1, chunk, width), BF),
            pltpu.VMEM((3, chunk, width), BF),
            pltpu.VMEM((n_l, chunk, width), BF),
        ]

    @staticmethod
    def sems(n_s, pieces=4):
        n_l = n_s // 2
        return [
            pltpu.SemaphoreType.DMA((3, pieces)),
            pltpu.SemaphoreType.DMA((n_l, pieces)),
            pltpu.SemaphoreType.DMA((n_l, pieces)),
            pltpu.SemaphoreType.DMA((n_l + 1, pieces)),
        ]

    def place(self, other):
        return (other >= 0) & (other < self.net.n_l)

    def fed(self, side):
        return self.place(self.net.z + 1 - 2 * side)

    def span(self, piece):
        return aligned(piece * self.rows, self.rows)

    def each_piece(self, act):
        pl.loop(0, self.pieces)(act)

    def to_mate(self, target, slot, piece):
        span = self.span(piece)
        return put(
            self.mate_out.at[slot, span],
            self.mate_in.at[target, span],
            self.mate_send.at[slot, piece],
            self.mate_recv.at[target, piece],
            seq=self.net.mate,
        )

    def onward(self, target, side, hop, piece):
        span = self.span(piece)
        slot = target + (self.net.n_l - target) * (1 - side) * (1 // hop)
        return put(
            self.out.at[target, span],
            self.coming.at[slot, span],
            self.send.at[target, piece],
            self.recv.at[slot, piece],
            seq=self.net.s + 4 * side - 2,
        )

    def came(self, slot, piece):
        place = self.coming.at[slot, self.span(piece)]
        put(place, place, self.send.at[0, 0], self.recv.at[slot, piece], seq=self.net.mate).wait_recv()

    def mate_sent(self, slot):
        self.each_piece(lambda piece: self.to_mate(self.net.z, slot, piece).wait_send())

    def begin_one(self, target, slot, produce):
        mine = aligned(self.net.c * self.chunk, self.chunk)
        theirs = aligned((1 - self.net.c) * self.chunk, self.chunk)

        def write(cols, value):
            self.tile[...] = value
            self.out[target, :, cols] = self.tile[mine, :].astype(BF)
            self.mate_out[slot, :, cols] = self.tile[theirs, :].astype(BF)

        produce(target, write)
        self.each_piece(lambda piece: self.to_mate(target, slot, piece).start())

    def leave(self, target, side, hop):
        @pl.when((hop > 0) & jnp.logical_not(self.fed(side)))
        def _():
            self.each_piece(lambda piece: self.pass_piece(target, side, hop, piece, False))

    def begin(self, produce, between=None):
        net = self.net

        @pl.loop(0, net.n_l)
        def _(j):
            hop = net.n_l - 1 - j

            def act(target, side):
                @pl.when((hop > 0) | (side == 0))
                def _():
                    @pl.when((hop > 0) & self.place(target + 2 * side - 1))
                    def _():
                        self.mate_sent(side)

                    self.begin_one(target, side + (2 - side) * (1 // (hop + 1)), produce)
                    self.leave(target, side, hop)

            net.sides(hop, act)
            if between is not None:
                pl.when(j == 1)(between)

    def pass_piece(self, target, side, hop, piece, fed):
        self.to_mate(target, 0, piece).wait_recv()
        span = self.span(piece)
        value = self.out[target, span, :].astype(F32) + self.mate_in[target, span, :].astype(F32)
        if fed:
            self.came(target, piece)
            value = value + self.coming[target, span, :].astype(F32)
        self.out[target, span, :] = value.astype(BF)
        self.onward(target, side, hop, piece).start()

    def open_total(self):
        net = self.net

        @self.each_piece
        def _(piece):
            self.to_mate(net.z, 0, piece).wait_recv()
            span = self.span(piece)
            self.total[span, :] = self.out[net.z, span, :].astype(F32) + self.mate_in[net.z, span, :].astype(F32)

    def wave(self, at, near=False, between=None):
        net = self.net
        above = at if near else net.n_l - at

        @pl.loop(0, 2)
        def _(turn):
            side = (1 - (2 * net.z) // net.n_l + turn) % 2
            target = net.n_l - 1 - above + (2 * above - net.n_l + 1) * side
            hop = (target - net.z) * (2 * side - 1)

            @self.each_piece
            def _(piece):
                span = self.span(piece)

                @pl.when(self.fed(side) & (hop > 0))
                def _():
                    self.pass_piece(target, side, hop, piece, True)

                @pl.when(self.fed(side) & (hop == 0))
                def _():
                    slot = net.z + (net.n_l - net.z) * (1 - side)
                    self.came(slot, piece)
                    self.total[span, :] = self.total[span, :] + self.coming[slot, span, :].astype(F32)

                if between is not None:
                    between(((at - 1) * 2 + turn) * self.pieces + piece)

    def finish(self):
        net = self.net
        self.mate_sent(2)
        for side in range(2):
            pl.when(self.place(net.z + 2 * side - 1))(functools.partial(self.mate_sent, side))

        @pl.loop(1, net.n_l)
        def _(hop):
            net.sides(
                hop,
                lambda target, side: self.each_piece(
                    lambda piece: self.onward(target, side, hop, piece).wait_send()
                ),
            )


class GridSum:
    def __init__(self, net, stage, came, sems):
        self.net, self.stage, self.came, self.sems = net, stage, came, sems
        self.half = stage.shape[1] // 2
        self.rows = next(r for r in (176, 128, 96, 64, 32, 16) if self.half % r == 0)
        self.cols = range(1, net.tall)
        self.along = range(1, net.wide)
        self.bases = self.layout(net.n_f)

    @staticmethod
    def layout(n_f):
        tall = 2 if n_f % 2 == 0 else 1
        wide = n_f // tall
        sizes = [(wide - 1) * tall, (tall - 1) * wide, tall - 1, wide - 1]
        return [sum(sizes[:at]) for at in range(5)]

    @staticmethod
    def scratch(n_f, rows, columns):
        count = GridSum.layout(n_f)[4]
        return [
            pltpu.VMEM((n_f, rows, columns), BF),
            pltpu.VMEM((count, rows // 2, columns), BF),
            pltpu.SemaphoreType.DMA((2, count + GridEnd.count(n_f))),
        ]

    def slot(self, kind, i, j):
        base = self.bases[kind]
        return base + [(j - 1) * self.net.tall + i, (i - 1) * self.net.wide + j, i - 1, j - 1][kind]

    def rank(self, i, j):
        net = self.net
        return ((net.a + i) % net.tall) * net.wide + (net.b + j) % net.wide

    def owner(self, at):
        return self.rank(at // self.net.wide, at % self.net.wide)

    def copy(self, kind, i, j):
        half = kind % 2
        along = kind in (0, 3)
        slot = self.slot(kind, i, j)
        at = i * self.net.wide + j
        return put(
            self.stage.at[at, pl.ds(half * self.half, self.half)],
            self.came.at[slot],
            self.sems.at[0, slot],
            self.sems.at[1, slot],
            fsdp=self.rank(0, j) if along else self.rank(i, 0),
        )

    def first(self, at):
        i, j = at // self.net.wide, at % self.net.wide

        @pl.when(j > 0)
        def _():
            self.copy(0, i, j).start()

        @pl.when(i > 0)
        def _():
            self.copy(1, i, j).start()

    def gather(self, half, at, slots, write):
        @pl.loop(0, self.half // self.rows)
        def _(step):
            span = aligned(half * self.half + step * self.rows, self.rows, 16)
            value = self.stage[at, span, :].astype(F32)
            for slot in slots:
                value = value + self.came[slot, aligned(step * self.rows, self.rows, 16), :].astype(F32)
            write(span, value)

    def wait(self, *copies):
        for kind, i, j in copies:
            self.copy(kind, i, j).wait_recv()
        return [self.slot(*copy) for copy in copies]

    def second(self):
        def keep(at):
            def write(span, value):
                self.stage[at, span, :] = value.astype(BF)

            return write

        for i in self.cols:
            at = i * self.net.wide
            self.gather(0, at, self.wait(*[(0, i, j) for j in self.along]), keep(at))
            self.copy(2, i, 0).start()
        for j in self.along:
            self.gather(1, j, self.wait(*[(1, i, j) for i in self.cols]), keep(j))
            self.copy(3, 0, j).start()

    def sum_first(self):
        def keep(at):
            def write(span, value):
                self.stage[at, span, :] = value.astype(BF)

            return write

        for i in range(self.net.tall):
            at = i * self.net.wide
            self.gather(0, at, self.wait(*[(0, i, j) for j in self.along]), keep(at))
        for j in range(self.net.wide):
            self.gather(1, j, self.wait(*[(1, i, j) for i in self.cols]), keep(j))

    def hand_on(self, out):
        net = self.net
        shards = [(0, 0), (0, 1), *[(i * net.wide, 0) for i in self.cols], *[(j, 1) for j in self.along]]
        return [
            pltpu.make_async_copy(
                self.stage.at[at, pl.ds(half * self.half, self.half)], out.at[k], self.sems.at[0, self.bases[4] + k]
            )
            for k, (at, half) in enumerate(shards)
        ]

    def last(self, out):
        def write(span, value):
            out[span, :] = value

        self.gather(
            0, 0, self.wait(*[(0, 0, j) for j in self.along], *[(2, i, 0) for i in self.cols]), write
        )
        self.gather(
            1, 0, self.wait(*[(1, i, 0) for i in self.cols], *[(3, 0, j) for j in self.along]), write
        )

    def finish_first(self):
        for i in range(self.net.tall):
            for j in range(self.net.wide):
                if j:
                    self.copy(0, i, j).wait_send()
                if i:
                    self.copy(1, i, j).wait_send()

    def finish(self):
        self.finish_first()
        for i in self.cols:
            self.copy(2, i, 0).wait_send()
        for j in self.along:
            self.copy(3, 0, j).wait_send()


class GridEnd:
    def __init__(self, net, sums, came, sems):
        self.net, self.sums, self.came, self.sems = net, sums, came, sems

    @staticmethod
    def count(n_f):
        tall = 2 if n_f % 2 == 0 else 1
        return tall + n_f // tall

    @staticmethod
    def scratch(n_f, rows, columns):
        count = GridEnd.count(n_f)
        return [
            pltpu.VMEM((count, rows // 2, columns), BF),
            pltpu.VMEM((count - 2, rows // 2, columns), BF),
            pltpu.SemaphoreType.DMA((2, count - 2)),
        ]

    def copies(self):
        net = self.net
        f = [((net.a + i) % net.tall) * net.wide + net.b for i in range(1, net.tall)]
        f += [net.a * net.wide + (net.b + j) % net.wide for j in range(1, net.wide)]
        return [
            put(self.sums.at[2 + k], self.came.at[k], self.sems.at[0, k], self.sems.at[1, k], fsdp=to)
            for k, to in enumerate(f)
        ]

    def start(self):
        for copy in self.copies():
            copy.start()

    def last(self, out):
        for copy in self.copies():
            copy.wait()
        half = self.sums.shape[1]
        rows = next(r for r in (176, 128, 96, 64, 32, 16) if half % r == 0)
        down = range(self.net.tall - 1)
        along = range(self.net.tall - 1, self.net.tall + self.net.wide - 2)
        for at, slots in enumerate((down, along)):

            @pl.loop(0, half // rows)
            def _(step):
                span = aligned(step * rows, rows, 16)
                value = self.sums[at, span, :].astype(F32)
                for slot in slots:
                    value = value + self.came[slot, span, :].astype(F32)
                out[aligned(at * half + step * rows, rows, 16), :] = value


class PacketSum:
    def __init__(self, net, out, seq_in, total, fsdp_in, sems):
        self.net, self.out, self.seq_in, self.total, self.fsdp_in, self.sems = net, out, seq_in, total, fsdp_in, sems

    @staticmethod
    def scratch(n_f, n_s):
        return [
            pltpu.VMEM((n_s, n_f, SMALL, 128), F32),
            pltpu.VMEM((n_s, n_f, SMALL, 128), F32),
            pltpu.VMEM((n_f, SMALL, 128), F32),
            pltpu.VMEM((n_f, SMALL, 128), F32),
            pltpu.SemaphoreType.DMA((2 * (n_f + n_s),)),
        ]

    def one(self, k):
        to = (self.net.s + k) % self.net.n_s
        return put(self.out.at[to], self.seq_in.at[k], self.sems.at[2 * k], self.sems.at[2 * k + 1], seq=to)

    def two(self, k):
        to = (self.net.f + k) % self.net.n_f
        at = 2 * (self.net.n_s + k)
        return put(self.total.at[to], self.fsdp_in.at[k], self.sems.at[at], self.sems.at[at + 1], fsdp=to)

    def start(self, terms, width):
        net = self.net
        per = 128 // width
        for tile in range(net.n_f * net.n_s // per):
            value = terms[:, tile * 128 : (tile + 1) * 128]
            for j in range(per):
                f, s = divmod(tile * per + j, net.n_s)
                self.out[s, f] = pltpu.roll(value, 128 - j * width, axis=1) if j else value
        for k in range(1, net.n_s):
            self.one(k).start()

    def middle(self):
        net = self.net
        total = self.out[net.s]
        for k in range(1, net.n_s):
            self.one(k).wait()
            total = total + self.seq_in[k]
        self.total[...] = total
        for k in range(1, net.n_f):
            self.two(k).start()

    def finish(self, result):
        net = self.net
        total = self.total[net.f]
        for k in range(1, net.n_f):
            self.two(k).wait()
            total = total + self.fsdp_in[k]
        result[...] = total


def norm_backward(rows, source, grad, gain, terms, at, write):
    terms[at : at + 2, :] = jnp.zeros((2, terms.shape[1]), F32)

    @pl.loop(0, rows // 32)
    def _(i):
        span = aligned(i * 32, 32)
        scaled, inverse = normalize(source[span, :].astype(F32))
        value = grad[span, :]
        upstream = value * gain
        inner = jnp.mean(upstream, -1, keepdims=True)
        cross = jnp.mean(upstream * scaled, -1, keepdims=True)
        terms[at : at + 1, :] = terms[at : at + 1, :] + jnp.sum(value * scaled, 0, keepdims=True)
        terms[at + 1 : at + 2, :] = terms[at + 1 : at + 2, :] + jnp.sum(value, 0, keepdims=True)
        write(i, span, inverse * (upstream - inner - scaled * cross))


def layer_kernel(
    tok,
    gain_one,
    shift_one,
    gain_two,
    shift_two,
    bias,
    wq_own,
    wo_own,
    wg_own,
    wu_own,
    wd_own,
    gout_own,
    cosine,
    sine,
    q_o,
    k_o,
    kt_o,
    v_o,
    att_o,
    lse_o,
    n1_o,
    gains_o,
    wq_o,
    wo_o,
    dm_o,
    datt_o,
    dmid_o,
    top_o,
    terms_o,
    gate_o,
    up_o,
    down_o,
    rows,
    gout,
    wq,
    wo,
    wg,
    wu,
    wd,
    q,
    k,
    kt,
    v,
    vt,
    ot,
    att,
    hidden,
    dgate,
    dup,
    mid,
    low,
    packet,
    packets,
    tiles,
    total,
    *rest,
):
    net = Net()
    chunk, width = tok.shape
    length = chunk * net.n_s
    depth = wq_own.shape[1]
    columns = wq_own.shape[2]
    heads = columns // HEAD
    pair = 2 * chunk
    buffers, rest = rest[:4], rest[4:]
    folds = []
    for _ in range(3):
        folds.append(Fold(net, tiles, total, *buffers, *rest[:4]))
        rest = rest[4:]
    att_fold, normed_fold, top_fold = folds
    line_sems = [rest[at : at + 3] for at in (0, 3, 6, 9)]
    rest = rest[12:]
    spread_sems, rest = rest[:5], rest[5:]
    gate_sum, up_sum, down_sum = [GridSum(net, *rest[at : at + 3]) for at in (0, 3, 6)]
    sums = (down_sum, gate_sum, up_sum)
    pk_sems, copy_sems, n1_sems = rest[9:]
    copies = Copies(copy_sems)
    n1 = att_fold.mate_out

    packet[...] = jnp.zeros(packet.shape, F32)
    own = gain_one.shape[1]
    for at, part in enumerate((gain_one, shift_one, gain_two, shift_two)):
        packet[at : at + 1, 0:own] = part[...].astype(F32)
    packet[4:7, 0:own] = bias[...].astype(F32)
    net.barrier()

    def wq_part(f, half):
        if half is None:
            return wq.at[:, aligned(f * depth, depth), :]
        return wq.at[:, aligned(f * depth + half * (depth // 2), depth // 2), :]

    spread_q = Spread(net, wq_own, wq_part, spread_sems[0])
    spread_o, spread_g, spread_u, spread_d = [
        Spread(net, own, columns_of(full, depth), sems)
        for own, full, sems in zip((wo_own, wg_own, wu_own, wd_own), (wo, wg, wu, wd), spread_sems[1:])
    ]
    pk = Packets(net, packet, packets, pk_sems)
    line = Line(net, tok, rows_of(rows, chunk), *line_sems[0])
    gout_line = Line(net, gout_own, rows_of(gout, chunk), *line_sems[1])
    n2_line = Line(net, low, rows_of(rows, chunk), *line_sems[2])
    dm_line = Line(net, low, rows_of(dm_o, chunk), *line_sems[3])

    def pairs(which, hop):
        net.sides(hop, lambda other, side: which.pair(other))

    def blocks(hop, act):
        def once(other, side):
            @pl.when((hop > 0) | (side == 0))
            def _():
                act(other, side)

        net.sides(hop, once)

    pk.start()
    line.start()
    spread_q.start()
    pk.middle()
    pk.finish()
    pk.unpack(gains_o, width // (net.n_f * net.n_s))

    def project_block(other, side):
        span = aligned(other * pair, pair)
        gain, shift = gains_o[0:1, :], gains_o[1:2, :]

        for part in range(2):

            @pl.loop(0, chunk // 32)
            def _(i):
                at = aligned((2 * other + part) * chunk + i * 32, 32)
                scaled, _ = normalize(rows[at, :].astype(F32))
                n1[part, aligned(i * 32, 32), :] = (scaled * gain + shift).astype(BF)

        keeps = [
            pltpu.make_async_copy(
                n1.at[part], n1_o.at[aligned((2 * other + part) * chunk, chunk)], n1_sems.at[part]
            )
            for part in range(2)
        ]
        for copy in keeps:
            copy.start()
        left = n1[0:2].reshape(pair, width)
        cols = aligned(net.s * columns, columns)
        tables = cosine[span, :], sine[span, :]
        for kind in range(3):
            value = dot(left, wq[kind]) + gains_o[4 + kind : 5 + kind, cols]
            if kind == 0:
                q[span, :] = rotary(value, *tables).astype(BF)
            elif kind == 1:
                value = rotary(value, *tables)
                k[span, :] = value.astype(BF)
                kt[...] = value.T.astype(BF)
            else:
                v[...] = value.astype(BF)
                vt[:, span] = value.T.astype(BF)
        for copy in (
            pltpu.make_async_copy(kt, kt_o.at[:, span], n1_sems.at[2]),
            pltpu.make_async_copy(v, v_o.at[span], n1_sems.at[3]),
        ):
            copy.start()
            keeps.append(copy)
        for copy in keeps:
            copy.wait()

    line.here()
    for hop in range(1, net.n_l - 1):
        line.step(hop)
        if hop == 1:
            spread_q.relay()
        pairs(line, hop)
    spread_o.start()
    spread_q.finish()
    spread_g.start()
    pl.loop(0, net.n_l - 1)(lambda hop: blocks(hop, project_block))
    spread_o.relay()
    spread_u.start()
    line.step(net.n_l - 1)
    gout_line.start()
    pairs(line, net.n_l - 1)
    blocks(net.n_l - 1, project_block)
    spread_d.start()
    q_copy = copies.start(q, q_o)
    for pair_of in ((wq, wq_o), (k, k_o)):
        copies.start(*pair_of)
    spread_o.finish()
    line.finish()

    def attend(i):
        lo, hi = i * pair, (i + 1) * pair

        @pl.loop(0, heads)
        def _(head):
            lane = lax.broadcasted_iota(jnp.int32, (1, columns), 1)
            here = jnp.where(lane // HEAD == head, HEAD**-0.5, 0.0).astype(BF)
            visible = lax.broadcasted_iota(jnp.int32, (pair, pair), 0) <= lax.broadcasted_iota(
                jnp.int32, (pair, pair), 1
            )
            head_rows = aligned(head * HEAD, HEAD)
            query = q[lo:hi, :] * here
            near = jnp.where(visible, dot_nt(k[lo:hi, :], query), NEG_LARGE)
            highest = jnp.max(near, 0, keepdims=True)
            if i:
                far = dot_nt(k[0:lo, :], query)
                highest = jnp.maximum(highest, jnp.max(far, 0, keepdims=True))
            near = jnp.exp(near - highest)
            sum_of = jnp.sum(near, 0, keepdims=True)
            out = dot(vt[head_rows, lo:hi], near.astype(BF))
            if i:
                far = jnp.exp(far - highest)
                sum_of = sum_of + jnp.sum(far, 0, keepdims=True)
                out = out + dot(vt[head_rows, 0:lo], far.astype(BF))
            ot[head_rows, :] = out / sum_of
            lse_o[pl.ds(head, 1), lo:hi] = highest + jnp.log(sum_of)

        att[lo:hi, :] = ot[...].T.astype(BF)

    def produce_attended(place, write):
        for i in range(net.n_l):
            pl.when(place == i)(functools.partial(attend, i))
        left = att[aligned(place * pair, pair), :]

        @pl.loop(0, width // TILE)
        def _(j):
            cols = aligned(j * TILE, TILE)
            write(cols, dot(left, wo[:, cols]))

    def relays():
        gout_line.step(1)
        spread_g.relay()

    att_fold.begin(produce_attended, relays)
    copies.start(att, att_o)
    copies.start(wo, wo_o)
    att_fold.open_total()
    for at in range(1, net.n_l):
        att_fold.wave(at)
        if at + 1 < net.n_l:
            gout_line.step(at + 1)
        if at == 1:
            spread_u.relay()
        if at == min(2, net.n_l - 1):
            spread_d.relay()
    gain_two, shift_two = gains_o[2:3, :], gains_o[3:4, :]

    @pl.loop(0, chunk // 32)
    def _(i):
        span = aligned(i * 32, 32)
        value = rows[aligned(net.s * chunk + i * 32, 32), :].astype(F32) + total[span, :]
        mid[span, :] = value
        scaled, _ = normalize(value)
        low[span, :] = (scaled * gain_two + shift_two).astype(BF)

    n2_line.start()
    att_fold.finish()
    gout_line.here()
    pl.loop(1, net.n_l)(lambda hop: pairs(gout_line, hop))

    def forward_block(other):
        span = aligned(other * pair, pair)
        right = rows[span, :]
        half = hidden.shape[0] // 2

        @pl.loop(0, 2)
        def _(part):
            units = aligned(part * half, half, 16)
            gate = dot_nt(wg[units, :], right)
            up = dot_nt(wu[units, :], right)
            back = dot_nt(wd[units, :], gout[span, :])
            sigma = jax.nn.sigmoid(gate)
            active = gate * sigma
            hidden[units, span] = (active * up).astype(BF)
            dgate[units, span] = (back * up * (sigma * (1.0 + gate * (1.0 - sigma)))).astype(BF)
            dup[units, span] = (back * active).astype(BF)

    def produce_normed(place, write):
        span = aligned(place * pair, pair)
        left, right = dgate[:, span].T, dup[:, span].T

        @pl.loop(0, width // TILE)
        def _(j):
            cols = aligned(j * TILE, TILE)
            write(cols, dot(left, wg[:, cols]) + dot(right, wu[:, cols]))

    def begin_normed(other, side, hop):
        @pl.when(hop > 1)
        def _():
            normed_fold.mate_sent(side)

        normed_fold.begin_one(other, side + (2 - side) * (1 // (hop + 1)), produce_normed)

    def forward_blocks(hop):
        def act(other, side):
            forward_block(other)

            @pl.when(jnp.logical_not(normed_fold.fed(side)))
            def _():
                begin_normed(other, side, hop)
                normed_fold.leave(other, side, hop)

        net.sides(hop, act)

    def begin_fed(hop):
        def act(other, side):
            @pl.when((hop == 0) | normed_fold.fed(side))
            def _():
                begin_normed(other, side, hop)

        blocks(hop, act)

    n2_line.here()
    for spread in (spread_g, spread_u, spread_d):
        spread.finish()
    forward_block(net.z)

    @pl.loop(1, net.n_l)
    def _(hop):
        n2_line.step(hop)
        pairs(n2_line, hop)
        forward_blocks(hop)
        begin_fed(hop - 1)

    begin_fed(net.n_l - 1)
    normed_fold.open_total()

    def weight_terms(task):
        at, kind = net.n_f - 1 - task // 3, task % 3
        cols = aligned(gate_sum.owner(at) * depth, depth)
        for way, (grid_sum, left, right) in enumerate(
            ((down_sum, hidden, gout), (gate_sum, dgate, rows), (up_sum, dup, rows))
        ):

            @pl.when(kind == way)
            def _():
                half = left.shape[0] // 2

                @pl.loop(0, 2)
                def _(part):
                    units = aligned(part * half, half, 16)
                    grid_sum.stage[at, units, :] = dot(left[units, :], right[:, cols]).astype(BF)

                grid_sum.first(at)

    tasks = 3 * net.n_f
    slots = 2 * normed_fold.pieces * (net.n_l - 1)
    each = -(-tasks // slots)

    def between(slot):
        @pl.loop(0, each)
        def _(i):
            pl.when(slot * each + i < tasks)(lambda: weight_terms(slot * each + i))

    for at in range(1, net.n_l):
        normed_fold.wave(at, near=True, between=between)
    n2_line.finish()

    def write_middle(i, span, value):
        value = value + gout[aligned(net.s * chunk + i * 32, 32), :].astype(F32)
        dmid_o[span, :] = value
        low[span, :] = value.astype(BF)

    terms_o[...] = jnp.zeros(terms_o.shape, F32)
    norm_backward(chunk, mid, total, gain_two, terms_o, 2, write_middle)
    dm_line.start()
    normed_fold.finish()

    def produce_top(place, write):
        left = hidden[:, aligned(place * pair, pair)].T

        @pl.loop(0, width // TILE)
        def _(j):
            cols = aligned(j * TILE, TILE)
            write(cols, dot(left, wd[:, cols]))

    copies.wait(q_copy)
    datt = q

    def back_block(other, side):
        span = aligned(other * pair, pair)
        copy = pltpu.make_async_copy(dm_o.at[span], rows.at[span], n1_sems.at[0])
        copy.start()
        copy.wait()
        datt[span, :] = dot_nt(rows[span, :], wo[...]).astype(BF)

    dm_line.here()
    dm_line.step(1)
    top_fold.begin(produce_top)
    back_block(net.z, 0)
    top_fold.open_total()
    for at in range(1, net.n_l):
        if at + 1 < net.n_l:
            dm_line.step(at + 1)
        top_fold.wave(at)
        pairs(dm_line, at)
        net.sides(at, back_block)
    copies.start(datt, datt_o)

    @pl.loop(0, chunk // 32)
    def _(i):
        span = aligned(i * 32, 32)
        top_fold.out[net.z, span, :] = (mid[span, :] + total[span, :]).astype(BF)

    copies.start(top_fold.out.at[net.z], top_o)
    top_fold.finish()
    gout_line.finish()
    dm_line.finish()
    hands = []
    for grid_sum, out in zip(sums, (down_o, gate_o, up_o)):
        grid_sum.sum_first()
        hands.extend(grid_sum.hand_on(out))
        for copy in grid_sum.hand_on(out):
            copy.start()
    for grid_sum in sums:
        grid_sum.finish_first()
    for copy in hands:
        copy.wait()
    copies.wait()


def layer_part(tokens, norms, wq, wo, wg, wu, wd, gout, tables):
    chunk, width = tokens.shape
    n_f, n_s = lax.axis_size("fsdp"), lax.axis_size("seq")
    length = chunk * n_s
    depth, columns = wq.shape[1:]
    units = wg.shape[0]
    shape = jax.ShapeDtypeStruct
    wide, head, turned, weight = (length, width), (length, columns), (units, length), (units, width)
    return pl.pallas_call(
        layer_kernel,
        name="layer",
        out_shape=[
            shape(head, BF),
            shape(head, BF),
            shape((columns, length), BF),
            shape(head, BF),
            shape(head, BF),
            shape((8, length), F32),
            shape(wide, BF),
            shape((SMALL, width), F32),
            shape((3, width, columns), BF),
            shape((columns, width), BF),
            shape(wide, BF),
            shape(head, BF),
            shape((chunk, width), F32),
            shape((chunk, width), BF),
            shape((SMALL, width), F32),
            *[shape((GridEnd.count(n_f), units // 2, depth), BF)] * 3,
        ],
        in_specs=[ANY, *[VMEM] * 5, *[ANY] * 6, VMEM, VMEM],
        out_specs=[*[ANY] * 5, VMEM, ANY, VMEM, *[ANY] * 4, VMEM, ANY, VMEM, *[ANY] * 3],
        scratch_shapes=[
            pltpu.VMEM(wide, BF),
            pltpu.VMEM(wide, BF),
            pltpu.VMEM((3, width, columns), BF),
            pltpu.VMEM((columns, width), BF),
            *[pltpu.VMEM(weight, BF)] * 3,
            pltpu.VMEM(head, BF),
            pltpu.VMEM(head, BF),
            pltpu.VMEM((columns, 2 * chunk), BF),
            pltpu.VMEM((2 * chunk, columns), BF),
            pltpu.VMEM((columns, length), BF),
            pltpu.VMEM((columns, 2 * chunk), F32),
            pltpu.VMEM(head, BF),
            *[pltpu.VMEM(turned, BF)] * 3,
            pltpu.VMEM((chunk, width), F32),
            pltpu.VMEM((chunk, width), BF),
            pltpu.VMEM((SMALL, 128), F32),
            pltpu.VMEM((n_s, n_f, SMALL, 128), F32),
            *Fold.shared(chunk, width),
            *Fold.buffers(n_s, chunk, width),
            *Fold.sems(n_s) * 3,
            *Line.sems(n_s) * 4,
            *[pltpu.SemaphoreType.DMA((Spread.count(n_f),))] * 5,
            *GridSum.scratch(n_f, units, depth) * 3,
            pltpu.SemaphoreType.DMA((Packets.count(n_f, n_s),)),
            pltpu.SemaphoreType.DMA((8,)),
            pltpu.SemaphoreType.DMA((4,)),
        ],
        compiler_params=pltpu.CompilerParams(
            collective_id=1, has_side_effects=True, vmem_limit_bytes=VMEM_BYTES
        ),
        cost_estimate=pl.CostEstimate(
            flops=2 * length * width * (4 * columns + 9 * units),
            bytes_accessed=8 * length * width,
            transcendentals=length * (length * columns // HEAD + units),
        ),
    )(tokens, *norms, wq, wo, wg, wu, wd, gout, *tables)


def back_kernel(
    datt_in,
    q_in,
    k_in,
    kt_in,
    v_in,
    att_in,
    wq_in,
    n1_in,
    dm_in,
    down_in,
    gate_in,
    up_in,
    lse,
    tok,
    dmid,
    gains,
    terms_in,
    cosine,
    sine,
    gin_o,
    small_o,
    out_o,
    qkv_o,
    down_o,
    gate_o,
    up_o,
    datt,
    q,
    k,
    kt,
    v,
    att,
    wq,
    n1,
    dm,
    dk,
    dv,
    dqt,
    dproj,
    terms,
    tiles,
    total,
    *rest,
):
    net = Net()
    chunk, width = tok.shape
    length, columns = q_in.shape
    heads = columns // HEAD
    pair = 2 * chunk
    depth = width // net.n_f
    block = 256
    buffers, rest = rest[:4], rest[4:]
    fold_sems, rest = rest[:4], rest[4:]
    packet_scratch, rest = rest[:5], rest[5:]
    out_sum, qkv_sum = GridSum(net, *rest[:3]), GridSum(net, *rest[3:6])
    ends = [GridEnd(net, *rest[at : at + 3]) for at in (6, 9, 12)]
    copy_sems, column_sems = rest[15:]

    copies = Copies(copy_sems)
    loads = [
        copies.start(src, dst)
        for src, dst in (
            (datt_in, datt),
            (q_in, q),
            (k_in, k),
            (kt_in, kt),
            (v_in, v),
            (att_in, att),
            (wq_in, wq),
            (down_in, ends[0].sums),
            (gate_in, ends[1].sums),
            (up_in, ends[2].sums),
        )
    ]
    def load(at, way):
        src, dst = ((n1_in, n1), (dm_in, dm))[way]
        cols = aligned(qkv_sum.owner(at) * depth, depth)
        return pltpu.make_async_copy(src.at[:, cols], dst.at[at % 2], column_sems.at[way, at % 2])

    for at in range(net.n_f - 1, max(net.n_f - 3, -1), -1):
        for way in range(2):
            load(at, way).start()

    @pl.loop(0, length // block)
    def _(i):
        span = aligned(i * block, block)
        dk[span, :] = jnp.zeros((block, columns), F32)
        dv[span, :] = jnp.zeros((block, columns), F32)

    net.barrier()
    copies.wait(*loads[7:])
    for end in ends:
        end.start()
    copies.wait(*loads[:5])

    @pl.loop(0, heads)
    def _(head):
        lane = lax.broadcasted_iota(jnp.int32, (1, columns), 1)
        here = jnp.where(lane // HEAD == head, 1.0, 0.0).astype(BF)
        scale = HEAD**-0.5
        visible = lax.broadcasted_iota(jnp.int32, (block, block), 0) <= lax.broadcasted_iota(
            jnp.int32, (block, block), 1
        )
        head_rows = aligned(head * HEAD, HEAD)
        for i in range(length // block):
            lo, hi = i * block, (i + 1) * block
            query = q[lo:hi, :] * (here * scale)
            upstream = datt[lo:hi, :] * here
            logsum = lse[pl.ds(head, 1), lo:hi]

            def part(at, end, mask):
                probs = jnp.exp(dot_nt(k[at:end, :], query) - logsum)
                if mask:
                    probs = jnp.where(visible, probs, 0.0)
                grads = dot_nt(v[at:end, :], upstream)
                dv[at:end, :] = dv[at:end, :] + dot(probs.astype(BF), upstream)
                return probs, grads, jnp.sum(probs * grads, 0, keepdims=True)

            def scored(at, end, probs, grads, inner):
                scores = (probs * (grads - inner)).astype(BF)
                dk[at:end, :] = dk[at:end, :] + dot(scores, query)
                return dot(kt[head_rows, at:end], scores)

            near, near_grads, inner = part(lo, hi, True)
            if i:
                far, far_grads, more = part(0, lo, False)
                inner = inner + more
            out = scored(lo, hi, near, near_grads, inner)
            if i:
                out = out + scored(0, lo, far, far_grads, inner)
            dqt[head_rows, lo:hi] = out * scale

    terms[...] = terms_in[...]
    bias_cols = aligned(net.s * columns, columns)

    @pl.loop(0, length // block)
    def _(i):
        span = aligned(i * block, block)
        tables = cosine[span, :], -sine[span, :]
        parts = [
            rotary(dqt[:, span].T.astype(BF).astype(F32), *tables).astype(BF),
            rotary(dk[span, :].astype(BF).astype(F32), *tables).astype(BF),
            dv[span, :].astype(BF),
        ]
        for kind in range(3):
            dproj[kind, span, :] = parts[kind]
            row = slice(4 + kind, 5 + kind)
            terms[row, bias_cols] = terms[row, bias_cols] + jnp.sum(parts[kind].astype(F32), 0, keepdims=True)

    def weight_terms(task):
        at = net.n_f - 1 - task // 2

        def loaded(way):
            load(at, way).wait()

        def next_load(way):
            pl.when(at >= 2)(lambda: load(at - 2, way).start())

        @pl.when(task % 2 == 0)
        def _():
            loaded(0)
            left = n1[at % 2].T
            for kind in range(3):
                qkv_sum.stage[at, kind * depth : (kind + 1) * depth, :] = dot(left, dproj[kind]).astype(BF)
            next_load(0)
            qkv_sum.first(at)

        @pl.when(task % 2 == 1)
        def _():
            loaded(1)
            out_sum.stage[at] = dot_tn(att[...], dm[at % 2]).astype(BF)
            next_load(1)
            out_sum.first(at)

    def produce(place, write):
        span = aligned(place * pair, pair)

        @pl.loop(0, width // TILE)
        def _(j):
            cols = aligned(j * TILE, TILE)
            value = dot_nt(dproj[0, span, :], wq[0, cols, :])
            for kind in range(1, 3):
                value = value + dot_nt(dproj[kind, span, :], wq[kind, cols, :])
            write(cols, value)

    fold = Fold(net, tiles, total, *buffers, *fold_sems)
    copies.wait()
    fold.begin(produce)
    fold.open_total()
    tasks = 2 * net.n_f
    waves = max(net.n_l - 2, 1)
    each = -(-tasks // (2 * fold.pieces * waves))

    def between(slot):
        @pl.loop(0, each)
        def _(i):
            pl.when(slot * each + i < tasks)(lambda: weight_terms(slot * each + i))

    for at in range(1, waves + 1):
        fold.wave(at, between=between)
    for at in range(waves + 1, net.n_l):
        fold.wave(at)

    def write_input(i, span, value):
        gin_o[span, :] = value + dmid[span, :]

    norm_backward(chunk, tok, total, gains[0:1, :], terms, 0, write_input)
    packet_sum = PacketSum(net, *packet_scratch)
    packet_sum.start(terms, width // (net.n_f * net.n_s))
    for grid_sum in (qkv_sum, out_sum):
        grid_sum.second()
    packet_sum.middle()
    for end, out in zip(ends, (down_o, gate_o, up_o)):
        end.last(out)
    packet_sum.finish(small_o)
    fold.finish()
    for grid_sum, out in ((qkv_sum, qkv_o), (out_sum, out_o)):
        grid_sum.last(out)
        grid_sum.finish()


def back_part(datt, q, k, kt, v, att, wq, n1, dm, down, gate, up, lse, tokens, dmid, gains, terms, tables):
    chunk, width = tokens.shape
    n_f, n_s = lax.axis_size("fsdp"), lax.axis_size("seq")
    length, columns = q.shape
    depth = width // n_f
    units = 2 * gate.shape[1]
    shape = jax.ShapeDtypeStruct
    return pl.pallas_call(
        back_kernel,
        name="back",
        out_shape=[
            shape((chunk, width), F32),
            shape((SMALL, 128), F32),
            shape((columns, depth), F32),
            shape((3 * depth, columns), F32),
            *[shape((units, depth), F32)] * 3,
        ],
        in_specs=[ANY] * 12 + [VMEM] * 7,
        out_specs=[VMEM] * 7,
        scratch_shapes=[
            pltpu.VMEM((length, columns), BF),
            pltpu.VMEM((length, columns), BF),
            pltpu.VMEM((length, columns), BF),
            pltpu.VMEM((columns, length), BF),
            pltpu.VMEM((length, columns), BF),
            pltpu.VMEM((length, columns), BF),
            pltpu.VMEM((3, width, columns), BF),
            pltpu.VMEM((2, length, depth), BF),
            pltpu.VMEM((2, length, depth), BF),
            pltpu.VMEM((length, columns), F32),
            pltpu.VMEM((length, columns), F32),
            pltpu.VMEM((columns, length), F32),
            pltpu.VMEM((3, length, columns), BF),
            pltpu.VMEM((SMALL, width), F32),
            *Fold.shared(chunk, width),
            *Fold.buffers(n_s, chunk, width),
            *Fold.sems(n_s),
            *PacketSum.scratch(n_f, n_s),
            *GridSum.scratch(n_f, columns, depth),
            *GridSum.scratch(n_f, 3 * depth, columns),
            *GridEnd.scratch(n_f, units, depth) * 3,
            pltpu.SemaphoreType.DMA((10,)),
            pltpu.SemaphoreType.DMA((2, 2)),
        ],
        compiler_params=pltpu.CompilerParams(
            collective_id=3, has_side_effects=True, vmem_limit_bytes=VMEM_BYTES
        ),
        cost_estimate=pl.CostEstimate(
            flops=2 * length * columns * (8 * width + 5 * length),
            bytes_accessed=4 * length * width,
            transcendentals=length * length * columns // HEAD,
        ),
    )(datt, q, k, kt, v, att, wq, n1, dm, down, gate, up, lse, tokens, dmid, gains, terms, *tables)


def outputs_kernel(small, *refs):
    sources, sems = refs[:7], refs[-1]
    targets, parts = refs[7:14], refs[14:19]
    own = parts[0].shape[1]
    copies = [
        pltpu.make_async_copy(src, dst, sems.at[at]) for at, (src, dst) in enumerate(zip(sources, targets))
    ]
    for copy in copies:
        copy.start()
    for at in range(4):
        parts[at][...] = small[at : at + 1, 0:own]
    parts[4][...] = small[4:7, 0:own]
    for copy in copies:
        copy.wait()


def outputs_part(small, own, *arrays):
    shape = jax.ShapeDtypeStruct
    return pl.pallas_call(
        outputs_kernel,
        name="outputs",
        out_shape=[shape(v.shape, v.dtype) for v in arrays]
        + [shape((1, own), F32)] * 4
        + [shape((3, own), F32)],
        in_specs=[VMEM] + [ANY] * 7,
        out_specs=[ANY] * 7 + [VMEM] * 5,
        scratch_shapes=[pltpu.SemaphoreType.DMA((7,))],
    )(small, *arrays)


def per_device(
    tokens,
    gain_one,
    shift_one,
    w_qkv,
    b_qkv,
    w_out,
    gain_two,
    shift_two,
    w_gate,
    w_up,
    w_down,
    grad_output,
):
    length = tokens.shape[1] * lax.axis_size("seq")
    width = gain_one.shape[0]
    norms = [v[None] for v in (gain_one, shift_one, gain_two, shift_two)] + [b_qkv]
    tables = rotary_tables(length)
    q, k, kt, v, att, lse, n1, gains, wq, _, dm, datt, dmid, top, terms, gate, up, down = layer_part(
        tokens[0], norms, w_qkv.transpose(1, 0, 2), w_out, w_gate.T, w_up.T, w_down, grad_output[0], tables
    )
    grad_input, small, out, qkv, down, gate, up = back_part(
        datt, q, k, kt, v, att, wq, n1, dm, down, gate, up, lse, tokens[0], dmid, gains, terms, tables
    )

    top, grad_input, qkv, out, gate, up, down, one, shift, two, shift_to, bias = outputs_part(
        small, width, top, grad_input, qkv, out, gate, up, down
    )
    return (
        top[None],
        grad_input[None],
        one[0],
        shift[0],
        qkv.reshape(3, -1, qkv.shape[1]).transpose(1, 0, 2),
        bias,
        out,
        two[0],
        shift_to[0],
        gate.T,
        up.T,
        down,
    )


def solution(mesh):
    whole = P(("fsdp", "seq"))
    rows = P("fsdp", "seq", None)
    inner = P("seq", "fsdp")
    outer = P("fsdp", "seq")
    heads = P("fsdp", None, "seq")
    bias = P(None, ("fsdp", "seq"))
    return jax.shard_map(
        per_device,
        mesh=mesh,
        in_specs=(rows, whole, whole, heads, bias, inner, whole, whole, outer, outer, inner, rows),
        out_specs=(rows, rows, whole, whole, heads, bias, inner, whole, whole, outer, outer, inner),
        check_vma=False,
    )
```

```python
import functools

import jax
import jax.numpy as jnp
import numpy as np
from jax import lax
from jax.experimental import pallas as pl
from jax.experimental.pallas import tpu as pltpu
from jax.sharding import PartitionSpec as P

HEAD = 64
ROT = 16
EPSILON = 1e-05
NEG_LARGE = -1e30
MESH = pl.DeviceIdType.MESH
ANY = pl.BlockSpec(memory_space=pl.ANY)
VMEM = pl.BlockSpec(memory_space=pltpu.VMEM)
BF = jnp.bfloat16
F32 = jnp.float32
VMEM_BYTES = 60 * 2**20
TILE = 512
SMALL = 8


def put(src, dst, send, recv, **device):
    return pltpu.make_async_remote_copy(
        src_ref=src, dst_ref=dst, send_sem=send, recv_sem=recv, device_id=device, device_id_type=MESH
    )


def dot(left, right):
    return jnp.dot(left, right, preferred_element_type=F32)


def dot_nt(left, right):
    return lax.dot_general(left, right, (((1,), (1,)), ((), ())), preferred_element_type=F32)


def dot_tn(left, right):
    return lax.dot_general(left, right, (((0,), (0,)), ((), ())), preferred_element_type=F32)


def aligned(start, size, unit=None):
    return pl.ds(pl.multiple_of(start, unit or size), size)


class Net:
    def __init__(self):
        self.n_f, self.n_s = lax.axis_size("fsdp"), lax.axis_size("seq")
        self.tall = 2 if self.n_f % 2 == 0 else 1
        self.wide = self.n_f // self.tall
        self.n_l = self.n_s // 2
        self.f, self.s = lax.axis_index("fsdp"), lax.axis_index("seq")
        self.a, self.b = self.f // self.wide, self.f % self.wide
        self.z, self.c = self.s // 2, self.s % 2
        self.mate = self.s + 1 - 2 * self.c

    def barrier(self):
        sem = pltpu.get_barrier_semaphore()
        for k in range(1, self.n_f):
            pl.semaphore_signal(
                sem, inc=1, device_id={"fsdp": (self.f + k) % self.n_f}, device_id_type=MESH
            )
        for k in range(1, self.n_s):
            pl.semaphore_signal(
                sem, inc=1, device_id={"seq": (self.s + k) % self.n_s}, device_id_type=MESH
            )
        pl.semaphore_wait(sem, self.n_f + self.n_s - 2)

    def sides(self, hop, act):
        @pl.loop(0, 2)
        def _(side):
            other = self.z + (2 * side - 1) * hop

            @pl.when((other >= 0) & (other < self.n_l))
            def _():
                act(other, side)


class Spread:
    def __init__(self, net, src, part, sems):
        self.net, self.src, self.part, self.sems = net, src, part, sems
        self.rows = [j for j in range(1, net.wide)]
        self.cols = [i for i in range(1, net.tall)]

    @staticmethod
    def count(n_f):
        tall = 2 if n_f % 2 == 0 else 1
        wide = n_f // tall
        return 1 + 2 * (wide - 1) + 2 * (tall - 1) + 4 * (wide - 1) * (tall - 1)

    def at(self, kind, i, j):
        w, t = len(self.rows), len(self.cols)
        base = {
            "own": 0,
            "row": 1,
            "col": 1 + 2 * w,
            "half0": 1 + 2 * w + 2 * t,
            "half1": 1 + 2 * w + 2 * t + 2 * w * t,
        }[kind]
        if kind == "own":
            return self.sems.at[0]
        k = j - 1 if kind == "row" else i - 1 if kind == "col" else (i - 1) * w + j - 1
        return self.sems.at[base + 2 * k], self.sems.at[base + 2 * k + 1]

    def rank(self, i, j):
        net = self.net
        return ((net.a + i) % net.tall) * net.wide + (net.b + j) % net.wide

    def back(self, i, j):
        net = self.net
        return ((net.a - i + net.tall) % net.tall) * net.wide + (net.b - j + net.wide) % net.wide

    def own(self):
        return pltpu.make_async_copy(self.src, self.part(self.net.f, None), self.at("own", 0, 0))

    def first(self, i, j):
        send, recv = self.at("row" if i == 0 else "col", i, j)
        place = self.part(self.net.f, None)
        return put(place, place, send, recv, fsdp=self.rank(i, j))

    def came(self, i, j):
        send, recv = self.at("row" if i == 0 else "col", i, j)
        place = self.part(self.back(i, j), None)
        return put(place, place, send, recv, fsdp=self.rank(i, j))

    def second(self, half, i, j, came=False):
        send, recv = self.at("half0" if half == 0 else "half1", i, j)
        origin = self.back(i, j) if came else self.back(0, j) if half == 0 else self.back(i, 0)
        place = self.part(origin, half)
        return put(place, place, send, recv, fsdp=self.rank(i, 0) if half == 0 else self.rank(0, j))

    def prepare(self):
        self.own().start()

    def start(self):
        self.own().wait()
        for i in self.cols:
            self.first(i, 0).start()
        for j in self.rows:
            self.first(0, j).start()

    def relay(self):
        for j in self.rows:
            self.came(0, j).wait_recv()
            for i in self.cols:
                self.second(0, i, j).start()
        for i in self.cols:
            self.came(i, 0).wait_recv()
            for j in self.rows:
                self.second(1, i, j).start()

    def finish(self):
        for j in self.rows:
            self.first(0, j).wait_send()
        for i in self.cols:
            self.first(i, 0).wait_send()
        for i in self.cols:
            for j in self.rows:
                for half in range(2):
                    self.second(half, i, j, came=True).wait_recv()
                    self.second(half, i, j).wait_send()


class Line:
    def __init__(self, net, src, part, recv, send, local):
        self.net, self.src, self.part, self.recv, self.send, self.local = net, src, part, recv, send, local
        self.pieces = recv.shape[1]
        self.rows = src.shape[0] // self.pieces

    @staticmethod
    def sems(n_s, pieces=2):
        return [
            pltpu.SemaphoreType.DMA((n_s, pieces)),
            pltpu.SemaphoreType.DMA((4, n_s // 2, pieces)),
            pltpu.SemaphoreType.DMA((1,)),
        ]

    def cut(self, ref, piece):
        return ref.at[aligned(piece * self.rows, self.rows)]

    def own(self):
        return pltpu.make_async_copy(self.src, self.part(self.net.s), self.local.at[0])

    def on_line(self, src, chunk, side, hop, piece):
        return put(
            self.cut(src, piece),
            self.cut(self.part(chunk), piece),
            self.send.at[side, hop, piece],
            self.recv.at[chunk, piece],
            seq=self.net.s + 2 - 4 * side,
        )

    def to_mate(self, src, chunk, side, hop, piece):
        return put(
            self.cut(src, piece),
            self.cut(self.part(chunk), piece),
            self.send.at[2 + side, hop, piece],
            self.recv.at[chunk, piece],
            seq=self.net.mate,
        )

    def goes_on(self, side):
        after = self.net.z + 1 - 2 * side
        return (after >= 0) & (after < self.net.n_l)

    def each_piece(self, act):
        pl.loop(0, self.pieces)(act)

    def prepare(self):
        self.own().start()

    def start(self):
        net = self.net
        self.own().wait()
        place = self.part(net.s)

        @self.each_piece
        def _(piece):
            for side in range(2):

                @pl.when(self.goes_on(side))
                def _():
                    self.on_line(place, net.s, side, 0, piece).start()

            self.to_mate(place, net.s, 0, 0, piece).start()

    def came(self, chunk, piece):
        place = self.cut(self.part(chunk), piece)
        put(place, place, self.send.at[0, 0, 0], self.recv.at[chunk, piece], seq=self.net.mate).wait_recv()

    def step(self, hop):
        net = self.net

        @self.each_piece
        def _(piece):
            def act(other, side):
                chunk = 2 * other + net.c
                self.came(chunk, piece)

                @pl.when(self.goes_on(side))
                def _():
                    self.on_line(self.part(chunk), chunk, side, hop, piece).start()

                self.to_mate(self.part(chunk), chunk, side, hop, piece).start()

            net.sides(hop, act)

    def pair(self, other):
        @self.each_piece
        def _(piece):
            self.came(2 * other + 1 - self.net.c, piece)

    def here(self):
        self.pair(self.net.z)

    def finish(self):
        net = self.net
        place = self.part(net.s)

        @self.each_piece
        def _(piece):
            for side in range(2):

                @pl.when(self.goes_on(side))
                def _():
                    self.on_line(place, net.s, side, 0, piece).wait_send()

            self.to_mate(place, net.s, 0, 0, piece).wait_send()

            @pl.loop(1, net.n_l)
            def _(hop):
                def act(other, side):
                    chunk = 2 * other + net.c

                    @pl.when(self.goes_on(side))
                    def _():
                        self.on_line(self.part(chunk), chunk, side, hop, piece).wait_send()

                    self.to_mate(self.part(chunk), chunk, side, hop, piece).wait_send()

                net.sides(hop, act)


class Packets:
    def __init__(self, net, src, buf, sems):
        self.net, self.src, self.buf, self.sems = net, src, buf, sems

    @staticmethod
    def count(n_f, n_s):
        return 1 + 2 * (n_f - 1) + 2 * (n_s - 1)

    def own(self):
        net = self.net
        return pltpu.make_async_copy(self.src, self.buf.at[net.s, net.f], self.sems.at[0])

    def one(self, k, came=False):
        net = self.net
        f = (net.f - k + net.n_f) % net.n_f if came else net.f
        place = self.buf.at[net.s, f]
        return put(
            place if came else self.src,
            place,
            self.sems.at[2 * k - 1],
            self.sems.at[2 * k],
            fsdp=(net.f + k) % net.n_f,
        )

    def two(self, k, came=False):
        net = self.net
        place = self.buf.at[(net.s - k + net.n_s) % net.n_s if came else net.s]
        at = 2 * (net.n_f - 1) + 2 * k - 1
        return put(place, place, self.sems.at[at], self.sems.at[at + 1], seq=(net.s + k) % net.n_s)

    def start(self):
        self.own().start()
        for k in range(1, self.net.n_f):
            self.one(k).start()

    def middle(self):
        self.own().wait()
        for k in range(1, self.net.n_f):
            self.one(k, came=True).wait_recv()
            self.one(k).wait_send()
        for k in range(1, self.net.n_s):
            self.two(k).start()

    def finish(self):
        for k in range(1, self.net.n_s):
            self.two(k, came=True).wait_recv()
            self.two(k).wait_send()

    def unpack(self, out, width):
        net = self.net
        per = 128 // width
        for tile in range(net.n_f * net.n_s // per):
            total = None
            for j in range(per):
                f, s = divmod(tile * per + j, net.n_s)
                piece = self.buf[s, f]
                if j:
                    piece = pltpu.roll(piece, j * width, axis=1)
                total = piece if total is None else total + piece
            out[:, tile * 128 : (tile + 1) * 128] = total


def rotary(values, cosine, sine):
    columns = values.shape[1]
    half = ROT // 2
    times = columns // 128

    def wide(table):
        return table if times == 1 else jnp.concatenate([table] * times, axis=1)

    lane = lax.broadcasted_iota(jnp.int32, values.shape, 1)
    other = jnp.where(
        lane % HEAD < half, pltpu.roll(values, columns - half, axis=1), pltpu.roll(values, half, axis=1)
    )
    return values * wide(cosine) + other * wide(sine)


def rotary_tables(length):
    half = ROT // 2
    freqs = np.float32(10000.0) ** (-np.arange(half, dtype=np.float32) * np.float32(2.0 / ROT))
    angles = np.arange(length, dtype=np.float32)[:, None] * freqs[None, :].astype(np.float32)
    cosine, sine = np.cos(angles), np.sin(angles)
    rest = np.zeros((length, HEAD - ROT), np.float32)
    keep = np.concatenate([cosine, cosine, rest + 1], 1)
    swap = np.concatenate([-sine, sine, rest], 1)
    return [np.tile(t, (1, 128 // HEAD)).astype(np.float32) for t in (keep, swap)]


def normalize(values):
    center = values - jnp.mean(values, -1, keepdims=True)
    inverse = lax.rsqrt(jnp.mean(center * center, -1, keepdims=True) + EPSILON)
    return center * inverse, inverse


class Copies:
    def __init__(self, sems):
        self.sems, self.all, self.open = sems, [], []

    def start(self, src, dst):
        copy = pltpu.make_async_copy(src, dst, self.sems.at[len(self.all)])
        copy.start()
        self.all.append(copy)
        self.open.append(copy)
        return copy

    def wait(self, *copies):
        for copy in copies or list(self.open):
            copy.wait()
            self.open = [c for c in self.open if c is not copy]


def columns_of(ref, depth):
    half_rows = ref.shape[0] // 2

    def part(f, half):
        span = aligned(f * depth, depth)
        if half is None:
            return ref.at[:, span]
        return ref.at[pl.ds(half * half_rows, half_rows), span]

    return part


def rows_of(ref, chunk):
    return lambda s: ref.at[aligned(s * chunk, chunk)]


class Fold:
    def __init__(self, net, tile, total, mate_in, coming, mate_out, out, mate_send, mate_recv, send, recv):
        self.net, self.tile, self.total = net, tile, total
        self.mate_in, self.coming, self.mate_out, self.out = mate_in, coming, mate_out, out
        self.mate_send, self.mate_recv, self.send, self.recv = mate_send, mate_recv, send, recv
        self.chunk = total.shape[0]
        self.pieces = recv.shape[1]
        self.rows = self.chunk // self.pieces

    @staticmethod
    def shared(chunk, width):
        return [pltpu.VMEM((2 * chunk, TILE), F32), pltpu.VMEM((chunk, width), F32)]

    @staticmethod
    def buffers(n_s, chunk, width):
        n_l = n_s // 2
        return [
            pltpu.VMEM((n_l, chunk, width), BF),
            pltpu.VMEM((n_l + 1, chunk, width), BF),
            pltpu.VMEM((3, chunk, width), BF),
            pltpu.VMEM((n_l, chunk, width), BF),
        ]

    @staticmethod
    def sems(n_s, pieces=4):
        n_l = n_s // 2
        return [
            pltpu.SemaphoreType.DMA((3, pieces)),
            pltpu.SemaphoreType.DMA((n_l, pieces)),
            pltpu.SemaphoreType.DMA((n_l, pieces)),
            pltpu.SemaphoreType.DMA((n_l + 1, pieces)),
        ]

    def place(self, other):
        return (other >= 0) & (other < self.net.n_l)

    def fed(self, side):
        return self.place(self.net.z + 1 - 2 * side)

    def span(self, piece):
        return aligned(piece * self.rows, self.rows)

    def each_piece(self, act):
        pl.loop(0, self.pieces)(act)

    def to_mate(self, target, slot, piece):
        span = self.span(piece)
        return put(
            self.mate_out.at[slot, span],
            self.mate_in.at[target, span],
            self.mate_send.at[slot, piece],
            self.mate_recv.at[target, piece],
            seq=self.net.mate,
        )

    def onward(self, target, side, hop, piece):
        span = self.span(piece)
        slot = target + (self.net.n_l - target) * (1 - side) * (1 // hop)
        return put(
            self.out.at[target, span],
            self.coming.at[slot, span],
            self.send.at[target, piece],
            self.recv.at[slot, piece],
            seq=self.net.s + 4 * side - 2,
        )

    def came(self, slot, piece):
        place = self.coming.at[slot, self.span(piece)]
        put(place, place, self.send.at[0, 0], self.recv.at[slot, piece], seq=self.net.mate).wait_recv()

    def mate_sent(self, slot):
        self.each_piece(lambda piece: self.to_mate(self.net.z, slot, piece).wait_send())

    def begin_one(self, target, slot, produce):
        mine = aligned(self.net.c * self.chunk, self.chunk)
        theirs = aligned((1 - self.net.c) * self.chunk, self.chunk)

        def write(cols, value):
            self.tile[...] = value
            self.out[target, :, cols] = self.tile[mine, :].astype(BF)
            self.mate_out[slot, :, cols] = self.tile[theirs, :].astype(BF)

        produce(target, write)
        self.each_piece(lambda piece: self.to_mate(target, slot, piece).start())

    def leave(self, target, side, hop):
        @pl.when((hop > 0) & jnp.logical_not(self.fed(side)))
        def _():
            self.each_piece(lambda piece: self.pass_piece(target, side, hop, piece, False))

    def begin(self, produce, between=None):
        net = self.net

        @pl.loop(0, net.n_l)
        def _(j):
            hop = net.n_l - 1 - j

            def act(target, side):
                @pl.when((hop > 0) | (side == 0))
                def _():
                    @pl.when((hop > 0) & self.place(target + 2 * side - 1))
                    def _():
                        self.mate_sent(side)

                    self.begin_one(target, side + (2 - side) * (1 // (hop + 1)), produce)
                    self.leave(target, side, hop)

            net.sides(hop, act)
            if between is not None:
                pl.when(j == 1)(between)

    def pass_piece(self, target, side, hop, piece, fed):
        self.to_mate(target, 0, piece).wait_recv()
        span = self.span(piece)
        value = self.out[target, span, :].astype(F32) + self.mate_in[target, span, :].astype(F32)
        if fed:
            self.came(target, piece)
            value = value + self.coming[target, span, :].astype(F32)
        self.out[target, span, :] = value.astype(BF)
        self.onward(target, side, hop, piece).start()

    def open_total(self):
        net = self.net

        @self.each_piece
        def _(piece):
            self.to_mate(net.z, 0, piece).wait_recv()
            span = self.span(piece)
            self.total[span, :] = self.out[net.z, span, :].astype(F32) + self.mate_in[net.z, span, :].astype(F32)

    def wave(self, at, near=False, between=None):
        net = self.net
        above = at if near else net.n_l - at

        @pl.loop(0, 2)
        def _(turn):
            side = (1 - (2 * net.z) // net.n_l + turn) % 2
            target = net.n_l - 1 - above + (2 * above - net.n_l + 1) * side
            hop = (target - net.z) * (2 * side - 1)

            @self.each_piece
            def _(piece):
                span = self.span(piece)

                @pl.when(self.fed(side) & (hop > 0))
                def _():
                    self.pass_piece(target, side, hop, piece, True)

                @pl.when(self.fed(side) & (hop == 0))
                def _():
                    slot = net.z + (net.n_l - net.z) * (1 - side)
                    self.came(slot, piece)
                    self.total[span, :] = self.total[span, :] + self.coming[slot, span, :].astype(F32)

                if between is not None:
                    between(((at - 1) * 2 + turn) * self.pieces + piece)

    def finish(self):
        net = self.net
        self.mate_sent(2)
        for side in range(2):
            pl.when(self.place(net.z + 2 * side - 1))(functools.partial(self.mate_sent, side))

        @pl.loop(1, net.n_l)
        def _(hop):
            net.sides(
                hop,
                lambda target, side: self.each_piece(
                    lambda piece: self.onward(target, side, hop, piece).wait_send()
                ),
            )


class GridSum:
    def __init__(self, net, stage, came, sems):
        self.net, self.stage, self.came, self.sems = net, stage, came, sems
        self.half = stage.shape[1] // 2
        self.rows = next(r for r in (176, 128, 96, 64, 32, 16) if self.half % r == 0)
        self.cols = range(1, net.tall)
        self.along = range(1, net.wide)
        self.bases = self.layout(net.n_f)

    @staticmethod
    def layout(n_f):
        tall = 2 if n_f % 2 == 0 else 1
        wide = n_f // tall
        sizes = [(wide - 1) * tall, (tall - 1) * wide, tall - 1, wide - 1]
        return [sum(sizes[:at]) for at in range(5)]

    @staticmethod
    def scratch(n_f, rows, columns):
        count = GridSum.layout(n_f)[4]
        return [
            pltpu.VMEM((n_f, rows, columns), BF),
            pltpu.VMEM((count, rows // 2, columns), BF),
            pltpu.SemaphoreType.DMA((2, count + GridEnd.count(n_f))),
        ]

    def slot(self, kind, i, j):
        base = self.bases[kind]
        return base + [(j - 1) * self.net.tall + i, (i - 1) * self.net.wide + j, i - 1, j - 1][kind]

    def rank(self, i, j):
        net = self.net
        return ((net.a + i) % net.tall) * net.wide + (net.b + j) % net.wide

    def owner(self, at):
        return self.rank(at // self.net.wide, at % self.net.wide)

    def copy(self, kind, i, j):
        half = kind % 2
        along = kind in (0, 3)
        slot = self.slot(kind, i, j)
        at = i * self.net.wide + j
        return put(
            self.stage.at[at, pl.ds(half * self.half, self.half)],
            self.came.at[slot],
            self.sems.at[0, slot],
            self.sems.at[1, slot],
            fsdp=self.rank(0, j) if along else self.rank(i, 0),
        )

    def first(self, at):
        i, j = at // self.net.wide, at % self.net.wide

        @pl.when(j > 0)
        def _():
            self.copy(0, i, j).start()

        @pl.when(i > 0)
        def _():
            self.copy(1, i, j).start()

    def gather(self, half, at, slots, write):
        @pl.loop(0, self.half // self.rows)
        def _(step):
            span = aligned(half * self.half + step * self.rows, self.rows, 16)
            value = self.stage[at, span, :].astype(F32)
            for slot in slots:
                value = value + self.came[slot, aligned(step * self.rows, self.rows, 16), :].astype(F32)
            write(span, value)

    def wait(self, *copies):
        for kind, i, j in copies:
            self.copy(kind, i, j).wait_recv()
        return [self.slot(*copy) for copy in copies]

    def second(self):
        def keep(at):
            def write(span, value):
                self.stage[at, span, :] = value.astype(BF)

            return write

        for i in self.cols:
            at = i * self.net.wide
            self.gather(0, at, self.wait(*[(0, i, j) for j in self.along]), keep(at))
            self.copy(2, i, 0).start()
        for j in self.along:
            self.gather(1, j, self.wait(*[(1, i, j) for i in self.cols]), keep(j))
            self.copy(3, 0, j).start()

    def sum_first(self):
        def keep(at):
            def write(span, value):
                self.stage[at, span, :] = value.astype(BF)

            return write

        for i in range(self.net.tall):
            at = i * self.net.wide
            self.gather(0, at, self.wait(*[(0, i, j) for j in self.along]), keep(at))
        for j in range(self.net.wide):
            self.gather(1, j, self.wait(*[(1, i, j) for i in self.cols]), keep(j))

    def hand_on(self, out):
        net = self.net
        shards = [(0, 0), (0, 1), *[(i * net.wide, 0) for i in self.cols], *[(j, 1) for j in self.along]]
        return [
            pltpu.make_async_copy(
                self.stage.at[at, pl.ds(half * self.half, self.half)], out.at[k], self.sems.at[0, self.bases[4] + k]
            )
            for k, (at, half) in enumerate(shards)
        ]

    def last(self, out):
        def write(span, value):
            out[span, :] = value

        self.gather(
            0, 0, self.wait(*[(0, 0, j) for j in self.along], *[(2, i, 0) for i in self.cols]), write
        )
        self.gather(
            1, 0, self.wait(*[(1, i, 0) for i in self.cols], *[(3, 0, j) for j in self.along]), write
        )

    def finish_first(self):
        for i in range(self.net.tall):
            for j in range(self.net.wide):
                if j:
                    self.copy(0, i, j).wait_send()
                if i:
                    self.copy(1, i, j).wait_send()

    def finish(self):
        self.finish_first()
        for i in self.cols:
            self.copy(2, i, 0).wait_send()
        for j in self.along:
            self.copy(3, 0, j).wait_send()


class GridEnd:
    def __init__(self, net, sums, came, sems):
        self.net, self.sums, self.came, self.sems = net, sums, came, sems

    @staticmethod
    def count(n_f):
        tall = 2 if n_f % 2 == 0 else 1
        return tall + n_f // tall

    @staticmethod
    def scratch(n_f, rows, columns):
        count = GridEnd.count(n_f)
        return [
            pltpu.VMEM((count, rows // 2, columns), BF),
            pltpu.VMEM((count - 2, rows // 2, columns), BF),
            pltpu.SemaphoreType.DMA((2, count - 2)),
        ]

    def copies(self):
        net = self.net
        f = [((net.a + i) % net.tall) * net.wide + net.b for i in range(1, net.tall)]
        f += [net.a * net.wide + (net.b + j) % net.wide for j in range(1, net.wide)]
        return [
            put(self.sums.at[2 + k], self.came.at[k], self.sems.at[0, k], self.sems.at[1, k], fsdp=to)
            for k, to in enumerate(f)
        ]

    def start(self):
        for copy in self.copies():
            copy.start()

    def last(self, out):
        for copy in self.copies():
            copy.wait()
        half = self.sums.shape[1]
        rows = next(r for r in (176, 128, 96, 64, 32, 16) if half % r == 0)
        down = range(self.net.tall - 1)
        along = range(self.net.tall - 1, self.net.tall + self.net.wide - 2)
        for at, slots in enumerate((down, along)):

            @pl.loop(0, half // rows)
            def _(step):
                span = aligned(step * rows, rows, 16)
                value = self.sums[at, span, :].astype(F32)
                for slot in slots:
                    value = value + self.came[slot, span, :].astype(F32)
                out[aligned(at * half + step * rows, rows, 16), :] = value


class PacketSum:
    def __init__(self, net, out, seq_in, total, fsdp_in, sems):
        self.net, self.out, self.seq_in, self.total, self.fsdp_in, self.sems = net, out, seq_in, total, fsdp_in, sems

    @staticmethod
    def scratch(n_f, n_s):
        return [
            pltpu.VMEM((n_s, n_f, SMALL, 128), F32),
            pltpu.VMEM((n_s, n_f, SMALL, 128), F32),
            pltpu.VMEM((n_f, SMALL, 128), F32),
            pltpu.VMEM((n_f, SMALL, 128), F32),
            pltpu.SemaphoreType.DMA((2 * (n_f + n_s),)),
        ]

    def one(self, k):
        to = (self.net.s + k) % self.net.n_s
        return put(self.out.at[to], self.seq_in.at[k], self.sems.at[2 * k], self.sems.at[2 * k + 1], seq=to)

    def two(self, k):
        to = (self.net.f + k) % self.net.n_f
        at = 2 * (self.net.n_s + k)
        return put(self.total.at[to], self.fsdp_in.at[k], self.sems.at[at], self.sems.at[at + 1], fsdp=to)

    def start(self, terms, width):
        net = self.net
        per = 128 // width
        for tile in range(net.n_f * net.n_s // per):
            value = terms[:, tile * 128 : (tile + 1) * 128]
            for j in range(per):
                f, s = divmod(tile * per + j, net.n_s)
                self.out[s, f] = pltpu.roll(value, 128 - j * width, axis=1) if j else value
        for k in range(1, net.n_s):
            self.one(k).start()

    def middle(self):
        net = self.net
        total = self.out[net.s]
        for k in range(1, net.n_s):
            self.one(k).wait()
            total = total + self.seq_in[k]
        self.total[...] = total
        for k in range(1, net.n_f):
            self.two(k).start()

    def finish(self, result):
        net = self.net
        total = self.total[net.f]
        for k in range(1, net.n_f):
            self.two(k).wait()
            total = total + self.fsdp_in[k]
        result[...] = total


def norm_backward(rows, source, grad, gain, terms, at, write):
    terms[at : at + 2, :] = jnp.zeros((2, terms.shape[1]), F32)

    @pl.loop(0, rows // 32)
    def _(i):
        span = aligned(i * 32, 32)
        scaled, inverse = normalize(source[span, :].astype(F32))
        value = grad[span, :]
        upstream = value * gain
        inner = jnp.mean(upstream, -1, keepdims=True)
        cross = jnp.mean(upstream * scaled, -1, keepdims=True)
        terms[at : at + 1, :] = terms[at : at + 1, :] + jnp.sum(value * scaled, 0, keepdims=True)
        terms[at + 1 : at + 2, :] = terms[at + 1 : at + 2, :] + jnp.sum(value, 0, keepdims=True)
        write(i, span, inverse * (upstream - inner - scaled * cross))


def layer_kernel(
    tok,
    gain_one,
    shift_one,
    gain_two,
    shift_two,
    bias,
    wq_own,
    wo_own,
    wg_own,
    wu_own,
    wd_own,
    gout_own,
    cosine,
    sine,
    q_o,
    k_o,
    kt_o,
    v_o,
    att_o,
    lse_o,
    n1_o,
    gains_o,
    wq_o,
    wo_o,
    dm_o,
    datt_o,
    dmid_o,
    top_o,
    terms_o,
    gate_o,
    up_o,
    down_o,
    rows,
    gout,
    wq,
    wo,
    wg,
    wu,
    wd,
    q,
    k,
    kt,
    v,
    vt,
    ot,
    att,
    hidden,
    dgate,
    dup,
    mid,
    low,
    packet,
    packets,
    tiles,
    total,
    *rest,
):
    net = Net()
    chunk, width = tok.shape
    length = chunk * net.n_s
    depth = wq_own.shape[1]
    columns = wq_own.shape[2]
    heads = columns // HEAD
    pair = 2 * chunk
    buffers, rest = rest[:4], rest[4:]
    folds = []
    for _ in range(3):
        folds.append(Fold(net, tiles, total, *buffers, *rest[:4]))
        rest = rest[4:]
    att_fold, normed_fold, top_fold = folds
    line_sems = [rest[at : at + 3] for at in (0, 3, 6, 9)]
    rest = rest[12:]
    spread_sems, rest = rest[:5], rest[5:]
    gate_sum, up_sum, down_sum = [GridSum(net, *rest[at : at + 3]) for at in (0, 3, 6)]
    sums = (down_sum, gate_sum, up_sum)
    pk_sems, copy_sems, n1_sems, free_sem = rest[9:]
    copies = Copies(copy_sems)
    n1 = att_fold.mate_out

    packet[...] = jnp.zeros(packet.shape, F32)
    own = gain_one.shape[1]
    for at, part in enumerate((gain_one, shift_one, gain_two, shift_two)):
        packet[at : at + 1, 0:own] = part[...].astype(F32)
    packet[4:7, 0:own] = bias[...].astype(F32)
    def wq_part(f, half):
        if half is None:
            return wq.at[:, aligned(f * depth, depth), :]
        return wq.at[:, aligned(f * depth + half * (depth // 2), depth // 2), :]

    spread_q = Spread(net, wq_own, wq_part, spread_sems[0])
    spread_o, spread_g, spread_u, spread_d = [
        Spread(net, own, columns_of(full, depth), sems)
        for own, full, sems in zip((wo_own, wg_own, wu_own, wd_own), (wo, wg, wu, wd), spread_sems[1:])
    ]
    pk = Packets(net, packet, packets, pk_sems)
    line = Line(net, tok, rows_of(rows, chunk), *line_sems[0])
    gout_line = Line(net, gout_own, rows_of(gout, chunk), *line_sems[1])
    n2_line = Line(net, low, rows_of(rows, chunk), *line_sems[2])
    dm_line = Line(net, low, rows_of(rows, chunk), *line_sems[3])

    for ready in (line, spread_q, spread_o, spread_g, spread_u, spread_d, gout_line):
        ready.prepare()
    net.barrier()

    def pairs(which, hop):
        net.sides(hop, lambda other, side: which.pair(other))

    def blocks(hop, act):
        def once(other, side):
            @pl.when((hop > 0) | (side == 0))
            def _():
                act(other, side)

        net.sides(hop, once)

    pk.start()
    line.start()
    spread_q.start()
    pk.middle()
    pk.finish()
    pk.unpack(gains_o, width // (net.n_f * net.n_s))

    def project_block(other, side):
        span = aligned(other * pair, pair)
        gain, shift = gains_o[0:1, :], gains_o[1:2, :]

        for part in range(2):

            @pl.loop(0, chunk // 32)
            def _(i):
                at = aligned((2 * other + part) * chunk + i * 32, 32)
                scaled, _ = normalize(rows[at, :].astype(F32))
                n1[part, aligned(i * 32, 32), :] = (scaled * gain + shift).astype(BF)

        keeps = [
            pltpu.make_async_copy(
                n1.at[part], n1_o.at[aligned((2 * other + part) * chunk, chunk)], n1_sems.at[part]
            )
            for part in range(2)
        ]
        for copy in keeps:
            copy.start()
        left = n1[0:2].reshape(pair, width)
        cols = aligned(net.s * columns, columns)
        tables = cosine[span, :], sine[span, :]
        for kind in range(3):
            value = dot(left, wq[kind]) + gains_o[4 + kind : 5 + kind, cols]
            if kind == 0:
                q[span, :] = rotary(value, *tables).astype(BF)
            elif kind == 1:
                value = rotary(value, *tables)
                k[span, :] = value.astype(BF)
                kt[...] = value.T.astype(BF)
            else:
                v[...] = value.astype(BF)
                vt[:, span] = value.T.astype(BF)
        for copy in (
            pltpu.make_async_copy(kt, kt_o.at[:, span], n1_sems.at[2]),
            pltpu.make_async_copy(v, v_o.at[span], n1_sems.at[3]),
        ):
            copy.start()
            keeps.append(copy)
        for copy in keeps:
            copy.wait()

    line.here()
    for hop in range(1, net.n_l - 1):
        line.step(hop)
        if hop == 1:
            spread_q.relay()
        pairs(line, hop)
    spread_o.start()
    spread_q.finish()
    spread_g.start()
    pl.loop(0, net.n_l - 1)(lambda hop: blocks(hop, project_block))
    spread_o.relay()
    spread_u.start()
    line.step(net.n_l - 1)
    gout_line.start()
    pairs(line, net.n_l - 1)
    blocks(net.n_l - 1, project_block)
    spread_d.start()
    q_copy = copies.start(q, q_o)
    for pair_of in ((wq, wq_o), (k, k_o)):
        copies.start(*pair_of)
    spread_o.finish()
    line.finish()

    def attend(i):
        lo, hi = i * pair, (i + 1) * pair

        @pl.loop(0, heads)
        def _(head):
            lane = lax.broadcasted_iota(jnp.int32, (1, columns), 1)
            here = jnp.where(lane // HEAD == head, HEAD**-0.5, 0.0).astype(BF)
            visible = lax.broadcasted_iota(jnp.int32, (pair, pair), 0) <= lax.broadcasted_iota(
                jnp.int32, (pair, pair), 1
            )
            head_rows = aligned(head * HEAD, HEAD)
            query = q[lo:hi, :] * here
            near = jnp.where(visible, dot_nt(k[lo:hi, :], query), NEG_LARGE)
            highest = jnp.max(near, 0, keepdims=True)
            if i:
                far = dot_nt(k[0:lo, :], query)
                highest = jnp.maximum(highest, jnp.max(far, 0, keepdims=True))
            near = jnp.exp(near - highest)
            sum_of = jnp.sum(near, 0, keepdims=True)
            out = dot(vt[head_rows, lo:hi], near.astype(BF))
            if i:
                far = jnp.exp(far - highest)
                sum_of = sum_of + jnp.sum(far, 0, keepdims=True)
                out = out + dot(vt[head_rows, 0:lo], far.astype(BF))
            ot[head_rows, :] = out / sum_of
            lse_o[pl.ds(head, 1), lo:hi] = highest + jnp.log(sum_of)

        att[lo:hi, :] = ot[...].T.astype(BF)

    def produce_attended(place, write):
        for i in range(net.n_l):
            pl.when(place == i)(functools.partial(attend, i))
        left = att[aligned(place * pair, pair), :]

        @pl.loop(0, width // TILE)
        def _(j):
            cols = aligned(j * TILE, TILE)
            write(cols, dot(left, wo[:, cols]))

    def relays():
        gout_line.step(1)
        spread_g.relay()

    att_fold.begin(produce_attended, relays)
    copies.start(att, att_o)
    copies.start(wo, wo_o)
    att_fold.open_total()
    for at in range(1, net.n_l):
        att_fold.wave(at)
        if at + 1 < net.n_l:
            gout_line.step(at + 1)
        if at == 1:
            spread_u.relay()
        if at == min(2, net.n_l - 1):
            spread_d.relay()
    gain_two, shift_two = gains_o[2:3, :], gains_o[3:4, :]

    @pl.loop(0, chunk // 32)
    def _(i):
        span = aligned(i * 32, 32)
        value = rows[aligned(net.s * chunk + i * 32, 32), :].astype(F32) + total[span, :]
        mid[span, :] = value
        scaled, _ = normalize(value)
        low[span, :] = (scaled * gain_two + shift_two).astype(BF)

    n2_line.prepare()
    n2_line.start()
    att_fold.finish()
    gout_line.here()
    pl.loop(1, net.n_l)(lambda hop: pairs(gout_line, hop))

    def forward_block(other):
        span = aligned(other * pair, pair)
        right = rows[span, :]
        half = hidden.shape[0] // 2

        @pl.loop(0, 2)
        def _(part):
            units = aligned(part * half, half, 16)
            gate = dot_nt(wg[units, :], right)
            up = dot_nt(wu[units, :], right)
            back = dot_nt(wd[units, :], gout[span, :])
            sigma = jax.nn.sigmoid(gate)
            active = gate * sigma
            hidden[units, span] = (active * up).astype(BF)
            dgate[units, span] = (back * up * (sigma * (1.0 + gate * (1.0 - sigma)))).astype(BF)
            dup[units, span] = (back * active).astype(BF)

    def produce_normed(place, write):
        span = aligned(place * pair, pair)
        left, right = dgate[:, span].T, dup[:, span].T

        @pl.loop(0, width // TILE)
        def _(j):
            cols = aligned(j * TILE, TILE)
            write(cols, dot(left, wg[:, cols]) + dot(right, wu[:, cols]))

    def begin_normed(other, side, hop):
        @pl.when(hop > 1)
        def _():
            normed_fold.mate_sent(side)

        normed_fold.begin_one(other, side + (2 - side) * (1 // (hop + 1)), produce_normed)

    def forward_blocks(hop):
        def act(other, side):
            forward_block(other)

            @pl.when(jnp.logical_not(normed_fold.fed(side)))
            def _():
                begin_normed(other, side, hop)
                normed_fold.leave(other, side, hop)

        net.sides(hop, act)

    def begin_fed(hop):
        def act(other, side):
            @pl.when((hop == 0) | normed_fold.fed(side))
            def _():
                begin_normed(other, side, hop)

        blocks(hop, act)

    n2_line.here()
    for spread in (spread_g, spread_u, spread_d):
        spread.finish()
    forward_block(net.z)

    @pl.loop(1, net.n_l)
    def _(hop):
        n2_line.step(hop)
        pairs(n2_line, hop)
        forward_blocks(hop)
        begin_fed(hop - 1)

    begin_fed(net.n_l - 1)
    normed_fold.open_total()

    def weight_terms(task):
        at, kind = net.n_f - 1 - task // 3, task % 3
        cols = aligned(gate_sum.owner(at) * depth, depth)
        for way, (grid_sum, left, right) in enumerate(
            ((down_sum, hidden, gout), (gate_sum, dgate, rows), (up_sum, dup, rows))
        ):

            @pl.when(kind == way)
            def _():
                half = left.shape[0] // 2

                @pl.loop(0, 2)
                def _(part):
                    units = aligned(part * half, half, 16)
                    grid_sum.stage[at, units, :] = dot(left[units, :], right[:, cols]).astype(BF)

                grid_sum.first(at)

    tasks = 3 * net.n_f
    slots = 2 * normed_fold.pieces * (net.n_l - 1)
    each = -(-tasks // slots)

    def between(slot):
        @pl.loop(0, each)
        def _(i):
            pl.when(slot * each + i < tasks)(lambda: weight_terms(slot * each + i))

    for at in range(1, net.n_l):
        normed_fold.wave(at, near=True, between=between)
    n2_line.finish()

    def beside(act):
        act(net.mate)
        for side in range(2):
            pl.when(n2_line.goes_on(side))(lambda: act(net.s + 2 - 4 * side))

    beside(lambda to: pl.semaphore_signal(free_sem, 1, device_id={"seq": to}, device_id_type=MESH))

    def write_middle(i, span, value):
        value = value + gout[aligned(net.s * chunk + i * 32, 32), :].astype(F32)
        dmid_o[span, :] = value
        low[span, :] = value.astype(BF)

    terms_o[...] = jnp.zeros(terms_o.shape, F32)
    norm_backward(chunk, mid, total, gain_two, terms_o, 2, write_middle)
    ends = (net.z + net.n_l - 1) // net.n_l + (2 * net.n_l - 2 - net.z) // net.n_l
    pl.semaphore_wait(free_sem, 1 + ends)
    dm_line.prepare()
    dm_line.start()
    normed_fold.finish()

    def produce_top(place, write):
        left = hidden[:, aligned(place * pair, pair)].T

        @pl.loop(0, width // TILE)
        def _(j):
            cols = aligned(j * TILE, TILE)
            write(cols, dot(left, wd[:, cols]))

    copies.wait(q_copy)
    datt = q

    def back_block(other, side):
        span = aligned(other * pair, pair)
        datt[span, :] = dot_nt(rows[span, :], wo[...]).astype(BF)

    dm_line.here()
    dm_line.step(1)
    top_fold.begin(produce_top)
    back_block(net.z, 0)
    top_fold.open_total()
    for at in range(1, net.n_l):
        if at + 1 < net.n_l:
            dm_line.step(at + 1)
        top_fold.wave(at)
        pairs(dm_line, at)
        net.sides(at, back_block)
    copies.start(datt, datt_o)
    copies.start(rows, dm_o)

    @pl.loop(0, chunk // 32)
    def _(i):
        span = aligned(i * 32, 32)
        top_fold.out[net.z, span, :] = (mid[span, :] + total[span, :]).astype(BF)

    copies.start(top_fold.out.at[net.z], top_o)
    top_fold.finish()
    gout_line.finish()
    dm_line.finish()
    hands = []
    for grid_sum, out in zip(sums, (down_o, gate_o, up_o)):
        grid_sum.sum_first()
        hands.extend(grid_sum.hand_on(out))
        for copy in grid_sum.hand_on(out):
            copy.start()
    for grid_sum in sums:
        grid_sum.finish_first()
    for copy in hands:
        copy.wait()
    copies.wait()


def layer_part(tokens, norms, wq, wo, wg, wu, wd, gout, tables):
    chunk, width = tokens.shape
    n_f, n_s = lax.axis_size("fsdp"), lax.axis_size("seq")
    length = chunk * n_s
    depth, columns = wq.shape[1:]
    units = wg.shape[0]
    shape = jax.ShapeDtypeStruct
    wide, head, turned, weight = (length, width), (length, columns), (units, length), (units, width)
    return pl.pallas_call(
        layer_kernel,
        name="layer",
        out_shape=[
            shape(head, BF),
            shape(head, BF),
            shape((columns, length), BF),
            shape(head, BF),
            shape(head, BF),
            shape((8, length), F32),
            shape(wide, BF),
            shape((SMALL, width), F32),
            shape((3, width, columns), BF),
            shape((columns, width), BF),
            shape(wide, BF),
            shape(head, BF),
            shape((chunk, width), F32),
            shape((chunk, width), BF),
            shape((SMALL, width), F32),
            *[shape((GridEnd.count(n_f), units // 2, depth), BF)] * 3,
        ],
        in_specs=[ANY, *[VMEM] * 5, *[ANY] * 6, VMEM, VMEM],
        out_specs=[*[ANY] * 5, VMEM, ANY, VMEM, *[ANY] * 4, VMEM, ANY, VMEM, *[ANY] * 3],
        scratch_shapes=[
            pltpu.VMEM(wide, BF),
            pltpu.VMEM(wide, BF),
            pltpu.VMEM((3, width, columns), BF),
            pltpu.VMEM((columns, width), BF),
            *[pltpu.VMEM(weight, BF)] * 3,
            pltpu.VMEM(head, BF),
            pltpu.VMEM(head, BF),
            pltpu.VMEM((columns, 2 * chunk), BF),
            pltpu.VMEM((2 * chunk, columns), BF),
            pltpu.VMEM((columns, length), BF),
            pltpu.VMEM((columns, 2 * chunk), F32),
            pltpu.VMEM(head, BF),
            *[pltpu.VMEM(turned, BF)] * 3,
            pltpu.VMEM((chunk, width), F32),
            pltpu.VMEM((chunk, width), BF),
            pltpu.VMEM((SMALL, 128), F32),
            pltpu.VMEM((n_s, n_f, SMALL, 128), F32),
            *Fold.shared(chunk, width),
            *Fold.buffers(n_s, chunk, width),
            *Fold.sems(n_s) * 3,
            *Line.sems(n_s) * 4,
            *[pltpu.SemaphoreType.DMA((Spread.count(n_f),))] * 5,
            *GridSum.scratch(n_f, units, depth) * 3,
            pltpu.SemaphoreType.DMA((Packets.count(n_f, n_s),)),
            pltpu.SemaphoreType.DMA((8,)),
            pltpu.SemaphoreType.DMA((4,)),
            pltpu.SemaphoreType.REGULAR,
        ],
        compiler_params=pltpu.CompilerParams(
            collective_id=1, has_side_effects=True, vmem_limit_bytes=VMEM_BYTES
        ),
        cost_estimate=pl.CostEstimate(
            flops=2 * length * width * (4 * columns + 9 * units),
            bytes_accessed=8 * length * width,
            transcendentals=length * (length * columns // HEAD + units),
        ),
    )(tokens, *norms, wq, wo, wg, wu, wd, gout, *tables)


def back_kernel(
    datt_in,
    q_in,
    k_in,
    kt_in,
    v_in,
    att_in,
    wq_in,
    n1_in,
    dm_in,
    down_in,
    gate_in,
    up_in,
    lse,
    tok,
    dmid,
    gains,
    terms_in,
    cosine,
    sine,
    gin_o,
    small_o,
    out_o,
    qkv_o,
    down_o,
    gate_o,
    up_o,
    datt,
    q,
    k,
    kt,
    v,
    att,
    wq,
    n1,
    dm,
    dk,
    dv,
    dqt,
    dproj,
    terms,
    tiles,
    total,
    *rest,
):
    net = Net()
    chunk, width = tok.shape
    length, columns = q_in.shape
    heads = columns // HEAD
    pair = 2 * chunk
    depth = width // net.n_f
    block = 256
    buffers, rest = rest[:4], rest[4:]
    fold_sems, rest = rest[:4], rest[4:]
    packet_scratch, rest = rest[:5], rest[5:]
    out_sum, qkv_sum = GridSum(net, *rest[:3]), GridSum(net, *rest[3:6])
    ends = [GridEnd(net, *rest[at : at + 3]) for at in (6, 9, 12)]
    copy_sems, column_sems = rest[15:]

    copies = Copies(copy_sems)
    loads = [
        copies.start(src, dst)
        for src, dst in (
            (datt_in, datt),
            (q_in, q),
            (k_in, k),
            (kt_in, kt),
            (v_in, v),
            (att_in, att),
            (wq_in, wq),
            (down_in, ends[0].sums),
            (gate_in, ends[1].sums),
            (up_in, ends[2].sums),
        )
    ]
    def load(at, way):
        src, dst = ((n1_in, n1), (dm_in, dm))[way]
        cols = aligned(qkv_sum.owner(at) * depth, depth)
        return pltpu.make_async_copy(src.at[:, cols], dst.at[at % 2], column_sems.at[way, at % 2])

    for at in range(net.n_f - 1, max(net.n_f - 3, -1), -1):
        for way in range(2):
            load(at, way).start()

    @pl.loop(0, length // block)
    def _(i):
        span = aligned(i * block, block)
        dk[span, :] = jnp.zeros((block, columns), F32)
        dv[span, :] = jnp.zeros((block, columns), F32)

    net.barrier()
    copies.wait(*loads[7:])
    for end in ends:
        end.start()
    copies.wait(*loads[:5])

    @pl.loop(0, heads)
    def _(head):
        lane = lax.broadcasted_iota(jnp.int32, (1, columns), 1)
        here = jnp.where(lane // HEAD == head, 1.0, 0.0).astype(BF)
        scale = HEAD**-0.5
        visible = lax.broadcasted_iota(jnp.int32, (block, block), 0) <= lax.broadcasted_iota(
            jnp.int32, (block, block), 1
        )
        head_rows = aligned(head * HEAD, HEAD)
        for i in range(length // block):
            lo, hi = i * block, (i + 1) * block
            query = q[lo:hi, :] * (here * scale)
            upstream = datt[lo:hi, :] * here
            logsum = lse[pl.ds(head, 1), lo:hi]

            def part(at, end, mask):
                probs = jnp.exp(dot_nt(k[at:end, :], query) - logsum)
                if mask:
                    probs = jnp.where(visible, probs, 0.0)
                grads = dot_nt(v[at:end, :], upstream)
                dv[at:end, :] = dv[at:end, :] + dot(probs.astype(BF), upstream)
                return probs, grads, jnp.sum(probs * grads, 0, keepdims=True)

            def scored(at, end, probs, grads, inner):
                scores = (probs * (grads - inner)).astype(BF)
                dk[at:end, :] = dk[at:end, :] + dot(scores, query)
                return dot(kt[head_rows, at:end], scores)

            near, near_grads, inner = part(lo, hi, True)
            if i:
                far, far_grads, more = part(0, lo, False)
                inner = inner + more
            out = scored(lo, hi, near, near_grads, inner)
            if i:
                out = out + scored(0, lo, far, far_grads, inner)
            dqt[head_rows, lo:hi] = out * scale

    terms[...] = terms_in[...]
    bias_cols = aligned(net.s * columns, columns)

    @pl.loop(0, length // block)
    def _(i):
        span = aligned(i * block, block)
        tables = cosine[span, :], -sine[span, :]
        parts = [
            rotary(dqt[:, span].T.astype(BF).astype(F32), *tables).astype(BF),
            rotary(dk[span, :].astype(BF).astype(F32), *tables).astype(BF),
            dv[span, :].astype(BF),
        ]
        for kind in range(3):
            dproj[kind, span, :] = parts[kind]
            row = slice(4 + kind, 5 + kind)
            terms[row, bias_cols] = terms[row, bias_cols] + jnp.sum(parts[kind].astype(F32), 0, keepdims=True)

    def weight_terms(task):
        at = net.n_f - 1 - task // 2

        def loaded(way):
            load(at, way).wait()

        def next_load(way):
            pl.when(at >= 2)(lambda: load(at - 2, way).start())

        @pl.when(task % 2 == 0)
        def _():
            loaded(0)
            left = n1[at % 2].T
            for kind in range(3):
                qkv_sum.stage[at, kind * depth : (kind + 1) * depth, :] = dot(left, dproj[kind]).astype(BF)
            next_load(0)
            qkv_sum.first(at)

        @pl.when(task % 2 == 1)
        def _():
            loaded(1)
            out_sum.stage[at] = dot_tn(att[...], dm[at % 2]).astype(BF)
            next_load(1)
            out_sum.first(at)

    def produce(place, write):
        span = aligned(place * pair, pair)

        @pl.loop(0, width // TILE)
        def _(j):
            cols = aligned(j * TILE, TILE)
            value = dot_nt(dproj[0, span, :], wq[0, cols, :])
            for kind in range(1, 3):
                value = value + dot_nt(dproj[kind, span, :], wq[kind, cols, :])
            write(cols, value)

    fold = Fold(net, tiles, total, *buffers, *fold_sems)
    copies.wait()
    fold.begin(produce)
    fold.open_total()
    tasks = 2 * net.n_f
    waves = max(net.n_l - 2, 1)
    each = -(-tasks // (2 * fold.pieces * waves))

    def between(slot):
        @pl.loop(0, each)
        def _(i):
            pl.when(slot * each + i < tasks)(lambda: weight_terms(slot * each + i))

    for at in range(1, waves + 1):
        fold.wave(at, between=between)
    for at in range(waves + 1, net.n_l):
        fold.wave(at)

    def write_input(i, span, value):
        gin_o[span, :] = value + dmid[span, :]

    norm_backward(chunk, tok, total, gains[0:1, :], terms, 0, write_input)
    packet_sum = PacketSum(net, *packet_scratch)
    packet_sum.start(terms, width // (net.n_f * net.n_s))
    for grid_sum in (qkv_sum, out_sum):
        grid_sum.second()
    packet_sum.middle()
    for end, out in zip(ends, (down_o, gate_o, up_o)):
        end.last(out)
    packet_sum.finish(small_o)
    fold.finish()
    for grid_sum, out in ((qkv_sum, qkv_o), (out_sum, out_o)):
        grid_sum.last(out)
        grid_sum.finish()


def back_part(datt, q, k, kt, v, att, wq, n1, dm, down, gate, up, lse, tokens, dmid, gains, terms, tables):
    chunk, width = tokens.shape
    n_f, n_s = lax.axis_size("fsdp"), lax.axis_size("seq")
    length, columns = q.shape
    depth = width // n_f
    units = 2 * gate.shape[1]
    shape = jax.ShapeDtypeStruct
    return pl.pallas_call(
        back_kernel,
        name="back",
        out_shape=[
            shape((chunk, width), F32),
            shape((SMALL, 128), F32),
            shape((columns, depth), F32),
            shape((3 * depth, columns), F32),
            *[shape((units, depth), F32)] * 3,
        ],
        in_specs=[ANY] * 12 + [VMEM] * 7,
        out_specs=[VMEM] * 7,
        scratch_shapes=[
            pltpu.VMEM((length, columns), BF),
            pltpu.VMEM((length, columns), BF),
            pltpu.VMEM((length, columns), BF),
            pltpu.VMEM((columns, length), BF),
            pltpu.VMEM((length, columns), BF),
            pltpu.VMEM((length, columns), BF),
            pltpu.VMEM((3, width, columns), BF),
            pltpu.VMEM((2, length, depth), BF),
            pltpu.VMEM((2, length, depth), BF),
            pltpu.VMEM((length, columns), F32),
            pltpu.VMEM((length, columns), F32),
            pltpu.VMEM((columns, length), F32),
            pltpu.VMEM((3, length, columns), BF),
            pltpu.VMEM((SMALL, width), F32),
            *Fold.shared(chunk, width),
            *Fold.buffers(n_s, chunk, width),
            *Fold.sems(n_s),
            *PacketSum.scratch(n_f, n_s),
            *GridSum.scratch(n_f, columns, depth),
            *GridSum.scratch(n_f, 3 * depth, columns),
            *GridEnd.scratch(n_f, units, depth) * 3,
            pltpu.SemaphoreType.DMA((10,)),
            pltpu.SemaphoreType.DMA((2, 2)),
        ],
        compiler_params=pltpu.CompilerParams(
            collective_id=3, has_side_effects=True, vmem_limit_bytes=VMEM_BYTES
        ),
        cost_estimate=pl.CostEstimate(
            flops=2 * length * columns * (8 * width + 5 * length),
            bytes_accessed=4 * length * width,
            transcendentals=length * length * columns // HEAD,
        ),
    )(datt, q, k, kt, v, att, wq, n1, dm, down, gate, up, lse, tokens, dmid, gains, terms, *tables)


def per_device(
    tokens,
    gain_one,
    shift_one,
    w_qkv,
    b_qkv,
    w_out,
    gain_two,
    shift_two,
    w_gate,
    w_up,
    w_down,
    grad_output,
):
    length = tokens.shape[1] * lax.axis_size("seq")
    width = gain_one.shape[0]
    norms = [v[None] for v in (gain_one, shift_one, gain_two, shift_two)] + [b_qkv]
    tables = rotary_tables(length)
    q, k, kt, v, att, lse, n1, gains, wq, _, dm, datt, dmid, top, terms, gate, up, down = layer_part(
        tokens[0], norms, w_qkv.transpose(1, 0, 2), w_out, w_gate.T, w_up.T, w_down, grad_output[0], tables
    )
    grad_input, small, out, qkv, down, gate, up = back_part(
        datt, q, k, kt, v, att, wq, n1, dm, down, gate, up, lse, tokens[0], dmid, gains, terms, tables
    )

    return (
        top[None],
        grad_input[None],
        small[0, :width],
        small[1, :width],
        qkv.reshape(3, -1, qkv.shape[1]).transpose(1, 0, 2),
        small[4:7, :width],
        out,
        small[2, :width],
        small[3, :width],
        gate.T,
        up.T,
        down,
    )


def solution(mesh):
    whole = P(("fsdp", "seq"))
    rows = P("fsdp", "seq", None)
    inner = P("seq", "fsdp")
    outer = P("fsdp", "seq")
    heads = P("fsdp", None, "seq")
    bias = P(None, ("fsdp", "seq"))
    return jax.shard_map(
        per_device,
        mesh=mesh,
        in_specs=(rows, whole, whole, heads, bias, inner, whole, whole, outer, outer, inner, rows),
        out_specs=(rows, rows, whole, whole, heads, bias, inner, whole, whole, outer, outer, inner),
        check_vma=False,
    )
```

```python
import functools

import jax
import jax.numpy as jnp
import numpy as np
from jax import lax
from jax.experimental import pallas as pl
from jax.experimental.pallas import tpu as pltpu
from jax.sharding import PartitionSpec as P

HEAD = 64
ROT = 16
EPSILON = 1e-05
NEG_LARGE = -1e30
MESH = pl.DeviceIdType.MESH
ANY = pl.BlockSpec(memory_space=pl.ANY)
VMEM = pl.BlockSpec(memory_space=pltpu.VMEM)
BF = jnp.bfloat16
F32 = jnp.float32
VMEM_BYTES = 60 * 2**20
TILE = 512
SMALL = 8


def put(src, dst, send, recv, **device):
    return pltpu.make_async_remote_copy(
        src_ref=src, dst_ref=dst, send_sem=send, recv_sem=recv, device_id=device, device_id_type=MESH
    )


def dot(left, right):
    return jnp.dot(left, right, preferred_element_type=F32)


def dot_nt(left, right):
    return lax.dot_general(left, right, (((1,), (1,)), ((), ())), preferred_element_type=F32)


def dot_tn(left, right):
    return lax.dot_general(left, right, (((0,), (0,)), ((), ())), preferred_element_type=F32)


def aligned(start, size, unit=None):
    return pl.ds(pl.multiple_of(start, unit or size), size)


class Net:
    def __init__(self):
        self.n_f, self.n_s = lax.axis_size("fsdp"), lax.axis_size("seq")
        self.tall = 2 if self.n_f % 2 == 0 else 1
        self.wide = self.n_f // self.tall
        self.n_l = self.n_s // 2
        self.f, self.s = lax.axis_index("fsdp"), lax.axis_index("seq")
        self.a, self.b = self.f // self.wide, self.f % self.wide
        self.z, self.c = self.s // 2, self.s % 2
        self.mate = self.s + 1 - 2 * self.c

    def barrier(self):
        sem = pltpu.get_barrier_semaphore()
        for k in range(1, self.n_f):
            pl.semaphore_signal(
                sem, inc=1, device_id={"fsdp": (self.f + k) % self.n_f}, device_id_type=MESH
            )
        for k in range(1, self.n_s):
            pl.semaphore_signal(
                sem, inc=1, device_id={"seq": (self.s + k) % self.n_s}, device_id_type=MESH
            )
        pl.semaphore_wait(sem, self.n_f + self.n_s - 2)

    def sides(self, hop, act):
        @pl.loop(0, 2)
        def _(side):
            other = self.z + (2 * side - 1) * hop

            @pl.when((other >= 0) & (other < self.n_l))
            def _():
                act(other, side)


class Spread:
    def __init__(self, net, src, part, sems):
        self.net, self.src, self.part, self.sems = net, src, part, sems
        self.rows = [j for j in range(1, net.wide)]
        self.cols = [i for i in range(1, net.tall)]

    @staticmethod
    def count(n_f):
        tall = 2 if n_f % 2 == 0 else 1
        wide = n_f // tall
        return 1 + 2 * (wide - 1) + 2 * (tall - 1) + 4 * (wide - 1) * (tall - 1)

    def at(self, kind, i, j):
        w, t = len(self.rows), len(self.cols)
        base = {
            "own": 0,
            "row": 1,
            "col": 1 + 2 * w,
            "half0": 1 + 2 * w + 2 * t,
            "half1": 1 + 2 * w + 2 * t + 2 * w * t,
        }[kind]
        if kind == "own":
            return self.sems.at[0]
        k = j - 1 if kind == "row" else i - 1 if kind == "col" else (i - 1) * w + j - 1
        return self.sems.at[base + 2 * k], self.sems.at[base + 2 * k + 1]

    def rank(self, i, j):
        net = self.net
        return ((net.a + i) % net.tall) * net.wide + (net.b + j) % net.wide

    def back(self, i, j):
        net = self.net
        return ((net.a - i + net.tall) % net.tall) * net.wide + (net.b - j + net.wide) % net.wide

    def own(self):
        return pltpu.make_async_copy(self.src, self.part(self.net.f, None), self.at("own", 0, 0))

    def first(self, i, j):
        send, recv = self.at("row" if i == 0 else "col", i, j)
        place = self.part(self.net.f, None)
        return put(place, place, send, recv, fsdp=self.rank(i, j))

    def came(self, i, j):
        send, recv = self.at("row" if i == 0 else "col", i, j)
        place = self.part(self.back(i, j), None)
        return put(place, place, send, recv, fsdp=self.rank(i, j))

    def second(self, half, i, j, came=False):
        send, recv = self.at("half0" if half == 0 else "half1", i, j)
        origin = self.back(i, j) if came else self.back(0, j) if half == 0 else self.back(i, 0)
        place = self.part(origin, half)
        return put(place, place, send, recv, fsdp=self.rank(i, 0) if half == 0 else self.rank(0, j))

    def prepare(self):
        self.own().start()

    def start(self):
        self.own().wait()
        for i in self.cols:
            self.first(i, 0).start()
        for j in self.rows:
            self.first(0, j).start()

    def relay(self):
        for j in self.rows:
            self.came(0, j).wait_recv()
            for i in self.cols:
                self.second(0, i, j).start()
        for i in self.cols:
            self.came(i, 0).wait_recv()
            for j in self.rows:
                self.second(1, i, j).start()

    def finish(self):
        for j in self.rows:
            self.first(0, j).wait_send()
        for i in self.cols:
            self.first(i, 0).wait_send()
        for i in self.cols:
            for j in self.rows:
                for half in range(2):
                    self.second(half, i, j, came=True).wait_recv()
                    self.second(half, i, j).wait_send()


class Line:
    def __init__(self, net, src, part, recv, send, local):
        self.net, self.src, self.part, self.recv, self.send, self.local = net, src, part, recv, send, local
        self.pieces = recv.shape[1]
        self.rows = src.shape[0] // self.pieces

    @staticmethod
    def sems(n_s, pieces=2):
        return [
            pltpu.SemaphoreType.DMA((n_s, pieces)),
            pltpu.SemaphoreType.DMA((4, n_s // 2, pieces)),
            pltpu.SemaphoreType.DMA((1,)),
        ]

    def cut(self, ref, piece):
        return ref.at[aligned(piece * self.rows, self.rows)]

    def own(self):
        return pltpu.make_async_copy(self.src, self.part(self.net.s), self.local.at[0])

    def on_line(self, src, chunk, side, hop, piece):
        return put(
            self.cut(src, piece),
            self.cut(self.part(chunk), piece),
            self.send.at[side, hop, piece],
            self.recv.at[chunk, piece],
            seq=self.net.s + 2 - 4 * side,
        )

    def to_mate(self, src, chunk, side, hop, piece):
        return put(
            self.cut(src, piece),
            self.cut(self.part(chunk), piece),
            self.send.at[2 + side, hop, piece],
            self.recv.at[chunk, piece],
            seq=self.net.mate,
        )

    def goes_on(self, side):
        after = self.net.z + 1 - 2 * side
        return (after >= 0) & (after < self.net.n_l)

    def each_piece(self, act):
        pl.loop(0, self.pieces)(act)

    def prepare(self):
        self.own().start()

    def start(self):
        net = self.net
        self.own().wait()
        place = self.part(net.s)

        @self.each_piece
        def _(piece):
            for side in range(2):

                @pl.when(self.goes_on(side))
                def _():
                    self.on_line(place, net.s, side, 0, piece).start()

            self.to_mate(place, net.s, 0, 0, piece).start()

    def came(self, chunk, piece):
        place = self.cut(self.part(chunk), piece)
        put(place, place, self.send.at[0, 0, 0], self.recv.at[chunk, piece], seq=self.net.mate).wait_recv()

    def step(self, hop):
        net = self.net

        @self.each_piece
        def _(piece):
            def act(other, side):
                chunk = 2 * other + net.c
                self.came(chunk, piece)

                @pl.when(self.goes_on(side))
                def _():
                    self.on_line(self.part(chunk), chunk, side, hop, piece).start()

                self.to_mate(self.part(chunk), chunk, side, hop, piece).start()

            net.sides(hop, act)

    def pair(self, other):
        @self.each_piece
        def _(piece):
            self.came(2 * other + 1 - self.net.c, piece)

    def here(self):
        self.pair(self.net.z)

    def finish(self):
        net = self.net
        place = self.part(net.s)

        @self.each_piece
        def _(piece):
            for side in range(2):

                @pl.when(self.goes_on(side))
                def _():
                    self.on_line(place, net.s, side, 0, piece).wait_send()

            self.to_mate(place, net.s, 0, 0, piece).wait_send()

            @pl.loop(1, net.n_l)
            def _(hop):
                def act(other, side):
                    chunk = 2 * other + net.c

                    @pl.when(self.goes_on(side))
                    def _():
                        self.on_line(self.part(chunk), chunk, side, hop, piece).wait_send()

                    self.to_mate(self.part(chunk), chunk, side, hop, piece).wait_send()

                net.sides(hop, act)


class Packets:
    def __init__(self, net, src, buf, sems):
        self.net, self.src, self.buf, self.sems = net, src, buf, sems

    @staticmethod
    def count(n_f, n_s):
        return 1 + 2 * (n_f - 1) + 2 * (n_s - 1)

    def own(self):
        net = self.net
        return pltpu.make_async_copy(self.src, self.buf.at[net.s, net.f], self.sems.at[0])

    def one(self, k, came=False):
        net = self.net
        f = (net.f - k + net.n_f) % net.n_f if came else net.f
        place = self.buf.at[net.s, f]
        return put(
            place if came else self.src,
            place,
            self.sems.at[2 * k - 1],
            self.sems.at[2 * k],
            fsdp=(net.f + k) % net.n_f,
        )

    def two(self, k, came=False):
        net = self.net
        place = self.buf.at[(net.s - k + net.n_s) % net.n_s if came else net.s]
        at = 2 * (net.n_f - 1) + 2 * k - 1
        return put(place, place, self.sems.at[at], self.sems.at[at + 1], seq=(net.s + k) % net.n_s)

    def start(self):
        self.own().start()
        for k in range(1, self.net.n_f):
            self.one(k).start()

    def middle(self):
        self.own().wait()
        for k in range(1, self.net.n_f):
            self.one(k, came=True).wait_recv()
            self.one(k).wait_send()
        for k in range(1, self.net.n_s):
            self.two(k).start()

    def finish(self):
        for k in range(1, self.net.n_s):
            self.two(k, came=True).wait_recv()
            self.two(k).wait_send()

    def unpack(self, out, width):
        net = self.net
        per = 128 // width
        for tile in range(net.n_f * net.n_s // per):
            total = None
            for j in range(per):
                f, s = divmod(tile * per + j, net.n_s)
                piece = self.buf[s, f]
                if j:
                    piece = pltpu.roll(piece, j * width, axis=1)
                total = piece if total is None else total + piece
            out[:, tile * 128 : (tile + 1) * 128] = total


def rotary(values, cosine, sine):
    columns = values.shape[1]
    half = ROT // 2
    times = columns // 128

    def wide(table):
        return table if times == 1 else jnp.concatenate([table] * times, axis=1)

    lane = lax.broadcasted_iota(jnp.int32, values.shape, 1)
    other = jnp.where(
        lane % HEAD < half, pltpu.roll(values, columns - half, axis=1), pltpu.roll(values, half, axis=1)
    )
    return values * wide(cosine) + other * wide(sine)


def rotary_tables(length):
    half = ROT // 2
    freqs = np.float32(10000.0) ** (-np.arange(half, dtype=np.float32) * np.float32(2.0 / ROT))
    angles = np.arange(length, dtype=np.float32)[:, None] * freqs[None, :].astype(np.float32)
    cosine, sine = np.cos(angles), np.sin(angles)
    rest = np.zeros((length, HEAD - ROT), np.float32)
    keep = np.concatenate([cosine, cosine, rest + 1], 1)
    swap = np.concatenate([-sine, sine, rest], 1)
    return [np.tile(t, (1, 128 // HEAD)).astype(np.float32) for t in (keep, swap)]


def normalize(values):
    center = values - jnp.mean(values, -1, keepdims=True)
    inverse = lax.rsqrt(jnp.mean(center * center, -1, keepdims=True) + EPSILON)
    return center * inverse, inverse


class Copies:
    def __init__(self, sems):
        self.sems, self.all, self.open = sems, [], []

    def start(self, src, dst):
        copy = pltpu.make_async_copy(src, dst, self.sems.at[len(self.all)])
        copy.start()
        self.all.append(copy)
        self.open.append(copy)
        return copy

    def wait(self, *copies):
        for copy in copies or list(self.open):
            copy.wait()
            self.open = [c for c in self.open if c is not copy]


def columns_of(ref, depth):
    half_rows = ref.shape[0] // 2

    def part(f, half):
        span = aligned(f * depth, depth)
        if half is None:
            return ref.at[:, span]
        return ref.at[pl.ds(half * half_rows, half_rows), span]

    return part


def rows_of(ref, chunk):
    return lambda s: ref.at[aligned(s * chunk, chunk)]


class Fold:
    def __init__(self, net, tile, total, mate_in, coming, mate_out, out, mate_send, mate_recv, send, recv):
        self.net, self.tile, self.total = net, tile, total
        self.mate_in, self.coming, self.mate_out, self.out = mate_in, coming, mate_out, out
        self.mate_send, self.mate_recv, self.send, self.recv = mate_send, mate_recv, send, recv
        self.chunk = total.shape[0]
        self.pieces = recv.shape[1]
        self.rows = self.chunk // self.pieces

    @staticmethod
    def shared(chunk, width):
        return [pltpu.VMEM((2 * chunk, TILE), F32), pltpu.VMEM((chunk, width), F32)]

    @staticmethod
    def buffers(n_s, chunk, width):
        n_l = n_s // 2
        return [
            pltpu.VMEM((n_l, chunk, width), BF),
            pltpu.VMEM((n_l + 1, chunk, width), BF),
            pltpu.VMEM((3, chunk, width), BF),
            pltpu.VMEM((n_l, chunk, width), BF),
        ]

    @staticmethod
    def sems(n_s, pieces=4):
        n_l = n_s // 2
        return [
            pltpu.SemaphoreType.DMA((3, pieces)),
            pltpu.SemaphoreType.DMA((n_l, pieces)),
            pltpu.SemaphoreType.DMA((n_l, pieces)),
            pltpu.SemaphoreType.DMA((n_l + 1, pieces)),
        ]

    def place(self, other):
        return (other >= 0) & (other < self.net.n_l)

    def fed(self, side):
        return self.place(self.net.z + 1 - 2 * side)

    def span(self, piece):
        return aligned(piece * self.rows, self.rows)

    def each_piece(self, act):
        pl.loop(0, self.pieces)(act)

    def to_mate(self, target, slot, piece):
        span = self.span(piece)
        return put(
            self.mate_out.at[slot, span],
            self.mate_in.at[target, span],
            self.mate_send.at[slot, piece],
            self.mate_recv.at[target, piece],
            seq=self.net.mate,
        )

    def onward(self, target, side, hop, piece):
        span = self.span(piece)
        slot = target + (self.net.n_l - target) * (1 - side) * (1 // hop)
        return put(
            self.out.at[target, span],
            self.coming.at[slot, span],
            self.send.at[target, piece],
            self.recv.at[slot, piece],
            seq=self.net.s + 4 * side - 2,
        )

    def came(self, slot, piece):
        place = self.coming.at[slot, self.span(piece)]
        put(place, place, self.send.at[0, 0], self.recv.at[slot, piece], seq=self.net.mate).wait_recv()

    def mate_sent(self, slot):
        self.each_piece(lambda piece: self.to_mate(self.net.z, slot, piece).wait_send())

    def begin_one(self, target, slot, produce):
        mine = aligned(self.net.c * self.chunk, self.chunk)
        theirs = aligned((1 - self.net.c) * self.chunk, self.chunk)

        def write(cols, value):
            self.tile[...] = value
            self.out[target, :, cols] = self.tile[mine, :].astype(BF)
            self.mate_out[slot, :, cols] = self.tile[theirs, :].astype(BF)

        produce(target, write)
        self.each_piece(lambda piece: self.to_mate(target, slot, piece).start())

    def leave(self, target, side, hop):
        @pl.when((hop > 0) & jnp.logical_not(self.fed(side)))
        def _():
            self.each_piece(lambda piece: self.pass_piece(target, side, hop, piece, False))

    def begin(self, produce, between=None):
        net = self.net

        @pl.loop(0, net.n_l)
        def _(j):
            hop = net.n_l - 1 - j

            def act(target, side):
                @pl.when((hop > 0) | (side == 0))
                def _():
                    @pl.when((hop > 0) & self.place(target + 2 * side - 1))
                    def _():
                        self.mate_sent(side)

                    self.begin_one(target, side + (2 - side) * (1 // (hop + 1)), produce)
                    self.leave(target, side, hop)

            net.sides(hop, act)
            if between is not None:
                pl.when(j == 1)(between)

    def pass_piece(self, target, side, hop, piece, fed):
        self.to_mate(target, 0, piece).wait_recv()
        span = self.span(piece)
        value = self.out[target, span, :].astype(F32) + self.mate_in[target, span, :].astype(F32)
        if fed:
            self.came(target, piece)
            value = value + self.coming[target, span, :].astype(F32)
        self.out[target, span, :] = value.astype(BF)
        self.onward(target, side, hop, piece).start()

    def open_total(self):
        net = self.net

        @self.each_piece
        def _(piece):
            self.to_mate(net.z, 0, piece).wait_recv()
            span = self.span(piece)
            self.total[span, :] = self.out[net.z, span, :].astype(F32) + self.mate_in[net.z, span, :].astype(F32)

    def wave(self, at, near=False, between=None):
        net = self.net
        above = at if near else net.n_l - at

        @pl.loop(0, 2)
        def _(turn):
            side = (1 - (2 * net.z) // net.n_l + turn) % 2
            target = net.n_l - 1 - above + (2 * above - net.n_l + 1) * side
            hop = (target - net.z) * (2 * side - 1)

            @self.each_piece
            def _(piece):
                span = self.span(piece)

                @pl.when(self.fed(side) & (hop > 0))
                def _():
                    self.pass_piece(target, side, hop, piece, True)

                @pl.when(self.fed(side) & (hop == 0))
                def _():
                    slot = net.z + (net.n_l - net.z) * (1 - side)
                    self.came(slot, piece)
                    self.total[span, :] = self.total[span, :] + self.coming[slot, span, :].astype(F32)

                if between is not None:
                    between(((at - 1) * 2 + turn) * self.pieces + piece)

    def finish(self):
        net = self.net
        self.mate_sent(2)
        for side in range(2):
            pl.when(self.place(net.z + 2 * side - 1))(functools.partial(self.mate_sent, side))

        @pl.loop(1, net.n_l)
        def _(hop):
            net.sides(
                hop,
                lambda target, side: self.each_piece(
                    lambda piece: self.onward(target, side, hop, piece).wait_send()
                ),
            )


class GridSum:
    def __init__(self, net, stage, came, sems):
        self.net, self.stage, self.came, self.sems = net, stage, came, sems
        self.half = stage.shape[1] // 2
        self.rows = next(r for r in (176, 128, 96, 64, 32, 16) if self.half % r == 0)
        self.cols = range(1, net.tall)
        self.along = range(1, net.wide)
        self.bases = self.layout(net.n_f)

    @staticmethod
    def layout(n_f):
        tall = 2 if n_f % 2 == 0 else 1
        wide = n_f // tall
        sizes = [(wide - 1) * tall, (tall - 1) * wide, tall - 1, wide - 1]
        return [sum(sizes[:at]) for at in range(5)]

    @staticmethod
    def scratch(n_f, rows, columns):
        count = GridSum.layout(n_f)[4]
        return [
            pltpu.VMEM((n_f, rows, columns), BF),
            pltpu.VMEM((count, rows // 2, columns), BF),
            pltpu.SemaphoreType.DMA((2, count + GridEnd.count(n_f))),
        ]

    def slot(self, kind, i, j):
        base = self.bases[kind]
        return base + [(j - 1) * self.net.tall + i, (i - 1) * self.net.wide + j, i - 1, j - 1][kind]

    def rank(self, i, j):
        net = self.net
        return ((net.a + i) % net.tall) * net.wide + (net.b + j) % net.wide

    def owner(self, at):
        return self.rank(at // self.net.wide, at % self.net.wide)

    def copy(self, kind, i, j):
        half = kind % 2
        along = kind in (0, 3)
        slot = self.slot(kind, i, j)
        at = i * self.net.wide + j
        return put(
            self.stage.at[at, pl.ds(half * self.half, self.half)],
            self.came.at[slot],
            self.sems.at[0, slot],
            self.sems.at[1, slot],
            fsdp=self.rank(0, j) if along else self.rank(i, 0),
        )

    def first(self, at):
        i, j = at // self.net.wide, at % self.net.wide

        @pl.when(j > 0)
        def _():
            self.copy(0, i, j).start()

        @pl.when(i > 0)
        def _():
            self.copy(1, i, j).start()

    def gather(self, half, at, slots, write):
        @pl.loop(0, self.half // self.rows)
        def _(step):
            span = aligned(half * self.half + step * self.rows, self.rows, 16)
            value = self.stage[at, span, :].astype(F32)
            for slot in slots:
                value = value + self.came[slot, aligned(step * self.rows, self.rows, 16), :].astype(F32)
            write(span, value)

    def wait(self, *copies):
        for kind, i, j in copies:
            self.copy(kind, i, j).wait_recv()
        return [self.slot(*copy) for copy in copies]

    def second(self):
        def keep(at):
            def write(span, value):
                self.stage[at, span, :] = value.astype(BF)

            return write

        for i in self.cols:
            at = i * self.net.wide
            self.gather(0, at, self.wait(*[(0, i, j) for j in self.along]), keep(at))
            self.copy(2, i, 0).start()
        for j in self.along:
            self.gather(1, j, self.wait(*[(1, i, j) for i in self.cols]), keep(j))
            self.copy(3, 0, j).start()

    def sum_first(self):
        def keep(at):
            def write(span, value):
                self.stage[at, span, :] = value.astype(BF)

            return write

        for i in range(self.net.tall):
            at = i * self.net.wide
            self.gather(0, at, self.wait(*[(0, i, j) for j in self.along]), keep(at))
        for j in range(self.net.wide):
            self.gather(1, j, self.wait(*[(1, i, j) for i in self.cols]), keep(j))

    def hand_on(self, out):
        net = self.net
        shards = [(0, 0), (0, 1), *[(i * net.wide, 0) for i in self.cols], *[(j, 1) for j in self.along]]
        return [
            pltpu.make_async_copy(
                self.stage.at[at, pl.ds(half * self.half, self.half)], out.at[k], self.sems.at[0, self.bases[4] + k]
            )
            for k, (at, half) in enumerate(shards)
        ]

    def last(self, out):
        def write(span, value):
            out[span, :] = value

        self.gather(
            0, 0, self.wait(*[(0, 0, j) for j in self.along], *[(2, i, 0) for i in self.cols]), write
        )
        self.gather(
            1, 0, self.wait(*[(1, i, 0) for i in self.cols], *[(3, 0, j) for j in self.along]), write
        )

    def finish_first(self):
        for i in range(self.net.tall):
            for j in range(self.net.wide):
                if j:
                    self.copy(0, i, j).wait_send()
                if i:
                    self.copy(1, i, j).wait_send()

    def finish(self):
        self.finish_first()
        for i in self.cols:
            self.copy(2, i, 0).wait_send()
        for j in self.along:
            self.copy(3, 0, j).wait_send()


class GridEnd:
    def __init__(self, net, sums, came, sems):
        self.net, self.sums, self.came, self.sems = net, sums, came, sems

    @staticmethod
    def count(n_f):
        tall = 2 if n_f % 2 == 0 else 1
        return tall + n_f // tall

    @staticmethod
    def scratch(n_f, rows, columns):
        count = GridEnd.count(n_f)
        return [
            pltpu.VMEM((count, rows // 2, columns), BF),
            pltpu.VMEM((count - 2, rows // 2, columns), BF),
            pltpu.SemaphoreType.DMA((2, count - 2)),
        ]

    def copies(self):
        net = self.net
        f = [((net.a + i) % net.tall) * net.wide + net.b for i in range(1, net.tall)]
        f += [net.a * net.wide + (net.b + j) % net.wide for j in range(1, net.wide)]
        return [
            put(self.sums.at[2 + k], self.came.at[k], self.sems.at[0, k], self.sems.at[1, k], fsdp=to)
            for k, to in enumerate(f)
        ]

    def start(self):
        for copy in self.copies():
            copy.start()

    def last(self, out):
        for copy in self.copies():
            copy.wait()
        half = self.sums.shape[1]
        rows = next(r for r in (176, 128, 96, 64, 32, 16) if half % r == 0)
        down = range(self.net.tall - 1)
        along = range(self.net.tall - 1, self.net.tall + self.net.wide - 2)
        for at, slots in enumerate((down, along)):

            @pl.loop(0, half // rows)
            def _(step):
                span = aligned(step * rows, rows, 16)
                value = self.sums[at, span, :].astype(F32)
                for slot in slots:
                    value = value + self.came[slot, span, :].astype(F32)
                out[aligned(at * half + step * rows, rows, 16), :] = value


class PacketSum:
    def __init__(self, net, out, seq_in, total, fsdp_in, sems):
        self.net, self.out, self.seq_in, self.total, self.fsdp_in, self.sems = net, out, seq_in, total, fsdp_in, sems

    @staticmethod
    def scratch(n_f, n_s):
        return [
            pltpu.VMEM((n_s, n_f, SMALL, 128), F32),
            pltpu.VMEM((n_s, n_f, SMALL, 128), F32),
            pltpu.VMEM((n_f, SMALL, 128), F32),
            pltpu.VMEM((n_f, SMALL, 128), F32),
            pltpu.SemaphoreType.DMA((2 * (n_f + n_s),)),
        ]

    def one(self, k):
        to = (self.net.s + k) % self.net.n_s
        return put(self.out.at[to], self.seq_in.at[k], self.sems.at[2 * k], self.sems.at[2 * k + 1], seq=to)

    def two(self, k):
        to = (self.net.f + k) % self.net.n_f
        at = 2 * (self.net.n_s + k)
        return put(self.total.at[to], self.fsdp_in.at[k], self.sems.at[at], self.sems.at[at + 1], fsdp=to)

    def start(self, terms, width):
        net = self.net
        per = 128 // width
        for tile in range(net.n_f * net.n_s // per):
            value = terms[:, tile * 128 : (tile + 1) * 128]
            for j in range(per):
                f, s = divmod(tile * per + j, net.n_s)
                self.out[s, f] = pltpu.roll(value, 128 - j * width, axis=1) if j else value
        for k in range(1, net.n_s):
            self.one(k).start()

    def middle(self):
        net = self.net
        total = self.out[net.s]
        for k in range(1, net.n_s):
            self.one(k).wait()
            total = total + self.seq_in[k]
        self.total[...] = total
        for k in range(1, net.n_f):
            self.two(k).start()

    def finish(self, result):
        net = self.net
        total = self.total[net.f]
        for k in range(1, net.n_f):
            self.two(k).wait()
            total = total + self.fsdp_in[k]
        result[...] = total


def norm_backward(rows, source, grad, gain, terms, at, write):
    terms[at : at + 2, :] = jnp.zeros((2, terms.shape[1]), F32)

    @pl.loop(0, rows // 32)
    def _(i):
        span = aligned(i * 32, 32)
        scaled, inverse = normalize(source[span, :].astype(F32))
        value = grad[span, :]
        upstream = value * gain
        inner = jnp.mean(upstream, -1, keepdims=True)
        cross = jnp.mean(upstream * scaled, -1, keepdims=True)
        terms[at : at + 1, :] = terms[at : at + 1, :] + jnp.sum(value * scaled, 0, keepdims=True)
        terms[at + 1 : at + 2, :] = terms[at + 1 : at + 2, :] + jnp.sum(value, 0, keepdims=True)
        write(i, span, inverse * (upstream - inner - scaled * cross))


def layer_kernel(
    tok,
    gain_one,
    shift_one,
    gain_two,
    shift_two,
    bias,
    wq_own,
    wo_own,
    wg_own,
    wu_own,
    wd_own,
    gout_own,
    cosine,
    sine,
    q_o,
    k_o,
    kt_o,
    v_o,
    att_o,
    lse_o,
    n1_o,
    gains_o,
    wq_o,
    wo_o,
    dm_o,
    datt_o,
    dmid_o,
    top_o,
    terms_o,
    gate_o,
    up_o,
    down_o,
    rows,
    gout,
    wq,
    wo,
    wg,
    wu,
    wd,
    q,
    k,
    kt,
    v,
    vt,
    ot,
    att,
    hidden,
    dgate,
    dup,
    mid,
    low,
    packet,
    packets,
    tiles,
    total,
    *rest,
):
    net = Net()
    chunk, width = tok.shape
    length = chunk * net.n_s
    depth = wq_own.shape[1]
    columns = wq_own.shape[2]
    heads = columns // HEAD
    pair = 2 * chunk
    buffers, rest = rest[:4], rest[4:]
    folds = []
    for _ in range(3):
        folds.append(Fold(net, tiles, total, *buffers, *rest[:4]))
        rest = rest[4:]
    att_fold, normed_fold, top_fold = folds
    line_sems = [rest[at : at + 3] for at in (0, 3, 6, 9)]
    rest = rest[12:]
    spread_sems, rest = rest[:5], rest[5:]
    gate_sum, up_sum, down_sum = [GridSum(net, *rest[at : at + 3]) for at in (0, 3, 6)]
    sums = (down_sum, gate_sum, up_sum)
    pk_sems, copy_sems, n1_sems, free_sem = rest[9:]
    copies = Copies(copy_sems)
    n1 = att_fold.mate_out

    packet[...] = jnp.zeros(packet.shape, F32)
    own = gain_one.shape[1]
    for at, part in enumerate((gain_one, shift_one, gain_two, shift_two)):
        packet[at : at + 1, 0:own] = part[...].astype(F32)
    packet[4:7, 0:own] = bias[...].astype(F32)
    def wq_part(f, half):
        if half is None:
            return wq.at[:, aligned(f * depth, depth), :]
        return wq.at[:, aligned(f * depth + half * (depth // 2), depth // 2), :]

    spread_q = Spread(net, wq_own, wq_part, spread_sems[0])
    spread_o, spread_g, spread_u, spread_d = [
        Spread(net, own, columns_of(full, depth), sems)
        for own, full, sems in zip((wo_own, wg_own, wu_own, wd_own), (wo, wg, wu, wd), spread_sems[1:])
    ]
    pk = Packets(net, packet, packets, pk_sems)
    line = Line(net, tok, rows_of(rows, chunk), *line_sems[0])
    gout_line = Line(net, gout_own, rows_of(gout, chunk), *line_sems[1])
    n2_line = Line(net, low, rows_of(rows, chunk), *line_sems[2])
    dm_line = Line(net, low, rows_of(rows, chunk), *line_sems[3])

    for ready in (line, spread_q, spread_o, spread_g, spread_u, spread_d, gout_line):
        ready.prepare()
    net.barrier()

    def pairs(which, hop):
        net.sides(hop, lambda other, side: which.pair(other))

    def blocks(hop, act):
        def once(other, side):
            @pl.when((hop > 0) | (side == 0))
            def _():
                act(other, side)

        net.sides(hop, once)

    pk.start()
    line.start()
    spread_q.start()
    pk.middle()
    pk.finish()
    pk.unpack(gains_o, width // (net.n_f * net.n_s))

    def project_block(other, side):
        span = aligned(other * pair, pair)
        gain, shift = gains_o[0:1, :], gains_o[1:2, :]

        for part in range(2):

            @pl.loop(0, chunk // 32)
            def _(i):
                at = aligned((2 * other + part) * chunk + i * 32, 32)
                scaled, _ = normalize(rows[at, :].astype(F32))
                n1[part, aligned(i * 32, 32), :] = (scaled * gain + shift).astype(BF)

        keeps = [
            pltpu.make_async_copy(
                n1.at[part], n1_o.at[aligned((2 * other + part) * chunk, chunk)], n1_sems.at[part]
            )
            for part in range(2)
        ]
        for copy in keeps:
            copy.start()
        left = n1[0:2].reshape(pair, width)
        cols = aligned(net.s * columns, columns)
        tables = cosine[span, :], sine[span, :]
        for kind in range(3):
            value = dot(left, wq[kind]) + gains_o[4 + kind : 5 + kind, cols]
            if kind == 0:
                q[span, :] = rotary(value, *tables).astype(BF)
            elif kind == 1:
                value = rotary(value, *tables)
                k[span, :] = value.astype(BF)
                kt[...] = value.T.astype(BF)
            else:
                v[...] = value.astype(BF)
                vt[:, span] = value.T.astype(BF)
        for copy in (
            pltpu.make_async_copy(kt, kt_o.at[:, span], n1_sems.at[2]),
            pltpu.make_async_copy(v, v_o.at[span], n1_sems.at[3]),
        ):
            copy.start()
            keeps.append(copy)
        for copy in keeps:
            copy.wait()

    line.here()
    for hop in range(1, net.n_l - 1):
        line.step(hop)
        if hop == 1:
            spread_q.relay()
        pairs(line, hop)
    spread_o.start()
    spread_q.finish()
    spread_g.start()
    pl.loop(0, net.n_l - 1)(lambda hop: blocks(hop, project_block))
    spread_o.relay()
    spread_u.start()
    line.step(net.n_l - 1)
    gout_line.start()
    pairs(line, net.n_l - 1)
    blocks(net.n_l - 1, project_block)
    spread_d.start()
    q_copy = copies.start(q, q_o)
    for pair_of in ((wq, wq_o), (k, k_o)):
        copies.start(*pair_of)
    spread_o.finish()
    line.finish()

    def attend(i):
        lo, hi = i * pair, (i + 1) * pair

        @pl.loop(0, heads)
        def _(head):
            lane = lax.broadcasted_iota(jnp.int32, (1, columns), 1)
            here = jnp.where(lane // HEAD == head, HEAD**-0.5, 0.0).astype(BF)
            visible = lax.broadcasted_iota(jnp.int32, (pair, pair), 0) <= lax.broadcasted_iota(
                jnp.int32, (pair, pair), 1
            )
            head_rows = aligned(head * HEAD, HEAD)
            query = q[lo:hi, :] * here
            near = jnp.where(visible, dot_nt(k[lo:hi, :], query), NEG_LARGE)
            highest = jnp.max(near, 0, keepdims=True)
            if i:
                far = dot_nt(k[0:lo, :], query)
                highest = jnp.maximum(highest, jnp.max(far, 0, keepdims=True))
            near = jnp.exp(near - highest)
            sum_of = jnp.sum(near, 0, keepdims=True)
            out = dot(vt[head_rows, lo:hi], near.astype(BF))
            if i:
                far = jnp.exp(far - highest)
                sum_of = sum_of + jnp.sum(far, 0, keepdims=True)
                out = out + dot(vt[head_rows, 0:lo], far.astype(BF))
            ot[head_rows, :] = out / sum_of
            lse_o[pl.ds(head, 1), lo:hi] = highest + jnp.log(sum_of)

        att[lo:hi, :] = ot[...].T.astype(BF)

    def produce_attended(place, write):
        for i in range(net.n_l):
            pl.when(place == i)(functools.partial(attend, i))
        left = att[aligned(place * pair, pair), :]

        @pl.loop(0, width // TILE)
        def _(j):
            cols = aligned(j * TILE, TILE)
            write(cols, dot(left, wo[:, cols]))

    def relays():
        gout_line.step(1)
        spread_g.relay()

    att_fold.begin(produce_attended, relays)
    copies.start(att, att_o)
    copies.start(wo, wo_o)
    att_fold.open_total()
    for at in range(1, net.n_l):
        att_fold.wave(at)
        if at + 1 < net.n_l:
            gout_line.step(at + 1)
        if at == 1:
            spread_u.relay()
        if at == min(2, net.n_l - 1):
            spread_d.relay()
    gain_two, shift_two = gains_o[2:3, :], gains_o[3:4, :]

    @pl.loop(0, chunk // 32)
    def _(i):
        span = aligned(i * 32, 32)
        value = rows[aligned(net.s * chunk + i * 32, 32), :].astype(F32) + total[span, :]
        mid[span, :] = value
        scaled, _ = normalize(value)
        low[span, :] = (scaled * gain_two + shift_two).astype(BF)

    n2_line.prepare()
    n2_line.start()
    att_fold.finish()
    gout_line.here()
    pl.loop(1, net.n_l)(lambda hop: pairs(gout_line, hop))

    def forward_block(other):
        span = aligned(other * pair, pair)
        right = rows[span, :]
        half = hidden.shape[0] // 2

        @pl.loop(0, 2)
        def _(part):
            units = aligned(part * half, half, 16)
            gate = dot_nt(wg[units, :], right)
            up = dot_nt(wu[units, :], right)
            back = dot_nt(wd[units, :], gout[span, :])
            sigma = jax.nn.sigmoid(gate)
            active = gate * sigma
            hidden[units, span] = (active * up).astype(BF)
            dgate[units, span] = (back * up * (sigma * (1.0 + gate * (1.0 - sigma)))).astype(BF)
            dup[units, span] = (back * active).astype(BF)

    def produce_normed(place, write):
        span = aligned(place * pair, pair)
        left, right = dgate[:, span].T, dup[:, span].T

        @pl.loop(0, width // TILE)
        def _(j):
            cols = aligned(j * TILE, TILE)
            write(cols, dot(left, wg[:, cols]) + dot(right, wu[:, cols]))

    def begin_normed(other, side, hop):
        @pl.when(hop > 1)
        def _():
            normed_fold.mate_sent(side)

        normed_fold.begin_one(other, side + (2 - side) * (1 // (hop + 1)), produce_normed)

    def forward_blocks(hop):
        def act(other, side):
            forward_block(other)

            @pl.when(jnp.logical_not(normed_fold.fed(side)))
            def _():
                begin_normed(other, side, hop)
                normed_fold.leave(other, side, hop)

        net.sides(hop, act)

    def begin_fed(hop):
        def act(other, side):
            @pl.when((hop == 0) | normed_fold.fed(side))
            def _():
                begin_normed(other, side, hop)

        blocks(hop, act)

    n2_line.here()
    for spread in (spread_g, spread_u, spread_d):
        spread.finish()
    forward_block(net.z)

    @pl.loop(1, net.n_l)
    def _(hop):
        n2_line.step(hop)
        pairs(n2_line, hop)
        forward_blocks(hop)
        begin_fed(hop - 1)

    begin_fed(net.n_l - 1)
    normed_fold.open_total()

    def weight_terms(task):
        at, kind = net.n_f - 1 - task // 3, task % 3
        cols = aligned(gate_sum.owner(at) * depth, depth)
        for way, (grid_sum, left, right) in enumerate(
            ((down_sum, hidden, gout), (gate_sum, dgate, rows), (up_sum, dup, rows))
        ):

            @pl.when(kind == way)
            def _():
                half = left.shape[0] // 2

                @pl.loop(0, 2)
                def _(part):
                    units = aligned(part * half, half, 16)
                    grid_sum.stage[at, units, :] = dot(left[units, :], right[:, cols]).astype(BF)

                grid_sum.first(at)

    tasks = 3 * net.n_f
    slots = 2 * normed_fold.pieces * (net.n_l - 1)
    each = -(-tasks // slots)

    def between(slot):
        @pl.loop(0, each)
        def _(i):
            pl.when(slot * each + i < tasks)(lambda: weight_terms(slot * each + i))

    for at in range(1, net.n_l):
        normed_fold.wave(at, near=True, between=between)
    n2_line.finish()

    def beside(act):
        act(net.mate)
        for side in range(2):
            pl.when(n2_line.goes_on(side))(lambda: act(net.s + 2 - 4 * side))

    beside(lambda to: pl.semaphore_signal(free_sem, 1, device_id={"seq": to}, device_id_type=MESH))

    def write_middle(i, span, value):
        value = value + gout[aligned(net.s * chunk + i * 32, 32), :].astype(F32)
        dmid_o[span, :] = value
        low[span, :] = value.astype(BF)

    terms_o[...] = jnp.zeros(terms_o.shape, F32)
    norm_backward(chunk, mid, total, gain_two, terms_o, 2, write_middle)
    ends = (net.z + net.n_l - 1) // net.n_l + (2 * net.n_l - 2 - net.z) // net.n_l
    pl.semaphore_wait(free_sem, 1 + ends)
    dm_line.prepare()
    dm_line.start()
    normed_fold.finish()

    def produce_top(place, write):
        left = hidden[:, aligned(place * pair, pair)].T

        @pl.loop(0, width // TILE)
        def _(j):
            cols = aligned(j * TILE, TILE)
            write(cols, dot(left, wd[:, cols]))

    copies.wait(q_copy)
    datt = q

    def back_block(other, side):
        span = aligned(other * pair, pair)
        datt[span, :] = dot_nt(rows[span, :], wo[...]).astype(BF)

    dm_line.here()
    dm_line.step(1)
    top_fold.begin(produce_top)
    back_block(net.z, 0)
    top_fold.open_total()
    for at in range(1, net.n_l):
        if at + 1 < net.n_l:
            dm_line.step(at + 1)
        top_fold.wave(at)
        pairs(dm_line, at)
        net.sides(at, back_block)
    copies.start(datt, datt_o)
    copies.start(rows, dm_o)

    @pl.loop(0, chunk // 32)
    def _(i):
        span = aligned(i * 32, 32)
        top_fold.out[net.z, span, :] = (mid[span, :] + total[span, :]).astype(BF)

    copies.start(top_fold.out.at[net.z], top_o)
    top_fold.finish()
    gout_line.finish()
    dm_line.finish()
    hands = []
    for grid_sum, out in zip(sums, (down_o, gate_o, up_o)):
        grid_sum.sum_first()
        hands.extend(grid_sum.hand_on(out))
        for copy in grid_sum.hand_on(out):
            copy.start()
    for grid_sum in sums:
        grid_sum.finish_first()
    for copy in hands:
        copy.wait()
    copies.wait()


def layer_part(tokens, norms, wq, wo, wg, wu, wd, gout, tables):
    chunk, width = tokens.shape
    n_f, n_s = lax.axis_size("fsdp"), lax.axis_size("seq")
    length = chunk * n_s
    depth, columns = wq.shape[1:]
    units = wg.shape[0]
    shape = jax.ShapeDtypeStruct
    wide, head, turned, weight = (length, width), (length, columns), (units, length), (units, width)
    return pl.pallas_call(
        layer_kernel,
        name="layer",
        out_shape=[
            shape(head, BF),
            shape(head, BF),
            shape((columns, length), BF),
            shape(head, BF),
            shape(head, BF),
            shape((8, length), F32),
            shape(wide, BF),
            shape((SMALL, width), F32),
            shape((3, width, columns), BF),
            shape((columns, width), BF),
            shape(wide, BF),
            shape(head, BF),
            shape((chunk, width), F32),
            shape((chunk, width), BF),
            shape((SMALL, width), F32),
            *[shape((GridEnd.count(n_f), units // 2, depth), BF)] * 3,
        ],
        in_specs=[ANY, *[VMEM] * 5, *[ANY] * 6, VMEM, VMEM],
        out_specs=[*[ANY] * 5, VMEM, ANY, VMEM, *[ANY] * 4, VMEM, ANY, VMEM, *[ANY] * 3],
        scratch_shapes=[
            pltpu.VMEM(wide, BF),
            pltpu.VMEM(wide, BF),
            pltpu.VMEM((3, width, columns), BF),
            pltpu.VMEM((columns, width), BF),
            *[pltpu.VMEM(weight, BF)] * 3,
            pltpu.VMEM(head, BF),
            pltpu.VMEM(head, BF),
            pltpu.VMEM((columns, 2 * chunk), BF),
            pltpu.VMEM((2 * chunk, columns), BF),
            pltpu.VMEM((columns, length), BF),
            pltpu.VMEM((columns, 2 * chunk), F32),
            pltpu.VMEM(head, BF),
            *[pltpu.VMEM(turned, BF)] * 3,
            pltpu.VMEM((chunk, width), F32),
            pltpu.VMEM((chunk, width), BF),
            pltpu.VMEM((SMALL, 128), F32),
            pltpu.VMEM((n_s, n_f, SMALL, 128), F32),
            *Fold.shared(chunk, width),
            *Fold.buffers(n_s, chunk, width),
            *Fold.sems(n_s) * 3,
            *Line.sems(n_s) * 4,
            *[pltpu.SemaphoreType.DMA((Spread.count(n_f),))] * 5,
            *GridSum.scratch(n_f, units, depth) * 3,
            pltpu.SemaphoreType.DMA((Packets.count(n_f, n_s),)),
            pltpu.SemaphoreType.DMA((8,)),
            pltpu.SemaphoreType.DMA((4,)),
            pltpu.SemaphoreType.REGULAR,
        ],
        compiler_params=pltpu.CompilerParams(
            collective_id=1, has_side_effects=True, vmem_limit_bytes=VMEM_BYTES
        ),
        cost_estimate=pl.CostEstimate(
            flops=2 * length * width * (4 * columns + 9 * units),
            bytes_accessed=8 * length * width,
            transcendentals=length * (length * columns // HEAD + units),
        ),
    )(tokens, *norms, wq, wo, wg, wu, wd, gout, *tables)


def back_kernel(
    datt_in,
    q_in,
    k_in,
    kt_in,
    v_in,
    att_in,
    wq_in,
    n1_in,
    dm_in,
    down_in,
    gate_in,
    up_in,
    lse,
    tok,
    dmid,
    gains,
    terms_in,
    cosine,
    sine,
    gin_o,
    small_o,
    out_o,
    qkv_o,
    down_o,
    gate_o,
    up_o,
    datt,
    q,
    k,
    kt,
    v,
    att,
    wq,
    n1,
    dm,
    query,
    upstream,
    inners,
    dk,
    dv,
    dqt,
    dproj,
    terms,
    tiles,
    total,
    *rest,
):
    net = Net()
    chunk, width = tok.shape
    length, columns = q_in.shape
    heads = columns // HEAD
    pair = 2 * chunk
    depth = width // net.n_f
    block = 256
    buffers, rest = rest[:4], rest[4:]
    fold_sems, rest = rest[:4], rest[4:]
    packet_scratch, rest = rest[:5], rest[5:]
    out_sum, qkv_sum = GridSum(net, *rest[:3]), GridSum(net, *rest[3:6])
    ends = [GridEnd(net, *rest[at : at + 3]) for at in (6, 9, 12)]
    copy_sems, column_sems = rest[15:]

    copies = Copies(copy_sems)
    loads = [
        copies.start(src, dst)
        for src, dst in (
            (datt_in, datt),
            (q_in, q),
            (k_in, k),
            (kt_in, kt),
            (v_in, v),
            (att_in, att),
            (wq_in, wq),
            (down_in, ends[0].sums),
            (gate_in, ends[1].sums),
            (up_in, ends[2].sums),
        )
    ]
    def load(at, way):
        src, dst = ((n1_in, n1), (dm_in, dm))[way]
        cols = aligned(qkv_sum.owner(at) * depth, depth)
        return pltpu.make_async_copy(src.at[:, cols], dst.at[at % 2], column_sems.at[way, at % 2])

    for at in range(net.n_f - 1, max(net.n_f - 3, -1), -1):
        for way in range(2):
            load(at, way).start()

    @pl.loop(0, length // block)
    def _(i):
        span = aligned(i * block, block)
        dk[span, :] = jnp.zeros((block, columns), F32)
        dv[span, :] = jnp.zeros((block, columns), F32)

    net.barrier()
    copies.wait(*loads[7:])
    for end in ends:
        end.start()
    copies.wait(*loads[:6])

    of_head = (
        lax.broadcasted_iota(jnp.int32, (8, columns), 1) // HEAD
        == lax.broadcasted_iota(jnp.int32, (8, columns), 0)
    ).astype(F32)

    @pl.loop(0, length // block)
    def _(i):
        span = aligned(i * block, block)
        product = datt[span, :].astype(F32) * att[span, :].astype(F32)
        inners[:, span] = lax.dot_general(
            of_head,
            product,
            (((1,), (1,)), ((), ())),
            precision=lax.Precision.HIGHEST,
            preferred_element_type=F32,
        )

    @pl.loop(0, heads)
    def _(head):
        lane = lax.broadcasted_iota(jnp.int32, (1, columns), 1)
        here = jnp.where(lane // HEAD == head, 1.0, 0.0).astype(BF)
        scale = HEAD**-0.5
        visible = lax.broadcasted_iota(jnp.int32, (block, block), 0) <= lax.broadcasted_iota(
            jnp.int32, (block, block), 1
        )
        head_rows = aligned(head * HEAD, HEAD)

        @pl.loop(0, length // block)
        def _(i):
            span = aligned(i * block, block)
            query[span, :] = q[span, :] * (here * scale)
            upstream[span, :] = datt[span, :] * here

        for j in range(length // block):
            at, end = j * block, (j + 1) * block
            keys, values, turned = k[at:end, :], v[at:end, :], kt[head_rows, at:end]

            def part(lo, hi, near):
                probs = jnp.exp(dot_nt(keys, query[lo:hi, :]) - lse[pl.ds(head, 1), lo:hi])
                if near:
                    probs = jnp.where(visible, probs, 0.0)
                grads = dot_nt(values, upstream[lo:hi, :])
                scores = (probs * (grads - inners[pl.ds(head, 1), lo:hi])).astype(BF)
                out = dot(turned, scores)
                dqt[head_rows, lo:hi] = dqt[head_rows, lo:hi] + out if j else out
                return dot(probs.astype(BF), upstream[lo:hi, :]), dot(scores, query[lo:hi, :])

            value_grads, key_grads = part(at, end, True)
            if end < length:
                more_values, more_keys = part(end, length, False)
                value_grads, key_grads = value_grads + more_values, key_grads + more_keys
            dv[at:end, :] = dv[at:end, :] + value_grads
            dk[at:end, :] = dk[at:end, :] + key_grads

    terms[...] = terms_in[...]
    bias_cols = aligned(net.s * columns, columns)

    @pl.loop(0, length // block)
    def _(i):
        span = aligned(i * block, block)
        tables = cosine[span, :], -sine[span, :]
        parts = [
            rotary((dqt[:, span].T * HEAD**-0.5).astype(BF).astype(F32), *tables).astype(BF),
            rotary(dk[span, :].astype(BF).astype(F32), *tables).astype(BF),
            dv[span, :].astype(BF),
        ]
        for kind in range(3):
            dproj[kind, span, :] = parts[kind]
            row = slice(4 + kind, 5 + kind)
            terms[row, bias_cols] = terms[row, bias_cols] + jnp.sum(parts[kind].astype(F32), 0, keepdims=True)

    def weight_terms(task):
        at = net.n_f - 1 - task // 2

        def loaded(way):
            load(at, way).wait()

        def next_load(way):
            pl.when(at >= 2)(lambda: load(at - 2, way).start())

        @pl.when(task % 2 == 0)
        def _():
            loaded(0)
            left = n1[at % 2].T
            for kind in range(3):
                qkv_sum.stage[at, kind * depth : (kind + 1) * depth, :] = dot(left, dproj[kind]).astype(BF)
            next_load(0)
            qkv_sum.first(at)

        @pl.when(task % 2 == 1)
        def _():
            loaded(1)
            out_sum.stage[at] = dot_tn(att[...], dm[at % 2]).astype(BF)
            next_load(1)
            out_sum.first(at)

    def produce(place, write):
        span = aligned(place * pair, pair)

        @pl.loop(0, width // TILE)
        def _(j):
            cols = aligned(j * TILE, TILE)
            value = dot_nt(dproj[0, span, :], wq[0, cols, :])
            for kind in range(1, 3):
                value = value + dot_nt(dproj[kind, span, :], wq[kind, cols, :])
            write(cols, value)

    fold = Fold(net, tiles, total, *buffers, *fold_sems)
    copies.wait()
    fold.begin(produce)
    fold.open_total()
    tasks = 2 * net.n_f
    waves = max(net.n_l - 2, 1)
    each = -(-tasks // (2 * fold.pieces * waves))

    def between(slot):
        @pl.loop(0, each)
        def _(i):
            pl.when(slot * each + i < tasks)(lambda: weight_terms(slot * each + i))

    for at in range(1, waves + 1):
        fold.wave(at, between=between)
    for at in range(waves + 1, net.n_l):
        fold.wave(at)

    def write_input(i, span, value):
        gin_o[span, :] = value + dmid[span, :]

    norm_backward(chunk, tok, total, gains[0:1, :], terms, 0, write_input)
    packet_sum = PacketSum(net, *packet_scratch)
    packet_sum.start(terms, width // (net.n_f * net.n_s))
    for grid_sum in (qkv_sum, out_sum):
        grid_sum.second()
    packet_sum.middle()
    for end, out in zip(ends, (down_o, gate_o, up_o)):
        end.last(out)
    packet_sum.finish(small_o)
    fold.finish()
    for grid_sum, out in ((qkv_sum, qkv_o), (out_sum, out_o)):
        grid_sum.last(out)
        grid_sum.finish()


def back_part(datt, q, k, kt, v, att, wq, n1, dm, down, gate, up, lse, tokens, dmid, gains, terms, tables):
    chunk, width = tokens.shape
    n_f, n_s = lax.axis_size("fsdp"), lax.axis_size("seq")
    length, columns = q.shape
    depth = width // n_f
    units = 2 * gate.shape[1]
    shape = jax.ShapeDtypeStruct
    return pl.pallas_call(
        back_kernel,
        name="back",
        out_shape=[
            shape((chunk, width), F32),
            shape((SMALL, 128), F32),
            shape((columns, depth), F32),
            shape((3 * depth, columns), F32),
            *[shape((units, depth), F32)] * 3,
        ],
        in_specs=[ANY] * 12 + [VMEM] * 7,
        out_specs=[VMEM] * 7,
        scratch_shapes=[
            pltpu.VMEM((length, columns), BF),
            pltpu.VMEM((length, columns), BF),
            pltpu.VMEM((length, columns), BF),
            pltpu.VMEM((columns, length), BF),
            pltpu.VMEM((length, columns), BF),
            pltpu.VMEM((length, columns), BF),
            pltpu.VMEM((3, width, columns), BF),
            pltpu.VMEM((2, length, depth), BF),
            pltpu.VMEM((2, length, depth), BF),
            pltpu.VMEM((length, columns), BF),
            pltpu.VMEM((length, columns), BF),
            pltpu.VMEM((8, length), F32),
            pltpu.VMEM((length, columns), F32),
            pltpu.VMEM((length, columns), F32),
            pltpu.VMEM((columns, length), F32),
            pltpu.VMEM((3, length, columns), BF),
            pltpu.VMEM((SMALL, width), F32),
            *Fold.shared(chunk, width),
            *Fold.buffers(n_s, chunk, width),
            *Fold.sems(n_s),
            *PacketSum.scratch(n_f, n_s),
            *GridSum.scratch(n_f, columns, depth),
            *GridSum.scratch(n_f, 3 * depth, columns),
            *GridEnd.scratch(n_f, units, depth) * 3,
            pltpu.SemaphoreType.DMA((10,)),
            pltpu.SemaphoreType.DMA((2, 2)),
        ],
        compiler_params=pltpu.CompilerParams(
            collective_id=3, has_side_effects=True, vmem_limit_bytes=VMEM_BYTES
        ),
        cost_estimate=pl.CostEstimate(
            flops=2 * length * columns * (8 * width + 5 * length),
            bytes_accessed=4 * length * width,
            transcendentals=length * length * columns // HEAD,
        ),
    )(datt, q, k, kt, v, att, wq, n1, dm, down, gate, up, lse, tokens, dmid, gains, terms, *tables)


def outputs_kernel(small, *refs):
    sources, targets, parts = refs[:7], refs[7:14], refs[14:]
    own = parts[0].shape[1]
    for src, dst in zip(sources, targets):
        dst[...] = src[...]
    for at in range(4):
        parts[at][...] = small[at : at + 1, 0:own]
    parts[4][...] = small[4:7, 0:own]


def outputs_part(small, own, *arrays):
    shape = jax.ShapeDtypeStruct
    return pl.pallas_call(
        outputs_kernel,
        name="outputs",
        out_shape=[shape(v.shape, v.dtype) for v in arrays]
        + [shape((1, own), F32)] * 4
        + [shape((3, own), F32)],
        in_specs=[VMEM] * 8,
        out_specs=[VMEM] * 12,
        compiler_params=pltpu.CompilerParams(vmem_limit_bytes=VMEM_BYTES),
    )(small, *arrays)


def per_device(
    tokens,
    gain_one,
    shift_one,
    w_qkv,
    b_qkv,
    w_out,
    gain_two,
    shift_two,
    w_gate,
    w_up,
    w_down,
    grad_output,
):
    length = tokens.shape[1] * lax.axis_size("seq")
    width = gain_one.shape[0]
    norms = [v[None] for v in (gain_one, shift_one, gain_two, shift_two)] + [b_qkv]
    tables = rotary_tables(length)
    q, k, kt, v, att, lse, n1, gains, wq, _, dm, datt, dmid, top, terms, gate, up, down = layer_part(
        tokens[0], norms, w_qkv.transpose(1, 0, 2), w_out, w_gate.T, w_up.T, w_down, grad_output[0], tables
    )
    grad_input, small, out, qkv, down, gate, up = back_part(
        datt, q, k, kt, v, att, wq, n1, dm, down, gate, up, lse, tokens[0], dmid, gains, terms, tables
    )

    top, grad_input, qkv, out, gate, up, down, one, shift, two, shift_to, bias = outputs_part(
        small, width, top, grad_input, qkv, out, gate, up, down
    )
    return (
        top[None],
        grad_input[None],
        one[0],
        shift[0],
        qkv.reshape(3, -1, qkv.shape[1]).transpose(1, 0, 2),
        bias,
        out,
        two[0],
        shift_to[0],
        gate.T,
        up.T,
        down,
    )


def solution(mesh):
    whole = P(("fsdp", "seq"))
    rows = P("fsdp", "seq", None)
    inner = P("seq", "fsdp")
    outer = P("fsdp", "seq")
    heads = P("fsdp", None, "seq")
    bias = P(None, ("fsdp", "seq"))
    return jax.shard_map(
        per_device,
        mesh=mesh,
        in_specs=(rows, whole, whole, heads, bias, inner, whole, whole, outer, outer, inner, rows),
        out_specs=(rows, rows, whole, whole, heads, bias, inner, whole, whole, outer, outer, inner),
        check_vma=False,
    )
```

```python
import functools

import jax
import jax.numpy as jnp
import numpy as np
from jax import lax
from jax.experimental import pallas as pl
from jax.experimental.pallas import tpu as pltpu
from jax.sharding import PartitionSpec as P

HEAD = 64
ROT = 16
EPSILON = 1e-05
NEG_LARGE = -1e30
MESH = pl.DeviceIdType.MESH
ANY = pl.BlockSpec(memory_space=pl.ANY)
VMEM = pl.BlockSpec(memory_space=pltpu.VMEM)
BF = jnp.bfloat16
F32 = jnp.float32
VMEM_BYTES = 60 * 2**20
TILE = 512
SMALL = 8


def put(src, dst, send, recv, **device):
    return pltpu.make_async_remote_copy(
        src_ref=src, dst_ref=dst, send_sem=send, recv_sem=recv, device_id=device, device_id_type=MESH
    )


def dot(left, right):
    return jnp.dot(left, right, preferred_element_type=F32)


def dot_nt(left, right):
    return lax.dot_general(left, right, (((1,), (1,)), ((), ())), preferred_element_type=F32)


def dot_tn(left, right):
    return lax.dot_general(left, right, (((0,), (0,)), ((), ())), preferred_element_type=F32)


def aligned(start, size, unit=None):
    return pl.ds(pl.multiple_of(start, unit or size), size)


class Net:
    def __init__(self):
        self.n_f, self.n_s = lax.axis_size("fsdp"), lax.axis_size("seq")
        self.tall = 2 if self.n_f % 2 == 0 else 1
        self.wide = self.n_f // self.tall
        self.n_l = self.n_s // 2
        self.f, self.s = lax.axis_index("fsdp"), lax.axis_index("seq")
        self.a, self.b = self.f // self.wide, self.f % self.wide
        self.z, self.c = self.s // 2, self.s % 2
        self.mate = self.s + 1 - 2 * self.c

    def barrier(self):
        sem = pltpu.get_barrier_semaphore()
        for k in range(1, self.n_f):
            pl.semaphore_signal(
                sem, inc=1, device_id={"fsdp": (self.f + k) % self.n_f}, device_id_type=MESH
            )
        for k in range(1, self.n_s):
            pl.semaphore_signal(
                sem, inc=1, device_id={"seq": (self.s + k) % self.n_s}, device_id_type=MESH
            )
        pl.semaphore_wait(sem, self.n_f + self.n_s - 2)

    def sides(self, hop, act):
        @pl.loop(0, 2)
        def _(side):
            other = self.z + (2 * side - 1) * hop

            @pl.when((other >= 0) & (other < self.n_l))
            def _():
                act(other, side)


class Spread:
    def __init__(self, net, src, part, sems):
        self.net, self.src, self.part, self.sems = net, src, part, sems
        self.rows = [j for j in range(1, net.wide)]
        self.cols = [i for i in range(1, net.tall)]

    @staticmethod
    def count(n_f):
        tall = 2 if n_f % 2 == 0 else 1
        wide = n_f // tall
        return 1 + 2 * (wide - 1) + 2 * (tall - 1) + 4 * (wide - 1) * (tall - 1)

    def at(self, kind, i, j):
        w, t = len(self.rows), len(self.cols)
        base = {
            "own": 0,
            "row": 1,
            "col": 1 + 2 * w,
            "half0": 1 + 2 * w + 2 * t,
            "half1": 1 + 2 * w + 2 * t + 2 * w * t,
        }[kind]
        if kind == "own":
            return self.sems.at[0]
        k = j - 1 if kind == "row" else i - 1 if kind == "col" else (i - 1) * w + j - 1
        return self.sems.at[base + 2 * k], self.sems.at[base + 2 * k + 1]

    def rank(self, i, j):
        net = self.net
        return ((net.a + i) % net.tall) * net.wide + (net.b + j) % net.wide

    def back(self, i, j):
        net = self.net
        return ((net.a - i + net.tall) % net.tall) * net.wide + (net.b - j + net.wide) % net.wide

    def own(self):
        return pltpu.make_async_copy(self.src, self.part(self.net.f, None), self.at("own", 0, 0))

    def first(self, i, j):
        send, recv = self.at("row" if i == 0 else "col", i, j)
        place = self.part(self.net.f, None)
        return put(place, place, send, recv, fsdp=self.rank(i, j))

    def came(self, i, j):
        send, recv = self.at("row" if i == 0 else "col", i, j)
        place = self.part(self.back(i, j), None)
        return put(place, place, send, recv, fsdp=self.rank(i, j))

    def second(self, half, i, j, came=False):
        send, recv = self.at("half0" if half == 0 else "half1", i, j)
        origin = self.back(i, j) if came else self.back(0, j) if half == 0 else self.back(i, 0)
        place = self.part(origin, half)
        return put(place, place, send, recv, fsdp=self.rank(i, 0) if half == 0 else self.rank(0, j))

    def prepare(self):
        self.own().start()

    def start(self):
        self.own().wait()
        for i in self.cols:
            self.first(i, 0).start()
        for j in self.rows:
            self.first(0, j).start()

    def relay(self):
        for j in self.rows:
            self.came(0, j).wait_recv()
            for i in self.cols:
                self.second(0, i, j).start()
        for i in self.cols:
            self.came(i, 0).wait_recv()
            for j in self.rows:
                self.second(1, i, j).start()

    def finish(self):
        for j in self.rows:
            self.first(0, j).wait_send()
        for i in self.cols:
            self.first(i, 0).wait_send()
        for i in self.cols:
            for j in self.rows:
                for half in range(2):
                    self.second(half, i, j, came=True).wait_recv()
                    self.second(half, i, j).wait_send()


class Line:
    def __init__(self, net, src, part, recv, send, local):
        self.net, self.src, self.part, self.recv, self.send, self.local = net, src, part, recv, send, local
        self.pieces = recv.shape[1]
        self.rows = src.shape[0] // self.pieces

    @staticmethod
    def sems(n_s, pieces=2):
        return [
            pltpu.SemaphoreType.DMA((n_s, pieces)),
            pltpu.SemaphoreType.DMA((4, n_s // 2, pieces)),
            pltpu.SemaphoreType.DMA((1,)),
        ]

    def cut(self, ref, piece):
        return ref.at[aligned(piece * self.rows, self.rows)]

    def own(self):
        return pltpu.make_async_copy(self.src, self.part(self.net.s), self.local.at[0])

    def on_line(self, src, chunk, side, hop, piece):
        return put(
            self.cut(src, piece),
            self.cut(self.part(chunk), piece),
            self.send.at[side, hop, piece],
            self.recv.at[chunk, piece],
            seq=self.net.s + 2 - 4 * side,
        )

    def to_mate(self, src, chunk, side, hop, piece):
        return put(
            self.cut(src, piece),
            self.cut(self.part(chunk), piece),
            self.send.at[2 + side, hop, piece],
            self.recv.at[chunk, piece],
            seq=self.net.mate,
        )

    def goes_on(self, side):
        after = self.net.z + 1 - 2 * side
        return (after >= 0) & (after < self.net.n_l)

    def each_piece(self, act):
        pl.loop(0, self.pieces)(act)

    def prepare(self):
        self.own().start()

    def start(self):
        net = self.net
        self.own().wait()
        place = self.part(net.s)

        @self.each_piece
        def _(piece):
            for side in range(2):

                @pl.when(self.goes_on(side))
                def _():
                    self.on_line(place, net.s, side, 0, piece).start()

            self.to_mate(place, net.s, 0, 0, piece).start()

    def came(self, chunk, piece):
        place = self.cut(self.part(chunk), piece)
        put(place, place, self.send.at[0, 0, 0], self.recv.at[chunk, piece], seq=self.net.mate).wait_recv()

    def step(self, hop):
        net = self.net

        @self.each_piece
        def _(piece):
            def act(other, side):
                chunk = 2 * other + net.c
                self.came(chunk, piece)

                @pl.when(self.goes_on(side))
                def _():
                    self.on_line(self.part(chunk), chunk, side, hop, piece).start()

                self.to_mate(self.part(chunk), chunk, side, hop, piece).start()

            net.sides(hop, act)

    def pair(self, other):
        @self.each_piece
        def _(piece):
            self.came(2 * other + 1 - self.net.c, piece)

    def here(self):
        self.pair(self.net.z)

    def finish(self):
        net = self.net
        place = self.part(net.s)

        @self.each_piece
        def _(piece):
            for side in range(2):

                @pl.when(self.goes_on(side))
                def _():
                    self.on_line(place, net.s, side, 0, piece).wait_send()

            self.to_mate(place, net.s, 0, 0, piece).wait_send()

            @pl.loop(1, net.n_l)
            def _(hop):
                def act(other, side):
                    chunk = 2 * other + net.c

                    @pl.when(self.goes_on(side))
                    def _():
                        self.on_line(self.part(chunk), chunk, side, hop, piece).wait_send()

                    self.to_mate(self.part(chunk), chunk, side, hop, piece).wait_send()

                net.sides(hop, act)


class Packets:
    def __init__(self, net, src, buf, sems):
        self.net, self.src, self.buf, self.sems = net, src, buf, sems

    @staticmethod
    def count(n_f, n_s):
        return 1 + 2 * (n_f - 1) + 2 * (n_s - 1)

    def own(self):
        net = self.net
        return pltpu.make_async_copy(self.src, self.buf.at[net.s, net.f], self.sems.at[0])

    def one(self, k, came=False):
        net = self.net
        f = (net.f - k + net.n_f) % net.n_f if came else net.f
        place = self.buf.at[net.s, f]
        return put(
            place if came else self.src,
            place,
            self.sems.at[2 * k - 1],
            self.sems.at[2 * k],
            fsdp=(net.f + k) % net.n_f,
        )

    def two(self, k, came=False):
        net = self.net
        place = self.buf.at[(net.s - k + net.n_s) % net.n_s if came else net.s]
        at = 2 * (net.n_f - 1) + 2 * k - 1
        return put(place, place, self.sems.at[at], self.sems.at[at + 1], seq=(net.s + k) % net.n_s)

    def start(self):
        self.own().start()
        for k in range(1, self.net.n_f):
            self.one(k).start()

    def middle(self):
        self.own().wait()
        for k in range(1, self.net.n_f):
            self.one(k, came=True).wait_recv()
            self.one(k).wait_send()
        for k in range(1, self.net.n_s):
            self.two(k).start()

    def finish(self):
        for k in range(1, self.net.n_s):
            self.two(k, came=True).wait_recv()
            self.two(k).wait_send()

    def unpack(self, out, width):
        net = self.net
        per = 128 // width
        for tile in range(net.n_f * net.n_s // per):
            total = None
            for j in range(per):
                f, s = divmod(tile * per + j, net.n_s)
                piece = self.buf[s, f]
                if j:
                    piece = pltpu.roll(piece, j * width, axis=1)
                total = piece if total is None else total + piece
            out[:, tile * 128 : (tile + 1) * 128] = total


def rotary(values, cosine, sine):
    columns = values.shape[1]
    half = ROT // 2
    times = columns // 128

    def wide(table):
        return table if times == 1 else jnp.concatenate([table] * times, axis=1)

    lane = lax.broadcasted_iota(jnp.int32, values.shape, 1)
    other = jnp.where(
        lane % HEAD < half, pltpu.roll(values, columns - half, axis=1), pltpu.roll(values, half, axis=1)
    )
    return values * wide(cosine) + other * wide(sine)


def rotary_tables(length):
    half = ROT // 2
    freqs = np.float32(10000.0) ** (-np.arange(half, dtype=np.float32) * np.float32(2.0 / ROT))
    angles = np.arange(length, dtype=np.float32)[:, None] * freqs[None, :].astype(np.float32)
    cosine, sine = np.cos(angles), np.sin(angles)
    rest = np.zeros((length, HEAD - ROT), np.float32)
    keep = np.concatenate([cosine, cosine, rest + 1], 1)
    swap = np.concatenate([-sine, sine, rest], 1)
    return [np.tile(t, (1, 128 // HEAD)).astype(np.float32) for t in (keep, swap)]


def normalize(values):
    center = values - jnp.mean(values, -1, keepdims=True)
    inverse = lax.rsqrt(jnp.mean(center * center, -1, keepdims=True) + EPSILON)
    return center * inverse, inverse


class Copies:
    def __init__(self, sems):
        self.sems, self.all, self.open = sems, [], []

    def start(self, src, dst):
        copy = pltpu.make_async_copy(src, dst, self.sems.at[len(self.all)])
        copy.start()
        self.all.append(copy)
        self.open.append(copy)
        return copy

    def wait(self, *copies):
        for copy in copies or list(self.open):
            copy.wait()
            self.open = [c for c in self.open if c is not copy]


def columns_of(ref, depth):
    half_rows = ref.shape[0] // 2

    def part(f, half):
        span = aligned(f * depth, depth)
        if half is None:
            return ref.at[:, span]
        return ref.at[pl.ds(half * half_rows, half_rows), span]

    return part


def rows_of(ref, chunk):
    return lambda s: ref.at[aligned(s * chunk, chunk)]


class Fold:
    def __init__(self, net, tile, total, mate_in, coming, mate_out, out, mate_send, mate_recv, send, recv):
        self.net, self.tile, self.total = net, tile, total
        self.mate_in, self.coming, self.mate_out, self.out = mate_in, coming, mate_out, out
        self.mate_send, self.mate_recv, self.send, self.recv = mate_send, mate_recv, send, recv
        self.chunk = total.shape[0]
        self.pieces = recv.shape[1]
        self.rows = self.chunk // self.pieces

    @staticmethod
    def shared(chunk, width):
        return [pltpu.VMEM((2 * chunk, TILE), F32), pltpu.VMEM((chunk, width), F32)]

    @staticmethod
    def buffers(n_s, chunk, width):
        n_l = n_s // 2
        return [
            pltpu.VMEM((n_l, chunk, width), BF),
            pltpu.VMEM((n_l + 1, chunk, width), BF),
            pltpu.VMEM((3, chunk, width), BF),
            pltpu.VMEM((n_l, chunk, width), BF),
        ]

    @staticmethod
    def sems(n_s, pieces=2):
        n_l = n_s // 2
        return [
            pltpu.SemaphoreType.DMA((3, pieces)),
            pltpu.SemaphoreType.DMA((n_l, pieces)),
            pltpu.SemaphoreType.DMA((n_l, pieces)),
            pltpu.SemaphoreType.DMA((n_l + 1, pieces)),
        ]

    def place(self, other):
        return (other >= 0) & (other < self.net.n_l)

    def fed(self, side):
        return self.place(self.net.z + 1 - 2 * side)

    def span(self, piece):
        return aligned(piece * self.rows, self.rows)

    def each_piece(self, act):
        pl.loop(0, self.pieces)(act)

    def to_mate(self, target, slot, piece):
        span = self.span(piece)
        return put(
            self.mate_out.at[slot, span],
            self.mate_in.at[target, span],
            self.mate_send.at[slot, piece],
            self.mate_recv.at[target, piece],
            seq=self.net.mate,
        )

    def onward(self, target, side, hop, piece):
        span = self.span(piece)
        slot = target + (self.net.n_l - target) * (1 - side) * (1 // hop)
        return put(
            self.out.at[target, span],
            self.coming.at[slot, span],
            self.send.at[target, piece],
            self.recv.at[slot, piece],
            seq=self.net.s + 4 * side - 2,
        )

    def came(self, slot, piece):
        place = self.coming.at[slot, self.span(piece)]
        put(place, place, self.send.at[0, 0], self.recv.at[slot, piece], seq=self.net.mate).wait_recv()

    def mate_sent(self, slot):
        self.each_piece(lambda piece: self.to_mate(self.net.z, slot, piece).wait_send())

    def begin_one(self, target, slot, produce):
        mine = aligned(self.net.c * self.chunk, self.chunk)
        theirs = aligned((1 - self.net.c) * self.chunk, self.chunk)

        def write(cols, value):
            self.tile[...] = value
            self.out[target, :, cols] = self.tile[mine, :].astype(BF)
            self.mate_out[slot, :, cols] = self.tile[theirs, :].astype(BF)

        produce(target, write)
        self.each_piece(lambda piece: self.to_mate(target, slot, piece).start())

    def leave(self, target, side, hop):
        @pl.when((hop > 0) & jnp.logical_not(self.fed(side)))
        def _():
            self.each_piece(lambda piece: self.pass_piece(target, side, hop, piece, False))

    def begin(self, produce, between=None):
        net = self.net

        @pl.loop(0, net.n_l)
        def _(j):
            hop = net.n_l - 1 - j

            def act(target, side):
                @pl.when((hop > 0) | (side == 0))
                def _():
                    @pl.when((hop > 0) & self.place(target + 2 * side - 1))
                    def _():
                        self.mate_sent(side)

                    self.begin_one(target, side + (2 - side) * (1 // (hop + 1)), produce)
                    self.leave(target, side, hop)

            net.sides(hop, act)
            if between is not None:
                pl.when(j == 1)(between)

    def pass_piece(self, target, side, hop, piece, fed):
        self.to_mate(target, 0, piece).wait_recv()
        span = self.span(piece)
        value = self.out[target, span, :].astype(F32) + self.mate_in[target, span, :].astype(F32)
        if fed:
            self.came(target, piece)
            value = value + self.coming[target, span, :].astype(F32)
        self.out[target, span, :] = value.astype(BF)
        self.onward(target, side, hop, piece).start()

    def open_total(self):
        net = self.net

        @self.each_piece
        def _(piece):
            self.to_mate(net.z, 0, piece).wait_recv()
            span = self.span(piece)
            self.total[span, :] = self.out[net.z, span, :].astype(F32) + self.mate_in[net.z, span, :].astype(F32)

    def wave(self, at, near=False, between=None):
        net = self.net
        above = at if near else net.n_l - at

        @pl.loop(0, 2)
        def _(turn):
            side = (1 - (2 * net.z) // net.n_l + turn) % 2
            target = net.n_l - 1 - above + (2 * above - net.n_l + 1) * side
            hop = (target - net.z) * (2 * side - 1)

            @self.each_piece
            def _(piece):
                span = self.span(piece)

                @pl.when(self.fed(side) & (hop > 0))
                def _():
                    self.pass_piece(target, side, hop, piece, True)

                @pl.when(self.fed(side) & (hop == 0))
                def _():
                    slot = net.z + (net.n_l - net.z) * (1 - side)
                    self.came(slot, piece)
                    self.total[span, :] = self.total[span, :] + self.coming[slot, span, :].astype(F32)

                if between is not None:
                    between(((at - 1) * 2 + turn) * self.pieces + piece)

    def finish(self):
        net = self.net
        self.mate_sent(2)
        for side in range(2):
            pl.when(self.place(net.z + 2 * side - 1))(functools.partial(self.mate_sent, side))

        @pl.loop(1, net.n_l)
        def _(hop):
            net.sides(
                hop,
                lambda target, side: self.each_piece(
                    lambda piece: self.onward(target, side, hop, piece).wait_send()
                ),
            )


class GridSum:
    def __init__(self, net, stage, came, sems):
        self.net, self.stage, self.came, self.sems = net, stage, came, sems
        self.half = stage.shape[1] // 2
        self.rows = next(r for r in (176, 128, 96, 64, 32, 16) if self.half % r == 0)
        self.cols = range(1, net.tall)
        self.along = range(1, net.wide)
        self.bases = self.layout(net.n_f)

    @staticmethod
    def layout(n_f):
        tall = 2 if n_f % 2 == 0 else 1
        wide = n_f // tall
        sizes = [(wide - 1) * tall, (tall - 1) * wide, tall - 1, wide - 1]
        return [sum(sizes[:at]) for at in range(5)]

    @staticmethod
    def scratch(n_f, rows, columns):
        count = GridSum.layout(n_f)[4]
        return [
            pltpu.VMEM((n_f, rows, columns), BF),
            pltpu.VMEM((count, rows // 2, columns), BF),
            pltpu.SemaphoreType.DMA((2, count + GridEnd.count(n_f))),
        ]

    def slot(self, kind, i, j):
        base = self.bases[kind]
        return base + [(j - 1) * self.net.tall + i, (i - 1) * self.net.wide + j, i - 1, j - 1][kind]

    def rank(self, i, j):
        net = self.net
        return ((net.a + i) % net.tall) * net.wide + (net.b + j) % net.wide

    def owner(self, at):
        return self.rank(at // self.net.wide, at % self.net.wide)

    def copy(self, kind, i, j):
        half = kind % 2
        along = kind in (0, 3)
        slot = self.slot(kind, i, j)
        at = i * self.net.wide + j
        return put(
            self.stage.at[at, pl.ds(half * self.half, self.half)],
            self.came.at[slot],
            self.sems.at[0, slot],
            self.sems.at[1, slot],
            fsdp=self.rank(0, j) if along else self.rank(i, 0),
        )

    def first(self, at):
        i, j = at // self.net.wide, at % self.net.wide

        @pl.when(j > 0)
        def _():
            self.copy(0, i, j).start()

        @pl.when(i > 0)
        def _():
            self.copy(1, i, j).start()

    def gather(self, half, at, slots, write):
        @pl.loop(0, self.half // self.rows)
        def _(step):
            span = aligned(half * self.half + step * self.rows, self.rows, 16)
            value = self.stage[at, span, :].astype(F32)
            for slot in slots:
                value = value + self.came[slot, aligned(step * self.rows, self.rows, 16), :].astype(F32)
            write(span, value)

    def wait(self, *copies):
        for kind, i, j in copies:
            self.copy(kind, i, j).wait_recv()
        return [self.slot(*copy) for copy in copies]

    def second(self):
        def keep(at):
            def write(span, value):
                self.stage[at, span, :] = value.astype(BF)

            return write

        for i in self.cols:
            at = i * self.net.wide
            self.gather(0, at, self.wait(*[(0, i, j) for j in self.along]), keep(at))
            self.copy(2, i, 0).start()
        for j in self.along:
            self.gather(1, j, self.wait(*[(1, i, j) for i in self.cols]), keep(j))
            self.copy(3, 0, j).start()

    def sum_first(self):
        def keep(at):
            def write(span, value):
                self.stage[at, span, :] = value.astype(BF)

            return write

        for i in range(self.net.tall):
            at = i * self.net.wide
            self.gather(0, at, self.wait(*[(0, i, j) for j in self.along]), keep(at))
        for j in range(self.net.wide):
            self.gather(1, j, self.wait(*[(1, i, j) for i in self.cols]), keep(j))

    def hand_on(self, out):
        net = self.net
        shards = [(0, 0), (0, 1), *[(i * net.wide, 0) for i in self.cols], *[(j, 1) for j in self.along]]
        return [
            pltpu.make_async_copy(
                self.stage.at[at, pl.ds(half * self.half, self.half)], out.at[k], self.sems.at[0, self.bases[4] + k]
            )
            for k, (at, half) in enumerate(shards)
        ]

    def last(self, out):
        def write(span, value):
            out[span, :] = value

        self.gather(
            0, 0, self.wait(*[(0, 0, j) for j in self.along], *[(2, i, 0) for i in self.cols]), write
        )
        self.gather(
            1, 0, self.wait(*[(1, i, 0) for i in self.cols], *[(3, 0, j) for j in self.along]), write
        )

    def finish_first(self):
        for i in range(self.net.tall):
            for j in range(self.net.wide):
                if j:
                    self.copy(0, i, j).wait_send()
                if i:
                    self.copy(1, i, j).wait_send()

    def finish(self):
        self.finish_first()
        for i in self.cols:
            self.copy(2, i, 0).wait_send()
        for j in self.along:
            self.copy(3, 0, j).wait_send()


class GridEnd:
    def __init__(self, net, sums, came, sems):
        self.net, self.sums, self.came, self.sems = net, sums, came, sems

    @staticmethod
    def count(n_f):
        tall = 2 if n_f % 2 == 0 else 1
        return tall + n_f // tall

    @staticmethod
    def scratch(n_f, rows, columns):
        count = GridEnd.count(n_f)
        return [
            pltpu.VMEM((count, rows // 2, columns), BF),
            pltpu.VMEM((count - 2, rows // 2, columns), BF),
            pltpu.SemaphoreType.DMA((2, count - 2)),
        ]

    def copies(self):
        net = self.net
        f = [((net.a + i) % net.tall) * net.wide + net.b for i in range(1, net.tall)]
        f += [net.a * net.wide + (net.b + j) % net.wide for j in range(1, net.wide)]
        return [
            put(self.sums.at[2 + k], self.came.at[k], self.sems.at[0, k], self.sems.at[1, k], fsdp=to)
            for k, to in enumerate(f)
        ]

    def start(self):
        for copy in self.copies():
            copy.start()

    def last(self, out):
        for copy in self.copies():
            copy.wait()
        half = self.sums.shape[1]
        rows = next(r for r in (176, 128, 96, 64, 32, 16) if half % r == 0)
        down = range(self.net.tall - 1)
        along = range(self.net.tall - 1, self.net.tall + self.net.wide - 2)
        for at, slots in enumerate((down, along)):

            @pl.loop(0, half // rows)
            def _(step):
                span = aligned(step * rows, rows, 16)
                value = self.sums[at, span, :].astype(F32)
                for slot in slots:
                    value = value + self.came[slot, span, :].astype(F32)
                out[aligned(at * half + step * rows, rows, 16), :] = value


class PacketSum:
    def __init__(self, net, out, seq_in, total, fsdp_in, sems):
        self.net, self.out, self.seq_in, self.total, self.fsdp_in, self.sems = net, out, seq_in, total, fsdp_in, sems

    @staticmethod
    def scratch(n_f, n_s):
        return [
            pltpu.VMEM((n_s, n_f, SMALL, 128), F32),
            pltpu.VMEM((n_s, n_f, SMALL, 128), F32),
            pltpu.VMEM((n_f, SMALL, 128), F32),
            pltpu.VMEM((n_f, SMALL, 128), F32),
            pltpu.SemaphoreType.DMA((2 * (n_f + n_s),)),
        ]

    def one(self, k):
        to = (self.net.s + k) % self.net.n_s
        return put(self.out.at[to], self.seq_in.at[k], self.sems.at[2 * k], self.sems.at[2 * k + 1], seq=to)

    def two(self, k):
        to = (self.net.f + k) % self.net.n_f
        at = 2 * (self.net.n_s + k)
        return put(self.total.at[to], self.fsdp_in.at[k], self.sems.at[at], self.sems.at[at + 1], fsdp=to)

    def start(self, terms, width):
        net = self.net
        per = 128 // width
        for tile in range(net.n_f * net.n_s // per):
            value = terms[:, tile * 128 : (tile + 1) * 128]
            for j in range(per):
                f, s = divmod(tile * per + j, net.n_s)
                self.out[s, f] = pltpu.roll(value, 128 - j * width, axis=1) if j else value
        for k in range(1, net.n_s):
            self.one(k).start()

    def middle(self):
        net = self.net
        total = self.out[net.s]
        for k in range(1, net.n_s):
            self.one(k).wait()
            total = total + self.seq_in[k]
        self.total[...] = total
        for k in range(1, net.n_f):
            self.two(k).start()

    def finish(self, result):
        net = self.net
        total = self.total[net.f]
        for k in range(1, net.n_f):
            self.two(k).wait()
            total = total + self.fsdp_in[k]
        result[...] = total


def norm_backward(rows, source, grad, gain, terms, at, write):
    terms[at : at + 2, :] = jnp.zeros((2, terms.shape[1]), F32)

    @pl.loop(0, rows // 32)
    def _(i):
        span = aligned(i * 32, 32)
        scaled, inverse = normalize(source[span, :].astype(F32))
        value = grad[span, :]
        upstream = value * gain
        inner = jnp.mean(upstream, -1, keepdims=True)
        cross = jnp.mean(upstream * scaled, -1, keepdims=True)
        terms[at : at + 1, :] = terms[at : at + 1, :] + jnp.sum(value * scaled, 0, keepdims=True)
        terms[at + 1 : at + 2, :] = terms[at + 1 : at + 2, :] + jnp.sum(value, 0, keepdims=True)
        write(i, span, inverse * (upstream - inner - scaled * cross))


def layer_kernel(
    tok,
    gain_one,
    shift_one,
    gain_two,
    shift_two,
    bias,
    wq_own,
    wo_own,
    wg_own,
    wu_own,
    wd_own,
    gout_own,
    cosine,
    sine,
    q_o,
    k_o,
    kt_o,
    v_o,
    att_o,
    lse_o,
    n1_o,
    gains_o,
    wq_o,
    wo_o,
    dm_o,
    datt_o,
    dmid_o,
    top_o,
    terms_o,
    gate_o,
    up_o,
    down_o,
    rows,
    gout,
    wq,
    wo,
    wg,
    wu,
    wd,
    q,
    k,
    kt,
    v,
    vt,
    ot,
    att,
    hidden,
    dgate,
    dup,
    mid,
    low,
    packet,
    packets,
    tiles,
    total,
    *rest,
):
    net = Net()
    chunk, width = tok.shape
    length = chunk * net.n_s
    depth = wq_own.shape[1]
    columns = wq_own.shape[2]
    heads = columns // HEAD
    pair = 2 * chunk
    buffers, rest = rest[:4], rest[4:]
    folds = []
    for _ in range(3):
        folds.append(Fold(net, tiles, total, *buffers, *rest[:4]))
        rest = rest[4:]
    att_fold, normed_fold, top_fold = folds
    line_sems = [rest[at : at + 3] for at in (0, 3, 6, 9)]
    rest = rest[12:]
    spread_sems, rest = rest[:5], rest[5:]
    gate_sum, up_sum, down_sum = [GridSum(net, *rest[at : at + 3]) for at in (0, 3, 6)]
    sums = (down_sum, gate_sum, up_sum)
    pk_sems, copy_sems, n1_sems, free_sem = rest[9:]
    copies = Copies(copy_sems)
    n1 = att_fold.mate_out

    packet[...] = jnp.zeros(packet.shape, F32)
    own = gain_one.shape[1]
    for at, part in enumerate((gain_one, shift_one, gain_two, shift_two)):
        packet[at : at + 1, 0:own] = part[...].astype(F32)
    packet[4:7, 0:own] = bias[...].astype(F32)
    def wq_part(f, half):
        if half is None:
            return wq.at[:, aligned(f * depth, depth), :]
        return wq.at[:, aligned(f * depth + half * (depth // 2), depth // 2), :]

    spread_q = Spread(net, wq_own, wq_part, spread_sems[0])
    spread_o, spread_g, spread_u, spread_d = [
        Spread(net, own, columns_of(full, depth), sems)
        for own, full, sems in zip((wo_own, wg_own, wu_own, wd_own), (wo, wg, wu, wd), spread_sems[1:])
    ]
    pk = Packets(net, packet, packets, pk_sems)
    line = Line(net, tok, rows_of(rows, chunk), *line_sems[0])
    gout_line = Line(net, gout_own, rows_of(gout, chunk), *line_sems[1])
    n2_line = Line(net, low, rows_of(rows, chunk), *line_sems[2])
    dm_line = Line(net, low, rows_of(rows, chunk), *line_sems[3])

    for ready in (line, spread_q, spread_o, spread_g, spread_u, spread_d, gout_line):
        ready.prepare()
    net.barrier()

    def pairs(which, hop):
        net.sides(hop, lambda other, side: which.pair(other))

    def blocks(hop, act):
        def once(other, side):
            @pl.when((hop > 0) | (side == 0))
            def _():
                act(other, side)

        net.sides(hop, once)

    pk.start()
    line.start()
    spread_q.start()
    pk.middle()
    pk.finish()
    pk.unpack(gains_o, width // (net.n_f * net.n_s))

    def project_block(other, side):
        span = aligned(other * pair, pair)
        gain, shift = gains_o[0:1, :], gains_o[1:2, :]

        for part in range(2):

            @pl.loop(0, chunk // 32)
            def _(i):
                at = aligned((2 * other + part) * chunk + i * 32, 32)
                scaled, _ = normalize(rows[at, :].astype(F32))
                n1[part, aligned(i * 32, 32), :] = (scaled * gain + shift).astype(BF)

        keeps = [
            pltpu.make_async_copy(
                n1.at[part], n1_o.at[aligned((2 * other + part) * chunk, chunk)], n1_sems.at[part]
            )
            for part in range(2)
        ]
        for copy in keeps:
            copy.start()
        left = n1[0:2].reshape(pair, width)
        cols = aligned(net.s * columns, columns)
        tables = cosine[span, :], sine[span, :]
        for kind in range(3):
            value = dot(left, wq[kind]) + gains_o[4 + kind : 5 + kind, cols]
            if kind == 0:
                q[span, :] = rotary(value, *tables).astype(BF)
            elif kind == 1:
                value = rotary(value, *tables)
                k[span, :] = value.astype(BF)
                kt[...] = value.T.astype(BF)
            else:
                v[...] = value.astype(BF)
                vt[:, span] = value.T.astype(BF)
        for copy in (
            pltpu.make_async_copy(kt, kt_o.at[:, span], n1_sems.at[2]),
            pltpu.make_async_copy(v, v_o.at[span], n1_sems.at[3]),
        ):
            copy.start()
            keeps.append(copy)
        for copy in keeps:
            copy.wait()

    line.here()
    for hop in range(1, net.n_l - 1):
        line.step(hop)
        if hop == 1:
            spread_q.relay()
        pairs(line, hop)
    spread_o.start()
    spread_q.finish()
    spread_g.start()
    pl.loop(0, net.n_l - 1)(lambda hop: blocks(hop, project_block))
    spread_o.relay()
    spread_u.start()
    line.step(net.n_l - 1)
    gout_line.start()
    pairs(line, net.n_l - 1)
    blocks(net.n_l - 1, project_block)
    spread_d.start()
    q_copy = copies.start(q, q_o)
    for pair_of in ((wq, wq_o), (k, k_o)):
        copies.start(*pair_of)
    spread_o.finish()
    line.finish()

    def attend(i):
        lo, hi = i * pair, (i + 1) * pair

        @pl.loop(0, heads)
        def _(head):
            lane = lax.broadcasted_iota(jnp.int32, (1, columns), 1)
            here = jnp.where(lane // HEAD == head, HEAD**-0.5, 0.0).astype(BF)
            visible = lax.broadcasted_iota(jnp.int32, (pair, pair), 0) <= lax.broadcasted_iota(
                jnp.int32, (pair, pair), 1
            )
            head_rows = aligned(head * HEAD, HEAD)
            query = q[lo:hi, :] * here
            near = jnp.where(visible, dot_nt(k[lo:hi, :], query), NEG_LARGE)
            highest = jnp.max(near, 0, keepdims=True)
            if i:
                far = dot_nt(k[0:lo, :], query)
                highest = jnp.maximum(highest, jnp.max(far, 0, keepdims=True))
            near = jnp.exp(near - highest)
            sum_of = jnp.sum(near, 0, keepdims=True)
            out = dot(vt[head_rows, lo:hi], near.astype(BF))
            if i:
                far = jnp.exp(far - highest)
                sum_of = sum_of + jnp.sum(far, 0, keepdims=True)
                out = out + dot(vt[head_rows, 0:lo], far.astype(BF))
            ot[head_rows, :] = out / sum_of
            lse_o[pl.ds(head, 1), lo:hi] = highest + jnp.log(sum_of)

        att[lo:hi, :] = ot[...].T.astype(BF)

    def produce_attended(place, write):
        for i in range(net.n_l):
            pl.when(place == i)(functools.partial(attend, i))
        left = att[aligned(place * pair, pair), :]

        @pl.loop(0, width // TILE)
        def _(j):
            cols = aligned(j * TILE, TILE)
            write(cols, dot(left, wo[:, cols]))

    def relays():
        gout_line.step(1)
        spread_g.relay()

    att_fold.begin(produce_attended, relays)
    copies.start(att, att_o)
    copies.start(wo, wo_o)
    att_fold.open_total()
    for at in range(1, net.n_l):
        att_fold.wave(at)
        if at + 1 < net.n_l:
            gout_line.step(at + 1)
        if at == 1:
            spread_u.relay()
        if at == min(2, net.n_l - 1):
            spread_d.relay()
    gain_two, shift_two = gains_o[2:3, :], gains_o[3:4, :]

    @pl.loop(0, chunk // 32)
    def _(i):
        span = aligned(i * 32, 32)
        value = rows[aligned(net.s * chunk + i * 32, 32), :].astype(F32) + total[span, :]
        mid[span, :] = value
        scaled, _ = normalize(value)
        low[span, :] = (scaled * gain_two + shift_two).astype(BF)

    n2_line.prepare()
    n2_line.start()
    att_fold.finish()
    gout_line.here()
    pl.loop(1, net.n_l)(lambda hop: pairs(gout_line, hop))

    def forward_block(other):
        span = aligned(other * pair, pair)
        right = rows[span, :]
        half = hidden.shape[0] // 2

        @pl.loop(0, 2)
        def _(part):
            units = aligned(part * half, half, 16)
            gate = dot_nt(wg[units, :], right)
            up = dot_nt(wu[units, :], right)
            back = dot_nt(wd[units, :], gout[span, :])
            sigma = jax.nn.sigmoid(gate)
            active = gate * sigma
            hidden[units, span] = (active * up).astype(BF)
            dgate[units, span] = (back * up * (sigma * (1.0 + gate * (1.0 - sigma)))).astype(BF)
            dup[units, span] = (back * active).astype(BF)

    def produce_normed(place, write):
        span = aligned(place * pair, pair)
        left, right = dgate[:, span].T, dup[:, span].T

        @pl.loop(0, width // TILE)
        def _(j):
            cols = aligned(j * TILE, TILE)
            write(cols, dot(left, wg[:, cols]) + dot(right, wu[:, cols]))

    def begin_normed(other, side, hop):
        @pl.when(hop > 1)
        def _():
            normed_fold.mate_sent(side)

        normed_fold.begin_one(other, side + (2 - side) * (1 // (hop + 1)), produce_normed)

    def forward_blocks(hop):
        def act(other, side):
            forward_block(other)

            @pl.when(jnp.logical_not(normed_fold.fed(side)))
            def _():
                begin_normed(other, side, hop)
                normed_fold.leave(other, side, hop)

        net.sides(hop, act)

    def begin_fed(hop):
        def act(other, side):
            @pl.when((hop == 0) | normed_fold.fed(side))
            def _():
                begin_normed(other, side, hop)

        blocks(hop, act)

    n2_line.here()
    for spread in (spread_g, spread_u, spread_d):
        spread.finish()
    forward_block(net.z)

    @pl.loop(1, net.n_l)
    def _(hop):
        n2_line.step(hop)
        pairs(n2_line, hop)
        forward_blocks(hop)
        begin_fed(hop - 1)

    begin_fed(net.n_l - 1)
    normed_fold.open_total()

    def weight_terms(task):
        at, kind = net.n_f - 1 - task // 3, task % 3
        cols = aligned(gate_sum.owner(at) * depth, depth)
        for way, (grid_sum, left, right) in enumerate(
            ((down_sum, hidden, gout), (gate_sum, dgate, rows), (up_sum, dup, rows))
        ):

            @pl.when(kind == way)
            def _():
                half = left.shape[0] // 2

                @pl.loop(0, 2)
                def _(part):
                    units = aligned(part * half, half, 16)
                    grid_sum.stage[at, units, :] = dot(left[units, :], right[:, cols]).astype(BF)

                grid_sum.first(at)

    tasks = 3 * net.n_f
    slots = 2 * normed_fold.pieces * (net.n_l - 1)
    each = -(-tasks // slots)

    def between(slot):
        @pl.loop(0, each)
        def _(i):
            pl.when(slot * each + i < tasks)(lambda: weight_terms(slot * each + i))

    for at in range(1, net.n_l):
        normed_fold.wave(at, near=True, between=between)
    n2_line.finish()

    def beside(act):
        act(net.mate)
        for side in range(2):
            pl.when(n2_line.goes_on(side))(lambda: act(net.s + 2 - 4 * side))

    beside(lambda to: pl.semaphore_signal(free_sem, 1, device_id={"seq": to}, device_id_type=MESH))

    def write_middle(i, span, value):
        value = value + gout[aligned(net.s * chunk + i * 32, 32), :].astype(F32)
        dmid_o[span, :] = value
        low[span, :] = value.astype(BF)

    terms_o[...] = jnp.zeros(terms_o.shape, F32)
    norm_backward(chunk, mid, total, gain_two, terms_o, 2, write_middle)
    ends = (net.z + net.n_l - 1) // net.n_l + (2 * net.n_l - 2 - net.z) // net.n_l
    pl.semaphore_wait(free_sem, 1 + ends)
    dm_line.prepare()
    dm_line.start()
    normed_fold.finish()

    def produce_top(place, write):
        left = hidden[:, aligned(place * pair, pair)].T

        @pl.loop(0, width // TILE)
        def _(j):
            cols = aligned(j * TILE, TILE)
            write(cols, dot(left, wd[:, cols]))

    copies.wait(q_copy)
    datt = q

    def back_block(other, side):
        span = aligned(other * pair, pair)
        datt[span, :] = dot_nt(rows[span, :], wo[...]).astype(BF)

    dm_line.here()
    dm_line.step(1)
    top_fold.begin(produce_top)
    back_block(net.z, 0)
    top_fold.open_total()
    for at in range(1, net.n_l):
        if at + 1 < net.n_l:
            dm_line.step(at + 1)
        top_fold.wave(at)
        pairs(dm_line, at)
        net.sides(at, back_block)
    copies.start(datt, datt_o)
    copies.start(rows, dm_o)

    @pl.loop(0, chunk // 32)
    def _(i):
        span = aligned(i * 32, 32)
        top_fold.out[net.z, span, :] = (mid[span, :] + total[span, :]).astype(BF)

    copies.start(top_fold.out.at[net.z], top_o)
    top_fold.finish()
    gout_line.finish()
    dm_line.finish()
    hands = []
    for grid_sum, out in zip(sums, (down_o, gate_o, up_o)):
        grid_sum.sum_first()
        hands.extend(grid_sum.hand_on(out))
        for copy in grid_sum.hand_on(out):
            copy.start()
    for grid_sum in sums:
        grid_sum.finish_first()
    for copy in hands:
        copy.wait()
    copies.wait()


def layer_part(tokens, norms, wq, wo, wg, wu, wd, gout, tables):
    chunk, width = tokens.shape
    n_f, n_s = lax.axis_size("fsdp"), lax.axis_size("seq")
    length = chunk * n_s
    depth, columns = wq.shape[1:]
    units = wg.shape[0]
    shape = jax.ShapeDtypeStruct
    wide, head, turned, weight = (length, width), (length, columns), (units, length), (units, width)
    return pl.pallas_call(
        layer_kernel,
        name="layer",
        out_shape=[
            shape(head, BF),
            shape(head, BF),
            shape((columns, length), BF),
            shape(head, BF),
            shape(head, BF),
            shape((8, length), F32),
            shape(wide, BF),
            shape((SMALL, width), F32),
            shape((3, width, columns), BF),
            shape((columns, width), BF),
            shape(wide, BF),
            shape(head, BF),
            shape((chunk, width), F32),
            shape((chunk, width), BF),
            shape((SMALL, width), F32),
            *[shape((GridEnd.count(n_f), units // 2, depth), BF)] * 3,
        ],
        in_specs=[ANY, *[VMEM] * 5, *[ANY] * 6, VMEM, VMEM],
        out_specs=[*[ANY] * 5, VMEM, ANY, VMEM, *[ANY] * 4, VMEM, ANY, VMEM, *[ANY] * 3],
        scratch_shapes=[
            pltpu.VMEM(wide, BF),
            pltpu.VMEM(wide, BF),
            pltpu.VMEM((3, width, columns), BF),
            pltpu.VMEM((columns, width), BF),
            *[pltpu.VMEM(weight, BF)] * 3,
            pltpu.VMEM(head, BF),
            pltpu.VMEM(head, BF),
            pltpu.VMEM((columns, 2 * chunk), BF),
            pltpu.VMEM((2 * chunk, columns), BF),
            pltpu.VMEM((columns, length), BF),
            pltpu.VMEM((columns, 2 * chunk), F32),
            pltpu.VMEM(head, BF),
            *[pltpu.VMEM(turned, BF)] * 3,
            pltpu.VMEM((chunk, width), F32),
            pltpu.VMEM((chunk, width), BF),
            pltpu.VMEM((SMALL, 128), F32),
            pltpu.VMEM((n_s, n_f, SMALL, 128), F32),
            *Fold.shared(chunk, width),
            *Fold.buffers(n_s, chunk, width),
            *Fold.sems(n_s) * 3,
            *Line.sems(n_s) * 4,
            *[pltpu.SemaphoreType.DMA((Spread.count(n_f),))] * 5,
            *GridSum.scratch(n_f, units, depth) * 3,
            pltpu.SemaphoreType.DMA((Packets.count(n_f, n_s),)),
            pltpu.SemaphoreType.DMA((8,)),
            pltpu.SemaphoreType.DMA((4,)),
            pltpu.SemaphoreType.REGULAR,
        ],
        compiler_params=pltpu.CompilerParams(
            collective_id=1, has_side_effects=True, vmem_limit_bytes=VMEM_BYTES
        ),
        cost_estimate=pl.CostEstimate(
            flops=2 * length * width * (4 * columns + 9 * units),
            bytes_accessed=8 * length * width,
            transcendentals=length * (length * columns // HEAD + units),
        ),
    )(tokens, *norms, wq, wo, wg, wu, wd, gout, *tables)


def back_kernel(
    datt_in,
    q_in,
    k_in,
    kt_in,
    v_in,
    att_in,
    wq_in,
    n1_in,
    dm_in,
    down_in,
    gate_in,
    up_in,
    lse,
    tok,
    dmid,
    gains,
    terms_in,
    cosine,
    sine,
    gin_o,
    small_o,
    out_o,
    qkv_o,
    down_o,
    gate_o,
    up_o,
    datt,
    q,
    k,
    kt,
    v,
    att,
    wq,
    n1,
    dm,
    query,
    upstream,
    inners,
    dk,
    dv,
    dqt,
    dproj,
    terms,
    tiles,
    total,
    *rest,
):
    net = Net()
    chunk, width = tok.shape
    length, columns = q_in.shape
    heads = columns // HEAD
    pair = 2 * chunk
    depth = width // net.n_f
    block = 256
    buffers, rest = rest[:4], rest[4:]
    fold_sems, rest = rest[:4], rest[4:]
    packet_scratch, rest = rest[:5], rest[5:]
    out_sum, qkv_sum = GridSum(net, *rest[:3]), GridSum(net, *rest[3:6])
    ends = [GridEnd(net, *rest[at : at + 3]) for at in (6, 9, 12)]
    copy_sems, column_sems = rest[15:]

    copies = Copies(copy_sems)
    loads = [
        copies.start(src, dst)
        for src, dst in (
            (datt_in, datt),
            (q_in, q),
            (k_in, k),
            (kt_in, kt),
            (v_in, v),
            (att_in, att),
            (wq_in, wq),
            (down_in, ends[0].sums),
            (gate_in, ends[1].sums),
            (up_in, ends[2].sums),
        )
    ]
    def load(at, way):
        src, dst = ((n1_in, n1), (dm_in, dm))[way]
        cols = aligned(qkv_sum.owner(at) * depth, depth)
        return pltpu.make_async_copy(src.at[:, cols], dst.at[at % 2], column_sems.at[way, at % 2])

    for at in range(net.n_f - 1, max(net.n_f - 3, -1), -1):
        for way in range(2):
            load(at, way).start()

    @pl.loop(0, length // block)
    def _(i):
        span = aligned(i * block, block)
        dk[span, :] = jnp.zeros((block, columns), F32)
        dv[span, :] = jnp.zeros((block, columns), F32)

    net.barrier()
    copies.wait(*loads[7:])
    for end in ends:
        end.start()
    copies.wait(*loads[:6])

    of_head = (
        lax.broadcasted_iota(jnp.int32, (8, columns), 1) // HEAD
        == lax.broadcasted_iota(jnp.int32, (8, columns), 0)
    ).astype(F32)

    @pl.loop(0, length // block)
    def _(i):
        span = aligned(i * block, block)
        product = datt[span, :].astype(F32) * att[span, :].astype(F32)
        inners[:, span] = lax.dot_general(
            of_head,
            product,
            (((1,), (1,)), ((), ())),
            precision=lax.Precision.HIGHEST,
            preferred_element_type=F32,
        )

    @pl.loop(0, heads)
    def _(head):
        lane = lax.broadcasted_iota(jnp.int32, (1, columns), 1)
        here = jnp.where(lane // HEAD == head, 1.0, 0.0).astype(BF)
        scale = HEAD**-0.5
        visible = lax.broadcasted_iota(jnp.int32, (block, block), 0) <= lax.broadcasted_iota(
            jnp.int32, (block, block), 1
        )
        head_rows = aligned(head * HEAD, HEAD)

        @pl.loop(0, length // block)
        def _(i):
            span = aligned(i * block, block)
            query[span, :] = q[span, :] * (here * scale)
            upstream[span, :] = datt[span, :] * here

        for j in range(length // block):
            at, end = j * block, (j + 1) * block
            keys, values, turned = k[at:end, :], v[at:end, :], kt[head_rows, at:end]

            def part(lo, hi, near):
                probs = jnp.exp(dot_nt(keys, query[lo:hi, :]) - lse[pl.ds(head, 1), lo:hi])
                if near:
                    probs = jnp.where(visible, probs, 0.0)
                grads = dot_nt(values, upstream[lo:hi, :])
                scores = (probs * (grads - inners[pl.ds(head, 1), lo:hi])).astype(BF)
                out = dot(turned, scores)
                dqt[head_rows, lo:hi] = dqt[head_rows, lo:hi] + out if j else out
                return dot(probs.astype(BF), upstream[lo:hi, :]), dot(scores, query[lo:hi, :])

            value_grads, key_grads = part(at, end, True)
            if end < length:
                more_values, more_keys = part(end, length, False)
                value_grads, key_grads = value_grads + more_values, key_grads + more_keys
            dv[at:end, :] = dv[at:end, :] + value_grads
            dk[at:end, :] = dk[at:end, :] + key_grads

    terms[...] = terms_in[...]
    bias_cols = aligned(net.s * columns, columns)

    @pl.loop(0, length // block)
    def _(i):
        span = aligned(i * block, block)
        tables = cosine[span, :], -sine[span, :]
        parts = [
            rotary((dqt[:, span].T * HEAD**-0.5).astype(BF).astype(F32), *tables).astype(BF),
            rotary(dk[span, :].astype(BF).astype(F32), *tables).astype(BF),
            dv[span, :].astype(BF),
        ]
        for kind in range(3):
            dproj[kind, span, :] = parts[kind]
            row = slice(4 + kind, 5 + kind)
            terms[row, bias_cols] = terms[row, bias_cols] + jnp.sum(parts[kind].astype(F32), 0, keepdims=True)

    def weight_terms(task):
        at = net.n_f - 1 - task // 2

        def loaded(way):
            load(at, way).wait()

        def next_load(way):
            pl.when(at >= 2)(lambda: load(at - 2, way).start())

        @pl.when(task % 2 == 0)
        def _():
            loaded(0)
            left = n1[at % 2].T
            for kind in range(3):
                qkv_sum.stage[at, kind * depth : (kind + 1) * depth, :] = dot(left, dproj[kind]).astype(BF)
            next_load(0)
            qkv_sum.first(at)

        @pl.when(task % 2 == 1)
        def _():
            loaded(1)
            out_sum.stage[at] = dot_tn(att[...], dm[at % 2]).astype(BF)
            next_load(1)
            out_sum.first(at)

    def produce(place, write):
        span = aligned(place * pair, pair)

        @pl.loop(0, width // TILE)
        def _(j):
            cols = aligned(j * TILE, TILE)
            value = dot_nt(dproj[0, span, :], wq[0, cols, :])
            for kind in range(1, 3):
                value = value + dot_nt(dproj[kind, span, :], wq[kind, cols, :])
            write(cols, value)

    fold = Fold(net, tiles, total, *buffers, *fold_sems)
    copies.wait()
    fold.begin(produce)
    fold.open_total()
    tasks = 2 * net.n_f
    waves = max(net.n_l - 2, 1)
    each = -(-tasks // (2 * fold.pieces * waves))

    def between(slot):
        @pl.loop(0, each)
        def _(i):
            pl.when(slot * each + i < tasks)(lambda: weight_terms(slot * each + i))

    for at in range(1, waves + 1):
        fold.wave(at, between=between)
    for at in range(waves + 1, net.n_l):
        fold.wave(at)

    def write_input(i, span, value):
        gin_o[span, :] = value + dmid[span, :]

    norm_backward(chunk, tok, total, gains[0:1, :], terms, 0, write_input)
    packet_sum = PacketSum(net, *packet_scratch)
    packet_sum.start(terms, width // (net.n_f * net.n_s))
    for grid_sum in (qkv_sum, out_sum):
        grid_sum.second()
    packet_sum.middle()
    for end, out in zip(ends, (down_o, gate_o, up_o)):
        end.last(out)
    packet_sum.finish(small_o)
    fold.finish()
    for grid_sum, out in ((qkv_sum, qkv_o), (out_sum, out_o)):
        grid_sum.last(out)
        grid_sum.finish()


def back_part(datt, q, k, kt, v, att, wq, n1, dm, down, gate, up, lse, tokens, dmid, gains, terms, tables):
    chunk, width = tokens.shape
    n_f, n_s = lax.axis_size("fsdp"), lax.axis_size("seq")
    length, columns = q.shape
    depth = width // n_f
    units = 2 * gate.shape[1]
    shape = jax.ShapeDtypeStruct
    return pl.pallas_call(
        back_kernel,
        name="back",
        out_shape=[
            shape((chunk, width), F32),
            shape((SMALL, 128), F32),
            shape((columns, depth), F32),
            shape((3 * depth, columns), F32),
            *[shape((units, depth), F32)] * 3,
        ],
        in_specs=[ANY] * 12 + [VMEM] * 7,
        out_specs=[VMEM] * 7,
        scratch_shapes=[
            pltpu.VMEM((length, columns), BF),
            pltpu.VMEM((length, columns), BF),
            pltpu.VMEM((length, columns), BF),
            pltpu.VMEM((columns, length), BF),
            pltpu.VMEM((length, columns), BF),
            pltpu.VMEM((length, columns), BF),
            pltpu.VMEM((3, width, columns), BF),
            pltpu.VMEM((2, length, depth), BF),
            pltpu.VMEM((2, length, depth), BF),
            pltpu.VMEM((length, columns), BF),
            pltpu.VMEM((length, columns), BF),
            pltpu.VMEM((8, length), F32),
            pltpu.VMEM((length, columns), F32),
            pltpu.VMEM((length, columns), F32),
            pltpu.VMEM((columns, length), F32),
            pltpu.VMEM((3, length, columns), BF),
            pltpu.VMEM((SMALL, width), F32),
            *Fold.shared(chunk, width),
            *Fold.buffers(n_s, chunk, width),
            *Fold.sems(n_s),
            *PacketSum.scratch(n_f, n_s),
            *GridSum.scratch(n_f, columns, depth),
            *GridSum.scratch(n_f, 3 * depth, columns),
            *GridEnd.scratch(n_f, units, depth) * 3,
            pltpu.SemaphoreType.DMA((10,)),
            pltpu.SemaphoreType.DMA((2, 2)),
        ],
        compiler_params=pltpu.CompilerParams(
            collective_id=3, has_side_effects=True, vmem_limit_bytes=VMEM_BYTES
        ),
        cost_estimate=pl.CostEstimate(
            flops=2 * length * columns * (8 * width + 5 * length),
            bytes_accessed=4 * length * width,
            transcendentals=length * length * columns // HEAD,
        ),
    )(datt, q, k, kt, v, att, wq, n1, dm, down, gate, up, lse, tokens, dmid, gains, terms, *tables)


def outputs_kernel(small, *refs):
    sources, targets, parts = refs[:7], refs[7:14], refs[14:]
    own = parts[0].shape[1]
    for src, dst in zip(sources, targets):
        dst[...] = src[...]
    for at in range(4):
        parts[at][...] = small[at : at + 1, 0:own]
    parts[4][...] = small[4:7, 0:own]


def outputs_part(small, own, *arrays):
    shape = jax.ShapeDtypeStruct
    return pl.pallas_call(
        outputs_kernel,
        name="outputs",
        out_shape=[shape(v.shape, v.dtype) for v in arrays]
        + [shape((1, own), F32)] * 4
        + [shape((3, own), F32)],
        in_specs=[VMEM] * 8,
        out_specs=[VMEM] * 12,
        compiler_params=pltpu.CompilerParams(vmem_limit_bytes=VMEM_BYTES),
    )(small, *arrays)


def per_device(
    tokens,
    gain_one,
    shift_one,
    w_qkv,
    b_qkv,
    w_out,
    gain_two,
    shift_two,
    w_gate,
    w_up,
    w_down,
    grad_output,
):
    length = tokens.shape[1] * lax.axis_size("seq")
    width = gain_one.shape[0]
    norms = [v[None] for v in (gain_one, shift_one, gain_two, shift_two)] + [b_qkv]
    tables = rotary_tables(length)
    q, k, kt, v, att, lse, n1, gains, wq, _, dm, datt, dmid, top, terms, gate, up, down = layer_part(
        tokens[0], norms, w_qkv.transpose(1, 0, 2), w_out, w_gate.T, w_up.T, w_down, grad_output[0], tables
    )
    grad_input, small, out, qkv, down, gate, up = back_part(
        datt, q, k, kt, v, att, wq, n1, dm, down, gate, up, lse, tokens[0], dmid, gains, terms, tables
    )

    top, grad_input, qkv, out, gate, up, down, one, shift, two, shift_to, bias = outputs_part(
        small, width, top, grad_input, qkv, out, gate, up, down
    )
    return (
        top[None],
        grad_input[None],
        one[0],
        shift[0],
        qkv.reshape(3, -1, qkv.shape[1]).transpose(1, 0, 2),
        bias,
        out,
        two[0],
        shift_to[0],
        gate.T,
        up.T,
        down,
    )


def solution(mesh):
    whole = P(("fsdp", "seq"))
    rows = P("fsdp", "seq", None)
    inner = P("seq", "fsdp")
    outer = P("fsdp", "seq")
    heads = P("fsdp", None, "seq")
    bias = P(None, ("fsdp", "seq"))
    return jax.shard_map(
        per_device,
        mesh=mesh,
        in_specs=(rows, whole, whole, heads, bias, inner, whole, whole, outer, outer, inner, rows),
        out_specs=(rows, rows, whole, whole, heads, bias, inner, whole, whole, outer, outer, inner),
        check_vma=False,
    )
```

```python
import functools

import jax
import jax.numpy as jnp
import numpy as np
from jax import lax
from jax.experimental import pallas as pl
from jax.experimental.pallas import tpu as pltpu
from jax.sharding import PartitionSpec as P

HEAD = 64
ROT = 16
EPSILON = 1e-05
NEG_LARGE = -1e30
MESH = pl.DeviceIdType.MESH
ANY = pl.BlockSpec(memory_space=pl.ANY)
VMEM = pl.BlockSpec(memory_space=pltpu.VMEM)
BF = jnp.bfloat16
F32 = jnp.float32
VMEM_BYTES = 60 * 2**20
TILE = 512
SMALL = 8


def put(src, dst, send, recv, **device):
    return pltpu.make_async_remote_copy(
        src_ref=src, dst_ref=dst, send_sem=send, recv_sem=recv, device_id=device, device_id_type=MESH
    )


def dot(left, right):
    return jnp.dot(left, right, preferred_element_type=F32)


def dot_nt(left, right):
    return lax.dot_general(left, right, (((1,), (1,)), ((), ())), preferred_element_type=F32)


def dot_tn(left, right):
    return lax.dot_general(left, right, (((0,), (0,)), ((), ())), preferred_element_type=F32)


def aligned(start, size, unit=None):
    return pl.ds(pl.multiple_of(start, unit or size), size)


class Net:
    def __init__(self):
        self.n_f, self.n_s = lax.axis_size("fsdp"), lax.axis_size("seq")
        self.tall = 2 if self.n_f % 2 == 0 else 1
        self.wide = self.n_f // self.tall
        self.n_l = self.n_s // 2
        self.f, self.s = lax.axis_index("fsdp"), lax.axis_index("seq")
        self.a, self.b = self.f // self.wide, self.f % self.wide
        self.z, self.c = self.s // 2, self.s % 2
        self.mate = self.s + 1 - 2 * self.c

    def barrier(self):
        sem = pltpu.get_barrier_semaphore()
        for k in range(1, self.n_f):
            pl.semaphore_signal(
                sem, inc=1, device_id={"fsdp": (self.f + k) % self.n_f}, device_id_type=MESH
            )
        for k in range(1, self.n_s):
            pl.semaphore_signal(
                sem, inc=1, device_id={"seq": (self.s + k) % self.n_s}, device_id_type=MESH
            )
        pl.semaphore_wait(sem, self.n_f + self.n_s - 2)

    def sides(self, hop, act):
        @pl.loop(0, 2)
        def _(side):
            other = self.z + (2 * side - 1) * hop

            @pl.when((other >= 0) & (other < self.n_l))
            def _():
                act(other, side)


class Spread:
    def __init__(self, net, src, part, sems):
        self.net, self.src, self.part, self.sems = net, src, part, sems
        self.rows = [j for j in range(1, net.wide)]
        self.cols = [i for i in range(1, net.tall)]

    @staticmethod
    def count(n_f):
        tall = 2 if n_f % 2 == 0 else 1
        wide = n_f // tall
        return 1 + 2 * (wide - 1) + 2 * (tall - 1) + 4 * (wide - 1) * (tall - 1)

    def at(self, kind, i, j):
        w, t = len(self.rows), len(self.cols)
        base = {
            "own": 0,
            "row": 1,
            "col": 1 + 2 * w,
            "half0": 1 + 2 * w + 2 * t,
            "half1": 1 + 2 * w + 2 * t + 2 * w * t,
        }[kind]
        if kind == "own":
            return self.sems.at[0]
        k = j - 1 if kind == "row" else i - 1 if kind == "col" else (i - 1) * w + j - 1
        return self.sems.at[base + 2 * k], self.sems.at[base + 2 * k + 1]

    def rank(self, i, j):
        net = self.net
        return ((net.a + i) % net.tall) * net.wide + (net.b + j) % net.wide

    def back(self, i, j):
        net = self.net
        return ((net.a - i + net.tall) % net.tall) * net.wide + (net.b - j + net.wide) % net.wide

    def own(self):
        return pltpu.make_async_copy(self.src, self.part(self.net.f, None), self.at("own", 0, 0))

    def first(self, i, j):
        send, recv = self.at("row" if i == 0 else "col", i, j)
        place = self.part(self.net.f, None)
        return put(place, place, send, recv, fsdp=self.rank(i, j))

    def came(self, i, j):
        send, recv = self.at("row" if i == 0 else "col", i, j)
        place = self.part(self.back(i, j), None)
        return put(place, place, send, recv, fsdp=self.rank(i, j))

    def second(self, half, i, j, came=False):
        send, recv = self.at("half0" if half == 0 else "half1", i, j)
        origin = self.back(i, j) if came else self.back(0, j) if half == 0 else self.back(i, 0)
        place = self.part(origin, half)
        return put(place, place, send, recv, fsdp=self.rank(i, 0) if half == 0 else self.rank(0, j))

    def prepare(self):
        self.own().start()

    def start(self):
        self.own().wait()
        for i in self.cols:
            self.first(i, 0).start()
        for j in self.rows:
            self.first(0, j).start()

    def relay(self):
        for j in self.rows:
            self.came(0, j).wait_recv()
            for i in self.cols:
                self.second(0, i, j).start()
        for i in self.cols:
            self.came(i, 0).wait_recv()
            for j in self.rows:
                self.second(1, i, j).start()

    def finish(self):
        for j in self.rows:
            self.first(0, j).wait_send()
        for i in self.cols:
            self.first(i, 0).wait_send()
        for i in self.cols:
            for j in self.rows:
                for half in range(2):
                    self.second(half, i, j, came=True).wait_recv()
                    self.second(half, i, j).wait_send()


class Line:
    def __init__(self, net, src, part, recv, send, local):
        self.net, self.src, self.part, self.recv, self.send, self.local = net, src, part, recv, send, local
        self.pieces = recv.shape[1]
        self.rows = src.shape[0] // self.pieces

    @staticmethod
    def sems(n_s, pieces=2):
        return [
            pltpu.SemaphoreType.DMA((n_s, pieces)),
            pltpu.SemaphoreType.DMA((4, n_s // 2, pieces)),
            pltpu.SemaphoreType.DMA((1,)),
        ]

    def cut(self, ref, piece):
        return ref.at[aligned(piece * self.rows, self.rows)]

    def own(self):
        return pltpu.make_async_copy(self.src, self.part(self.net.s), self.local.at[0])

    def on_line(self, src, chunk, side, hop, piece):
        return put(
            self.cut(src, piece),
            self.cut(self.part(chunk), piece),
            self.send.at[side, hop, piece],
            self.recv.at[chunk, piece],
            seq=self.net.s + 2 - 4 * side,
        )

    def to_mate(self, src, chunk, side, hop, piece):
        return put(
            self.cut(src, piece),
            self.cut(self.part(chunk), piece),
            self.send.at[2 + side, hop, piece],
            self.recv.at[chunk, piece],
            seq=self.net.mate,
        )

    def goes_on(self, side):
        after = self.net.z + 1 - 2 * side
        return (after >= 0) & (after < self.net.n_l)

    def each_piece(self, act):
        pl.loop(0, self.pieces)(act)

    def prepare(self):
        self.own().start()

    def start(self):
        net = self.net
        self.own().wait()
        place = self.part(net.s)

        @self.each_piece
        def _(piece):
            for side in range(2):

                @pl.when(self.goes_on(side))
                def _():
                    self.on_line(place, net.s, side, 0, piece).start()

            self.to_mate(place, net.s, 0, 0, piece).start()

    def came(self, chunk, piece):
        place = self.cut(self.part(chunk), piece)
        put(place, place, self.send.at[0, 0, 0], self.recv.at[chunk, piece], seq=self.net.mate).wait_recv()

    def step(self, hop):
        net = self.net

        @self.each_piece
        def _(piece):
            def act(other, side):
                chunk = 2 * other + net.c
                self.came(chunk, piece)

                @pl.when(self.goes_on(side))
                def _():
                    self.on_line(self.part(chunk), chunk, side, hop, piece).start()

                self.to_mate(self.part(chunk), chunk, side, hop, piece).start()

            net.sides(hop, act)

    def pair(self, other):
        @self.each_piece
        def _(piece):
            self.came(2 * other + 1 - self.net.c, piece)

    def here(self):
        self.pair(self.net.z)

    def finish(self):
        net = self.net
        place = self.part(net.s)

        @self.each_piece
        def _(piece):
            for side in range(2):

                @pl.when(self.goes_on(side))
                def _():
                    self.on_line(place, net.s, side, 0, piece).wait_send()

            self.to_mate(place, net.s, 0, 0, piece).wait_send()

            @pl.loop(1, net.n_l)
            def _(hop):
                def act(other, side):
                    chunk = 2 * other + net.c

                    @pl.when(self.goes_on(side))
                    def _():
                        self.on_line(self.part(chunk), chunk, side, hop, piece).wait_send()

                    self.to_mate(self.part(chunk), chunk, side, hop, piece).wait_send()

                net.sides(hop, act)


class Packets:
    def __init__(self, net, src, buf, sems):
        self.net, self.src, self.buf, self.sems = net, src, buf, sems

    @staticmethod
    def count(n_f, n_s):
        return 1 + 2 * (n_f - 1) + 2 * (n_s - 1)

    def own(self):
        net = self.net
        return pltpu.make_async_copy(self.src, self.buf.at[net.s, net.f], self.sems.at[0])

    def one(self, k, came=False):
        net = self.net
        f = (net.f - k + net.n_f) % net.n_f if came else net.f
        place = self.buf.at[net.s, f]
        return put(
            place if came else self.src,
            place,
            self.sems.at[2 * k - 1],
            self.sems.at[2 * k],
            fsdp=(net.f + k) % net.n_f,
        )

    def two(self, k, came=False):
        net = self.net
        place = self.buf.at[(net.s - k + net.n_s) % net.n_s if came else net.s]
        at = 2 * (net.n_f - 1) + 2 * k - 1
        return put(place, place, self.sems.at[at], self.sems.at[at + 1], seq=(net.s + k) % net.n_s)

    def start(self):
        self.own().start()
        for k in range(1, self.net.n_f):
            self.one(k).start()

    def middle(self):
        self.own().wait()
        for k in range(1, self.net.n_f):
            self.one(k, came=True).wait_recv()
            self.one(k).wait_send()
        for k in range(1, self.net.n_s):
            self.two(k).start()

    def finish(self):
        for k in range(1, self.net.n_s):
            self.two(k, came=True).wait_recv()
            self.two(k).wait_send()

    def unpack(self, out, width):
        net = self.net
        per = 128 // width
        for tile in range(net.n_f * net.n_s // per):
            total = None
            for j in range(per):
                f, s = divmod(tile * per + j, net.n_s)
                piece = self.buf[s, f]
                if j:
                    piece = pltpu.roll(piece, j * width, axis=1)
                total = piece if total is None else total + piece
            out[:, tile * 128 : (tile + 1) * 128] = total


def rotary(values, cosine, sine):
    columns = values.shape[1]
    half = ROT // 2
    times = columns // 128

    def wide(table):
        return table if times == 1 else jnp.concatenate([table] * times, axis=1)

    lane = lax.broadcasted_iota(jnp.int32, values.shape, 1)
    other = jnp.where(
        lane % HEAD < half, pltpu.roll(values, columns - half, axis=1), pltpu.roll(values, half, axis=1)
    )
    return values * wide(cosine) + other * wide(sine)


def rotary_tables(length):
    half = ROT // 2
    freqs = np.float32(10000.0) ** (-np.arange(half, dtype=np.float32) * np.float32(2.0 / ROT))
    angles = np.arange(length, dtype=np.float32)[:, None] * freqs[None, :].astype(np.float32)
    cosine, sine = np.cos(angles), np.sin(angles)
    rest = np.zeros((length, HEAD - ROT), np.float32)
    keep = np.concatenate([cosine, cosine, rest + 1], 1)
    swap = np.concatenate([-sine, sine, rest], 1)
    return [np.tile(t, (1, 128 // HEAD)).astype(np.float32) for t in (keep, swap)]


def normalize(values):
    center = values - jnp.mean(values, -1, keepdims=True)
    inverse = lax.rsqrt(jnp.mean(center * center, -1, keepdims=True) + EPSILON)
    return center * inverse, inverse


class Copies:
    def __init__(self, sems):
        self.sems, self.all, self.open = sems, [], []

    def start(self, src, dst):
        copy = pltpu.make_async_copy(src, dst, self.sems.at[len(self.all)])
        copy.start()
        self.all.append(copy)
        self.open.append(copy)
        return copy

    def wait(self, *copies):
        for copy in copies or list(self.open):
            copy.wait()
            self.open = [c for c in self.open if c is not copy]


def columns_of(ref, depth):
    half_rows = ref.shape[0] // 2

    def part(f, half):
        span = aligned(f * depth, depth)
        if half is None:
            return ref.at[:, span]
        return ref.at[pl.ds(half * half_rows, half_rows), span]

    return part


def rows_of(ref, chunk):
    return lambda s: ref.at[aligned(s * chunk, chunk)]


class Fold:
    def __init__(self, net, tile, total, mate_in, coming, mate_out, out, mate_send, mate_recv, send, recv):
        self.net, self.tile, self.total = net, tile, total
        self.mate_in, self.coming, self.mate_out, self.out = mate_in, coming, mate_out, out
        self.mate_send, self.mate_recv, self.send, self.recv = mate_send, mate_recv, send, recv
        self.chunk = total.shape[0]
        self.pieces = recv.shape[1]
        self.rows = self.chunk // self.pieces

    @staticmethod
    def shared(chunk, width):
        return [pltpu.VMEM((2 * chunk, TILE), F32), pltpu.VMEM((chunk, width), F32)]

    @staticmethod
    def buffers(n_s, chunk, width):
        n_l = n_s // 2
        return [
            pltpu.VMEM((n_l, chunk, width), BF),
            pltpu.VMEM((n_l + 1, chunk, width), BF),
            pltpu.VMEM((3, chunk, width), BF),
            pltpu.VMEM((n_l, chunk, width), BF),
        ]

    @staticmethod
    def sems(n_s, pieces=4):
        n_l = n_s // 2
        return [
            pltpu.SemaphoreType.DMA((3, pieces)),
            pltpu.SemaphoreType.DMA((n_l, pieces)),
            pltpu.SemaphoreType.DMA((n_l, pieces)),
            pltpu.SemaphoreType.DMA((n_l + 1, pieces)),
        ]

    def place(self, other):
        return (other >= 0) & (other < self.net.n_l)

    def fed(self, side):
        return self.place(self.net.z + 1 - 2 * side)

    def span(self, piece):
        return aligned(piece * self.rows, self.rows)

    def each_piece(self, act):
        pl.loop(0, self.pieces)(act)

    def to_mate(self, target, slot, piece):
        span = self.span(piece)
        return put(
            self.mate_out.at[slot, span],
            self.mate_in.at[target, span],
            self.mate_send.at[slot, piece],
            self.mate_recv.at[target, piece],
            seq=self.net.mate,
        )

    def onward(self, target, side, hop, piece):
        span = self.span(piece)
        slot = target + (self.net.n_l - target) * (1 - side) * (1 // hop)
        return put(
            self.out.at[target, span],
            self.coming.at[slot, span],
            self.send.at[target, piece],
            self.recv.at[slot, piece],
            seq=self.net.s + 4 * side - 2,
        )

    def came(self, slot, piece):
        place = self.coming.at[slot, self.span(piece)]
        put(place, place, self.send.at[0, 0], self.recv.at[slot, piece], seq=self.net.mate).wait_recv()

    def mate_sent(self, slot):
        self.each_piece(lambda piece: self.to_mate(self.net.z, slot, piece).wait_send())

    def begin_one(self, target, slot, produce):
        mine = aligned(self.net.c * self.chunk, self.chunk)
        theirs = aligned((1 - self.net.c) * self.chunk, self.chunk)

        def write(cols, value):
            self.tile[...] = value
            self.out[target, :, cols] = self.tile[mine, :].astype(BF)
            self.mate_out[slot, :, cols] = self.tile[theirs, :].astype(BF)

        produce(target, write)
        self.each_piece(lambda piece: self.to_mate(target, slot, piece).start())

    def leave(self, target, side, hop):
        @pl.when((hop > 0) & jnp.logical_not(self.fed(side)))
        def _():
            self.each_piece(lambda piece: self.pass_piece(target, side, hop, piece, False))

    def begin(self, produce, between=None):
        net = self.net

        @pl.loop(0, net.n_l)
        def _(j):
            hop = net.n_l - 1 - j

            def act(target, side):
                @pl.when((hop > 0) | (side == 0))
                def _():
                    @pl.when((hop > 0) & self.place(target + 2 * side - 1))
                    def _():
                        self.mate_sent(side)

                    self.begin_one(target, side + (2 - side) * (1 // (hop + 1)), produce)
                    self.leave(target, side, hop)

            net.sides(hop, act)
            if between is not None:
                pl.when(j == 1)(between)

    def pass_piece(self, target, side, hop, piece, fed):
        self.to_mate(target, 0, piece).wait_recv()
        span = self.span(piece)
        value = self.out[target, span, :].astype(F32) + self.mate_in[target, span, :].astype(F32)
        if fed:
            self.came(target, piece)
            value = value + self.coming[target, span, :].astype(F32)
        self.out[target, span, :] = value.astype(BF)
        self.onward(target, side, hop, piece).start()

    def open_total(self):
        net = self.net

        @self.each_piece
        def _(piece):
            self.to_mate(net.z, 0, piece).wait_recv()
            span = self.span(piece)
            self.total[span, :] = self.out[net.z, span, :].astype(F32) + self.mate_in[net.z, span, :].astype(F32)

    def wave(self, at, near=False, between=None):
        net = self.net
        above = at if near else net.n_l - at

        @pl.loop(0, 2)
        def _(turn):
            side = (1 - (2 * net.z) // net.n_l + turn) % 2
            target = net.n_l - 1 - above + (2 * above - net.n_l + 1) * side
            hop = (target - net.z) * (2 * side - 1)

            @self.each_piece
            def _(piece):
                span = self.span(piece)

                @pl.when(self.fed(side) & (hop > 0))
                def _():
                    self.pass_piece(target, side, hop, piece, True)

                @pl.when(self.fed(side) & (hop == 0))
                def _():
                    slot = net.z + (net.n_l - net.z) * (1 - side)
                    self.came(slot, piece)
                    self.total[span, :] = self.total[span, :] + self.coming[slot, span, :].astype(F32)

                if between is not None:
                    between(((at - 1) * 2 + turn) * self.pieces + piece)

    def passes_between(self, wave, near, between):
        net = self.net
        above = wave if near else net.n_l - wave

        @pl.loop(0, 2)
        def _(turn):
            side = (1 - (2 * net.z) // net.n_l + turn) % 2
            target = net.n_l - 1 - above + (2 * above - net.n_l + 1) * side
            hop = (target - net.z) * (2 * side - 1)

            @self.each_piece
            def _(piece):
                @pl.when((hop > 0) & self.fed(side))
                def _():
                    self.pass_piece(target, side, hop, piece, True)

                between(turn, piece)

    def finals(self):
        net = self.net

        @self.each_piece
        def _(piece):
            self.to_mate(net.z, 0, piece).wait_recv()
            span = self.span(piece)
            self.total[span, :] = self.out[net.z, span, :].astype(F32) + self.mate_in[net.z, span, :].astype(F32)

        @pl.loop(0, 2)
        def _(turn):
            side = (1 - (2 * net.z) // net.n_l + turn) % 2

            @pl.when(self.fed(side))
            def _():
                slot = net.z + (net.n_l - net.z) * (1 - side)

                @self.each_piece
                def _(piece):
                    span = self.span(piece)
                    self.came(slot, piece)
                    self.total[span, :] = self.total[span, :] + self.coming[slot, span, :].astype(F32)

    def finish(self):
        net = self.net
        self.mate_sent(2)
        for side in range(2):
            pl.when(self.place(net.z + 2 * side - 1))(functools.partial(self.mate_sent, side))

        @pl.loop(1, net.n_l)
        def _(hop):
            net.sides(
                hop,
                lambda target, side: self.each_piece(
                    lambda piece: self.onward(target, side, hop, piece).wait_send()
                ),
            )


class GridSum:
    def __init__(self, net, stage, came, sems):
        self.net, self.stage, self.came, self.sems = net, stage, came, sems
        self.half = stage.shape[1] // 2
        self.rows = next(r for r in (176, 128, 96, 64, 32, 16) if self.half % r == 0)
        self.cols = range(1, net.tall)
        self.along = range(1, net.wide)
        self.bases = self.layout(net.n_f)

    @staticmethod
    def layout(n_f):
        tall = 2 if n_f % 2 == 0 else 1
        wide = n_f // tall
        sizes = [(wide - 1) * tall, (tall - 1) * wide, tall - 1, wide - 1]
        return [sum(sizes[:at]) for at in range(5)]

    @staticmethod
    def scratch(n_f, rows, columns):
        count = GridSum.layout(n_f)[4]
        return [
            pltpu.VMEM((n_f, rows, columns), BF),
            pltpu.VMEM((count, rows // 2, columns), BF),
            pltpu.SemaphoreType.DMA((2, count + GridEnd.count(n_f))),
        ]

    def slot(self, kind, i, j):
        base = self.bases[kind]
        return base + [(j - 1) * self.net.tall + i, (i - 1) * self.net.wide + j, i - 1, j - 1][kind]

    def rank(self, i, j):
        net = self.net
        return ((net.a + i) % net.tall) * net.wide + (net.b + j) % net.wide

    def owner(self, at):
        return self.rank(at // self.net.wide, at % self.net.wide)

    def copy(self, kind, i, j):
        half = kind % 2
        along = kind in (0, 3)
        slot = self.slot(kind, i, j)
        at = i * self.net.wide + j
        return put(
            self.stage.at[at, pl.ds(half * self.half, self.half)],
            self.came.at[slot],
            self.sems.at[0, slot],
            self.sems.at[1, slot],
            fsdp=self.rank(0, j) if along else self.rank(i, 0),
        )

    def first(self, at):
        i, j = at // self.net.wide, at % self.net.wide

        @pl.when(j > 0)
        def _():
            self.copy(0, i, j).start()

        @pl.when(i > 0)
        def _():
            self.copy(1, i, j).start()

    def gather(self, half, at, slots, write):
        @pl.loop(0, self.half // self.rows)
        def _(step):
            span = aligned(half * self.half + step * self.rows, self.rows, 16)
            value = self.stage[at, span, :].astype(F32)
            for slot in slots:
                value = value + self.came[slot, aligned(step * self.rows, self.rows, 16), :].astype(F32)
            write(span, value)

    def wait(self, *copies):
        for kind, i, j in copies:
            self.copy(kind, i, j).wait_recv()
        return [self.slot(*copy) for copy in copies]

    def second(self):
        def keep(at):
            def write(span, value):
                self.stage[at, span, :] = value.astype(BF)

            return write

        for i in self.cols:
            at = i * self.net.wide
            self.gather(0, at, self.wait(*[(0, i, j) for j in self.along]), keep(at))
            self.copy(2, i, 0).start()
        for j in self.along:
            self.gather(1, j, self.wait(*[(1, i, j) for i in self.cols]), keep(j))
            self.copy(3, 0, j).start()

    def sum_first(self):
        def keep(at):
            def write(span, value):
                self.stage[at, span, :] = value.astype(BF)

            return write

        for i in range(self.net.tall):
            at = i * self.net.wide
            self.gather(0, at, self.wait(*[(0, i, j) for j in self.along]), keep(at))
        for j in range(self.net.wide):
            self.gather(1, j, self.wait(*[(1, i, j) for i in self.cols]), keep(j))

    def hand_on(self, out):
        net = self.net
        shards = [(0, 0), (0, 1), *[(i * net.wide, 0) for i in self.cols], *[(j, 1) for j in self.along]]
        return [
            pltpu.make_async_copy(
                self.stage.at[at, pl.ds(half * self.half, self.half)], out.at[k], self.sems.at[0, self.bases[4] + k]
            )
            for k, (at, half) in enumerate(shards)
        ]

    def last(self, out):
        def write(span, value):
            out[span, :] = value

        self.gather(
            0, 0, self.wait(*[(0, 0, j) for j in self.along], *[(2, i, 0) for i in self.cols]), write
        )
        self.gather(
            1, 0, self.wait(*[(1, i, 0) for i in self.cols], *[(3, 0, j) for j in self.along]), write
        )

    def finish_first(self):
        for i in range(self.net.tall):
            for j in range(self.net.wide):
                if j:
                    self.copy(0, i, j).wait_send()
                if i:
                    self.copy(1, i, j).wait_send()

    def finish(self):
        self.finish_first()
        for i in self.cols:
            self.copy(2, i, 0).wait_send()
        for j in self.along:
            self.copy(3, 0, j).wait_send()


class GridEnd:
    def __init__(self, net, sums, came, sems):
        self.net, self.sums, self.came, self.sems = net, sums, came, sems

    @staticmethod
    def count(n_f):
        tall = 2 if n_f % 2 == 0 else 1
        return tall + n_f // tall

    @staticmethod
    def scratch(n_f, rows, columns):
        count = GridEnd.count(n_f)
        return [
            pltpu.VMEM((count, rows // 2, columns), BF),
            pltpu.VMEM((count - 2, rows // 2, columns), BF),
            pltpu.SemaphoreType.DMA((2, count - 2)),
        ]

    def copies(self):
        net = self.net
        f = [((net.a + i) % net.tall) * net.wide + net.b for i in range(1, net.tall)]
        f += [net.a * net.wide + (net.b + j) % net.wide for j in range(1, net.wide)]
        return [
            put(self.sums.at[2 + k], self.came.at[k], self.sems.at[0, k], self.sems.at[1, k], fsdp=to)
            for k, to in enumerate(f)
        ]

    def start(self):
        for copy in self.copies():
            copy.start()

    def last(self, out):
        for copy in self.copies():
            copy.wait()
        half = self.sums.shape[1]
        rows = next(r for r in (176, 128, 96, 64, 32, 16) if half % r == 0)
        down = range(self.net.tall - 1)
        along = range(self.net.tall - 1, self.net.tall + self.net.wide - 2)
        for at, slots in enumerate((down, along)):

            @pl.loop(0, half // rows)
            def _(step):
                span = aligned(step * rows, rows, 16)
                value = self.sums[at, span, :].astype(F32)
                for slot in slots:
                    value = value + self.came[slot, span, :].astype(F32)
                out[aligned(at * half + step * rows, rows, 16), :] = value


class PacketSum:
    def __init__(self, net, out, seq_in, total, fsdp_in, sems):
        self.net, self.out, self.seq_in, self.total, self.fsdp_in, self.sems = net, out, seq_in, total, fsdp_in, sems

    @staticmethod
    def scratch(n_f, n_s):
        return [
            pltpu.VMEM((n_s, n_f, SMALL, 128), F32),
            pltpu.VMEM((n_s, n_f, SMALL, 128), F32),
            pltpu.VMEM((n_f, SMALL, 128), F32),
            pltpu.VMEM((n_f, SMALL, 128), F32),
            pltpu.SemaphoreType.DMA((2 * (n_f + n_s),)),
        ]

    def one(self, k):
        to = (self.net.s + k) % self.net.n_s
        return put(self.out.at[to], self.seq_in.at[k], self.sems.at[2 * k], self.sems.at[2 * k + 1], seq=to)

    def two(self, k):
        to = (self.net.f + k) % self.net.n_f
        at = 2 * (self.net.n_s + k)
        return put(self.total.at[to], self.fsdp_in.at[k], self.sems.at[at], self.sems.at[at + 1], fsdp=to)

    def start(self, terms, width):
        net = self.net
        per = 128 // width
        for tile in range(net.n_f * net.n_s // per):
            value = terms[:, tile * 128 : (tile + 1) * 128]
            for j in range(per):
                f, s = divmod(tile * per + j, net.n_s)
                self.out[s, f] = pltpu.roll(value, 128 - j * width, axis=1) if j else value
        for k in range(1, net.n_s):
            self.one(k).start()

    def middle(self):
        net = self.net
        total = self.out[net.s]
        for k in range(1, net.n_s):
            self.one(k).wait()
            total = total + self.seq_in[k]
        self.total[...] = total
        for k in range(1, net.n_f):
            self.two(k).start()

    def finish(self, result):
        net = self.net
        total = self.total[net.f]
        for k in range(1, net.n_f):
            self.two(k).wait()
            total = total + self.fsdp_in[k]
        result[...] = total


def norm_backward(rows, source, grad, gain, terms, at, write):
    terms[at : at + 2, :] = jnp.zeros((2, terms.shape[1]), F32)

    @pl.loop(0, rows // 32)
    def _(i):
        span = aligned(i * 32, 32)
        scaled, inverse = normalize(source[span, :].astype(F32))
        value = grad[span, :]
        upstream = value * gain
        inner = jnp.mean(upstream, -1, keepdims=True)
        cross = jnp.mean(upstream * scaled, -1, keepdims=True)
        terms[at : at + 1, :] = terms[at : at + 1, :] + jnp.sum(value * scaled, 0, keepdims=True)
        terms[at + 1 : at + 2, :] = terms[at + 1 : at + 2, :] + jnp.sum(value, 0, keepdims=True)
        write(i, span, inverse * (upstream - inner - scaled * cross))


def layer_kernel(
    tok,
    gain_one,
    shift_one,
    gain_two,
    shift_two,
    bias,
    wq_own,
    wo_own,
    wg_own,
    wu_own,
    wd_own,
    gout_own,
    cosine,
    sine,
    q_o,
    k_o,
    kt_o,
    v_o,
    att_o,
    lse_o,
    n1_o,
    gains_o,
    wq_o,
    wo_o,
    dm_o,
    datt_o,
    dmid_o,
    top_o,
    terms_o,
    gate_o,
    up_o,
    down_o,
    rows,
    gout,
    wq,
    wo,
    wg,
    wu,
    wd,
    q,
    k,
    kt,
    v,
    vt,
    ot,
    att,
    hidden,
    dgate,
    dup,
    mid,
    low,
    packet,
    packets,
    tiles,
    total,
    *rest,
):
    net = Net()
    chunk, width = tok.shape
    length = chunk * net.n_s
    depth = wq_own.shape[1]
    columns = wq_own.shape[2]
    heads = columns // HEAD
    pair = 2 * chunk
    buffers, rest = rest[:4], rest[4:]
    folds = []
    for _ in range(3):
        folds.append(Fold(net, tiles, total, *buffers, *rest[:4]))
        rest = rest[4:]
    att_fold, normed_fold, top_fold = folds
    line_sems = [rest[at : at + 3] for at in (0, 3, 6, 9)]
    rest = rest[12:]
    spread_sems, rest = rest[:5], rest[5:]
    gate_sum, up_sum, down_sum = [GridSum(net, *rest[at : at + 3]) for at in (0, 3, 6)]
    sums = (down_sum, gate_sum, up_sum)
    pk_sems, copy_sems, n1_sems, free_sem = rest[9:]
    copies = Copies(copy_sems)
    n1 = att_fold.mate_out

    packet[...] = jnp.zeros(packet.shape, F32)
    own = gain_one.shape[1]
    for at, part in enumerate((gain_one, shift_one, gain_two, shift_two)):
        packet[at : at + 1, 0:own] = part[...].astype(F32)
    packet[4:7, 0:own] = bias[...].astype(F32)
    def wq_part(f, half):
        if half is None:
            return wq.at[:, aligned(f * depth, depth), :]
        return wq.at[:, aligned(f * depth + half * (depth // 2), depth // 2), :]

    spread_q = Spread(net, wq_own, wq_part, spread_sems[0])
    spread_o, spread_g, spread_u, spread_d = [
        Spread(net, own, columns_of(full, depth), sems)
        for own, full, sems in zip((wo_own, wg_own, wu_own, wd_own), (wo, wg, wu, wd), spread_sems[1:])
    ]
    pk = Packets(net, packet, packets, pk_sems)
    line = Line(net, tok, rows_of(rows, chunk), *line_sems[0])
    gout_line = Line(net, gout_own, rows_of(gout, chunk), *line_sems[1])
    n2_line = Line(net, low, rows_of(rows, chunk), *line_sems[2])
    dm_line = Line(net, low, rows_of(rows, chunk), *line_sems[3])

    for ready in (line, spread_q, spread_o, spread_g, spread_u, spread_d, gout_line):
        ready.prepare()
    net.barrier()

    def pairs(which, hop):
        net.sides(hop, lambda other, side: which.pair(other))

    def blocks(hop, act):
        def once(other, side):
            @pl.when((hop > 0) | (side == 0))
            def _():
                act(other, side)

        net.sides(hop, once)

    pk.start()
    line.start()
    spread_q.start()
    pk.middle()
    pk.finish()
    pk.unpack(gains_o, width // (net.n_f * net.n_s))

    def project_block(other, side):
        span = aligned(other * pair, pair)
        gain, shift = gains_o[0:1, :], gains_o[1:2, :]

        for part in range(2):

            @pl.loop(0, chunk // 32)
            def _(i):
                at = aligned((2 * other + part) * chunk + i * 32, 32)
                scaled, _ = normalize(rows[at, :].astype(F32))
                n1[part, aligned(i * 32, 32), :] = (scaled * gain + shift).astype(BF)

        keeps = [
            pltpu.make_async_copy(
                n1.at[part], n1_o.at[aligned((2 * other + part) * chunk, chunk)], n1_sems.at[part]
            )
            for part in range(2)
        ]
        for copy in keeps:
            copy.start()
        left = n1[0:2].reshape(pair, width)
        cols = aligned(net.s * columns, columns)
        tables = cosine[span, :], sine[span, :]
        for kind in range(3):
            value = dot(left, wq[kind]) + gains_o[4 + kind : 5 + kind, cols]
            if kind == 0:
                q[span, :] = rotary(value, *tables).astype(BF)
            elif kind == 1:
                value = rotary(value, *tables)
                k[span, :] = value.astype(BF)
                kt[...] = value.T.astype(BF)
            else:
                v[...] = value.astype(BF)
                vt[:, span] = value.T.astype(BF)
        for copy in (
            pltpu.make_async_copy(kt, kt_o.at[:, span], n1_sems.at[2]),
            pltpu.make_async_copy(v, v_o.at[span], n1_sems.at[3]),
        ):
            copy.start()
            keeps.append(copy)
        for copy in keeps:
            copy.wait()

    line.here()
    for hop in range(1, net.n_l - 1):
        line.step(hop)
        if hop == 1:
            spread_q.relay()
        pairs(line, hop)
    spread_o.start()
    spread_q.finish()
    spread_g.start()
    pl.loop(0, net.n_l - 1)(lambda hop: blocks(hop, project_block))
    spread_o.relay()
    spread_u.start()
    line.step(net.n_l - 1)
    gout_line.start()
    pairs(line, net.n_l - 1)
    blocks(net.n_l - 1, project_block)
    q_copy = copies.start(q, q_o)
    for pair_of in ((wq, wq_o), (k, k_o)):
        copies.start(*pair_of)
    spread_o.finish()
    line.finish()

    def attend(i):
        lo, hi = i * pair, (i + 1) * pair

        @pl.loop(0, heads)
        def _(head):
            lane = lax.broadcasted_iota(jnp.int32, (1, columns), 1)
            here = jnp.where(lane // HEAD == head, HEAD**-0.5, 0.0).astype(BF)
            visible = lax.broadcasted_iota(jnp.int32, (pair, pair), 0) <= lax.broadcasted_iota(
                jnp.int32, (pair, pair), 1
            )
            head_rows = aligned(head * HEAD, HEAD)
            query = q[lo:hi, :] * here
            near = jnp.where(visible, dot_nt(k[lo:hi, :], query), NEG_LARGE)
            highest = jnp.max(near, 0, keepdims=True)
            if i:
                far = dot_nt(k[0:lo, :], query)
                highest = jnp.maximum(highest, jnp.max(far, 0, keepdims=True))
            near = jnp.exp(near - highest)
            sum_of = jnp.sum(near, 0, keepdims=True)
            out = dot(vt[head_rows, lo:hi], near.astype(BF))
            if i:
                far = jnp.exp(far - highest)
                sum_of = sum_of + jnp.sum(far, 0, keepdims=True)
                out = out + dot(vt[head_rows, 0:lo], far.astype(BF))
            ot[head_rows, :] = out / sum_of
            lse_o[pl.ds(head, 1), lo:hi] = highest + jnp.log(sum_of)

        att[lo:hi, :] = ot[...].T.astype(BF)

    def produce_attended(place, write):
        for i in range(net.n_l):
            pl.when(place == i)(functools.partial(attend, i))
        left = att[aligned(place * pair, pair), :]

        @pl.loop(0, width // TILE)
        def _(j):
            cols = aligned(j * TILE, TILE)
            write(cols, dot(left, wo[:, cols]))

    def relays():
        gout_line.step(1)
        spread_d.start()

    att_fold.begin(produce_attended, relays)
    copies.start(att, att_o)
    copies.start(wo, wo_o)
    if net.n_l > 2:
        gout_line.step(2)
    att_fold.open_total()
    spread_g.relay()
    for at in range(1, net.n_l):
        if 2 < at + 1 < net.n_l:
            gout_line.step(at + 1)
        att_fold.wave(at)
        if at == 1:
            spread_u.relay()
        if at == min(2, net.n_l - 1):
            spread_d.relay()
    gain_two, shift_two = gains_o[2:3, :], gains_o[3:4, :]

    @pl.loop(0, chunk // 32)
    def _(i):
        span = aligned(i * 32, 32)
        value = rows[aligned(net.s * chunk + i * 32, 32), :].astype(F32) + total[span, :]
        mid[span, :] = value
        scaled, _ = normalize(value)
        low[span, :] = (scaled * gain_two + shift_two).astype(BF)

    n2_line.prepare()
    n2_line.start()
    att_fold.finish()
    gout_line.here()
    pl.loop(1, net.n_l)(lambda hop: pairs(gout_line, hop))

    def forward_block(other):
        span = aligned(other * pair, pair)
        right = rows[span, :]
        half = hidden.shape[0] // 2

        @pl.loop(0, 2)
        def _(part):
            units = aligned(part * half, half, 16)
            gate = dot_nt(wg[units, :], right)
            up = dot_nt(wu[units, :], right)
            back = dot_nt(wd[units, :], gout[span, :])
            sigma = jax.nn.sigmoid(gate)
            active = gate * sigma
            hidden[units, span] = (active * up).astype(BF)
            dgate[units, span] = (back * up * (sigma * (1.0 + gate * (1.0 - sigma)))).astype(BF)
            dup[units, span] = (back * active).astype(BF)

    def produce_normed(place, write):
        span = aligned(place * pair, pair)
        left, right = dgate[:, span].T, dup[:, span].T

        @pl.loop(0, width // TILE)
        def _(j):
            cols = aligned(j * TILE, TILE)
            write(cols, dot(left, wg[:, cols]) + dot(right, wu[:, cols]))

    def begin_normed(other, side, hop):
        @pl.when(hop > 1)
        def _():
            normed_fold.mate_sent(side)

        normed_fold.begin_one(other, side + (2 - side) * (1 // (hop + 1)), produce_normed)

    def forward_blocks(hop):
        def act(other, side):
            forward_block(other)

            @pl.when(jnp.logical_not(normed_fold.fed(side)))
            def _():
                begin_normed(other, side, hop)
                normed_fold.leave(other, side, hop)

        net.sides(hop, act)

    def begin_fed(hop):
        def act(other, side):
            pl.when(normed_fold.fed(side))(lambda: begin_normed(other, side, hop))

        net.sides(hop, act)

    n2_line.here()
    for spread in (spread_g, spread_u, spread_d):
        spread.finish()
    forward_block(net.z)

    @pl.loop(1, net.n_l)
    def _(hop):
        n2_line.step(hop)
        pairs(n2_line, hop)
        pl.when(hop == 1)(lambda: normed_fold.begin_one(net.z, 2, produce_normed))
        forward_blocks(hop)
        pl.when(hop > 1)(lambda: begin_fed(hop - 1))

    begin_fed(net.n_l - 1)

    def weight_terms(task):
        at, kind = net.n_f - 1 - task // 3, task % 3
        cols = aligned(gate_sum.owner(at) * depth, depth)
        for way, (grid_sum, left, right) in enumerate(
            ((down_sum, hidden, gout), (gate_sum, dgate, rows), (up_sum, dup, rows))
        ):

            @pl.when(kind == way)
            def _():
                half = left.shape[0] // 2

                @pl.loop(0, 2)
                def _(part):
                    units = aligned(part * half, half, 16)
                    grid_sum.stage[at, units, :] = dot(left[units, :], right[:, cols]).astype(BF)

                grid_sum.first(at)

    tasks = 3 * net.n_f
    waves = max(net.n_l - 2, 1)
    each = -(-tasks // (2 * normed_fold.pieces * waves))
    for wave in range(net.n_l - waves, net.n_l):

        def between(turn, piece):
            slot = ((wave - net.n_l + waves) * 2 + turn) * normed_fold.pieces + piece

            @pl.loop(0, each)
            def _(i):
                pl.when(slot * each + i < tasks)(lambda: weight_terms(slot * each + i))

        normed_fold.passes_between(wave, True, between)
    normed_fold.finals()
    n2_line.finish()

    def beside(act):
        act(net.mate)
        for side in range(2):
            pl.when(n2_line.goes_on(side))(lambda: act(net.s + 2 - 4 * side))

    beside(lambda to: pl.semaphore_signal(free_sem, 1, device_id={"seq": to}, device_id_type=MESH))

    def write_middle(i, span, value):
        value = value + gout[aligned(net.s * chunk + i * 32, 32), :].astype(F32)
        dmid_o[span, :] = value
        low[span, :] = value.astype(BF)

    terms_o[...] = jnp.zeros(terms_o.shape, F32)
    norm_backward(chunk, mid, total, gain_two, terms_o, 2, write_middle)
    ends = (net.z + net.n_l - 1) // net.n_l + (2 * net.n_l - 2 - net.z) // net.n_l
    pl.semaphore_wait(free_sem, 1 + ends)
    dm_line.prepare()
    dm_line.start()
    normed_fold.finish()

    def produce_top(place, write):
        left = hidden[:, aligned(place * pair, pair)].T

        @pl.loop(0, width // TILE)
        def _(j):
            cols = aligned(j * TILE, TILE)
            write(cols, dot(left, wd[:, cols]))

    copies.wait(q_copy)
    datt = q

    def back_block(other, side):
        span = aligned(other * pair, pair)
        datt[span, :] = dot_nt(rows[span, :], wo[...]).astype(BF)

    dm_line.here()
    dm_line.step(1)
    top_fold.begin(produce_top)
    back_block(net.z, 0)
    top_fold.open_total()
    for at in range(1, net.n_l):
        if at + 1 < net.n_l:
            dm_line.step(at + 1)
        top_fold.wave(at)
        pairs(dm_line, at)
        net.sides(at, back_block)
    copies.start(datt, datt_o)
    copies.start(rows, dm_o)

    @pl.loop(0, chunk // 32)
    def _(i):
        span = aligned(i * 32, 32)
        top_fold.out[net.z, span, :] = (mid[span, :] + total[span, :]).astype(BF)

    copies.start(top_fold.out.at[net.z], top_o)
    top_fold.finish()
    gout_line.finish()
    dm_line.finish()
    hands = []
    for grid_sum, out in zip(sums, (down_o, gate_o, up_o)):
        grid_sum.sum_first()
        hands.extend(grid_sum.hand_on(out))
        for copy in grid_sum.hand_on(out):
            copy.start()
    for grid_sum in sums:
        grid_sum.finish_first()
    for copy in hands:
        copy.wait()
    copies.wait()


def layer_part(tokens, norms, wq, wo, wg, wu, wd, gout, tables):
    chunk, width = tokens.shape
    n_f, n_s = lax.axis_size("fsdp"), lax.axis_size("seq")
    length = chunk * n_s
    depth, columns = wq.shape[1:]
    units = wg.shape[0]
    shape = jax.ShapeDtypeStruct
    wide, head, turned, weight = (length, width), (length, columns), (units, length), (units, width)
    return pl.pallas_call(
        layer_kernel,
        name="layer",
        out_shape=[
            shape(head, BF),
            shape(head, BF),
            shape((columns, length), BF),
            shape(head, BF),
            shape(head, BF),
            shape((8, length), F32),
            shape(wide, BF),
            shape((SMALL, width), F32),
            shape((3, width, columns), BF),
            shape((columns, width), BF),
            shape(wide, BF),
            shape(head, BF),
            shape((chunk, width), F32),
            shape((chunk, width), BF),
            shape((SMALL, width), F32),
            *[shape((GridEnd.count(n_f), units // 2, depth), BF)] * 3,
        ],
        in_specs=[ANY, *[VMEM] * 5, *[ANY] * 6, VMEM, VMEM],
        out_specs=[*[ANY] * 5, VMEM, ANY, VMEM, *[ANY] * 4, VMEM, ANY, VMEM, *[ANY] * 3],
        scratch_shapes=[
            pltpu.VMEM(wide, BF),
            pltpu.VMEM(wide, BF),
            pltpu.VMEM((3, width, columns), BF),
            pltpu.VMEM((columns, width), BF),
            *[pltpu.VMEM(weight, BF)] * 3,
            pltpu.VMEM(head, BF),
            pltpu.VMEM(head, BF),
            pltpu.VMEM((columns, 2 * chunk), BF),
            pltpu.VMEM((2 * chunk, columns), BF),
            pltpu.VMEM((columns, length), BF),
            pltpu.VMEM((columns, 2 * chunk), F32),
            pltpu.VMEM(head, BF),
            *[pltpu.VMEM(turned, BF)] * 3,
            pltpu.VMEM((chunk, width), F32),
            pltpu.VMEM((chunk, width), BF),
            pltpu.VMEM((SMALL, 128), F32),
            pltpu.VMEM((n_s, n_f, SMALL, 128), F32),
            *Fold.shared(chunk, width),
            *Fold.buffers(n_s, chunk, width),
            *Fold.sems(n_s) * 3,
            *Line.sems(n_s) * 4,
            *[pltpu.SemaphoreType.DMA((Spread.count(n_f),))] * 5,
            *GridSum.scratch(n_f, units, depth) * 3,
            pltpu.SemaphoreType.DMA((Packets.count(n_f, n_s),)),
            pltpu.SemaphoreType.DMA((8,)),
            pltpu.SemaphoreType.DMA((4,)),
            pltpu.SemaphoreType.REGULAR,
        ],
        compiler_params=pltpu.CompilerParams(
            collective_id=1, has_side_effects=True, vmem_limit_bytes=VMEM_BYTES
        ),
        cost_estimate=pl.CostEstimate(
            flops=2 * length * width * (4 * columns + 9 * units),
            bytes_accessed=8 * length * width,
            transcendentals=length * (length * columns // HEAD + units),
        ),
    )(tokens, *norms, wq, wo, wg, wu, wd, gout, *tables)


def back_kernel(
    datt_in,
    q_in,
    k_in,
    kt_in,
    v_in,
    att_in,
    wq_in,
    n1_in,
    dm_in,
    down_in,
    gate_in,
    up_in,
    lse,
    tok,
    dmid,
    gains,
    terms_in,
    cosine,
    sine,
    gin_o,
    small_o,
    out_o,
    qkv_o,
    down_o,
    gate_o,
    up_o,
    datt,
    q,
    k,
    kt,
    v,
    att,
    wq,
    n1,
    dm,
    query,
    upstream,
    inners,
    dk,
    dv,
    dqt,
    dproj,
    terms,
    tiles,
    total,
    *rest,
):
    net = Net()
    chunk, width = tok.shape
    length, columns = q_in.shape
    heads = columns // HEAD
    pair = 2 * chunk
    depth = width // net.n_f
    block = 256
    buffers, rest = rest[:4], rest[4:]
    fold_sems, rest = rest[:4], rest[4:]
    packet_scratch, rest = rest[:5], rest[5:]
    out_sum, qkv_sum = GridSum(net, *rest[:3]), GridSum(net, *rest[3:6])
    ends = [GridEnd(net, *rest[at : at + 3]) for at in (6, 9, 12)]
    copy_sems, column_sems = rest[15:]

    copies = Copies(copy_sems)
    loads = [
        copies.start(src, dst)
        for src, dst in (
            (datt_in, datt),
            (q_in, q),
            (k_in, k),
            (kt_in, kt),
            (v_in, v),
            (att_in, att),
            (wq_in, wq),
            (down_in, ends[0].sums),
            (gate_in, ends[1].sums),
            (up_in, ends[2].sums),
        )
    ]
    def load(at, way):
        src, dst = ((n1_in, n1), (dm_in, dm))[way]
        cols = aligned(qkv_sum.owner(at) * depth, depth)
        return pltpu.make_async_copy(src.at[:, cols], dst.at[at % 2], column_sems.at[way, at % 2])

    for at in range(net.n_f - 1, max(net.n_f - 3, -1), -1):
        for way in range(2):
            load(at, way).start()

    @pl.loop(0, length // block)
    def _(i):
        span = aligned(i * block, block)
        dk[span, :] = jnp.zeros((block, columns), F32)
        dv[span, :] = jnp.zeros((block, columns), F32)

    net.barrier()
    copies.wait(*loads[:6])

    def start_ends():
        for load_of in loads[7:]:
            load_of.wait()
        for end in ends:
            end.start()


    of_head = (
        lax.broadcasted_iota(jnp.int32, (8, columns), 1) // HEAD
        == lax.broadcasted_iota(jnp.int32, (8, columns), 0)
    ).astype(F32)

    @pl.loop(0, length // block)
    def _(i):
        span = aligned(i * block, block)
        product = datt[span, :].astype(F32) * att[span, :].astype(F32)
        inners[:, span] = lax.dot_general(
            of_head,
            product,
            (((1,), (1,)), ((), ())),
            precision=lax.Precision.HIGHEST,
            preferred_element_type=F32,
        )

    @pl.loop(0, heads)
    def _(head):
        lane = lax.broadcasted_iota(jnp.int32, (1, columns), 1)
        here = jnp.where(lane // HEAD == head, 1.0, 0.0).astype(BF)
        scale = HEAD**-0.5
        visible = lax.broadcasted_iota(jnp.int32, (block, block), 0) <= lax.broadcasted_iota(
            jnp.int32, (block, block), 1
        )
        head_rows = aligned(head * HEAD, HEAD)

        @pl.loop(0, length // block)
        def _(i):
            span = aligned(i * block, block)
            query[span, :] = q[span, :] * (here * scale)
            upstream[span, :] = datt[span, :] * here

        pl.when(head == min(1, heads - 1))(start_ends)

        for j in range(length // block):
            at, end = j * block, (j + 1) * block
            keys, values, turned = k[at:end, :], v[at:end, :], kt[head_rows, at:end]

            def part(lo, hi, near):
                probs = jnp.exp(dot_nt(keys, query[lo:hi, :]) - lse[pl.ds(head, 1), lo:hi])
                if near:
                    probs = jnp.where(visible, probs, 0.0)
                grads = dot_nt(values, upstream[lo:hi, :])
                scores = (probs * (grads - inners[pl.ds(head, 1), lo:hi])).astype(BF)
                out = dot(turned, scores)
                dqt[head_rows, lo:hi] = dqt[head_rows, lo:hi] + out if j else out
                return dot(probs.astype(BF), upstream[lo:hi, :]), dot(scores, query[lo:hi, :])

            value_grads, key_grads = part(at, end, True)
            if end < length:
                more_values, more_keys = part(end, length, False)
                value_grads, key_grads = value_grads + more_values, key_grads + more_keys
            dv[at:end, :] = dv[at:end, :] + value_grads
            dk[at:end, :] = dk[at:end, :] + key_grads

    terms[...] = terms_in[...]
    bias_cols = aligned(net.s * columns, columns)

    @pl.loop(0, length // block)
    def _(i):
        span = aligned(i * block, block)
        tables = cosine[span, :], -sine[span, :]
        parts = [
            rotary((dqt[:, span].T * HEAD**-0.5).astype(BF).astype(F32), *tables).astype(BF),
            rotary(dk[span, :].astype(BF).astype(F32), *tables).astype(BF),
            dv[span, :].astype(BF),
        ]
        for kind in range(3):
            dproj[kind, span, :] = parts[kind]
            row = slice(4 + kind, 5 + kind)
            terms[row, bias_cols] = terms[row, bias_cols] + jnp.sum(parts[kind].astype(F32), 0, keepdims=True)

    def weight_terms(task):
        at = net.n_f - 1 - task // 2

        def loaded(way):
            load(at, way).wait()

        def next_load(way):
            pl.when(at >= 2)(lambda: load(at - 2, way).start())

        @pl.when(task % 2 == 0)
        def _():
            loaded(0)
            left = n1[at % 2].T
            for kind in range(3):
                qkv_sum.stage[at, kind * depth : (kind + 1) * depth, :] = dot(left, dproj[kind]).astype(BF)
            next_load(0)
            qkv_sum.first(at)

        @pl.when(task % 2 == 1)
        def _():
            loaded(1)
            out_sum.stage[at] = dot_tn(att[...], dm[at % 2]).astype(BF)
            next_load(1)
            out_sum.first(at)

    def produce(place, write):
        span = aligned(place * pair, pair)

        @pl.loop(0, width // TILE)
        def _(j):
            cols = aligned(j * TILE, TILE)
            value = dot_nt(dproj[0, span, :], wq[0, cols, :])
            for kind in range(1, 3):
                value = value + dot_nt(dproj[kind, span, :], wq[kind, cols, :])
            write(cols, value)

    fold = Fold(net, tiles, total, *buffers, *fold_sems)
    copies.wait(loads[6])
    fold.begin(produce)
    fold.open_total()
    tasks = 2 * net.n_f
    waves = max(net.n_l - 2, 1)
    each = -(-tasks // (2 * fold.pieces * waves))

    def between(slot):
        @pl.loop(0, each)
        def _(i):
            pl.when(slot * each + i < tasks)(lambda: weight_terms(slot * each + i))

    for at in range(1, waves + 1):
        fold.wave(at, between=between)
    for at in range(waves + 1, net.n_l):
        fold.wave(at)

    def write_input(i, span, value):
        gin_o[span, :] = value + dmid[span, :]

    norm_backward(chunk, tok, total, gains[0:1, :], terms, 0, write_input)
    packet_sum = PacketSum(net, *packet_scratch)
    packet_sum.start(terms, width // (net.n_f * net.n_s))
    for grid_sum in (qkv_sum, out_sum):
        grid_sum.second()
    packet_sum.middle()
    for end, out in zip(ends, (down_o, gate_o, up_o)):
        end.last(out)
    packet_sum.finish(small_o)
    fold.finish()
    for grid_sum, out in ((qkv_sum, qkv_o), (out_sum, out_o)):
        grid_sum.last(out)
        grid_sum.finish()


def back_part(datt, q, k, kt, v, att, wq, n1, dm, down, gate, up, lse, tokens, dmid, gains, terms, tables):
    chunk, width = tokens.shape
    n_f, n_s = lax.axis_size("fsdp"), lax.axis_size("seq")
    length, columns = q.shape
    depth = width // n_f
    units = 2 * gate.shape[1]
    shape = jax.ShapeDtypeStruct
    return pl.pallas_call(
        back_kernel,
        name="back",
        out_shape=[
            shape((chunk, width), F32),
            shape((SMALL, 128), F32),
            shape((columns, depth), F32),
            shape((3 * depth, columns), F32),
            *[shape((units, depth), F32)] * 3,
        ],
        in_specs=[ANY] * 12 + [VMEM] * 7,
        out_specs=[VMEM] * 7,
        scratch_shapes=[
            pltpu.VMEM((length, columns), BF),
            pltpu.VMEM((length, columns), BF),
            pltpu.VMEM((length, columns), BF),
            pltpu.VMEM((columns, length), BF),
            pltpu.VMEM((length, columns), BF),
            pltpu.VMEM((length, columns), BF),
            pltpu.VMEM((3, width, columns), BF),
            pltpu.VMEM((2, length, depth), BF),
            pltpu.VMEM((2, length, depth), BF),
            pltpu.VMEM((length, columns), BF),
            pltpu.VMEM((length, columns), BF),
            pltpu.VMEM((8, length), F32),
            pltpu.VMEM((length, columns), F32),
            pltpu.VMEM((length, columns), F32),
            pltpu.VMEM((columns, length), F32),
            pltpu.VMEM((3, length, columns), BF),
            pltpu.VMEM((SMALL, width), F32),
            *Fold.shared(chunk, width),
            *Fold.buffers(n_s, chunk, width),
            *Fold.sems(n_s, 8),
            *PacketSum.scratch(n_f, n_s),
            *GridSum.scratch(n_f, columns, depth),
            *GridSum.scratch(n_f, 3 * depth, columns),
            *GridEnd.scratch(n_f, units, depth) * 3,
            pltpu.SemaphoreType.DMA((10,)),
            pltpu.SemaphoreType.DMA((2, 2)),
        ],
        compiler_params=pltpu.CompilerParams(
            collective_id=3, has_side_effects=True, vmem_limit_bytes=VMEM_BYTES
        ),
        cost_estimate=pl.CostEstimate(
            flops=2 * length * columns * (8 * width + 5 * length),
            bytes_accessed=4 * length * width,
            transcendentals=length * length * columns // HEAD,
        ),
    )(datt, q, k, kt, v, att, wq, n1, dm, down, gate, up, lse, tokens, dmid, gains, terms, *tables)


def outputs_kernel(small, *refs):
    sources, targets, parts = refs[:7], refs[7:14], refs[14:]
    own = parts[0].shape[1]
    for src, dst in zip(sources, targets):
        dst[...] = src[...]
    for at in range(4):
        parts[at][...] = small[at : at + 1, 0:own]
    parts[4][...] = small[4:7, 0:own]


def outputs_part(small, own, *arrays):
    shape = jax.ShapeDtypeStruct
    return pl.pallas_call(
        outputs_kernel,
        name="outputs",
        out_shape=[shape(v.shape, v.dtype) for v in arrays]
        + [shape((1, own), F32)] * 4
        + [shape((3, own), F32)],
        in_specs=[VMEM] * 8,
        out_specs=[VMEM] * 12,
        compiler_params=pltpu.CompilerParams(vmem_limit_bytes=VMEM_BYTES),
    )(small, *arrays)


def per_device(
    tokens,
    gain_one,
    shift_one,
    w_qkv,
    b_qkv,
    w_out,
    gain_two,
    shift_two,
    w_gate,
    w_up,
    w_down,
    grad_output,
):
    length = tokens.shape[1] * lax.axis_size("seq")
    width = gain_one.shape[0]
    norms = [v[None] for v in (gain_one, shift_one, gain_two, shift_two)] + [b_qkv]
    tables = rotary_tables(length)
    q, k, kt, v, att, lse, n1, gains, wq, _, dm, datt, dmid, top, terms, gate, up, down = layer_part(
        tokens[0], norms, w_qkv.transpose(1, 0, 2), w_out, w_gate.T, w_up.T, w_down, grad_output[0], tables
    )
    grad_input, small, out, qkv, down, gate, up = back_part(
        datt, q, k, kt, v, att, wq, n1, dm, down, gate, up, lse, tokens[0], dmid, gains, terms, tables
    )

    top, grad_input, qkv, out, gate, up, down, one, shift, two, shift_to, bias = outputs_part(
        small, width, top, grad_input, qkv, out, gate, up, down
    )
    return (
        top[None],
        grad_input[None],
        one[0],
        shift[0],
        qkv.reshape(3, -1, qkv.shape[1]).transpose(1, 0, 2),
        bias,
        out,
        two[0],
        shift_to[0],
        gate.T,
        up.T,
        down,
    )


def solution(mesh):
    whole = P(("fsdp", "seq"))
    rows = P("fsdp", "seq", None)
    inner = P("seq", "fsdp")
    outer = P("fsdp", "seq")
    heads = P("fsdp", None, "seq")
    bias = P(None, ("fsdp", "seq"))
    return jax.shard_map(
        per_device,
        mesh=mesh,
        in_specs=(rows, whole, whole, heads, bias, inner, whole, whole, outer, outer, inner, rows),
        out_specs=(rows, rows, whole, whole, heads, bias, inner, whole, whole, outer, outer, inner),
        check_vma=False,
    )
```

```python
import functools

import jax
import jax.numpy as jnp
import numpy as np
from jax import lax
from jax.experimental import pallas as pl
from jax.experimental.pallas import tpu as pltpu
from jax.sharding import PartitionSpec as P

HEAD = 64
ROT = 16
EPSILON = 1e-05
NEG_LARGE = -1e30
MESH = pl.DeviceIdType.MESH
ANY = pl.BlockSpec(memory_space=pl.ANY)
VMEM = pl.BlockSpec(memory_space=pltpu.VMEM)
BF = jnp.bfloat16
F32 = jnp.float32
VMEM_BYTES = 60 * 2**20
TILE = 512
SMALL = 8


def put(src, dst, send, recv, **device):
    return pltpu.make_async_remote_copy(
        src_ref=src, dst_ref=dst, send_sem=send, recv_sem=recv, device_id=device, device_id_type=MESH
    )


def dot(left, right):
    return jnp.dot(left, right, preferred_element_type=F32)


def dot_nt(left, right):
    return lax.dot_general(left, right, (((1,), (1,)), ((), ())), preferred_element_type=F32)


def dot_tn(left, right):
    return lax.dot_general(left, right, (((0,), (0,)), ((), ())), preferred_element_type=F32)


def aligned(start, size, unit=None):
    return pl.ds(pl.multiple_of(start, unit or size), size)


class Net:
    def __init__(self):
        self.n_f, self.n_s = lax.axis_size("fsdp"), lax.axis_size("seq")
        self.tall = 2 if self.n_f % 2 == 0 else 1
        self.wide = self.n_f // self.tall
        self.n_l = self.n_s // 2
        self.f, self.s = lax.axis_index("fsdp"), lax.axis_index("seq")
        self.a, self.b = self.f // self.wide, self.f % self.wide
        self.z, self.c = self.s // 2, self.s % 2
        self.mate = self.s + 1 - 2 * self.c

    def barrier(self):
        sem = pltpu.get_barrier_semaphore()
        for k in range(1, self.n_f):
            pl.semaphore_signal(
                sem, inc=1, device_id={"fsdp": (self.f + k) % self.n_f}, device_id_type=MESH
            )
        for k in range(1, self.n_s):
            pl.semaphore_signal(
                sem, inc=1, device_id={"seq": (self.s + k) % self.n_s}, device_id_type=MESH
            )
        pl.semaphore_wait(sem, self.n_f + self.n_s - 2)

    def sides(self, hop, act):
        @pl.loop(0, 2)
        def _(side):
            other = self.z + (2 * side - 1) * hop

            @pl.when((other >= 0) & (other < self.n_l))
            def _():
                act(other, side)


class Spread:
    def __init__(self, net, src, part, sems):
        self.net, self.src, self.part, self.sems = net, src, part, sems
        self.rows = [j for j in range(1, net.wide)]
        self.cols = [i for i in range(1, net.tall)]

    @staticmethod
    def count(n_f):
        tall = 2 if n_f % 2 == 0 else 1
        wide = n_f // tall
        return 1 + 2 * (wide - 1) + 2 * (tall - 1) + 4 * (wide - 1) * (tall - 1)

    def at(self, kind, i, j):
        w, t = len(self.rows), len(self.cols)
        base = {
            "own": 0,
            "row": 1,
            "col": 1 + 2 * w,
            "half0": 1 + 2 * w + 2 * t,
            "half1": 1 + 2 * w + 2 * t + 2 * w * t,
        }[kind]
        if kind == "own":
            return self.sems.at[0]
        k = j - 1 if kind == "row" else i - 1 if kind == "col" else (i - 1) * w + j - 1
        return self.sems.at[base + 2 * k], self.sems.at[base + 2 * k + 1]

    def rank(self, i, j):
        net = self.net
        return ((net.a + i) % net.tall) * net.wide + (net.b + j) % net.wide

    def back(self, i, j):
        net = self.net
        return ((net.a - i + net.tall) % net.tall) * net.wide + (net.b - j + net.wide) % net.wide

    def own(self):
        return pltpu.make_async_copy(self.src, self.part(self.net.f, None), self.at("own", 0, 0))

    def first(self, i, j):
        send, recv = self.at("row" if i == 0 else "col", i, j)
        place = self.part(self.net.f, None)
        return put(place, place, send, recv, fsdp=self.rank(i, j))

    def came(self, i, j):
        send, recv = self.at("row" if i == 0 else "col", i, j)
        place = self.part(self.back(i, j), None)
        return put(place, place, send, recv, fsdp=self.rank(i, j))

    def second(self, half, i, j, came=False):
        send, recv = self.at("half0" if half == 0 else "half1", i, j)
        origin = self.back(i, j) if came else self.back(0, j) if half == 0 else self.back(i, 0)
        place = self.part(origin, half)
        return put(place, place, send, recv, fsdp=self.rank(i, 0) if half == 0 else self.rank(0, j))

    def prepare(self):
        self.own().start()

    def start(self):
        self.own().wait()
        for i in self.cols:
            self.first(i, 0).start()
        for j in self.rows:
            self.first(0, j).start()

    def relay(self):
        for j in self.rows:
            self.came(0, j).wait_recv()
            for i in self.cols:
                self.second(0, i, j).start()
        for i in self.cols:
            self.came(i, 0).wait_recv()
            for j in self.rows:
                self.second(1, i, j).start()

    def finish(self):
        for j in self.rows:
            self.first(0, j).wait_send()
        for i in self.cols:
            self.first(i, 0).wait_send()
        for i in self.cols:
            for j in self.rows:
                for half in range(2):
                    self.second(half, i, j, came=True).wait_recv()
                    self.second(half, i, j).wait_send()


class Line:
    def __init__(self, net, src, part, recv, send, local):
        self.net, self.src, self.part, self.recv, self.send, self.local = net, src, part, recv, send, local
        self.pieces = recv.shape[1]
        self.rows = src.shape[0] // self.pieces

    @staticmethod
    def sems(n_s, pieces=2):
        return [
            pltpu.SemaphoreType.DMA((n_s, pieces)),
            pltpu.SemaphoreType.DMA((4, n_s // 2, pieces)),
            pltpu.SemaphoreType.DMA((1,)),
        ]

    def cut(self, ref, piece):
        return ref.at[aligned(piece * self.rows, self.rows)]

    def own(self):
        return pltpu.make_async_copy(self.src, self.part(self.net.s), self.local.at[0])

    def on_line(self, src, chunk, side, hop, piece):
        return put(
            self.cut(src, piece),
            self.cut(self.part(chunk), piece),
            self.send.at[side, hop, piece],
            self.recv.at[chunk, piece],
            seq=self.net.s + 2 - 4 * side,
        )

    def to_mate(self, src, chunk, side, hop, piece):
        return put(
            self.cut(src, piece),
            self.cut(self.part(chunk), piece),
            self.send.at[2 + side, hop, piece],
            self.recv.at[chunk, piece],
            seq=self.net.mate,
        )

    def goes_on(self, side):
        after = self.net.z + 1 - 2 * side
        return (after >= 0) & (after < self.net.n_l)

    def each_piece(self, act):
        pl.loop(0, self.pieces)(act)

    def prepare(self):
        self.own().start()

    def start(self):
        net = self.net
        self.own().wait()
        place = self.part(net.s)

        @self.each_piece
        def _(piece):
            for side in range(2):

                @pl.when(self.goes_on(side))
                def _():
                    self.on_line(place, net.s, side, 0, piece).start()

            self.to_mate(place, net.s, 0, 0, piece).start()

    def came(self, chunk, piece):
        place = self.cut(self.part(chunk), piece)
        put(place, place, self.send.at[0, 0, 0], self.recv.at[chunk, piece], seq=self.net.mate).wait_recv()

    def step(self, hop):
        net = self.net

        @self.each_piece
        def _(piece):
            def act(other, side):
                chunk = 2 * other + net.c
                self.came(chunk, piece)

                @pl.when(self.goes_on(side))
                def _():
                    self.on_line(self.part(chunk), chunk, side, hop, piece).start()

                self.to_mate(self.part(chunk), chunk, side, hop, piece).start()

            net.sides(hop, act)

    def pair(self, other):
        @self.each_piece
        def _(piece):
            self.came(2 * other + 1 - self.net.c, piece)

    def here(self):
        self.pair(self.net.z)

    def finish(self):
        net = self.net
        place = self.part(net.s)

        @self.each_piece
        def _(piece):
            for side in range(2):

                @pl.when(self.goes_on(side))
                def _():
                    self.on_line(place, net.s, side, 0, piece).wait_send()

            self.to_mate(place, net.s, 0, 0, piece).wait_send()

            @pl.loop(1, net.n_l)
            def _(hop):
                def act(other, side):
                    chunk = 2 * other + net.c

                    @pl.when(self.goes_on(side))
                    def _():
                        self.on_line(self.part(chunk), chunk, side, hop, piece).wait_send()

                    self.to_mate(self.part(chunk), chunk, side, hop, piece).wait_send()

                net.sides(hop, act)


class Packets:
    def __init__(self, net, src, buf, sems):
        self.net, self.src, self.buf, self.sems = net, src, buf, sems

    @staticmethod
    def count(n_f, n_s):
        return 1 + 2 * (n_f - 1) + 2 * (n_s - 1)

    def own(self):
        net = self.net
        return pltpu.make_async_copy(self.src, self.buf.at[net.s, net.f], self.sems.at[0])

    def one(self, k, came=False):
        net = self.net
        f = (net.f - k + net.n_f) % net.n_f if came else net.f
        place = self.buf.at[net.s, f]
        return put(
            place if came else self.src,
            place,
            self.sems.at[2 * k - 1],
            self.sems.at[2 * k],
            fsdp=(net.f + k) % net.n_f,
        )

    def two(self, k, came=False):
        net = self.net
        place = self.buf.at[(net.s - k + net.n_s) % net.n_s if came else net.s]
        at = 2 * (net.n_f - 1) + 2 * k - 1
        return put(place, place, self.sems.at[at], self.sems.at[at + 1], seq=(net.s + k) % net.n_s)

    def start(self):
        self.own().start()
        for k in range(1, self.net.n_f):
            self.one(k).start()

    def middle(self):
        self.own().wait()
        for k in range(1, self.net.n_f):
            self.one(k, came=True).wait_recv()
            self.one(k).wait_send()
        for k in range(1, self.net.n_s):
            self.two(k).start()

    def finish(self):
        for k in range(1, self.net.n_s):
            self.two(k, came=True).wait_recv()
            self.two(k).wait_send()

    def unpack(self, out, width):
        net = self.net
        per = 128 // width
        for tile in range(net.n_f * net.n_s // per):
            total = None
            for j in range(per):
                f, s = divmod(tile * per + j, net.n_s)
                piece = self.buf[s, f]
                if j:
                    piece = pltpu.roll(piece, j * width, axis=1)
                total = piece if total is None else total + piece
            out[:, tile * 128 : (tile + 1) * 128] = total


def rotary(values, cosine, sine):
    columns = values.shape[1]
    half = ROT // 2
    times = columns // 128

    def wide(table):
        return table if times == 1 else jnp.concatenate([table] * times, axis=1)

    lane = lax.broadcasted_iota(jnp.int32, values.shape, 1)
    other = jnp.where(
        lane % HEAD < half, pltpu.roll(values, columns - half, axis=1), pltpu.roll(values, half, axis=1)
    )
    return values * wide(cosine) + other * wide(sine)


def rotary_tables(length):
    half = ROT // 2
    freqs = np.float32(10000.0) ** (-np.arange(half, dtype=np.float32) * np.float32(2.0 / ROT))
    angles = np.arange(length, dtype=np.float32)[:, None] * freqs[None, :].astype(np.float32)
    cosine, sine = np.cos(angles), np.sin(angles)
    rest = np.zeros((length, HEAD - ROT), np.float32)
    keep = np.concatenate([cosine, cosine, rest + 1], 1)
    swap = np.concatenate([-sine, sine, rest], 1)
    return [np.tile(t, (1, 128 // HEAD)).astype(np.float32) for t in (keep, swap)]


def normalize(values):
    center = values - jnp.mean(values, -1, keepdims=True)
    inverse = lax.rsqrt(jnp.mean(center * center, -1, keepdims=True) + EPSILON)
    return center * inverse, inverse


class Copies:
    def __init__(self, sems):
        self.sems, self.all, self.open = sems, [], []

    def start(self, src, dst):
        copy = pltpu.make_async_copy(src, dst, self.sems.at[len(self.all)])
        copy.start()
        self.all.append(copy)
        self.open.append(copy)
        return copy

    def wait(self, *copies):
        for copy in copies or list(self.open):
            copy.wait()
            self.open = [c for c in self.open if c is not copy]


def columns_of(ref, depth):
    half_rows = ref.shape[0] // 2

    def part(f, half):
        span = aligned(f * depth, depth)
        if half is None:
            return ref.at[:, span]
        return ref.at[pl.ds(half * half_rows, half_rows), span]

    return part


def rows_of(ref, chunk):
    return lambda s: ref.at[aligned(s * chunk, chunk)]


class Fold:
    def __init__(self, net, tile, total, mate_in, coming, mate_out, out, mate_send, mate_recv, send, recv):
        self.net, self.tile, self.total = net, tile, total
        self.mate_in, self.coming, self.mate_out, self.out = mate_in, coming, mate_out, out
        self.mate_send, self.mate_recv, self.send, self.recv = mate_send, mate_recv, send, recv
        self.chunk = total.shape[0]
        self.pieces = recv.shape[1]
        self.rows = self.chunk // self.pieces

    @staticmethod
    def shared(chunk, width):
        return [pltpu.VMEM((2 * chunk, TILE), F32), pltpu.VMEM((chunk, width), F32)]

    @staticmethod
    def buffers(n_s, chunk, width):
        n_l = n_s // 2
        return [
            pltpu.VMEM((n_l, chunk, width), BF),
            pltpu.VMEM((n_l + 1, chunk, width), BF),
            pltpu.VMEM((3, chunk, width), BF),
            pltpu.VMEM((n_l, chunk, width), BF),
        ]

    @staticmethod
    def sems(n_s, pieces=4):
        n_l = n_s // 2
        return [
            pltpu.SemaphoreType.DMA((3, pieces)),
            pltpu.SemaphoreType.DMA((n_l, pieces)),
            pltpu.SemaphoreType.DMA((n_l, pieces)),
            pltpu.SemaphoreType.DMA((n_l + 1, pieces)),
        ]

    def place(self, other):
        return (other >= 0) & (other < self.net.n_l)

    def fed(self, side):
        return self.place(self.net.z + 1 - 2 * side)

    def span(self, piece):
        return aligned(piece * self.rows, self.rows)

    def each_piece(self, act):
        pl.loop(0, self.pieces)(act)

    def to_mate(self, target, slot, piece):
        span = self.span(piece)
        return put(
            self.mate_out.at[slot, span],
            self.mate_in.at[target, span],
            self.mate_send.at[slot, piece],
            self.mate_recv.at[target, piece],
            seq=self.net.mate,
        )

    def onward(self, target, side, hop, piece):
        span = self.span(piece)
        slot = target + (self.net.n_l - target) * (1 - side) * (1 // hop)
        return put(
            self.out.at[target, span],
            self.coming.at[slot, span],
            self.send.at[target, piece],
            self.recv.at[slot, piece],
            seq=self.net.s + 4 * side - 2,
        )

    def came(self, slot, piece):
        place = self.coming.at[slot, self.span(piece)]
        put(place, place, self.send.at[0, 0], self.recv.at[slot, piece], seq=self.net.mate).wait_recv()

    def mate_sent(self, slot):
        self.each_piece(lambda piece: self.to_mate(self.net.z, slot, piece).wait_send())

    def begin_one(self, target, slot, produce):
        mine = aligned(self.net.c * self.chunk, self.chunk)
        theirs = aligned((1 - self.net.c) * self.chunk, self.chunk)

        def write(cols, value):
            self.tile[...] = value
            self.out[target, :, cols] = self.tile[mine, :].astype(BF)
            self.mate_out[slot, :, cols] = self.tile[theirs, :].astype(BF)

        produce(target, write)
        self.each_piece(lambda piece: self.to_mate(target, slot, piece).start())

    def leave(self, target, side, hop):
        @pl.when((hop > 0) & jnp.logical_not(self.fed(side)))
        def _():
            self.each_piece(lambda piece: self.pass_piece(target, side, hop, piece, False))

    def begin(self, produce, between=None, meanwhile=None):
        net = self.net

        @pl.loop(0, net.n_l)
        def _(j):
            hop = net.n_l - 1 - j

            @pl.loop(0, 2)
            def _(side):
                target = net.z + (2 * side - 1) * hop
                here = self.place(target) & ((hop > 0) | (side == 0))

                @pl.when(here)
                def _():
                    @pl.when((hop > 0) & self.place(target + 2 * side - 1))
                    def _():
                        self.mate_sent(side)

                    self.begin_one(target, side + (2 - side) * (1 // (hop + 1)), produce)

                if meanwhile is not None:
                    pl.when(hop > 0)(lambda: meanwhile(2 * j + side))

                pl.when(here)(lambda: self.leave(target, side, hop))

            if between is not None:
                pl.when(j == 1)(between)

    def pass_piece(self, target, side, hop, piece, fed):
        self.to_mate(target, 0, piece).wait_recv()
        span = self.span(piece)
        value = self.out[target, span, :].astype(F32) + self.mate_in[target, span, :].astype(F32)
        if fed:
            self.came(target, piece)
            value = value + self.coming[target, span, :].astype(F32)
        self.out[target, span, :] = value.astype(BF)
        self.onward(target, side, hop, piece).start()

    def open_total(self):
        net = self.net

        @self.each_piece
        def _(piece):
            self.to_mate(net.z, 0, piece).wait_recv()
            span = self.span(piece)
            self.total[span, :] = self.out[net.z, span, :].astype(F32) + self.mate_in[net.z, span, :].astype(F32)

    def wave(self, at, near=False, between=None):
        net = self.net
        above = at if near else net.n_l - at

        @pl.loop(0, 2)
        def _(turn):
            side = (1 - (2 * net.z) // net.n_l + turn) % 2
            target = net.n_l - 1 - above + (2 * above - net.n_l + 1) * side
            hop = (target - net.z) * (2 * side - 1)

            @self.each_piece
            def _(piece):
                span = self.span(piece)

                @pl.when(self.fed(side) & (hop > 0))
                def _():
                    self.pass_piece(target, side, hop, piece, True)

                @pl.when(self.fed(side) & (hop == 0))
                def _():
                    slot = net.z + (net.n_l - net.z) * (1 - side)
                    self.came(slot, piece)
                    self.total[span, :] = self.total[span, :] + self.coming[slot, span, :].astype(F32)

                if between is not None:
                    between(((at - 1) * 2 + turn) * self.pieces + piece)

    def passes_between(self, wave, near, between):
        net = self.net
        above = wave if near else net.n_l - wave

        @pl.loop(0, 2)
        def _(turn):
            side = (1 - (2 * net.z) // net.n_l + turn) % 2
            target = net.n_l - 1 - above + (2 * above - net.n_l + 1) * side
            hop = (target - net.z) * (2 * side - 1)

            @self.each_piece
            def _(piece):
                @pl.when((hop > 0) & self.fed(side))
                def _():
                    self.pass_piece(target, side, hop, piece, True)

                between(turn, piece)

    def finals(self):
        net = self.net

        @self.each_piece
        def _(piece):
            self.to_mate(net.z, 0, piece).wait_recv()
            span = self.span(piece)
            self.total[span, :] = self.out[net.z, span, :].astype(F32) + self.mate_in[net.z, span, :].astype(F32)

        @pl.loop(0, 2)
        def _(turn):
            side = (1 - (2 * net.z) // net.n_l + turn) % 2

            @pl.when(self.fed(side))
            def _():
                slot = net.z + (net.n_l - net.z) * (1 - side)

                @self.each_piece
                def _(piece):
                    span = self.span(piece)
                    self.came(slot, piece)
                    self.total[span, :] = self.total[span, :] + self.coming[slot, span, :].astype(F32)

    def finish(self):
        net = self.net
        self.mate_sent(2)
        for side in range(2):
            pl.when(self.place(net.z + 2 * side - 1))(functools.partial(self.mate_sent, side))

        @pl.loop(1, net.n_l)
        def _(hop):
            net.sides(
                hop,
                lambda target, side: self.each_piece(
                    lambda piece: self.onward(target, side, hop, piece).wait_send()
                ),
            )


class GridSum:
    def __init__(self, net, stage, came, sems):
        self.net, self.stage, self.came, self.sems = net, stage, came, sems
        self.half = stage.shape[1] // 2
        self.rows = next(r for r in (176, 128, 96, 64, 32, 16) if self.half % r == 0)
        self.cols = range(1, net.tall)
        self.along = range(1, net.wide)
        self.bases = self.layout(net.n_f)

    @staticmethod
    def layout(n_f):
        tall = 2 if n_f % 2 == 0 else 1
        wide = n_f // tall
        sizes = [(wide - 1) * tall, (tall - 1) * wide, tall - 1, wide - 1]
        return [sum(sizes[:at]) for at in range(5)]

    @staticmethod
    def scratch(n_f, rows, columns):
        count = GridSum.layout(n_f)[4]
        return [
            pltpu.VMEM((n_f, rows, columns), BF),
            pltpu.VMEM((count, rows // 2, columns), BF),
            pltpu.SemaphoreType.DMA((2, count + GridEnd.count(n_f))),
        ]

    def slot(self, kind, i, j):
        base = self.bases[kind]
        return base + [(j - 1) * self.net.tall + i, (i - 1) * self.net.wide + j, i - 1, j - 1][kind]

    def rank(self, i, j):
        net = self.net
        return ((net.a + i) % net.tall) * net.wide + (net.b + j) % net.wide

    def owner(self, at):
        return self.rank(at // self.net.wide, at % self.net.wide)

    def copy(self, kind, i, j):
        half = kind % 2
        along = kind in (0, 3)
        slot = self.slot(kind, i, j)
        at = i * self.net.wide + j
        return put(
            self.stage.at[at, pl.ds(half * self.half, self.half)],
            self.came.at[slot],
            self.sems.at[0, slot],
            self.sems.at[1, slot],
            fsdp=self.rank(0, j) if along else self.rank(i, 0),
        )

    def first(self, at):
        i, j = at // self.net.wide, at % self.net.wide

        @pl.when(j > 0)
        def _():
            self.copy(0, i, j).start()

        @pl.when(i > 0)
        def _():
            self.copy(1, i, j).start()

    def gather(self, half, at, slots, write):
        @pl.loop(0, self.half // self.rows)
        def _(step):
            span = aligned(half * self.half + step * self.rows, self.rows, 16)
            value = self.stage[at, span, :].astype(F32)
            for slot in slots:
                value = value + self.came[slot, aligned(step * self.rows, self.rows, 16), :].astype(F32)
            write(span, value)

    def wait(self, *copies):
        for kind, i, j in copies:
            self.copy(kind, i, j).wait_recv()
        return [self.slot(*copy) for copy in copies]

    def second(self):
        def keep(at):
            def write(span, value):
                self.stage[at, span, :] = value.astype(BF)

            return write

        for i in self.cols:
            at = i * self.net.wide
            self.gather(0, at, self.wait(*[(0, i, j) for j in self.along]), keep(at))
            self.copy(2, i, 0).start()
        for j in self.along:
            self.gather(1, j, self.wait(*[(1, i, j) for i in self.cols]), keep(j))
            self.copy(3, 0, j).start()

    def sum_first(self):
        def keep(at):
            def write(span, value):
                self.stage[at, span, :] = value.astype(BF)

            return write

        for i in range(self.net.tall):
            at = i * self.net.wide
            self.gather(0, at, self.wait(*[(0, i, j) for j in self.along]), keep(at))
        for j in range(self.net.wide):
            self.gather(1, j, self.wait(*[(1, i, j) for i in self.cols]), keep(j))

    def hand_on(self, out):
        net = self.net
        shards = [(0, 0), (0, 1), *[(i * net.wide, 0) for i in self.cols], *[(j, 1) for j in self.along]]
        return [
            pltpu.make_async_copy(
                self.stage.at[at, pl.ds(half * self.half, self.half)], out.at[k], self.sems.at[0, self.bases[4] + k]
            )
            for k, (at, half) in enumerate(shards)
        ]

    def last(self, out):
        def write(span, value):
            out[span, :] = value

        self.gather(
            0, 0, self.wait(*[(0, 0, j) for j in self.along], *[(2, i, 0) for i in self.cols]), write
        )
        self.gather(
            1, 0, self.wait(*[(1, i, 0) for i in self.cols], *[(3, 0, j) for j in self.along]), write
        )

    def finish_first(self):
        for i in range(self.net.tall):
            for j in range(self.net.wide):
                if j:
                    self.copy(0, i, j).wait_send()
                if i:
                    self.copy(1, i, j).wait_send()

    def finish(self):
        self.finish_first()
        for i in self.cols:
            self.copy(2, i, 0).wait_send()
        for j in self.along:
            self.copy(3, 0, j).wait_send()


class GridEnd:
    def __init__(self, net, sums, came, sems):
        self.net, self.sums, self.came, self.sems = net, sums, came, sems

    @staticmethod
    def count(n_f):
        tall = 2 if n_f % 2 == 0 else 1
        return tall + n_f // tall

    @staticmethod
    def scratch(n_f, rows, columns):
        count = GridEnd.count(n_f)
        return [
            pltpu.VMEM((count, rows // 2, columns), BF),
            pltpu.VMEM((count - 2, rows // 2, columns), BF),
            pltpu.SemaphoreType.DMA((2, count - 2)),
        ]

    def copies(self):
        net = self.net
        f = [((net.a + i) % net.tall) * net.wide + net.b for i in range(1, net.tall)]
        f += [net.a * net.wide + (net.b + j) % net.wide for j in range(1, net.wide)]
        return [
            put(self.sums.at[2 + k], self.came.at[k], self.sems.at[0, k], self.sems.at[1, k], fsdp=to)
            for k, to in enumerate(f)
        ]

    def start(self):
        for copy in self.copies():
            copy.start()

    def last(self, out):
        for copy in self.copies():
            copy.wait()
        half = self.sums.shape[1]
        rows = next(r for r in (176, 128, 96, 64, 32, 16) if half % r == 0)
        down = range(self.net.tall - 1)
        along = range(self.net.tall - 1, self.net.tall + self.net.wide - 2)
        for at, slots in enumerate((down, along)):

            @pl.loop(0, half // rows)
            def _(step):
                span = aligned(step * rows, rows, 16)
                value = self.sums[at, span, :].astype(F32)
                for slot in slots:
                    value = value + self.came[slot, span, :].astype(F32)
                out[aligned(at * half + step * rows, rows, 16), :] = value


class PacketSum:
    def __init__(self, net, out, seq_in, total, fsdp_in, sems):
        self.net, self.out, self.seq_in, self.total, self.fsdp_in, self.sems = net, out, seq_in, total, fsdp_in, sems

    @staticmethod
    def scratch(n_f, n_s):
        return [
            pltpu.VMEM((n_s, n_f, SMALL, 128), F32),
            pltpu.VMEM((n_s, n_f, SMALL, 128), F32),
            pltpu.VMEM((n_f, SMALL, 128), F32),
            pltpu.VMEM((n_f, SMALL, 128), F32),
            pltpu.SemaphoreType.DMA((2 * (n_f + n_s),)),
        ]

    def one(self, k):
        to = (self.net.s + k) % self.net.n_s
        return put(self.out.at[to], self.seq_in.at[k], self.sems.at[2 * k], self.sems.at[2 * k + 1], seq=to)

    def two(self, k):
        to = (self.net.f + k) % self.net.n_f
        at = 2 * (self.net.n_s + k)
        return put(self.total.at[to], self.fsdp_in.at[k], self.sems.at[at], self.sems.at[at + 1], fsdp=to)

    def start(self, terms, width):
        net = self.net
        per = 128 // width
        for tile in range(net.n_f * net.n_s // per):
            value = terms[:, tile * 128 : (tile + 1) * 128]
            for j in range(per):
                f, s = divmod(tile * per + j, net.n_s)
                self.out[s, f] = pltpu.roll(value, 128 - j * width, axis=1) if j else value
        for k in range(1, net.n_s):
            self.one(k).start()

    def middle(self):
        net = self.net
        total = self.out[net.s]
        for k in range(1, net.n_s):
            self.one(k).wait()
            total = total + self.seq_in[k]
        self.total[...] = total
        for k in range(1, net.n_f):
            self.two(k).start()

    def finish(self, result):
        net = self.net
        total = self.total[net.f]
        for k in range(1, net.n_f):
            self.two(k).wait()
            total = total + self.fsdp_in[k]
        result[...] = total


def norm_backward(rows, source, grad, gain, terms, at, write):
    terms[at : at + 2, :] = jnp.zeros((2, terms.shape[1]), F32)

    @pl.loop(0, rows // 32, unroll=2)
    def _(i):
        span = aligned(i * 32, 32)
        scaled, inverse = normalize(source[span, :].astype(F32))
        value = grad[span, :]
        upstream = value * gain
        inner = jnp.mean(upstream, -1, keepdims=True)
        cross = jnp.mean(upstream * scaled, -1, keepdims=True)
        terms[at : at + 1, :] = terms[at : at + 1, :] + jnp.sum(value * scaled, 0, keepdims=True)
        terms[at + 1 : at + 2, :] = terms[at + 1 : at + 2, :] + jnp.sum(value, 0, keepdims=True)
        write(i, span, inverse * (upstream - inner - scaled * cross))


def layer_kernel(
    tok,
    gain_one,
    shift_one,
    gain_two,
    shift_two,
    bias,
    wq_own,
    wo_own,
    wg_own,
    wu_own,
    wd_own,
    gout_own,
    cosine,
    sine,
    q_o,
    k_o,
    kt_o,
    v_o,
    att_o,
    lse_o,
    n1_o,
    gains_o,
    wq_o,
    wo_o,
    dm_o,
    datt_o,
    dmid_o,
    top_o,
    terms_o,
    gate_o,
    up_o,
    down_o,
    rows,
    gout,
    wq,
    wo,
    wg,
    wu,
    wd,
    q,
    k,
    kt,
    v,
    vt,
    ot,
    att,
    hidden,
    dgate,
    dup,
    mid,
    low,
    packet,
    packets,
    tiles,
    total,
    *rest,
):
    net = Net()
    chunk, width = tok.shape
    length = chunk * net.n_s
    depth = wq_own.shape[1]
    columns = wq_own.shape[2]
    heads = columns // HEAD
    pair = 2 * chunk
    buffers, rest = rest[:4], rest[4:]
    folds = []
    for _ in range(3):
        folds.append(Fold(net, tiles, total, *buffers, *rest[:4]))
        rest = rest[4:]
    att_fold, normed_fold, top_fold = folds
    line_sems = [rest[at : at + 3] for at in (0, 3, 6, 9)]
    rest = rest[12:]
    spread_sems, rest = rest[:5], rest[5:]
    gate_sum, up_sum, down_sum = [GridSum(net, *rest[at : at + 3]) for at in (0, 3, 6)]
    sums = (down_sum, gate_sum, up_sum)
    pk_sems, copy_sems, n1_sems, free_sem = rest[9:]
    copies = Copies(copy_sems)
    n1 = att_fold.mate_out

    packet[...] = jnp.zeros(packet.shape, F32)
    own = gain_one.shape[1]
    for at, part in enumerate((gain_one, shift_one, gain_two, shift_two)):
        packet[at : at + 1, 0:own] = part[...].astype(F32)
    packet[4:7, 0:own] = bias[...].astype(F32)
    def wq_part(f, half):
        if half is None:
            return wq.at[:, aligned(f * depth, depth), :]
        return wq.at[:, aligned(f * depth + half * (depth // 2), depth // 2), :]

    spread_q = Spread(net, wq_own, wq_part, spread_sems[0])
    spread_o, spread_g, spread_u, spread_d = [
        Spread(net, own, columns_of(full, depth), sems)
        for own, full, sems in zip((wo_own, wg_own, wu_own, wd_own), (wo, wg, wu, wd), spread_sems[1:])
    ]
    pk = Packets(net, packet, packets, pk_sems)
    line = Line(net, tok, rows_of(rows, chunk), *line_sems[0])
    gout_line = Line(net, gout_own, rows_of(gout, chunk), *line_sems[1])
    n2_line = Line(net, low, rows_of(rows, chunk), *line_sems[2])
    dm_line = Line(net, low, rows_of(rows, chunk), *line_sems[3])

    for ready in (line, spread_q, spread_o, spread_g, spread_u, spread_d, gout_line):
        ready.prepare()
    net.barrier()

    def pairs(which, hop):
        net.sides(hop, lambda other, side: which.pair(other))

    def blocks(hop, act):
        def once(other, side):
            @pl.when((hop > 0) | (side == 0))
            def _():
                act(other, side)

        net.sides(hop, once)

    pk.start()
    line.start()
    spread_q.start()
    pk.middle()
    pk.finish()
    pk.unpack(gains_o, width // (net.n_f * net.n_s))

    def project_block(other, side):
        span = aligned(other * pair, pair)
        gain, shift = gains_o[0:1, :], gains_o[1:2, :]

        for part in range(2):

            @pl.loop(0, chunk // 32, unroll=2)
            def _(i):
                at = aligned((2 * other + part) * chunk + i * 32, 32)
                scaled, _ = normalize(rows[at, :].astype(F32))
                n1[part, aligned(i * 32, 32), :] = (scaled * gain + shift).astype(BF)

        keeps = [
            pltpu.make_async_copy(
                n1.at[part], n1_o.at[aligned((2 * other + part) * chunk, chunk)], n1_sems.at[part]
            )
            for part in range(2)
        ]
        for copy in keeps:
            copy.start()
        left = n1[0:2].reshape(pair, width)
        cols = aligned(net.s * columns, columns)
        tables = cosine[span, :], sine[span, :]
        for kind in range(3):
            value = dot(left, wq[kind]) + gains_o[4 + kind : 5 + kind, cols]
            if kind == 0:
                q[span, :] = rotary(value, *tables).astype(BF)
            elif kind == 1:
                value = rotary(value, *tables)
                k[span, :] = value.astype(BF)
                kt[...] = value.T.astype(BF)
            else:
                v[...] = value.astype(BF)
                vt[:, span] = value.T.astype(BF)
        for copy in (
            pltpu.make_async_copy(kt, kt_o.at[:, span], n1_sems.at[2]),
            pltpu.make_async_copy(v, v_o.at[span], n1_sems.at[3]),
        ):
            copy.start()
            keeps.append(copy)
        for copy in keeps:
            copy.wait()

    line.here()
    for hop in range(1, net.n_l - 1):
        line.step(hop)
        if hop == 1:
            spread_q.relay()
        pairs(line, hop)
    spread_o.start()
    spread_q.finish()
    spread_g.start()
    pl.loop(0, net.n_l - 1)(lambda hop: blocks(hop, project_block))
    spread_o.relay()
    spread_u.start()
    line.step(net.n_l - 1)
    gout_line.start()
    pairs(line, net.n_l - 1)
    blocks(net.n_l - 1, project_block)
    q_copy = copies.start(q, q_o)
    for pair_of in ((wq, wq_o), (k, k_o)):
        copies.start(*pair_of)
    spread_o.finish()
    line.finish()

    def attend(i):
        lo, hi = i * pair, (i + 1) * pair

        @pl.loop(0, heads)
        def _(head):
            lane = lax.broadcasted_iota(jnp.int32, (1, columns), 1)
            here = jnp.where(lane // HEAD == head, HEAD**-0.5, 0.0).astype(BF)
            visible = lax.broadcasted_iota(jnp.int32, (pair, pair), 0) <= lax.broadcasted_iota(
                jnp.int32, (pair, pair), 1
            )
            head_rows = aligned(head * HEAD, HEAD)
            query = q[lo:hi, :] * here
            near = jnp.where(visible, dot_nt(k[lo:hi, :], query), NEG_LARGE)
            highest = jnp.max(near, 0, keepdims=True)
            if i:
                far = dot_nt(k[0:lo, :], query)
                highest = jnp.maximum(highest, jnp.max(far, 0, keepdims=True))
            near = jnp.exp(near - highest)
            sum_of = jnp.sum(near, 0, keepdims=True)
            out = dot(vt[head_rows, lo:hi], near.astype(BF))
            if i:
                far = jnp.exp(far - highest)
                sum_of = sum_of + jnp.sum(far, 0, keepdims=True)
                out = out + dot(vt[head_rows, 0:lo], far.astype(BF))
            ot[head_rows, :] = out / sum_of
            lse_o[pl.ds(head, 1), lo:hi] = highest + jnp.log(sum_of)

        att[lo:hi, :] = ot[...].T.astype(BF)

    def produce_attended(place, write):
        for i in range(net.n_l):
            pl.when(place == i)(functools.partial(attend, i))
        left = att[aligned(place * pair, pair), :]

        @pl.loop(0, width // TILE)
        def _(j):
            cols = aligned(j * TILE, TILE)
            write(cols, dot(left, wo[:, cols]))

    def relays():
        gout_line.step(1)
        spread_d.start()

    att_fold.begin(produce_attended, relays)
    copies.start(att, att_o)
    copies.start(wo, wo_o)
    if net.n_l > 2:
        gout_line.step(2)
    att_fold.open_total()
    spread_g.relay()
    for at in range(1, net.n_l):
        if 2 < at + 1 < net.n_l:
            gout_line.step(at + 1)
        att_fold.wave(at)
        if at == 1:
            spread_u.relay()
        if at == min(2, net.n_l - 1):
            spread_d.relay()
    gain_two, shift_two = gains_o[2:3, :], gains_o[3:4, :]

    @pl.loop(0, chunk // 32, unroll=2)
    def _(i):
        span = aligned(i * 32, 32)
        value = rows[aligned(net.s * chunk + i * 32, 32), :].astype(F32) + total[span, :]
        mid[span, :] = value
        scaled, _ = normalize(value)
        low[span, :] = (scaled * gain_two + shift_two).astype(BF)

    n2_line.prepare()
    n2_line.start()
    att_fold.finish()
    gout_line.here()
    pl.loop(1, net.n_l)(lambda hop: pairs(gout_line, hop))

    def forward_block(other):
        span = aligned(other * pair, pair)
        right = rows[span, :]
        half = hidden.shape[0] // 2

        @pl.loop(0, 2)
        def _(part):
            units = aligned(part * half, half, 16)
            gate = dot_nt(wg[units, :], right)
            up = dot_nt(wu[units, :], right)
            back = dot_nt(wd[units, :], gout[span, :])
            sigma = jax.nn.sigmoid(gate)
            active = gate * sigma
            hidden[units, span] = (active * up).astype(BF)
            dgate[units, span] = (back * up * (sigma * (1.0 + gate * (1.0 - sigma)))).astype(BF)
            dup[units, span] = (back * active).astype(BF)

    def produce_normed(place, write):
        span = aligned(place * pair, pair)
        left, right = dgate[:, span].T, dup[:, span].T

        @pl.loop(0, width // TILE)
        def _(j):
            cols = aligned(j * TILE, TILE)
            write(cols, dot(left, wg[:, cols]) + dot(right, wu[:, cols]))

    def begin_normed(other, side, hop):
        @pl.when(hop > 1)
        def _():
            normed_fold.mate_sent(side)

        normed_fold.begin_one(other, side + (2 - side) * (1 // (hop + 1)), produce_normed)

    def forward_blocks(hop):
        def act(other, side):
            forward_block(other)

            @pl.when(jnp.logical_not(normed_fold.fed(side)))
            def _():
                begin_normed(other, side, hop)
                normed_fold.leave(other, side, hop)

        net.sides(hop, act)

    def begin_fed(hop):
        def act(other, side):
            pl.when(normed_fold.fed(side))(lambda: begin_normed(other, side, hop))

        net.sides(hop, act)

    n2_line.here()
    for spread in (spread_g, spread_u, spread_d):
        spread.finish()
    forward_block(net.z)

    @pl.loop(1, net.n_l)
    def _(hop):
        n2_line.step(hop)
        pairs(n2_line, hop)
        pl.when(hop == 1)(lambda: normed_fold.begin_one(net.z, 2, produce_normed))
        forward_blocks(hop)
        pl.when(hop > 1)(lambda: begin_fed(hop - 1))

    begin_fed(net.n_l - 1)

    def weight_terms(task):
        at, kind = net.n_f - 1 - task // 3, task % 3
        cols = aligned(gate_sum.owner(at) * depth, depth)
        for way, (grid_sum, left, right) in enumerate(
            ((down_sum, hidden, gout), (gate_sum, dgate, rows), (up_sum, dup, rows))
        ):

            @pl.when(kind == way)
            def _():
                half = left.shape[0] // 2

                @pl.loop(0, 2)
                def _(part):
                    units = aligned(part * half, half, 16)
                    grid_sum.stage[at, units, :] = dot(left[units, :], right[:, cols]).astype(BF)

                grid_sum.first(at)

    tasks = 3 * net.n_f
    waves = max(net.n_l - 2, 1)
    each = -(-tasks // (2 * normed_fold.pieces * waves))
    for wave in range(net.n_l - waves, net.n_l):

        def between(turn, piece):
            slot = ((wave - net.n_l + waves) * 2 + turn) * normed_fold.pieces + piece

            @pl.loop(0, each)
            def _(i):
                pl.when(slot * each + i < tasks)(lambda: weight_terms(slot * each + i))

        normed_fold.passes_between(wave, True, between)
    normed_fold.finals()
    n2_line.finish()

    def beside(act):
        act(net.mate)
        for side in range(2):
            pl.when(n2_line.goes_on(side))(lambda: act(net.s + 2 - 4 * side))

    beside(lambda to: pl.semaphore_signal(free_sem, 1, device_id={"seq": to}, device_id_type=MESH))

    def write_middle(i, span, value):
        value = value + gout[aligned(net.s * chunk + i * 32, 32), :].astype(F32)
        dmid_o[span, :] = value
        low[span, :] = value.astype(BF)

    terms_o[...] = jnp.zeros(terms_o.shape, F32)
    norm_backward(chunk, mid, total, gain_two, terms_o, 2, write_middle)
    ends = (net.z + net.n_l - 1) // net.n_l + (2 * net.n_l - 2 - net.z) // net.n_l
    pl.semaphore_wait(free_sem, 1 + ends)
    dm_line.prepare()
    dm_line.start()
    normed_fold.finish()

    def produce_top(place, write):
        left = hidden[:, aligned(place * pair, pair)].T

        @pl.loop(0, width // TILE)
        def _(j):
            cols = aligned(j * TILE, TILE)
            write(cols, dot(left, wd[:, cols]))

    copies.wait(q_copy)
    datt = q

    def back_block(other, side):
        span = aligned(other * pair, pair)
        datt[span, :] = dot_nt(rows[span, :], wo[...]).astype(BF)

    dm_line.here()
    dm_line.step(1)
    top_fold.begin(produce_top)
    back_block(net.z, 0)
    top_fold.open_total()
    for at in range(1, net.n_l):
        if at + 1 < net.n_l:
            dm_line.step(at + 1)
        top_fold.wave(at)
        pairs(dm_line, at)
        net.sides(at, back_block)
    copies.start(datt, datt_o)
    copies.start(rows, dm_o)

    @pl.loop(0, chunk // 32)
    def _(i):
        span = aligned(i * 32, 32)
        top_fold.out[net.z, span, :] = (mid[span, :] + total[span, :]).astype(BF)

    copies.start(top_fold.out.at[net.z], top_o)
    top_fold.finish()
    gout_line.finish()
    dm_line.finish()
    hands = []
    for grid_sum, out in zip(sums, (down_o, gate_o, up_o)):
        grid_sum.sum_first()
        hands.extend(grid_sum.hand_on(out))
        for copy in grid_sum.hand_on(out):
            copy.start()
    for grid_sum in sums:
        grid_sum.finish_first()
    for copy in hands:
        copy.wait()
    copies.wait()


def layer_part(tokens, norms, wq, wo, wg, wu, wd, gout, tables):
    chunk, width = tokens.shape
    n_f, n_s = lax.axis_size("fsdp"), lax.axis_size("seq")
    length = chunk * n_s
    depth, columns = wq.shape[1:]
    units = wg.shape[0]
    shape = jax.ShapeDtypeStruct
    wide, head, turned, weight = (length, width), (length, columns), (units, length), (units, width)
    return pl.pallas_call(
        layer_kernel,
        name="layer",
        out_shape=[
            shape(head, BF),
            shape(head, BF),
            shape((columns, length), BF),
            shape(head, BF),
            shape(head, BF),
            shape((8, length), F32),
            shape(wide, BF),
            shape((SMALL, width), F32),
            shape((3, width, columns), BF),
            shape((columns, width), BF),
            shape(wide, BF),
            shape(head, BF),
            shape((chunk, width), F32),
            shape((chunk, width), BF),
            shape((SMALL, width), F32),
            *[shape((GridEnd.count(n_f), units // 2, depth), BF)] * 3,
        ],
        in_specs=[ANY, *[VMEM] * 5, *[ANY] * 6, VMEM, VMEM],
        out_specs=[*[ANY] * 5, VMEM, ANY, VMEM, *[ANY] * 4, VMEM, ANY, VMEM, *[ANY] * 3],
        scratch_shapes=[
            pltpu.VMEM(wide, BF),
            pltpu.VMEM(wide, BF),
            pltpu.VMEM((3, width, columns), BF),
            pltpu.VMEM((columns, width), BF),
            *[pltpu.VMEM(weight, BF)] * 3,
            pltpu.VMEM(head, BF),
            pltpu.VMEM(head, BF),
            pltpu.VMEM((columns, 2 * chunk), BF),
            pltpu.VMEM((2 * chunk, columns), BF),
            pltpu.VMEM((columns, length), BF),
            pltpu.VMEM((columns, 2 * chunk), F32),
            pltpu.VMEM(head, BF),
            *[pltpu.VMEM(turned, BF)] * 3,
            pltpu.VMEM((chunk, width), F32),
            pltpu.VMEM((chunk, width), BF),
            pltpu.VMEM((SMALL, 128), F32),
            pltpu.VMEM((n_s, n_f, SMALL, 128), F32),
            *Fold.shared(chunk, width),
            *Fold.buffers(n_s, chunk, width),
            *Fold.sems(n_s) * 3,
            *Line.sems(n_s) * 4,
            *[pltpu.SemaphoreType.DMA((Spread.count(n_f),))] * 5,
            *GridSum.scratch(n_f, units, depth) * 3,
            pltpu.SemaphoreType.DMA((Packets.count(n_f, n_s),)),
            pltpu.SemaphoreType.DMA((8,)),
            pltpu.SemaphoreType.DMA((4,)),
            pltpu.SemaphoreType.REGULAR,
        ],
        compiler_params=pltpu.CompilerParams(
            collective_id=1, has_side_effects=True, vmem_limit_bytes=VMEM_BYTES
        ),
        cost_estimate=pl.CostEstimate(
            flops=2 * length * width * (4 * columns + 9 * units),
            bytes_accessed=8 * length * width,
            transcendentals=length * (length * columns // HEAD + units),
        ),
    )(tokens, *norms, wq, wo, wg, wu, wd, gout, *tables)


def back_kernel(
    datt_in,
    q_in,
    k_in,
    kt_in,
    v_in,
    att_in,
    wq_in,
    n1_in,
    dm_in,
    down_in,
    gate_in,
    up_in,
    lse,
    tok,
    dmid,
    gains,
    terms_in,
    cosine,
    sine,
    gin_o,
    small_o,
    out_o,
    qkv_o,
    down_o,
    gate_o,
    up_o,
    datt,
    q,
    k,
    kt,
    v,
    att,
    wq,
    n1,
    dm,
    query,
    upstream,
    inners,
    dk,
    dv,
    dqt,
    dproj,
    terms,
    tiles,
    total,
    *rest,
):
    net = Net()
    chunk, width = tok.shape
    length, columns = q_in.shape
    heads = columns // HEAD
    pair = 2 * chunk
    depth = width // net.n_f
    block = 256
    buffers, rest = rest[:4], rest[4:]
    fold_sems, rest = rest[:4], rest[4:]
    packet_scratch, rest = rest[:5], rest[5:]
    out_sum, qkv_sum = GridSum(net, *rest[:3]), GridSum(net, *rest[3:6])
    ends = [GridEnd(net, *rest[at : at + 3]) for at in (6, 9, 12)]
    copy_sems, column_sems = rest[15:]

    copies = Copies(copy_sems)
    loads = [
        copies.start(src, dst)
        for src, dst in (
            (datt_in, datt),
            (q_in, q),
            (k_in, k),
            (kt_in, kt),
            (v_in, v),
            (att_in, att),
            (wq_in, wq),
            (down_in, ends[0].sums),
            (gate_in, ends[1].sums),
            (up_in, ends[2].sums),
        )
    ]
    def load(at, way):
        src, dst = ((n1_in, n1), (dm_in, dm))[way]
        cols = aligned(qkv_sum.owner(at) * depth, depth)
        return pltpu.make_async_copy(src.at[:, cols], dst.at[at % 2], column_sems.at[way, at % 2])

    for at in range(net.n_f - 1, max(net.n_f - 3, -1), -1):
        for way in range(2):
            load(at, way).start()

    @pl.loop(0, length // block)
    def _(i):
        span = aligned(i * block, block)
        dk[span, :] = jnp.zeros((block, columns), F32)
        dv[span, :] = jnp.zeros((block, columns), F32)

    net.barrier()
    copies.wait(*loads[:6])

    def start_ends():
        for load_of in loads[7:]:
            load_of.wait()
        for end in ends:
            end.start()


    of_head = (
        lax.broadcasted_iota(jnp.int32, (8, columns), 1) // HEAD
        == lax.broadcasted_iota(jnp.int32, (8, columns), 0)
    ).astype(F32)

    @pl.loop(0, length // block)
    def _(i):
        span = aligned(i * block, block)
        product = datt[span, :].astype(F32) * att[span, :].astype(F32)
        inners[:, span] = lax.dot_general(
            of_head,
            product,
            (((1,), (1,)), ((), ())),
            precision=lax.Precision.HIGHEST,
            preferred_element_type=F32,
        )

    @pl.loop(0, heads)
    def _(head):
        lane = lax.broadcasted_iota(jnp.int32, (1, columns), 1)
        here = jnp.where(lane // HEAD == head, 1.0, 0.0).astype(BF)
        scale = HEAD**-0.5
        visible = lax.broadcasted_iota(jnp.int32, (block, block), 0) <= lax.broadcasted_iota(
            jnp.int32, (block, block), 1
        )
        head_rows = aligned(head * HEAD, HEAD)

        @pl.loop(0, length // block)
        def _(i):
            span = aligned(i * block, block)
            query[span, :] = q[span, :] * (here * scale)
            upstream[span, :] = datt[span, :] * here

        pl.when(head == min(1, heads - 1))(start_ends)

        for j in range(length // block):
            at, end = j * block, (j + 1) * block
            keys, values, turned = k[at:end, :], v[at:end, :], kt[head_rows, at:end]

            def part(lo, hi, near):
                probs = jnp.exp(dot_nt(keys, query[lo:hi, :]) - lse[pl.ds(head, 1), lo:hi])
                if near:
                    probs = jnp.where(visible, probs, 0.0)
                grads = dot_nt(values, upstream[lo:hi, :])
                scores = (probs * (grads - inners[pl.ds(head, 1), lo:hi])).astype(BF)
                out = dot(turned, scores)
                dqt[head_rows, lo:hi] = dqt[head_rows, lo:hi] + out if j else out
                return dot(probs.astype(BF), upstream[lo:hi, :]), dot(scores, query[lo:hi, :])

            value_grads, key_grads = part(at, end, True)
            if end < length:
                more_values, more_keys = part(end, length, False)
                value_grads, key_grads = value_grads + more_values, key_grads + more_keys
            dv[at:end, :] = dv[at:end, :] + value_grads
            dk[at:end, :] = dk[at:end, :] + key_grads

    terms[...] = terms_in[...]
    bias_cols = aligned(net.s * columns, columns)

    @pl.loop(0, length // block)
    def _(i):
        span = aligned(i * block, block)
        tables = cosine[span, :], -sine[span, :]
        parts = [
            rotary((dqt[:, span].T * HEAD**-0.5).astype(BF).astype(F32), *tables).astype(BF),
            rotary(dk[span, :].astype(BF).astype(F32), *tables).astype(BF),
            dv[span, :].astype(BF),
        ]
        for kind in range(3):
            dproj[kind, span, :] = parts[kind]
            row = slice(4 + kind, 5 + kind)
            terms[row, bias_cols] = terms[row, bias_cols] + jnp.sum(parts[kind].astype(F32), 0, keepdims=True)

    def weight_terms(task):
        at = net.n_f - 1 - task // 2

        def loaded(way):
            load(at, way).wait()

        def next_load(way):
            pl.when(at >= 2)(lambda: load(at - 2, way).start())

        @pl.when(task % 2 == 0)
        def _():
            loaded(0)
            left = n1[at % 2].T
            for kind in range(3):
                qkv_sum.stage[at, kind * depth : (kind + 1) * depth, :] = dot(left, dproj[kind]).astype(BF)
            next_load(0)
            qkv_sum.first(at)

        @pl.when(task % 2 == 1)
        def _():
            loaded(1)
            out_sum.stage[at] = dot_tn(att[...], dm[at % 2]).astype(BF)
            next_load(1)
            out_sum.first(at)

    def produce(place, write):
        span = aligned(place * pair, pair)

        @pl.loop(0, width // TILE)
        def _(j):
            cols = aligned(j * TILE, TILE)
            value = dot_nt(dproj[0, span, :], wq[0, cols, :])
            for kind in range(1, 3):
                value = value + dot_nt(dproj[kind, span, :], wq[kind, cols, :])
            write(cols, value)

    fold = Fold(net, tiles, total, *buffers, *fold_sems)
    copies.wait(loads[6])
    tasks = 2 * net.n_f
    ahead = 2 * (net.n_l - 1)

    def meanwhile(task):
        pl.when(task < tasks)(lambda: weight_terms(task))

    fold.begin(produce, meanwhile=meanwhile)
    fold.open_total()
    waves = max(net.n_l - 2, 1)
    each = -(-max(tasks - ahead, 0) // (2 * fold.pieces * waves))

    def between(slot):
        @pl.loop(0, each)
        def _(i):
            task = ahead + slot * each + i
            pl.when(task < tasks)(lambda: weight_terms(task))

    for at in range(1, waves + 1):
        fold.wave(at, between=between)
    for at in range(waves + 1, net.n_l):
        fold.wave(at)

    def write_input(i, span, value):
        gin_o[span, :] = value + dmid[span, :]

    norm_backward(chunk, tok, total, gains[0:1, :], terms, 0, write_input)
    packet_sum = PacketSum(net, *packet_scratch)
    packet_sum.start(terms, width // (net.n_f * net.n_s))
    for grid_sum in (qkv_sum, out_sum):
        grid_sum.second()
    packet_sum.middle()
    for end, out in zip(ends, (down_o, gate_o, up_o)):
        end.last(out)
    packet_sum.finish(small_o)
    fold.finish()
    for grid_sum, out in ((qkv_sum, qkv_o), (out_sum, out_o)):
        grid_sum.last(out)
        grid_sum.finish()


def back_part(datt, q, k, kt, v, att, wq, n1, dm, down, gate, up, lse, tokens, dmid, gains, terms, tables):
    chunk, width = tokens.shape
    n_f, n_s = lax.axis_size("fsdp"), lax.axis_size("seq")
    length, columns = q.shape
    depth = width // n_f
    units = 2 * gate.shape[1]
    shape = jax.ShapeDtypeStruct
    return pl.pallas_call(
        back_kernel,
        name="back",
        out_shape=[
            shape((chunk, width), F32),
            shape((SMALL, 128), F32),
            shape((columns, depth), F32),
            shape((3 * depth, columns), F32),
            *[shape((units, depth), F32)] * 3,
        ],
        in_specs=[ANY] * 12 + [VMEM] * 7,
        out_specs=[VMEM] * 7,
        scratch_shapes=[
            pltpu.VMEM((length, columns), BF),
            pltpu.VMEM((length, columns), BF),
            pltpu.VMEM((length, columns), BF),
            pltpu.VMEM((columns, length), BF),
            pltpu.VMEM((length, columns), BF),
            pltpu.VMEM((length, columns), BF),
            pltpu.VMEM((3, width, columns), BF),
            pltpu.VMEM((2, length, depth), BF),
            pltpu.VMEM((2, length, depth), BF),
            pltpu.VMEM((length, columns), BF),
            pltpu.VMEM((length, columns), BF),
            pltpu.VMEM((8, length), F32),
            pltpu.VMEM((length, columns), F32),
            pltpu.VMEM((length, columns), F32),
            pltpu.VMEM((columns, length), F32),
            pltpu.VMEM((3, length, columns), BF),
            pltpu.VMEM((SMALL, width), F32),
            *Fold.shared(chunk, width),
            *Fold.buffers(n_s, chunk, width),
            *Fold.sems(n_s, 8),
            *PacketSum.scratch(n_f, n_s),
            *GridSum.scratch(n_f, columns, depth),
            *GridSum.scratch(n_f, 3 * depth, columns),
            *GridEnd.scratch(n_f, units, depth) * 3,
            pltpu.SemaphoreType.DMA((10,)),
            pltpu.SemaphoreType.DMA((2, 2)),
        ],
        compiler_params=pltpu.CompilerParams(
            collective_id=3, has_side_effects=True, vmem_limit_bytes=VMEM_BYTES
        ),
        cost_estimate=pl.CostEstimate(
            flops=2 * length * columns * (8 * width + 5 * length),
            bytes_accessed=4 * length * width,
            transcendentals=length * length * columns // HEAD,
        ),
    )(datt, q, k, kt, v, att, wq, n1, dm, down, gate, up, lse, tokens, dmid, gains, terms, *tables)


def outputs_kernel(small, *refs):
    sources, targets, parts = refs[:7], refs[7:14], refs[14:]
    own = parts[0].shape[1]
    for src, dst in zip(sources, targets):
        dst[...] = src[...]

    @pl.when(pl.program_id(0) == 0)
    def _():
        for at in range(4):
            parts[at][...] = small[at : at + 1, 0:own]
        parts[4][...] = small[4:7, 0:own]


def outputs_part(small, own, *arrays):
    shape = jax.ShapeDtypeStruct
    steps = 4
    strips = [pl.BlockSpec((v.shape[0] // steps, v.shape[1]), lambda i: (i, 0)) for v in arrays]
    whole = lambda *sizes: pl.BlockSpec(sizes, lambda i: (0, 0))
    return pl.pallas_call(
        outputs_kernel,
        name="outputs",
        grid=(steps,),
        out_shape=[shape(v.shape, v.dtype) for v in arrays]
        + [shape((1, own), F32)] * 4
        + [shape((3, own), F32)],
        in_specs=[whole(*small.shape), *strips],
        out_specs=[*strips, *[whole(1, own)] * 4, whole(3, own)],
        compiler_params=pltpu.CompilerParams(vmem_limit_bytes=VMEM_BYTES),
    )(small, *arrays)


def per_device(
    tokens,
    gain_one,
    shift_one,
    w_qkv,
    b_qkv,
    w_out,
    gain_two,
    shift_two,
    w_gate,
    w_up,
    w_down,
    grad_output,
):
    length = tokens.shape[1] * lax.axis_size("seq")
    width = gain_one.shape[0]
    norms = [v[None] for v in (gain_one, shift_one, gain_two, shift_two)] + [b_qkv]
    tables = rotary_tables(length)
    q, k, kt, v, att, lse, n1, gains, wq, _, dm, datt, dmid, top, terms, gate, up, down = layer_part(
        tokens[0], norms, w_qkv.transpose(1, 0, 2), w_out, w_gate.T, w_up.T, w_down, grad_output[0], tables
    )
    grad_input, small, out, qkv, down, gate, up = back_part(
        datt, q, k, kt, v, att, wq, n1, dm, down, gate, up, lse, tokens[0], dmid, gains, terms, tables
    )

    top, grad_input, qkv, out, gate, up, down, one, shift, two, shift_to, bias = outputs_part(
        small, width, top, grad_input, qkv, out, gate, up, down
    )
    return (
        top[None],
        grad_input[None],
        one[0],
        shift[0],
        qkv.reshape(3, -1, qkv.shape[1]).transpose(1, 0, 2),
        bias,
        out,
        two[0],
        shift_to[0],
        gate.T,
        up.T,
        down,
    )


def solution(mesh):
    whole = P(("fsdp", "seq"))
    rows = P("fsdp", "seq", None)
    inner = P("seq", "fsdp")
    outer = P("fsdp", "seq")
    heads = P("fsdp", None, "seq")
    bias = P(None, ("fsdp", "seq"))
    return jax.shard_map(
        per_device,
        mesh=mesh,
        in_specs=(rows, whole, whole, heads, bias, inner, whole, whole, outer, outer, inner, rows),
        out_specs=(rows, rows, whole, whole, heads, bias, inner, whole, whole, outer, outer, inner),
        check_vma=False,
    )
```

```python
import functools

import jax
import jax.numpy as jnp
import numpy as np
from jax import lax
from jax.experimental import pallas as pl
from jax.experimental.pallas import tpu as pltpu
from jax.sharding import PartitionSpec as P

HEAD = 64
ROT = 16
EPSILON = 1e-05
NEG_LARGE = -1e30
MESH = pl.DeviceIdType.MESH
ANY = pl.BlockSpec(memory_space=pl.ANY)
VMEM = pl.BlockSpec(memory_space=pltpu.VMEM)
BF = jnp.bfloat16
F32 = jnp.float32
VMEM_BYTES = 60 * 2**20
TILE = 512
SMALL = 8


def put(src, dst, send, recv, **device):
    return pltpu.make_async_remote_copy(
        src_ref=src, dst_ref=dst, send_sem=send, recv_sem=recv, device_id=device, device_id_type=MESH
    )


def dot(left, right):
    return jnp.dot(left, right, preferred_element_type=F32)


def dot_nt(left, right):
    return lax.dot_general(left, right, (((1,), (1,)), ((), ())), preferred_element_type=F32)


def dot_tn(left, right):
    return lax.dot_general(left, right, (((0,), (0,)), ((), ())), preferred_element_type=F32)


def turned(values):
    size = values.shape[1]
    same = lax.broadcasted_iota(jnp.int32, (size, size), 0) == lax.broadcasted_iota(
        jnp.int32, (size, size), 1
    )
    return dot_nt(jnp.where(same, 1.0, 0.0).astype(BF), values).astype(BF)


def aligned(start, size, unit=None):
    return pl.ds(pl.multiple_of(start, unit or size), size)


class Net:
    def __init__(self):
        self.n_f, self.n_s = lax.axis_size("fsdp"), lax.axis_size("seq")
        self.tall = 2 if self.n_f % 2 == 0 else 1
        self.wide = self.n_f // self.tall
        self.n_l = self.n_s // 2
        self.f, self.s = lax.axis_index("fsdp"), lax.axis_index("seq")
        self.a, self.b = self.f // self.wide, self.f % self.wide
        self.z, self.c = self.s // 2, self.s % 2
        self.mate = self.s + 1 - 2 * self.c

    def barrier(self):
        sem = pltpu.get_barrier_semaphore()
        for k in range(1, self.n_f):
            pl.semaphore_signal(
                sem, inc=1, device_id={"fsdp": (self.f + k) % self.n_f}, device_id_type=MESH
            )
        for k in range(1, self.n_s):
            pl.semaphore_signal(
                sem, inc=1, device_id={"seq": (self.s + k) % self.n_s}, device_id_type=MESH
            )
        pl.semaphore_wait(sem, self.n_f + self.n_s - 2)

    def sides(self, hop, act):
        @pl.loop(0, 2)
        def _(side):
            other = self.z + (2 * side - 1) * hop

            @pl.when((other >= 0) & (other < self.n_l))
            def _():
                act(other, side)


class Spread:
    def __init__(self, net, src, part, sems):
        self.net, self.src, self.part, self.sems = net, src, part, sems
        self.rows = [j for j in range(1, net.wide)]
        self.cols = [i for i in range(1, net.tall)]

    @staticmethod
    def count(n_f):
        tall = 2 if n_f % 2 == 0 else 1
        wide = n_f // tall
        return 1 + 2 * (wide - 1) + 2 * (tall - 1) + 4 * (wide - 1) * (tall - 1)

    def at(self, kind, i, j):
        w, t = len(self.rows), len(self.cols)
        base = {
            "own": 0,
            "row": 1,
            "col": 1 + 2 * w,
            "half0": 1 + 2 * w + 2 * t,
            "half1": 1 + 2 * w + 2 * t + 2 * w * t,
        }[kind]
        if kind == "own":
            return self.sems.at[0]
        k = j - 1 if kind == "row" else i - 1 if kind == "col" else (i - 1) * w + j - 1
        return self.sems.at[base + 2 * k], self.sems.at[base + 2 * k + 1]

    def rank(self, i, j):
        net = self.net
        return ((net.a + i) % net.tall) * net.wide + (net.b + j) % net.wide

    def back(self, i, j):
        net = self.net
        return ((net.a - i + net.tall) % net.tall) * net.wide + (net.b - j + net.wide) % net.wide

    def own(self):
        return pltpu.make_async_copy(self.src, self.part(self.net.f, None), self.at("own", 0, 0))

    def first(self, i, j):
        send, recv = self.at("row" if i == 0 else "col", i, j)
        place = self.part(self.net.f, None)
        return put(place, place, send, recv, fsdp=self.rank(i, j))

    def came(self, i, j):
        send, recv = self.at("row" if i == 0 else "col", i, j)
        place = self.part(self.back(i, j), None)
        return put(place, place, send, recv, fsdp=self.rank(i, j))

    def second(self, half, i, j, came=False):
        send, recv = self.at("half0" if half == 0 else "half1", i, j)
        origin = self.back(i, j) if came else self.back(0, j) if half == 0 else self.back(i, 0)
        place = self.part(origin, half)
        return put(place, place, send, recv, fsdp=self.rank(i, 0) if half == 0 else self.rank(0, j))

    def prepare(self):
        self.own().start()

    def start(self):
        self.own().wait()
        for i in self.cols:
            self.first(i, 0).start()
        for j in self.rows:
            self.first(0, j).start()

    def relay(self):
        for j in self.rows:
            self.came(0, j).wait_recv()
            for i in self.cols:
                self.second(0, i, j).start()
        for i in self.cols:
            self.came(i, 0).wait_recv()
            for j in self.rows:
                self.second(1, i, j).start()

    def finish(self):
        for j in self.rows:
            self.first(0, j).wait_send()
        for i in self.cols:
            self.first(i, 0).wait_send()
        for i in self.cols:
            for j in self.rows:
                for half in range(2):
                    self.second(half, i, j, came=True).wait_recv()
                    self.second(half, i, j).wait_send()


class Line:
    def __init__(self, net, src, part, recv, send, local):
        self.net, self.src, self.part, self.recv, self.send, self.local = net, src, part, recv, send, local
        self.pieces = recv.shape[1]
        self.rows = src.shape[0] // self.pieces

    @staticmethod
    def sems(n_s, pieces=2):
        return [
            pltpu.SemaphoreType.DMA((n_s, pieces)),
            pltpu.SemaphoreType.DMA((4, n_s // 2, pieces)),
            pltpu.SemaphoreType.DMA((1,)),
        ]

    def cut(self, ref, piece):
        return ref.at[aligned(piece * self.rows, self.rows)]

    def own(self):
        return pltpu.make_async_copy(self.src, self.part(self.net.s), self.local.at[0])

    def on_line(self, src, chunk, side, hop, piece):
        return put(
            self.cut(src, piece),
            self.cut(self.part(chunk), piece),
            self.send.at[side, hop, piece],
            self.recv.at[chunk, piece],
            seq=self.net.s + 2 - 4 * side,
        )

    def to_mate(self, src, chunk, side, hop, piece):
        return put(
            self.cut(src, piece),
            self.cut(self.part(chunk), piece),
            self.send.at[2 + side, hop, piece],
            self.recv.at[chunk, piece],
            seq=self.net.mate,
        )

    def goes_on(self, side):
        after = self.net.z + 1 - 2 * side
        return (after >= 0) & (after < self.net.n_l)

    def each_piece(self, act):
        pl.loop(0, self.pieces)(act)

    def prepare(self):
        self.own().start()

    def start(self):
        net = self.net
        self.own().wait()
        place = self.part(net.s)

        @self.each_piece
        def _(piece):
            for side in range(2):

                @pl.when(self.goes_on(side))
                def _():
                    self.on_line(place, net.s, side, 0, piece).start()

            self.to_mate(place, net.s, 0, 0, piece).start()

    def came(self, chunk, piece):
        place = self.cut(self.part(chunk), piece)
        put(place, place, self.send.at[0, 0, 0], self.recv.at[chunk, piece], seq=self.net.mate).wait_recv()

    def step(self, hop):
        net = self.net

        @self.each_piece
        def _(piece):
            def act(other, side):
                chunk = 2 * other + net.c
                self.came(chunk, piece)

                @pl.when(self.goes_on(side))
                def _():
                    self.on_line(self.part(chunk), chunk, side, hop, piece).start()

                self.to_mate(self.part(chunk), chunk, side, hop, piece).start()

            net.sides(hop, act)

    def pair(self, other):
        @self.each_piece
        def _(piece):
            self.came(2 * other + 1 - self.net.c, piece)

    def here(self):
        self.pair(self.net.z)

    def finish(self):
        net = self.net
        place = self.part(net.s)

        @self.each_piece
        def _(piece):
            for side in range(2):

                @pl.when(self.goes_on(side))
                def _():
                    self.on_line(place, net.s, side, 0, piece).wait_send()

            self.to_mate(place, net.s, 0, 0, piece).wait_send()

            @pl.loop(1, net.n_l)
            def _(hop):
                def act(other, side):
                    chunk = 2 * other + net.c

                    @pl.when(self.goes_on(side))
                    def _():
                        self.on_line(self.part(chunk), chunk, side, hop, piece).wait_send()

                    self.to_mate(self.part(chunk), chunk, side, hop, piece).wait_send()

                net.sides(hop, act)


class Packets:
    def __init__(self, net, src, buf, sems):
        self.net, self.src, self.buf, self.sems = net, src, buf, sems

    @staticmethod
    def count(n_f, n_s):
        return 1 + 2 * (n_f - 1) + 2 * (n_s - 1)

    def own(self):
        net = self.net
        return pltpu.make_async_copy(self.src, self.buf.at[net.s, net.f], self.sems.at[0])

    def one(self, k, came=False):
        net = self.net
        f = (net.f - k + net.n_f) % net.n_f if came else net.f
        place = self.buf.at[net.s, f]
        return put(
            place if came else self.src,
            place,
            self.sems.at[2 * k - 1],
            self.sems.at[2 * k],
            fsdp=(net.f + k) % net.n_f,
        )

    def two(self, k, came=False):
        net = self.net
        place = self.buf.at[(net.s - k + net.n_s) % net.n_s if came else net.s]
        at = 2 * (net.n_f - 1) + 2 * k - 1
        return put(place, place, self.sems.at[at], self.sems.at[at + 1], seq=(net.s + k) % net.n_s)

    def start(self):
        self.own().start()
        for k in range(1, self.net.n_f):
            self.one(k).start()

    def middle(self):
        self.own().wait()
        for k in range(1, self.net.n_f):
            self.one(k, came=True).wait_recv()
            self.one(k).wait_send()
        for k in range(1, self.net.n_s):
            self.two(k).start()

    def finish(self):
        for k in range(1, self.net.n_s):
            self.two(k, came=True).wait_recv()
            self.two(k).wait_send()

    def unpack(self, out, width):
        net = self.net
        per = 128 // width
        for tile in range(net.n_f * net.n_s // per):
            total = None
            for j in range(per):
                f, s = divmod(tile * per + j, net.n_s)
                piece = self.buf[s, f]
                if j:
                    piece = pltpu.roll(piece, j * width, axis=1)
                total = piece if total is None else total + piece
            out[:, tile * 128 : (tile + 1) * 128] = total


def rotary(values, cosine, sine):
    columns = values.shape[1]
    half = ROT // 2
    times = columns // 128

    def wide(table):
        return table if times == 1 else jnp.concatenate([table] * times, axis=1)

    lane = lax.broadcasted_iota(jnp.int32, values.shape, 1)
    other = jnp.where(
        lane % HEAD < half, pltpu.roll(values, columns - half, axis=1), pltpu.roll(values, half, axis=1)
    )
    return values * wide(cosine) + other * wide(sine)


def rotary_tables(length):
    half = ROT // 2
    freqs = np.float32(10000.0) ** (-np.arange(half, dtype=np.float32) * np.float32(2.0 / ROT))
    angles = np.arange(length, dtype=np.float32)[:, None] * freqs[None, :].astype(np.float32)
    cosine, sine = np.cos(angles), np.sin(angles)
    rest = np.zeros((length, HEAD - ROT), np.float32)
    keep = np.concatenate([cosine, cosine, rest + 1], 1)
    swap = np.concatenate([-sine, sine, rest], 1)
    return [np.tile(t, (1, 128 // HEAD)).astype(np.float32) for t in (keep, swap)]


def normalize(values):
    center = values - jnp.mean(values, -1, keepdims=True)
    inverse = lax.rsqrt(jnp.mean(center * center, -1, keepdims=True) + EPSILON)
    return center * inverse, inverse


class Copies:
    def __init__(self, sems):
        self.sems, self.all, self.open = sems, [], []

    def start(self, src, dst):
        copy = pltpu.make_async_copy(src, dst, self.sems.at[len(self.all)])
        copy.start()
        self.all.append(copy)
        self.open.append(copy)
        return copy

    def wait(self, *copies):
        for copy in copies or list(self.open):
            copy.wait()
            self.open = [c for c in self.open if c is not copy]


def columns_of(ref, depth):
    half_rows = ref.shape[0] // 2

    def part(f, half):
        span = aligned(f * depth, depth)
        if half is None:
            return ref.at[:, span]
        return ref.at[pl.ds(half * half_rows, half_rows), span]

    return part


def rows_of(ref, chunk):
    return lambda s: ref.at[aligned(s * chunk, chunk)]


class Fold:
    def __init__(self, net, tile, total, mate_in, coming, mate_out, out, mate_send, mate_recv, send, recv):
        self.net, self.tile, self.total = net, tile, total
        self.mate_in, self.coming, self.mate_out, self.out = mate_in, coming, mate_out, out
        self.mate_send, self.mate_recv, self.send, self.recv = mate_send, mate_recv, send, recv
        self.chunk = total.shape[0]
        self.pieces = recv.shape[1]
        self.rows = self.chunk // self.pieces

    @staticmethod
    def shared(chunk, width):
        return [pltpu.VMEM((2 * chunk, TILE), F32), pltpu.VMEM((chunk, width), F32)]

    @staticmethod
    def buffers(n_s, chunk, width):
        n_l = n_s // 2
        return [
            pltpu.VMEM((n_l, chunk, width), BF),
            pltpu.VMEM((n_l + 1, chunk, width), BF),
            pltpu.VMEM((3, chunk, width), BF),
            pltpu.VMEM((n_l, chunk, width), BF),
        ]

    @staticmethod
    def sems(n_s, pieces=4):
        n_l = n_s // 2
        return [
            pltpu.SemaphoreType.DMA((3, pieces)),
            pltpu.SemaphoreType.DMA((n_l, pieces)),
            pltpu.SemaphoreType.DMA((n_l, pieces)),
            pltpu.SemaphoreType.DMA((n_l + 1, pieces)),
        ]

    def place(self, other):
        return (other >= 0) & (other < self.net.n_l)

    def fed(self, side):
        return self.place(self.net.z + 1 - 2 * side)

    def span(self, piece):
        return aligned(piece * self.rows, self.rows)

    def each_piece(self, act):
        pl.loop(0, self.pieces)(act)

    def to_mate(self, target, slot, piece):
        span = self.span(piece)
        return put(
            self.mate_out.at[slot, span],
            self.mate_in.at[target, span],
            self.mate_send.at[slot, piece],
            self.mate_recv.at[target, piece],
            seq=self.net.mate,
        )

    def onward(self, target, side, hop, piece):
        span = self.span(piece)
        slot = target + (self.net.n_l - target) * (1 - side) * (1 // hop)
        return put(
            self.out.at[target, span],
            self.coming.at[slot, span],
            self.send.at[target, piece],
            self.recv.at[slot, piece],
            seq=self.net.s + 4 * side - 2,
        )

    def came(self, slot, piece):
        place = self.coming.at[slot, self.span(piece)]
        put(place, place, self.send.at[0, 0], self.recv.at[slot, piece], seq=self.net.mate).wait_recv()

    def mate_sent(self, slot):
        self.each_piece(lambda piece: self.to_mate(self.net.z, slot, piece).wait_send())

    def begin_one(self, target, slot, produce):
        mine = aligned(self.net.c * self.chunk, self.chunk)
        theirs = aligned((1 - self.net.c) * self.chunk, self.chunk)

        def write(cols, value):
            self.tile[...] = value
            self.out[target, :, cols] = self.tile[mine, :].astype(BF)
            self.mate_out[slot, :, cols] = self.tile[theirs, :].astype(BF)

        produce(target, write)
        self.each_piece(lambda piece: self.to_mate(target, slot, piece).start())

    def leave(self, target, side, hop):
        @pl.when((hop > 0) & jnp.logical_not(self.fed(side)))
        def _():
            self.each_piece(lambda piece: self.pass_piece(target, side, hop, piece, False))

    def begin(self, produce, between=None, meanwhile=None):
        net = self.net

        @pl.loop(0, net.n_l)
        def _(j):
            hop = net.n_l - 1 - j

            @pl.loop(0, 2)
            def _(side):
                target = net.z + (2 * side - 1) * hop
                here = self.place(target) & ((hop > 0) | (side == 0))

                @pl.when(here)
                def _():
                    @pl.when((hop > 0) & self.place(target + 2 * side - 1))
                    def _():
                        self.mate_sent(side)

                    self.begin_one(target, side + (2 - side) * (1 // (hop + 1)), produce)

                if meanwhile is not None:
                    pl.when(hop > 0)(lambda: meanwhile(2 * j + side))

                pl.when(here)(lambda: self.leave(target, side, hop))

            if between is not None:
                pl.when(j == 1)(between)

    def pass_piece(self, target, side, hop, piece, fed):
        self.to_mate(target, 0, piece).wait_recv()
        span = self.span(piece)
        value = self.out[target, span, :].astype(F32) + self.mate_in[target, span, :].astype(F32)
        if fed:
            self.came(target, piece)
            value = value + self.coming[target, span, :].astype(F32)
        self.out[target, span, :] = value.astype(BF)
        self.onward(target, side, hop, piece).start()

    def open_total(self):
        net = self.net

        @self.each_piece
        def _(piece):
            self.to_mate(net.z, 0, piece).wait_recv()
            span = self.span(piece)
            self.total[span, :] = self.out[net.z, span, :].astype(F32) + self.mate_in[net.z, span, :].astype(F32)

    def wave(self, at, near=False, between=None):
        net = self.net
        above = at if near else net.n_l - at

        @pl.loop(0, 2)
        def _(turn):
            side = (1 - (2 * net.z) // net.n_l + turn) % 2
            target = net.n_l - 1 - above + (2 * above - net.n_l + 1) * side
            hop = (target - net.z) * (2 * side - 1)

            @self.each_piece
            def _(piece):
                span = self.span(piece)

                @pl.when(self.fed(side) & (hop > 0))
                def _():
                    self.pass_piece(target, side, hop, piece, True)

                @pl.when(self.fed(side) & (hop == 0))
                def _():
                    slot = net.z + (net.n_l - net.z) * (1 - side)
                    self.came(slot, piece)
                    self.total[span, :] = self.total[span, :] + self.coming[slot, span, :].astype(F32)

                if between is not None:
                    between(((at - 1) * 2 + turn) * self.pieces + piece)

    def passes_between(self, wave, near, between):
        net = self.net
        above = wave if near else net.n_l - wave

        @pl.loop(0, 2)
        def _(turn):
            side = (1 - (2 * net.z) // net.n_l + turn) % 2
            target = net.n_l - 1 - above + (2 * above - net.n_l + 1) * side
            hop = (target - net.z) * (2 * side - 1)

            @self.each_piece
            def _(piece):
                @pl.when((hop > 0) & self.fed(side))
                def _():
                    self.pass_piece(target, side, hop, piece, True)

                between(turn, piece)

    def finals(self):
        net = self.net

        @self.each_piece
        def _(piece):
            self.to_mate(net.z, 0, piece).wait_recv()
            span = self.span(piece)
            self.total[span, :] = self.out[net.z, span, :].astype(F32) + self.mate_in[net.z, span, :].astype(F32)

        @pl.loop(0, 2)
        def _(turn):
            side = (1 - (2 * net.z) // net.n_l + turn) % 2

            @pl.when(self.fed(side))
            def _():
                slot = net.z + (net.n_l - net.z) * (1 - side)

                @self.each_piece
                def _(piece):
                    span = self.span(piece)
                    self.came(slot, piece)
                    self.total[span, :] = self.total[span, :] + self.coming[slot, span, :].astype(F32)

    def finish(self):
        net = self.net
        self.mate_sent(2)
        for side in range(2):
            pl.when(self.place(net.z + 2 * side - 1))(functools.partial(self.mate_sent, side))

        @pl.loop(1, net.n_l)
        def _(hop):
            net.sides(
                hop,
                lambda target, side: self.each_piece(
                    lambda piece: self.onward(target, side, hop, piece).wait_send()
                ),
            )


class GridSum:
    def __init__(self, net, stage, came, sems):
        self.net, self.stage, self.came, self.sems = net, stage, came, sems
        self.half = stage.shape[1] // 2
        self.rows = next(r for r in (176, 128, 96, 64, 32, 16) if self.half % r == 0)
        self.cols = range(1, net.tall)
        self.along = range(1, net.wide)
        self.bases = self.layout(net.n_f)

    @staticmethod
    def layout(n_f):
        tall = 2 if n_f % 2 == 0 else 1
        wide = n_f // tall
        sizes = [(wide - 1) * tall, (tall - 1) * wide, tall - 1, wide - 1]
        return [sum(sizes[:at]) for at in range(5)]

    @staticmethod
    def scratch(n_f, rows, columns):
        count = GridSum.layout(n_f)[4]
        return [
            pltpu.VMEM((n_f, rows, columns), BF),
            pltpu.VMEM((count, rows // 2, columns), BF),
            pltpu.SemaphoreType.DMA((2, count + GridEnd.count(n_f))),
        ]

    def slot(self, kind, i, j):
        base = self.bases[kind]
        return base + [(j - 1) * self.net.tall + i, (i - 1) * self.net.wide + j, i - 1, j - 1][kind]

    def rank(self, i, j):
        net = self.net
        return ((net.a + i) % net.tall) * net.wide + (net.b + j) % net.wide

    def owner(self, at):
        return self.rank(at // self.net.wide, at % self.net.wide)

    def copy(self, kind, i, j):
        half = kind % 2
        along = kind in (0, 3)
        slot = self.slot(kind, i, j)
        at = i * self.net.wide + j
        return put(
            self.stage.at[at, pl.ds(half * self.half, self.half)],
            self.came.at[slot],
            self.sems.at[0, slot],
            self.sems.at[1, slot],
            fsdp=self.rank(0, j) if along else self.rank(i, 0),
        )

    def first(self, at):
        i, j = at // self.net.wide, at % self.net.wide

        @pl.when(j > 0)
        def _():
            self.copy(0, i, j).start()

        @pl.when(i > 0)
        def _():
            self.copy(1, i, j).start()

    def gather(self, half, at, slots, write):
        @pl.loop(0, self.half // self.rows)
        def _(step):
            span = aligned(half * self.half + step * self.rows, self.rows, 16)
            value = self.stage[at, span, :].astype(F32)
            for slot in slots:
                value = value + self.came[slot, aligned(step * self.rows, self.rows, 16), :].astype(F32)
            write(span, value)

    def wait(self, *copies):
        for kind, i, j in copies:
            self.copy(kind, i, j).wait_recv()
        return [self.slot(*copy) for copy in copies]

    def second(self):
        def keep(at):
            def write(span, value):
                self.stage[at, span, :] = value.astype(BF)

            return write

        for i in self.cols:
            at = i * self.net.wide
            self.gather(0, at, self.wait(*[(0, i, j) for j in self.along]), keep(at))
            self.copy(2, i, 0).start()
        for j in self.along:
            self.gather(1, j, self.wait(*[(1, i, j) for i in self.cols]), keep(j))
            self.copy(3, 0, j).start()

    def sum_first(self):
        def keep(at):
            def write(span, value):
                self.stage[at, span, :] = value.astype(BF)

            return write

        for i in range(self.net.tall):
            at = i * self.net.wide
            self.gather(0, at, self.wait(*[(0, i, j) for j in self.along]), keep(at))
        for j in range(self.net.wide):
            self.gather(1, j, self.wait(*[(1, i, j) for i in self.cols]), keep(j))

    def hand_on(self, out):
        net = self.net
        shards = [(0, 0), (0, 1), *[(i * net.wide, 0) for i in self.cols], *[(j, 1) for j in self.along]]
        return [
            pltpu.make_async_copy(
                self.stage.at[at, pl.ds(half * self.half, self.half)], out.at[k], self.sems.at[0, self.bases[4] + k]
            )
            for k, (at, half) in enumerate(shards)
        ]

    def last(self, out):
        def write(span, value):
            out[span, :] = value

        self.gather(
            0, 0, self.wait(*[(0, 0, j) for j in self.along], *[(2, i, 0) for i in self.cols]), write
        )
        self.gather(
            1, 0, self.wait(*[(1, i, 0) for i in self.cols], *[(3, 0, j) for j in self.along]), write
        )

    def finish_first(self):
        for i in range(self.net.tall):
            for j in range(self.net.wide):
                if j:
                    self.copy(0, i, j).wait_send()
                if i:
                    self.copy(1, i, j).wait_send()

    def finish(self):
        self.finish_first()
        for i in self.cols:
            self.copy(2, i, 0).wait_send()
        for j in self.along:
            self.copy(3, 0, j).wait_send()


class GridEnd:
    def __init__(self, net, sums, came, sems):
        self.net, self.sums, self.came, self.sems = net, sums, came, sems

    @staticmethod
    def count(n_f):
        tall = 2 if n_f % 2 == 0 else 1
        return tall + n_f // tall

    @staticmethod
    def scratch(n_f, rows, columns):
        count = GridEnd.count(n_f)
        return [
            pltpu.VMEM((count, rows // 2, columns), BF),
            pltpu.VMEM((count - 2, rows // 2, columns), BF),
            pltpu.SemaphoreType.DMA((2, count - 2)),
        ]

    def copies(self):
        net = self.net
        f = [((net.a + i) % net.tall) * net.wide + net.b for i in range(1, net.tall)]
        f += [net.a * net.wide + (net.b + j) % net.wide for j in range(1, net.wide)]
        return [
            put(self.sums.at[2 + k], self.came.at[k], self.sems.at[0, k], self.sems.at[1, k], fsdp=to)
            for k, to in enumerate(f)
        ]

    def start(self):
        for copy in self.copies():
            copy.start()

    def last(self, out):
        for copy in self.copies():
            copy.wait()
        half = self.sums.shape[1]
        rows = next(r for r in (176, 128, 96, 64, 32, 16) if half % r == 0)
        down = range(self.net.tall - 1)
        along = range(self.net.tall - 1, self.net.tall + self.net.wide - 2)
        for at, slots in enumerate((down, along)):

            @pl.loop(0, half // rows)
            def _(step):
                span = aligned(step * rows, rows, 16)
                value = self.sums[at, span, :].astype(F32)
                for slot in slots:
                    value = value + self.came[slot, span, :].astype(F32)
                out[aligned(at * half + step * rows, rows, 16), :] = value


class PacketSum:
    def __init__(self, net, out, seq_in, total, fsdp_in, sems):
        self.net, self.out, self.seq_in, self.total, self.fsdp_in, self.sems = net, out, seq_in, total, fsdp_in, sems

    @staticmethod
    def scratch(n_f, n_s):
        return [
            pltpu.VMEM((n_s, n_f, SMALL, 128), F32),
            pltpu.VMEM((n_s, n_f, SMALL, 128), F32),
            pltpu.VMEM((n_f, SMALL, 128), F32),
            pltpu.VMEM((n_f, SMALL, 128), F32),
            pltpu.SemaphoreType.DMA((2 * (n_f + n_s),)),
        ]

    def one(self, k):
        to = (self.net.s + k) % self.net.n_s
        return put(self.out.at[to], self.seq_in.at[k], self.sems.at[2 * k], self.sems.at[2 * k + 1], seq=to)

    def two(self, k):
        to = (self.net.f + k) % self.net.n_f
        at = 2 * (self.net.n_s + k)
        return put(self.total.at[to], self.fsdp_in.at[k], self.sems.at[at], self.sems.at[at + 1], fsdp=to)

    def start(self, terms, width):
        net = self.net
        per = 128 // width
        for tile in range(net.n_f * net.n_s // per):
            value = terms[:, tile * 128 : (tile + 1) * 128]
            for j in range(per):
                f, s = divmod(tile * per + j, net.n_s)
                self.out[s, f] = pltpu.roll(value, 128 - j * width, axis=1) if j else value
        for k in range(1, net.n_s):
            self.one(k).start()

    def middle(self):
        net = self.net
        total = self.out[net.s]
        for k in range(1, net.n_s):
            self.one(k).wait()
            total = total + self.seq_in[k]
        self.total[...] = total
        for k in range(1, net.n_f):
            self.two(k).start()

    def finish(self, result):
        net = self.net
        total = self.total[net.f]
        for k in range(1, net.n_f):
            self.two(k).wait()
            total = total + self.fsdp_in[k]
        result[...] = total


def norm_backward(rows, source, grad, gain, terms, at, write):
    terms[at : at + 2, :] = jnp.zeros((2, terms.shape[1]), F32)

    @pl.loop(0, rows // 32, unroll=2)
    def _(i):
        span = aligned(i * 32, 32)
        scaled, inverse = normalize(source[span, :].astype(F32))
        value = grad[span, :]
        upstream = value * gain
        inner = jnp.mean(upstream, -1, keepdims=True)
        cross = jnp.mean(upstream * scaled, -1, keepdims=True)
        terms[at : at + 1, :] = terms[at : at + 1, :] + jnp.sum(value * scaled, 0, keepdims=True)
        terms[at + 1 : at + 2, :] = terms[at + 1 : at + 2, :] + jnp.sum(value, 0, keepdims=True)
        write(i, span, inverse * (upstream - inner - scaled * cross))


def layer_kernel(
    tok,
    gain_one,
    shift_one,
    gain_two,
    shift_two,
    bias,
    wq_own,
    wo_own,
    wg_own,
    wu_own,
    wd_own,
    gout_own,
    cosine,
    sine,
    q_o,
    k_o,
    kt_o,
    v_o,
    att_o,
    att_t_o,
    lse_o,
    n1_o,
    gains_o,
    wq_o,
    wo_o,
    dm_o,
    datt_o,
    dmid_o,
    top_o,
    terms_o,
    gate_o,
    up_o,
    down_o,
    rows,
    gout,
    wq,
    wo,
    wg,
    wu,
    wd,
    q,
    k,
    kt,
    v,
    vt,
    ot,
    att,
    att_t,
    hidden,
    dgate,
    dup,
    mid,
    low,
    packet,
    packets,
    tiles,
    total,
    *rest,
):
    net = Net()
    chunk, width = tok.shape
    length = chunk * net.n_s
    depth = wq_own.shape[1]
    columns = wq_own.shape[2]
    heads = columns // HEAD
    pair = 2 * chunk
    buffers, rest = rest[:4], rest[4:]
    folds = []
    for _ in range(3):
        folds.append(Fold(net, tiles, total, *buffers, *rest[:4]))
        rest = rest[4:]
    att_fold, normed_fold, top_fold = folds
    line_sems = [rest[at : at + 3] for at in (0, 3, 6, 9)]
    rest = rest[12:]
    spread_sems, rest = rest[:5], rest[5:]
    gate_sum, up_sum, down_sum = [GridSum(net, *rest[at : at + 3]) for at in (0, 3, 6)]
    sums = (down_sum, gate_sum, up_sum)
    pk_sems, copy_sems, n1_sems, free_sem = rest[9:]
    copies = Copies(copy_sems)
    n1 = att_fold.mate_out

    packet[...] = jnp.zeros(packet.shape, F32)
    own = gain_one.shape[1]
    for at, part in enumerate((gain_one, shift_one, gain_two, shift_two)):
        packet[at : at + 1, 0:own] = part[...].astype(F32)
    packet[4:7, 0:own] = bias[...].astype(F32)
    def wq_part(f, half):
        if half is None:
            return wq.at[:, aligned(f * depth, depth), :]
        return wq.at[:, aligned(f * depth + half * (depth // 2), depth // 2), :]

    spread_q = Spread(net, wq_own, wq_part, spread_sems[0])
    spread_o, spread_g, spread_u, spread_d = [
        Spread(net, own, columns_of(full, depth), sems)
        for own, full, sems in zip((wo_own, wg_own, wu_own, wd_own), (wo, wg, wu, wd), spread_sems[1:])
    ]
    pk = Packets(net, packet, packets, pk_sems)
    line = Line(net, tok, rows_of(rows, chunk), *line_sems[0])
    gout_line = Line(net, gout_own, rows_of(gout, chunk), *line_sems[1])
    n2_line = Line(net, low, rows_of(rows, chunk), *line_sems[2])
    dm_line = Line(net, low, rows_of(rows, chunk), *line_sems[3])

    for ready in (line, spread_q, spread_o, spread_g, spread_u, spread_d, gout_line):
        ready.prepare()
    net.barrier()

    def pairs(which, hop):
        net.sides(hop, lambda other, side: which.pair(other))

    def blocks(hop, act):
        def once(other, side):
            @pl.when((hop > 0) | (side == 0))
            def _():
                act(other, side)

        net.sides(hop, once)

    pk.start()
    line.start()
    spread_q.start()
    pk.middle()
    pk.finish()
    pk.unpack(gains_o, width // (net.n_f * net.n_s))

    def project_block(other, side):
        span = aligned(other * pair, pair)
        gain, shift = gains_o[0:1, :], gains_o[1:2, :]

        for part in range(2):

            @pl.loop(0, chunk // 32, unroll=2)
            def _(i):
                at = aligned((2 * other + part) * chunk + i * 32, 32)
                scaled, _ = normalize(rows[at, :].astype(F32))
                n1[part, aligned(i * 32, 32), :] = (scaled * gain + shift).astype(BF)

        keeps = [
            pltpu.make_async_copy(
                n1.at[part], n1_o.at[aligned((2 * other + part) * chunk, chunk)], n1_sems.at[part]
            )
            for part in range(2)
        ]
        for copy in keeps:
            copy.start()
        left = n1[0:2].reshape(pair, width)
        cols = aligned(net.s * columns, columns)
        tables = cosine[span, :], sine[span, :]
        for kind in range(3):
            value = dot(left, wq[kind]) + gains_o[4 + kind : 5 + kind, cols]
            if kind == 0:
                q[span, :] = rotary(value, *tables).astype(BF)
            elif kind == 1:
                value = rotary(value, *tables).astype(BF)
                k[span, :] = value
                kt[...] = turned(value)
            else:
                value = value.astype(BF)
                v[...] = value
                vt[:, span] = turned(value)
        for copy in (
            pltpu.make_async_copy(kt, kt_o.at[:, span], n1_sems.at[2]),
            pltpu.make_async_copy(v, v_o.at[span], n1_sems.at[3]),
        ):
            copy.start()
            keeps.append(copy)
        for copy in keeps:
            copy.wait()

    line.here()
    for hop in range(1, net.n_l - 1):
        line.step(hop)
        if hop == 1:
            spread_q.relay()
        pairs(line, hop)
    spread_o.start()
    spread_q.finish()
    spread_g.start()
    pl.loop(0, net.n_l - 1)(lambda hop: blocks(hop, project_block))
    spread_o.relay()
    spread_u.start()
    line.step(net.n_l - 1)
    gout_line.start()
    pairs(line, net.n_l - 1)
    blocks(net.n_l - 1, project_block)
    q_copy = copies.start(q, q_o)
    for pair_of in ((wq, wq_o), (k, k_o)):
        copies.start(*pair_of)
    spread_o.finish()
    line.finish()

    def attend(i):
        lo, hi = i * pair, (i + 1) * pair

        @pl.loop(0, heads)
        def _(head):
            lane = lax.broadcasted_iota(jnp.int32, (1, columns), 1)
            here = jnp.where(lane // HEAD == head, HEAD**-0.5, 0.0).astype(BF)
            visible = lax.broadcasted_iota(jnp.int32, (pair, pair), 0) <= lax.broadcasted_iota(
                jnp.int32, (pair, pair), 1
            )
            head_rows = aligned(head * HEAD, HEAD)
            query = q[lo:hi, :] * here
            near = jnp.where(visible, dot_nt(k[lo:hi, :], query), NEG_LARGE)
            highest = jnp.max(near, 0, keepdims=True)
            if i:
                far = dot_nt(k[0:lo, :], query)
                highest = jnp.maximum(highest, jnp.max(far, 0, keepdims=True))
            near = jnp.exp(near - highest)
            sum_of = jnp.sum(near, 0, keepdims=True)
            out = dot(vt[head_rows, lo:hi], near.astype(BF))
            if i:
                far = jnp.exp(far - highest)
                sum_of = sum_of + jnp.sum(far, 0, keepdims=True)
                out = out + dot(vt[head_rows, 0:lo], far.astype(BF))
            ot[head_rows, :] = out / sum_of
            lse_o[pl.ds(head, 1), lo:hi] = highest + jnp.log(sum_of)

        att_t[:, lo:hi] = ot[...].astype(BF)
        att[lo:hi, :] = turned(att_t[:, lo:hi])

    def produce_attended(place, write):
        for i in range(net.n_l):
            pl.when(place == i)(functools.partial(attend, i))
        left = att[aligned(place * pair, pair), :]

        @pl.loop(0, width // TILE)
        def _(j):
            cols = aligned(j * TILE, TILE)
            write(cols, dot(left, wo[:, cols]))

    def relays():
        gout_line.step(1)
        spread_d.start()

    att_fold.begin(produce_attended, relays)
    copies.start(att, att_o)
    copies.start(att_t, att_t_o)
    copies.start(wo, wo_o)
    if net.n_l > 2:
        gout_line.step(2)
    att_fold.open_total()
    spread_g.relay()
    for at in range(1, net.n_l):
        if 2 < at + 1 < net.n_l:
            gout_line.step(at + 1)
        att_fold.wave(at)
        if at == 1:
            spread_u.relay()
        if at == min(2, net.n_l - 1):
            spread_d.relay()
    gain_two, shift_two = gains_o[2:3, :], gains_o[3:4, :]

    @pl.loop(0, chunk // 32, unroll=2)
    def _(i):
        span = aligned(i * 32, 32)
        value = rows[aligned(net.s * chunk + i * 32, 32), :].astype(F32) + total[span, :]
        mid[span, :] = value
        scaled, _ = normalize(value)
        low[span, :] = (scaled * gain_two + shift_two).astype(BF)

    n2_line.prepare()
    n2_line.start()
    att_fold.finish()
    gout_line.here()
    pl.loop(1, net.n_l)(lambda hop: pairs(gout_line, hop))

    def forward_block(other):
        span = aligned(other * pair, pair)
        right = rows[span, :]
        half = hidden.shape[0] // 2

        @pl.loop(0, 2)
        def _(part):
            units = aligned(part * half, half, 16)
            gate = dot_nt(wg[units, :], right)
            up = dot_nt(wu[units, :], right)
            back = dot_nt(wd[units, :], gout[span, :])
            sigma = jax.nn.sigmoid(gate)
            active = gate * sigma
            hidden[units, span] = (active * up).astype(BF)
            dgate[units, span] = (back * up * (sigma * (1.0 + gate * (1.0 - sigma)))).astype(BF)
            dup[units, span] = (back * active).astype(BF)

    def produce_normed(place, write):
        span = aligned(place * pair, pair)
        left, right = turned(dgate[:, span]), turned(dup[:, span])

        @pl.loop(0, width // TILE)
        def _(j):
            cols = aligned(j * TILE, TILE)
            write(cols, dot(left, wg[:, cols]) + dot(right, wu[:, cols]))

    def begin_normed(other, side, hop):
        @pl.when(hop > 1)
        def _():
            normed_fold.mate_sent(side)

        normed_fold.begin_one(other, side + (2 - side) * (1 // (hop + 1)), produce_normed)

    def forward_blocks(hop):
        def act(other, side):
            forward_block(other)

            @pl.when(jnp.logical_not(normed_fold.fed(side)))
            def _():
                begin_normed(other, side, hop)
                normed_fold.leave(other, side, hop)

        net.sides(hop, act)

    def begin_fed(hop):
        def act(other, side):
            pl.when(normed_fold.fed(side))(lambda: begin_normed(other, side, hop))

        net.sides(hop, act)

    n2_line.here()
    for spread in (spread_g, spread_u, spread_d):
        spread.finish()
    forward_block(net.z)

    @pl.loop(1, net.n_l)
    def _(hop):
        n2_line.step(hop)
        pairs(n2_line, hop)
        pl.when(hop == 1)(lambda: normed_fold.begin_one(net.z, 2, produce_normed))
        forward_blocks(hop)
        pl.when(hop > 1)(lambda: begin_fed(hop - 1))

    begin_fed(net.n_l - 1)

    def weight_terms(task):
        at, kind = net.n_f - 1 - task // 3, task % 3
        cols = aligned(gate_sum.owner(at) * depth, depth)
        for way, (grid_sum, left, right) in enumerate(
            ((down_sum, hidden, gout), (gate_sum, dgate, rows), (up_sum, dup, rows))
        ):

            @pl.when(kind == way)
            def _():
                half = left.shape[0] // 2

                @pl.loop(0, 2)
                def _(part):
                    units = aligned(part * half, half, 16)
                    grid_sum.stage[at, units, :] = dot(left[units, :], right[:, cols]).astype(BF)

                grid_sum.first(at)

    tasks = 3 * net.n_f
    waves = max(net.n_l - 2, 1)
    each = -(-tasks // (2 * normed_fold.pieces * waves))
    for wave in range(net.n_l - waves, net.n_l):

        def between(turn, piece):
            slot = ((wave - net.n_l + waves) * 2 + turn) * normed_fold.pieces + piece

            @pl.loop(0, each)
            def _(i):
                pl.when(slot * each + i < tasks)(lambda: weight_terms(slot * each + i))

        normed_fold.passes_between(wave, True, between)
    normed_fold.finals()
    n2_line.finish()

    def beside(act):
        act(net.mate)
        for side in range(2):
            pl.when(n2_line.goes_on(side))(lambda: act(net.s + 2 - 4 * side))

    beside(lambda to: pl.semaphore_signal(free_sem, 1, device_id={"seq": to}, device_id_type=MESH))

    def write_middle(i, span, value):
        value = value + gout[aligned(net.s * chunk + i * 32, 32), :].astype(F32)
        dmid_o[span, :] = value
        low[span, :] = value.astype(BF)

    terms_o[...] = jnp.zeros(terms_o.shape, F32)
    norm_backward(chunk, mid, total, gain_two, terms_o, 2, write_middle)
    ends = (net.z + net.n_l - 1) // net.n_l + (2 * net.n_l - 2 - net.z) // net.n_l
    pl.semaphore_wait(free_sem, 1 + ends)
    dm_line.prepare()
    dm_line.start()
    normed_fold.finish()

    def produce_top(place, write):
        left = turned(hidden[:, aligned(place * pair, pair)])

        @pl.loop(0, width // TILE)
        def _(j):
            cols = aligned(j * TILE, TILE)
            write(cols, dot(left, wd[:, cols]))

    copies.wait(q_copy)
    datt = q

    def back_block(other, side):
        span = aligned(other * pair, pair)
        datt[span, :] = dot_nt(rows[span, :], wo[...]).astype(BF)

    dm_line.here()
    dm_line.step(1)
    top_fold.begin(produce_top)
    back_block(net.z, 0)
    top_fold.open_total()
    for at in range(1, net.n_l):
        if at + 1 < net.n_l:
            dm_line.step(at + 1)
        top_fold.wave(at)
        pairs(dm_line, at)
        net.sides(at, back_block)
    copies.start(datt, datt_o)
    copies.start(rows, dm_o)

    @pl.loop(0, chunk // 32)
    def _(i):
        span = aligned(i * 32, 32)
        top_fold.out[net.z, span, :] = (mid[span, :] + total[span, :]).astype(BF)

    copies.start(top_fold.out.at[net.z], top_o)
    top_fold.finish()
    gout_line.finish()
    dm_line.finish()
    hands = []
    for grid_sum, out in zip(sums, (down_o, gate_o, up_o)):
        grid_sum.sum_first()
        hands.extend(grid_sum.hand_on(out))
        for copy in grid_sum.hand_on(out):
            copy.start()
    for grid_sum in sums:
        grid_sum.finish_first()
    for copy in hands:
        copy.wait()
    copies.wait()


def layer_part(tokens, norms, wq, wo, wg, wu, wd, gout, tables):
    chunk, width = tokens.shape
    n_f, n_s = lax.axis_size("fsdp"), lax.axis_size("seq")
    length = chunk * n_s
    depth, columns = wq.shape[1:]
    units = wg.shape[0]
    shape = jax.ShapeDtypeStruct
    wide, head, turned, weight = (length, width), (length, columns), (units, length), (units, width)
    return pl.pallas_call(
        layer_kernel,
        name="layer",
        out_shape=[
            shape(head, BF),
            shape(head, BF),
            shape((columns, length), BF),
            shape(head, BF),
            shape(head, BF),
            shape((columns, length), BF),
            shape((8, length), F32),
            shape(wide, BF),
            shape((SMALL, width), F32),
            shape((3, width, columns), BF),
            shape((columns, width), BF),
            shape(wide, BF),
            shape(head, BF),
            shape((chunk, width), F32),
            shape((chunk, width), BF),
            shape((SMALL, width), F32),
            *[shape((GridEnd.count(n_f), units // 2, depth), BF)] * 3,
        ],
        in_specs=[ANY, *[VMEM] * 5, *[ANY] * 6, VMEM, VMEM],
        out_specs=[*[ANY] * 6, VMEM, ANY, VMEM, *[ANY] * 4, VMEM, ANY, VMEM, *[ANY] * 3],
        scratch_shapes=[
            pltpu.VMEM(wide, BF),
            pltpu.VMEM(wide, BF),
            pltpu.VMEM((3, width, columns), BF),
            pltpu.VMEM((columns, width), BF),
            *[pltpu.VMEM(weight, BF)] * 3,
            pltpu.VMEM(head, BF),
            pltpu.VMEM(head, BF),
            pltpu.VMEM((columns, 2 * chunk), BF),
            pltpu.VMEM((2 * chunk, columns), BF),
            pltpu.VMEM((columns, length), BF),
            pltpu.VMEM((columns, 2 * chunk), F32),
            pltpu.VMEM(head, BF),
            pltpu.VMEM((columns, length), BF),
            *[pltpu.VMEM(turned, BF)] * 3,
            pltpu.VMEM((chunk, width), F32),
            pltpu.VMEM((chunk, width), BF),
            pltpu.VMEM((SMALL, 128), F32),
            pltpu.VMEM((n_s, n_f, SMALL, 128), F32),
            *Fold.shared(chunk, width),
            *Fold.buffers(n_s, chunk, width),
            *Fold.sems(n_s) * 3,
            *Line.sems(n_s) * 4,
            *[pltpu.SemaphoreType.DMA((Spread.count(n_f),))] * 5,
            *GridSum.scratch(n_f, units, depth) * 3,
            pltpu.SemaphoreType.DMA((Packets.count(n_f, n_s),)),
            pltpu.SemaphoreType.DMA((9,)),
            pltpu.SemaphoreType.DMA((4,)),
            pltpu.SemaphoreType.REGULAR,
        ],
        compiler_params=pltpu.CompilerParams(
            collective_id=1, has_side_effects=True, vmem_limit_bytes=VMEM_BYTES
        ),
        cost_estimate=pl.CostEstimate(
            flops=2 * length * width * (4 * columns + 9 * units),
            bytes_accessed=8 * length * width,
            transcendentals=length * (length * columns // HEAD + units),
        ),
    )(tokens, *norms, wq, wo, wg, wu, wd, gout, *tables)


def back_kernel(
    datt_in,
    q_in,
    k_in,
    kt_in,
    v_in,
    att_in,
    att_t_in,
    wq_in,
    n1_in,
    dm_in,
    down_in,
    gate_in,
    up_in,
    lse,
    tok,
    dmid,
    gains,
    terms_in,
    cosine,
    sine,
    gin_o,
    small_o,
    out_o,
    qkv_o,
    down_o,
    gate_o,
    up_o,
    datt,
    q,
    k,
    kt,
    v,
    att,
    att_t,
    wq,
    n1,
    dm,
    query,
    upstream,
    inners,
    dk,
    dv,
    dqt,
    dproj,
    dproj_t,
    terms,
    tiles,
    total,
    *rest,
):
    net = Net()
    chunk, width = tok.shape
    length, columns = q_in.shape
    heads = columns // HEAD
    pair = 2 * chunk
    depth = width // net.n_f
    block = 256
    buffers, rest = rest[:4], rest[4:]
    fold_sems, rest = rest[:4], rest[4:]
    packet_scratch, rest = rest[:5], rest[5:]
    out_sum, qkv_sum = GridSum(net, *rest[:3]), GridSum(net, *rest[3:6])
    ends = [GridEnd(net, *rest[at : at + 3]) for at in (6, 9, 12)]
    copy_sems, column_sems = rest[15:]

    copies = Copies(copy_sems)
    loads = [
        copies.start(src, dst)
        for src, dst in (
            (datt_in, datt),
            (q_in, q),
            (k_in, k),
            (kt_in, kt),
            (v_in, v),
            (att_in, att),
            (att_t_in, att_t),
            (wq_in, wq),
            (down_in, ends[0].sums),
            (gate_in, ends[1].sums),
            (up_in, ends[2].sums),
        )
    ]
    def load(at, way):
        src, dst = ((n1_in, n1), (dm_in, dm))[way]
        cols = aligned(qkv_sum.owner(at) * depth, depth)
        return pltpu.make_async_copy(src.at[:, cols], dst.at[at % 2], column_sems.at[way, at % 2])

    for at in range(net.n_f - 1, max(net.n_f - 3, -1), -1):
        for way in range(2):
            load(at, way).start()

    @pl.loop(0, length // block)
    def _(i):
        span = aligned(i * block, block)
        dk[span, :] = jnp.zeros((block, columns), F32)
        dv[span, :] = jnp.zeros((block, columns), F32)

    net.barrier()
    copies.wait(*loads[:6])

    def start_ends():
        for load_of in loads[8:]:
            load_of.wait()
        for end in ends:
            end.start()


    of_head = (
        lax.broadcasted_iota(jnp.int32, (8, columns), 1) // HEAD
        == lax.broadcasted_iota(jnp.int32, (8, columns), 0)
    ).astype(F32)

    @pl.loop(0, length // block)
    def _(i):
        span = aligned(i * block, block)
        product = datt[span, :].astype(F32) * att[span, :].astype(F32)
        inners[:, span] = lax.dot_general(
            of_head,
            product,
            (((1,), (1,)), ((), ())),
            precision=lax.Precision.HIGHEST,
            preferred_element_type=F32,
        )

    @pl.loop(0, heads)
    def _(head):
        lane = lax.broadcasted_iota(jnp.int32, (1, columns), 1)
        here = jnp.where(lane // HEAD == head, 1.0, 0.0).astype(BF)
        scale = HEAD**-0.5
        visible = lax.broadcasted_iota(jnp.int32, (block, block), 0) <= lax.broadcasted_iota(
            jnp.int32, (block, block), 1
        )
        head_rows = aligned(head * HEAD, HEAD)

        @pl.loop(0, length // block)
        def _(i):
            span = aligned(i * block, block)
            query[span, :] = q[span, :] * (here * scale)
            upstream[span, :] = datt[span, :] * here

        pl.when(head == min(1, heads - 1))(start_ends)

        for j in range(length // block):
            at, end = j * block, (j + 1) * block
            keys, values, turned = k[at:end, :], v[at:end, :], kt[head_rows, at:end]

            def part(lo, hi, near):
                probs = jnp.exp(dot_nt(keys, query[lo:hi, :]) - lse[pl.ds(head, 1), lo:hi])
                if near:
                    probs = jnp.where(visible, probs, 0.0)
                grads = dot_nt(values, upstream[lo:hi, :])
                scores = (probs * (grads - inners[pl.ds(head, 1), lo:hi])).astype(BF)
                out = dot(turned, scores)
                dqt[head_rows, lo:hi] = dqt[head_rows, lo:hi] + out if j else out
                return dot(probs.astype(BF), upstream[lo:hi, :]), dot(scores, query[lo:hi, :])

            value_grads, key_grads = part(at, end, True)
            if end < length:
                more_values, more_keys = part(end, length, False)
                value_grads, key_grads = value_grads + more_values, key_grads + more_keys
            dv[at:end, :] = dv[at:end, :] + value_grads
            dk[at:end, :] = dk[at:end, :] + key_grads

    terms[...] = terms_in[...]
    bias_cols = aligned(net.s * columns, columns)

    @pl.loop(0, length // block)
    def _(i):
        span = aligned(i * block, block)
        tables = cosine[span, :], -sine[span, :]
        parts = [
            rotary(turned((dqt[:, span] * HEAD**-0.5).astype(BF)).astype(F32), *tables).astype(BF),
            rotary(dk[span, :].astype(BF).astype(F32), *tables).astype(BF),
            dv[span, :].astype(BF),
        ]
        for kind in range(3):
            dproj[kind, span, :] = parts[kind]
            dproj_t[kind, :, span] = turned(parts[kind])
            row = slice(4 + kind, 5 + kind)
            terms[row, bias_cols] = terms[row, bias_cols] + jnp.sum(parts[kind].astype(F32), 0, keepdims=True)

    def weight_terms(task):
        at = net.n_f - 1 - task // 2

        def loaded(way):
            load(at, way).wait()

        def next_load(way):
            pl.when(at >= 2)(lambda: load(at - 2, way).start())

        @pl.when(task % 2 == 0)
        def _():
            loaded(0)
            right = n1[at % 2]
            for kind in range(3):
                rows = slice(kind * columns, (kind + 1) * columns)
                qkv_sum.stage[at, rows, :] = dot(dproj_t[kind], right).astype(BF)
            next_load(0)
            qkv_sum.first(at)

        @pl.when(task % 2 == 1)
        def _():
            loaded(1)
            out_sum.stage[at] = dot(att_t[...], dm[at % 2]).astype(BF)
            next_load(1)
            out_sum.first(at)

    def produce(place, write):
        span = aligned(place * pair, pair)

        @pl.loop(0, width // TILE)
        def _(j):
            cols = aligned(j * TILE, TILE)
            value = dot_nt(dproj[0, span, :], wq[0, cols, :])
            for kind in range(1, 3):
                value = value + dot_nt(dproj[kind, span, :], wq[kind, cols, :])
            write(cols, value)

    fold = Fold(net, tiles, total, *buffers, *fold_sems)
    copies.wait(*loads[6:8])
    tasks = 2 * net.n_f
    ahead = 2 * (net.n_l - 1)

    def meanwhile(task):
        pl.when(task < tasks)(lambda: weight_terms(task))

    fold.begin(produce, meanwhile=meanwhile)
    fold.open_total()
    waves = max(net.n_l - 2, 1)
    each = -(-max(tasks - ahead, 0) // (2 * fold.pieces * waves))

    def between(slot):
        @pl.loop(0, each)
        def _(i):
            task = ahead + slot * each + i
            pl.when(task < tasks)(lambda: weight_terms(task))

    for at in range(1, waves + 1):
        fold.wave(at, between=between)
    for at in range(waves + 1, net.n_l):
        fold.wave(at)

    def write_input(i, span, value):
        gin_o[span, :] = value + dmid[span, :]

    norm_backward(chunk, tok, total, gains[0:1, :], terms, 0, write_input)
    packet_sum = PacketSum(net, *packet_scratch)
    packet_sum.start(terms, width // (net.n_f * net.n_s))
    for grid_sum in (qkv_sum, out_sum):
        grid_sum.second()
    packet_sum.middle()
    for end, out in zip(ends, (down_o, gate_o, up_o)):
        end.last(out)
    packet_sum.finish(small_o)
    fold.finish()
    for grid_sum, out in ((qkv_sum, qkv_o), (out_sum, out_o)):
        grid_sum.last(out)
        grid_sum.finish()


def back_part(datt, q, k, kt, v, att, att_t, wq, n1, dm, down, gate, up, lse, tokens, dmid, gains, terms, tables):
    chunk, width = tokens.shape
    n_f, n_s = lax.axis_size("fsdp"), lax.axis_size("seq")
    length, columns = q.shape
    depth = width // n_f
    units = 2 * gate.shape[1]
    shape = jax.ShapeDtypeStruct
    return pl.pallas_call(
        back_kernel,
        name="back",
        out_shape=[
            shape((chunk, width), F32),
            shape((SMALL, 128), F32),
            shape((columns, depth), F32),
            shape((3 * columns, depth), F32),
            *[shape((units, depth), F32)] * 3,
        ],
        in_specs=[ANY] * 13 + [VMEM] * 7,
        out_specs=[VMEM] * 7,
        scratch_shapes=[
            pltpu.VMEM((length, columns), BF),
            pltpu.VMEM((length, columns), BF),
            pltpu.VMEM((length, columns), BF),
            pltpu.VMEM((columns, length), BF),
            pltpu.VMEM((length, columns), BF),
            pltpu.VMEM((length, columns), BF),
            pltpu.VMEM((columns, length), BF),
            pltpu.VMEM((3, width, columns), BF),
            pltpu.VMEM((2, length, depth), BF),
            pltpu.VMEM((2, length, depth), BF),
            pltpu.VMEM((length, columns), BF),
            pltpu.VMEM((length, columns), BF),
            pltpu.VMEM((8, length), F32),
            pltpu.VMEM((length, columns), F32),
            pltpu.VMEM((length, columns), F32),
            pltpu.VMEM((columns, length), F32),
            pltpu.VMEM((3, length, columns), BF),
            pltpu.VMEM((3, columns, length), BF),
            pltpu.VMEM((SMALL, width), F32),
            *Fold.shared(chunk, width),
            *Fold.buffers(n_s, chunk, width),
            *Fold.sems(n_s, 8),
            *PacketSum.scratch(n_f, n_s),
            *GridSum.scratch(n_f, columns, depth),
            *GridSum.scratch(n_f, 3 * columns, depth),
            *GridEnd.scratch(n_f, units, depth) * 3,
            pltpu.SemaphoreType.DMA((11,)),
            pltpu.SemaphoreType.DMA((2, 2)),
        ],
        compiler_params=pltpu.CompilerParams(
            collective_id=3, has_side_effects=True, vmem_limit_bytes=VMEM_BYTES
        ),
        cost_estimate=pl.CostEstimate(
            flops=2 * length * columns * (8 * width + 5 * length),
            bytes_accessed=4 * length * width,
            transcendentals=length * length * columns // HEAD,
        ),
    )(datt, q, k, kt, v, att, att_t, wq, n1, dm, down, gate, up, lse, tokens, dmid, gains, terms, *tables)


def outputs_kernel(small, *refs):
    sources, targets, parts = refs[:7], refs[7:14], refs[14:]
    own = parts[0].shape[1]
    for src, dst in zip(sources, targets):
        if src.shape == dst.shape:
            dst[...] = src[...]
        else:
            rows, columns = src.shape[0] // 3, src.shape[1]
            for kind in range(3):
                dst[kind * columns : (kind + 1) * columns, :] = src[kind * rows : (kind + 1) * rows, :].T
    for at in range(4):
        parts[at][...] = small[at : at + 1, 0:own]
    parts[4][...] = small[4:7, 0:own]


def outputs_part(small, own, *arrays):
    shape = jax.ShapeDtypeStruct
    return pl.pallas_call(
        outputs_kernel,
        name="outputs",
        out_shape=[shape((3 * v.shape[1], v.shape[0] // 3) if at == 2 else v.shape, v.dtype) for at, v in enumerate(arrays)]
        + [shape((1, own), F32)] * 4
        + [shape((3, own), F32)],
        in_specs=[VMEM] * 8,
        out_specs=[VMEM] * 12,
        compiler_params=pltpu.CompilerParams(vmem_limit_bytes=VMEM_BYTES),
    )(small, *arrays)


def per_device(
    tokens,
    gain_one,
    shift_one,
    w_qkv,
    b_qkv,
    w_out,
    gain_two,
    shift_two,
    w_gate,
    w_up,
    w_down,
    grad_output,
):
    length = tokens.shape[1] * lax.axis_size("seq")
    width = gain_one.shape[0]
    norms = [v[None] for v in (gain_one, shift_one, gain_two, shift_two)] + [b_qkv]
    tables = rotary_tables(length)
    q, k, kt, v, att, att_t, lse, n1, gains, wq, _, dm, datt, dmid, top, terms, gate, up, down = layer_part(
        tokens[0], norms, w_qkv.transpose(1, 0, 2), w_out, w_gate.T, w_up.T, w_down, grad_output[0], tables
    )
    grad_input, small, out, qkv, down, gate, up = back_part(
        datt, q, k, kt, v, att, att_t, wq, n1, dm, down, gate, up, lse, tokens[0], dmid, gains, terms, tables
    )

    top, grad_input, qkv, out, gate, up, down, one, shift, two, shift_to, bias = outputs_part(
        small, width, top, grad_input, qkv, out, gate, up, down
    )
    return (
        top[None],
        grad_input[None],
        one[0],
        shift[0],
        qkv.reshape(3, -1, qkv.shape[1]).transpose(1, 0, 2),
        bias,
        out,
        two[0],
        shift_to[0],
        gate.T,
        up.T,
        down,
    )


def solution(mesh):
    whole = P(("fsdp", "seq"))
    rows = P("fsdp", "seq", None)
    inner = P("seq", "fsdp")
    outer = P("fsdp", "seq")
    heads = P("fsdp", None, "seq")
    bias = P(None, ("fsdp", "seq"))
    return jax.shard_map(
        per_device,
        mesh=mesh,
        in_specs=(rows, whole, whole, heads, bias, inner, whole, whole, outer, outer, inner, rows),
        out_specs=(rows, rows, whole, whole, heads, bias, inner, whole, whole, outer, outer, inner),
        check_vma=False,
    )
```

```python
import functools

import jax
import jax.numpy as jnp
import numpy as np
from jax import lax
from jax.experimental import pallas as pl
from jax.experimental.pallas import tpu as pltpu
from jax.sharding import PartitionSpec as P

HEAD = 64
ROT = 16
EPSILON = 1e-05
NEG_LARGE = -1e30
MESH = pl.DeviceIdType.MESH
ANY = pl.BlockSpec(memory_space=pl.ANY)
VMEM = pl.BlockSpec(memory_space=pltpu.VMEM)
BF = jnp.bfloat16
F32 = jnp.float32
VMEM_BYTES = 60 * 2**20
TILE = 512
SMALL = 8


def put(src, dst, send, recv, **device):
    return pltpu.make_async_remote_copy(
        src_ref=src, dst_ref=dst, send_sem=send, recv_sem=recv, device_id=device, device_id_type=MESH
    )


def dot(left, right):
    return jnp.dot(left, right, preferred_element_type=F32)


def dot_nt(left, right):
    return lax.dot_general(left, right, (((1,), (1,)), ((), ())), preferred_element_type=F32)


def dot_tn(left, right):
    return lax.dot_general(left, right, (((0,), (0,)), ((), ())), preferred_element_type=F32)


def turned(values):
    size = values.shape[1]
    same = lax.broadcasted_iota(jnp.int32, (size, size), 0) == lax.broadcasted_iota(
        jnp.int32, (size, size), 1
    )
    return dot_nt(jnp.where(same, 1.0, 0.0).astype(BF), values).astype(BF)


def aligned(start, size, unit=None):
    return pl.ds(pl.multiple_of(start, unit or size), size)


class Net:
    def __init__(self):
        self.n_f, self.n_s = lax.axis_size("fsdp"), lax.axis_size("seq")
        self.tall = 2 if self.n_f % 2 == 0 else 1
        self.wide = self.n_f // self.tall
        self.n_l = self.n_s // 2
        self.f, self.s = lax.axis_index("fsdp"), lax.axis_index("seq")
        self.a, self.b = self.f // self.wide, self.f % self.wide
        self.z, self.c = self.s // 2, self.s % 2
        self.mate = self.s + 1 - 2 * self.c

    def barrier(self):
        sem = pltpu.get_barrier_semaphore()
        for k in range(1, self.n_f):
            pl.semaphore_signal(
                sem, inc=1, device_id={"fsdp": (self.f + k) % self.n_f}, device_id_type=MESH
            )
        for k in range(1, self.n_s):
            pl.semaphore_signal(
                sem, inc=1, device_id={"seq": (self.s + k) % self.n_s}, device_id_type=MESH
            )
        pl.semaphore_wait(sem, self.n_f + self.n_s - 2)

    def sides(self, hop, act):
        @pl.loop(0, 2)
        def _(side):
            other = self.z + (2 * side - 1) * hop

            @pl.when((other >= 0) & (other < self.n_l))
            def _():
                act(other, side)


class Spread:
    def __init__(self, net, src, part, sems):
        self.net, self.src, self.part, self.sems = net, src, part, sems
        self.rows = [j for j in range(1, net.wide)]
        self.cols = [i for i in range(1, net.tall)]

    @staticmethod
    def count(n_f):
        tall = 2 if n_f % 2 == 0 else 1
        wide = n_f // tall
        return 1 + 2 * (wide - 1) + 2 * (tall - 1) + 4 * (wide - 1) * (tall - 1)

    def at(self, kind, i, j):
        w, t = len(self.rows), len(self.cols)
        base = {
            "own": 0,
            "row": 1,
            "col": 1 + 2 * w,
            "half0": 1 + 2 * w + 2 * t,
            "half1": 1 + 2 * w + 2 * t + 2 * w * t,
        }[kind]
        if kind == "own":
            return self.sems.at[0]
        k = j - 1 if kind == "row" else i - 1 if kind == "col" else (i - 1) * w + j - 1
        return self.sems.at[base + 2 * k], self.sems.at[base + 2 * k + 1]

    def rank(self, i, j):
        net = self.net
        return ((net.a + i) % net.tall) * net.wide + (net.b + j) % net.wide

    def back(self, i, j):
        net = self.net
        return ((net.a - i + net.tall) % net.tall) * net.wide + (net.b - j + net.wide) % net.wide

    def own(self):
        return pltpu.make_async_copy(self.src, self.part(self.net.f, None), self.at("own", 0, 0))

    def first(self, i, j):
        send, recv = self.at("row" if i == 0 else "col", i, j)
        place = self.part(self.net.f, None)
        return put(place, place, send, recv, fsdp=self.rank(i, j))

    def came(self, i, j):
        send, recv = self.at("row" if i == 0 else "col", i, j)
        place = self.part(self.back(i, j), None)
        return put(place, place, send, recv, fsdp=self.rank(i, j))

    def second(self, half, i, j, came=False):
        send, recv = self.at("half0" if half == 0 else "half1", i, j)
        origin = self.back(i, j) if came else self.back(0, j) if half == 0 else self.back(i, 0)
        place = self.part(origin, half)
        return put(place, place, send, recv, fsdp=self.rank(i, 0) if half == 0 else self.rank(0, j))

    def prepare(self):
        self.own().start()

    def start(self):
        self.own().wait()
        for i in self.cols:
            self.first(i, 0).start()
        for j in self.rows:
            self.first(0, j).start()

    def relay(self):
        for j in self.rows:
            self.came(0, j).wait_recv()
            for i in self.cols:
                self.second(0, i, j).start()
        for i in self.cols:
            self.came(i, 0).wait_recv()
            for j in self.rows:
                self.second(1, i, j).start()

    def finish(self):
        for j in self.rows:
            self.first(0, j).wait_send()
        for i in self.cols:
            self.first(i, 0).wait_send()
        for i in self.cols:
            for j in self.rows:
                for half in range(2):
                    self.second(half, i, j, came=True).wait_recv()
                    self.second(half, i, j).wait_send()


class Line:
    def __init__(self, net, src, part, recv, send, local):
        self.net, self.src, self.part, self.recv, self.send, self.local = net, src, part, recv, send, local
        self.pieces = recv.shape[1]
        self.rows = src.shape[0] // self.pieces

    @staticmethod
    def sems(n_s, pieces=2):
        return [
            pltpu.SemaphoreType.DMA((n_s, pieces)),
            pltpu.SemaphoreType.DMA((4, n_s // 2, pieces)),
            pltpu.SemaphoreType.DMA((1,)),
        ]

    def cut(self, ref, piece):
        return ref.at[aligned(piece * self.rows, self.rows)]

    def own(self):
        return pltpu.make_async_copy(self.src, self.part(self.net.s), self.local.at[0])

    def on_line(self, src, chunk, side, hop, piece):
        return put(
            self.cut(src, piece),
            self.cut(self.part(chunk), piece),
            self.send.at[side, hop, piece],
            self.recv.at[chunk, piece],
            seq=self.net.s + 2 - 4 * side,
        )

    def to_mate(self, src, chunk, side, hop, piece):
        return put(
            self.cut(src, piece),
            self.cut(self.part(chunk), piece),
            self.send.at[2 + side, hop, piece],
            self.recv.at[chunk, piece],
            seq=self.net.mate,
        )

    def goes_on(self, side):
        after = self.net.z + 1 - 2 * side
        return (after >= 0) & (after < self.net.n_l)

    def each_piece(self, act):
        pl.loop(0, self.pieces)(act)

    def prepare(self):
        self.own().start()

    def start(self):
        net = self.net
        self.own().wait()
        place = self.part(net.s)

        @self.each_piece
        def _(piece):
            for side in range(2):

                @pl.when(self.goes_on(side))
                def _():
                    self.on_line(place, net.s, side, 0, piece).start()

            self.to_mate(place, net.s, 0, 0, piece).start()

    def came(self, chunk, piece):
        place = self.cut(self.part(chunk), piece)
        put(place, place, self.send.at[0, 0, 0], self.recv.at[chunk, piece], seq=self.net.mate).wait_recv()

    def step(self, hop):
        net = self.net

        @self.each_piece
        def _(piece):
            def act(other, side):
                chunk = 2 * other + net.c
                self.came(chunk, piece)

                @pl.when(self.goes_on(side))
                def _():
                    self.on_line(self.part(chunk), chunk, side, hop, piece).start()

                self.to_mate(self.part(chunk), chunk, side, hop, piece).start()

            net.sides(hop, act)

    def pair(self, other):
        @self.each_piece
        def _(piece):
            self.came(2 * other + 1 - self.net.c, piece)

    def here(self):
        self.pair(self.net.z)

    def finish(self):
        net = self.net
        place = self.part(net.s)

        @self.each_piece
        def _(piece):
            for side in range(2):

                @pl.when(self.goes_on(side))
                def _():
                    self.on_line(place, net.s, side, 0, piece).wait_send()

            self.to_mate(place, net.s, 0, 0, piece).wait_send()

            @pl.loop(1, net.n_l)
            def _(hop):
                def act(other, side):
                    chunk = 2 * other + net.c

                    @pl.when(self.goes_on(side))
                    def _():
                        self.on_line(self.part(chunk), chunk, side, hop, piece).wait_send()

                    self.to_mate(self.part(chunk), chunk, side, hop, piece).wait_send()

                net.sides(hop, act)


class Packets:
    def __init__(self, net, src, buf, sems):
        self.net, self.src, self.buf, self.sems = net, src, buf, sems

    @staticmethod
    def count(n_f, n_s):
        return 1 + 2 * (n_f - 1) + 2 * (n_s - 1)

    def own(self):
        net = self.net
        return pltpu.make_async_copy(self.src, self.buf.at[net.s, net.f], self.sems.at[0])

    def one(self, k, came=False):
        net = self.net
        f = (net.f - k + net.n_f) % net.n_f if came else net.f
        place = self.buf.at[net.s, f]
        return put(
            place if came else self.src,
            place,
            self.sems.at[2 * k - 1],
            self.sems.at[2 * k],
            fsdp=(net.f + k) % net.n_f,
        )

    def two(self, k, came=False):
        net = self.net
        place = self.buf.at[(net.s - k + net.n_s) % net.n_s if came else net.s]
        at = 2 * (net.n_f - 1) + 2 * k - 1
        return put(place, place, self.sems.at[at], self.sems.at[at + 1], seq=(net.s + k) % net.n_s)

    def start(self):
        self.own().start()
        for k in range(1, self.net.n_f):
            self.one(k).start()

    def middle(self):
        self.own().wait()
        for k in range(1, self.net.n_f):
            self.one(k, came=True).wait_recv()
            self.one(k).wait_send()
        for k in range(1, self.net.n_s):
            self.two(k).start()

    def finish(self):
        for k in range(1, self.net.n_s):
            self.two(k, came=True).wait_recv()
            self.two(k).wait_send()

    def unpack(self, out, width):
        net = self.net
        per = 128 // width
        for tile in range(net.n_f * net.n_s // per):
            total = None
            for j in range(per):
                f, s = divmod(tile * per + j, net.n_s)
                piece = self.buf[s, f]
                if j:
                    piece = pltpu.roll(piece, j * width, axis=1)
                total = piece if total is None else total + piece
            out[:, tile * 128 : (tile + 1) * 128] = total


def rotary(values, cosine, sine):
    columns = values.shape[1]
    half = ROT // 2
    times = columns // 128

    def wide(table):
        return table if times == 1 else jnp.concatenate([table] * times, axis=1)

    lane = lax.broadcasted_iota(jnp.int32, values.shape, 1)
    other = jnp.where(
        lane % HEAD < half, pltpu.roll(values, columns - half, axis=1), pltpu.roll(values, half, axis=1)
    )
    return values * wide(cosine) + other * wide(sine)


def rotary_tables(length):
    half = ROT // 2
    freqs = np.float32(10000.0) ** (-np.arange(half, dtype=np.float32) * np.float32(2.0 / ROT))
    angles = np.arange(length, dtype=np.float32)[:, None] * freqs[None, :].astype(np.float32)
    cosine, sine = np.cos(angles), np.sin(angles)
    rest = np.zeros((length, HEAD - ROT), np.float32)
    keep = np.concatenate([cosine, cosine, rest + 1], 1)
    swap = np.concatenate([-sine, sine, rest], 1)
    return [np.tile(t, (1, 128 // HEAD)).astype(np.float32) for t in (keep, swap)]


def normalize(values):
    center = values - jnp.mean(values, -1, keepdims=True)
    inverse = lax.rsqrt(jnp.mean(center * center, -1, keepdims=True) + EPSILON)
    return center * inverse, inverse


class Copies:
    def __init__(self, sems):
        self.sems, self.all, self.open = sems, [], []

    def start(self, src, dst):
        copy = pltpu.make_async_copy(src, dst, self.sems.at[len(self.all)])
        copy.start()
        self.all.append(copy)
        self.open.append(copy)
        return copy

    def wait(self, *copies):
        for copy in copies or list(self.open):
            copy.wait()
            self.open = [c for c in self.open if c is not copy]


def columns_of(ref, depth):
    half_rows = ref.shape[0] // 2

    def part(f, half):
        span = aligned(f * depth, depth)
        if half is None:
            return ref.at[:, span]
        return ref.at[pl.ds(half * half_rows, half_rows), span]

    return part


def rows_of(ref, chunk):
    return lambda s: ref.at[aligned(s * chunk, chunk)]


class Fold:
    def __init__(self, net, tile, total, mate_in, coming, mate_out, out, mate_send, mate_recv, send, recv):
        self.net, self.tile, self.total = net, tile, total
        self.mate_in, self.coming, self.mate_out, self.out = mate_in, coming, mate_out, out
        self.mate_send, self.mate_recv, self.send, self.recv = mate_send, mate_recv, send, recv
        self.chunk = total.shape[0]
        self.pieces = recv.shape[1]
        self.rows = self.chunk // self.pieces

    @staticmethod
    def shared(chunk, width):
        return [pltpu.VMEM((2 * chunk, TILE), F32), pltpu.VMEM((chunk, width), F32)]

    @staticmethod
    def buffers(n_s, chunk, width):
        n_l = n_s // 2
        return [
            pltpu.VMEM((n_l, chunk, width), BF),
            pltpu.VMEM((n_l + 1, chunk, width), BF),
            pltpu.VMEM((3, chunk, width), BF),
            pltpu.VMEM((n_l, chunk, width), BF),
        ]

    @staticmethod
    def sems(n_s, pieces=4):
        n_l = n_s // 2
        return [
            pltpu.SemaphoreType.DMA((3, pieces)),
            pltpu.SemaphoreType.DMA((n_l, pieces)),
            pltpu.SemaphoreType.DMA((n_l, pieces)),
            pltpu.SemaphoreType.DMA((n_l + 1, pieces)),
        ]

    def place(self, other):
        return (other >= 0) & (other < self.net.n_l)

    def fed(self, side):
        return self.place(self.net.z + 1 - 2 * side)

    def span(self, piece):
        return aligned(piece * self.rows, self.rows)

    def each_piece(self, act):
        pl.loop(0, self.pieces)(act)

    def to_mate(self, target, slot, piece):
        span = self.span(piece)
        return put(
            self.mate_out.at[slot, span],
            self.mate_in.at[target, span],
            self.mate_send.at[slot, piece],
            self.mate_recv.at[target, piece],
            seq=self.net.mate,
        )

    def onward(self, target, side, hop, piece):
        span = self.span(piece)
        slot = target + (self.net.n_l - target) * (1 - side) * (1 // hop)
        return put(
            self.out.at[target, span],
            self.coming.at[slot, span],
            self.send.at[target, piece],
            self.recv.at[slot, piece],
            seq=self.net.s + 4 * side - 2,
        )

    def came(self, slot, piece):
        place = self.coming.at[slot, self.span(piece)]
        put(place, place, self.send.at[0, 0], self.recv.at[slot, piece], seq=self.net.mate).wait_recv()

    def mate_sent(self, slot):
        self.each_piece(lambda piece: self.to_mate(self.net.z, slot, piece).wait_send())

    def begin_one(self, target, slot, produce):
        mine = aligned(self.net.c * self.chunk, self.chunk)
        theirs = aligned((1 - self.net.c) * self.chunk, self.chunk)

        def write(cols, value):
            self.tile[...] = value
            self.out[target, :, cols] = self.tile[mine, :].astype(BF)
            self.mate_out[slot, :, cols] = self.tile[theirs, :].astype(BF)

        produce(target, write)
        self.each_piece(lambda piece: self.to_mate(target, slot, piece).start())

    def leave(self, target, side, hop):
        @pl.when((hop > 0) & jnp.logical_not(self.fed(side)))
        def _():
            self.each_piece(lambda piece: self.pass_piece(target, side, hop, piece, False))

    def begin(self, produce, between=None, meanwhile=None):
        net = self.net

        @pl.loop(0, net.n_l)
        def _(j):
            hop = net.n_l - 1 - j

            @pl.loop(0, 2)
            def _(side):
                target = net.z + (2 * side - 1) * hop
                here = self.place(target) & ((hop > 0) | (side == 0))

                @pl.when(here)
                def _():
                    @pl.when((hop > 0) & self.place(target + 2 * side - 1))
                    def _():
                        self.mate_sent(side)

                    self.begin_one(target, side + (2 - side) * (1 // (hop + 1)), produce)

                if meanwhile is not None:
                    pl.when(hop > 0)(lambda: meanwhile(2 * j + side))

                pl.when(here)(lambda: self.leave(target, side, hop))

            if between is not None:
                pl.when(j == 1)(between)

    def pass_piece(self, target, side, hop, piece, fed):
        self.to_mate(target, 0, piece).wait_recv()
        span = self.span(piece)
        value = self.out[target, span, :].astype(F32) + self.mate_in[target, span, :].astype(F32)
        if fed:
            self.came(target, piece)
            value = value + self.coming[target, span, :].astype(F32)
        self.out[target, span, :] = value.astype(BF)
        self.onward(target, side, hop, piece).start()

    def open_total(self):
        net = self.net

        @self.each_piece
        def _(piece):
            self.to_mate(net.z, 0, piece).wait_recv()
            span = self.span(piece)
            self.total[span, :] = self.out[net.z, span, :].astype(F32) + self.mate_in[net.z, span, :].astype(F32)

    def wave(self, at, near=False, between=None):
        net = self.net
        above = at if near else net.n_l - at

        @pl.loop(0, 2)
        def _(turn):
            side = (1 - (2 * net.z) // net.n_l + turn) % 2
            target = net.n_l - 1 - above + (2 * above - net.n_l + 1) * side
            hop = (target - net.z) * (2 * side - 1)

            @self.each_piece
            def _(piece):
                span = self.span(piece)

                @pl.when(self.fed(side) & (hop > 0))
                def _():
                    self.pass_piece(target, side, hop, piece, True)

                @pl.when(self.fed(side) & (hop == 0))
                def _():
                    slot = net.z + (net.n_l - net.z) * (1 - side)
                    self.came(slot, piece)
                    self.total[span, :] = self.total[span, :] + self.coming[slot, span, :].astype(F32)

                if between is not None:
                    between(((at - 1) * 2 + turn) * self.pieces + piece)

    def passes_between(self, wave, near, between):
        net = self.net
        above = wave if near else net.n_l - wave

        @pl.loop(0, 2)
        def _(turn):
            side = (1 - (2 * net.z) // net.n_l + turn) % 2
            target = net.n_l - 1 - above + (2 * above - net.n_l + 1) * side
            hop = (target - net.z) * (2 * side - 1)

            @self.each_piece
            def _(piece):
                @pl.when((hop > 0) & self.fed(side))
                def _():
                    self.pass_piece(target, side, hop, piece, True)

                between(turn, piece)

    def finals(self):
        net = self.net

        @self.each_piece
        def _(piece):
            self.to_mate(net.z, 0, piece).wait_recv()
            span = self.span(piece)
            self.total[span, :] = self.out[net.z, span, :].astype(F32) + self.mate_in[net.z, span, :].astype(F32)

        @pl.loop(0, 2)
        def _(turn):
            side = (1 - (2 * net.z) // net.n_l + turn) % 2

            @pl.when(self.fed(side))
            def _():
                slot = net.z + (net.n_l - net.z) * (1 - side)

                @self.each_piece
                def _(piece):
                    span = self.span(piece)
                    self.came(slot, piece)
                    self.total[span, :] = self.total[span, :] + self.coming[slot, span, :].astype(F32)

    def finish(self):
        net = self.net
        self.mate_sent(2)
        for side in range(2):
            pl.when(self.place(net.z + 2 * side - 1))(functools.partial(self.mate_sent, side))

        @pl.loop(1, net.n_l)
        def _(hop):
            net.sides(
                hop,
                lambda target, side: self.each_piece(
                    lambda piece: self.onward(target, side, hop, piece).wait_send()
                ),
            )


class GridSum:
    def __init__(self, net, stage, came, sems):
        self.net, self.stage, self.came, self.sems = net, stage, came, sems
        self.half = stage.shape[1] // 2
        self.rows = next(r for r in (176, 128, 96, 64, 32, 16) if self.half % r == 0)
        self.cols = range(1, net.tall)
        self.along = range(1, net.wide)
        self.bases = self.layout(net.n_f)

    @staticmethod
    def layout(n_f):
        tall = 2 if n_f % 2 == 0 else 1
        wide = n_f // tall
        sizes = [(wide - 1) * tall, (tall - 1) * wide, tall - 1, wide - 1]
        return [sum(sizes[:at]) for at in range(5)]

    @staticmethod
    def scratch(n_f, rows, columns):
        count = GridSum.layout(n_f)[4]
        return [
            pltpu.VMEM((n_f, rows, columns), BF),
            pltpu.VMEM((count, rows // 2, columns), BF),
            pltpu.SemaphoreType.DMA((2, count + GridEnd.count(n_f))),
        ]

    def slot(self, kind, i, j):
        base = self.bases[kind]
        return base + [(j - 1) * self.net.tall + i, (i - 1) * self.net.wide + j, i - 1, j - 1][kind]

    def rank(self, i, j):
        net = self.net
        return ((net.a + i) % net.tall) * net.wide + (net.b + j) % net.wide

    def owner(self, at):
        return self.rank(at // self.net.wide, at % self.net.wide)

    def copy(self, kind, i, j):
        half = kind % 2
        along = kind in (0, 3)
        slot = self.slot(kind, i, j)
        at = i * self.net.wide + j
        return put(
            self.stage.at[at, pl.ds(half * self.half, self.half)],
            self.came.at[slot],
            self.sems.at[0, slot],
            self.sems.at[1, slot],
            fsdp=self.rank(0, j) if along else self.rank(i, 0),
        )

    def first(self, at):
        i, j = at // self.net.wide, at % self.net.wide

        @pl.when(j > 0)
        def _():
            self.copy(0, i, j).start()

        @pl.when(i > 0)
        def _():
            self.copy(1, i, j).start()

    def gather(self, half, at, slots, write):
        @pl.loop(0, self.half // self.rows)
        def _(step):
            span = aligned(half * self.half + step * self.rows, self.rows, 16)
            value = self.stage[at, span, :].astype(F32)
            for slot in slots:
                value = value + self.came[slot, aligned(step * self.rows, self.rows, 16), :].astype(F32)
            write(span, value)

    def wait(self, *copies):
        for kind, i, j in copies:
            self.copy(kind, i, j).wait_recv()
        return [self.slot(*copy) for copy in copies]

    def second(self):
        def keep(at):
            def write(span, value):
                self.stage[at, span, :] = value.astype(BF)

            return write

        for i in self.cols:
            at = i * self.net.wide
            self.gather(0, at, self.wait(*[(0, i, j) for j in self.along]), keep(at))
            self.copy(2, i, 0).start()
        for j in self.along:
            self.gather(1, j, self.wait(*[(1, i, j) for i in self.cols]), keep(j))
            self.copy(3, 0, j).start()

    def sum_first(self):
        def keep(at):
            def write(span, value):
                self.stage[at, span, :] = value.astype(BF)

            return write

        for i in range(self.net.tall):
            at = i * self.net.wide
            self.gather(0, at, self.wait(*[(0, i, j) for j in self.along]), keep(at))
        for j in range(self.net.wide):
            self.gather(1, j, self.wait(*[(1, i, j) for i in self.cols]), keep(j))

    def hand_on(self, out):
        net = self.net
        shards = [(0, 0), (0, 1), *[(i * net.wide, 0) for i in self.cols], *[(j, 1) for j in self.along]]
        return [
            pltpu.make_async_copy(
                self.stage.at[at, pl.ds(half * self.half, self.half)], out.at[k], self.sems.at[0, self.bases[4] + k]
            )
            for k, (at, half) in enumerate(shards)
        ]

    def last(self, out):
        def write(span, value):
            out[span, :] = value

        self.gather(
            0, 0, self.wait(*[(0, 0, j) for j in self.along], *[(2, i, 0) for i in self.cols]), write
        )
        self.gather(
            1, 0, self.wait(*[(1, i, 0) for i in self.cols], *[(3, 0, j) for j in self.along]), write
        )

    def finish_first(self):
        for i in range(self.net.tall):
            for j in range(self.net.wide):
                if j:
                    self.copy(0, i, j).wait_send()
                if i:
                    self.copy(1, i, j).wait_send()

    def finish(self):
        self.finish_first()
        for i in self.cols:
            self.copy(2, i, 0).wait_send()
        for j in self.along:
            self.copy(3, 0, j).wait_send()


class GridEnd:
    def __init__(self, net, sums, came, sems):
        self.net, self.sums, self.came, self.sems = net, sums, came, sems

    @staticmethod
    def count(n_f):
        tall = 2 if n_f % 2 == 0 else 1
        return tall + n_f // tall

    @staticmethod
    def scratch(n_f, rows, columns):
        count = GridEnd.count(n_f)
        return [
            pltpu.VMEM((count, rows // 2, columns), BF),
            pltpu.VMEM((count - 2, rows // 2, columns), BF),
            pltpu.SemaphoreType.DMA((2, count - 2)),
        ]

    def copies(self):
        net = self.net
        f = [((net.a + i) % net.tall) * net.wide + net.b for i in range(1, net.tall)]
        f += [net.a * net.wide + (net.b + j) % net.wide for j in range(1, net.wide)]
        return [
            put(self.sums.at[2 + k], self.came.at[k], self.sems.at[0, k], self.sems.at[1, k], fsdp=to)
            for k, to in enumerate(f)
        ]

    def start(self):
        for copy in self.copies():
            copy.start()

    def last(self, out):
        for copy in self.copies():
            copy.wait()
        half = self.sums.shape[1]
        rows = next(r for r in (176, 128, 96, 64, 32, 16) if half % r == 0)
        down = range(self.net.tall - 1)
        along = range(self.net.tall - 1, self.net.tall + self.net.wide - 2)
        for at, slots in enumerate((down, along)):

            @pl.loop(0, half // rows)
            def _(step):
                span = aligned(step * rows, rows, 16)
                value = self.sums[at, span, :].astype(F32)
                for slot in slots:
                    value = value + self.came[slot, span, :].astype(F32)
                out[aligned(at * half + step * rows, rows, 16), :] = value


class PacketSum:
    def __init__(self, net, out, seq_in, total, fsdp_in, sems):
        self.net, self.out, self.seq_in, self.total, self.fsdp_in, self.sems = net, out, seq_in, total, fsdp_in, sems

    @staticmethod
    def scratch(n_f, n_s):
        return [
            pltpu.VMEM((n_s, n_f, SMALL, 128), F32),
            pltpu.VMEM((n_s, n_f, SMALL, 128), F32),
            pltpu.VMEM((n_f, SMALL, 128), F32),
            pltpu.VMEM((n_f, SMALL, 128), F32),
            pltpu.SemaphoreType.DMA((2 * (n_f + n_s),)),
        ]

    def one(self, k):
        to = (self.net.s + k) % self.net.n_s
        return put(self.out.at[to], self.seq_in.at[k], self.sems.at[2 * k], self.sems.at[2 * k + 1], seq=to)

    def two(self, k):
        to = (self.net.f + k) % self.net.n_f
        at = 2 * (self.net.n_s + k)
        return put(self.total.at[to], self.fsdp_in.at[k], self.sems.at[at], self.sems.at[at + 1], fsdp=to)

    def start(self, terms, width):
        net = self.net
        per = 128 // width
        for tile in range(net.n_f * net.n_s // per):
            value = terms[:, tile * 128 : (tile + 1) * 128]
            for j in range(per):
                f, s = divmod(tile * per + j, net.n_s)
                self.out[s, f] = pltpu.roll(value, 128 - j * width, axis=1) if j else value
        for k in range(1, net.n_s):
            self.one(k).start()

    def middle(self):
        net = self.net
        total = self.out[net.s]
        for k in range(1, net.n_s):
            self.one(k).wait()
            total = total + self.seq_in[k]
        self.total[...] = total
        for k in range(1, net.n_f):
            self.two(k).start()

    def finish(self, result):
        net = self.net
        total = self.total[net.f]
        for k in range(1, net.n_f):
            self.two(k).wait()
            total = total + self.fsdp_in[k]
        result[...] = total


def norm_backward(rows, source, grad, gain, terms, at, write):
    terms[at : at + 2, :] = jnp.zeros((2, terms.shape[1]), F32)

    @pl.loop(0, rows // 32, unroll=2)
    def _(i):
        span = aligned(i * 32, 32)
        scaled, inverse = normalize(source[span, :].astype(F32))
        value = grad[span, :]
        upstream = value * gain
        inner = jnp.mean(upstream, -1, keepdims=True)
        cross = jnp.mean(upstream * scaled, -1, keepdims=True)
        terms[at : at + 1, :] = terms[at : at + 1, :] + jnp.sum(value * scaled, 0, keepdims=True)
        terms[at + 1 : at + 2, :] = terms[at + 1 : at + 2, :] + jnp.sum(value, 0, keepdims=True)
        write(i, span, inverse * (upstream - inner - scaled * cross))


def layer_kernel(
    tok,
    gain_one,
    shift_one,
    gain_two,
    shift_two,
    bias,
    wq_own,
    wo_own,
    wg_own,
    wu_own,
    wd_own,
    gout_own,
    cosine,
    sine,
    q_o,
    k_o,
    kt_o,
    v_o,
    att_o,
    att_t_o,
    lse_o,
    n1_o,
    gains_o,
    wq_o,
    wo_o,
    dm_o,
    datt_o,
    dmid_o,
    top_o,
    terms_o,
    gate_o,
    up_o,
    down_o,
    rows,
    gout,
    wq,
    wo,
    wg,
    wu,
    wd,
    q,
    k,
    kt,
    v,
    vt,
    ot,
    att,
    att_t,
    hidden,
    dgate,
    dup,
    mid,
    low,
    packet,
    packets,
    tiles,
    total,
    *rest,
):
    net = Net()
    chunk, width = tok.shape
    length = chunk * net.n_s
    depth = wq_own.shape[1]
    columns = wq_own.shape[2]
    heads = columns // HEAD
    pair = 2 * chunk
    buffers, rest = rest[:4], rest[4:]
    folds = []
    for _ in range(3):
        folds.append(Fold(net, tiles, total, *buffers, *rest[:4]))
        rest = rest[4:]
    att_fold, normed_fold, top_fold = folds
    line_sems = [rest[at : at + 3] for at in (0, 3, 6, 9)]
    rest = rest[12:]
    spread_sems, rest = rest[:5], rest[5:]
    gate_sum, up_sum, down_sum = [GridSum(net, *rest[at : at + 3]) for at in (0, 3, 6)]
    sums = (down_sum, gate_sum, up_sum)
    pk_sems, copy_sems, n1_sems, free_sem = rest[9:]
    copies = Copies(copy_sems)
    n1 = att_fold.mate_out

    packet[...] = jnp.zeros(packet.shape, F32)
    own = gain_one.shape[1]
    for at, part in enumerate((gain_one, shift_one, gain_two, shift_two)):
        packet[at : at + 1, 0:own] = part[...].astype(F32)
    packet[4:7, 0:own] = bias[...].astype(F32)
    def wq_part(f, half):
        if half is None:
            return wq.at[:, aligned(f * depth, depth), :]
        return wq.at[:, aligned(f * depth + half * (depth // 2), depth // 2), :]

    spread_q = Spread(net, wq_own, wq_part, spread_sems[0])
    spread_o, spread_g, spread_u, spread_d = [
        Spread(net, own, columns_of(full, depth), sems)
        for own, full, sems in zip((wo_own, wg_own, wu_own, wd_own), (wo, wg, wu, wd), spread_sems[1:])
    ]
    pk = Packets(net, packet, packets, pk_sems)
    line = Line(net, tok, rows_of(rows, chunk), *line_sems[0])
    gout_line = Line(net, gout_own, rows_of(gout, chunk), *line_sems[1])
    n2_line = Line(net, low, rows_of(rows, chunk), *line_sems[2])
    dm_line = Line(net, low, rows_of(rows, chunk), *line_sems[3])

    for ready in (line, spread_q, spread_o, spread_g, spread_u, spread_d, gout_line):
        ready.prepare()
    net.barrier()

    def pairs(which, hop):
        net.sides(hop, lambda other, side: which.pair(other))

    def blocks(hop, act):
        def once(other, side):
            @pl.when((hop > 0) | (side == 0))
            def _():
                act(other, side)

        net.sides(hop, once)

    pk.start()
    line.start()
    spread_q.start()
    pk.middle()
    pk.finish()
    pk.unpack(gains_o, width // (net.n_f * net.n_s))

    def project_block(other, side):
        span = aligned(other * pair, pair)
        gain, shift = gains_o[0:1, :], gains_o[1:2, :]

        for part in range(2):

            @pl.loop(0, chunk // 32, unroll=2)
            def _(i):
                at = aligned((2 * other + part) * chunk + i * 32, 32)
                scaled, _ = normalize(rows[at, :].astype(F32))
                n1[part, aligned(i * 32, 32), :] = (scaled * gain + shift).astype(BF)

        keeps = [
            pltpu.make_async_copy(
                n1.at[part], n1_o.at[aligned((2 * other + part) * chunk, chunk)], n1_sems.at[part]
            )
            for part in range(2)
        ]
        for copy in keeps:
            copy.start()
        left = n1[0:2].reshape(pair, width)
        cols = aligned(net.s * columns, columns)
        tables = cosine[span, :], sine[span, :]
        for kind in range(3):
            value = dot(left, wq[kind]) + gains_o[4 + kind : 5 + kind, cols]
            if kind == 0:
                q[span, :] = rotary(value, *tables).astype(BF)
            elif kind == 1:
                value = rotary(value, *tables).astype(BF)
                k[span, :] = value
                kt[...] = turned(value)
            else:
                value = value.astype(BF)
                v[...] = value
                vt[:, span] = turned(value)
        for copy in (
            pltpu.make_async_copy(kt, kt_o.at[:, span], n1_sems.at[2]),
            pltpu.make_async_copy(v, v_o.at[span], n1_sems.at[3]),
        ):
            copy.start()
            keeps.append(copy)
        for copy in keeps:
            copy.wait()

    line.here()
    for hop in range(1, net.n_l - 1):
        line.step(hop)
        if hop == 1:
            spread_q.relay()
        pairs(line, hop)
    spread_o.start()
    spread_q.finish()
    spread_g.start()
    pl.loop(0, net.n_l - 1)(lambda hop: blocks(hop, project_block))
    spread_o.relay()
    spread_u.start()
    line.step(net.n_l - 1)
    gout_line.start()
    pairs(line, net.n_l - 1)
    blocks(net.n_l - 1, project_block)
    q_copy = copies.start(q, q_o)
    for pair_of in ((wq, wq_o), (k, k_o)):
        copies.start(*pair_of)
    spread_o.finish()
    line.finish()

    def attend(i):
        lo, hi = i * pair, (i + 1) * pair

        @pl.loop(0, heads)
        def _(head):
            lane = lax.broadcasted_iota(jnp.int32, (1, columns), 1)
            here = jnp.where(lane // HEAD == head, HEAD**-0.5, 0.0).astype(BF)
            visible = lax.broadcasted_iota(jnp.int32, (pair, pair), 0) <= lax.broadcasted_iota(
                jnp.int32, (pair, pair), 1
            )
            head_rows = aligned(head * HEAD, HEAD)
            query = q[lo:hi, :] * here
            near = jnp.where(visible, dot_nt(k[lo:hi, :], query), NEG_LARGE)
            highest = jnp.max(near, 0, keepdims=True)
            if i:
                far = dot_nt(k[0:lo, :], query)
                highest = jnp.maximum(highest, jnp.max(far, 0, keepdims=True))
            near = jnp.exp(near - highest)
            sum_of = jnp.sum(near, 0, keepdims=True)
            out = dot(vt[head_rows, lo:hi], near.astype(BF))
            if i:
                far = jnp.exp(far - highest)
                sum_of = sum_of + jnp.sum(far, 0, keepdims=True)
                out = out + dot(vt[head_rows, 0:lo], far.astype(BF))
            ot[head_rows, :] = out / sum_of
            lse_o[pl.ds(head, 1), lo:hi] = highest + jnp.log(sum_of)

        att_t[:, lo:hi] = ot[...].astype(BF)
        att[lo:hi, :] = turned(att_t[:, lo:hi])

    def produce_attended(place, write):
        for i in range(net.n_l):
            pl.when(place == i)(functools.partial(attend, i))
        left = att[aligned(place * pair, pair), :]

        @pl.loop(0, width // TILE)
        def _(j):
            cols = aligned(j * TILE, TILE)
            write(cols, dot(left, wo[:, cols]))

    def relays():
        gout_line.step(1)
        spread_d.start()

    att_fold.begin(produce_attended, relays)
    copies.start(att, att_o)
    copies.start(att_t, att_t_o)
    copies.start(wo, wo_o)
    if net.n_l > 2:
        gout_line.step(2)
    att_fold.open_total()
    spread_g.relay()
    for at in range(1, net.n_l):
        if 2 < at + 1 < net.n_l:
            gout_line.step(at + 1)
        att_fold.wave(at)
        if at == 1:
            spread_u.relay()
        if at == min(2, net.n_l - 1):
            spread_d.relay()
    gain_two, shift_two = gains_o[2:3, :], gains_o[3:4, :]

    @pl.loop(0, chunk // 32, unroll=2)
    def _(i):
        span = aligned(i * 32, 32)
        value = rows[aligned(net.s * chunk + i * 32, 32), :].astype(F32) + total[span, :]
        mid[span, :] = value
        scaled, _ = normalize(value)
        low[span, :] = (scaled * gain_two + shift_two).astype(BF)

    n2_line.prepare()
    n2_line.start()
    att_fold.finish()
    gout_line.here()
    pl.loop(1, net.n_l)(lambda hop: pairs(gout_line, hop))

    def forward_block(other):
        span = aligned(other * pair, pair)
        right = rows[span, :]
        half = hidden.shape[0] // 2

        @pl.loop(0, 2)
        def _(part):
            units = aligned(part * half, half, 16)
            gate = dot_nt(wg[units, :], right)
            up = dot_nt(wu[units, :], right)
            back = dot_nt(wd[units, :], gout[span, :])
            sigma = jax.nn.sigmoid(gate)
            active = gate * sigma
            hidden[units, span] = (active * up).astype(BF)
            dgate[units, span] = (back * up * (sigma * (1.0 + gate * (1.0 - sigma)))).astype(BF)
            dup[units, span] = (back * active).astype(BF)

    def produce_normed(place, write):
        span = aligned(place * pair, pair)
        left, right = turned(dgate[:, span]), turned(dup[:, span])

        @pl.loop(0, width // TILE)
        def _(j):
            cols = aligned(j * TILE, TILE)
            write(cols, dot(left, wg[:, cols]) + dot(right, wu[:, cols]))

    def begin_normed(other, side, hop):
        @pl.when(hop > 1)
        def _():
            normed_fold.mate_sent(side)

        normed_fold.begin_one(other, side + (2 - side) * (1 // (hop + 1)), produce_normed)

    def forward_blocks(hop):
        def act(other, side):
            forward_block(other)

            @pl.when(jnp.logical_not(normed_fold.fed(side)))
            def _():
                begin_normed(other, side, hop)
                normed_fold.leave(other, side, hop)

        net.sides(hop, act)

    def begin_fed(hop):
        def act(other, side):
            pl.when(normed_fold.fed(side))(lambda: begin_normed(other, side, hop))

        net.sides(hop, act)

    n2_line.here()
    for spread in (spread_g, spread_u, spread_d):
        spread.finish()
    forward_block(net.z)

    @pl.loop(1, net.n_l)
    def _(hop):
        n2_line.step(hop)
        pairs(n2_line, hop)
        pl.when(hop == 1)(lambda: normed_fold.begin_one(net.z, 2, produce_normed))
        forward_blocks(hop)
        pl.when(hop > 1)(lambda: begin_fed(hop - 1))

    begin_fed(net.n_l - 1)

    def weight_terms(task):
        at, kind = net.n_f - 1 - task // 3, task % 3
        cols = aligned(gate_sum.owner(at) * depth, depth)
        for way, (grid_sum, left, right) in enumerate(
            ((down_sum, hidden, gout), (gate_sum, dgate, rows), (up_sum, dup, rows))
        ):

            @pl.when(kind == way)
            def _():
                half = left.shape[0] // 2

                @pl.loop(0, 2)
                def _(part):
                    units = aligned(part * half, half, 16)
                    grid_sum.stage[at, units, :] = dot(left[units, :], right[:, cols]).astype(BF)

                grid_sum.first(at)

    tasks = 3 * net.n_f
    waves = max(net.n_l - 2, 1)
    each = -(-tasks // (2 * normed_fold.pieces * waves))
    for wave in range(net.n_l - waves, net.n_l):

        def between(turn, piece):
            slot = ((wave - net.n_l + waves) * 2 + turn) * normed_fold.pieces + piece

            @pl.loop(0, each)
            def _(i):
                pl.when(slot * each + i < tasks)(lambda: weight_terms(slot * each + i))

        normed_fold.passes_between(wave, True, between)
    normed_fold.finals()
    n2_line.finish()

    def beside(act):
        act(net.mate)
        for side in range(2):
            pl.when(n2_line.goes_on(side))(lambda: act(net.s + 2 - 4 * side))

    beside(lambda to: pl.semaphore_signal(free_sem, 1, device_id={"seq": to}, device_id_type=MESH))

    def write_middle(i, span, value):
        value = value + gout[aligned(net.s * chunk + i * 32, 32), :].astype(F32)
        dmid_o[span, :] = value
        low[span, :] = value.astype(BF)

    terms_o[...] = jnp.zeros(terms_o.shape, F32)
    norm_backward(chunk, mid, total, gain_two, terms_o, 2, write_middle)
    ends = (net.z + net.n_l - 1) // net.n_l + (2 * net.n_l - 2 - net.z) // net.n_l
    pl.semaphore_wait(free_sem, 1 + ends)
    dm_line.prepare()
    dm_line.start()
    normed_fold.finish()

    def produce_top(place, write):
        left = turned(hidden[:, aligned(place * pair, pair)])

        @pl.loop(0, width // TILE)
        def _(j):
            cols = aligned(j * TILE, TILE)
            write(cols, dot(left, wd[:, cols]))

    copies.wait(q_copy)
    datt = q

    def back_block(other, side):
        span = aligned(other * pair, pair)
        datt[span, :] = dot_nt(rows[span, :], wo[...]).astype(BF)

    dm_line.here()
    dm_line.step(1)
    top_fold.begin(produce_top)
    back_block(net.z, 0)
    top_fold.open_total()
    for at in range(1, net.n_l):
        if at + 1 < net.n_l:
            dm_line.step(at + 1)
        top_fold.wave(at)
        pairs(dm_line, at)
        net.sides(at, back_block)
    copies.start(datt, datt_o)
    copies.start(rows, dm_o)

    @pl.loop(0, chunk // 32)
    def _(i):
        span = aligned(i * 32, 32)
        top_fold.out[net.z, span, :] = (mid[span, :] + total[span, :]).astype(BF)

    copies.start(top_fold.out.at[net.z], top_o)
    top_fold.finish()
    gout_line.finish()
    dm_line.finish()
    hands = []
    for grid_sum, out in zip(sums, (down_o, gate_o, up_o)):
        grid_sum.sum_first()
        hands.extend(grid_sum.hand_on(out))
        for copy in grid_sum.hand_on(out):
            copy.start()
    for grid_sum in sums:
        grid_sum.finish_first()
    for copy in hands:
        copy.wait()
    copies.wait()


def layer_part(tokens, norms, wq, wo, wg, wu, wd, gout, tables):
    chunk, width = tokens.shape
    n_f, n_s = lax.axis_size("fsdp"), lax.axis_size("seq")
    length = chunk * n_s
    depth, columns = wq.shape[1:]
    units = wg.shape[0]
    shape = jax.ShapeDtypeStruct
    wide, head, turned, weight = (length, width), (length, columns), (units, length), (units, width)
    return pl.pallas_call(
        layer_kernel,
        name="layer",
        out_shape=[
            shape(head, BF),
            shape(head, BF),
            shape((columns, length), BF),
            shape(head, BF),
            shape(head, BF),
            shape((columns, length), BF),
            shape((8, length), F32),
            shape(wide, BF),
            shape((SMALL, width), F32),
            shape((3, width, columns), BF),
            shape((columns, width), BF),
            shape(wide, BF),
            shape(head, BF),
            shape((chunk, width), F32),
            shape((chunk, width), BF),
            shape((SMALL, width), F32),
            *[shape((GridEnd.count(n_f), units // 2, depth), BF)] * 3,
        ],
        in_specs=[ANY, *[VMEM] * 5, *[ANY] * 6, VMEM, VMEM],
        out_specs=[*[ANY] * 6, VMEM, ANY, VMEM, *[ANY] * 4, VMEM, ANY, VMEM, *[ANY] * 3],
        scratch_shapes=[
            pltpu.VMEM(wide, BF),
            pltpu.VMEM(wide, BF),
            pltpu.VMEM((3, width, columns), BF),
            pltpu.VMEM((columns, width), BF),
            *[pltpu.VMEM(weight, BF)] * 3,
            pltpu.VMEM(head, BF),
            pltpu.VMEM(head, BF),
            pltpu.VMEM((columns, 2 * chunk), BF),
            pltpu.VMEM((2 * chunk, columns), BF),
            pltpu.VMEM((columns, length), BF),
            pltpu.VMEM((columns, 2 * chunk), F32),
            pltpu.VMEM(head, BF),
            pltpu.VMEM((columns, length), BF),
            *[pltpu.VMEM(turned, BF)] * 3,
            pltpu.VMEM((chunk, width), F32),
            pltpu.VMEM((chunk, width), BF),
            pltpu.VMEM((SMALL, 128), F32),
            pltpu.VMEM((n_s, n_f, SMALL, 128), F32),
            *Fold.shared(chunk, width),
            *Fold.buffers(n_s, chunk, width),
            *Fold.sems(n_s) * 3,
            *Line.sems(n_s) * 4,
            *[pltpu.SemaphoreType.DMA((Spread.count(n_f),))] * 5,
            *GridSum.scratch(n_f, units, depth) * 3,
            pltpu.SemaphoreType.DMA((Packets.count(n_f, n_s),)),
            pltpu.SemaphoreType.DMA((9,)),
            pltpu.SemaphoreType.DMA((4,)),
            pltpu.SemaphoreType.REGULAR,
        ],
        compiler_params=pltpu.CompilerParams(
            collective_id=1, has_side_effects=True, vmem_limit_bytes=VMEM_BYTES
        ),
        cost_estimate=pl.CostEstimate(
            flops=2 * length * width * (4 * columns + 9 * units),
            bytes_accessed=8 * length * width,
            transcendentals=length * (length * columns // HEAD + units),
        ),
    )(tokens, *norms, wq, wo, wg, wu, wd, gout, *tables)


def attend_back_kernel(
    datt, q, k, kt, v, att, lse, cosine, sine, dproj, dproj_t, bias, query, upstream, inners, dk, dv, dqt
):
    length, columns = q.shape
    heads = columns // HEAD
    block = 2 * 128

    @pl.loop(0, length // block)
    def _(i):
        span = aligned(i * block, block)
        dk[span, :] = jnp.zeros((block, columns), F32)
        dv[span, :] = jnp.zeros((block, columns), F32)

    of_head = (
        lax.broadcasted_iota(jnp.int32, (8, columns), 1) // HEAD
        == lax.broadcasted_iota(jnp.int32, (8, columns), 0)
    ).astype(F32)

    @pl.loop(0, length // block)
    def _(i):
        span = aligned(i * block, block)
        product = datt[span, :].astype(F32) * att[span, :].astype(F32)
        inners[:, span] = lax.dot_general(
            of_head,
            product,
            (((1,), (1,)), ((), ())),
            precision=lax.Precision.HIGHEST,
            preferred_element_type=F32,
        )

    @pl.loop(0, heads)
    def _(head):
        lane = lax.broadcasted_iota(jnp.int32, (1, columns), 1)
        here = jnp.where(lane // HEAD == head, 1.0, 0.0).astype(BF)
        scale = HEAD**-0.5
        visible = lax.broadcasted_iota(jnp.int32, (block, block), 0) <= lax.broadcasted_iota(
            jnp.int32, (block, block), 1
        )
        head_rows = aligned(head * HEAD, HEAD)

        @pl.loop(0, length // block)
        def _(i):
            span = aligned(i * block, block)
            query[span, :] = q[span, :] * (here * scale)
            upstream[span, :] = datt[span, :] * here

        for j in range(length // block):
            at, end = j * block, (j + 1) * block
            keys, values, turned = k[at:end, :], v[at:end, :], kt[head_rows, at:end]

            def part(lo, hi, near):
                probs = jnp.exp(dot_nt(keys, query[lo:hi, :]) - lse[pl.ds(head, 1), lo:hi])
                if near:
                    probs = jnp.where(visible, probs, 0.0)
                grads = dot_nt(values, upstream[lo:hi, :])
                scores = (probs * (grads - inners[pl.ds(head, 1), lo:hi])).astype(BF)
                out = dot(turned, scores)
                dqt[head_rows, lo:hi] = dqt[head_rows, lo:hi] + out if j else out
                return dot(probs.astype(BF), upstream[lo:hi, :]), dot(scores, query[lo:hi, :])

            value_grads, key_grads = part(at, end, True)
            if end < length:
                more_values, more_keys = part(end, length, False)
                value_grads, key_grads = value_grads + more_values, key_grads + more_keys
            dv[at:end, :] = dv[at:end, :] + value_grads
            dk[at:end, :] = dk[at:end, :] + key_grads

    bias[...] = jnp.zeros(bias.shape, F32)

    @pl.loop(0, length // block)
    def _(i):
        span = aligned(i * block, block)
        tables = cosine[span, :], -sine[span, :]
        parts = [
            rotary(turned((dqt[:, span] * HEAD**-0.5).astype(BF)).astype(F32), *tables).astype(BF),
            rotary(dk[span, :].astype(BF).astype(F32), *tables).astype(BF),
            dv[span, :].astype(BF),
        ]
        for kind in range(3):
            dproj[kind, span, :] = parts[kind]
            dproj_t[kind, :, span] = turned(parts[kind])
            row = slice(4 + kind, 5 + kind)
            bias[row, :] = bias[row, :] + jnp.sum(parts[kind].astype(F32), 0, keepdims=True)


def attend_back_part(datt, q, k, kt, v, att, lse, tables):
    length, columns = q.shape
    shape = jax.ShapeDtypeStruct
    head = pltpu.VMEM((length, columns), BF)
    return pl.pallas_call(
        attend_back_kernel,
        name="attend_back",
        out_shape=[shape((3, length, columns), BF), shape((3, columns, length), BF), shape((SMALL, columns), F32)],
        in_specs=[VMEM] * 9,
        out_specs=[VMEM] * 3,
        scratch_shapes=[
            head,
            head,
            pltpu.VMEM((8, length), F32),
            pltpu.VMEM((length, columns), F32),
            pltpu.VMEM((length, columns), F32),
            pltpu.VMEM((columns, length), F32),
        ],
        compiler_params=pltpu.CompilerParams(vmem_limit_bytes=VMEM_BYTES),
    )(datt, q, k, kt, v, att, lse, *tables)


def back_kernel(
    dproj_in,
    dproj_t_in,
    att_t_in,
    wq_in,
    n1_in,
    dm_in,
    down_in,
    gate_in,
    up_in,
    tok,
    dmid,
    gains,
    terms_in,
    bias,
    gin_o,
    small_o,
    out_o,
    qkv_o,
    down_o,
    gate_o,
    up_o,
    dproj,
    dproj_t,
    att_t,
    wq,
    n1,
    dm,
    terms,
    tiles,
    total,
    *rest,
):
    net = Net()
    chunk, width = tok.shape
    columns = dproj_in.shape[2]
    pair = 2 * chunk
    depth = width // net.n_f
    buffers, rest = rest[:4], rest[4:]
    fold_sems, rest = rest[:4], rest[4:]
    packet_scratch, rest = rest[:5], rest[5:]
    out_sum, qkv_sum = GridSum(net, *rest[:3]), GridSum(net, *rest[3:6])
    ends = [GridEnd(net, *rest[at : at + 3]) for at in (6, 9, 12)]
    copy_sems, column_sems = rest[15:]

    copies = Copies(copy_sems)
    loads = [
        copies.start(src, dst)
        for src, dst in (
            (dproj_in, dproj),
            (wq_in, wq),
            (dproj_t_in, dproj_t),
            (att_t_in, att_t),
            (down_in, ends[0].sums),
            (gate_in, ends[1].sums),
            (up_in, ends[2].sums),
        )
    ]

    def load(at, way):
        src, dst = ((n1_in, n1), (dm_in, dm))[way]
        cols = aligned(qkv_sum.owner(at) * depth, depth)
        return pltpu.make_async_copy(src.at[:, cols], dst.at[at % 2], column_sems.at[way, at % 2])

    for at in range(net.n_f - 1, max(net.n_f - 3, -1), -1):
        for way in range(2):
            load(at, way).start()

    bias_cols = aligned(net.s * columns, columns)
    terms[...] = terms_in[...]
    terms[4:7, bias_cols] = bias[4:7, :]
    net.barrier()
    def weight_terms(task):
        at = net.n_f - 1 - task // 2

        def loaded(way):
            load(at, way).wait()

        def next_load(way):
            pl.when(at >= 2)(lambda: load(at - 2, way).start())

        @pl.when(task % 2 == 0)
        def _():
            loaded(0)
            right = n1[at % 2]
            for kind in range(3):
                rows = slice(kind * columns, (kind + 1) * columns)
                qkv_sum.stage[at, rows, :] = dot(dproj_t[kind], right).astype(BF)
            next_load(0)
            qkv_sum.first(at)

        @pl.when(task % 2 == 1)
        def _():
            loaded(1)
            out_sum.stage[at] = dot(att_t[...], dm[at % 2]).astype(BF)
            next_load(1)
            out_sum.first(at)

    def produce(place, write):
        span = aligned(place * pair, pair)

        @pl.loop(0, width // TILE)
        def _(j):
            cols = aligned(j * TILE, TILE)
            value = dot_nt(dproj[0, span, :], wq[0, cols, :])
            for kind in range(1, 3):
                value = value + dot_nt(dproj[kind, span, :], wq[kind, cols, :])
            write(cols, value)

    fold = Fold(net, tiles, total, *buffers, *fold_sems)
    copies.wait(*loads[:4])
    tasks = 2 * net.n_f
    ahead = 2 * (net.n_l - 1)

    def meanwhile(task):
        pl.when(task < tasks)(lambda: weight_terms(task))

    fold.begin(produce, meanwhile=meanwhile)
    copies.wait()
    for end in ends:
        end.start()
    fold.open_total()
    waves = max(net.n_l - 2, 1)
    each = -(-max(tasks - ahead, 0) // (2 * fold.pieces * waves))

    def between(slot):
        @pl.loop(0, each)
        def _(i):
            task = ahead + slot * each + i
            pl.when(task < tasks)(lambda: weight_terms(task))

    for at in range(1, waves + 1):
        fold.wave(at, between=between)
    for at in range(waves + 1, net.n_l):
        fold.wave(at)

    def write_input(i, span, value):
        gin_o[span, :] = value + dmid[span, :]

    norm_backward(chunk, tok, total, gains[0:1, :], terms, 0, write_input)
    packet_sum = PacketSum(net, *packet_scratch)
    packet_sum.start(terms, width // (net.n_f * net.n_s))
    for grid_sum in (qkv_sum, out_sum):
        grid_sum.second()
    packet_sum.middle()
    for end, out in zip(ends, (down_o, gate_o, up_o)):
        end.last(out)
    packet_sum.finish(small_o)
    fold.finish()
    for grid_sum, out in ((qkv_sum, qkv_o), (out_sum, out_o)):
        grid_sum.last(out)
        grid_sum.finish()


def back_part(dproj, dproj_t, att_t, wq, n1, dm, down, gate, up, tokens, dmid, gains, terms, bias):
    chunk, width = tokens.shape
    n_f, n_s = lax.axis_size("fsdp"), lax.axis_size("seq")
    length, columns = dproj.shape[1:]
    depth = width // n_f
    units = 2 * gate.shape[1]
    shape = jax.ShapeDtypeStruct
    return pl.pallas_call(
        back_kernel,
        name="back",
        out_shape=[
            shape((chunk, width), F32),
            shape((SMALL, 128), F32),
            shape((columns, depth), F32),
            shape((3 * columns, depth), F32),
            *[shape((units, depth), F32)] * 3,
        ],
        in_specs=[ANY] * 9 + [VMEM] * 5,
        out_specs=[VMEM] * 7,
        scratch_shapes=[
            pltpu.VMEM((3, length, columns), BF),
            pltpu.VMEM((3, columns, length), BF),
            pltpu.VMEM((columns, length), BF),
            pltpu.VMEM((3, width, columns), BF),
            pltpu.VMEM((2, length, depth), BF),
            pltpu.VMEM((2, length, depth), BF),
            pltpu.VMEM((SMALL, width), F32),
            *Fold.shared(chunk, width),
            *Fold.buffers(n_s, chunk, width),
            *Fold.sems(n_s, 8),
            *PacketSum.scratch(n_f, n_s),
            *GridSum.scratch(n_f, columns, depth),
            *GridSum.scratch(n_f, 3 * columns, depth),
            *GridEnd.scratch(n_f, units, depth) * 3,
            pltpu.SemaphoreType.DMA((7,)),
            pltpu.SemaphoreType.DMA((2, 2)),
        ],
        compiler_params=pltpu.CompilerParams(
            collective_id=3, has_side_effects=True, vmem_limit_bytes=VMEM_BYTES
        ),
        cost_estimate=pl.CostEstimate(
            flops=2 * length * columns * (8 * width + 5 * length),
            bytes_accessed=4 * length * width,
            transcendentals=length * length * columns // HEAD,
        ),
    )(dproj, dproj_t, att_t, wq, n1, dm, down, gate, up, tokens, dmid, gains, terms, bias)


def outputs_kernel(small, *refs):
    sources, targets, parts = refs[:7], refs[7:14], refs[14:]
    own = parts[0].shape[1]
    for src, dst in zip(sources, targets):
        if src.shape == dst.shape:
            dst[...] = src[...]
        else:
            rows, columns = src.shape[0] // 3, src.shape[1]
            for kind in range(3):
                dst[kind * columns : (kind + 1) * columns, :] = src[kind * rows : (kind + 1) * rows, :].T
    for at in range(4):
        parts[at][...] = small[at : at + 1, 0:own]
    parts[4][...] = small[4:7, 0:own]


def outputs_part(small, own, *arrays):
    shape = jax.ShapeDtypeStruct
    return pl.pallas_call(
        outputs_kernel,
        name="outputs",
        out_shape=[shape((3 * v.shape[1], v.shape[0] // 3) if at == 2 else v.shape, v.dtype) for at, v in enumerate(arrays)]
        + [shape((1, own), F32)] * 4
        + [shape((3, own), F32)],
        in_specs=[VMEM] * 8,
        out_specs=[VMEM] * 12,
        compiler_params=pltpu.CompilerParams(vmem_limit_bytes=VMEM_BYTES),
    )(small, *arrays)


def per_device(
    tokens,
    gain_one,
    shift_one,
    w_qkv,
    b_qkv,
    w_out,
    gain_two,
    shift_two,
    w_gate,
    w_up,
    w_down,
    grad_output,
):
    length = tokens.shape[1] * lax.axis_size("seq")
    width = gain_one.shape[0]
    norms = [v[None] for v in (gain_one, shift_one, gain_two, shift_two)] + [b_qkv]
    tables = rotary_tables(length)
    q, k, kt, v, att, att_t, lse, n1, gains, wq, _, dm, datt, dmid, top, terms, gate, up, down = layer_part(
        tokens[0], norms, w_qkv.transpose(1, 0, 2), w_out, w_gate.T, w_up.T, w_down, grad_output[0], tables
    )
    dproj, dproj_t, bias = attend_back_part(datt, q, k, kt, v, att, lse, tables)
    grad_input, small, out, qkv, down, gate, up = back_part(
        dproj, dproj_t, att_t, wq, n1, dm, down, gate, up, tokens[0], dmid, gains, terms, bias
    )

    top, grad_input, qkv, out, gate, up, down, one, shift, two, shift_to, bias = outputs_part(
        small, width, top, grad_input, qkv, out, gate, up, down
    )
    return (
        top[None],
        grad_input[None],
        one[0],
        shift[0],
        qkv.reshape(3, -1, qkv.shape[1]).transpose(1, 0, 2),
        bias,
        out,
        two[0],
        shift_to[0],
        gate.T,
        up.T,
        down,
    )


def solution(mesh):
    whole = P(("fsdp", "seq"))
    rows = P("fsdp", "seq", None)
    inner = P("seq", "fsdp")
    outer = P("fsdp", "seq")
    heads = P("fsdp", None, "seq")
    bias = P(None, ("fsdp", "seq"))
    return jax.shard_map(
        per_device,
        mesh=mesh,
        in_specs=(rows, whole, whole, heads, bias, inner, whole, whole, outer, outer, inner, rows),
        out_specs=(rows, rows, whole, whole, heads, bias, inner, whole, whole, outer, outer, inner),
        check_vma=False,
    )
```

```python
import functools

import jax
import jax.numpy as jnp
import numpy as np
from jax import lax
from jax.experimental import pallas as pl
from jax.experimental.pallas import tpu as pltpu
from jax.sharding import PartitionSpec as P

HEAD = 64
ROT = 16
EPSILON = 1e-05
NEG_LARGE = -1e30
MESH = pl.DeviceIdType.MESH
ANY = pl.BlockSpec(memory_space=pl.ANY)
VMEM = pl.BlockSpec(memory_space=pltpu.VMEM)
BF = jnp.bfloat16
F32 = jnp.float32
VMEM_BYTES = 60 * 2**20
TILE = 512
SMALL = 8


def put(src, dst, send, recv, **device):
    return pltpu.make_async_remote_copy(
        src_ref=src, dst_ref=dst, send_sem=send, recv_sem=recv, device_id=device, device_id_type=MESH
    )


def dot(left, right):
    return jnp.dot(left, right, preferred_element_type=F32)


def dot_nt(left, right):
    return lax.dot_general(left, right, (((1,), (1,)), ((), ())), preferred_element_type=F32)


def dot_tn(left, right):
    return lax.dot_general(left, right, (((0,), (0,)), ((), ())), preferred_element_type=F32)


def turned(values):
    size = values.shape[1]
    same = lax.broadcasted_iota(jnp.int32, (size, size), 0) == lax.broadcasted_iota(
        jnp.int32, (size, size), 1
    )
    return dot_nt(jnp.where(same, 1.0, 0.0).astype(BF), values).astype(BF)


def aligned(start, size, unit=None):
    return pl.ds(pl.multiple_of(start, unit or size), size)


class Net:
    def __init__(self):
        self.n_f, self.n_s = lax.axis_size("fsdp"), lax.axis_size("seq")
        self.tall = 2 if self.n_f % 2 == 0 else 1
        self.wide = self.n_f // self.tall
        self.n_l = self.n_s // 2
        self.f, self.s = lax.axis_index("fsdp"), lax.axis_index("seq")
        self.a, self.b = self.f // self.wide, self.f % self.wide
        self.z, self.c = self.s // 2, self.s % 2
        self.mate = self.s + 1 - 2 * self.c

    def barrier(self):
        sem = pltpu.get_barrier_semaphore()
        for k in range(1, self.n_f):
            pl.semaphore_signal(
                sem, inc=1, device_id={"fsdp": (self.f + k) % self.n_f}, device_id_type=MESH
            )
        for k in range(1, self.n_s):
            pl.semaphore_signal(
                sem, inc=1, device_id={"seq": (self.s + k) % self.n_s}, device_id_type=MESH
            )
        pl.semaphore_wait(sem, self.n_f + self.n_s - 2)

    def sides(self, hop, act):
        @pl.loop(0, 2)
        def _(side):
            other = self.z + (2 * side - 1) * hop

            @pl.when((other >= 0) & (other < self.n_l))
            def _():
                act(other, side)


class Spread:
    def __init__(self, net, src, part, sems):
        self.net, self.src, self.part, self.sems = net, src, part, sems
        self.rows = [j for j in range(1, net.wide)]
        self.cols = [i for i in range(1, net.tall)]

    @staticmethod
    def count(n_f):
        tall = 2 if n_f % 2 == 0 else 1
        wide = n_f // tall
        return 1 + 2 * (wide - 1) + 2 * (tall - 1) + 4 * (wide - 1) * (tall - 1)

    def at(self, kind, i, j):
        w, t = len(self.rows), len(self.cols)
        base = {
            "own": 0,
            "row": 1,
            "col": 1 + 2 * w,
            "half0": 1 + 2 * w + 2 * t,
            "half1": 1 + 2 * w + 2 * t + 2 * w * t,
        }[kind]
        if kind == "own":
            return self.sems.at[0]
        k = j - 1 if kind == "row" else i - 1 if kind == "col" else (i - 1) * w + j - 1
        return self.sems.at[base + 2 * k], self.sems.at[base + 2 * k + 1]

    def rank(self, i, j):
        net = self.net
        return ((net.a + i) % net.tall) * net.wide + (net.b + j) % net.wide

    def back(self, i, j):
        net = self.net
        return ((net.a - i + net.tall) % net.tall) * net.wide + (net.b - j + net.wide) % net.wide

    def own(self):
        return pltpu.make_async_copy(self.src, self.part(self.net.f, None), self.at("own", 0, 0))

    def first(self, i, j):
        send, recv = self.at("row" if i == 0 else "col", i, j)
        place = self.part(self.net.f, None)
        return put(place, place, send, recv, fsdp=self.rank(i, j))

    def came(self, i, j):
        send, recv = self.at("row" if i == 0 else "col", i, j)
        place = self.part(self.back(i, j), None)
        return put(place, place, send, recv, fsdp=self.rank(i, j))

    def second(self, half, i, j, came=False):
        send, recv = self.at("half0" if half == 0 else "half1", i, j)
        origin = self.back(i, j) if came else self.back(0, j) if half == 0 else self.back(i, 0)
        place = self.part(origin, half)
        return put(place, place, send, recv, fsdp=self.rank(i, 0) if half == 0 else self.rank(0, j))

    def prepare(self):
        self.own().start()

    def start(self):
        self.own().wait()
        for i in self.cols:
            self.first(i, 0).start()
        for j in self.rows:
            self.first(0, j).start()

    def relay(self):
        for j in self.rows:
            self.came(0, j).wait_recv()
            for i in self.cols:
                self.second(0, i, j).start()
        for i in self.cols:
            self.came(i, 0).wait_recv()
            for j in self.rows:
                self.second(1, i, j).start()

    def finish(self):
        for j in self.rows:
            self.first(0, j).wait_send()
        for i in self.cols:
            self.first(i, 0).wait_send()
        for i in self.cols:
            for j in self.rows:
                for half in range(2):
                    self.second(half, i, j, came=True).wait_recv()
                    self.second(half, i, j).wait_send()


class Line:
    def __init__(self, net, src, part, recv, send, local):
        self.net, self.src, self.part, self.recv, self.send, self.local = net, src, part, recv, send, local
        self.pieces = recv.shape[1]
        self.rows = src.shape[0] // self.pieces

    @staticmethod
    def sems(n_s, pieces=2):
        return [
            pltpu.SemaphoreType.DMA((n_s, pieces)),
            pltpu.SemaphoreType.DMA((4, n_s // 2, pieces)),
            pltpu.SemaphoreType.DMA((1,)),
        ]

    def cut(self, ref, piece):
        return ref.at[aligned(piece * self.rows, self.rows)]

    def own(self):
        return pltpu.make_async_copy(self.src, self.part(self.net.s), self.local.at[0])

    def on_line(self, src, chunk, side, hop, piece):
        return put(
            self.cut(src, piece),
            self.cut(self.part(chunk), piece),
            self.send.at[side, hop, piece],
            self.recv.at[chunk, piece],
            seq=self.net.s + 2 - 4 * side,
        )

    def to_mate(self, src, chunk, side, hop, piece):
        return put(
            self.cut(src, piece),
            self.cut(self.part(chunk), piece),
            self.send.at[2 + side, hop, piece],
            self.recv.at[chunk, piece],
            seq=self.net.mate,
        )

    def goes_on(self, side):
        after = self.net.z + 1 - 2 * side
        return (after >= 0) & (after < self.net.n_l)

    def each_piece(self, act):
        pl.loop(0, self.pieces)(act)

    def prepare(self):
        self.own().start()

    def start(self):
        net = self.net
        self.own().wait()
        place = self.part(net.s)

        @self.each_piece
        def _(piece):
            for side in range(2):

                @pl.when(self.goes_on(side))
                def _():
                    self.on_line(place, net.s, side, 0, piece).start()

            self.to_mate(place, net.s, 0, 0, piece).start()

    def came(self, chunk, piece):
        place = self.cut(self.part(chunk), piece)
        put(place, place, self.send.at[0, 0, 0], self.recv.at[chunk, piece], seq=self.net.mate).wait_recv()

    def step(self, hop):
        net = self.net

        @self.each_piece
        def _(piece):
            def act(other, side):
                chunk = 2 * other + net.c
                self.came(chunk, piece)

                @pl.when(self.goes_on(side))
                def _():
                    self.on_line(self.part(chunk), chunk, side, hop, piece).start()

                self.to_mate(self.part(chunk), chunk, side, hop, piece).start()

            net.sides(hop, act)

    def pair(self, other):
        @self.each_piece
        def _(piece):
            self.came(2 * other + 1 - self.net.c, piece)

    def here(self):
        self.pair(self.net.z)

    def finish(self):
        net = self.net
        place = self.part(net.s)

        @self.each_piece
        def _(piece):
            for side in range(2):

                @pl.when(self.goes_on(side))
                def _():
                    self.on_line(place, net.s, side, 0, piece).wait_send()

            self.to_mate(place, net.s, 0, 0, piece).wait_send()

            @pl.loop(1, net.n_l)
            def _(hop):
                def act(other, side):
                    chunk = 2 * other + net.c

                    @pl.when(self.goes_on(side))
                    def _():
                        self.on_line(self.part(chunk), chunk, side, hop, piece).wait_send()

                    self.to_mate(self.part(chunk), chunk, side, hop, piece).wait_send()

                net.sides(hop, act)


class Packets:
    def __init__(self, net, src, buf, sems):
        self.net, self.src, self.buf, self.sems = net, src, buf, sems

    @staticmethod
    def count(n_f, n_s):
        return 1 + 2 * (n_f - 1) + 2 * (n_s - 1)

    def own(self):
        net = self.net
        return pltpu.make_async_copy(self.src, self.buf.at[net.s, net.f], self.sems.at[0])

    def one(self, k, came=False):
        net = self.net
        f = (net.f - k + net.n_f) % net.n_f if came else net.f
        place = self.buf.at[net.s, f]
        return put(
            place if came else self.src,
            place,
            self.sems.at[2 * k - 1],
            self.sems.at[2 * k],
            fsdp=(net.f + k) % net.n_f,
        )

    def two(self, k, came=False):
        net = self.net
        place = self.buf.at[(net.s - k + net.n_s) % net.n_s if came else net.s]
        at = 2 * (net.n_f - 1) + 2 * k - 1
        return put(place, place, self.sems.at[at], self.sems.at[at + 1], seq=(net.s + k) % net.n_s)

    def start(self):
        self.own().start()
        for k in range(1, self.net.n_f):
            self.one(k).start()

    def middle(self):
        self.own().wait()
        for k in range(1, self.net.n_f):
            self.one(k, came=True).wait_recv()
            self.one(k).wait_send()
        for k in range(1, self.net.n_s):
            self.two(k).start()

    def finish(self):
        for k in range(1, self.net.n_s):
            self.two(k, came=True).wait_recv()
            self.two(k).wait_send()

    def unpack(self, out, width):
        net = self.net
        per = 128 // width
        for tile in range(net.n_f * net.n_s // per):
            total = None
            for j in range(per):
                f, s = divmod(tile * per + j, net.n_s)
                piece = self.buf[s, f]
                if j:
                    piece = pltpu.roll(piece, j * width, axis=1)
                total = piece if total is None else total + piece
            out[:, tile * 128 : (tile + 1) * 128] = total


def rotary(values, cosine, sine):
    columns = values.shape[1]
    half = ROT // 2
    times = columns // 128

    def wide(table):
        return table if times == 1 else jnp.concatenate([table] * times, axis=1)

    lane = lax.broadcasted_iota(jnp.int32, values.shape, 1)
    other = jnp.where(
        lane % HEAD < half, pltpu.roll(values, columns - half, axis=1), pltpu.roll(values, half, axis=1)
    )
    return values * wide(cosine) + other * wide(sine)


def rotary_tables(length):
    half = ROT // 2
    freqs = np.float32(10000.0) ** (-np.arange(half, dtype=np.float32) * np.float32(2.0 / ROT))
    angles = np.arange(length, dtype=np.float32)[:, None] * freqs[None, :].astype(np.float32)
    cosine, sine = np.cos(angles), np.sin(angles)
    rest = np.zeros((length, HEAD - ROT), np.float32)
    keep = np.concatenate([cosine, cosine, rest + 1], 1)
    swap = np.concatenate([-sine, sine, rest], 1)
    return [np.tile(t, (1, 128 // HEAD)).astype(np.float32) for t in (keep, swap)]


def normalize(values):
    center = values - jnp.mean(values, -1, keepdims=True)
    inverse = lax.rsqrt(jnp.mean(center * center, -1, keepdims=True) + EPSILON)
    return center * inverse, inverse


class Copies:
    def __init__(self, sems):
        self.sems, self.all, self.open = sems, [], []

    def start(self, src, dst):
        copy = pltpu.make_async_copy(src, dst, self.sems.at[len(self.all)])
        copy.start()
        self.all.append(copy)
        self.open.append(copy)
        return copy

    def wait(self, *copies):
        for copy in copies or list(self.open):
            copy.wait()
            self.open = [c for c in self.open if c is not copy]


def columns_of(ref, depth):
    half_rows = ref.shape[0] // 2

    def part(f, half):
        span = aligned(f * depth, depth)
        if half is None:
            return ref.at[:, span]
        return ref.at[pl.ds(half * half_rows, half_rows), span]

    return part


def rows_of(ref, chunk):
    return lambda s: ref.at[aligned(s * chunk, chunk)]


class Fold:
    def __init__(self, net, tile, total, mate_in, coming, mate_out, out, mate_send, mate_recv, send, recv):
        self.net, self.tile, self.total = net, tile, total
        self.mate_in, self.coming, self.mate_out, self.out = mate_in, coming, mate_out, out
        self.mate_send, self.mate_recv, self.send, self.recv = mate_send, mate_recv, send, recv
        self.chunk = total.shape[0]
        self.pieces = recv.shape[1]
        self.rows = self.chunk // self.pieces

    @staticmethod
    def shared(chunk, width):
        return [pltpu.VMEM((2 * chunk, TILE), F32), pltpu.VMEM((chunk, width), F32)]

    @staticmethod
    def buffers(n_s, chunk, width):
        n_l = n_s // 2
        return [
            pltpu.VMEM((n_l, chunk, width), BF),
            pltpu.VMEM((n_l + 1, chunk, width), BF),
            pltpu.VMEM((3, chunk, width), BF),
            pltpu.VMEM((n_l, chunk, width), BF),
        ]

    @staticmethod
    def sems(n_s, pieces=4):
        n_l = n_s // 2
        return [
            pltpu.SemaphoreType.DMA((3, pieces)),
            pltpu.SemaphoreType.DMA((n_l, pieces)),
            pltpu.SemaphoreType.DMA((n_l, pieces)),
            pltpu.SemaphoreType.DMA((n_l + 1, pieces)),
        ]

    def place(self, other):
        return (other >= 0) & (other < self.net.n_l)

    def fed(self, side):
        return self.place(self.net.z + 1 - 2 * side)

    def span(self, piece):
        return aligned(piece * self.rows, self.rows)

    def each_piece(self, act):
        pl.loop(0, self.pieces)(act)

    def to_mate(self, target, slot, piece):
        span = self.span(piece)
        return put(
            self.mate_out.at[slot, span],
            self.mate_in.at[target, span],
            self.mate_send.at[slot, piece],
            self.mate_recv.at[target, piece],
            seq=self.net.mate,
        )

    def onward(self, target, side, hop, piece):
        span = self.span(piece)
        slot = target + (self.net.n_l - target) * (1 - side) * (1 // hop)
        return put(
            self.out.at[target, span],
            self.coming.at[slot, span],
            self.send.at[target, piece],
            self.recv.at[slot, piece],
            seq=self.net.s + 4 * side - 2,
        )

    def came(self, slot, piece):
        place = self.coming.at[slot, self.span(piece)]
        put(place, place, self.send.at[0, 0], self.recv.at[slot, piece], seq=self.net.mate).wait_recv()

    def mate_sent(self, slot):
        self.each_piece(lambda piece: self.to_mate(self.net.z, slot, piece).wait_send())

    def begin_one(self, target, slot, produce):
        mine = aligned(self.net.c * self.chunk, self.chunk)
        theirs = aligned((1 - self.net.c) * self.chunk, self.chunk)

        def write(cols, value):
            self.tile[...] = value
            self.out[target, :, cols] = self.tile[mine, :].astype(BF)
            self.mate_out[slot, :, cols] = self.tile[theirs, :].astype(BF)

        produce(target, write)
        self.each_piece(lambda piece: self.to_mate(target, slot, piece).start())

    def leave(self, target, side, hop):
        @pl.when((hop > 0) & jnp.logical_not(self.fed(side)))
        def _():
            self.each_piece(lambda piece: self.pass_piece(target, side, hop, piece, False))

    def begin(self, produce, between=None, meanwhile=None):
        net = self.net

        @pl.loop(0, net.n_l)
        def _(j):
            hop = net.n_l - 1 - j

            @pl.loop(0, 2)
            def _(side):
                target = net.z + (2 * side - 1) * hop
                here = self.place(target) & ((hop > 0) | (side == 0))

                @pl.when(here)
                def _():
                    @pl.when((hop > 0) & self.place(target + 2 * side - 1))
                    def _():
                        self.mate_sent(side)

                    self.begin_one(target, side + (2 - side) * (1 // (hop + 1)), produce)

                if meanwhile is not None:
                    pl.when(hop > 0)(lambda: meanwhile(2 * j + side))

                pl.when(here)(lambda: self.leave(target, side, hop))

            if between is not None:
                pl.when(j == 1)(between)

    def pass_piece(self, target, side, hop, piece, fed):
        self.to_mate(target, 0, piece).wait_recv()
        span = self.span(piece)
        value = self.out[target, span, :].astype(F32) + self.mate_in[target, span, :].astype(F32)
        if fed:
            self.came(target, piece)
            value = value + self.coming[target, span, :].astype(F32)
        self.out[target, span, :] = value.astype(BF)
        self.onward(target, side, hop, piece).start()

    def open_total(self):
        net = self.net

        @self.each_piece
        def _(piece):
            self.to_mate(net.z, 0, piece).wait_recv()
            span = self.span(piece)
            self.total[span, :] = self.out[net.z, span, :].astype(F32) + self.mate_in[net.z, span, :].astype(F32)

    def wave(self, at, near=False, between=None):
        net = self.net
        above = at if near else net.n_l - at

        @pl.loop(0, 2)
        def _(turn):
            side = (1 - (2 * net.z) // net.n_l + turn) % 2
            target = net.n_l - 1 - above + (2 * above - net.n_l + 1) * side
            hop = (target - net.z) * (2 * side - 1)

            @self.each_piece
            def _(piece):
                span = self.span(piece)

                @pl.when(self.fed(side) & (hop > 0))
                def _():
                    self.pass_piece(target, side, hop, piece, True)

                @pl.when(self.fed(side) & (hop == 0))
                def _():
                    slot = net.z + (net.n_l - net.z) * (1 - side)
                    self.came(slot, piece)
                    self.total[span, :] = self.total[span, :] + self.coming[slot, span, :].astype(F32)

                if between is not None:
                    between(((at - 1) * 2 + turn) * self.pieces + piece)

    def begin_at(self, place, produce, meanwhile):
        net = self.net
        side = (place - net.z + net.n_l - 1) // net.n_l
        here = 1 - side - (net.z - place + net.n_l - 1) // net.n_l
        hop = (place - net.z) * (2 * side - 1)
        first = (place == 0) | ((side == 1) & (hop == 1)) | (here == 1)
        pl.when(jnp.logical_not(first))(lambda: self.mate_sent(side))
        self.begin_one(place, side + (2 - side) * here, produce)
        meanwhile()
        self.leave(place, side, hop)

    def passes_rising(self, wave, between):
        net = self.net

        @pl.loop(0, 2)
        def _(turn):
            side = (1 - (2 * net.z) // net.n_l + turn) % 2
            target = wave - 1 + side
            hop = (target - net.z) * (2 * side - 1)

            @self.each_piece
            def _(piece):
                @pl.when((hop > 0) & self.fed(side))
                def _():
                    self.pass_piece(target, side, hop, piece, True)

                between(turn, piece)

    def passes_between(self, wave, near, between):
        net = self.net
        above = wave if near else net.n_l - wave

        @pl.loop(0, 2)
        def _(turn):
            side = (1 - (2 * net.z) // net.n_l + turn) % 2
            target = net.n_l - 1 - above + (2 * above - net.n_l + 1) * side
            hop = (target - net.z) * (2 * side - 1)

            @self.each_piece
            def _(piece):
                @pl.when((hop > 0) & self.fed(side))
                def _():
                    self.pass_piece(target, side, hop, piece, True)

                between(turn, piece)

    def finals(self):
        net = self.net

        @self.each_piece
        def _(piece):
            self.to_mate(net.z, 0, piece).wait_recv()
            span = self.span(piece)
            self.total[span, :] = self.out[net.z, span, :].astype(F32) + self.mate_in[net.z, span, :].astype(F32)

        @pl.loop(0, 2)
        def _(turn):
            side = (1 - (2 * net.z) // net.n_l + turn) % 2

            @pl.when(self.fed(side))
            def _():
                slot = net.z + (net.n_l - net.z) * (1 - side)

                @self.each_piece
                def _(piece):
                    span = self.span(piece)
                    self.came(slot, piece)
                    self.total[span, :] = self.total[span, :] + self.coming[slot, span, :].astype(F32)

    def finish(self):
        net = self.net
        self.mate_sent(2)
        for side in range(2):
            pl.when(self.place(net.z + 2 * side - 1))(functools.partial(self.mate_sent, side))

        @pl.loop(1, net.n_l)
        def _(hop):
            net.sides(
                hop,
                lambda target, side: self.each_piece(
                    lambda piece: self.onward(target, side, hop, piece).wait_send()
                ),
            )


class GridSum:
    def __init__(self, net, stage, came, sems):
        self.net, self.stage, self.came, self.sems = net, stage, came, sems
        self.half = stage.shape[1] // 2
        self.rows = next(r for r in (176, 128, 96, 64, 32, 16) if self.half % r == 0)
        self.cols = range(1, net.tall)
        self.along = range(1, net.wide)
        self.bases = self.layout(net.n_f)

    @staticmethod
    def layout(n_f):
        tall = 2 if n_f % 2 == 0 else 1
        wide = n_f // tall
        sizes = [(wide - 1) * tall, (tall - 1) * wide, tall - 1, wide - 1]
        return [sum(sizes[:at]) for at in range(5)]

    @staticmethod
    def scratch(n_f, rows, columns):
        count = GridSum.layout(n_f)[4]
        return [
            pltpu.VMEM((n_f, rows, columns), BF),
            pltpu.VMEM((count, rows // 2, columns), BF),
            pltpu.SemaphoreType.DMA((2, count + GridEnd.count(n_f))),
        ]

    def slot(self, kind, i, j):
        base = self.bases[kind]
        return base + [(j - 1) * self.net.tall + i, (i - 1) * self.net.wide + j, i - 1, j - 1][kind]

    def rank(self, i, j):
        net = self.net
        return ((net.a + i) % net.tall) * net.wide + (net.b + j) % net.wide

    def owner(self, at):
        return self.rank(at // self.net.wide, at % self.net.wide)

    def copy(self, kind, i, j):
        half = kind % 2
        along = kind in (0, 3)
        slot = self.slot(kind, i, j)
        at = i * self.net.wide + j
        return put(
            self.stage.at[at, pl.ds(half * self.half, self.half)],
            self.came.at[slot],
            self.sems.at[0, slot],
            self.sems.at[1, slot],
            fsdp=self.rank(0, j) if along else self.rank(i, 0),
        )

    def first(self, at):
        i, j = at // self.net.wide, at % self.net.wide

        @pl.when(j > 0)
        def _():
            self.copy(0, i, j).start()

        @pl.when(i > 0)
        def _():
            self.copy(1, i, j).start()

    def gather(self, half, at, slots, write):
        @pl.loop(0, self.half // self.rows)
        def _(step):
            span = aligned(half * self.half + step * self.rows, self.rows, 16)
            value = self.stage[at, span, :].astype(F32)
            for slot in slots:
                value = value + self.came[slot, aligned(step * self.rows, self.rows, 16), :].astype(F32)
            write(span, value)

    def wait(self, *copies):
        for kind, i, j in copies:
            self.copy(kind, i, j).wait_recv()
        return [self.slot(*copy) for copy in copies]

    def second(self):
        for i in self.cols:
            at = i * self.net.wide
            self.gather(0, at, self.wait(*[(0, i, j) for j in self.along]), self.keep(at))
            self.copy(2, i, 0).start()
        for j in self.along:
            self.gather(1, j, self.wait(*[(1, i, j) for i in self.cols]), self.keep(j))
            self.copy(3, 0, j).start()

    def keep(self, at):
        def write(span, value):
            self.stage[at, span, :] = value.astype(BF)

        return write

    def sum_first(self, own_only=False):
        for i in range(1 if own_only else self.net.tall):
            at = i * self.net.wide
            self.gather(0, at, self.wait(*[(0, i, j) for j in self.along]), self.keep(at))
        for j in range(1 if own_only else self.net.wide):
            self.gather(1, j, self.wait(*[(1, i, j) for i in self.cols]), self.keep(j))

    def hand_on(self, out, done=False):
        net = self.net
        shards = [(0, 0), (0, 1), *[(i * net.wide, 0) for i in self.cols], *[(j, 1) for j in self.along]]
        sources = [self.stage.at[at, pl.ds(half * self.half, self.half)] for at, half in shards]
        if done:
            came = self.wait(*[(2, i, 0) for i in self.cols], *[(3, 0, j) for j in self.along])
            sources[2:] = [self.came.at[slot] for slot in came]
        return [
            pltpu.make_async_copy(source, out.at[k], self.sems.at[0, self.bases[4] + k])
            for k, source in enumerate(sources)
        ]

    def last(self, out):
        def write(span, value):
            out[span, :] = value

        self.gather(
            0, 0, self.wait(*[(0, 0, j) for j in self.along], *[(2, i, 0) for i in self.cols]), write
        )
        self.gather(
            1, 0, self.wait(*[(1, i, 0) for i in self.cols], *[(3, 0, j) for j in self.along]), write
        )

    def finish_first(self):
        for i in range(self.net.tall):
            for j in range(self.net.wide):
                if j:
                    self.copy(0, i, j).wait_send()
                if i:
                    self.copy(1, i, j).wait_send()

    def finish(self):
        self.finish_first()
        for i in self.cols:
            self.copy(2, i, 0).wait_send()
        for j in self.along:
            self.copy(3, 0, j).wait_send()


class GridEnd:
    def __init__(self, net, sums, came=None, sems=None):
        self.net, self.sums, self.came, self.sems = net, sums, came, sems

    @staticmethod
    def count(n_f):
        tall = 2 if n_f % 2 == 0 else 1
        return tall + n_f // tall

    @staticmethod
    def scratch(n_f, rows, columns):
        count = GridEnd.count(n_f)
        sums = pltpu.VMEM((count, rows // 2, columns), BF)
        return [
            sums,
            sums,
            sums,
            pltpu.VMEM((count - 2, rows // 2, columns), BF),
            pltpu.SemaphoreType.DMA((2, count - 2)),
        ]

    def copies(self):
        net = self.net
        f = [((net.a + i) % net.tall) * net.wide + net.b for i in range(1, net.tall)]
        f += [net.a * net.wide + (net.b + j) % net.wide for j in range(1, net.wide)]
        return [
            put(self.sums.at[2 + k], self.came.at[k], self.sems.at[0, k], self.sems.at[1, k], fsdp=to)
            for k, to in enumerate(f)
        ]

    def start(self):
        for copy in self.copies():
            copy.start()

    def last(self, out):
        came, base = self.sums, 2
        if self.came is not None:
            came, base = self.came, 0
            for copy in self.copies():
                copy.wait()
        half = self.sums.shape[1]
        rows = next(r for r in (176, 128, 96, 64, 32, 16) if half % r == 0)
        down = range(self.net.tall - 1)
        along = range(self.net.tall - 1, self.net.tall + self.net.wide - 2)
        for at, slots in enumerate((down, along)):

            @pl.loop(0, half // rows)
            def _(step):
                span = aligned(step * rows, rows, 16)
                value = self.sums[at, span, :].astype(F32)
                for slot in slots:
                    value = value + came[base + slot, span, :].astype(F32)
                out[aligned(at * half + step * rows, rows, 16), :] = value


class PacketSum:
    def __init__(self, net, out, seq_in, total, fsdp_in, sems):
        self.net, self.out, self.seq_in, self.total, self.fsdp_in, self.sems = net, out, seq_in, total, fsdp_in, sems

    @staticmethod
    def scratch(n_f, n_s):
        return [
            pltpu.VMEM((n_s, n_f, SMALL, 128), F32),
            pltpu.VMEM((n_s, n_f, SMALL, 128), F32),
            pltpu.VMEM((n_f, SMALL, 128), F32),
            pltpu.VMEM((n_f, SMALL, 128), F32),
            pltpu.SemaphoreType.DMA((2 * (n_f + n_s),)),
        ]

    def one(self, k):
        to = (self.net.s + k) % self.net.n_s
        return put(self.out.at[to], self.seq_in.at[k], self.sems.at[2 * k], self.sems.at[2 * k + 1], seq=to)

    def two(self, k):
        to = (self.net.f + k) % self.net.n_f
        at = 2 * (self.net.n_s + k)
        return put(self.total.at[to], self.fsdp_in.at[k], self.sems.at[at], self.sems.at[at + 1], fsdp=to)

    def start(self, terms, width):
        net = self.net
        per = 128 // width
        for tile in range(net.n_f * net.n_s // per):
            value = terms[:, tile * 128 : (tile + 1) * 128]
            for j in range(per):
                f, s = divmod(tile * per + j, net.n_s)
                self.out[s, f] = pltpu.roll(value, 128 - j * width, axis=1) if j else value
        for k in range(1, net.n_s):
            self.one(k).start()

    def middle(self):
        net = self.net
        total = self.out[net.s]
        for k in range(1, net.n_s):
            self.one(k).wait()
            total = total + self.seq_in[k]
        self.total[...] = total
        for k in range(1, net.n_f):
            self.two(k).start()

    def finish(self, result):
        net = self.net
        total = self.total[net.f]
        for k in range(1, net.n_f):
            self.two(k).wait()
            total = total + self.fsdp_in[k]
        result[...] = total


def norm_backward(rows, source, grad, gain, terms, at, write):
    terms[at : at + 2, :] = jnp.zeros((2, terms.shape[1]), F32)

    @pl.loop(0, rows // 32, unroll=2)
    def _(i):
        span = aligned(i * 32, 32)
        scaled, inverse = normalize(source[span, :].astype(F32))
        value = grad[span, :]
        upstream = value * gain
        inner = jnp.mean(upstream, -1, keepdims=True)
        cross = jnp.mean(upstream * scaled, -1, keepdims=True)
        terms[at : at + 1, :] = terms[at : at + 1, :] + jnp.sum(value * scaled, 0, keepdims=True)
        terms[at + 1 : at + 2, :] = terms[at + 1 : at + 2, :] + jnp.sum(value, 0, keepdims=True)
        write(i, span, inverse * (upstream - inner - scaled * cross))


def layer_kernel(
    tok,
    gain_one,
    shift_one,
    gain_two,
    shift_two,
    bias,
    wq_own,
    wo_own,
    wg_own,
    wu_own,
    wd_own,
    gout_own,
    cosine,
    sine,
    q_o,
    k_o,
    kt_o,
    v_o,
    att_o,
    att_t_o,
    lse_o,
    n1_o,
    gains_o,
    wq_o,
    wo_o,
    dm_o,
    datt_o,
    dmid_o,
    top_o,
    terms_o,
    gate_o,
    up_o,
    down_o,
    rows,
    gout,
    wq,
    wo,
    wg,
    wu,
    wd,
    q,
    k,
    kt,
    v,
    vt,
    ot,
    att,
    att_t,
    hidden,
    dgate,
    dup,
    mid,
    low,
    packet,
    packets,
    tiles,
    total,
    *rest,
):
    net = Net()
    chunk, width = tok.shape
    length = chunk * net.n_s
    depth = wq_own.shape[1]
    columns = wq_own.shape[2]
    heads = columns // HEAD
    pair = 2 * chunk
    buffers, rest = rest[:4], rest[4:]
    folds = []
    for _ in range(3):
        folds.append(Fold(net, tiles, total, *buffers, *rest[:4]))
        rest = rest[4:]
    att_fold, normed_fold, top_fold = folds
    line_sems = [rest[at : at + 3] for at in (0, 3, 6, 9)]
    rest = rest[12:]
    spread_sems, rest = rest[:5], rest[5:]
    gate_sum, up_sum, down_sum = [GridSum(net, *rest[at : at + 3]) for at in (0, 3, 6)]
    sums = (down_sum, gate_sum, up_sum)
    pk_sems, copy_sems, n1_sems, free_sem = rest[9:]
    copies = Copies(copy_sems)
    n1 = att_fold.mate_out

    packet[...] = jnp.zeros(packet.shape, F32)
    own = gain_one.shape[1]
    for at, part in enumerate((gain_one, shift_one, gain_two, shift_two)):
        packet[at : at + 1, 0:own] = part[...].astype(F32)
    packet[4:7, 0:own] = bias[...].astype(F32)
    def wq_part(f, half):
        if half is None:
            return wq.at[:, aligned(f * depth, depth), :]
        return wq.at[:, aligned(f * depth + half * (depth // 2), depth // 2), :]

    spread_q = Spread(net, wq_own, wq_part, spread_sems[0])
    spread_o, spread_g, spread_u, spread_d = [
        Spread(net, own, columns_of(full, depth), sems)
        for own, full, sems in zip((wo_own, wg_own, wu_own, wd_own), (wo, wg, wu, wd), spread_sems[1:])
    ]
    pk = Packets(net, packet, packets, pk_sems)
    line = Line(net, tok, rows_of(rows, chunk), *line_sems[0])
    gout_line = Line(net, gout_own, rows_of(gout, chunk), *line_sems[1])
    n2_line = Line(net, low, rows_of(rows, chunk), *line_sems[2])
    dm_line = Line(net, low, rows_of(rows, chunk), *line_sems[3])

    for ready in (line, spread_q, spread_o, spread_g, spread_u, spread_d, gout_line):
        ready.prepare()
    net.barrier()

    def pairs(which, hop):
        net.sides(hop, lambda other, side: which.pair(other))

    def blocks(hop, act):
        def once(other, side):
            @pl.when((hop > 0) | (side == 0))
            def _():
                act(other, side)

        net.sides(hop, once)

    pk.start()
    line.start()
    spread_q.start()
    pk.middle()
    pk.finish()
    pk.unpack(gains_o, width // (net.n_f * net.n_s))

    def project_block(other, side):
        span = aligned(other * pair, pair)
        gain, shift = gains_o[0:1, :], gains_o[1:2, :]

        for part in range(2):

            @pl.loop(0, chunk // 32, unroll=2)
            def _(i):
                at = aligned((2 * other + part) * chunk + i * 32, 32)
                scaled, _ = normalize(rows[at, :].astype(F32))
                n1[part, aligned(i * 32, 32), :] = (scaled * gain + shift).astype(BF)

        keeps = [
            pltpu.make_async_copy(
                n1.at[part], n1_o.at[aligned((2 * other + part) * chunk, chunk)], n1_sems.at[part]
            )
            for part in range(2)
        ]
        for copy in keeps:
            copy.start()
        left = n1[0:2].reshape(pair, width)
        cols = aligned(net.s * columns, columns)
        tables = cosine[span, :], sine[span, :]
        for kind in range(3):
            value = dot(left, wq[kind]) + gains_o[4 + kind : 5 + kind, cols]
            if kind == 0:
                q[span, :] = rotary(value, *tables).astype(BF)
            elif kind == 1:
                value = rotary(value, *tables).astype(BF)
                k[span, :] = value
                kt[...] = turned(value)
            else:
                value = value.astype(BF)
                v[...] = value
                vt[:, span] = turned(value)
        for copy in (
            pltpu.make_async_copy(kt, kt_o.at[:, span], n1_sems.at[2]),
            pltpu.make_async_copy(v, v_o.at[span], n1_sems.at[3]),
        ):
            copy.start()
            keeps.append(copy)
        for copy in keeps:
            copy.wait()

    line.here()
    for hop in range(1, net.n_l - 1):
        line.step(hop)
        if hop == 1:
            spread_q.relay()
        pairs(line, hop)
    spread_o.start()
    spread_q.finish()
    spread_g.start()
    pl.loop(0, net.n_l - 1)(lambda hop: blocks(hop, project_block))
    spread_o.relay()
    spread_u.start()
    line.step(net.n_l - 1)
    gout_line.start()
    pairs(line, net.n_l - 1)
    blocks(net.n_l - 1, project_block)
    q_copy = copies.start(q, q_o)
    for pair_of in ((wq, wq_o), (k, k_o)):
        copies.start(*pair_of)
    spread_o.finish()
    line.finish()

    def attend(i):
        lo, hi = i * pair, (i + 1) * pair

        @pl.loop(0, heads)
        def _(head):
            lane = lax.broadcasted_iota(jnp.int32, (1, columns), 1)
            here = jnp.where(lane // HEAD == head, HEAD**-0.5, 0.0).astype(BF)
            visible = lax.broadcasted_iota(jnp.int32, (pair, pair), 0) <= lax.broadcasted_iota(
                jnp.int32, (pair, pair), 1
            )
            head_rows = aligned(head * HEAD, HEAD)
            query = q[lo:hi, :] * here
            near = jnp.where(visible, dot_nt(k[lo:hi, :], query), NEG_LARGE)
            highest = jnp.max(near, 0, keepdims=True)
            if i:
                far = dot_nt(k[0:lo, :], query)
                highest = jnp.maximum(highest, jnp.max(far, 0, keepdims=True))
            near = jnp.exp(near - highest)
            sum_of = jnp.sum(near, 0, keepdims=True)
            out = dot(vt[head_rows, lo:hi], near.astype(BF))
            if i:
                far = jnp.exp(far - highest)
                sum_of = sum_of + jnp.sum(far, 0, keepdims=True)
                out = out + dot(vt[head_rows, 0:lo], far.astype(BF))
            ot[head_rows, :] = out / sum_of
            lse_o[pl.ds(head, 1), lo:hi] = highest + jnp.log(sum_of)

        att_t[:, lo:hi] = ot[...].astype(BF)
        att[lo:hi, :] = turned(att_t[:, lo:hi])

    def produce_attended(place, write):
        for i in range(net.n_l):
            pl.when(place == i)(functools.partial(attend, i))
        left = att[aligned(place * pair, pair), :]

        @pl.loop(0, width // TILE)
        def _(j):
            cols = aligned(j * TILE, TILE)
            write(cols, dot(left, wo[:, cols]))

    def relays():
        gout_line.step(1)
        spread_d.start()

    att_fold.begin(produce_attended, relays)
    copies.start(att, att_o)
    copies.start(att_t, att_t_o)
    copies.start(wo, wo_o)
    if net.n_l > 2:
        gout_line.step(2)
    att_fold.open_total()
    spread_g.relay()
    for at in range(1, net.n_l):
        if 2 < at + 1 < net.n_l:
            gout_line.step(at + 1)
        att_fold.wave(at)
        if at == 1:
            spread_u.relay()
        if at == min(2, net.n_l - 1):
            spread_d.relay()
    gain_two, shift_two = gains_o[2:3, :], gains_o[3:4, :]

    @pl.loop(0, chunk // 32, unroll=2)
    def _(i):
        span = aligned(i * 32, 32)
        value = rows[aligned(net.s * chunk + i * 32, 32), :].astype(F32) + total[span, :]
        mid[span, :] = value
        scaled, _ = normalize(value)
        low[span, :] = (scaled * gain_two + shift_two).astype(BF)

    n2_line.prepare()
    n2_line.start()
    att_fold.finish()
    gout_line.here()
    pl.loop(1, net.n_l)(lambda hop: pairs(gout_line, hop))

    def forward_block(other):
        span = aligned(other * pair, pair)
        right = rows[span, :]
        half = hidden.shape[0] // 2

        @pl.loop(0, 2)
        def _(part):
            units = aligned(part * half, half, 16)
            gate = dot_nt(wg[units, :], right)
            up = dot_nt(wu[units, :], right)
            back = dot_nt(wd[units, :], gout[span, :])
            sigma = jax.nn.sigmoid(gate)
            active = gate * sigma
            hidden[units, span] = (active * up).astype(BF)
            dgate[units, span] = (back * up * (sigma * (1.0 + gate * (1.0 - sigma)))).astype(BF)
            dup[units, span] = (back * active).astype(BF)

    def produce_normed(place, write):
        span = aligned(place * pair, pair)
        left, right = turned(dgate[:, span]), turned(dup[:, span])

        @pl.loop(0, width // TILE)
        def _(j):
            cols = aligned(j * TILE, TILE)
            write(cols, dot(left, wg[:, cols]) + dot(right, wu[:, cols]))

    def begin_normed(other, side, hop):
        @pl.when(hop > 1)
        def _():
            normed_fold.mate_sent(side)

        normed_fold.begin_one(other, side + (2 - side) * (1 // (hop + 1)), produce_normed)

    def forward_blocks(hop):
        def act(other, side):
            forward_block(other)

            @pl.when(jnp.logical_not(normed_fold.fed(side)))
            def _():
                begin_normed(other, side, hop)
                normed_fold.leave(other, side, hop)

        net.sides(hop, act)

    def begin_fed(hop):
        def act(other, side):
            pl.when(normed_fold.fed(side))(lambda: begin_normed(other, side, hop))

        net.sides(hop, act)

    n2_line.here()
    for spread in (spread_g, spread_u, spread_d):
        spread.finish()
    forward_block(net.z)

    @pl.loop(1, net.n_l)
    def _(hop):
        n2_line.step(hop)
        pairs(n2_line, hop)
        pl.when(hop == 1)(lambda: normed_fold.begin_one(net.z, 2, produce_normed))
        forward_blocks(hop)
        pl.when(hop > 1)(lambda: begin_fed(hop - 1))

    begin_fed(net.n_l - 1)

    def weight_terms(task):
        at, kind = net.n_f - 1 - task // 3, task % 3
        cols = aligned(gate_sum.owner(at) * depth, depth)
        for way, (grid_sum, left, right) in enumerate(
            ((down_sum, hidden, gout), (gate_sum, dgate, rows), (up_sum, dup, rows))
        ):

            @pl.when(kind == way)
            def _():
                half = left.shape[0] // 2

                @pl.loop(0, 2)
                def _(part):
                    units = aligned(part * half, half, 16)
                    grid_sum.stage[at, units, :] = dot(left[units, :], right[:, cols]).astype(BF)

                grid_sum.first(at)

    tasks = 3 * net.n_f
    waves = max(net.n_l - 2, 1)
    each = -(-tasks // (2 * normed_fold.pieces * waves))
    for wave in range(net.n_l - waves, net.n_l):

        def between(turn, piece):
            slot = ((wave - net.n_l + waves) * 2 + turn) * normed_fold.pieces + piece

            @pl.loop(0, each)
            def _(i):
                pl.when(slot * each + i < tasks)(lambda: weight_terms(slot * each + i))

        normed_fold.passes_between(wave, True, between)
    normed_fold.finals()
    n2_line.finish()

    def beside(act):
        act(net.mate)
        for side in range(2):
            pl.when(n2_line.goes_on(side))(lambda: act(net.s + 2 - 4 * side))

    beside(lambda to: pl.semaphore_signal(free_sem, 1, device_id={"seq": to}, device_id_type=MESH))

    def write_middle(i, span, value):
        value = value + gout[aligned(net.s * chunk + i * 32, 32), :].astype(F32)
        dmid_o[span, :] = value
        low[span, :] = value.astype(BF)

    terms_o[...] = jnp.zeros(terms_o.shape, F32)
    norm_backward(chunk, mid, total, gain_two, terms_o, 2, write_middle)
    ends = (net.z + net.n_l - 1) // net.n_l + (2 * net.n_l - 2 - net.z) // net.n_l
    pl.semaphore_wait(free_sem, 1 + ends)
    dm_line.prepare()
    dm_line.start()
    normed_fold.finish()

    def produce_top(place, write):
        left = turned(hidden[:, aligned(place * pair, pair)])

        @pl.loop(0, width // TILE)
        def _(j):
            cols = aligned(j * TILE, TILE)
            write(cols, dot(left, wd[:, cols]))

    copies.wait(q_copy)
    datt = q

    def back_block(other, side):
        span = aligned(other * pair, pair)
        datt[span, :] = dot_nt(rows[span, :], wo[...]).astype(BF)

    dm_line.here()
    dm_line.step(1)
    top_fold.begin(produce_top)
    back_block(net.z, 0)
    top_fold.open_total()
    for at in range(1, net.n_l):
        if at + 1 < net.n_l:
            dm_line.step(at + 1)
        top_fold.wave(at)
        if at == max(net.n_l - 2, 1):
            for grid_sum in sums[:2]:
                grid_sum.second()
        pairs(dm_line, at)
        net.sides(at, back_block)
    copies.start(datt, datt_o)
    copies.start(rows, dm_o)

    @pl.loop(0, chunk // 32)
    def _(i):
        span = aligned(i * 32, 32)
        top_fold.out[net.z, span, :] = (mid[span, :] + total[span, :]).astype(BF)

    copies.start(top_fold.out.at[net.z], top_o)
    top_fold.finish()
    gout_line.finish()
    dm_line.finish()
    hands = []
    for grid_sum, out in zip(sums, (down_o, gate_o, up_o)):
        grid_sum.sum_first(grid_sum in sums[:2])
        hands.extend(grid_sum.hand_on(out, grid_sum in sums[:2]))
        for copy in hands[-GridEnd.count(net.n_f) :]:
            copy.start()
    for grid_sum in sums[:2]:
        grid_sum.finish()
    sums[2].finish_first()
    for copy in hands:
        copy.wait()
    copies.wait()


def layer_part(tokens, norms, wq, wo, wg, wu, wd, gout, tables):
    chunk, width = tokens.shape
    n_f, n_s = lax.axis_size("fsdp"), lax.axis_size("seq")
    length = chunk * n_s
    depth, columns = wq.shape[1:]
    units = wg.shape[0]
    shape = jax.ShapeDtypeStruct
    wide, head, turned, weight = (length, width), (length, columns), (units, length), (units, width)
    return pl.pallas_call(
        layer_kernel,
        name="layer",
        out_shape=[
            shape(head, BF),
            shape(head, BF),
            shape((columns, length), BF),
            shape(head, BF),
            shape(head, BF),
            shape((columns, length), BF),
            shape((8, length), F32),
            shape(wide, BF),
            shape((SMALL, width), F32),
            shape((3, width, columns), BF),
            shape((columns, width), BF),
            shape(wide, BF),
            shape(head, BF),
            shape((chunk, width), F32),
            shape((chunk, width), BF),
            shape((SMALL, width), F32),
            *[shape((GridEnd.count(n_f), units // 2, depth), BF)] * 3,
        ],
        in_specs=[ANY, *[VMEM] * 5, *[ANY] * 6, VMEM, VMEM],
        out_specs=[*[ANY] * 6, VMEM, ANY, VMEM, *[ANY] * 4, VMEM, ANY, VMEM, *[ANY] * 3],
        scratch_shapes=[
            pltpu.VMEM(wide, BF),
            pltpu.VMEM(wide, BF),
            pltpu.VMEM((3, width, columns), BF),
            pltpu.VMEM((columns, width), BF),
            *[pltpu.VMEM(weight, BF)] * 3,
            pltpu.VMEM(head, BF),
            pltpu.VMEM(head, BF),
            pltpu.VMEM((columns, 2 * chunk), BF),
            pltpu.VMEM((2 * chunk, columns), BF),
            pltpu.VMEM((columns, length), BF),
            pltpu.VMEM((columns, 2 * chunk), F32),
            pltpu.VMEM(head, BF),
            pltpu.VMEM((columns, length), BF),
            *[pltpu.VMEM(turned, BF)] * 3,
            pltpu.VMEM((chunk, width), F32),
            pltpu.VMEM((chunk, width), BF),
            pltpu.VMEM((SMALL, 128), F32),
            pltpu.VMEM((n_s, n_f, SMALL, 128), F32),
            *Fold.shared(chunk, width),
            *Fold.buffers(n_s, chunk, width),
            *Fold.sems(n_s) * 3,
            *Line.sems(n_s) * 4,
            *[pltpu.SemaphoreType.DMA((Spread.count(n_f),))] * 5,
            *GridSum.scratch(n_f, units, depth) * 3,
            pltpu.SemaphoreType.DMA((Packets.count(n_f, n_s),)),
            pltpu.SemaphoreType.DMA((9,)),
            pltpu.SemaphoreType.DMA((4,)),
            pltpu.SemaphoreType.REGULAR,
        ],
        compiler_params=pltpu.CompilerParams(
            collective_id=1, has_side_effects=True, vmem_limit_bytes=VMEM_BYTES
        ),
        cost_estimate=pl.CostEstimate(
            flops=2 * length * width * (4 * columns + 9 * units),
            bytes_accessed=8 * length * width,
            transcendentals=length * (length * columns // HEAD + units),
        ),
    )(tokens, *norms, wq, wo, wg, wu, wd, gout, *tables)


def back_kernel(
    datt_in,
    q_in,
    k_in,
    kt_in,
    v_in,
    att_in,
    att_t_in,
    wq_in,
    n1_in,
    dm_in,
    down_in,
    gate_in,
    up_in,
    lse,
    tok,
    dmid,
    gains,
    terms_in,
    cosine,
    sine,
    gin_o,
    small_o,
    out_o,
    qkv_o,
    down_o,
    gate_o,
    up_o,
    datt,
    q,
    k,
    kt,
    v,
    att,
    att_t,
    wq,
    n1,
    dm,
    query,
    upstream,
    inners,
    dk,
    dv,
    dqt,
    dproj,
    dproj_t,
    terms,
    tiles,
    total,
    *rest,
):
    net = Net()
    chunk, width = tok.shape
    length, columns = q_in.shape
    heads = columns // HEAD
    pair = 2 * chunk
    depth = width // net.n_f
    block = 256
    buffers, rest = rest[:4], rest[4:]
    fold_sems, rest = rest[:4], rest[4:]
    packet_scratch, rest = rest[:5], rest[5:]
    out_sum, qkv_sum = GridSum(net, *rest[:3]), GridSum(net, *rest[3:6])
    ends = [GridEnd(net, rest[6]), GridEnd(net, rest[7]), GridEnd(net, *rest[8:11])]
    copy_sems, column_sems = rest[11:]

    copies = Copies(copy_sems)
    loads = [
        copies.start(src, dst)
        for src, dst in (
            (datt_in, datt),
            (q_in, q),
            (k_in, k),
            (kt_in, kt),
            (v_in, v),
            (att_in, att),
            (att_t_in, att_t),
            (wq_in, wq),
            (down_in, ends[0].sums),
            (gate_in, ends[1].sums),
            (up_in, ends[2].sums),
        )
    ]
    def load(at, way):
        src, dst = ((n1_in, n1), (dm_in, dm))[way]
        cols = aligned(qkv_sum.owner(at) * depth, depth)
        return pltpu.make_async_copy(src.at[:, cols], dst.at[at % 2], column_sems.at[way, at % 2])

    for at in range(net.n_f - 1, max(net.n_f - 3, -1), -1):
        for way in range(2):
            load(at, way).start()

    def out_terms(at):
        load(at, 1).wait()
        out_sum.stage[at] = dot(att_t[...], dm[at % 2]).astype(BF)
        pl.when(at >= 2)(lambda: load(at - 2, 1).start())
        out_sum.first(at)

    def qkv_terms(at):
        load(at, 0).wait()
        right = n1[at % 2]
        for kind in range(3):
            rows = slice(kind * columns, (kind + 1) * columns)
            qkv_sum.stage[at, rows, :] = dot(dproj_t[kind], right).astype(BF)
        pl.when(at >= 2)(lambda: load(at - 2, 0).start())
        qkv_sum.first(at)

    def produce(place, write):
        span = aligned(place * pair, pair)

        @pl.loop(0, width // TILE)
        def _(j):
            cols = aligned(j * TILE, TILE)
            value = dot_nt(dproj[0, span, :], wq[0, cols, :])
            for kind in range(1, 3):
                value = value + dot_nt(dproj[kind, span, :], wq[kind, cols, :])
            write(cols, value)

    terms[...] = terms_in[...]
    bias_cols = aligned(net.s * columns, columns)
    of_head = (
        lax.broadcasted_iota(jnp.int32, (8, columns), 1) // HEAD
        == lax.broadcasted_iota(jnp.int32, (8, columns), 0)
    ).astype(F32)
    visible = lax.broadcasted_iota(jnp.int32, (block, block), 0) <= lax.broadcasted_iota(
        jnp.int32, (block, block), 1
    )
    scale = HEAD**-0.5
    net.barrier()
    copies.wait(*loads[:6])

    @pl.loop(0, length // block)
    def _(i):
        span = aligned(i * block, block)
        product = datt[span, :].astype(F32) * att[span, :].astype(F32)
        inners[:, span] = lax.dot_general(
            of_head,
            product,
            (((1,), (1,)), ((), ())),
            precision=lax.Precision.HIGHEST,
            preferred_element_type=F32,
        )
        lane = lax.broadcasted_iota(jnp.int32, (1, columns), 1)
        for head in range(heads):
            here = jnp.where(lane // HEAD == head, 1.0, 0.0).astype(BF)
            query[head, span, :] = q[span, :] * (here * scale)
            upstream[head, span, :] = datt[span, :] * here

    copies.wait(*loads[6:8])
    fold = Fold(net, tiles, total, *buffers, *fold_sems)

    for j in range(length // block):
        at, end = j * block, (j + 1) * block
        dk[...] = jnp.zeros(dk.shape, F32)
        dv[...] = jnp.zeros(dv.shape, F32)

        @pl.loop(0, heads)
        def _(head):
            head_rows = aligned(head * HEAD, HEAD)
            keys, values, keys_t = k[at:end, :], v[at:end, :], kt[head_rows, at:end]

            def part(lo, hi, near):
                probs = jnp.exp(dot_nt(keys, query[head, lo:hi, :]) - lse[pl.ds(head, 1), lo:hi])
                if near:
                    probs = jnp.where(visible, probs, 0.0)
                grads = dot_nt(values, upstream[head, lo:hi, :])
                scores = (probs * (grads - inners[pl.ds(head, 1), lo:hi])).astype(BF)
                out = dot(keys_t, scores)
                dqt[head_rows, lo:hi] = dqt[head_rows, lo:hi] + out if j else out
                return dot(probs.astype(BF), upstream[head, lo:hi, :]), dot(scores, query[head, lo:hi, :])

            value_grads, key_grads = part(at, end, True)
            if end < length:
                more_values, more_keys = part(end, length, False)
                value_grads, key_grads = value_grads + more_values, key_grads + more_keys
            dv[...] = dv[...] + value_grads
            dk[...] = dk[...] + key_grads

        span = slice(at, end)
        tables = cosine[span, :], -sine[span, :]
        parts = [
            rotary(turned((dqt[:, span] * scale).astype(BF)).astype(F32), *tables).astype(BF),
            rotary(dk[...].astype(BF).astype(F32), *tables).astype(BF),
            dv[...].astype(BF),
        ]
        for kind in range(3):
            dproj[kind, span, :] = parts[kind]
            dproj_t[kind, :, span] = turned(parts[kind])
            row = slice(4 + kind, 5 + kind)
            terms[row, bias_cols] = terms[row, bias_cols] + jnp.sum(parts[kind].astype(F32), 0, keepdims=True)

        def meanwhile():
            if j < net.n_f:
                out_terms(net.n_f - 1 - j)

        fold.begin_at(j, produce, meanwhile)
        if j == 1:
            copies.wait()
            ends[2].start()

    for at in range(net.n_f - 1 - length // block, -1, -1):
        out_terms(at)
    ahead = min(2, net.n_f)
    for i in range(ahead):
        qkv_terms(net.n_f - 1 - i)
    out_sum.second()
    slots = 2 * fold.pieces * (net.n_l - 1)
    each = -(-(net.n_f - ahead) // slots)
    for wave in range(1, net.n_l):

        def between(turn, piece):
            slot = ((wave - 1) * 2 + turn) * fold.pieces + piece

            @pl.loop(0, each)
            def _(i):
                task = ahead + slot * each + i
                pl.when(task < net.n_f)(lambda: qkv_terms(net.n_f - 1 - task))

        fold.passes_rising(wave, between)
    fold.finals()

    def write_input(i, span, value):
        gin_o[span, :] = value + dmid[span, :]

    norm_backward(chunk, tok, total, gains[0:1, :], terms, 0, write_input)
    packet_sum = PacketSum(net, *packet_scratch)
    packet_sum.start(terms, width // (net.n_f * net.n_s))
    qkv_sum.second()
    packet_sum.middle()
    for end, out in zip(ends, (down_o, gate_o, up_o)):
        end.last(out)
    packet_sum.finish(small_o)
    fold.finish()
    for grid_sum, out in ((qkv_sum, qkv_o), (out_sum, out_o)):
        grid_sum.last(out)
        grid_sum.finish()


def back_part(datt, q, k, kt, v, att, att_t, wq, n1, dm, down, gate, up, lse, tokens, dmid, gains, terms, tables):
    chunk, width = tokens.shape
    n_f, n_s = lax.axis_size("fsdp"), lax.axis_size("seq")
    length, columns = q.shape
    depth = width // n_f
    units = 2 * gate.shape[1]
    shape = jax.ShapeDtypeStruct
    return pl.pallas_call(
        back_kernel,
        name="back",
        out_shape=[
            shape((chunk, width), F32),
            shape((SMALL, 128), F32),
            shape((columns, depth), F32),
            shape((3 * columns, depth), F32),
            *[shape((units, depth), F32)] * 3,
        ],
        in_specs=[ANY] * 13 + [VMEM] * 7,
        out_specs=[VMEM] * 7,
        scratch_shapes=[
            pltpu.VMEM((length, columns), BF),
            pltpu.VMEM((length, columns), BF),
            pltpu.VMEM((length, columns), BF),
            pltpu.VMEM((columns, length), BF),
            pltpu.VMEM((length, columns), BF),
            pltpu.VMEM((length, columns), BF),
            pltpu.VMEM((columns, length), BF),
            pltpu.VMEM((3, width, columns), BF),
            pltpu.VMEM((2, length, depth), BF),
            pltpu.VMEM((2, length, depth), BF),
            pltpu.VMEM((columns // HEAD, length, columns), BF),
            pltpu.VMEM((columns // HEAD, length, columns), BF),
            pltpu.VMEM((8, length), F32),
            pltpu.VMEM((2 * chunk, columns), F32),
            pltpu.VMEM((2 * chunk, columns), F32),
            pltpu.VMEM((columns, length), F32),
            pltpu.VMEM((3, length, columns), BF),
            pltpu.VMEM((3, columns, length), BF),
            pltpu.VMEM((SMALL, width), F32),
            *Fold.shared(chunk, width),
            *Fold.buffers(n_s, chunk, width),
            *Fold.sems(n_s, 8),
            *PacketSum.scratch(n_f, n_s),
            *GridSum.scratch(n_f, columns, depth),
            *GridSum.scratch(n_f, 3 * columns, depth),
            *GridEnd.scratch(n_f, units, depth),
            pltpu.SemaphoreType.DMA((11,)),
            pltpu.SemaphoreType.DMA((2, 2)),
        ],
        compiler_params=pltpu.CompilerParams(
            collective_id=3, has_side_effects=True, vmem_limit_bytes=VMEM_BYTES
        ),
        cost_estimate=pl.CostEstimate(
            flops=2 * length * columns * (8 * width + 5 * length),
            bytes_accessed=4 * length * width,
            transcendentals=length * length * columns // HEAD,
        ),
    )(datt, q, k, kt, v, att, att_t, wq, n1, dm, down, gate, up, lse, tokens, dmid, gains, terms, *tables)


def outputs_kernel(small, *refs):
    sources, targets, parts = refs[:7], refs[7:14], refs[14:]
    own = parts[0].shape[1]
    for src, dst in zip(sources, targets):
        if src.shape == dst.shape:
            dst[...] = src[...]
        else:
            rows, columns = src.shape[0] // 3, src.shape[1]
            for kind in range(3):
                dst[kind * columns : (kind + 1) * columns, :] = src[kind * rows : (kind + 1) * rows, :].T
    for at in range(4):
        parts[at][...] = small[at : at + 1, 0:own]
    parts[4][...] = small[4:7, 0:own]


def outputs_part(small, own, *arrays):
    shape = jax.ShapeDtypeStruct
    return pl.pallas_call(
        outputs_kernel,
        name="outputs",
        out_shape=[shape((3 * v.shape[1], v.shape[0] // 3) if at == 2 else v.shape, v.dtype) for at, v in enumerate(arrays)]
        + [shape((1, own), F32)] * 4
        + [shape((3, own), F32)],
        in_specs=[VMEM] * 8,
        out_specs=[VMEM] * 12,
        compiler_params=pltpu.CompilerParams(vmem_limit_bytes=VMEM_BYTES),
    )(small, *arrays)


def per_device(
    tokens,
    gain_one,
    shift_one,
    w_qkv,
    b_qkv,
    w_out,
    gain_two,
    shift_two,
    w_gate,
    w_up,
    w_down,
    grad_output,
):
    length = tokens.shape[1] * lax.axis_size("seq")
    width = gain_one.shape[0]
    norms = [v[None] for v in (gain_one, shift_one, gain_two, shift_two)] + [b_qkv]
    tables = rotary_tables(length)
    q, k, kt, v, att, att_t, lse, n1, gains, wq, _, dm, datt, dmid, top, terms, gate, up, down = layer_part(
        tokens[0], norms, w_qkv.transpose(1, 0, 2), w_out, w_gate.T, w_up.T, w_down, grad_output[0], tables
    )
    grad_input, small, out, qkv, down, gate, up = back_part(
        datt, q, k, kt, v, att, att_t, wq, n1, dm, down, gate, up, lse, tokens[0], dmid, gains, terms, tables
    )

    top, grad_input, qkv, out, gate, up, down, one, shift, two, shift_to, bias = outputs_part(
        small, width, top, grad_input, qkv, out, gate, up, down
    )
    return (
        top[None],
        grad_input[None],
        one[0],
        shift[0],
        qkv.reshape(3, -1, qkv.shape[1]).transpose(1, 0, 2),
        bias,
        out,
        two[0],
        shift_to[0],
        gate.T,
        up.T,
        down,
    )


def solution(mesh):
    whole = P(("fsdp", "seq"))
    rows = P("fsdp", "seq", None)
    inner = P("seq", "fsdp")
    outer = P("fsdp", "seq")
    heads = P("fsdp", None, "seq")
    bias = P(None, ("fsdp", "seq"))
    return jax.shard_map(
        per_device,
        mesh=mesh,
        in_specs=(rows, whole, whole, heads, bias, inner, whole, whole, outer, outer, inner, rows),
        out_specs=(rows, rows, whole, whole, heads, bias, inner, whole, whole, outer, outer, inner),
        check_vma=False,
    )
```

```python
import functools

import jax
import jax.numpy as jnp
import numpy as np
from jax import lax
from jax.experimental import pallas as pl
from jax.experimental.pallas import tpu as pltpu
from jax.sharding import PartitionSpec as P

HEAD = 64
ROT = 16
EPSILON = 1e-05
NEG_LARGE = -1e30
MESH = pl.DeviceIdType.MESH
ANY = pl.BlockSpec(memory_space=pl.ANY)
VMEM = pl.BlockSpec(memory_space=pltpu.VMEM)
BF = jnp.bfloat16
F32 = jnp.float32
VMEM_BYTES = 60 * 2**20
TILE = 512
SMALL = 8


def put(src, dst, send, recv, **device):
    return pltpu.make_async_remote_copy(
        src_ref=src, dst_ref=dst, send_sem=send, recv_sem=recv, device_id=device, device_id_type=MESH
    )


def dot(left, right):
    return jnp.dot(left, right, preferred_element_type=F32)


def dot_nt(left, right):
    return lax.dot_general(left, right, (((1,), (1,)), ((), ())), preferred_element_type=F32)


def dot_tn(left, right):
    return lax.dot_general(left, right, (((0,), (0,)), ((), ())), preferred_element_type=F32)


def aligned(start, size, unit=None):
    return pl.ds(pl.multiple_of(start, unit or size), size)


class Net:
    def __init__(self):
        self.n_f, self.n_s = lax.axis_size("fsdp"), lax.axis_size("seq")
        self.tall = 2 if self.n_f % 2 == 0 else 1
        self.wide = self.n_f // self.tall
        self.n_l = self.n_s // 2
        self.f, self.s = lax.axis_index("fsdp"), lax.axis_index("seq")
        self.a, self.b = self.f // self.wide, self.f % self.wide
        self.z, self.c = self.s // 2, self.s % 2
        self.mate = self.s + 1 - 2 * self.c

    def barrier(self):
        sem = pltpu.get_barrier_semaphore()
        for k in range(1, self.n_f):
            pl.semaphore_signal(
                sem, inc=1, device_id={"fsdp": (self.f + k) % self.n_f}, device_id_type=MESH
            )
        for k in range(1, self.n_s):
            pl.semaphore_signal(
                sem, inc=1, device_id={"seq": (self.s + k) % self.n_s}, device_id_type=MESH
            )
        pl.semaphore_wait(sem, self.n_f + self.n_s - 2)

    def sides(self, hop, act):
        @pl.loop(0, 2)
        def _(side):
            other = self.z + (2 * side - 1) * hop

            @pl.when((other >= 0) & (other < self.n_l))
            def _():
                act(other, side)


class Spread:
    def __init__(self, net, src, part, sems):
        self.net, self.src, self.part, self.sems = net, src, part, sems
        self.rows = [j for j in range(1, net.wide)]
        self.cols = [i for i in range(1, net.tall)]

    @staticmethod
    def count(n_f):
        tall = 2 if n_f % 2 == 0 else 1
        wide = n_f // tall
        return 1 + 2 * (wide - 1) + 2 * (tall - 1) + 4 * (wide - 1) * (tall - 1)

    def at(self, kind, i, j):
        w, t = len(self.rows), len(self.cols)
        base = {
            "own": 0,
            "row": 1,
            "col": 1 + 2 * w,
            "half0": 1 + 2 * w + 2 * t,
            "half1": 1 + 2 * w + 2 * t + 2 * w * t,
        }[kind]
        if kind == "own":
            return self.sems.at[0]
        k = j - 1 if kind == "row" else i - 1 if kind == "col" else (i - 1) * w + j - 1
        return self.sems.at[base + 2 * k], self.sems.at[base + 2 * k + 1]

    def rank(self, i, j):
        net = self.net
        return ((net.a + i) % net.tall) * net.wide + (net.b + j) % net.wide

    def back(self, i, j):
        net = self.net
        return ((net.a - i + net.tall) % net.tall) * net.wide + (net.b - j + net.wide) % net.wide

    def own(self):
        return pltpu.make_async_copy(self.src, self.part(self.net.f, None), self.at("own", 0, 0))

    def first(self, i, j):
        send, recv = self.at("row" if i == 0 else "col", i, j)
        place = self.part(self.net.f, None)
        return put(place, place, send, recv, fsdp=self.rank(i, j))

    def came(self, i, j):
        send, recv = self.at("row" if i == 0 else "col", i, j)
        place = self.part(self.back(i, j), None)
        return put(place, place, send, recv, fsdp=self.rank(i, j))

    def second(self, half, i, j, came=False):
        send, recv = self.at("half0" if half == 0 else "half1", i, j)
        origin = self.back(i, j) if came else self.back(0, j) if half == 0 else self.back(i, 0)
        place = self.part(origin, half)
        return put(place, place, send, recv, fsdp=self.rank(i, 0) if half == 0 else self.rank(0, j))

    def prepare(self):
        self.own().start()

    def start(self):
        self.own().wait()
        for i in self.cols:
            self.first(i, 0).start()
        for j in self.rows:
            self.first(0, j).start()

    def relay(self):
        for j in self.rows:
            self.came(0, j).wait_recv()
            for i in self.cols:
                self.second(0, i, j).start()
        for i in self.cols:
            self.came(i, 0).wait_recv()
            for j in self.rows:
                self.second(1, i, j).start()

    def finish(self):
        for j in self.rows:
            self.first(0, j).wait_send()
        for i in self.cols:
            self.first(i, 0).wait_send()
        for i in self.cols:
            for j in self.rows:
                for half in range(2):
                    self.second(half, i, j, came=True).wait_recv()
                    self.second(half, i, j).wait_send()


class Line:
    def __init__(self, net, src, part, recv, send, local):
        self.net, self.src, self.part, self.recv, self.send, self.local = net, src, part, recv, send, local
        self.pieces = recv.shape[1]
        self.rows = src.shape[0] // self.pieces

    @staticmethod
    def sems(n_s, pieces=2):
        return [
            pltpu.SemaphoreType.DMA((n_s, pieces)),
            pltpu.SemaphoreType.DMA((4, n_s // 2, pieces)),
            pltpu.SemaphoreType.DMA((1,)),
        ]

    def cut(self, ref, piece):
        return ref.at[aligned(piece * self.rows, self.rows)]

    def own(self):
        return pltpu.make_async_copy(self.src, self.part(self.net.s), self.local.at[0])

    def on_line(self, src, chunk, side, hop, piece):
        return put(
            self.cut(src, piece),
            self.cut(self.part(chunk), piece),
            self.send.at[side, hop, piece],
            self.recv.at[chunk, piece],
            seq=self.net.s + 2 - 4 * side,
        )

    def to_mate(self, src, chunk, side, hop, piece):
        return put(
            self.cut(src, piece),
            self.cut(self.part(chunk), piece),
            self.send.at[2 + side, hop, piece],
            self.recv.at[chunk, piece],
            seq=self.net.mate,
        )

    def goes_on(self, side):
        after = self.net.z + 1 - 2 * side
        return (after >= 0) & (after < self.net.n_l)

    def each_piece(self, act):
        pl.loop(0, self.pieces)(act)

    def prepare(self):
        self.own().start()

    def start(self):
        net = self.net
        self.own().wait()
        place = self.part(net.s)

        @self.each_piece
        def _(piece):
            for side in range(2):

                @pl.when(self.goes_on(side))
                def _():
                    self.on_line(place, net.s, side, 0, piece).start()

            self.to_mate(place, net.s, 0, 0, piece).start()

    def came(self, chunk, piece):
        place = self.cut(self.part(chunk), piece)
        put(place, place, self.send.at[0, 0, 0], self.recv.at[chunk, piece], seq=self.net.mate).wait_recv()

    def step(self, hop):
        net = self.net

        @self.each_piece
        def _(piece):
            def act(other, side):
                chunk = 2 * other + net.c
                self.came(chunk, piece)

                @pl.when(self.goes_on(side))
                def _():
                    self.on_line(self.part(chunk), chunk, side, hop, piece).start()

                self.to_mate(self.part(chunk), chunk, side, hop, piece).start()

            net.sides(hop, act)

    def pair(self, other):
        @self.each_piece
        def _(piece):
            self.came(2 * other + 1 - self.net.c, piece)

    def here(self):
        self.pair(self.net.z)

    def finish(self):
        net = self.net
        place = self.part(net.s)

        @self.each_piece
        def _(piece):
            for side in range(2):

                @pl.when(self.goes_on(side))
                def _():
                    self.on_line(place, net.s, side, 0, piece).wait_send()

            self.to_mate(place, net.s, 0, 0, piece).wait_send()

            @pl.loop(1, net.n_l)
            def _(hop):
                def act(other, side):
                    chunk = 2 * other + net.c

                    @pl.when(self.goes_on(side))
                    def _():
                        self.on_line(self.part(chunk), chunk, side, hop, piece).wait_send()

                    self.to_mate(self.part(chunk), chunk, side, hop, piece).wait_send()

                net.sides(hop, act)


class Packets:
    def __init__(self, net, src, buf, sems):
        self.net, self.src, self.buf, self.sems = net, src, buf, sems

    @staticmethod
    def count(n_f, n_s):
        return 1 + 2 * (n_f - 1) + 2 * (n_s - 1)

    def own(self):
        net = self.net
        return pltpu.make_async_copy(self.src, self.buf.at[net.s, net.f], self.sems.at[0])

    def one(self, k, came=False):
        net = self.net
        f = (net.f - k + net.n_f) % net.n_f if came else net.f
        place = self.buf.at[net.s, f]
        return put(
            place if came else self.src,
            place,
            self.sems.at[2 * k - 1],
            self.sems.at[2 * k],
            fsdp=(net.f + k) % net.n_f,
        )

    def two(self, k, came=False):
        net = self.net
        place = self.buf.at[(net.s - k + net.n_s) % net.n_s if came else net.s]
        at = 2 * (net.n_f - 1) + 2 * k - 1
        return put(place, place, self.sems.at[at], self.sems.at[at + 1], seq=(net.s + k) % net.n_s)

    def start(self):
        self.own().start()
        for k in range(1, self.net.n_f):
            self.one(k).start()

    def middle(self):
        self.own().wait()
        for k in range(1, self.net.n_f):
            self.one(k, came=True).wait_recv()
            self.one(k).wait_send()
        for k in range(1, self.net.n_s):
            self.two(k).start()

    def finish(self):
        for k in range(1, self.net.n_s):
            self.two(k, came=True).wait_recv()
            self.two(k).wait_send()

    def unpack(self, out, width):
        net = self.net
        per = 128 // width
        for tile in range(net.n_f * net.n_s // per):
            total = None
            for j in range(per):
                f, s = divmod(tile * per + j, net.n_s)
                piece = self.buf[s, f]
                if j:
                    piece = pltpu.roll(piece, j * width, axis=1)
                total = piece if total is None else total + piece
            out[:, tile * 128 : (tile + 1) * 128] = total


def rotary(values, cosine, sine):
    columns = values.shape[1]
    half = ROT // 2
    times = columns // 128

    def wide(table):
        return table if times == 1 else jnp.concatenate([table] * times, axis=1)

    lane = lax.broadcasted_iota(jnp.int32, values.shape, 1)
    other = jnp.where(
        lane % HEAD < half, pltpu.roll(values, columns - half, axis=1), pltpu.roll(values, half, axis=1)
    )
    return values * wide(cosine) + other * wide(sine)


def rotary_tables(length):
    half = ROT // 2
    freqs = np.float32(10000.0) ** (-np.arange(half, dtype=np.float32) * np.float32(2.0 / ROT))
    angles = np.arange(length, dtype=np.float32)[:, None] * freqs[None, :].astype(np.float32)
    cosine, sine = np.cos(angles), np.sin(angles)
    rest = np.zeros((length, HEAD - ROT), np.float32)
    keep = np.concatenate([cosine, cosine, rest + 1], 1)
    swap = np.concatenate([-sine, sine, rest], 1)
    return [np.tile(t, (1, 128 // HEAD)).astype(np.float32) for t in (keep, swap)]


def normalize(values):
    center = values - jnp.mean(values, -1, keepdims=True)
    inverse = lax.rsqrt(jnp.mean(center * center, -1, keepdims=True) + EPSILON)
    return center * inverse, inverse


class Copies:
    def __init__(self, sems):
        self.sems, self.all, self.open = sems, [], []

    def start(self, src, dst):
        copy = pltpu.make_async_copy(src, dst, self.sems.at[len(self.all)])
        copy.start()
        self.all.append(copy)
        self.open.append(copy)
        return copy

    def wait(self, *copies):
        for copy in copies or list(self.open):
            copy.wait()
            self.open = [c for c in self.open if c is not copy]


def columns_of(ref, depth):
    half_rows = ref.shape[0] // 2

    def part(f, half):
        span = aligned(f * depth, depth)
        if half is None:
            return ref.at[:, span]
        return ref.at[pl.ds(half * half_rows, half_rows), span]

    return part


def rows_of(ref, chunk):
    return lambda s: ref.at[aligned(s * chunk, chunk)]


class Fold:
    def __init__(self, net, tile, total, mate_in, coming, mate_out, out, mate_send, mate_recv, send, recv):
        self.net, self.tile, self.total = net, tile, total
        self.mate_in, self.coming, self.mate_out, self.out = mate_in, coming, mate_out, out
        self.mate_send, self.mate_recv, self.send, self.recv = mate_send, mate_recv, send, recv
        self.chunk = total.shape[0]
        self.pieces = recv.shape[1]
        self.rows = self.chunk // self.pieces

    @staticmethod
    def shared(chunk, width):
        return [pltpu.VMEM((2 * chunk, TILE), F32), pltpu.VMEM((chunk, width), F32)]

    @staticmethod
    def buffers(n_s, chunk, width):
        n_l = n_s // 2
        return [
            pltpu.VMEM((n_l, chunk, width), BF),
            pltpu.VMEM((n_l + 1, chunk, width), BF),
            pltpu.VMEM((3, chunk, width), BF),
            pltpu.VMEM((n_l, chunk, width), BF),
        ]

    @staticmethod
    def sems(n_s, pieces=4):
        n_l = n_s // 2
        return [
            pltpu.SemaphoreType.DMA((3, pieces)),
            pltpu.SemaphoreType.DMA((n_l, pieces)),
            pltpu.SemaphoreType.DMA((n_l, pieces)),
            pltpu.SemaphoreType.DMA((n_l + 1, pieces)),
        ]

    def place(self, other):
        return (other >= 0) & (other < self.net.n_l)

    def fed(self, side):
        return self.place(self.net.z + 1 - 2 * side)

    def span(self, piece):
        return aligned(piece * self.rows, self.rows)

    def each_piece(self, act):
        pl.loop(0, self.pieces)(act)

    def to_mate(self, target, slot, piece):
        span = self.span(piece)
        return put(
            self.mate_out.at[slot, span],
            self.mate_in.at[target, span],
            self.mate_send.at[slot, piece],
            self.mate_recv.at[target, piece],
            seq=self.net.mate,
        )

    def onward(self, target, side, hop, piece):
        span = self.span(piece)
        slot = target + (self.net.n_l - target) * (1 - side) * (1 // hop)
        return put(
            self.out.at[target, span],
            self.coming.at[slot, span],
            self.send.at[target, piece],
            self.recv.at[slot, piece],
            seq=self.net.s + 4 * side - 2,
        )

    def came(self, slot, piece):
        place = self.coming.at[slot, self.span(piece)]
        put(place, place, self.send.at[0, 0], self.recv.at[slot, piece], seq=self.net.mate).wait_recv()

    def mate_sent(self, slot):
        self.each_piece(lambda piece: self.to_mate(self.net.z, slot, piece).wait_send())

    def begin_one(self, target, slot, produce):
        mine = aligned(self.net.c * self.chunk, self.chunk)
        theirs = aligned((1 - self.net.c) * self.chunk, self.chunk)

        def write(cols, value):
            self.tile[...] = value
            self.out[target, :, cols] = self.tile[mine, :].astype(BF)
            self.mate_out[slot, :, cols] = self.tile[theirs, :].astype(BF)

        produce(target, write)
        self.each_piece(lambda piece: self.to_mate(target, slot, piece).start())

    def leave(self, target, side, hop):
        @pl.when((hop > 0) & jnp.logical_not(self.fed(side)))
        def _():
            self.each_piece(lambda piece: self.pass_piece(target, side, hop, piece, False))

    def begin(self, produce, between=None, meanwhile=None):
        net = self.net

        @pl.loop(0, net.n_l)
        def _(j):
            hop = net.n_l - 1 - j

            @pl.loop(0, 2)
            def _(side):
                target = net.z + (2 * side - 1) * hop
                here = self.place(target) & ((hop > 0) | (side == 0))

                @pl.when(here)
                def _():
                    @pl.when((hop > 0) & self.place(target + 2 * side - 1))
                    def _():
                        self.mate_sent(side)

                    self.begin_one(target, side + (2 - side) * (1 // (hop + 1)), produce)

                if meanwhile is not None:
                    pl.when(hop > 0)(lambda: meanwhile(2 * j + side))

                pl.when(here)(lambda: self.leave(target, side, hop))

            if between is not None:
                pl.when(j == 1)(between)

    def pass_piece(self, target, side, hop, piece, fed):
        self.to_mate(target, 0, piece).wait_recv()
        span = self.span(piece)
        value = self.out[target, span, :].astype(F32) + self.mate_in[target, span, :].astype(F32)
        if fed:
            self.came(target, piece)
            value = value + self.coming[target, span, :].astype(F32)
        self.out[target, span, :] = value.astype(BF)
        self.onward(target, side, hop, piece).start()

    def open_total(self):
        net = self.net

        @self.each_piece
        def _(piece):
            self.to_mate(net.z, 0, piece).wait_recv()
            span = self.span(piece)
            self.total[span, :] = self.out[net.z, span, :].astype(F32) + self.mate_in[net.z, span, :].astype(F32)

    def wave(self, at, near=False, between=None):
        net = self.net
        above = at if near else net.n_l - at

        @pl.loop(0, 2)
        def _(turn):
            side = (1 - (2 * net.z) // net.n_l + turn) % 2
            target = net.n_l - 1 - above + (2 * above - net.n_l + 1) * side
            hop = (target - net.z) * (2 * side - 1)

            @self.each_piece
            def _(piece):
                span = self.span(piece)

                @pl.when(self.fed(side) & (hop > 0))
                def _():
                    self.pass_piece(target, side, hop, piece, True)

                @pl.when(self.fed(side) & (hop == 0))
                def _():
                    slot = net.z + (net.n_l - net.z) * (1 - side)
                    self.came(slot, piece)
                    self.total[span, :] = self.total[span, :] + self.coming[slot, span, :].astype(F32)

                if between is not None:
                    between(((at - 1) * 2 + turn) * self.pieces + piece)

    def passes_between(self, wave, near, between):
        net = self.net
        above = wave if near else net.n_l - wave

        @pl.loop(0, 2)
        def _(turn):
            side = (1 - (2 * net.z) // net.n_l + turn) % 2
            target = net.n_l - 1 - above + (2 * above - net.n_l + 1) * side
            hop = (target - net.z) * (2 * side - 1)

            @self.each_piece
            def _(piece):
                @pl.when((hop > 0) & self.fed(side))
                def _():
                    self.pass_piece(target, side, hop, piece, True)

                between(turn, piece)

    def finals(self):
        net = self.net

        @self.each_piece
        def _(piece):
            self.to_mate(net.z, 0, piece).wait_recv()
            span = self.span(piece)
            self.total[span, :] = self.out[net.z, span, :].astype(F32) + self.mate_in[net.z, span, :].astype(F32)

        @pl.loop(0, 2)
        def _(turn):
            side = (1 - (2 * net.z) // net.n_l + turn) % 2

            @pl.when(self.fed(side))
            def _():
                slot = net.z + (net.n_l - net.z) * (1 - side)

                @self.each_piece
                def _(piece):
                    span = self.span(piece)
                    self.came(slot, piece)
                    self.total[span, :] = self.total[span, :] + self.coming[slot, span, :].astype(F32)

    def finish(self):
        net = self.net
        self.mate_sent(2)
        for side in range(2):
            pl.when(self.place(net.z + 2 * side - 1))(functools.partial(self.mate_sent, side))

        @pl.loop(1, net.n_l)
        def _(hop):
            net.sides(
                hop,
                lambda target, side: self.each_piece(
                    lambda piece: self.onward(target, side, hop, piece).wait_send()
                ),
            )


class GridSum:
    def __init__(self, net, stage, came, sems):
        self.net, self.stage, self.came, self.sems = net, stage, came, sems
        self.half = stage.shape[1] // 2
        self.rows = next(r for r in (176, 128, 96, 64, 32, 16) if self.half % r == 0)
        self.cols = range(1, net.tall)
        self.along = range(1, net.wide)
        self.bases = self.layout(net.n_f)

    @staticmethod
    def layout(n_f):
        tall = 2 if n_f % 2 == 0 else 1
        wide = n_f // tall
        sizes = [(wide - 1) * tall, (tall - 1) * wide, tall - 1, wide - 1]
        return [sum(sizes[:at]) for at in range(5)]

    @staticmethod
    def scratch(n_f, rows, columns):
        count = GridSum.layout(n_f)[4]
        return [
            pltpu.VMEM((n_f, rows, columns), BF),
            pltpu.VMEM((count, rows // 2, columns), BF),
            pltpu.SemaphoreType.DMA((2, count + GridEnd.count(n_f))),
        ]

    def slot(self, kind, i, j):
        base = self.bases[kind]
        return base + [(j - 1) * self.net.tall + i, (i - 1) * self.net.wide + j, i - 1, j - 1][kind]

    def rank(self, i, j):
        net = self.net
        return ((net.a + i) % net.tall) * net.wide + (net.b + j) % net.wide

    def owner(self, at):
        return self.rank(at // self.net.wide, at % self.net.wide)

    def copy(self, kind, i, j):
        half = kind % 2
        along = kind in (0, 3)
        slot = self.slot(kind, i, j)
        at = i * self.net.wide + j
        return put(
            self.stage.at[at, pl.ds(half * self.half, self.half)],
            self.came.at[slot],
            self.sems.at[0, slot],
            self.sems.at[1, slot],
            fsdp=self.rank(0, j) if along else self.rank(i, 0),
        )

    def first(self, at):
        i, j = at // self.net.wide, at % self.net.wide

        @pl.when(j > 0)
        def _():
            self.copy(0, i, j).start()

        @pl.when(i > 0)
        def _():
            self.copy(1, i, j).start()

    def gather(self, half, at, slots, write):
        @pl.loop(0, self.half // self.rows)
        def _(step):
            span = aligned(half * self.half + step * self.rows, self.rows, 16)
            value = self.stage[at, span, :].astype(F32)
            for slot in slots:
                value = value + self.came[slot, aligned(step * self.rows, self.rows, 16), :].astype(F32)
            write(span, value)

    def wait(self, *copies):
        for kind, i, j in copies:
            self.copy(kind, i, j).wait_recv()
        return [self.slot(*copy) for copy in copies]

    def second(self):
        def keep(at):
            def write(span, value):
                self.stage[at, span, :] = value.astype(BF)

            return write

        for i in self.cols:
            at = i * self.net.wide
            self.gather(0, at, self.wait(*[(0, i, j) for j in self.along]), keep(at))
            self.copy(2, i, 0).start()
        for j in self.along:
            self.gather(1, j, self.wait(*[(1, i, j) for i in self.cols]), keep(j))
            self.copy(3, 0, j).start()

    def sum_first(self):
        def keep(at):
            def write(span, value):
                self.stage[at, span, :] = value.astype(BF)

            return write

        for i in range(self.net.tall):
            at = i * self.net.wide
            self.gather(0, at, self.wait(*[(0, i, j) for j in self.along]), keep(at))
        for j in range(self.net.wide):
            self.gather(1, j, self.wait(*[(1, i, j) for i in self.cols]), keep(j))

    def hand_on(self, out):
        net = self.net
        shards = [(0, 0), (0, 1), *[(i * net.wide, 0) for i in self.cols], *[(j, 1) for j in self.along]]
        return [
            pltpu.make_async_copy(
                self.stage.at[at, pl.ds(half * self.half, self.half)], out.at[k], self.sems.at[0, self.bases[4] + k]
            )
            for k, (at, half) in enumerate(shards)
        ]

    def last(self, out):
        def write(span, value):
            out[span, :] = value

        self.gather(
            0, 0, self.wait(*[(0, 0, j) for j in self.along], *[(2, i, 0) for i in self.cols]), write
        )
        self.gather(
            1, 0, self.wait(*[(1, i, 0) for i in self.cols], *[(3, 0, j) for j in self.along]), write
        )

    def finish_first(self):
        for i in range(self.net.tall):
            for j in range(self.net.wide):
                if j:
                    self.copy(0, i, j).wait_send()
                if i:
                    self.copy(1, i, j).wait_send()

    def finish(self):
        self.finish_first()
        for i in self.cols:
            self.copy(2, i, 0).wait_send()
        for j in self.along:
            self.copy(3, 0, j).wait_send()


class GridEnd:
    def __init__(self, net, sums, came, sems):
        self.net, self.sums, self.came, self.sems = net, sums, came, sems

    @staticmethod
    def count(n_f):
        tall = 2 if n_f % 2 == 0 else 1
        return tall + n_f // tall

    @staticmethod
    def scratch(n_f, rows, columns):
        count = GridEnd.count(n_f)
        return [
            pltpu.VMEM((count, rows // 2, columns), BF),
            pltpu.VMEM((count - 2, rows // 2, columns), BF),
            pltpu.SemaphoreType.DMA((2, count - 2)),
        ]

    def copies(self):
        net = self.net
        f = [((net.a + i) % net.tall) * net.wide + net.b for i in range(1, net.tall)]
        f += [net.a * net.wide + (net.b + j) % net.wide for j in range(1, net.wide)]
        return [
            put(self.sums.at[2 + k], self.came.at[k], self.sems.at[0, k], self.sems.at[1, k], fsdp=to)
            for k, to in enumerate(f)
        ]

    def start(self):
        for copy in self.copies():
            copy.start()

    def last(self, out):
        for copy in self.copies():
            copy.wait()
        half = self.sums.shape[1]
        rows = next(r for r in (176, 128, 96, 64, 32, 16) if half % r == 0)
        down = range(self.net.tall - 1)
        along = range(self.net.tall - 1, self.net.tall + self.net.wide - 2)
        for at, slots in enumerate((down, along)):

            @pl.loop(0, half // rows)
            def _(step):
                span = aligned(step * rows, rows, 16)
                value = self.sums[at, span, :].astype(F32)
                for slot in slots:
                    value = value + self.came[slot, span, :].astype(F32)
                out[aligned(at * half + step * rows, rows, 16), :] = value


class PacketSum:
    def __init__(self, net, out, seq_in, total, fsdp_in, sems):
        self.net, self.out, self.seq_in, self.total, self.fsdp_in, self.sems = net, out, seq_in, total, fsdp_in, sems

    @staticmethod
    def scratch(n_f, n_s):
        return [
            pltpu.VMEM((n_s, n_f, SMALL, 128), F32),
            pltpu.VMEM((n_s, n_f, SMALL, 128), F32),
            pltpu.VMEM((n_f, SMALL, 128), F32),
            pltpu.VMEM((n_f, SMALL, 128), F32),
            pltpu.SemaphoreType.DMA((2 * (n_f + n_s),)),
        ]

    def one(self, k):
        to = (self.net.s + k) % self.net.n_s
        return put(self.out.at[to], self.seq_in.at[k], self.sems.at[2 * k], self.sems.at[2 * k + 1], seq=to)

    def two(self, k):
        to = (self.net.f + k) % self.net.n_f
        at = 2 * (self.net.n_s + k)
        return put(self.total.at[to], self.fsdp_in.at[k], self.sems.at[at], self.sems.at[at + 1], fsdp=to)

    def start(self, terms, width):
        net = self.net
        per = 128 // width
        for tile in range(net.n_f * net.n_s // per):
            value = terms[:, tile * 128 : (tile + 1) * 128]
            for j in range(per):
                f, s = divmod(tile * per + j, net.n_s)
                self.out[s, f] = pltpu.roll(value, 128 - j * width, axis=1) if j else value
        for k in range(1, net.n_s):
            self.one(k).start()

    def middle(self):
        net = self.net
        total = self.out[net.s]
        for k in range(1, net.n_s):
            self.one(k).wait()
            total = total + self.seq_in[k]
        self.total[...] = total
        for k in range(1, net.n_f):
            self.two(k).start()

    def finish(self, result):
        net = self.net
        total = self.total[net.f]
        for k in range(1, net.n_f):
            self.two(k).wait()
            total = total + self.fsdp_in[k]
        result[...] = total


def norm_backward(rows, source, grad, gain, terms, at, write):
    terms[at : at + 2, :] = jnp.zeros((2, terms.shape[1]), F32)

    @pl.loop(0, rows // 32, unroll=2)
    def _(i):
        span = aligned(i * 32, 32)
        scaled, inverse = normalize(source[span, :].astype(F32))
        value = grad[span, :]
        upstream = value * gain
        inner = jnp.mean(upstream, -1, keepdims=True)
        cross = jnp.mean(upstream * scaled, -1, keepdims=True)
        terms[at : at + 1, :] = terms[at : at + 1, :] + jnp.sum(value * scaled, 0, keepdims=True)
        terms[at + 1 : at + 2, :] = terms[at + 1 : at + 2, :] + jnp.sum(value, 0, keepdims=True)
        write(i, span, inverse * (upstream - inner - scaled * cross))


def layer_kernel(
    tok,
    gain_one,
    shift_one,
    gain_two,
    shift_two,
    bias,
    wq_own,
    wo_own,
    wg_own,
    wu_own,
    wd_own,
    gout_own,
    cosine,
    sine,
    q_o,
    k_o,
    kt_o,
    v_o,
    att_o,
    lse_o,
    n1_o,
    gains_o,
    wq_o,
    wo_o,
    dm_o,
    datt_o,
    dmid_o,
    top_o,
    terms_o,
    gate_o,
    up_o,
    down_o,
    rows,
    gout,
    wq,
    wo,
    wg,
    wu,
    wd,
    q,
    k,
    kt,
    v,
    vt,
    ot,
    att,
    hidden,
    dgate,
    dup,
    mid,
    low,
    packet,
    packets,
    tiles,
    total,
    *rest,
):
    net = Net()
    chunk, width = tok.shape
    length = chunk * net.n_s
    depth = wq_own.shape[1]
    columns = wq_own.shape[2]
    heads = columns // HEAD
    pair = 2 * chunk
    buffers, rest = rest[:4], rest[4:]
    folds = []
    for _ in range(3):
        folds.append(Fold(net, tiles, total, *buffers, *rest[:4]))
        rest = rest[4:]
    att_fold, normed_fold, top_fold = folds
    line_sems = [rest[at : at + 3] for at in (0, 3, 6, 9)]
    rest = rest[12:]
    spread_sems, rest = rest[:5], rest[5:]
    gate_sum, up_sum, down_sum = [GridSum(net, *rest[at : at + 3]) for at in (0, 3, 6)]
    sums = (down_sum, gate_sum, up_sum)
    pk_sems, copy_sems, n1_sems, free_sem = rest[9:]
    copies = Copies(copy_sems)
    n1 = att_fold.mate_out

    packet[...] = jnp.zeros(packet.shape, F32)
    own = gain_one.shape[1]
    for at, part in enumerate((gain_one, shift_one, gain_two, shift_two)):
        packet[at : at + 1, 0:own] = part[...].astype(F32)
    packet[4:7, 0:own] = bias[...].astype(F32)
    def wq_part(f, half):
        if half is None:
            return wq.at[:, aligned(f * depth, depth), :]
        return wq.at[:, aligned(f * depth + half * (depth // 2), depth // 2), :]

    spread_q = Spread(net, wq_own, wq_part, spread_sems[0])
    spread_o, spread_g, spread_u, spread_d = [
        Spread(net, own, columns_of(full, depth), sems)
        for own, full, sems in zip((wo_own, wg_own, wu_own, wd_own), (wo, wg, wu, wd), spread_sems[1:])
    ]
    pk = Packets(net, packet, packets, pk_sems)
    line = Line(net, tok, rows_of(rows, chunk), *line_sems[0])
    gout_line = Line(net, gout_own, rows_of(gout, chunk), *line_sems[1])
    n2_line = Line(net, low, rows_of(rows, chunk), *line_sems[2])
    dm_line = Line(net, low, rows_of(rows, chunk), *line_sems[3])

    for ready in (line, spread_q, spread_o, spread_g, spread_u, spread_d, gout_line):
        ready.prepare()
    net.barrier()

    def pairs(which, hop):
        net.sides(hop, lambda other, side: which.pair(other))

    def blocks(hop, act):
        def once(other, side):
            @pl.when((hop > 0) | (side == 0))
            def _():
                act(other, side)

        net.sides(hop, once)

    pk.start()
    line.start()
    spread_q.start()
    pk.middle()
    pk.finish()
    pk.unpack(gains_o, width // (net.n_f * net.n_s))

    def project_block(other, side):
        span = aligned(other * pair, pair)
        gain, shift = gains_o[0:1, :], gains_o[1:2, :]

        for part in range(2):

            @pl.loop(0, chunk // 32, unroll=2)
            def _(i):
                at = aligned((2 * other + part) * chunk + i * 32, 32)
                scaled, _ = normalize(rows[at, :].astype(F32))
                n1[part, aligned(i * 32, 32), :] = (scaled * gain + shift).astype(BF)

        keeps = [
            pltpu.make_async_copy(
                n1.at[part], n1_o.at[aligned((2 * other + part) * chunk, chunk)], n1_sems.at[part]
            )
            for part in range(2)
        ]
        for copy in keeps:
            copy.start()
        left = n1[0:2].reshape(pair, width)
        cols = aligned(net.s * columns, columns)
        tables = cosine[span, :], sine[span, :]
        for kind in range(3):
            value = dot(left, wq[kind]) + gains_o[4 + kind : 5 + kind, cols]
            if kind == 0:
                q[span, :] = rotary(value, *tables).astype(BF)
            elif kind == 1:
                value = rotary(value, *tables)
                k[span, :] = value.astype(BF)
                kt[...] = value.T.astype(BF)
            else:
                v[...] = value.astype(BF)
                vt[:, span] = value.T.astype(BF)
        for copy in (
            pltpu.make_async_copy(kt, kt_o.at[:, span], n1_sems.at[2]),
            pltpu.make_async_copy(v, v_o.at[span], n1_sems.at[3]),
        ):
            copy.start()
            keeps.append(copy)
        for copy in keeps:
            copy.wait()

    line.here()
    for hop in range(1, net.n_l - 1):
        line.step(hop)
        if hop == 1:
            spread_q.relay()
        pairs(line, hop)
    spread_o.start()
    spread_q.finish()
    spread_g.start()
    pl.loop(0, net.n_l - 1)(lambda hop: blocks(hop, project_block))
    spread_o.relay()
    spread_u.start()
    line.step(net.n_l - 1)
    gout_line.start()
    pairs(line, net.n_l - 1)
    blocks(net.n_l - 1, project_block)
    q_copy = copies.start(q, q_o)
    for pair_of in ((wq, wq_o), (k, k_o)):
        copies.start(*pair_of)
    spread_o.finish()
    line.finish()

    def attend(i):
        lo, hi = i * pair, (i + 1) * pair

        @pl.loop(0, heads)
        def _(head):
            lane = lax.broadcasted_iota(jnp.int32, (1, columns), 1)
            here = jnp.where(lane // HEAD == head, HEAD**-0.5, 0.0).astype(BF)
            visible = lax.broadcasted_iota(jnp.int32, (pair, pair), 0) <= lax.broadcasted_iota(
                jnp.int32, (pair, pair), 1
            )
            head_rows = aligned(head * HEAD, HEAD)
            query = q[lo:hi, :] * here
            near = jnp.where(visible, dot_nt(k[lo:hi, :], query), NEG_LARGE)
            highest = jnp.max(near, 0, keepdims=True)
            if i:
                far = dot_nt(k[0:lo, :], query)
                highest = jnp.maximum(highest, jnp.max(far, 0, keepdims=True))
            near = jnp.exp(near - highest)
            sum_of = jnp.sum(near, 0, keepdims=True)
            out = dot(vt[head_rows, lo:hi], near.astype(BF))
            if i:
                far = jnp.exp(far - highest)
                sum_of = sum_of + jnp.sum(far, 0, keepdims=True)
                out = out + dot(vt[head_rows, 0:lo], far.astype(BF))
            ot[head_rows, :] = out / sum_of
            lse_o[pl.ds(head, 1), lo:hi] = highest + jnp.log(sum_of)

        att[lo:hi, :] = ot[...].T.astype(BF)

    def produce_attended(place, write):
        for i in range(net.n_l):
            pl.when(place == i)(functools.partial(attend, i))
        left = att[aligned(place * pair, pair), :]

        @pl.loop(0, width // TILE)
        def _(j):
            cols = aligned(j * TILE, TILE)
            write(cols, dot(left, wo[:, cols]))

    def relays():
        gout_line.step(1)
        spread_d.start()

    att_fold.begin(produce_attended, relays)
    copies.start(att, att_o)
    copies.start(wo, wo_o)
    if net.n_l > 2:
        gout_line.step(2)
    att_fold.open_total()
    spread_g.relay()
    for at in range(1, net.n_l):
        if 2 < at + 1 < net.n_l:
            gout_line.step(at + 1)
        att_fold.wave(at)
        if at == 1:
            spread_u.relay()
        if at == min(2, net.n_l - 1):
            spread_d.relay()
    gain_two, shift_two = gains_o[2:3, :], gains_o[3:4, :]

    @pl.loop(0, chunk // 32, unroll=2)
    def _(i):
        span = aligned(i * 32, 32)
        value = rows[aligned(net.s * chunk + i * 32, 32), :].astype(F32) + total[span, :]
        mid[span, :] = value
        scaled, _ = normalize(value)
        low[span, :] = (scaled * gain_two + shift_two).astype(BF)

    n2_line.prepare()
    n2_line.start()
    att_fold.finish()
    gout_line.here()
    pl.loop(1, net.n_l)(lambda hop: pairs(gout_line, hop))

    def forward_block(other):
        span = aligned(other * pair, pair)
        right = rows[span, :]
        half = hidden.shape[0] // 2

        @pl.loop(0, 2)
        def _(part):
            units = aligned(part * half, half, 16)
            gate = dot_nt(wg[units, :], right)
            up = dot_nt(wu[units, :], right)
            back = dot_nt(wd[units, :], gout[span, :])
            sigma = jax.nn.sigmoid(gate)
            active = gate * sigma
            hidden[units, span] = (active * up).astype(BF)
            dgate[units, span] = (back * up * (sigma * (1.0 + gate * (1.0 - sigma)))).astype(BF)
            dup[units, span] = (back * active).astype(BF)

    def produce_normed(place, write):
        span = aligned(place * pair, pair)
        left, right = dgate[:, span].T, dup[:, span].T

        @pl.loop(0, width // TILE)
        def _(j):
            cols = aligned(j * TILE, TILE)
            write(cols, dot(left, wg[:, cols]) + dot(right, wu[:, cols]))

    def begin_normed(other, side, hop):
        @pl.when(hop > 1)
        def _():
            normed_fold.mate_sent(side)

        normed_fold.begin_one(other, side + (2 - side) * (1 // (hop + 1)), produce_normed)

    def forward_blocks(hop):
        def act(other, side):
            forward_block(other)

            @pl.when(jnp.logical_not(normed_fold.fed(side)))
            def _():
                begin_normed(other, side, hop)
                normed_fold.leave(other, side, hop)

        net.sides(hop, act)

    def begin_fed(hop):
        def act(other, side):
            pl.when(normed_fold.fed(side))(lambda: begin_normed(other, side, hop))

        net.sides(hop, act)

    n2_line.here()
    for spread in (spread_g, spread_u, spread_d):
        spread.finish()
    forward_block(net.z)

    @pl.loop(1, net.n_l)
    def _(hop):
        n2_line.step(hop)
        pairs(n2_line, hop)
        pl.when(hop == 1)(lambda: normed_fold.begin_one(net.z, 2, produce_normed))
        forward_blocks(hop)
        pl.when(hop > 1)(lambda: begin_fed(hop - 1))

    begin_fed(net.n_l - 1)

    def weight_terms(task):
        at, kind = net.n_f - 1 - task // 3, task % 3
        cols = aligned(gate_sum.owner(at) * depth, depth)
        for way, (grid_sum, left, right) in enumerate(
            ((down_sum, hidden, gout), (gate_sum, dgate, rows), (up_sum, dup, rows))
        ):

            @pl.when(kind == way)
            def _():
                half = left.shape[0] // 2

                @pl.loop(0, 2)
                def _(part):
                    units = aligned(part * half, half, 16)
                    grid_sum.stage[at, units, :] = dot(left[units, :], right[:, cols]).astype(BF)

                grid_sum.first(at)

    tasks = 3 * net.n_f
    waves = max(net.n_l - 2, 1)
    each = -(-tasks // (2 * normed_fold.pieces * waves))
    for wave in range(net.n_l - waves, net.n_l):

        def between(turn, piece):
            slot = ((wave - net.n_l + waves) * 2 + turn) * normed_fold.pieces + piece

            @pl.loop(0, each)
            def _(i):
                pl.when(slot * each + i < tasks)(lambda: weight_terms(slot * each + i))

        normed_fold.passes_between(wave, True, between)
    normed_fold.finals()
    n2_line.finish()

    def beside(act):
        act(net.mate)
        for side in range(2):
            pl.when(n2_line.goes_on(side))(lambda: act(net.s + 2 - 4 * side))

    beside(lambda to: pl.semaphore_signal(free_sem, 1, device_id={"seq": to}, device_id_type=MESH))

    def write_middle(i, span, value):
        value = value + gout[aligned(net.s * chunk + i * 32, 32), :].astype(F32)
        dmid_o[span, :] = value
        low[span, :] = value.astype(BF)

    terms_o[...] = jnp.zeros(terms_o.shape, F32)
    norm_backward(chunk, mid, total, gain_two, terms_o, 2, write_middle)
    ends = (net.z + net.n_l - 1) // net.n_l + (2 * net.n_l - 2 - net.z) // net.n_l
    pl.semaphore_wait(free_sem, 1 + ends)
    dm_line.prepare()
    dm_line.start()
    normed_fold.finish()

    def produce_top(place, write):
        left = hidden[:, aligned(place * pair, pair)].T

        @pl.loop(0, width // TILE)
        def _(j):
            cols = aligned(j * TILE, TILE)
            write(cols, dot(left, wd[:, cols]))

    copies.wait(q_copy)
    datt = q

    def back_block(other, side):
        span = aligned(other * pair, pair)
        datt[span, :] = dot_nt(rows[span, :], wo[...]).astype(BF)

    dm_line.here()
    dm_line.step(1)
    top_fold.begin(produce_top)
    back_block(net.z, 0)
    top_fold.open_total()
    for at in range(1, net.n_l):
        if at + 1 < net.n_l:
            dm_line.step(at + 1)
        top_fold.wave(at)
        pairs(dm_line, at)
        net.sides(at, back_block)
    copies.start(datt, datt_o)
    copies.start(rows, dm_o)

    @pl.loop(0, chunk // 32)
    def _(i):
        span = aligned(i * 32, 32)
        top_fold.out[net.z, span, :] = (mid[span, :] + total[span, :]).astype(BF)

    copies.start(top_fold.out.at[net.z], top_o)
    top_fold.finish()
    gout_line.finish()
    dm_line.finish()
    hands = []
    for grid_sum, out in zip(sums, (down_o, gate_o, up_o)):
        grid_sum.sum_first()
        hands.extend(grid_sum.hand_on(out))
        for copy in grid_sum.hand_on(out):
            copy.start()
    for grid_sum in sums:
        grid_sum.finish_first()
    for copy in hands:
        copy.wait()
    copies.wait()


def layer_part(tokens, norms, wq, wo, wg, wu, wd, gout, tables):
    chunk, width = tokens.shape
    n_f, n_s = lax.axis_size("fsdp"), lax.axis_size("seq")
    length = chunk * n_s
    depth, columns = wq.shape[1:]
    units = wg.shape[0]
    shape = jax.ShapeDtypeStruct
    wide, head, turned, weight = (length, width), (length, columns), (units, length), (units, width)
    return pl.pallas_call(
        layer_kernel,
        name="layer",
        out_shape=[
            shape(head, BF),
            shape(head, BF),
            shape((columns, length), BF),
            shape(head, BF),
            shape(head, BF),
            shape((8, length), F32),
            shape(wide, BF),
            shape((SMALL, width), F32),
            shape((3, width, columns), BF),
            shape((columns, width), BF),
            shape(wide, BF),
            shape(head, BF),
            shape((chunk, width), F32),
            shape((chunk, width), BF),
            shape((SMALL, width), F32),
            *[shape((GridEnd.count(n_f), units // 2, depth), BF)] * 3,
        ],
        in_specs=[ANY, *[VMEM] * 5, *[ANY] * 6, VMEM, VMEM],
        out_specs=[*[ANY] * 5, VMEM, ANY, VMEM, *[ANY] * 4, VMEM, ANY, VMEM, *[ANY] * 3],
        scratch_shapes=[
            pltpu.VMEM(wide, BF),
            pltpu.VMEM(wide, BF),
            pltpu.VMEM((3, width, columns), BF),
            pltpu.VMEM((columns, width), BF),
            *[pltpu.VMEM(weight, BF)] * 3,
            pltpu.VMEM(head, BF),
            pltpu.VMEM(head, BF),
            pltpu.VMEM((columns, 2 * chunk), BF),
            pltpu.VMEM((2 * chunk, columns), BF),
            pltpu.VMEM((columns, length), BF),
            pltpu.VMEM((columns, 2 * chunk), F32),
            pltpu.VMEM(head, BF),
            *[pltpu.VMEM(turned, BF)] * 3,
            pltpu.VMEM((chunk, width), F32),
            pltpu.VMEM((chunk, width), BF),
            pltpu.VMEM((SMALL, 128), F32),
            pltpu.VMEM((n_s, n_f, SMALL, 128), F32),
            *Fold.shared(chunk, width),
            *Fold.buffers(n_s, chunk, width),
            *Fold.sems(n_s) * 3,
            *Line.sems(n_s) * 4,
            *[pltpu.SemaphoreType.DMA((Spread.count(n_f),))] * 5,
            *GridSum.scratch(n_f, units, depth) * 3,
            pltpu.SemaphoreType.DMA((Packets.count(n_f, n_s),)),
            pltpu.SemaphoreType.DMA((8,)),
            pltpu.SemaphoreType.DMA((4,)),
            pltpu.SemaphoreType.REGULAR,
        ],
        compiler_params=pltpu.CompilerParams(
            collective_id=1, has_side_effects=True, vmem_limit_bytes=VMEM_BYTES
        ),
        cost_estimate=pl.CostEstimate(
            flops=2 * length * width * (4 * columns + 9 * units),
            bytes_accessed=8 * length * width,
            transcendentals=length * (length * columns // HEAD + units),
        ),
    )(tokens, *norms, wq, wo, wg, wu, wd, gout, *tables)


def back_kernel(
    datt_in,
    q_in,
    k_in,
    kt_in,
    v_in,
    att_in,
    wq_in,
    n1_in,
    dm_in,
    down_in,
    gate_in,
    up_in,
    lse,
    tok,
    dmid,
    gains,
    terms_in,
    cosine,
    sine,
    gin_o,
    small_o,
    out_o,
    qkv_o,
    down_o,
    gate_o,
    up_o,
    datt,
    q,
    k,
    kt,
    v,
    att,
    wq,
    n1,
    dm,
    query,
    upstream,
    inners,
    dk,
    dv,
    dqt,
    dproj,
    terms,
    tiles,
    total,
    *rest,
):
    net = Net()
    chunk, width = tok.shape
    length, columns = q_in.shape
    heads = columns // HEAD
    pair = 2 * chunk
    depth = width // net.n_f
    block = 256
    buffers, rest = rest[:4], rest[4:]
    fold_sems, rest = rest[:4], rest[4:]
    packet_scratch, rest = rest[:5], rest[5:]
    out_sum, qkv_sum = GridSum(net, *rest[:3]), GridSum(net, *rest[3:6])
    ends = [GridEnd(net, *rest[at : at + 3]) for at in (6, 9, 12)]
    copy_sems, column_sems = rest[15:]

    copies = Copies(copy_sems)
    loads = [
        copies.start(src, dst)
        for src, dst in (
            (datt_in, datt),
            (q_in, q),
            (k_in, k),
            (kt_in, kt),
            (v_in, v),
            (att_in, att),
            (wq_in, wq),
            (down_in, ends[0].sums),
            (gate_in, ends[1].sums),
            (up_in, ends[2].sums),
        )
    ]
    def load(at, way):
        src, dst = ((n1_in, n1), (dm_in, dm))[way]
        cols = aligned(qkv_sum.owner(at) * depth, depth)
        return pltpu.make_async_copy(src.at[:, cols], dst.at[at % 2], column_sems.at[way, at % 2])

    for at in range(net.n_f - 1, max(net.n_f - 3, -1), -1):
        for way in range(2):
            load(at, way).start()

    @pl.loop(0, length // block)
    def _(i):
        span = aligned(i * block, block)
        dk[span, :] = jnp.zeros((block, columns), F32)
        dv[span, :] = jnp.zeros((block, columns), F32)

    net.barrier()
    copies.wait(*loads[:6])

    def start_ends():
        for load_of in loads[7:]:
            load_of.wait()
        for end in ends:
            end.start()


    of_head = (
        lax.broadcasted_iota(jnp.int32, (8, columns), 1) // HEAD
        == lax.broadcasted_iota(jnp.int32, (8, columns), 0)
    ).astype(F32)

    @pl.loop(0, length // block)
    def _(i):
        span = aligned(i * block, block)
        product = datt[span, :].astype(F32) * att[span, :].astype(F32)
        inners[:, span] = lax.dot_general(
            of_head,
            product,
            (((1,), (1,)), ((), ())),
            precision=lax.Precision.HIGHEST,
            preferred_element_type=F32,
        )

    @pl.loop(0, heads)
    def _(head):
        lane = lax.broadcasted_iota(jnp.int32, (1, columns), 1)
        here = jnp.where(lane // HEAD == head, 1.0, 0.0).astype(BF)
        scale = HEAD**-0.5
        visible = lax.broadcasted_iota(jnp.int32, (block, block), 0) <= lax.broadcasted_iota(
            jnp.int32, (block, block), 1
        )
        head_rows = aligned(head * HEAD, HEAD)

        @pl.loop(0, length // block)
        def _(i):
            span = aligned(i * block, block)
            query[span, :] = q[span, :] * (here * scale)
            upstream[span, :] = datt[span, :] * here

        pl.when(head == min(1, heads - 1))(start_ends)

        for j in range(length // block):
            at, end = j * block, (j + 1) * block
            keys, values, turned = k[at:end, :], v[at:end, :], kt[head_rows, at:end]

            def part(lo, hi, near):
                probs = jnp.exp(dot_nt(keys, query[lo:hi, :]) - lse[pl.ds(head, 1), lo:hi])
                if near:
                    probs = jnp.where(visible, probs, 0.0)
                grads = dot_nt(values, upstream[lo:hi, :])
                scores = (probs * (grads - inners[pl.ds(head, 1), lo:hi])).astype(BF)
                out = dot(turned, scores)
                dqt[head_rows, lo:hi] = dqt[head_rows, lo:hi] + out if j else out
                return dot(probs.astype(BF), upstream[lo:hi, :]), dot(scores, query[lo:hi, :])

            value_grads, key_grads = part(at, end, True)
            if end < length:
                more_values, more_keys = part(end, length, False)
                value_grads, key_grads = value_grads + more_values, key_grads + more_keys
            dv[at:end, :] = dv[at:end, :] + value_grads
            dk[at:end, :] = dk[at:end, :] + key_grads

    terms[...] = terms_in[...]
    bias_cols = aligned(net.s * columns, columns)

    @pl.loop(0, length // block)
    def _(i):
        span = aligned(i * block, block)
        tables = cosine[span, :], -sine[span, :]
        parts = [
            rotary((dqt[:, span].T * HEAD**-0.5).astype(BF).astype(F32), *tables).astype(BF),
            rotary(dk[span, :].astype(BF).astype(F32), *tables).astype(BF),
            dv[span, :].astype(BF),
        ]
        for kind in range(3):
            dproj[kind, span, :] = parts[kind]
            row = slice(4 + kind, 5 + kind)
            terms[row, bias_cols] = terms[row, bias_cols] + jnp.sum(parts[kind].astype(F32), 0, keepdims=True)

    def weight_terms(task):
        at = net.n_f - 1 - task // 2

        def loaded(way):
            load(at, way).wait()

        def next_load(way):
            pl.when(at >= 2)(lambda: load(at - 2, way).start())

        @pl.when(task % 2 == 0)
        def _():
            loaded(0)
            left = n1[at % 2].T
            for kind in range(3):
                qkv_sum.stage[at, kind * depth : (kind + 1) * depth, :] = dot(left, dproj[kind]).astype(BF)
            next_load(0)
            qkv_sum.first(at)

        @pl.when(task % 2 == 1)
        def _():
            loaded(1)
            out_sum.stage[at] = dot_tn(att[...], dm[at % 2]).astype(BF)
            next_load(1)
            out_sum.first(at)

    def produce(place, write):
        span = aligned(place * pair, pair)

        @pl.loop(0, width // TILE)
        def _(j):
            cols = aligned(j * TILE, TILE)
            value = dot_nt(dproj[0, span, :], wq[0, cols, :])
            for kind in range(1, 3):
                value = value + dot_nt(dproj[kind, span, :], wq[kind, cols, :])
            write(cols, value)

    fold = Fold(net, tiles, total, *buffers, *fold_sems)
    copies.wait(loads[6])
    tasks = 2 * net.n_f
    ahead = 2 * (net.n_l - 1)

    def meanwhile(task):
        pl.when(task < tasks)(lambda: weight_terms(task))

    fold.begin(produce, meanwhile=meanwhile)
    fold.open_total()
    waves = max(net.n_l - 2, 1)
    each = -(-max(tasks - ahead, 0) // (2 * fold.pieces * waves))

    def between(slot):
        @pl.loop(0, each)
        def _(i):
            task = ahead + slot * each + i
            pl.when(task < tasks)(lambda: weight_terms(task))

    for at in range(1, waves + 1):
        fold.wave(at, between=between)
    for grid_sum in (qkv_sum, out_sum):
        grid_sum.second()
    for at in range(waves + 1, net.n_l):
        fold.wave(at)

    def write_input(i, span, value):
        gin_o[span, :] = value + dmid[span, :]

    norm_backward(chunk, tok, total, gains[0:1, :], terms, 0, write_input)
    packet_sum = PacketSum(net, *packet_scratch)
    packet_sum.start(terms, width // (net.n_f * net.n_s))
    packet_sum.middle()
    for end, out in zip(ends, (down_o, gate_o, up_o)):
        end.last(out)
    packet_sum.finish(small_o)
    fold.finish()
    for grid_sum, out in ((qkv_sum, qkv_o), (out_sum, out_o)):
        grid_sum.last(out)
        grid_sum.finish()


def back_part(datt, q, k, kt, v, att, wq, n1, dm, down, gate, up, lse, tokens, dmid, gains, terms, tables):
    chunk, width = tokens.shape
    n_f, n_s = lax.axis_size("fsdp"), lax.axis_size("seq")
    length, columns = q.shape
    depth = width // n_f
    units = 2 * gate.shape[1]
    shape = jax.ShapeDtypeStruct
    return pl.pallas_call(
        back_kernel,
        name="back",
        out_shape=[
            shape((chunk, width), F32),
            shape((SMALL, 128), F32),
            shape((columns, depth), F32),
            shape((3 * depth, columns), F32),
            *[shape((units, depth), F32)] * 3,
        ],
        in_specs=[ANY] * 12 + [VMEM] * 7,
        out_specs=[VMEM] * 7,
        scratch_shapes=[
            pltpu.VMEM((length, columns), BF),
            pltpu.VMEM((length, columns), BF),
            pltpu.VMEM((length, columns), BF),
            pltpu.VMEM((columns, length), BF),
            pltpu.VMEM((length, columns), BF),
            pltpu.VMEM((length, columns), BF),
            pltpu.VMEM((3, width, columns), BF),
            pltpu.VMEM((2, length, depth), BF),
            pltpu.VMEM((2, length, depth), BF),
            pltpu.VMEM((length, columns), BF),
            pltpu.VMEM((length, columns), BF),
            pltpu.VMEM((8, length), F32),
            pltpu.VMEM((length, columns), F32),
            pltpu.VMEM((length, columns), F32),
            pltpu.VMEM((columns, length), F32),
            pltpu.VMEM((3, length, columns), BF),
            pltpu.VMEM((SMALL, width), F32),
            *Fold.shared(chunk, width),
            *Fold.buffers(n_s, chunk, width),
            *Fold.sems(n_s, 8),
            *PacketSum.scratch(n_f, n_s),
            *GridSum.scratch(n_f, columns, depth),
            *GridSum.scratch(n_f, 3 * depth, columns),
            *GridEnd.scratch(n_f, units, depth) * 3,
            pltpu.SemaphoreType.DMA((10,)),
            pltpu.SemaphoreType.DMA((2, 2)),
        ],
        compiler_params=pltpu.CompilerParams(
            collective_id=3, has_side_effects=True, vmem_limit_bytes=VMEM_BYTES
        ),
        cost_estimate=pl.CostEstimate(
            flops=2 * length * columns * (8 * width + 5 * length),
            bytes_accessed=4 * length * width,
            transcendentals=length * length * columns // HEAD,
        ),
    )(datt, q, k, kt, v, att, wq, n1, dm, down, gate, up, lse, tokens, dmid, gains, terms, *tables)


def outputs_kernel(small, *refs):
    sources, targets, parts = refs[:7], refs[7:14], refs[14:]
    own = parts[0].shape[1]
    for src, dst in zip(sources, targets):
        dst[...] = src[...]
    for at in range(4):
        parts[at][...] = small[at : at + 1, 0:own]
    parts[4][...] = small[4:7, 0:own]


def outputs_part(small, own, *arrays):
    shape = jax.ShapeDtypeStruct
    return pl.pallas_call(
        outputs_kernel,
        name="outputs",
        out_shape=[shape(v.shape, v.dtype) for v in arrays]
        + [shape((1, own), F32)] * 4
        + [shape((3, own), F32)],
        in_specs=[VMEM] * 8,
        out_specs=[VMEM] * 12,
        compiler_params=pltpu.CompilerParams(vmem_limit_bytes=VMEM_BYTES),
    )(small, *arrays)


def per_device(
    tokens,
    gain_one,
    shift_one,
    w_qkv,
    b_qkv,
    w_out,
    gain_two,
    shift_two,
    w_gate,
    w_up,
    w_down,
    grad_output,
):
    length = tokens.shape[1] * lax.axis_size("seq")
    width = gain_one.shape[0]
    norms = [v[None] for v in (gain_one, shift_one, gain_two, shift_two)] + [b_qkv]
    tables = rotary_tables(length)
    q, k, kt, v, att, lse, n1, gains, wq, _, dm, datt, dmid, top, terms, gate, up, down = layer_part(
        tokens[0], norms, w_qkv.transpose(1, 0, 2), w_out, w_gate.T, w_up.T, w_down, grad_output[0], tables
    )
    grad_input, small, out, qkv, down, gate, up = back_part(
        datt, q, k, kt, v, att, wq, n1, dm, down, gate, up, lse, tokens[0], dmid, gains, terms, tables
    )

    top, grad_input, qkv, out, gate, up, down, one, shift, two, shift_to, bias = outputs_part(
        small, width, top, grad_input, qkv, out, gate, up, down
    )
    return (
        top[None],
        grad_input[None],
        one[0],
        shift[0],
        qkv.reshape(3, -1, qkv.shape[1]).transpose(1, 0, 2),
        bias,
        out,
        two[0],
        shift_to[0],
        gate.T,
        up.T,
        down,
    )


def solution(mesh):
    whole = P(("fsdp", "seq"))
    rows = P("fsdp", "seq", None)
    inner = P("seq", "fsdp")
    outer = P("fsdp", "seq")
    heads = P("fsdp", None, "seq")
    bias = P(None, ("fsdp", "seq"))
    return jax.shard_map(
        per_device,
        mesh=mesh,
        in_specs=(rows, whole, whole, heads, bias, inner, whole, whole, outer, outer, inner, rows),
        out_specs=(rows, rows, whole, whole, heads, bias, inner, whole, whole, outer, outer, inner),
        check_vma=False,
    )
```

```python
import functools

import jax
import jax.numpy as jnp
import numpy as np
from jax import lax
from jax.experimental import pallas as pl
from jax.experimental.pallas import tpu as pltpu
from jax.sharding import PartitionSpec as P

HEAD = 64
ROT = 16
EPSILON = 1e-05
NEG_LARGE = -1e30
MESH = pl.DeviceIdType.MESH
ANY = pl.BlockSpec(memory_space=pl.ANY)
VMEM = pl.BlockSpec(memory_space=pltpu.VMEM)
BF = jnp.bfloat16
F32 = jnp.float32
VMEM_BYTES = 60 * 2**20
TILE = 512
SMALL = 8


def put(src, dst, send, recv, **device):
    return pltpu.make_async_remote_copy(
        src_ref=src, dst_ref=dst, send_sem=send, recv_sem=recv, device_id=device, device_id_type=MESH
    )


def dot(left, right):
    return jnp.dot(left, right, preferred_element_type=F32)


def dot_nt(left, right):
    return lax.dot_general(left, right, (((1,), (1,)), ((), ())), preferred_element_type=F32)


def dot_tn(left, right):
    return lax.dot_general(left, right, (((0,), (0,)), ((), ())), preferred_element_type=F32)


def aligned(start, size, unit=None):
    return pl.ds(pl.multiple_of(start, unit or size), size)


class Net:
    def __init__(self):
        self.n_f, self.n_s = lax.axis_size("fsdp"), lax.axis_size("seq")
        self.tall = 2 if self.n_f % 2 == 0 else 1
        self.wide = self.n_f // self.tall
        self.n_l = self.n_s // 2
        self.f, self.s = lax.axis_index("fsdp"), lax.axis_index("seq")
        self.a, self.b = self.f // self.wide, self.f % self.wide
        self.z, self.c = self.s // 2, self.s % 2
        self.mate = self.s + 1 - 2 * self.c

    def barrier(self):
        sem = pltpu.get_barrier_semaphore()
        for k in range(1, self.n_f):
            pl.semaphore_signal(
                sem, inc=1, device_id={"fsdp": (self.f + k) % self.n_f}, device_id_type=MESH
            )
        for k in range(1, self.n_s):
            pl.semaphore_signal(
                sem, inc=1, device_id={"seq": (self.s + k) % self.n_s}, device_id_type=MESH
            )
        pl.semaphore_wait(sem, self.n_f + self.n_s - 2)

    def sides(self, hop, act):
        @pl.loop(0, 2)
        def _(side):
            other = self.z + (2 * side - 1) * hop

            @pl.when((other >= 0) & (other < self.n_l))
            def _():
                act(other, side)


class Spread:
    def __init__(self, net, src, part, sems):
        self.net, self.src, self.part, self.sems = net, src, part, sems
        self.rows = [j for j in range(1, net.wide)]
        self.cols = [i for i in range(1, net.tall)]

    @staticmethod
    def count(n_f):
        tall = 2 if n_f % 2 == 0 else 1
        wide = n_f // tall
        return 1 + 2 * (wide - 1) + 2 * (tall - 1) + 4 * (wide - 1) * (tall - 1)

    def at(self, kind, i, j):
        w, t = len(self.rows), len(self.cols)
        base = {
            "own": 0,
            "row": 1,
            "col": 1 + 2 * w,
            "half0": 1 + 2 * w + 2 * t,
            "half1": 1 + 2 * w + 2 * t + 2 * w * t,
        }[kind]
        if kind == "own":
            return self.sems.at[0]
        k = j - 1 if kind == "row" else i - 1 if kind == "col" else (i - 1) * w + j - 1
        return self.sems.at[base + 2 * k], self.sems.at[base + 2 * k + 1]

    def rank(self, i, j):
        net = self.net
        return ((net.a + i) % net.tall) * net.wide + (net.b + j) % net.wide

    def back(self, i, j):
        net = self.net
        return ((net.a - i + net.tall) % net.tall) * net.wide + (net.b - j + net.wide) % net.wide

    def own(self):
        return pltpu.make_async_copy(self.src, self.part(self.net.f, None), self.at("own", 0, 0))

    def first(self, i, j):
        send, recv = self.at("row" if i == 0 else "col", i, j)
        place = self.part(self.net.f, None)
        return put(place, place, send, recv, fsdp=self.rank(i, j))

    def came(self, i, j):
        send, recv = self.at("row" if i == 0 else "col", i, j)
        place = self.part(self.back(i, j), None)
        return put(place, place, send, recv, fsdp=self.rank(i, j))

    def second(self, half, i, j, came=False):
        send, recv = self.at("half0" if half == 0 else "half1", i, j)
        origin = self.back(i, j) if came else self.back(0, j) if half == 0 else self.back(i, 0)
        place = self.part(origin, half)
        return put(place, place, send, recv, fsdp=self.rank(i, 0) if half == 0 else self.rank(0, j))

    def prepare(self):
        self.own().start()

    def start(self):
        self.own().wait()
        for i in self.cols:
            self.first(i, 0).start()
        for j in self.rows:
            self.first(0, j).start()

    def relay(self):
        for j in self.rows:
            self.came(0, j).wait_recv()
            for i in self.cols:
                self.second(0, i, j).start()
        for i in self.cols:
            self.came(i, 0).wait_recv()
            for j in self.rows:
                self.second(1, i, j).start()

    def finish(self):
        for j in self.rows:
            self.first(0, j).wait_send()
        for i in self.cols:
            self.first(i, 0).wait_send()
        for i in self.cols:
            for j in self.rows:
                for half in range(2):
                    self.second(half, i, j, came=True).wait_recv()
                    self.second(half, i, j).wait_send()


class Line:
    def __init__(self, net, src, part, recv, send, local):
        self.net, self.src, self.part, self.recv, self.send, self.local = net, src, part, recv, send, local
        self.pieces = recv.shape[1]
        self.rows = src.shape[0] // self.pieces

    @staticmethod
    def sems(n_s, pieces=2):
        return [
            pltpu.SemaphoreType.DMA((n_s, pieces)),
            pltpu.SemaphoreType.DMA((4, n_s // 2, pieces)),
            pltpu.SemaphoreType.DMA((1,)),
        ]

    def cut(self, ref, piece):
        return ref.at[aligned(piece * self.rows, self.rows)]

    def own(self):
        return pltpu.make_async_copy(self.src, self.part(self.net.s), self.local.at[0])

    def on_line(self, src, chunk, side, hop, piece):
        return put(
            self.cut(src, piece),
            self.cut(self.part(chunk), piece),
            self.send.at[side, hop, piece],
            self.recv.at[chunk, piece],
            seq=self.net.s + 2 - 4 * side,
        )

    def to_mate(self, src, chunk, side, hop, piece):
        return put(
            self.cut(src, piece),
            self.cut(self.part(chunk), piece),
            self.send.at[2 + side, hop, piece],
            self.recv.at[chunk, piece],
            seq=self.net.mate,
        )

    def goes_on(self, side):
        after = self.net.z + 1 - 2 * side
        return (after >= 0) & (after < self.net.n_l)

    def each_piece(self, act):
        pl.loop(0, self.pieces)(act)

    def prepare(self):
        self.own().start()

    def start(self):
        net = self.net
        self.own().wait()
        place = self.part(net.s)

        @self.each_piece
        def _(piece):
            for side in range(2):

                @pl.when(self.goes_on(side))
                def _():
                    self.on_line(place, net.s, side, 0, piece).start()

            self.to_mate(place, net.s, 0, 0, piece).start()

    def came(self, chunk, piece):
        place = self.cut(self.part(chunk), piece)
        put(place, place, self.send.at[0, 0, 0], self.recv.at[chunk, piece], seq=self.net.mate).wait_recv()

    def step(self, hop):
        net = self.net

        @self.each_piece
        def _(piece):
            def act(other, side):
                chunk = 2 * other + net.c
                self.came(chunk, piece)

                @pl.when(self.goes_on(side))
                def _():
                    self.on_line(self.part(chunk), chunk, side, hop, piece).start()

                self.to_mate(self.part(chunk), chunk, side, hop, piece).start()

            net.sides(hop, act)

    def pair(self, other):
        @self.each_piece
        def _(piece):
            self.came(2 * other + 1 - self.net.c, piece)

    def here(self):
        self.pair(self.net.z)

    def finish(self):
        net = self.net
        place = self.part(net.s)

        @self.each_piece
        def _(piece):
            for side in range(2):

                @pl.when(self.goes_on(side))
                def _():
                    self.on_line(place, net.s, side, 0, piece).wait_send()

            self.to_mate(place, net.s, 0, 0, piece).wait_send()

            @pl.loop(1, net.n_l)
            def _(hop):
                def act(other, side):
                    chunk = 2 * other + net.c

                    @pl.when(self.goes_on(side))
                    def _():
                        self.on_line(self.part(chunk), chunk, side, hop, piece).wait_send()

                    self.to_mate(self.part(chunk), chunk, side, hop, piece).wait_send()

                net.sides(hop, act)


class Packets:
    def __init__(self, net, src, buf, sems):
        self.net, self.src, self.buf, self.sems = net, src, buf, sems

    @staticmethod
    def count(n_f, n_s):
        return 1 + 2 * (n_f - 1) + 2 * (n_s - 1)

    def own(self):
        net = self.net
        return pltpu.make_async_copy(self.src, self.buf.at[net.s, net.f], self.sems.at[0])

    def one(self, k, came=False):
        net = self.net
        f = (net.f - k + net.n_f) % net.n_f if came else net.f
        place = self.buf.at[net.s, f]
        return put(
            place if came else self.src,
            place,
            self.sems.at[2 * k - 1],
            self.sems.at[2 * k],
            fsdp=(net.f + k) % net.n_f,
        )

    def two(self, k, came=False):
        net = self.net
        place = self.buf.at[(net.s - k + net.n_s) % net.n_s if came else net.s]
        at = 2 * (net.n_f - 1) + 2 * k - 1
        return put(place, place, self.sems.at[at], self.sems.at[at + 1], seq=(net.s + k) % net.n_s)

    def start(self):
        self.own().start()
        for k in range(1, self.net.n_f):
            self.one(k).start()

    def middle(self):
        self.own().wait()
        for k in range(1, self.net.n_f):
            self.one(k, came=True).wait_recv()
            self.one(k).wait_send()
        for k in range(1, self.net.n_s):
            self.two(k).start()

    def finish(self):
        for k in range(1, self.net.n_s):
            self.two(k, came=True).wait_recv()
            self.two(k).wait_send()

    def unpack(self, out, width):
        net = self.net
        per = 128 // width
        for tile in range(net.n_f * net.n_s // per):
            total = None
            for j in range(per):
                f, s = divmod(tile * per + j, net.n_s)
                piece = self.buf[s, f]
                if j:
                    piece = pltpu.roll(piece, j * width, axis=1)
                total = piece if total is None else total + piece
            out[:, tile * 128 : (tile + 1) * 128] = total


def rotary(values, cosine, sine):
    columns = values.shape[1]
    half = ROT // 2
    times = columns // 128

    def wide(table):
        return table if times == 1 else jnp.concatenate([table] * times, axis=1)

    lane = lax.broadcasted_iota(jnp.int32, values.shape, 1)
    other = jnp.where(
        lane % HEAD < half, pltpu.roll(values, columns - half, axis=1), pltpu.roll(values, half, axis=1)
    )
    return values * wide(cosine) + other * wide(sine)


def rotary_tables(length):
    half = ROT // 2
    freqs = np.float32(10000.0) ** (-np.arange(half, dtype=np.float32) * np.float32(2.0 / ROT))
    angles = np.arange(length, dtype=np.float32)[:, None] * freqs[None, :].astype(np.float32)
    cosine, sine = np.cos(angles), np.sin(angles)
    rest = np.zeros((length, HEAD - ROT), np.float32)
    keep = np.concatenate([cosine, cosine, rest + 1], 1)
    swap = np.concatenate([-sine, sine, rest], 1)
    return [np.tile(t, (1, 128 // HEAD)).astype(np.float32) for t in (keep, swap)]


def normalize(values):
    center = values - jnp.mean(values, -1, keepdims=True)
    inverse = lax.rsqrt(jnp.mean(center * center, -1, keepdims=True) + EPSILON)
    return center * inverse, inverse


class Copies:
    def __init__(self, sems):
        self.sems, self.all, self.open = sems, [], []

    def start(self, src, dst):
        copy = pltpu.make_async_copy(src, dst, self.sems.at[len(self.all)])
        copy.start()
        self.all.append(copy)
        self.open.append(copy)
        return copy

    def wait(self, *copies):
        for copy in copies or list(self.open):
            copy.wait()
            self.open = [c for c in self.open if c is not copy]


def columns_of(ref, depth):
    half_rows = ref.shape[0] // 2

    def part(f, half):
        span = aligned(f * depth, depth)
        if half is None:
            return ref.at[:, span]
        return ref.at[pl.ds(half * half_rows, half_rows), span]

    return part


def rows_of(ref, chunk):
    return lambda s: ref.at[aligned(s * chunk, chunk)]


class Fold:
    def __init__(self, net, tile, total, mate_in, coming, mate_out, out, mate_send, mate_recv, send, recv):
        self.net, self.tile, self.total = net, tile, total
        self.mate_in, self.coming, self.mate_out, self.out = mate_in, coming, mate_out, out
        self.mate_send, self.mate_recv, self.send, self.recv = mate_send, mate_recv, send, recv
        self.chunk = total.shape[0]
        self.pieces = recv.shape[1]
        self.rows = self.chunk // self.pieces

    @staticmethod
    def shared(chunk, width):
        return [pltpu.VMEM((2 * chunk, TILE), F32), pltpu.VMEM((chunk, width), F32)]

    @staticmethod
    def buffers(n_s, chunk, width):
        n_l = n_s // 2
        return [
            pltpu.VMEM((n_l, chunk, width), BF),
            pltpu.VMEM((n_l + 1, chunk, width), BF),
            pltpu.VMEM((3, chunk, width), BF),
            pltpu.VMEM((n_l, chunk, width), BF),
        ]

    @staticmethod
    def sems(n_s, pieces=4):
        n_l = n_s // 2
        return [
            pltpu.SemaphoreType.DMA((3, pieces)),
            pltpu.SemaphoreType.DMA((n_l, pieces)),
            pltpu.SemaphoreType.DMA((n_l, pieces)),
            pltpu.SemaphoreType.DMA((n_l + 1, pieces)),
        ]

    def place(self, other):
        return (other >= 0) & (other < self.net.n_l)

    def fed(self, side):
        return self.place(self.net.z + 1 - 2 * side)

    def span(self, piece):
        return aligned(piece * self.rows, self.rows)

    def each_piece(self, act):
        pl.loop(0, self.pieces)(act)

    def to_mate(self, target, slot, piece):
        span = self.span(piece)
        return put(
            self.mate_out.at[slot, span],
            self.mate_in.at[target, span],
            self.mate_send.at[slot, piece],
            self.mate_recv.at[target, piece],
            seq=self.net.mate,
        )

    def onward(self, target, side, hop, piece):
        span = self.span(piece)
        slot = target + (self.net.n_l - target) * (1 - side) * (1 // hop)
        return put(
            self.out.at[target, span],
            self.coming.at[slot, span],
            self.send.at[target, piece],
            self.recv.at[slot, piece],
            seq=self.net.s + 4 * side - 2,
        )

    def came(self, slot, piece):
        place = self.coming.at[slot, self.span(piece)]
        put(place, place, self.send.at[0, 0], self.recv.at[slot, piece], seq=self.net.mate).wait_recv()

    def mate_sent(self, slot):
        self.each_piece(lambda piece: self.to_mate(self.net.z, slot, piece).wait_send())

    def begin_one(self, target, slot, produce):
        mine = aligned(self.net.c * self.chunk, self.chunk)
        theirs = aligned((1 - self.net.c) * self.chunk, self.chunk)

        def write(cols, value):
            self.tile[...] = value
            self.out[target, :, cols] = self.tile[mine, :].astype(BF)
            self.mate_out[slot, :, cols] = self.tile[theirs, :].astype(BF)

        produce(target, write)
        self.each_piece(lambda piece: self.to_mate(target, slot, piece).start())

    def leave(self, target, side, hop):
        @pl.when((hop > 0) & jnp.logical_not(self.fed(side)))
        def _():
            self.each_piece(lambda piece: self.pass_piece(target, side, hop, piece, False))

    def begin(self, produce, between=None):
        net = self.net

        @pl.loop(0, net.n_l)
        def _(j):
            hop = net.n_l - 1 - j

            def act(target, side):
                @pl.when((hop > 0) | (side == 0))
                def _():
                    @pl.when((hop > 0) & self.place(target + 2 * side - 1))
                    def _():
                        self.mate_sent(side)

                    self.begin_one(target, side + (2 - side) * (1 // (hop + 1)), produce)
                    self.leave(target, side, hop)

            net.sides(hop, act)
            if between is not None:
                pl.when(j == 1)(between)

    def pass_piece(self, target, side, hop, piece, fed):
        self.to_mate(target, 0, piece).wait_recv()
        span = self.span(piece)
        value = self.out[target, span, :].astype(F32) + self.mate_in[target, span, :].astype(F32)
        if fed:
            self.came(target, piece)
            value = value + self.coming[target, span, :].astype(F32)
        self.out[target, span, :] = value.astype(BF)
        self.onward(target, side, hop, piece).start()

    def open_total(self):
        net = self.net

        @self.each_piece
        def _(piece):
            self.to_mate(net.z, 0, piece).wait_recv()
            span = self.span(piece)
            self.total[span, :] = self.out[net.z, span, :].astype(F32) + self.mate_in[net.z, span, :].astype(F32)

    def wave(self, at, near=False, between=None):
        net = self.net
        above = at if near else net.n_l - at

        @pl.loop(0, 2)
        def _(turn):
            side = (1 - (2 * net.z) // net.n_l + turn) % 2
            target = net.n_l - 1 - above + (2 * above - net.n_l + 1) * side
            hop = (target - net.z) * (2 * side - 1)

            @self.each_piece
            def _(piece):
                span = self.span(piece)

                @pl.when(self.fed(side) & (hop > 0))
                def _():
                    self.pass_piece(target, side, hop, piece, True)

                @pl.when(self.fed(side) & (hop == 0))
                def _():
                    slot = net.z + (net.n_l - net.z) * (1 - side)
                    self.came(slot, piece)
                    self.total[span, :] = self.total[span, :] + self.coming[slot, span, :].astype(F32)

                if between is not None:
                    between(((at - 1) * 2 + turn) * self.pieces + piece)

    def passes_between(self, wave, near, between):
        net = self.net
        above = wave if near else net.n_l - wave

        @pl.loop(0, 2)
        def _(turn):
            side = (1 - (2 * net.z) // net.n_l + turn) % 2
            target = net.n_l - 1 - above + (2 * above - net.n_l + 1) * side
            hop = (target - net.z) * (2 * side - 1)

            @self.each_piece
            def _(piece):
                @pl.when((hop > 0) & self.fed(side))
                def _():
                    self.pass_piece(target, side, hop, piece, True)

                between(turn, piece)

    def finals(self):
        net = self.net

        @self.each_piece
        def _(piece):
            self.to_mate(net.z, 0, piece).wait_recv()
            span = self.span(piece)
            self.total[span, :] = self.out[net.z, span, :].astype(F32) + self.mate_in[net.z, span, :].astype(F32)

        @pl.loop(0, 2)
        def _(turn):
            side = (1 - (2 * net.z) // net.n_l + turn) % 2

            @pl.when(self.fed(side))
            def _():
                slot = net.z + (net.n_l - net.z) * (1 - side)

                @self.each_piece
                def _(piece):
                    span = self.span(piece)
                    self.came(slot, piece)
                    self.total[span, :] = self.total[span, :] + self.coming[slot, span, :].astype(F32)

    def finish(self):
        net = self.net
        self.mate_sent(2)
        for side in range(2):
            pl.when(self.place(net.z + 2 * side - 1))(functools.partial(self.mate_sent, side))

        @pl.loop(1, net.n_l)
        def _(hop):
            net.sides(
                hop,
                lambda target, side: self.each_piece(
                    lambda piece: self.onward(target, side, hop, piece).wait_send()
                ),
            )


class GridSum:
    def __init__(self, net, stage, came, sems):
        self.net, self.stage, self.came, self.sems = net, stage, came, sems
        self.half = stage.shape[1] // 2
        self.rows = next(r for r in (176, 128, 96, 64, 32, 16) if self.half % r == 0)
        self.cols = range(1, net.tall)
        self.along = range(1, net.wide)
        self.bases = self.layout(net.n_f)

    @staticmethod
    def layout(n_f):
        tall = 2 if n_f % 2 == 0 else 1
        wide = n_f // tall
        sizes = [(wide - 1) * tall, (tall - 1) * wide, tall - 1, wide - 1]
        return [sum(sizes[:at]) for at in range(5)]

    @staticmethod
    def scratch(n_f, rows, columns):
        count = GridSum.layout(n_f)[4]
        return [
            pltpu.VMEM((n_f, rows, columns), BF),
            pltpu.VMEM((count, rows // 2, columns), BF),
            pltpu.SemaphoreType.DMA((2, count + GridEnd.count(n_f))),
        ]

    def slot(self, kind, i, j):
        base = self.bases[kind]
        return base + [(j - 1) * self.net.tall + i, (i - 1) * self.net.wide + j, i - 1, j - 1][kind]

    def rank(self, i, j):
        net = self.net
        return ((net.a + i) % net.tall) * net.wide + (net.b + j) % net.wide

    def owner(self, at):
        return self.rank(at // self.net.wide, at % self.net.wide)

    def copy(self, kind, i, j):
        half = kind % 2
        along = kind in (0, 3)
        slot = self.slot(kind, i, j)
        at = i * self.net.wide + j
        return put(
            self.stage.at[at, pl.ds(half * self.half, self.half)],
            self.came.at[slot],
            self.sems.at[0, slot],
            self.sems.at[1, slot],
            fsdp=self.rank(0, j) if along else self.rank(i, 0),
        )

    def first(self, at):
        i, j = at // self.net.wide, at % self.net.wide

        @pl.when(j > 0)
        def _():
            self.copy(0, i, j).start()

        @pl.when(i > 0)
        def _():
            self.copy(1, i, j).start()

    def gather(self, half, at, slots, write):
        @pl.loop(0, self.half // self.rows)
        def _(step):
            span = aligned(half * self.half + step * self.rows, self.rows, 16)
            value = self.stage[at, span, :].astype(F32)
            for slot in slots:
                value = value + self.came[slot, aligned(step * self.rows, self.rows, 16), :].astype(F32)
            write(span, value)

    def wait(self, *copies):
        for kind, i, j in copies:
            self.copy(kind, i, j).wait_recv()
        return [self.slot(*copy) for copy in copies]

    def second(self):
        def keep(at):
            def write(span, value):
                self.stage[at, span, :] = value.astype(BF)

            return write

        for i in self.cols:
            at = i * self.net.wide
            self.gather(0, at, self.wait(*[(0, i, j) for j in self.along]), keep(at))
            self.copy(2, i, 0).start()
        for j in self.along:
            self.gather(1, j, self.wait(*[(1, i, j) for i in self.cols]), keep(j))
            self.copy(3, 0, j).start()

    def sum_first(self):
        def keep(at):
            def write(span, value):
                self.stage[at, span, :] = value.astype(BF)

            return write

        for i in range(self.net.tall):
            at = i * self.net.wide
            self.gather(0, at, self.wait(*[(0, i, j) for j in self.along]), keep(at))
        for j in range(self.net.wide):
            self.gather(1, j, self.wait(*[(1, i, j) for i in self.cols]), keep(j))

    def hand_on(self, out):
        net = self.net
        shards = [(0, 0), (0, 1), *[(i * net.wide, 0) for i in self.cols], *[(j, 1) for j in self.along]]
        return [
            pltpu.make_async_copy(
                self.stage.at[at, pl.ds(half * self.half, self.half)], out.at[k], self.sems.at[0, self.bases[4] + k]
            )
            for k, (at, half) in enumerate(shards)
        ]

    def last(self, out):
        def write(span, value):
            out[span, :] = value

        self.gather(
            0, 0, self.wait(*[(0, 0, j) for j in self.along], *[(2, i, 0) for i in self.cols]), write
        )
        self.gather(
            1, 0, self.wait(*[(1, i, 0) for i in self.cols], *[(3, 0, j) for j in self.along]), write
        )

    def finish_first(self):
        for i in range(self.net.tall):
            for j in range(self.net.wide):
                if j:
                    self.copy(0, i, j).wait_send()
                if i:
                    self.copy(1, i, j).wait_send()

    def finish(self):
        self.finish_first()
        for i in self.cols:
            self.copy(2, i, 0).wait_send()
        for j in self.along:
            self.copy(3, 0, j).wait_send()


class GridEnd:
    def __init__(self, net, sums, came, sems):
        self.net, self.sums, self.came, self.sems = net, sums, came, sems

    @staticmethod
    def count(n_f):
        tall = 2 if n_f % 2 == 0 else 1
        return tall + n_f // tall

    @staticmethod
    def scratch(n_f, rows, columns):
        count = GridEnd.count(n_f)
        return [pltpu.VMEM((count, rows // 2, columns), BF), pltpu.SemaphoreType.DMA((2, count - 2))]

    def copies(self):
        net = self.net
        f = [((net.a + i) % net.tall) * net.wide + net.b for i in range(1, net.tall)]
        f += [net.a * net.wide + (net.b + j) % net.wide for j in range(1, net.wide)]
        return [
            put(self.sums.at[2 + k], self.came.at[k], self.sems.at[0, k], self.sems.at[1, k], fsdp=to)
            for k, to in enumerate(f)
        ]

    def start(self):
        for copy in self.copies():
            copy.start()

    def finish(self):
        for copy in self.copies():
            copy.wait()


class PacketSum:
    def __init__(self, net, out, seq_in, total, fsdp_in, sems):
        self.net, self.out, self.seq_in, self.total, self.fsdp_in, self.sems = net, out, seq_in, total, fsdp_in, sems

    @staticmethod
    def scratch(n_f, n_s):
        return [
            pltpu.VMEM((n_s, n_f, SMALL, 128), F32),
            pltpu.VMEM((n_s, n_f, SMALL, 128), F32),
            pltpu.VMEM((n_f, SMALL, 128), F32),
            pltpu.VMEM((n_f, SMALL, 128), F32),
            pltpu.SemaphoreType.DMA((2 * (n_f + n_s),)),
        ]

    def one(self, k):
        to = (self.net.s + k) % self.net.n_s
        return put(self.out.at[to], self.seq_in.at[k], self.sems.at[2 * k], self.sems.at[2 * k + 1], seq=to)

    def two(self, k):
        to = (self.net.f + k) % self.net.n_f
        at = 2 * (self.net.n_s + k)
        return put(self.total.at[to], self.fsdp_in.at[k], self.sems.at[at], self.sems.at[at + 1], fsdp=to)

    def start(self, terms, width):
        net = self.net
        per = 128 // width
        for tile in range(net.n_f * net.n_s // per):
            value = terms[:, tile * 128 : (tile + 1) * 128]
            for j in range(per):
                f, s = divmod(tile * per + j, net.n_s)
                self.out[s, f] = pltpu.roll(value, 128 - j * width, axis=1) if j else value
        for k in range(1, net.n_s):
            self.one(k).start()

    def middle(self):
        net = self.net
        total = self.out[net.s]
        for k in range(1, net.n_s):
            self.one(k).wait()
            total = total + self.seq_in[k]
        self.total[...] = total
        for k in range(1, net.n_f):
            self.two(k).start()

    def finish(self, result):
        net = self.net
        total = self.total[net.f]
        for k in range(1, net.n_f):
            self.two(k).wait()
            total = total + self.fsdp_in[k]
        result[...] = total


def norm_backward(rows, source, grad, gain, terms, at, write):
    terms[at : at + 2, :] = jnp.zeros((2, terms.shape[1]), F32)

    @pl.loop(0, rows // 32)
    def _(i):
        span = aligned(i * 32, 32)
        scaled, inverse = normalize(source[span, :].astype(F32))
        value = grad[span, :]
        upstream = value * gain
        inner = jnp.mean(upstream, -1, keepdims=True)
        cross = jnp.mean(upstream * scaled, -1, keepdims=True)
        terms[at : at + 1, :] = terms[at : at + 1, :] + jnp.sum(value * scaled, 0, keepdims=True)
        terms[at + 1 : at + 2, :] = terms[at + 1 : at + 2, :] + jnp.sum(value, 0, keepdims=True)
        write(i, span, inverse * (upstream - inner - scaled * cross))


def layer_kernel(
    tok,
    gain_one,
    shift_one,
    gain_two,
    shift_two,
    bias,
    wq_own,
    wo_own,
    wg_own,
    wu_own,
    wd_own,
    gout_own,
    cosine,
    sine,
    q_o,
    k_o,
    kt_o,
    v_o,
    att_o,
    lse_o,
    n1_o,
    gains_o,
    wq_o,
    wo_o,
    dm_o,
    datt_o,
    dmid_o,
    top_o,
    terms_o,
    gate_o,
    up_o,
    down_o,
    rows,
    gout,
    wq,
    wo,
    wg,
    wu,
    wd,
    q,
    k,
    kt,
    v,
    vt,
    ot,
    att,
    hidden,
    dgate,
    dup,
    mid,
    low,
    packet,
    packets,
    tiles,
    total,
    *rest,
):
    net = Net()
    chunk, width = tok.shape
    length = chunk * net.n_s
    depth = wq_own.shape[1]
    columns = wq_own.shape[2]
    heads = columns // HEAD
    pair = 2 * chunk
    buffers, rest = rest[:4], rest[4:]
    folds = []
    for _ in range(3):
        folds.append(Fold(net, tiles, total, *buffers, *rest[:4]))
        rest = rest[4:]
    att_fold, normed_fold, top_fold = folds
    line_sems = [rest[at : at + 3] for at in (0, 3, 6, 9)]
    rest = rest[12:]
    spread_sems, rest = rest[:5], rest[5:]
    gate_sum, up_sum, down_sum = [GridSum(net, *rest[at : at + 3]) for at in (0, 3, 6)]
    sums = (down_sum, gate_sum, up_sum)
    pk_sems, copy_sems, n1_sems, dm_sems, free_sem = rest[9:]
    copies = Copies(copy_sems)
    n1 = att_fold.mate_out

    packet[...] = jnp.zeros(packet.shape, F32)
    own = gain_one.shape[1]
    for at, part in enumerate((gain_one, shift_one, gain_two, shift_two)):
        packet[at : at + 1, 0:own] = part[...].astype(F32)
    packet[4:7, 0:own] = bias[...].astype(F32)
    def wq_part(f, half):
        if half is None:
            return wq.at[:, aligned(f * depth, depth), :]
        return wq.at[:, aligned(f * depth + half * (depth // 2), depth // 2), :]

    spread_q = Spread(net, wq_own, wq_part, spread_sems[0])
    spread_o, spread_g, spread_u, spread_d = [
        Spread(net, own, columns_of(full, depth), sems)
        for own, full, sems in zip((wo_own, wg_own, wu_own, wd_own), (wo, wg, wu, wd), spread_sems[1:])
    ]
    pk = Packets(net, packet, packets, pk_sems)
    line = Line(net, tok, rows_of(rows, chunk), *line_sems[0])
    gout_line = Line(net, gout_own, rows_of(gout, chunk), *line_sems[1])
    n2_line = Line(net, low, rows_of(rows, chunk), *line_sems[2])
    dm_line = Line(net, low, rows_of(rows, chunk), *line_sems[3])

    for ready in (line, spread_q, spread_o, spread_g, spread_u, spread_d, gout_line):
        ready.prepare()
    net.barrier()

    def pairs(which, hop):
        net.sides(hop, lambda other, side: which.pair(other))

    def blocks(hop, act):
        def once(other, side):
            @pl.when((hop > 0) | (side == 0))
            def _():
                act(other, side)

        net.sides(hop, once)

    pk.start()
    line.start()
    spread_q.start()
    pk.middle()
    pk.finish()
    pk.unpack(gains_o, width // (net.n_f * net.n_s))

    def project_block(other, side):
        span = aligned(other * pair, pair)
        gain, shift = gains_o[0:1, :], gains_o[1:2, :]

        for part in range(2):

            @pl.loop(0, chunk // 32)
            def _(i):
                at = aligned((2 * other + part) * chunk + i * 32, 32)
                scaled, _ = normalize(rows[at, :].astype(F32))
                n1[part, aligned(i * 32, 32), :] = (scaled * gain + shift).astype(BF)

        keeps = [
            pltpu.make_async_copy(
                n1.at[part], n1_o.at[aligned((2 * other + part) * chunk, chunk)], n1_sems.at[part]
            )
            for part in range(2)
        ]
        for copy in keeps:
            copy.start()
        left = n1[0:2].reshape(pair, width)
        cols = aligned(net.s * columns, columns)
        tables = cosine[span, :], sine[span, :]
        for kind in range(3):
            value = dot(left, wq[kind]) + gains_o[4 + kind : 5 + kind, cols]
            if kind == 0:
                q[span, :] = rotary(value, *tables).astype(BF)
            elif kind == 1:
                value = rotary(value, *tables)
                k[span, :] = value.astype(BF)
                kt[...] = value.T.astype(BF)
            else:
                v[...] = value.astype(BF)
                vt[:, span] = value.T.astype(BF)
        for copy in (
            pltpu.make_async_copy(kt, kt_o.at[:, span], n1_sems.at[2]),
            pltpu.make_async_copy(v, v_o.at[span], n1_sems.at[3]),
        ):
            copy.start()
            keeps.append(copy)
        for copy in keeps:
            copy.wait()

    line.here()
    for hop in range(1, net.n_l - 1):
        line.step(hop)
        if hop == 1:
            spread_q.relay()
        pairs(line, hop)
    spread_o.start()
    spread_q.finish()
    spread_g.start()
    pl.loop(0, net.n_l - 1)(lambda hop: blocks(hop, project_block))
    spread_o.relay()
    spread_u.start()
    line.step(net.n_l - 1)
    gout_line.start()
    pairs(line, net.n_l - 1)
    blocks(net.n_l - 1, project_block)
    q_copy = copies.start(q, q_o)
    for pair_of in ((wq, wq_o), (k, k_o)):
        copies.start(*pair_of)
    spread_o.finish()
    line.finish()

    def attend(i):
        lo, hi = i * pair, (i + 1) * pair

        @pl.loop(0, heads)
        def _(head):
            lane = lax.broadcasted_iota(jnp.int32, (1, columns), 1)
            here = jnp.where(lane // HEAD == head, HEAD**-0.5, 0.0).astype(BF)
            visible = lax.broadcasted_iota(jnp.int32, (pair, pair), 0) <= lax.broadcasted_iota(
                jnp.int32, (pair, pair), 1
            )
            head_rows = aligned(head * HEAD, HEAD)
            query = q[lo:hi, :] * here
            near = jnp.where(visible, dot_nt(k[lo:hi, :], query), NEG_LARGE)
            highest = jnp.max(near, 0, keepdims=True)
            if i:
                far = dot_nt(k[0:lo, :], query)
                highest = jnp.maximum(highest, jnp.max(far, 0, keepdims=True))
            near = jnp.exp(near - highest)
            sum_of = jnp.sum(near, 0, keepdims=True)
            out = dot(vt[head_rows, lo:hi], near.astype(BF))
            if i:
                far = jnp.exp(far - highest)
                sum_of = sum_of + jnp.sum(far, 0, keepdims=True)
                out = out + dot(vt[head_rows, 0:lo], far.astype(BF))
            ot[head_rows, :] = out / sum_of
            lse_o[pl.ds(head, 1), lo:hi] = highest + jnp.log(sum_of)

        att[lo:hi, :] = ot[...].T.astype(BF)

    def produce_attended(place, write):
        for i in range(net.n_l):
            pl.when(place == i)(functools.partial(attend, i))
        left = att[aligned(place * pair, pair), :]

        @pl.loop(0, width // TILE)
        def _(j):
            cols = aligned(j * TILE, TILE)
            write(cols, dot(left, wo[:, cols]))

    def relays():
        gout_line.step(1)
        spread_d.start()

    att_fold.begin(produce_attended, relays)
    copies.start(att, att_o)
    copies.start(wo, wo_o)
    if net.n_l > 2:
        gout_line.step(2)
    att_fold.open_total()
    spread_g.relay()
    for at in range(1, net.n_l):
        if 2 < at + 1 < net.n_l:
            gout_line.step(at + 1)
        att_fold.wave(at)
        if at == 1:
            spread_u.relay()
        if at == min(2, net.n_l - 1):
            spread_d.relay()
    gain_two, shift_two = gains_o[2:3, :], gains_o[3:4, :]

    @pl.loop(0, chunk // 32)
    def _(i):
        span = aligned(i * 32, 32)
        value = rows[aligned(net.s * chunk + i * 32, 32), :].astype(F32) + total[span, :]
        mid[span, :] = value
        scaled, _ = normalize(value)
        low[span, :] = (scaled * gain_two + shift_two).astype(BF)

    n2_line.prepare()
    n2_line.start()
    att_fold.finish()
    gout_line.here()
    pl.loop(1, net.n_l)(lambda hop: pairs(gout_line, hop))

    def forward_block(other):
        span = aligned(other * pair, pair)
        right = rows[span, :]
        half = hidden.shape[0] // 2

        @pl.loop(0, 2)
        def _(part):
            units = aligned(part * half, half, 16)
            gate = dot_nt(wg[units, :], right)
            up = dot_nt(wu[units, :], right)
            back = dot_nt(wd[units, :], gout[span, :])
            sigma = jax.nn.sigmoid(gate)
            active = gate * sigma
            hidden[units, span] = (active * up).astype(BF)
            dgate[units, span] = (back * up * (sigma * (1.0 + gate * (1.0 - sigma)))).astype(BF)
            dup[units, span] = (back * active).astype(BF)

    def produce_normed(place, write):
        span = aligned(place * pair, pair)
        left, right = dgate[:, span].T, dup[:, span].T

        @pl.loop(0, width // TILE)
        def _(j):
            cols = aligned(j * TILE, TILE)
            write(cols, dot(left, wg[:, cols]) + dot(right, wu[:, cols]))

    def begin_normed(other, side, hop):
        @pl.when(hop > 1)
        def _():
            normed_fold.mate_sent(side)

        normed_fold.begin_one(other, side + (2 - side) * (1 // (hop + 1)), produce_normed)

    def forward_blocks(hop):
        def act(other, side):
            forward_block(other)

            @pl.when(jnp.logical_not(normed_fold.fed(side)))
            def _():
                begin_normed(other, side, hop)
                normed_fold.leave(other, side, hop)

        net.sides(hop, act)

    def begin_fed(hop):
        def act(other, side):
            pl.when(normed_fold.fed(side))(lambda: begin_normed(other, side, hop))

        net.sides(hop, act)

    n2_line.here()
    for spread in (spread_g, spread_u, spread_d):
        spread.finish()
    forward_block(net.z)

    @pl.loop(1, net.n_l)
    def _(hop):
        n2_line.step(hop)
        pairs(n2_line, hop)
        pl.when(hop == 1)(lambda: normed_fold.begin_one(net.z, 2, produce_normed))
        forward_blocks(hop)
        pl.when(hop > 1)(lambda: begin_fed(hop - 1))

    begin_fed(net.n_l - 1)

    def weight_terms(task):
        at, kind = net.n_f - 1 - task // 3, task % 3
        cols = aligned(gate_sum.owner(at) * depth, depth)
        for way, (grid_sum, left, right) in enumerate(
            ((down_sum, hidden, gout), (gate_sum, dgate, rows), (up_sum, dup, rows))
        ):

            @pl.when(kind == way)
            def _():
                half = left.shape[0] // 2

                @pl.loop(0, 2)
                def _(part):
                    units = aligned(part * half, half, 16)
                    grid_sum.stage[at, units, :] = dot(left[units, :], right[:, cols]).astype(BF)

                grid_sum.first(at)

    tasks = 3 * net.n_f
    waves = max(net.n_l - 2, 1)
    each = -(-tasks // (2 * normed_fold.pieces * waves))
    for wave in range(net.n_l - waves, net.n_l):

        def between(turn, piece):
            slot = ((wave - net.n_l + waves) * 2 + turn) * normed_fold.pieces + piece

            @pl.loop(0, each)
            def _(i):
                pl.when(slot * each + i < tasks)(lambda: weight_terms(slot * each + i))

        normed_fold.passes_between(wave, True, between)
    normed_fold.finals()
    n2_line.finish()

    def beside(act):
        act(net.mate)
        for side in range(2):
            pl.when(n2_line.goes_on(side))(lambda: act(net.s + 2 - 4 * side))

    beside(lambda to: pl.semaphore_signal(free_sem, 1, device_id={"seq": to}, device_id_type=MESH))

    def write_middle(i, span, value):
        value = value + gout[aligned(net.s * chunk + i * 32, 32), :].astype(F32)
        dmid_o[span, :] = value
        low[span, :] = value.astype(BF)

    terms_o[...] = jnp.zeros(terms_o.shape, F32)
    norm_backward(chunk, mid, total, gain_two, terms_o, 2, write_middle)
    ends = (net.z + net.n_l - 1) // net.n_l + (2 * net.n_l - 2 - net.z) // net.n_l
    pl.semaphore_wait(free_sem, 1 + ends)
    dm_line.prepare()
    dm_line.start()
    normed_fold.finish()

    def produce_top(place, write):
        left = hidden[:, aligned(place * pair, pair)].T

        @pl.loop(0, width // TILE)
        def _(j):
            cols = aligned(j * TILE, TILE)
            write(cols, dot(left, wd[:, cols]))

    copies.wait(q_copy)
    datt = q

    def dm_copy(other):
        span = aligned(other * pair, pair)
        return pltpu.make_async_copy(rows.at[span], dm_o.at[span], dm_sems.at[other])

    def back_block(other, side):
        span = aligned(other * pair, pair)
        dm_copy(other).start()
        datt[span, :] = dot_nt(rows[span, :], wo[...]).astype(BF)

    dm_line.here()
    dm_line.step(1)
    top_fold.begin(produce_top)
    back_block(net.z, 0)
    top_fold.open_total()
    for at in range(1, net.n_l):
        if at + 1 < net.n_l:
            dm_line.step(at + 1)
        top_fold.wave(at)
        pairs(dm_line, at)
        net.sides(at, back_block)
    copies.start(datt, datt_o)

    @pl.loop(0, chunk // 32)
    def _(i):
        span = aligned(i * 32, 32)
        top_fold.out[net.z, span, :] = (mid[span, :] + total[span, :]).astype(BF)

    copies.start(top_fold.out.at[net.z], top_o)
    top_fold.finish()
    gout_line.finish()
    dm_line.finish()
    hands = []
    for grid_sum, out in zip(sums, (down_o, gate_o, up_o)):
        grid_sum.sum_first()
        hands.extend(grid_sum.hand_on(out))
        for copy in grid_sum.hand_on(out):
            copy.start()
    for grid_sum in sums:
        grid_sum.finish_first()
    for copy in hands:
        copy.wait()
    copies.wait()
    pl.loop(0, net.n_l)(lambda other: dm_copy(other).wait())


def layer_part(tokens, norms, wq, wo, wg, wu, wd, gout, tables):
    chunk, width = tokens.shape
    n_f, n_s = lax.axis_size("fsdp"), lax.axis_size("seq")
    length = chunk * n_s
    depth, columns = wq.shape[1:]
    units = wg.shape[0]
    shape = jax.ShapeDtypeStruct
    wide, head, turned, weight = (length, width), (length, columns), (units, length), (units, width)
    return pl.pallas_call(
        layer_kernel,
        name="layer",
        out_shape=[
            shape(head, BF),
            shape(head, BF),
            shape((columns, length), BF),
            shape(head, BF),
            shape(head, BF),
            shape((8, length), F32),
            shape(wide, BF),
            shape((SMALL, width), F32),
            shape((3, width, columns), BF),
            shape((columns, width), BF),
            shape(wide, BF),
            shape(head, BF),
            shape((chunk, width), F32),
            shape((chunk, width), BF),
            shape((SMALL, width), F32),
            *[shape((GridEnd.count(n_f), units // 2, depth), BF)] * 3,
        ],
        in_specs=[ANY, *[VMEM] * 5, *[ANY] * 6, VMEM, VMEM],
        out_specs=[*[ANY] * 5, VMEM, ANY, VMEM, *[ANY] * 4, VMEM, ANY, VMEM, *[ANY] * 3],
        scratch_shapes=[
            pltpu.VMEM(wide, BF),
            pltpu.VMEM(wide, BF),
            pltpu.VMEM((3, width, columns), BF),
            pltpu.VMEM((columns, width), BF),
            *[pltpu.VMEM(weight, BF)] * 3,
            pltpu.VMEM(head, BF),
            pltpu.VMEM(head, BF),
            pltpu.VMEM((columns, 2 * chunk), BF),
            pltpu.VMEM((2 * chunk, columns), BF),
            pltpu.VMEM((columns, length), BF),
            pltpu.VMEM((columns, 2 * chunk), F32),
            pltpu.VMEM(head, BF),
            *[pltpu.VMEM(turned, BF)] * 3,
            pltpu.VMEM((chunk, width), F32),
            pltpu.VMEM((chunk, width), BF),
            pltpu.VMEM((SMALL, 128), F32),
            pltpu.VMEM((n_s, n_f, SMALL, 128), F32),
            *Fold.shared(chunk, width),
            *Fold.buffers(n_s, chunk, width),
            *Fold.sems(n_s) * 3,
            *Line.sems(n_s) * 4,
            *[pltpu.SemaphoreType.DMA((Spread.count(n_f),))] * 5,
            *GridSum.scratch(n_f, units, depth) * 3,
            pltpu.SemaphoreType.DMA((Packets.count(n_f, n_s),)),
            pltpu.SemaphoreType.DMA((8,)),
            pltpu.SemaphoreType.DMA((4,)),
            pltpu.SemaphoreType.DMA((n_s // 2,)),
            pltpu.SemaphoreType.REGULAR,
        ],
        compiler_params=pltpu.CompilerParams(
            collective_id=1, has_side_effects=True, vmem_limit_bytes=VMEM_BYTES
        ),
        cost_estimate=pl.CostEstimate(
            flops=2 * length * width * (4 * columns + 9 * units),
            bytes_accessed=8 * length * width,
            transcendentals=length * (length * columns // HEAD + units),
        ),
    )(tokens, *norms, wq, wo, wg, wu, wd, gout, *tables)


def back_kernel(
    datt_in,
    q_in,
    k_in,
    kt_in,
    v_in,
    att_in,
    wq_in,
    n1_in,
    dm_in,
    down_in,
    gate_in,
    up_in,
    lse,
    tok,
    dmid,
    gains,
    terms_in,
    cosine,
    sine,
    gin_o,
    small_o,
    out_o,
    qkv_o,
    down_o,
    gate_o,
    up_o,
    datt,
    q,
    k,
    kt,
    v,
    att,
    wq,
    n1,
    dm,
    query,
    upstream,
    inners,
    dk,
    dv,
    dqt,
    dproj,
    terms,
    tiles,
    total,
    *rest,
):
    net = Net()
    chunk, width = tok.shape
    length, columns = q_in.shape
    heads = columns // HEAD
    pair = 2 * chunk
    depth = width // net.n_f
    block = 256
    buffers, rest = rest[:4], rest[4:]
    fold_sems, rest = rest[:4], rest[4:]
    packet_scratch, rest = rest[:5], rest[5:]
    out_sum, qkv_sum = GridSum(net, *rest[:3]), GridSum(net, *rest[3:6])
    ends = [
        GridEnd(net, rest[at], came, rest[at + 1]) for at, came in ((6, down_o), (8, gate_o), (10, up_o))
    ]
    copy_sems, column_sems = rest[12:]

    copies = Copies(copy_sems)
    loads = [
        copies.start(src, dst)
        for src, dst in (
            (datt_in, datt),
            (q_in, q),
            (k_in, k),
            (kt_in, kt),
            (v_in, v),
            (att_in, att),
            (wq_in, wq),
            (down_in, ends[0].sums),
            (gate_in, ends[1].sums),
            (up_in, ends[2].sums),
        )
    ]
    def load(at, way):
        src, dst = ((n1_in, n1), (dm_in, dm))[way]
        cols = aligned(qkv_sum.owner(at) * depth, depth)
        return pltpu.make_async_copy(src.at[:, cols], dst.at[at % 2], column_sems.at[way, at % 2])

    for at in range(net.n_f - 1, max(net.n_f - 3, -1), -1):
        for way in range(2):
            load(at, way).start()

    @pl.loop(0, length // block)
    def _(i):
        span = aligned(i * block, block)
        dk[span, :] = jnp.zeros((block, columns), F32)
        dv[span, :] = jnp.zeros((block, columns), F32)

    net.barrier()
    copies.wait(*loads[:6])

    def start_ends():
        for load_of in loads[7:]:
            load_of.wait()
        for end in ends:
            end.start()


    of_head = (
        lax.broadcasted_iota(jnp.int32, (8, columns), 1) // HEAD
        == lax.broadcasted_iota(jnp.int32, (8, columns), 0)
    ).astype(F32)

    @pl.loop(0, length // block)
    def _(i):
        span = aligned(i * block, block)
        product = datt[span, :].astype(F32) * att[span, :].astype(F32)
        inners[:, span] = lax.dot_general(
            of_head,
            product,
            (((1,), (1,)), ((), ())),
            precision=lax.Precision.HIGHEST,
            preferred_element_type=F32,
        )

    @pl.loop(0, heads)
    def _(head):
        lane = lax.broadcasted_iota(jnp.int32, (1, columns), 1)
        here = jnp.where(lane // HEAD == head, 1.0, 0.0).astype(BF)
        scale = HEAD**-0.5
        visible = lax.broadcasted_iota(jnp.int32, (block, block), 0) <= lax.broadcasted_iota(
            jnp.int32, (block, block), 1
        )
        head_rows = aligned(head * HEAD, HEAD)

        @pl.loop(0, length // block)
        def _(i):
            span = aligned(i * block, block)
            query[span, :] = q[span, :] * (here * scale)
            upstream[span, :] = datt[span, :] * here

        pl.when(head == min(1, heads - 1))(start_ends)

        for j in range(length // block):
            at, end = j * block, (j + 1) * block
            keys, values, turned = k[at:end, :], v[at:end, :], kt[head_rows, at:end]

            def part(lo, hi, near):
                probs = jnp.exp(dot_nt(keys, query[lo:hi, :]) - lse[pl.ds(head, 1), lo:hi])
                if near:
                    probs = jnp.where(visible, probs, 0.0)
                grads = dot_nt(values, upstream[lo:hi, :])
                scores = (probs * (grads - inners[pl.ds(head, 1), lo:hi])).astype(BF)
                out = dot(turned, scores)
                dqt[head_rows, lo:hi] = dqt[head_rows, lo:hi] + out if j else out
                return dot(probs.astype(BF), upstream[lo:hi, :]), dot(scores, query[lo:hi, :])

            value_grads, key_grads = part(at, end, True)
            if end < length:
                more_values, more_keys = part(end, length, False)
                value_grads, key_grads = value_grads + more_values, key_grads + more_keys
            dv[at:end, :] = dv[at:end, :] + value_grads
            dk[at:end, :] = dk[at:end, :] + key_grads

    terms[...] = terms_in[...]
    bias_cols = aligned(net.s * columns, columns)

    @pl.loop(0, length // block)
    def _(i):
        span = aligned(i * block, block)
        tables = cosine[span, :], -sine[span, :]
        parts = [
            rotary((dqt[:, span].T * HEAD**-0.5).astype(BF).astype(F32), *tables).astype(BF),
            rotary(dk[span, :].astype(BF).astype(F32), *tables).astype(BF),
            dv[span, :].astype(BF),
        ]
        for kind in range(3):
            dproj[kind, span, :] = parts[kind]
            row = slice(4 + kind, 5 + kind)
            terms[row, bias_cols] = terms[row, bias_cols] + jnp.sum(parts[kind].astype(F32), 0, keepdims=True)

    def weight_terms(task):
        at = net.n_f - 1 - task // 2

        def loaded(way):
            load(at, way).wait()

        def next_load(way):
            pl.when(at >= 2)(lambda: load(at - 2, way).start())

        @pl.when(task % 2 == 0)
        def _():
            loaded(0)
            left = n1[at % 2].T
            for kind in range(3):
                qkv_sum.stage[at, kind * depth : (kind + 1) * depth, :] = dot(left, dproj[kind]).astype(BF)
            next_load(0)
            qkv_sum.first(at)

        @pl.when(task % 2 == 1)
        def _():
            loaded(1)
            out_sum.stage[at] = dot_tn(att[...], dm[at % 2]).astype(BF)
            next_load(1)
            out_sum.first(at)

    def produce(place, write):
        span = aligned(place * pair, pair)

        @pl.loop(0, width // TILE)
        def _(j):
            cols = aligned(j * TILE, TILE)
            value = dot_nt(dproj[0, span, :], wq[0, cols, :])
            for kind in range(1, 3):
                value = value + dot_nt(dproj[kind, span, :], wq[kind, cols, :])
            write(cols, value)

    fold = Fold(net, tiles, total, *buffers, *fold_sems)
    copies.wait(loads[6])
    fold.begin(produce)
    fold.open_total()
    tasks = 2 * net.n_f
    waves = max(net.n_l - 2, 1)
    each = -(-tasks // (2 * fold.pieces * waves))

    def between(slot):
        @pl.loop(0, each)
        def _(i):
            pl.when(slot * each + i < tasks)(lambda: weight_terms(slot * each + i))

    for at in range(1, waves + 1):
        fold.wave(at, between=between)
    for at in range(waves + 1, net.n_l):
        fold.wave(at)

    def write_input(i, span, value):
        gin_o[span, :] = value + dmid[span, :]

    norm_backward(chunk, tok, total, gains[0:1, :], terms, 0, write_input)
    packet_sum = PacketSum(net, *packet_scratch)
    packet_sum.start(terms, width // (net.n_f * net.n_s))
    for grid_sum in (qkv_sum, out_sum):
        grid_sum.second()
    packet_sum.middle()
    packet_sum.finish(small_o)
    for end in ends:
        end.finish()
    fold.finish()
    for grid_sum, out in ((qkv_sum, qkv_o), (out_sum, out_o)):
        grid_sum.last(out)
        grid_sum.finish()


def back_part(datt, q, k, kt, v, att, wq, n1, dm, down, gate, up, lse, tokens, dmid, gains, terms, tables):
    chunk, width = tokens.shape
    n_f, n_s = lax.axis_size("fsdp"), lax.axis_size("seq")
    length, columns = q.shape
    depth = width // n_f
    units = 2 * gate.shape[1]
    shape = jax.ShapeDtypeStruct
    return pl.pallas_call(
        back_kernel,
        name="back",
        out_shape=[
            shape((chunk, width), F32),
            shape((SMALL, 128), F32),
            shape((columns, depth), F32),
            shape((3 * depth, columns), F32),
            *[shape((GridEnd.count(n_f) - 2, units // 2, depth), BF)] * 3,
        ],
        in_specs=[ANY] * 12 + [VMEM] * 7,
        out_specs=[VMEM] * 4 + [ANY] * 3,
        scratch_shapes=[
            pltpu.VMEM((length, columns), BF),
            pltpu.VMEM((length, columns), BF),
            pltpu.VMEM((length, columns), BF),
            pltpu.VMEM((columns, length), BF),
            pltpu.VMEM((length, columns), BF),
            pltpu.VMEM((length, columns), BF),
            pltpu.VMEM((3, width, columns), BF),
            pltpu.VMEM((2, length, depth), BF),
            pltpu.VMEM((2, length, depth), BF),
            pltpu.VMEM((length, columns), BF),
            pltpu.VMEM((length, columns), BF),
            pltpu.VMEM((8, length), F32),
            pltpu.VMEM((length, columns), F32),
            pltpu.VMEM((length, columns), F32),
            pltpu.VMEM((columns, length), F32),
            pltpu.VMEM((3, length, columns), BF),
            pltpu.VMEM((SMALL, width), F32),
            *Fold.shared(chunk, width),
            *Fold.buffers(n_s, chunk, width),
            *Fold.sems(n_s, 8),
            *PacketSum.scratch(n_f, n_s),
            *GridSum.scratch(n_f, columns, depth),
            *GridSum.scratch(n_f, 3 * depth, columns),
            *GridEnd.scratch(n_f, units, depth) * 3,
            pltpu.SemaphoreType.DMA((10,)),
            pltpu.SemaphoreType.DMA((2, 2)),
        ],
        compiler_params=pltpu.CompilerParams(
            collective_id=3, has_side_effects=True, vmem_limit_bytes=VMEM_BYTES
        ),
        cost_estimate=pl.CostEstimate(
            flops=2 * length * columns * (8 * width + 5 * length),
            bytes_accessed=4 * length * width,
            transcendentals=length * length * columns // HEAD,
        ),
    )(datt, q, k, kt, v, att, wq, n1, dm, down, gate, up, lse, tokens, dmid, gains, terms, *tables)


def outputs_kernel(tall, small, *refs):
    plain, sums, came, refs = refs[:4], refs[4:7], refs[7:10], refs[10:]
    results, totals, parts = refs[:4], refs[4:7], refs[7:]
    own = parts[0].shape[1]
    for src, dst in zip(plain, results):
        dst[...] = src[...]
    for so_far, last, dst in zip(sums, came, totals):
        half = so_far.shape[1]
        count = last.shape[0]
        for at, slots in enumerate((range(tall - 1), range(tall - 1, count))):
            value = so_far[at].astype(F32)
            for slot in slots:
                value = value + last[slot].astype(F32)
            dst[at * half : (at + 1) * half, :] = value
    for at in range(4):
        parts[at][...] = small[at : at + 1, 0:own]
    parts[4][...] = small[4:7, 0:own]


def outputs_part(small, own, plain, sums, came):
    shape = jax.ShapeDtypeStruct
    tall = 2 if lax.axis_size("fsdp") % 2 == 0 else 1
    return pl.pallas_call(
        functools.partial(outputs_kernel, tall),
        name="outputs",
        out_shape=[shape(v.shape, v.dtype) for v in plain]
        + [shape((2 * v.shape[1], v.shape[2]), F32) for v in sums]
        + [shape((1, own), F32)] * 4
        + [shape((3, own), F32)],
        in_specs=[VMEM] * 11,
        out_specs=[VMEM] * 12,
        compiler_params=pltpu.CompilerParams(vmem_limit_bytes=VMEM_BYTES),
    )(small, *plain, *sums, *came)


def per_device(
    tokens,
    gain_one,
    shift_one,
    w_qkv,
    b_qkv,
    w_out,
    gain_two,
    shift_two,
    w_gate,
    w_up,
    w_down,
    grad_output,
):
    length = tokens.shape[1] * lax.axis_size("seq")
    width = gain_one.shape[0]
    norms = [v[None] for v in (gain_one, shift_one, gain_two, shift_two)] + [b_qkv]
    tables = rotary_tables(length)
    q, k, kt, v, att, lse, n1, gains, wq, _, dm, datt, dmid, top, terms, gate, up, down = layer_part(
        tokens[0], norms, w_qkv.transpose(1, 0, 2), w_out, w_gate.T, w_up.T, w_down, grad_output[0], tables
    )
    grad_input, small, out, qkv, *came = back_part(
        datt, q, k, kt, v, att, wq, n1, dm, down, gate, up, lse, tokens[0], dmid, gains, terms, tables
    )

    top, grad_input, qkv, out, down, gate, up, one, shift, two, shift_to, bias = outputs_part(
        small, width, (top, grad_input, qkv, out), (down, gate, up), came
    )
    return (
        top[None],
        grad_input[None],
        one[0],
        shift[0],
        qkv.reshape(3, -1, qkv.shape[1]).transpose(1, 0, 2),
        bias,
        out,
        two[0],
        shift_to[0],
        gate.T,
        up.T,
        down,
    )


def solution(mesh):
    whole = P(("fsdp", "seq"))
    rows = P("fsdp", "seq", None)
    inner = P("seq", "fsdp")
    outer = P("fsdp", "seq")
    heads = P("fsdp", None, "seq")
    bias = P(None, ("fsdp", "seq"))
    return jax.shard_map(
        per_device,
        mesh=mesh,
        in_specs=(rows, whole, whole, heads, bias, inner, whole, whole, outer, outer, inner, rows),
        out_specs=(rows, rows, whole, whole, heads, bias, inner, whole, whole, outer, outer, inner),
        check_vma=False,
    )
```

```python
import functools

import jax
import jax.numpy as jnp
import numpy as np
from jax import lax
from jax.experimental import pallas as pl
from jax.experimental.pallas import tpu as pltpu
from jax.sharding import PartitionSpec as P

HEAD = 64
ROT = 16
EPSILON = 1e-05
NEG_LARGE = -1e30
MESH = pl.DeviceIdType.MESH
ANY = pl.BlockSpec(memory_space=pl.ANY)
VMEM = pl.BlockSpec(memory_space=pltpu.VMEM)
BF = jnp.bfloat16
F32 = jnp.float32
VMEM_BYTES = 60 * 2**20
TILE = 512
SMALL = 8


def put(src, dst, send, recv, **device):
    return pltpu.make_async_remote_copy(
        src_ref=src, dst_ref=dst, send_sem=send, recv_sem=recv, device_id=device, device_id_type=MESH
    )


def dot(left, right):
    return jnp.dot(left, right, preferred_element_type=F32)


def dot_nt(left, right):
    return lax.dot_general(left, right, (((1,), (1,)), ((), ())), preferred_element_type=F32)


def dot_tn(left, right):
    return lax.dot_general(left, right, (((0,), (0,)), ((), ())), preferred_element_type=F32)


def aligned(start, size, unit=None):
    return pl.ds(pl.multiple_of(start, unit or size), size)


class Net:
    def __init__(self):
        self.n_f, self.n_s = lax.axis_size("fsdp"), lax.axis_size("seq")
        self.tall = 2 if self.n_f % 2 == 0 else 1
        self.wide = self.n_f // self.tall
        self.n_l = self.n_s // 2
        self.f, self.s = lax.axis_index("fsdp"), lax.axis_index("seq")
        self.a, self.b = self.f // self.wide, self.f % self.wide
        self.z, self.c = self.s // 2, self.s % 2
        self.mate = self.s + 1 - 2 * self.c

    def barrier(self):
        sem = pltpu.get_barrier_semaphore()
        for k in range(1, self.n_f):
            pl.semaphore_signal(
                sem, inc=1, device_id={"fsdp": (self.f + k) % self.n_f}, device_id_type=MESH
            )
        for k in range(1, self.n_s):
            pl.semaphore_signal(
                sem, inc=1, device_id={"seq": (self.s + k) % self.n_s}, device_id_type=MESH
            )
        pl.semaphore_wait(sem, self.n_f + self.n_s - 2)

    def sides(self, hop, act):
        @pl.loop(0, 2)
        def _(side):
            other = self.z + (2 * side - 1) * hop

            @pl.when((other >= 0) & (other < self.n_l))
            def _():
                act(other, side)


class Spread:
    def __init__(self, net, src, part, sems):
        self.net, self.src, self.part, self.sems = net, src, part, sems
        self.rows = [j for j in range(1, net.wide)]
        self.cols = [i for i in range(1, net.tall)]

    @staticmethod
    def count(n_f):
        tall = 2 if n_f % 2 == 0 else 1
        wide = n_f // tall
        return 1 + 2 * (wide - 1) + 2 * (tall - 1) + 4 * (wide - 1) * (tall - 1)

    def at(self, kind, i, j):
        w, t = len(self.rows), len(self.cols)
        base = {
            "own": 0,
            "row": 1,
            "col": 1 + 2 * w,
            "half0": 1 + 2 * w + 2 * t,
            "half1": 1 + 2 * w + 2 * t + 2 * w * t,
        }[kind]
        if kind == "own":
            return self.sems.at[0]
        k = j - 1 if kind == "row" else i - 1 if kind == "col" else (i - 1) * w + j - 1
        return self.sems.at[base + 2 * k], self.sems.at[base + 2 * k + 1]

    def rank(self, i, j):
        net = self.net
        return ((net.a + i) % net.tall) * net.wide + (net.b + j) % net.wide

    def back(self, i, j):
        net = self.net
        return ((net.a - i + net.tall) % net.tall) * net.wide + (net.b - j + net.wide) % net.wide

    def own(self):
        return pltpu.make_async_copy(self.src, self.part(self.net.f, None), self.at("own", 0, 0))

    def first(self, i, j):
        send, recv = self.at("row" if i == 0 else "col", i, j)
        place = self.part(self.net.f, None)
        return put(place, place, send, recv, fsdp=self.rank(i, j))

    def came(self, i, j):
        send, recv = self.at("row" if i == 0 else "col", i, j)
        place = self.part(self.back(i, j), None)
        return put(place, place, send, recv, fsdp=self.rank(i, j))

    def second(self, half, i, j, came=False):
        send, recv = self.at("half0" if half == 0 else "half1", i, j)
        origin = self.back(i, j) if came else self.back(0, j) if half == 0 else self.back(i, 0)
        place = self.part(origin, half)
        return put(place, place, send, recv, fsdp=self.rank(i, 0) if half == 0 else self.rank(0, j))

    def prepare(self):
        self.own().start()

    def start(self):
        self.own().wait()
        for i in self.cols:
            self.first(i, 0).start()
        for j in self.rows:
            self.first(0, j).start()

    def relay(self):
        for j in self.rows:
            self.came(0, j).wait_recv()
            for i in self.cols:
                self.second(0, i, j).start()
        for i in self.cols:
            self.came(i, 0).wait_recv()
            for j in self.rows:
                self.second(1, i, j).start()

    def finish(self):
        for j in self.rows:
            self.first(0, j).wait_send()
        for i in self.cols:
            self.first(i, 0).wait_send()
        for i in self.cols:
            for j in self.rows:
                for half in range(2):
                    self.second(half, i, j, came=True).wait_recv()
                    self.second(half, i, j).wait_send()


class Line:
    def __init__(self, net, src, part, recv, send, local):
        self.net, self.src, self.part, self.recv, self.send, self.local = net, src, part, recv, send, local
        self.pieces = recv.shape[1]
        self.rows = src.shape[0] // self.pieces

    @staticmethod
    def sems(n_s, pieces=2):
        return [
            pltpu.SemaphoreType.DMA((n_s, pieces)),
            pltpu.SemaphoreType.DMA((4, n_s // 2, pieces)),
            pltpu.SemaphoreType.DMA((1,)),
        ]

    def cut(self, ref, piece):
        return ref.at[aligned(piece * self.rows, self.rows)]

    def own(self):
        return pltpu.make_async_copy(self.src, self.part(self.net.s), self.local.at[0])

    def on_line(self, src, chunk, side, hop, piece):
        return put(
            self.cut(src, piece),
            self.cut(self.part(chunk), piece),
            self.send.at[side, hop, piece],
            self.recv.at[chunk, piece],
            seq=self.net.s + 2 - 4 * side,
        )

    def to_mate(self, src, chunk, side, hop, piece):
        return put(
            self.cut(src, piece),
            self.cut(self.part(chunk), piece),
            self.send.at[2 + side, hop, piece],
            self.recv.at[chunk, piece],
            seq=self.net.mate,
        )

    def goes_on(self, side):
        after = self.net.z + 1 - 2 * side
        return (after >= 0) & (after < self.net.n_l)

    def each_piece(self, act):
        pl.loop(0, self.pieces)(act)

    def prepare(self):
        self.own().start()

    def start(self):
        net = self.net
        self.own().wait()
        place = self.part(net.s)

        @self.each_piece
        def _(piece):
            for side in range(2):

                @pl.when(self.goes_on(side))
                def _():
                    self.on_line(place, net.s, side, 0, piece).start()

            self.to_mate(place, net.s, 0, 0, piece).start()

    def came(self, chunk, piece):
        place = self.cut(self.part(chunk), piece)
        put(place, place, self.send.at[0, 0, 0], self.recv.at[chunk, piece], seq=self.net.mate).wait_recv()

    def step(self, hop):
        net = self.net

        @self.each_piece
        def _(piece):
            def act(other, side):
                chunk = 2 * other + net.c
                self.came(chunk, piece)

                @pl.when(self.goes_on(side))
                def _():
                    self.on_line(self.part(chunk), chunk, side, hop, piece).start()

                self.to_mate(self.part(chunk), chunk, side, hop, piece).start()

            net.sides(hop, act)

    def pair(self, other):
        @self.each_piece
        def _(piece):
            self.came(2 * other + 1 - self.net.c, piece)

    def here(self):
        self.pair(self.net.z)

    def finish(self):
        net = self.net
        place = self.part(net.s)

        @self.each_piece
        def _(piece):
            for side in range(2):

                @pl.when(self.goes_on(side))
                def _():
                    self.on_line(place, net.s, side, 0, piece).wait_send()

            self.to_mate(place, net.s, 0, 0, piece).wait_send()

            @pl.loop(1, net.n_l)
            def _(hop):
                def act(other, side):
                    chunk = 2 * other + net.c

                    @pl.when(self.goes_on(side))
                    def _():
                        self.on_line(self.part(chunk), chunk, side, hop, piece).wait_send()

                    self.to_mate(self.part(chunk), chunk, side, hop, piece).wait_send()

                net.sides(hop, act)


class Packets:
    def __init__(self, net, src, buf, sems):
        self.net, self.src, self.buf, self.sems = net, src, buf, sems

    @staticmethod
    def count(n_f, n_s):
        return 1 + 2 * (n_f - 1) + 2 * (n_s - 1)

    def own(self):
        net = self.net
        return pltpu.make_async_copy(self.src, self.buf.at[net.s, net.f], self.sems.at[0])

    def one(self, k, came=False):
        net = self.net
        f = (net.f - k + net.n_f) % net.n_f if came else net.f
        place = self.buf.at[net.s, f]
        return put(
            place if came else self.src,
            place,
            self.sems.at[2 * k - 1],
            self.sems.at[2 * k],
            fsdp=(net.f + k) % net.n_f,
        )

    def two(self, k, came=False):
        net = self.net
        place = self.buf.at[(net.s - k + net.n_s) % net.n_s if came else net.s]
        at = 2 * (net.n_f - 1) + 2 * k - 1
        return put(place, place, self.sems.at[at], self.sems.at[at + 1], seq=(net.s + k) % net.n_s)

    def start(self):
        self.own().start()
        for k in range(1, self.net.n_f):
            self.one(k).start()

    def middle(self):
        self.own().wait()
        for k in range(1, self.net.n_f):
            self.one(k, came=True).wait_recv()
            self.one(k).wait_send()
        for k in range(1, self.net.n_s):
            self.two(k).start()

    def finish(self):
        for k in range(1, self.net.n_s):
            self.two(k, came=True).wait_recv()
            self.two(k).wait_send()

    def unpack(self, out, width):
        net = self.net
        per = 128 // width
        for tile in range(net.n_f * net.n_s // per):
            total = None
            for j in range(per):
                f, s = divmod(tile * per + j, net.n_s)
                piece = self.buf[s, f]
                if j:
                    piece = pltpu.roll(piece, j * width, axis=1)
                total = piece if total is None else total + piece
            out[:, tile * 128 : (tile + 1) * 128] = total


def rotary(values, cosine, sine):
    columns = values.shape[1]
    half = ROT // 2
    times = columns // 128

    def wide(table):
        return table if times == 1 else jnp.concatenate([table] * times, axis=1)

    lane = lax.broadcasted_iota(jnp.int32, values.shape, 1)
    other = jnp.where(
        lane % HEAD < half, pltpu.roll(values, columns - half, axis=1), pltpu.roll(values, half, axis=1)
    )
    return values * wide(cosine) + other * wide(sine)


def rotary_tables(length):
    half = ROT // 2
    freqs = np.float32(10000.0) ** (-np.arange(half, dtype=np.float32) * np.float32(2.0 / ROT))
    angles = np.arange(length, dtype=np.float32)[:, None] * freqs[None, :].astype(np.float32)
    cosine, sine = np.cos(angles), np.sin(angles)
    rest = np.zeros((length, HEAD - ROT), np.float32)
    keep = np.concatenate([cosine, cosine, rest + 1], 1)
    swap = np.concatenate([-sine, sine, rest], 1)
    return [np.tile(t, (1, 128 // HEAD)).astype(np.float32) for t in (keep, swap)]


def normalize(values):
    center = values - jnp.mean(values, -1, keepdims=True)
    inverse = lax.rsqrt(jnp.mean(center * center, -1, keepdims=True) + EPSILON)
    return center * inverse, inverse


class Copies:
    def __init__(self, sems):
        self.sems, self.all, self.open = sems, [], []

    def start(self, src, dst):
        copy = pltpu.make_async_copy(src, dst, self.sems.at[len(self.all)])
        copy.start()
        self.all.append(copy)
        self.open.append(copy)
        return copy

    def wait(self, *copies):
        for copy in copies or list(self.open):
            copy.wait()
            self.open = [c for c in self.open if c is not copy]


def columns_of(ref, depth):
    half_rows = ref.shape[0] // 2

    def part(f, half):
        span = aligned(f * depth, depth)
        if half is None:
            return ref.at[:, span]
        return ref.at[pl.ds(half * half_rows, half_rows), span]

    return part


def rows_of(ref, chunk):
    return lambda s: ref.at[aligned(s * chunk, chunk)]


class Fold:
    def __init__(self, net, tile, total, mate_in, coming, mate_out, out, mate_send, mate_recv, send, recv):
        self.net, self.tile, self.total = net, tile, total
        self.mate_in, self.coming, self.mate_out, self.out = mate_in, coming, mate_out, out
        self.mate_send, self.mate_recv, self.send, self.recv = mate_send, mate_recv, send, recv
        self.chunk = total.shape[0]
        self.pieces = recv.shape[1]
        self.rows = self.chunk // self.pieces

    @staticmethod
    def shared(chunk, width):
        return [pltpu.VMEM((2 * chunk, TILE), F32), pltpu.VMEM((chunk, width), F32)]

    @staticmethod
    def buffers(n_s, chunk, width):
        n_l = n_s // 2
        return [
            pltpu.VMEM((n_l, chunk, width), BF),
            pltpu.VMEM((n_l + 1, chunk, width), BF),
            pltpu.VMEM((3, chunk, width), BF),
            pltpu.VMEM((n_l, chunk, width), BF),
        ]

    @staticmethod
    def sems(n_s, pieces=4):
        n_l = n_s // 2
        return [
            pltpu.SemaphoreType.DMA((3, pieces)),
            pltpu.SemaphoreType.DMA((n_l, pieces)),
            pltpu.SemaphoreType.DMA((n_l, pieces)),
            pltpu.SemaphoreType.DMA((n_l + 1, pieces)),
        ]

    def place(self, other):
        return (other >= 0) & (other < self.net.n_l)

    def fed(self, side):
        return self.place(self.net.z + 1 - 2 * side)

    def span(self, piece):
        return aligned(piece * self.rows, self.rows)

    def each_piece(self, act):
        pl.loop(0, self.pieces)(act)

    def to_mate(self, target, slot, piece):
        span = self.span(piece)
        return put(
            self.mate_out.at[slot, span],
            self.mate_in.at[target, span],
            self.mate_send.at[slot, piece],
            self.mate_recv.at[target, piece],
            seq=self.net.mate,
        )

    def onward(self, target, side, hop, piece):
        span = self.span(piece)
        slot = target + (self.net.n_l - target) * (1 - side) * (1 // hop)
        return put(
            self.out.at[target, span],
            self.coming.at[slot, span],
            self.send.at[target, piece],
            self.recv.at[slot, piece],
            seq=self.net.s + 4 * side - 2,
        )

    def came(self, slot, piece):
        place = self.coming.at[slot, self.span(piece)]
        put(place, place, self.send.at[0, 0], self.recv.at[slot, piece], seq=self.net.mate).wait_recv()

    def mate_sent(self, slot):
        self.each_piece(lambda piece: self.to_mate(self.net.z, slot, piece).wait_send())

    def begin_one(self, target, slot, produce):
        mine = aligned(self.net.c * self.chunk, self.chunk)
        theirs = aligned((1 - self.net.c) * self.chunk, self.chunk)

        def write(cols, value):
            self.tile[...] = value
            self.out[target, :, cols] = self.tile[mine, :].astype(BF)
            self.mate_out[slot, :, cols] = self.tile[theirs, :].astype(BF)

        produce(target, write)
        self.each_piece(lambda piece: self.to_mate(target, slot, piece).start())

    def leave(self, target, side, hop):
        @pl.when((hop > 0) & jnp.logical_not(self.fed(side)))
        def _():
            self.each_piece(lambda piece: self.pass_piece(target, side, hop, piece, False))

    def begin(self, produce, between=None):
        net = self.net

        @pl.loop(0, net.n_l)
        def _(j):
            hop = net.n_l - 1 - j

            def act(target, side):
                @pl.when((hop > 0) | (side == 0))
                def _():
                    @pl.when((hop > 0) & self.place(target + 2 * side - 1))
                    def _():
                        self.mate_sent(side)

                    self.begin_one(target, side + (2 - side) * (1 // (hop + 1)), produce)
                    self.leave(target, side, hop)

            net.sides(hop, act)
            if between is not None:
                pl.when(j == 1)(between)

    def pass_piece(self, target, side, hop, piece, fed):
        self.to_mate(target, 0, piece).wait_recv()
        span = self.span(piece)
        value = self.out[target, span, :].astype(F32) + self.mate_in[target, span, :].astype(F32)
        if fed:
            self.came(target, piece)
            value = value + self.coming[target, span, :].astype(F32)
        self.out[target, span, :] = value.astype(BF)
        self.onward(target, side, hop, piece).start()

    def open_total(self):
        net = self.net

        @self.each_piece
        def _(piece):
            self.to_mate(net.z, 0, piece).wait_recv()
            span = self.span(piece)
            self.total[span, :] = self.out[net.z, span, :].astype(F32) + self.mate_in[net.z, span, :].astype(F32)

    def wave(self, at, near=False, between=None):
        net = self.net
        above = at if near else net.n_l - at

        @pl.loop(0, 2)
        def _(turn):
            side = (1 - (2 * net.z) // net.n_l + turn) % 2
            target = net.n_l - 1 - above + (2 * above - net.n_l + 1) * side
            hop = (target - net.z) * (2 * side - 1)

            @self.each_piece
            def _(piece):
                span = self.span(piece)

                @pl.when(self.fed(side) & (hop > 0))
                def _():
                    self.pass_piece(target, side, hop, piece, True)

                @pl.when(self.fed(side) & (hop == 0))
                def _():
                    slot = net.z + (net.n_l - net.z) * (1 - side)
                    self.came(slot, piece)
                    self.total[span, :] = self.total[span, :] + self.coming[slot, span, :].astype(F32)

                if between is not None:
                    between(((at - 1) * 2 + turn) * self.pieces + piece)

    def passes_between(self, wave, near, between):
        net = self.net
        above = wave if near else net.n_l - wave

        @pl.loop(0, 2)
        def _(turn):
            side = (1 - (2 * net.z) // net.n_l + turn) % 2
            target = net.n_l - 1 - above + (2 * above - net.n_l + 1) * side
            hop = (target - net.z) * (2 * side - 1)

            @self.each_piece
            def _(piece):
                @pl.when((hop > 0) & self.fed(side))
                def _():
                    self.pass_piece(target, side, hop, piece, True)

                between(turn, piece)

    def finals(self):
        net = self.net

        @self.each_piece
        def _(piece):
            self.to_mate(net.z, 0, piece).wait_recv()
            span = self.span(piece)
            self.total[span, :] = self.out[net.z, span, :].astype(F32) + self.mate_in[net.z, span, :].astype(F32)

        @pl.loop(0, 2)
        def _(turn):
            side = (1 - (2 * net.z) // net.n_l + turn) % 2

            @pl.when(self.fed(side))
            def _():
                slot = net.z + (net.n_l - net.z) * (1 - side)

                @self.each_piece
                def _(piece):
                    span = self.span(piece)
                    self.came(slot, piece)
                    self.total[span, :] = self.total[span, :] + self.coming[slot, span, :].astype(F32)

    def finish(self):
        net = self.net
        self.mate_sent(2)
        for side in range(2):
            pl.when(self.place(net.z + 2 * side - 1))(functools.partial(self.mate_sent, side))

        @pl.loop(1, net.n_l)
        def _(hop):
            net.sides(
                hop,
                lambda target, side: self.each_piece(
                    lambda piece: self.onward(target, side, hop, piece).wait_send()
                ),
            )


class GridSum:
    def __init__(self, net, stage, came, sems):
        self.net, self.stage, self.came, self.sems = net, stage, came, sems
        self.half = stage.shape[1] // 2
        self.rows = next(r for r in (176, 128, 96, 64, 32, 16) if self.half % r == 0)
        self.cols = range(1, net.tall)
        self.along = range(1, net.wide)
        self.bases = self.layout(net.n_f)

    @staticmethod
    def layout(n_f):
        tall = 2 if n_f % 2 == 0 else 1
        wide = n_f // tall
        sizes = [(wide - 1) * tall, (tall - 1) * wide, tall - 1, wide - 1]
        return [sum(sizes[:at]) for at in range(5)]

    @staticmethod
    def scratch(n_f, rows, columns):
        count = GridSum.layout(n_f)[4]
        return [
            pltpu.VMEM((n_f, rows, columns), BF),
            pltpu.VMEM((count, rows // 2, columns), BF),
            pltpu.SemaphoreType.DMA((2, count + GridEnd.count(n_f))),
        ]

    def slot(self, kind, i, j):
        base = self.bases[kind]
        return base + [(j - 1) * self.net.tall + i, (i - 1) * self.net.wide + j, i - 1, j - 1][kind]

    def rank(self, i, j):
        net = self.net
        return ((net.a + i) % net.tall) * net.wide + (net.b + j) % net.wide

    def owner(self, at):
        return self.rank(at // self.net.wide, at % self.net.wide)

    def copy(self, kind, i, j):
        half = kind % 2
        along = kind in (0, 3)
        slot = self.slot(kind, i, j)
        at = i * self.net.wide + j
        return put(
            self.stage.at[at, pl.ds(half * self.half, self.half)],
            self.came.at[slot],
            self.sems.at[0, slot],
            self.sems.at[1, slot],
            fsdp=self.rank(0, j) if along else self.rank(i, 0),
        )

    def first(self, at):
        i, j = at // self.net.wide, at % self.net.wide

        @pl.when(j > 0)
        def _():
            self.copy(0, i, j).start()

        @pl.when(i > 0)
        def _():
            self.copy(1, i, j).start()

    def gather(self, half, at, slots, write):
        @pl.loop(0, self.half // self.rows)
        def _(step):
            span = aligned(half * self.half + step * self.rows, self.rows, 16)
            value = self.stage[at, span, :].astype(F32)
            for slot in slots:
                value = value + self.came[slot, aligned(step * self.rows, self.rows, 16), :].astype(F32)
            write(span, value)

    def wait(self, *copies):
        for kind, i, j in copies:
            self.copy(kind, i, j).wait_recv()
        return [self.slot(*copy) for copy in copies]

    def second(self):
        def keep(at):
            def write(span, value):
                self.stage[at, span, :] = value.astype(BF)

            return write

        for i in self.cols:
            at = i * self.net.wide
            self.gather(0, at, self.wait(*[(0, i, j) for j in self.along]), keep(at))
            self.copy(2, i, 0).start()
        for j in self.along:
            self.gather(1, j, self.wait(*[(1, i, j) for i in self.cols]), keep(j))
            self.copy(3, 0, j).start()

    def sum_first(self):
        def keep(at):
            def write(span, value):
                self.stage[at, span, :] = value.astype(BF)

            return write

        for i in range(self.net.tall):
            at = i * self.net.wide
            self.gather(0, at, self.wait(*[(0, i, j) for j in self.along]), keep(at))
        for j in range(self.net.wide):
            self.gather(1, j, self.wait(*[(1, i, j) for i in self.cols]), keep(j))

    def hand_on(self, out):
        net = self.net
        shards = [(0, 0), (0, 1), *[(i * net.wide, 0) for i in self.cols], *[(j, 1) for j in self.along]]
        return [
            pltpu.make_async_copy(
                self.stage.at[at, pl.ds(half * self.half, self.half)], out.at[k], self.sems.at[0, self.bases[4] + k]
            )
            for k, (at, half) in enumerate(shards)
        ]

    def last(self, out):
        def write(span, value):
            out[span, :] = value

        self.gather(
            0, 0, self.wait(*[(0, 0, j) for j in self.along], *[(2, i, 0) for i in self.cols]), write
        )
        self.gather(
            1, 0, self.wait(*[(1, i, 0) for i in self.cols], *[(3, 0, j) for j in self.along]), write
        )

    def finish_first(self):
        for i in range(self.net.tall):
            for j in range(self.net.wide):
                if j:
                    self.copy(0, i, j).wait_send()
                if i:
                    self.copy(1, i, j).wait_send()

    def finish(self):
        self.finish_first()
        for i in self.cols:
            self.copy(2, i, 0).wait_send()
        for j in self.along:
            self.copy(3, 0, j).wait_send()


class GridEnd:
    def __init__(self, net, sums, came, sems):
        self.net, self.sums, self.came, self.sems = net, sums, came, sems

    @staticmethod
    def count(n_f):
        tall = 2 if n_f % 2 == 0 else 1
        return tall + n_f // tall

    @staticmethod
    def scratch(n_f, rows, columns):
        count = GridEnd.count(n_f)
        return [pltpu.VMEM((count, rows // 2, columns), BF), pltpu.SemaphoreType.DMA((2, count - 2))]

    def copies(self):
        net = self.net
        f = [((net.a + i) % net.tall) * net.wide + net.b for i in range(1, net.tall)]
        f += [net.a * net.wide + (net.b + j) % net.wide for j in range(1, net.wide)]
        return [
            put(self.sums.at[2 + k], self.came.at[k], self.sems.at[0, k], self.sems.at[1, k], fsdp=to)
            for k, to in enumerate(f)
        ]

    def start(self):
        for copy in self.copies():
            copy.start()

    def finish(self):
        for copy in self.copies():
            copy.wait()


class PacketSum:
    def __init__(self, net, out, seq_in, total, fsdp_in, sems):
        self.net, self.out, self.seq_in, self.total, self.fsdp_in, self.sems = net, out, seq_in, total, fsdp_in, sems

    @staticmethod
    def scratch(n_f, n_s):
        return [
            pltpu.VMEM((n_s, n_f, SMALL, 128), F32),
            pltpu.VMEM((n_s, n_f, SMALL, 128), F32),
            pltpu.VMEM((n_f, SMALL, 128), F32),
            pltpu.VMEM((n_f, SMALL, 128), F32),
            pltpu.SemaphoreType.DMA((2 * (n_f + n_s),)),
        ]

    def one(self, k):
        to = (self.net.s + k) % self.net.n_s
        return put(self.out.at[to], self.seq_in.at[k], self.sems.at[2 * k], self.sems.at[2 * k + 1], seq=to)

    def two(self, k):
        to = (self.net.f + k) % self.net.n_f
        at = 2 * (self.net.n_s + k)
        return put(self.total.at[to], self.fsdp_in.at[k], self.sems.at[at], self.sems.at[at + 1], fsdp=to)

    def start(self, terms, width):
        net = self.net
        per = 128 // width
        for tile in range(net.n_f * net.n_s // per):
            value = terms[:, tile * 128 : (tile + 1) * 128]
            for j in range(per):
                f, s = divmod(tile * per + j, net.n_s)
                self.out[s, f] = pltpu.roll(value, 128 - j * width, axis=1) if j else value
        for k in range(1, net.n_s):
            self.one(k).start()

    def middle(self):
        net = self.net
        total = self.out[net.s]
        for k in range(1, net.n_s):
            self.one(k).wait()
            total = total + self.seq_in[k]
        self.total[...] = total
        for k in range(1, net.n_f):
            self.two(k).start()

    def finish(self, result):
        net = self.net
        total = self.total[net.f]
        for k in range(1, net.n_f):
            self.two(k).wait()
            total = total + self.fsdp_in[k]
        result[...] = total


def norm_backward(rows, source, grad, gain, terms, at, write):
    terms[at : at + 2, :] = jnp.zeros((2, terms.shape[1]), F32)

    @pl.loop(0, rows // 32)
    def _(i):
        span = aligned(i * 32, 32)
        scaled, inverse = normalize(source[span, :].astype(F32))
        value = grad[span, :]
        upstream = value * gain
        inner = jnp.mean(upstream, -1, keepdims=True)
        cross = jnp.mean(upstream * scaled, -1, keepdims=True)
        terms[at : at + 1, :] = terms[at : at + 1, :] + jnp.sum(value * scaled, 0, keepdims=True)
        terms[at + 1 : at + 2, :] = terms[at + 1 : at + 2, :] + jnp.sum(value, 0, keepdims=True)
        write(i, span, inverse * (upstream - inner - scaled * cross))


def layer_kernel(
    tok,
    gain_one,
    shift_one,
    gain_two,
    shift_two,
    bias,
    wq_own,
    wo_own,
    wg_own,
    wu_own,
    wd_own,
    gout_own,
    cosine,
    sine,
    q_o,
    k_o,
    kt_o,
    v_o,
    att_o,
    lse_o,
    n1_o,
    gains_o,
    wq_o,
    wo_o,
    dm_o,
    datt_o,
    dmid_o,
    top_o,
    terms_o,
    gate_o,
    up_o,
    down_o,
    rows,
    gout,
    wq,
    wo,
    wg,
    wu,
    wd,
    q,
    k,
    kt,
    v,
    vt,
    ot,
    att,
    hidden,
    dgate,
    dup,
    mid,
    low,
    packet,
    packets,
    tiles,
    total,
    *rest,
):
    net = Net()
    chunk, width = tok.shape
    length = chunk * net.n_s
    depth = wq_own.shape[1]
    columns = wq_own.shape[2]
    heads = columns // HEAD
    pair = 2 * chunk
    buffers, rest = rest[:4], rest[4:]
    folds = []
    for _ in range(3):
        folds.append(Fold(net, tiles, total, *buffers, *rest[:4]))
        rest = rest[4:]
    att_fold, normed_fold, top_fold = folds
    line_sems = [rest[at : at + 3] for at in (0, 3, 6, 9)]
    rest = rest[12:]
    spread_sems, rest = rest[:5], rest[5:]
    gate_sum, up_sum, down_sum = [GridSum(net, *rest[at : at + 3]) for at in (0, 3, 6)]
    sums = (down_sum, gate_sum, up_sum)
    pk_sems, copy_sems, n1_sems, dm_sems, free_sem = rest[9:]
    copies = Copies(copy_sems)
    n1 = att_fold.mate_out

    packet[...] = jnp.zeros(packet.shape, F32)
    own = gain_one.shape[1]
    for at, part in enumerate((gain_one, shift_one, gain_two, shift_two)):
        packet[at : at + 1, 0:own] = part[...].astype(F32)
    packet[4:7, 0:own] = bias[...].astype(F32)
    def wq_part(f, half):
        if half is None:
            return wq.at[:, aligned(f * depth, depth), :]
        return wq.at[:, aligned(f * depth + half * (depth // 2), depth // 2), :]

    spread_q = Spread(net, wq_own, wq_part, spread_sems[0])
    spread_o, spread_g, spread_u, spread_d = [
        Spread(net, own, columns_of(full, depth), sems)
        for own, full, sems in zip((wo_own, wg_own, wu_own, wd_own), (wo, wg, wu, wd), spread_sems[1:])
    ]
    pk = Packets(net, packet, packets, pk_sems)
    line = Line(net, tok, rows_of(rows, chunk), *line_sems[0])
    gout_line = Line(net, gout_own, rows_of(gout, chunk), *line_sems[1])
    n2_line = Line(net, low, rows_of(rows, chunk), *line_sems[2])
    dm_line = Line(net, low, rows_of(rows, chunk), *line_sems[3])

    for ready in (line, spread_q, spread_o, spread_g, spread_u, spread_d, gout_line):
        ready.prepare()
    net.barrier()

    def pairs(which, hop):
        net.sides(hop, lambda other, side: which.pair(other))

    def blocks(hop, act):
        def once(other, side):
            @pl.when((hop > 0) | (side == 0))
            def _():
                act(other, side)

        net.sides(hop, once)

    pk.start()
    line.start()
    spread_q.start()
    pk.middle()
    pk.finish()
    pk.unpack(gains_o, width // (net.n_f * net.n_s))

    def project_block(other, side):
        span = aligned(other * pair, pair)
        gain, shift = gains_o[0:1, :], gains_o[1:2, :]

        for part in range(2):

            @pl.loop(0, chunk // 32)
            def _(i):
                at = aligned((2 * other + part) * chunk + i * 32, 32)
                scaled, _ = normalize(rows[at, :].astype(F32))
                n1[part, aligned(i * 32, 32), :] = (scaled * gain + shift).astype(BF)

        keeps = [
            pltpu.make_async_copy(
                n1.at[part], n1_o.at[aligned((2 * other + part) * chunk, chunk)], n1_sems.at[part]
            )
            for part in range(2)
        ]
        for copy in keeps:
            copy.start()
        left = n1[0:2].reshape(pair, width)
        cols = aligned(net.s * columns, columns)
        tables = cosine[span, :], sine[span, :]
        for kind in range(3):
            value = dot(left, wq[kind]) + gains_o[4 + kind : 5 + kind, cols]
            if kind == 0:
                q[span, :] = rotary(value, *tables).astype(BF)
            elif kind == 1:
                value = rotary(value, *tables)
                k[span, :] = value.astype(BF)
                kt[...] = value.T.astype(BF)
            else:
                v[...] = value.astype(BF)
                vt[:, span] = value.T.astype(BF)
        for copy in (
            pltpu.make_async_copy(kt, kt_o.at[:, span], n1_sems.at[2]),
            pltpu.make_async_copy(v, v_o.at[span], n1_sems.at[3]),
        ):
            copy.start()
            keeps.append(copy)
        for copy in keeps:
            copy.wait()

    line.here()
    for hop in range(1, net.n_l - 1):
        line.step(hop)
        if hop == 1:
            spread_q.relay()
        pairs(line, hop)
    spread_o.start()
    spread_q.finish()
    spread_g.start()
    pl.loop(0, net.n_l - 1)(lambda hop: blocks(hop, project_block))
    spread_o.relay()
    spread_u.start()
    line.step(net.n_l - 1)
    gout_line.start()
    pairs(line, net.n_l - 1)
    blocks(net.n_l - 1, project_block)
    q_copy = copies.start(q, q_o)
    for pair_of in ((wq, wq_o), (k, k_o)):
        copies.start(*pair_of)
    spread_o.finish()
    line.finish()

    def attend(i):
        lo, hi = i * pair, (i + 1) * pair

        @pl.loop(0, heads, unroll=2)
        def _(head):
            lane = lax.broadcasted_iota(jnp.int32, (1, columns), 1)
            here = jnp.where(lane // HEAD == head, HEAD**-0.5, 0.0).astype(BF)
            visible = lax.broadcasted_iota(jnp.int32, (pair, pair), 0) <= lax.broadcasted_iota(
                jnp.int32, (pair, pair), 1
            )
            head_rows = aligned(head * HEAD, HEAD)
            query = q[lo:hi, :] * here
            near = jnp.where(visible, dot_nt(k[lo:hi, :], query), NEG_LARGE)
            highest = jnp.max(near, 0, keepdims=True)
            if i:
                far = dot_nt(k[0:lo, :], query)
                highest = jnp.maximum(highest, jnp.max(far, 0, keepdims=True))
            near = jnp.exp(near - highest)
            sum_of = jnp.sum(near, 0, keepdims=True)
            out = dot(vt[head_rows, lo:hi], near.astype(BF))
            if i:
                far = jnp.exp(far - highest)
                sum_of = sum_of + jnp.sum(far, 0, keepdims=True)
                out = out + dot(vt[head_rows, 0:lo], far.astype(BF))
            ot[head_rows, :] = out / sum_of
            lse_o[pl.ds(head, 1), lo:hi] = highest + jnp.log(sum_of)

        att[lo:hi, :] = ot[...].T.astype(BF)

    def produce_attended(place, write):
        for i in range(net.n_l):
            pl.when(place == i)(functools.partial(attend, i))
        left = att[aligned(place * pair, pair), :]

        @pl.loop(0, width // TILE)
        def _(j):
            cols = aligned(j * TILE, TILE)
            write(cols, dot(left, wo[:, cols]))

    def relays():
        gout_line.step(1)
        spread_d.start()

    att_fold.begin(produce_attended, relays)
    copies.start(att, att_o)
    copies.start(wo, wo_o)
    if net.n_l > 2:
        gout_line.step(2)
    att_fold.open_total()
    spread_g.relay()
    for at in range(1, net.n_l):
        if 2 < at + 1 < net.n_l:
            gout_line.step(at + 1)
        att_fold.wave(at)
        if at == 1:
            spread_u.relay()
        if at == min(2, net.n_l - 1):
            spread_d.relay()
    gain_two, shift_two = gains_o[2:3, :], gains_o[3:4, :]

    @pl.loop(0, chunk // 32)
    def _(i):
        span = aligned(i * 32, 32)
        value = rows[aligned(net.s * chunk + i * 32, 32), :].astype(F32) + total[span, :]
        mid[span, :] = value
        scaled, _ = normalize(value)
        low[span, :] = (scaled * gain_two + shift_two).astype(BF)

    n2_line.prepare()
    n2_line.start()
    att_fold.finish()
    gout_line.here()
    pl.loop(1, net.n_l)(lambda hop: pairs(gout_line, hop))

    def forward_block(other):
        span = aligned(other * pair, pair)
        right = rows[span, :]
        half = hidden.shape[0] // 2

        @pl.loop(0, 2)
        def _(part):
            units = aligned(part * half, half, 16)
            gate = dot_nt(wg[units, :], right)
            up = dot_nt(wu[units, :], right)
            back = dot_nt(wd[units, :], gout[span, :])
            sigma = jax.nn.sigmoid(gate)
            active = gate * sigma
            hidden[units, span] = (active * up).astype(BF)
            dgate[units, span] = (back * up * (sigma * (1.0 + gate * (1.0 - sigma)))).astype(BF)
            dup[units, span] = (back * active).astype(BF)

    def produce_normed(place, write):
        span = aligned(place * pair, pair)
        left, right = dgate[:, span].T, dup[:, span].T

        @pl.loop(0, width // TILE)
        def _(j):
            cols = aligned(j * TILE, TILE)
            write(cols, dot(left, wg[:, cols]) + dot(right, wu[:, cols]))

    def begin_normed(other, side, hop):
        @pl.when(hop > 1)
        def _():
            normed_fold.mate_sent(side)

        normed_fold.begin_one(other, side + (2 - side) * (1 // (hop + 1)), produce_normed)

    def forward_blocks(hop):
        def act(other, side):
            forward_block(other)

            @pl.when(jnp.logical_not(normed_fold.fed(side)))
            def _():
                begin_normed(other, side, hop)
                normed_fold.leave(other, side, hop)

        net.sides(hop, act)

    def begin_fed(hop):
        def act(other, side):
            pl.when(normed_fold.fed(side))(lambda: begin_normed(other, side, hop))

        net.sides(hop, act)

    n2_line.here()
    for spread in (spread_g, spread_u, spread_d):
        spread.finish()
    forward_block(net.z)

    @pl.loop(1, net.n_l)
    def _(hop):
        n2_line.step(hop)
        pairs(n2_line, hop)
        pl.when(hop == 1)(lambda: normed_fold.begin_one(net.z, 2, produce_normed))
        forward_blocks(hop)
        pl.when(hop > 1)(lambda: begin_fed(hop - 1))

    begin_fed(net.n_l - 1)

    def weight_terms(task):
        at, kind = net.n_f - 1 - task // 3, task % 3
        cols = aligned(gate_sum.owner(at) * depth, depth)
        for way, (grid_sum, left, right) in enumerate(
            ((down_sum, hidden, gout), (gate_sum, dgate, rows), (up_sum, dup, rows))
        ):

            @pl.when(kind == way)
            def _():
                half = left.shape[0] // 2

                @pl.loop(0, 2)
                def _(part):
                    units = aligned(part * half, half, 16)
                    grid_sum.stage[at, units, :] = dot(left[units, :], right[:, cols]).astype(BF)

                grid_sum.first(at)

    tasks = 3 * net.n_f
    waves = max(net.n_l - 2, 1)
    each = -(-tasks // (2 * normed_fold.pieces * waves))
    for wave in range(net.n_l - waves, net.n_l):

        def between(turn, piece):
            slot = ((wave - net.n_l + waves) * 2 + turn) * normed_fold.pieces + piece

            @pl.loop(0, each)
            def _(i):
                pl.when(slot * each + i < tasks)(lambda: weight_terms(slot * each + i))

        normed_fold.passes_between(wave, True, between)
    normed_fold.finals()
    n2_line.finish()

    def beside(act):
        act(net.mate)
        for side in range(2):
            pl.when(n2_line.goes_on(side))(lambda: act(net.s + 2 - 4 * side))

    beside(lambda to: pl.semaphore_signal(free_sem, 1, device_id={"seq": to}, device_id_type=MESH))

    def write_middle(i, span, value):
        value = value + gout[aligned(net.s * chunk + i * 32, 32), :].astype(F32)
        dmid_o[span, :] = value
        low[span, :] = value.astype(BF)

    terms_o[...] = jnp.zeros(terms_o.shape, F32)
    norm_backward(chunk, mid, total, gain_two, terms_o, 2, write_middle)
    ends = (net.z + net.n_l - 1) // net.n_l + (2 * net.n_l - 2 - net.z) // net.n_l
    pl.semaphore_wait(free_sem, 1 + ends)
    dm_line.prepare()
    dm_line.start()
    normed_fold.finish()

    def produce_top(place, write):
        left = hidden[:, aligned(place * pair, pair)].T

        @pl.loop(0, width // TILE)
        def _(j):
            cols = aligned(j * TILE, TILE)
            write(cols, dot(left, wd[:, cols]))

    copies.wait(q_copy)
    datt = q

    def dm_copy(other):
        span = aligned(other * pair, pair)
        return pltpu.make_async_copy(rows.at[span], dm_o.at[span], dm_sems.at[other])

    def back_block(other, side):
        span = aligned(other * pair, pair)
        dm_copy(other).start()
        datt[span, :] = dot_nt(rows[span, :], wo[...]).astype(BF)

    dm_line.here()
    dm_line.step(1)
    top_fold.begin(produce_top)
    back_block(net.z, 0)
    top_fold.open_total()
    for at in range(1, net.n_l):
        if at + 1 < net.n_l:
            dm_line.step(at + 1)
        top_fold.wave(at)
        pairs(dm_line, at)
        net.sides(at, back_block)
    copies.start(datt, datt_o)

    @pl.loop(0, chunk // 32)
    def _(i):
        span = aligned(i * 32, 32)
        top_fold.out[net.z, span, :] = (mid[span, :] + total[span, :]).astype(BF)

    copies.start(top_fold.out.at[net.z], top_o)
    top_fold.finish()
    gout_line.finish()
    dm_line.finish()
    hands = []
    for grid_sum, out in zip(sums, (down_o, gate_o, up_o)):
        grid_sum.sum_first()
        hands.extend(grid_sum.hand_on(out))
        for copy in grid_sum.hand_on(out):
            copy.start()
    for grid_sum in sums:
        grid_sum.finish_first()
    for copy in hands:
        copy.wait()
    copies.wait()
    pl.loop(0, net.n_l)(lambda other: dm_copy(other).wait())


def layer_part(tokens, norms, wq, wo, wg, wu, wd, gout, tables):
    chunk, width = tokens.shape
    n_f, n_s = lax.axis_size("fsdp"), lax.axis_size("seq")
    length = chunk * n_s
    depth, columns = wq.shape[1:]
    units = wg.shape[0]
    shape = jax.ShapeDtypeStruct
    wide, head, turned, weight = (length, width), (length, columns), (units, length), (units, width)
    return pl.pallas_call(
        layer_kernel,
        name="layer",
        out_shape=[
            shape(head, BF),
            shape(head, BF),
            shape((columns, length), BF),
            shape(head, BF),
            shape(head, BF),
            shape((8, length), F32),
            shape(wide, BF),
            shape((SMALL, width), F32),
            shape((3, width, columns), BF),
            shape((columns, width), BF),
            shape(wide, BF),
            shape(head, BF),
            shape((chunk, width), F32),
            shape((chunk, width), BF),
            shape((SMALL, width), F32),
            *[shape((GridEnd.count(n_f), units // 2, depth), BF)] * 3,
        ],
        in_specs=[ANY, *[VMEM] * 5, *[ANY] * 6, VMEM, VMEM],
        out_specs=[*[ANY] * 5, VMEM, ANY, VMEM, *[ANY] * 4, VMEM, ANY, VMEM, *[ANY] * 3],
        scratch_shapes=[
            pltpu.VMEM(wide, BF),
            pltpu.VMEM(wide, BF),
            pltpu.VMEM((3, width, columns), BF),
            pltpu.VMEM((columns, width), BF),
            *[pltpu.VMEM(weight, BF)] * 3,
            pltpu.VMEM(head, BF),
            pltpu.VMEM(head, BF),
            pltpu.VMEM((columns, 2 * chunk), BF),
            pltpu.VMEM((2 * chunk, columns), BF),
            pltpu.VMEM((columns, length), BF),
            pltpu.VMEM((columns, 2 * chunk), F32),
            pltpu.VMEM(head, BF),
            *[pltpu.VMEM(turned, BF)] * 3,
            pltpu.VMEM((chunk, width), F32),
            pltpu.VMEM((chunk, width), BF),
            pltpu.VMEM((SMALL, 128), F32),
            pltpu.VMEM((n_s, n_f, SMALL, 128), F32),
            *Fold.shared(chunk, width),
            *Fold.buffers(n_s, chunk, width),
            *Fold.sems(n_s) * 3,
            *Line.sems(n_s) * 4,
            *[pltpu.SemaphoreType.DMA((Spread.count(n_f),))] * 5,
            *GridSum.scratch(n_f, units, depth) * 3,
            pltpu.SemaphoreType.DMA((Packets.count(n_f, n_s),)),
            pltpu.SemaphoreType.DMA((8,)),
            pltpu.SemaphoreType.DMA((4,)),
            pltpu.SemaphoreType.DMA((n_s // 2,)),
            pltpu.SemaphoreType.REGULAR,
        ],
        compiler_params=pltpu.CompilerParams(
            collective_id=1, has_side_effects=True, vmem_limit_bytes=VMEM_BYTES
        ),
        cost_estimate=pl.CostEstimate(
            flops=2 * length * width * (4 * columns + 9 * units),
            bytes_accessed=8 * length * width,
            transcendentals=length * (length * columns // HEAD + units),
        ),
    )(tokens, *norms, wq, wo, wg, wu, wd, gout, *tables)


def back_kernel(
    datt_in,
    q_in,
    k_in,
    kt_in,
    v_in,
    att_in,
    wq_in,
    n1_in,
    dm_in,
    down_in,
    gate_in,
    up_in,
    lse,
    tok,
    dmid,
    gains,
    terms_in,
    cosine,
    sine,
    gin_o,
    small_o,
    out_o,
    qkv_o,
    down_o,
    gate_o,
    up_o,
    datt,
    q,
    k,
    kt,
    v,
    att,
    wq,
    n1,
    dm,
    query,
    upstream,
    inners,
    dk,
    dv,
    dqt,
    dproj,
    terms,
    tiles,
    total,
    *rest,
):
    net = Net()
    chunk, width = tok.shape
    length, columns = q_in.shape
    heads = columns // HEAD
    pair = 2 * chunk
    depth = width // net.n_f
    block = 256
    buffers, rest = rest[:4], rest[4:]
    fold_sems, rest = rest[:4], rest[4:]
    packet_scratch, rest = rest[:5], rest[5:]
    out_sum, qkv_sum = GridSum(net, *rest[:3]), GridSum(net, *rest[3:6])
    ends = [
        GridEnd(net, rest[at], came, rest[at + 1]) for at, came in ((6, down_o), (8, gate_o), (10, up_o))
    ]
    copy_sems, column_sems = rest[12:]

    copies = Copies(copy_sems)
    loads = [
        copies.start(src, dst)
        for src, dst in (
            (datt_in, datt),
            (q_in, q),
            (k_in, k),
            (kt_in, kt),
            (v_in, v),
            (att_in, att),
            (wq_in, wq),
            (down_in, ends[0].sums),
            (gate_in, ends[1].sums),
            (up_in, ends[2].sums),
        )
    ]
    def load(at, way):
        src, dst = ((n1_in, n1), (dm_in, dm))[way]
        cols = aligned(qkv_sum.owner(at) * depth, depth)
        return pltpu.make_async_copy(src.at[:, cols], dst.at[at % 2], column_sems.at[way, at % 2])

    for at in range(net.n_f - 1, max(net.n_f - 3, -1), -1):
        for way in range(2):
            load(at, way).start()

    @pl.loop(0, length // block)
    def _(i):
        span = aligned(i * block, block)
        dk[span, :] = jnp.zeros((block, columns), F32)
        dv[span, :] = jnp.zeros((block, columns), F32)

    net.barrier()
    copies.wait(*loads[:6])

    def start_ends():
        for load_of in loads[7:]:
            load_of.wait()
        for end in ends:
            end.start()


    of_head = (
        lax.broadcasted_iota(jnp.int32, (8, columns), 1) // HEAD
        == lax.broadcasted_iota(jnp.int32, (8, columns), 0)
    ).astype(F32)

    @pl.loop(0, length // block)
    def _(i):
        span = aligned(i * block, block)
        product = datt[span, :].astype(F32) * att[span, :].astype(F32)
        inners[:, span] = lax.dot_general(
            of_head,
            product,
            (((1,), (1,)), ((), ())),
            precision=lax.Precision.HIGHEST,
            preferred_element_type=F32,
        )

    @pl.loop(0, heads, unroll=2)
    def _(head):
        lane = lax.broadcasted_iota(jnp.int32, (1, columns), 1)
        here = jnp.where(lane // HEAD == head, 1.0, 0.0).astype(BF)
        scale = HEAD**-0.5
        visible = lax.broadcasted_iota(jnp.int32, (block, block), 0) <= lax.broadcasted_iota(
            jnp.int32, (block, block), 1
        )
        head_rows = aligned(head * HEAD, HEAD)

        @pl.loop(0, length // block)
        def _(i):
            span = aligned(i * block, block)
            query[span, :] = q[span, :] * (here * scale)
            upstream[span, :] = datt[span, :] * here

        pl.when(head == min(1, heads - 1))(start_ends)

        for j in range(length // block):
            at, end = j * block, (j + 1) * block
            keys, values, turned = k[at:end, :], v[at:end, :], kt[head_rows, at:end]

            def part(lo, hi, near):
                probs = jnp.exp(dot_nt(keys, query[lo:hi, :]) - lse[pl.ds(head, 1), lo:hi])
                if near:
                    probs = jnp.where(visible, probs, 0.0)
                grads = dot_nt(values, upstream[lo:hi, :])
                scores = (probs * (grads - inners[pl.ds(head, 1), lo:hi])).astype(BF)
                out = dot(turned, scores)
                dqt[head_rows, lo:hi] = dqt[head_rows, lo:hi] + out if j else out
                return dot(probs.astype(BF), upstream[lo:hi, :]), dot(scores, query[lo:hi, :])

            value_grads, key_grads = part(at, end, True)
            if end < length:
                more_values, more_keys = part(end, length, False)
                value_grads, key_grads = value_grads + more_values, key_grads + more_keys
            dv[at:end, :] = dv[at:end, :] + value_grads
            dk[at:end, :] = dk[at:end, :] + key_grads

    terms[...] = terms_in[...]
    bias_cols = aligned(net.s * columns, columns)

    @pl.loop(0, length // block)
    def _(i):
        span = aligned(i * block, block)
        tables = cosine[span, :], -sine[span, :]
        parts = [
            rotary((dqt[:, span].T * HEAD**-0.5).astype(BF).astype(F32), *tables).astype(BF),
            rotary(dk[span, :].astype(BF).astype(F32), *tables).astype(BF),
            dv[span, :].astype(BF),
        ]
        for kind in range(3):
            dproj[kind, span, :] = parts[kind]
            row = slice(4 + kind, 5 + kind)
            terms[row, bias_cols] = terms[row, bias_cols] + jnp.sum(parts[kind].astype(F32), 0, keepdims=True)

    def weight_terms(task):
        at = net.n_f - 1 - task // 2

        def loaded(way):
            load(at, way).wait()

        def next_load(way):
            pl.when(at >= 2)(lambda: load(at - 2, way).start())

        @pl.when(task % 2 == 0)
        def _():
            loaded(0)
            left = n1[at % 2].T
            for kind in range(3):
                qkv_sum.stage[at, kind * depth : (kind + 1) * depth, :] = dot(left, dproj[kind]).astype(BF)
            next_load(0)
            qkv_sum.first(at)

        @pl.when(task % 2 == 1)
        def _():
            loaded(1)
            out_sum.stage[at] = dot_tn(att[...], dm[at % 2]).astype(BF)
            next_load(1)
            out_sum.first(at)

    def produce(place, write):
        span = aligned(place * pair, pair)

        @pl.loop(0, width // TILE)
        def _(j):
            cols = aligned(j * TILE, TILE)
            value = dot_nt(dproj[0, span, :], wq[0, cols, :])
            for kind in range(1, 3):
                value = value + dot_nt(dproj[kind, span, :], wq[kind, cols, :])
            write(cols, value)

    fold = Fold(net, tiles, total, *buffers, *fold_sems)
    copies.wait(loads[6])
    fold.begin(produce)
    fold.open_total()
    tasks = 2 * net.n_f
    waves = max(net.n_l - 2, 1)
    each = -(-tasks // (2 * fold.pieces * waves))

    def between(slot):
        @pl.loop(0, each)
        def _(i):
            pl.when(slot * each + i < tasks)(lambda: weight_terms(slot * each + i))

    for at in range(1, waves + 1):
        fold.wave(at, between=between)
    for at in range(waves + 1, net.n_l):
        fold.wave(at)

    def write_input(i, span, value):
        gin_o[span, :] = value + dmid[span, :]

    norm_backward(chunk, tok, total, gains[0:1, :], terms, 0, write_input)
    packet_sum = PacketSum(net, *packet_scratch)
    packet_sum.start(terms, width // (net.n_f * net.n_s))
    for grid_sum in (qkv_sum, out_sum):
        grid_sum.second()
    packet_sum.middle()
    packet_sum.finish(small_o)
    for end in ends:
        end.finish()
    fold.finish()
    for grid_sum, out in ((qkv_sum, qkv_o), (out_sum, out_o)):
        grid_sum.last(out)
        grid_sum.finish()


def back_part(datt, q, k, kt, v, att, wq, n1, dm, down, gate, up, lse, tokens, dmid, gains, terms, tables):
    chunk, width = tokens.shape
    n_f, n_s = lax.axis_size("fsdp"), lax.axis_size("seq")
    length, columns = q.shape
    depth = width // n_f
    units = 2 * gate.shape[1]
    shape = jax.ShapeDtypeStruct
    return pl.pallas_call(
        back_kernel,
        name="back",
        out_shape=[
            shape((chunk, width), F32),
            shape((SMALL, 128), F32),
            shape((columns, depth), F32),
            shape((3 * depth, columns), F32),
            *[shape((GridEnd.count(n_f) - 2, units // 2, depth), BF)] * 3,
        ],
        in_specs=[ANY] * 12 + [VMEM] * 7,
        out_specs=[VMEM] * 4 + [ANY] * 3,
        scratch_shapes=[
            pltpu.VMEM((length, columns), BF),
            pltpu.VMEM((length, columns), BF),
            pltpu.VMEM((length, columns), BF),
            pltpu.VMEM((columns, length), BF),
            pltpu.VMEM((length, columns), BF),
            pltpu.VMEM((length, columns), BF),
            pltpu.VMEM((3, width, columns), BF),
            pltpu.VMEM((2, length, depth), BF),
            pltpu.VMEM((2, length, depth), BF),
            pltpu.VMEM((length, columns), BF),
            pltpu.VMEM((length, columns), BF),
            pltpu.VMEM((8, length), F32),
            pltpu.VMEM((length, columns), F32),
            pltpu.VMEM((length, columns), F32),
            pltpu.VMEM((columns, length), F32),
            pltpu.VMEM((3, length, columns), BF),
            pltpu.VMEM((SMALL, width), F32),
            *Fold.shared(chunk, width),
            *Fold.buffers(n_s, chunk, width),
            *Fold.sems(n_s, 8),
            *PacketSum.scratch(n_f, n_s),
            *GridSum.scratch(n_f, columns, depth),
            *GridSum.scratch(n_f, 3 * depth, columns),
            *GridEnd.scratch(n_f, units, depth) * 3,
            pltpu.SemaphoreType.DMA((10,)),
            pltpu.SemaphoreType.DMA((2, 2)),
        ],
        compiler_params=pltpu.CompilerParams(
            collective_id=3, has_side_effects=True, vmem_limit_bytes=VMEM_BYTES
        ),
        cost_estimate=pl.CostEstimate(
            flops=2 * length * columns * (8 * width + 5 * length),
            bytes_accessed=4 * length * width,
            transcendentals=length * length * columns // HEAD,
        ),
    )(datt, q, k, kt, v, att, wq, n1, dm, down, gate, up, lse, tokens, dmid, gains, terms, *tables)


def outputs_kernel(tall, small, *refs):
    plain, sums, came, refs = refs[:4], refs[4:7], refs[7:10], refs[10:]
    results, totals, parts = refs[:4], refs[4:7], refs[7:]
    own = parts[0].shape[1]
    for src, dst in zip(plain, results):
        dst[...] = src[...]
    for so_far, last, dst in zip(sums, came, totals):
        half = so_far.shape[1]
        count = last.shape[0]
        for at, slots in enumerate((range(tall - 1), range(tall - 1, count))):
            value = so_far[at].astype(F32)
            for slot in slots:
                value = value + last[slot].astype(F32)
            dst[at * half : (at + 1) * half, :] = value
    for at in range(4):
        parts[at][...] = small[at : at + 1, 0:own]
    parts[4][...] = small[4:7, 0:own]


def outputs_part(small, own, plain, sums, came):
    shape = jax.ShapeDtypeStruct
    tall = 2 if lax.axis_size("fsdp") % 2 == 0 else 1
    return pl.pallas_call(
        functools.partial(outputs_kernel, tall),
        name="outputs",
        out_shape=[shape(v.shape, v.dtype) for v in plain]
        + [shape((2 * v.shape[1], v.shape[2]), F32) for v in sums]
        + [shape((1, own), F32)] * 4
        + [shape((3, own), F32)],
        in_specs=[VMEM] * 11,
        out_specs=[VMEM] * 12,
        compiler_params=pltpu.CompilerParams(vmem_limit_bytes=VMEM_BYTES),
    )(small, *plain, *sums, *came)


def per_device(
    tokens,
    gain_one,
    shift_one,
    w_qkv,
    b_qkv,
    w_out,
    gain_two,
    shift_two,
    w_gate,
    w_up,
    w_down,
    grad_output,
):
    length = tokens.shape[1] * lax.axis_size("seq")
    width = gain_one.shape[0]
    norms = [v[None] for v in (gain_one, shift_one, gain_two, shift_two)] + [b_qkv]
    tables = rotary_tables(length)
    q, k, kt, v, att, lse, n1, gains, wq, _, dm, datt, dmid, top, terms, gate, up, down = layer_part(
        tokens[0], norms, w_qkv.transpose(1, 0, 2), w_out, w_gate.T, w_up.T, w_down, grad_output[0], tables
    )
    grad_input, small, out, qkv, *came = back_part(
        datt, q, k, kt, v, att, wq, n1, dm, down, gate, up, lse, tokens[0], dmid, gains, terms, tables
    )

    top, grad_input, qkv, out, down, gate, up, one, shift, two, shift_to, bias = outputs_part(
        small, width, (top, grad_input, qkv, out), (down, gate, up), came
    )
    return (
        top[None],
        grad_input[None],
        one[0],
        shift[0],
        qkv.reshape(3, -1, qkv.shape[1]).transpose(1, 0, 2),
        bias,
        out,
        two[0],
        shift_to[0],
        gate.T,
        up.T,
        down,
    )


def solution(mesh):
    whole = P(("fsdp", "seq"))
    rows = P("fsdp", "seq", None)
    inner = P("seq", "fsdp")
    outer = P("fsdp", "seq")
    heads = P("fsdp", None, "seq")
    bias = P(None, ("fsdp", "seq"))
    return jax.shard_map(
        per_device,
        mesh=mesh,
        in_specs=(rows, whole, whole, heads, bias, inner, whole, whole, outer, outer, inner, rows),
        out_specs=(rows, rows, whole, whole, heads, bias, inner, whole, whole, outer, outer, inner),
        check_vma=False,
    )
```

```python
import functools

import jax
import jax.numpy as jnp
import numpy as np
from jax import lax
from jax.experimental import pallas as pl
from jax.experimental.pallas import tpu as pltpu
from jax.sharding import PartitionSpec as P

HEAD = 64
ROT = 16
EPSILON = 1e-05
NEG_LARGE = -1e30
MESH = pl.DeviceIdType.MESH
ANY = pl.BlockSpec(memory_space=pl.ANY)
VMEM = pl.BlockSpec(memory_space=pltpu.VMEM)
BF = jnp.bfloat16
F32 = jnp.float32
VMEM_BYTES = 60 * 2**20
TILE = 512
SMALL = 8


def put(src, dst, send, recv, **device):
    return pltpu.make_async_remote_copy(
        src_ref=src, dst_ref=dst, send_sem=send, recv_sem=recv, device_id=device, device_id_type=MESH
    )


def dot(left, right):
    return jnp.dot(left, right, preferred_element_type=F32)


def dot_nt(left, right):
    return lax.dot_general(left, right, (((1,), (1,)), ((), ())), preferred_element_type=F32)


def dot_tn(left, right):
    return lax.dot_general(left, right, (((0,), (0,)), ((), ())), preferred_element_type=F32)


def aligned(start, size, unit=None):
    return pl.ds(pl.multiple_of(start, unit or size), size)


class Net:
    def __init__(self):
        self.n_f, self.n_s = lax.axis_size("fsdp"), lax.axis_size("seq")
        self.tall = 2 if self.n_f % 2 == 0 else 1
        self.wide = self.n_f // self.tall
        self.n_l = self.n_s // 2
        self.f, self.s = lax.axis_index("fsdp"), lax.axis_index("seq")
        self.a, self.b = self.f // self.wide, self.f % self.wide
        self.z, self.c = self.s // 2, self.s % 2
        self.mate = self.s + 1 - 2 * self.c

    def barrier(self):
        sem = pltpu.get_barrier_semaphore()
        for k in range(1, self.n_f):
            pl.semaphore_signal(
                sem, inc=1, device_id={"fsdp": (self.f + k) % self.n_f}, device_id_type=MESH
            )
        for k in range(1, self.n_s):
            pl.semaphore_signal(
                sem, inc=1, device_id={"seq": (self.s + k) % self.n_s}, device_id_type=MESH
            )
        pl.semaphore_wait(sem, self.n_f + self.n_s - 2)

    def sides(self, hop, act):
        @pl.loop(0, 2)
        def _(side):
            other = self.z + (2 * side - 1) * hop

            @pl.when((other >= 0) & (other < self.n_l))
            def _():
                act(other, side)


class Spread:
    def __init__(self, net, src, part, sems):
        self.net, self.src, self.part, self.sems = net, src, part, sems
        self.rows = [j for j in range(1, net.wide)]
        self.cols = [i for i in range(1, net.tall)]

    @staticmethod
    def count(n_f):
        tall = 2 if n_f % 2 == 0 else 1
        wide = n_f // tall
        return 1 + 2 * (wide - 1) + 2 * (tall - 1) + 4 * (wide - 1) * (tall - 1)

    def at(self, kind, i, j):
        w, t = len(self.rows), len(self.cols)
        base = {
            "own": 0,
            "row": 1,
            "col": 1 + 2 * w,
            "half0": 1 + 2 * w + 2 * t,
            "half1": 1 + 2 * w + 2 * t + 2 * w * t,
        }[kind]
        if kind == "own":
            return self.sems.at[0]
        k = j - 1 if kind == "row" else i - 1 if kind == "col" else (i - 1) * w + j - 1
        return self.sems.at[base + 2 * k], self.sems.at[base + 2 * k + 1]

    def rank(self, i, j):
        net = self.net
        return ((net.a + i) % net.tall) * net.wide + (net.b + j) % net.wide

    def back(self, i, j):
        net = self.net
        return ((net.a - i + net.tall) % net.tall) * net.wide + (net.b - j + net.wide) % net.wide

    def own(self):
        return pltpu.make_async_copy(self.src, self.part(self.net.f, None), self.at("own", 0, 0))

    def first(self, i, j):
        send, recv = self.at("row" if i == 0 else "col", i, j)
        place = self.part(self.net.f, None)
        return put(place, place, send, recv, fsdp=self.rank(i, j))

    def came(self, i, j):
        send, recv = self.at("row" if i == 0 else "col", i, j)
        place = self.part(self.back(i, j), None)
        return put(place, place, send, recv, fsdp=self.rank(i, j))

    def second(self, half, i, j, came=False):
        send, recv = self.at("half0" if half == 0 else "half1", i, j)
        origin = self.back(i, j) if came else self.back(0, j) if half == 0 else self.back(i, 0)
        place = self.part(origin, half)
        return put(place, place, send, recv, fsdp=self.rank(i, 0) if half == 0 else self.rank(0, j))

    def prepare(self):
        self.own().start()

    def start(self):
        self.own().wait()
        for i in self.cols:
            self.first(i, 0).start()
        for j in self.rows:
            self.first(0, j).start()

    def relay(self):
        for j in self.rows:
            self.came(0, j).wait_recv()
            for i in self.cols:
                self.second(0, i, j).start()
        for i in self.cols:
            self.came(i, 0).wait_recv()
            for j in self.rows:
                self.second(1, i, j).start()

    def finish(self):
        for j in self.rows:
            self.first(0, j).wait_send()
        for i in self.cols:
            self.first(i, 0).wait_send()
        for i in self.cols:
            for j in self.rows:
                for half in range(2):
                    self.second(half, i, j, came=True).wait_recv()
                    self.second(half, i, j).wait_send()


class Line:
    def __init__(self, net, src, part, recv, send, local):
        self.net, self.src, self.part, self.recv, self.send, self.local = net, src, part, recv, send, local
        self.pieces = recv.shape[1]
        self.rows = src.shape[0] // self.pieces

    @staticmethod
    def sems(n_s, pieces=1):
        return [
            pltpu.SemaphoreType.DMA((n_s, pieces)),
            pltpu.SemaphoreType.DMA((4, n_s // 2, pieces)),
            pltpu.SemaphoreType.DMA((1,)),
        ]

    def cut(self, ref, piece):
        return ref.at[aligned(piece * self.rows, self.rows)]

    def own(self):
        return pltpu.make_async_copy(self.src, self.part(self.net.s), self.local.at[0])

    def on_line(self, src, chunk, side, hop, piece):
        return put(
            self.cut(src, piece),
            self.cut(self.part(chunk), piece),
            self.send.at[side, hop, piece],
            self.recv.at[chunk, piece],
            seq=self.net.s + 2 - 4 * side,
        )

    def to_mate(self, src, chunk, side, hop, piece):
        return put(
            self.cut(src, piece),
            self.cut(self.part(chunk), piece),
            self.send.at[2 + side, hop, piece],
            self.recv.at[chunk, piece],
            seq=self.net.mate,
        )

    def goes_on(self, side):
        after = self.net.z + 1 - 2 * side
        return (after >= 0) & (after < self.net.n_l)

    def each_piece(self, act):
        pl.loop(0, self.pieces)(act)

    def prepare(self):
        self.own().start()

    def start(self):
        net = self.net
        self.own().wait()
        place = self.part(net.s)

        @self.each_piece
        def _(piece):
            for side in range(2):

                @pl.when(self.goes_on(side))
                def _():
                    self.on_line(place, net.s, side, 0, piece).start()

            self.to_mate(place, net.s, 0, 0, piece).start()

    def came(self, chunk, piece):
        place = self.cut(self.part(chunk), piece)
        put(place, place, self.send.at[0, 0, 0], self.recv.at[chunk, piece], seq=self.net.mate).wait_recv()

    def step(self, hop):
        net = self.net

        @self.each_piece
        def _(piece):
            def act(other, side):
                chunk = 2 * other + net.c
                self.came(chunk, piece)

                @pl.when(self.goes_on(side))
                def _():
                    self.on_line(self.part(chunk), chunk, side, hop, piece).start()

                self.to_mate(self.part(chunk), chunk, side, hop, piece).start()

            net.sides(hop, act)

    def pair(self, other):
        @self.each_piece
        def _(piece):
            self.came(2 * other + 1 - self.net.c, piece)

    def here(self):
        self.pair(self.net.z)

    def finish(self):
        net = self.net
        place = self.part(net.s)

        @self.each_piece
        def _(piece):
            for side in range(2):

                @pl.when(self.goes_on(side))
                def _():
                    self.on_line(place, net.s, side, 0, piece).wait_send()

            self.to_mate(place, net.s, 0, 0, piece).wait_send()

            @pl.loop(1, net.n_l)
            def _(hop):
                def act(other, side):
                    chunk = 2 * other + net.c

                    @pl.when(self.goes_on(side))
                    def _():
                        self.on_line(self.part(chunk), chunk, side, hop, piece).wait_send()

                    self.to_mate(self.part(chunk), chunk, side, hop, piece).wait_send()

                net.sides(hop, act)


class Packets:
    def __init__(self, net, src, buf, sems):
        self.net, self.src, self.buf, self.sems = net, src, buf, sems

    @staticmethod
    def count(n_f, n_s):
        return 1 + 2 * (n_f - 1) + 2 * (n_s - 1)

    def own(self):
        net = self.net
        return pltpu.make_async_copy(self.src, self.buf.at[net.s, net.f], self.sems.at[0])

    def one(self, k, came=False):
        net = self.net
        f = (net.f - k + net.n_f) % net.n_f if came else net.f
        place = self.buf.at[net.s, f]
        return put(
            place if came else self.src,
            place,
            self.sems.at[2 * k - 1],
            self.sems.at[2 * k],
            fsdp=(net.f + k) % net.n_f,
        )

    def two(self, k, came=False):
        net = self.net
        place = self.buf.at[(net.s - k + net.n_s) % net.n_s if came else net.s]
        at = 2 * (net.n_f - 1) + 2 * k - 1
        return put(place, place, self.sems.at[at], self.sems.at[at + 1], seq=(net.s + k) % net.n_s)

    def start(self):
        self.own().start()
        for k in range(1, self.net.n_f):
            self.one(k).start()

    def middle(self):
        self.own().wait()
        for k in range(1, self.net.n_f):
            self.one(k, came=True).wait_recv()
            self.one(k).wait_send()
        for k in range(1, self.net.n_s):
            self.two(k).start()

    def finish(self):
        for k in range(1, self.net.n_s):
            self.two(k, came=True).wait_recv()
            self.two(k).wait_send()

    def unpack(self, out, width):
        net = self.net
        per = 128 // width
        for tile in range(net.n_f * net.n_s // per):
            total = None
            for j in range(per):
                f, s = divmod(tile * per + j, net.n_s)
                piece = self.buf[s, f]
                if j:
                    piece = pltpu.roll(piece, j * width, axis=1)
                total = piece if total is None else total + piece
            out[:, tile * 128 : (tile + 1) * 128] = total


def rotary(values, cosine, sine):
    columns = values.shape[1]
    half = ROT // 2
    times = columns // 128

    def wide(table):
        return table if times == 1 else jnp.concatenate([table] * times, axis=1)

    lane = lax.broadcasted_iota(jnp.int32, values.shape, 1)
    other = jnp.where(
        lane % HEAD < half, pltpu.roll(values, columns - half, axis=1), pltpu.roll(values, half, axis=1)
    )
    return values * wide(cosine) + other * wide(sine)


def rotary_tables(length):
    half = ROT // 2
    freqs = np.float32(10000.0) ** (-np.arange(half, dtype=np.float32) * np.float32(2.0 / ROT))
    angles = np.arange(length, dtype=np.float32)[:, None] * freqs[None, :].astype(np.float32)
    cosine, sine = np.cos(angles), np.sin(angles)
    rest = np.zeros((length, HEAD - ROT), np.float32)
    keep = np.concatenate([cosine, cosine, rest + 1], 1)
    swap = np.concatenate([-sine, sine, rest], 1)
    return [np.tile(t, (1, 128 // HEAD)).astype(np.float32) for t in (keep, swap)]


def normalize(values):
    center = values - jnp.mean(values, -1, keepdims=True)
    inverse = lax.rsqrt(jnp.mean(center * center, -1, keepdims=True) + EPSILON)
    return center * inverse, inverse


class Copies:
    def __init__(self, sems):
        self.sems, self.all, self.open = sems, [], []

    def start(self, src, dst):
        copy = pltpu.make_async_copy(src, dst, self.sems.at[len(self.all)])
        copy.start()
        self.all.append(copy)
        self.open.append(copy)
        return copy

    def wait(self, *copies):
        for copy in copies or list(self.open):
            copy.wait()
            self.open = [c for c in self.open if c is not copy]


def columns_of(ref, depth):
    half_rows = ref.shape[0] // 2

    def part(f, half):
        span = aligned(f * depth, depth)
        if half is None:
            return ref.at[:, span]
        return ref.at[pl.ds(half * half_rows, half_rows), span]

    return part


def rows_of(ref, chunk):
    return lambda s: ref.at[aligned(s * chunk, chunk)]


class Fold:
    def __init__(self, net, tile, total, mate_in, coming, mate_out, out, mate_send, mate_recv, send, recv):
        self.net, self.tile, self.total = net, tile, total
        self.mate_in, self.coming, self.mate_out, self.out = mate_in, coming, mate_out, out
        self.mate_send, self.mate_recv, self.send, self.recv = mate_send, mate_recv, send, recv
        self.chunk = total.shape[0]
        self.pieces = recv.shape[1]
        self.rows = self.chunk // self.pieces

    @staticmethod
    def shared(chunk, width):
        return [pltpu.VMEM((2 * chunk, TILE), F32), pltpu.VMEM((chunk, width), F32)]

    @staticmethod
    def buffers(n_s, chunk, width):
        n_l = n_s // 2
        return [
            pltpu.VMEM((n_l, chunk, width), BF),
            pltpu.VMEM((n_l + 1, chunk, width), BF),
            pltpu.VMEM((3, chunk, width), BF),
            pltpu.VMEM((n_l, chunk, width), BF),
        ]

    @staticmethod
    def sems(n_s, pieces=4):
        n_l = n_s // 2
        return [
            pltpu.SemaphoreType.DMA((3, pieces)),
            pltpu.SemaphoreType.DMA((n_l, pieces)),
            pltpu.SemaphoreType.DMA((n_l, pieces)),
            pltpu.SemaphoreType.DMA((n_l + 1, pieces)),
        ]

    def place(self, other):
        return (other >= 0) & (other < self.net.n_l)

    def fed(self, side):
        return self.place(self.net.z + 1 - 2 * side)

    def span(self, piece):
        return aligned(piece * self.rows, self.rows)

    def each_piece(self, act):
        pl.loop(0, self.pieces)(act)

    def to_mate(self, target, slot, piece):
        span = self.span(piece)
        return put(
            self.mate_out.at[slot, span],
            self.mate_in.at[target, span],
            self.mate_send.at[slot, piece],
            self.mate_recv.at[target, piece],
            seq=self.net.mate,
        )

    def onward(self, target, side, hop, piece):
        span = self.span(piece)
        slot = target + (self.net.n_l - target) * (1 - side) * (1 // hop)
        return put(
            self.out.at[target, span],
            self.coming.at[slot, span],
            self.send.at[target, piece],
            self.recv.at[slot, piece],
            seq=self.net.s + 4 * side - 2,
        )

    def came(self, slot, piece):
        place = self.coming.at[slot, self.span(piece)]
        put(place, place, self.send.at[0, 0], self.recv.at[slot, piece], seq=self.net.mate).wait_recv()

    def mate_sent(self, slot):
        self.each_piece(lambda piece: self.to_mate(self.net.z, slot, piece).wait_send())

    def begin_one(self, target, slot, produce):
        mine = aligned(self.net.c * self.chunk, self.chunk)
        theirs = aligned((1 - self.net.c) * self.chunk, self.chunk)

        def write(cols, value):
            self.tile[...] = value
            self.out[target, :, cols] = self.tile[mine, :].astype(BF)
            self.mate_out[slot, :, cols] = self.tile[theirs, :].astype(BF)

        produce(target, write)
        self.each_piece(lambda piece: self.to_mate(target, slot, piece).start())

    def leave(self, target, side, hop):
        @pl.when((hop > 0) & jnp.logical_not(self.fed(side)))
        def _():
            self.each_piece(lambda piece: self.pass_piece(target, side, hop, piece, False))

    def begin(self, produce, between=None):
        net = self.net

        @pl.loop(0, net.n_l)
        def _(j):
            hop = net.n_l - 1 - j

            def act(target, side):
                @pl.when((hop > 0) | (side == 0))
                def _():
                    @pl.when((hop > 0) & self.place(target + 2 * side - 1))
                    def _():
                        self.mate_sent(side)

                    self.begin_one(target, side + (2 - side) * (1 // (hop + 1)), produce)
                    self.leave(target, side, hop)

            net.sides(hop, act)
            if between is not None:
                pl.when(j == 1)(between)

    def pass_piece(self, target, side, hop, piece, fed):
        self.to_mate(target, 0, piece).wait_recv()
        span = self.span(piece)
        value = self.out[target, span, :].astype(F32) + self.mate_in[target, span, :].astype(F32)
        if fed:
            self.came(target, piece)
            value = value + self.coming[target, span, :].astype(F32)
        self.out[target, span, :] = value.astype(BF)
        self.onward(target, side, hop, piece).start()

    def open_total(self):
        net = self.net

        @self.each_piece
        def _(piece):
            self.to_mate(net.z, 0, piece).wait_recv()
            span = self.span(piece)
            self.total[span, :] = self.out[net.z, span, :].astype(F32) + self.mate_in[net.z, span, :].astype(F32)

    def wave(self, at, near=False, between=None):
        net = self.net
        above = at if near else net.n_l - at

        @pl.loop(0, 2)
        def _(turn):
            side = (1 - (2 * net.z) // net.n_l + turn) % 2
            target = net.n_l - 1 - above + (2 * above - net.n_l + 1) * side
            hop = (target - net.z) * (2 * side - 1)

            @self.each_piece
            def _(piece):
                span = self.span(piece)

                @pl.when(self.fed(side) & (hop > 0))
                def _():
                    self.pass_piece(target, side, hop, piece, True)

                @pl.when(self.fed(side) & (hop == 0))
                def _():
                    slot = net.z + (net.n_l - net.z) * (1 - side)
                    self.came(slot, piece)
                    self.total[span, :] = self.total[span, :] + self.coming[slot, span, :].astype(F32)

                if between is not None:
                    between(((at - 1) * 2 + turn) * self.pieces + piece)

    def passes_between(self, wave, near, between):
        net = self.net
        above = wave if near else net.n_l - wave

        @pl.loop(0, 2)
        def _(turn):
            side = (1 - (2 * net.z) // net.n_l + turn) % 2
            target = net.n_l - 1 - above + (2 * above - net.n_l + 1) * side
            hop = (target - net.z) * (2 * side - 1)

            @self.each_piece
            def _(piece):
                @pl.when((hop > 0) & self.fed(side))
                def _():
                    self.pass_piece(target, side, hop, piece, True)

                between(turn, piece)

    def finals(self):
        net = self.net

        @self.each_piece
        def _(piece):
            self.to_mate(net.z, 0, piece).wait_recv()
            span = self.span(piece)
            self.total[span, :] = self.out[net.z, span, :].astype(F32) + self.mate_in[net.z, span, :].astype(F32)

        @pl.loop(0, 2)
        def _(turn):
            side = (1 - (2 * net.z) // net.n_l + turn) % 2

            @pl.when(self.fed(side))
            def _():
                slot = net.z + (net.n_l - net.z) * (1 - side)

                @self.each_piece
                def _(piece):
                    span = self.span(piece)
                    self.came(slot, piece)
                    self.total[span, :] = self.total[span, :] + self.coming[slot, span, :].astype(F32)

    def finish(self):
        net = self.net
        self.mate_sent(2)
        for side in range(2):
            pl.when(self.place(net.z + 2 * side - 1))(functools.partial(self.mate_sent, side))

        @pl.loop(1, net.n_l)
        def _(hop):
            net.sides(
                hop,
                lambda target, side: self.each_piece(
                    lambda piece: self.onward(target, side, hop, piece).wait_send()
                ),
            )


class GridSum:
    def __init__(self, net, stage, came, sems):
        self.net, self.stage, self.came, self.sems = net, stage, came, sems
        self.half = stage.shape[1] // 2
        self.rows = next(r for r in (176, 128, 96, 64, 32, 16) if self.half % r == 0)
        self.cols = range(1, net.tall)
        self.along = range(1, net.wide)
        self.bases = self.layout(net.n_f)

    @staticmethod
    def layout(n_f):
        tall = 2 if n_f % 2 == 0 else 1
        wide = n_f // tall
        sizes = [(wide - 1) * tall, (tall - 1) * wide, tall - 1, wide - 1]
        return [sum(sizes[:at]) for at in range(5)]

    @staticmethod
    def scratch(n_f, rows, columns):
        count = GridSum.layout(n_f)[4]
        return [
            pltpu.VMEM((n_f, rows, columns), BF),
            pltpu.VMEM((count, rows // 2, columns), BF),
            pltpu.SemaphoreType.DMA((2, count + GridEnd.count(n_f))),
        ]

    def slot(self, kind, i, j):
        base = self.bases[kind]
        return base + [(j - 1) * self.net.tall + i, (i - 1) * self.net.wide + j, i - 1, j - 1][kind]

    def rank(self, i, j):
        net = self.net
        return ((net.a + i) % net.tall) * net.wide + (net.b + j) % net.wide

    def owner(self, at):
        return self.rank(at // self.net.wide, at % self.net.wide)

    def copy(self, kind, i, j):
        half = kind % 2
        along = kind in (0, 3)
        slot = self.slot(kind, i, j)
        at = i * self.net.wide + j
        return put(
            self.stage.at[at, pl.ds(half * self.half, self.half)],
            self.came.at[slot],
            self.sems.at[0, slot],
            self.sems.at[1, slot],
            fsdp=self.rank(0, j) if along else self.rank(i, 0),
        )

    def first(self, at):
        i, j = at // self.net.wide, at % self.net.wide

        @pl.when(j > 0)
        def _():
            self.copy(0, i, j).start()

        @pl.when(i > 0)
        def _():
            self.copy(1, i, j).start()

    def gather(self, half, at, slots, write):
        @pl.loop(0, self.half // self.rows)
        def _(step):
            span = aligned(half * self.half + step * self.rows, self.rows, 16)
            value = self.stage[at, span, :].astype(F32)
            for slot in slots:
                value = value + self.came[slot, aligned(step * self.rows, self.rows, 16), :].astype(F32)
            write(span, value)

    def wait(self, *copies):
        for kind, i, j in copies:
            self.copy(kind, i, j).wait_recv()
        return [self.slot(*copy) for copy in copies]

    def second(self):
        def keep(at):
            def write(span, value):
                self.stage[at, span, :] = value.astype(BF)

            return write

        for i in self.cols:
            at = i * self.net.wide
            self.gather(0, at, self.wait(*[(0, i, j) for j in self.along]), keep(at))
            self.copy(2, i, 0).start()
        for j in self.along:
            self.gather(1, j, self.wait(*[(1, i, j) for i in self.cols]), keep(j))
            self.copy(3, 0, j).start()

    def sum_first(self):
        def keep(at):
            def write(span, value):
                self.stage[at, span, :] = value.astype(BF)

            return write

        for i in range(self.net.tall):
            at = i * self.net.wide
            self.gather(0, at, self.wait(*[(0, i, j) for j in self.along]), keep(at))
        for j in range(self.net.wide):
            self.gather(1, j, self.wait(*[(1, i, j) for i in self.cols]), keep(j))

    def hand_on(self, out):
        net = self.net
        shards = [(0, 0), (0, 1), *[(i * net.wide, 0) for i in self.cols], *[(j, 1) for j in self.along]]
        return [
            pltpu.make_async_copy(
                self.stage.at[at, pl.ds(half * self.half, self.half)], out.at[k], self.sems.at[0, self.bases[4] + k]
            )
            for k, (at, half) in enumerate(shards)
        ]

    def last(self, out):
        def write(span, value):
            out[span, :] = value

        self.gather(
            0, 0, self.wait(*[(0, 0, j) for j in self.along], *[(2, i, 0) for i in self.cols]), write
        )
        self.gather(
            1, 0, self.wait(*[(1, i, 0) for i in self.cols], *[(3, 0, j) for j in self.along]), write
        )

    def finish_first(self):
        for i in range(self.net.tall):
            for j in range(self.net.wide):
                if j:
                    self.copy(0, i, j).wait_send()
                if i:
                    self.copy(1, i, j).wait_send()

    def finish(self):
        self.finish_first()
        for i in self.cols:
            self.copy(2, i, 0).wait_send()
        for j in self.along:
            self.copy(3, 0, j).wait_send()


class GridEnd:
    def __init__(self, net, sums, came, sems):
        self.net, self.sums, self.came, self.sems = net, sums, came, sems

    @staticmethod
    def count(n_f):
        tall = 2 if n_f % 2 == 0 else 1
        return tall + n_f // tall

    @staticmethod
    def scratch(n_f, rows, columns):
        count = GridEnd.count(n_f)
        return [pltpu.VMEM((count, rows // 2, columns), BF), pltpu.SemaphoreType.DMA((2, count - 2))]

    def copies(self):
        net = self.net
        f = [((net.a + i) % net.tall) * net.wide + net.b for i in range(1, net.tall)]
        f += [net.a * net.wide + (net.b + j) % net.wide for j in range(1, net.wide)]
        return [
            put(self.sums.at[2 + k], self.came.at[k], self.sems.at[0, k], self.sems.at[1, k], fsdp=to)
            for k, to in enumerate(f)
        ]

    def start(self):
        for copy in self.copies():
            copy.start()

    def finish(self):
        for copy in self.copies():
            copy.wait()


class PacketSum:
    def __init__(self, net, out, seq_in, total, fsdp_in, sems):
        self.net, self.out, self.seq_in, self.total, self.fsdp_in, self.sems = net, out, seq_in, total, fsdp_in, sems

    @staticmethod
    def scratch(n_f, n_s):
        return [
            pltpu.VMEM((n_s, n_f, SMALL, 128), F32),
            pltpu.VMEM((n_s, n_f, SMALL, 128), F32),
            pltpu.VMEM((n_f, SMALL, 128), F32),
            pltpu.VMEM((n_f, SMALL, 128), F32),
            pltpu.SemaphoreType.DMA((2 * (n_f + n_s),)),
        ]

    def one(self, k):
        to = (self.net.s + k) % self.net.n_s
        return put(self.out.at[to], self.seq_in.at[k], self.sems.at[2 * k], self.sems.at[2 * k + 1], seq=to)

    def two(self, k):
        to = (self.net.f + k) % self.net.n_f
        at = 2 * (self.net.n_s + k)
        return put(self.total.at[to], self.fsdp_in.at[k], self.sems.at[at], self.sems.at[at + 1], fsdp=to)

    def start(self, terms, width):
        net = self.net
        per = 128 // width
        for tile in range(net.n_f * net.n_s // per):
            value = terms[:, tile * 128 : (tile + 1) * 128]
            for j in range(per):
                f, s = divmod(tile * per + j, net.n_s)
                self.out[s, f] = pltpu.roll(value, 128 - j * width, axis=1) if j else value
        for k in range(1, net.n_s):
            self.one(k).start()

    def middle(self):
        net = self.net
        total = self.out[net.s]
        for k in range(1, net.n_s):
            self.one(k).wait()
            total = total + self.seq_in[k]
        self.total[...] = total
        for k in range(1, net.n_f):
            self.two(k).start()

    def finish(self, result):
        net = self.net
        total = self.total[net.f]
        for k in range(1, net.n_f):
            self.two(k).wait()
            total = total + self.fsdp_in[k]
        result[...] = total


def norm_backward(rows, source, grad, gain, terms, at, write):
    terms[at : at + 2, :] = jnp.zeros((2, terms.shape[1]), F32)

    @pl.loop(0, rows // 32)
    def _(i):
        span = aligned(i * 32, 32)
        scaled, inverse = normalize(source[span, :].astype(F32))
        value = grad[span, :]
        upstream = value * gain
        inner = jnp.mean(upstream, -1, keepdims=True)
        cross = jnp.mean(upstream * scaled, -1, keepdims=True)
        terms[at : at + 1, :] = terms[at : at + 1, :] + jnp.sum(value * scaled, 0, keepdims=True)
        terms[at + 1 : at + 2, :] = terms[at + 1 : at + 2, :] + jnp.sum(value, 0, keepdims=True)
        write(i, span, inverse * (upstream - inner - scaled * cross))


def layer_kernel(
    tok,
    gain_one,
    shift_one,
    gain_two,
    shift_two,
    bias,
    wq_own,
    wo_own,
    wg_own,
    wu_own,
    wd_own,
    gout_own,
    cosine,
    sine,
    q_o,
    k_o,
    kt_o,
    v_o,
    att_o,
    lse_o,
    n1_o,
    gains_o,
    wq_o,
    wo_o,
    dm_o,
    datt_o,
    dmid_o,
    top_o,
    terms_o,
    gate_o,
    up_o,
    down_o,
    rows,
    gout,
    wq,
    wo,
    wg,
    wu,
    wd,
    q,
    k,
    kt,
    v,
    vt,
    ot,
    att,
    hidden,
    dgate,
    dup,
    mid,
    low,
    packet,
    packets,
    tiles,
    total,
    *rest,
):
    net = Net()
    chunk, width = tok.shape
    length = chunk * net.n_s
    depth = wq_own.shape[1]
    columns = wq_own.shape[2]
    heads = columns // HEAD
    pair = 2 * chunk
    buffers, rest = rest[:4], rest[4:]
    folds = []
    for _ in range(3):
        folds.append(Fold(net, tiles, total, *buffers, *rest[:4]))
        rest = rest[4:]
    att_fold, normed_fold, top_fold = folds
    line_sems = [rest[at : at + 3] for at in (0, 3, 6, 9)]
    rest = rest[12:]
    spread_sems, rest = rest[:5], rest[5:]
    gate_sum, up_sum, down_sum = [GridSum(net, *rest[at : at + 3]) for at in (0, 3, 6)]
    sums = (down_sum, gate_sum, up_sum)
    pk_sems, copy_sems, n1_sems, dm_sems, free_sem = rest[9:]
    copies = Copies(copy_sems)
    n1 = att_fold.mate_out

    packet[...] = jnp.zeros(packet.shape, F32)
    own = gain_one.shape[1]
    for at, part in enumerate((gain_one, shift_one, gain_two, shift_two)):
        packet[at : at + 1, 0:own] = part[...].astype(F32)
    packet[4:7, 0:own] = bias[...].astype(F32)
    def wq_part(f, half):
        if half is None:
            return wq.at[:, aligned(f * depth, depth), :]
        return wq.at[:, aligned(f * depth + half * (depth // 2), depth // 2), :]

    spread_q = Spread(net, wq_own, wq_part, spread_sems[0])
    spread_o, spread_g, spread_u, spread_d = [
        Spread(net, own, columns_of(full, depth), sems)
        for own, full, sems in zip((wo_own, wg_own, wu_own, wd_own), (wo, wg, wu, wd), spread_sems[1:])
    ]
    pk = Packets(net, packet, packets, pk_sems)
    line = Line(net, tok, rows_of(rows, chunk), *line_sems[0])
    gout_line = Line(net, gout_own, rows_of(gout, chunk), *line_sems[1])
    n2_line = Line(net, low, rows_of(rows, chunk), *line_sems[2])
    dm_line = Line(net, low, rows_of(rows, chunk), *line_sems[3])

    for ready in (line, spread_q, spread_o, spread_g, spread_u, spread_d, gout_line):
        ready.prepare()
    net.barrier()

    def pairs(which, hop):
        net.sides(hop, lambda other, side: which.pair(other))

    def blocks(hop, act):
        def once(other, side):
            @pl.when((hop > 0) | (side == 0))
            def _():
                act(other, side)

        net.sides(hop, once)

    pk.start()
    line.start()
    spread_q.start()
    pk.middle()
    pk.finish()
    pk.unpack(gains_o, width // (net.n_f * net.n_s))

    def project_block(other, side):
        span = aligned(other * pair, pair)
        gain, shift = gains_o[0:1, :], gains_o[1:2, :]

        for part in range(2):

            @pl.loop(0, chunk // 32)
            def _(i):
                at = aligned((2 * other + part) * chunk + i * 32, 32)
                scaled, _ = normalize(rows[at, :].astype(F32))
                n1[part, aligned(i * 32, 32), :] = (scaled * gain + shift).astype(BF)

        keeps = [
            pltpu.make_async_copy(
                n1.at[part], n1_o.at[aligned((2 * other + part) * chunk, chunk)], n1_sems.at[part]
            )
            for part in range(2)
        ]
        for copy in keeps:
            copy.start()
        left = n1[0:2].reshape(pair, width)
        cols = aligned(net.s * columns, columns)
        tables = cosine[span, :], sine[span, :]
        for kind in range(3):
            value = dot(left, wq[kind]) + gains_o[4 + kind : 5 + kind, cols]
            if kind == 0:
                q[span, :] = rotary(value, *tables).astype(BF)
            elif kind == 1:
                value = rotary(value, *tables)
                k[span, :] = value.astype(BF)
                kt[...] = value.T.astype(BF)
            else:
                v[...] = value.astype(BF)
                vt[:, span] = value.T.astype(BF)
        for copy in (
            pltpu.make_async_copy(kt, kt_o.at[:, span], n1_sems.at[2]),
            pltpu.make_async_copy(v, v_o.at[span], n1_sems.at[3]),
        ):
            copy.start()
            keeps.append(copy)
        for copy in keeps:
            copy.wait()

    line.here()
    for hop in range(1, net.n_l - 1):
        line.step(hop)
        if hop == 1:
            spread_q.relay()
        pairs(line, hop)
    spread_o.start()
    spread_q.finish()
    spread_g.start()
    pl.loop(0, net.n_l - 1)(lambda hop: blocks(hop, project_block))
    spread_o.relay()
    spread_u.start()
    line.step(net.n_l - 1)
    gout_line.start()
    pairs(line, net.n_l - 1)
    blocks(net.n_l - 1, project_block)
    q_copy = copies.start(q, q_o)
    for pair_of in ((wq, wq_o), (k, k_o)):
        copies.start(*pair_of)
    spread_o.finish()
    line.finish()

    def attend(i):
        lo, hi = i * pair, (i + 1) * pair

        @pl.loop(0, heads, unroll=2)
        def _(head):
            lane = lax.broadcasted_iota(jnp.int32, (1, columns), 1)
            here = jnp.where(lane // HEAD == head, HEAD**-0.5, 0.0).astype(BF)
            visible = lax.broadcasted_iota(jnp.int32, (pair, pair), 0) <= lax.broadcasted_iota(
                jnp.int32, (pair, pair), 1
            )
            head_rows = aligned(head * HEAD, HEAD)
            query = q[lo:hi, :] * here
            near = jnp.where(visible, dot_nt(k[lo:hi, :], query), NEG_LARGE)
            highest = jnp.max(near, 0, keepdims=True)
            if i:
                far = dot_nt(k[0:lo, :], query)
                highest = jnp.maximum(highest, jnp.max(far, 0, keepdims=True))
            near = jnp.exp(near - highest)
            sum_of = jnp.sum(near, 0, keepdims=True)
            out = dot(vt[head_rows, lo:hi], near.astype(BF))
            if i:
                far = jnp.exp(far - highest)
                sum_of = sum_of + jnp.sum(far, 0, keepdims=True)
                out = out + dot(vt[head_rows, 0:lo], far.astype(BF))
            ot[head_rows, :] = out / sum_of
            lse_o[pl.ds(head, 1), lo:hi] = highest + jnp.log(sum_of)

        att[lo:hi, :] = ot[...].T.astype(BF)

    def produce_attended(place, write):
        for i in range(net.n_l):
            pl.when(place == i)(functools.partial(attend, i))
        left = att[aligned(place * pair, pair), :]

        @pl.loop(0, width // TILE)
        def _(j):
            cols = aligned(j * TILE, TILE)
            write(cols, dot(left, wo[:, cols]))

    def relays():
        gout_line.step(1)
        spread_d.start()

    att_fold.begin(produce_attended, relays)
    copies.start(att, att_o)
    copies.start(wo, wo_o)
    if net.n_l > 2:
        gout_line.step(2)
    att_fold.open_total()
    spread_g.relay()
    for at in range(1, net.n_l):
        if 2 < at + 1 < net.n_l:
            gout_line.step(at + 1)
        att_fold.wave(at)
        if at == 1:
            spread_u.relay()
        if at == min(2, net.n_l - 1):
            spread_d.relay()
    gain_two, shift_two = gains_o[2:3, :], gains_o[3:4, :]

    @pl.loop(0, chunk // 32)
    def _(i):
        span = aligned(i * 32, 32)
        value = rows[aligned(net.s * chunk + i * 32, 32), :].astype(F32) + total[span, :]
        mid[span, :] = value
        scaled, _ = normalize(value)
        low[span, :] = (scaled * gain_two + shift_two).astype(BF)

    n2_line.prepare()
    n2_line.start()
    att_fold.finish()
    gout_line.here()
    pl.loop(1, net.n_l)(lambda hop: pairs(gout_line, hop))

    def forward_block(other):
        span = aligned(other * pair, pair)
        right = rows[span, :]
        half = hidden.shape[0] // 2

        @pl.loop(0, 2)
        def _(part):
            units = aligned(part * half, half, 16)
            gate = dot_nt(wg[units, :], right)
            up = dot_nt(wu[units, :], right)
            back = dot_nt(wd[units, :], gout[span, :])
            sigma = jax.nn.sigmoid(gate)
            active = gate * sigma
            hidden[units, span] = (active * up).astype(BF)
            dgate[units, span] = (back * up * (sigma * (1.0 + gate * (1.0 - sigma)))).astype(BF)
            dup[units, span] = (back * active).astype(BF)

    def produce_normed(place, write):
        span = aligned(place * pair, pair)
        left, right = dgate[:, span].T, dup[:, span].T

        @pl.loop(0, width // TILE)
        def _(j):
            cols = aligned(j * TILE, TILE)
            write(cols, dot(left, wg[:, cols]) + dot(right, wu[:, cols]))

    def begin_normed(other, side, hop):
        @pl.when(hop > 1)
        def _():
            normed_fold.mate_sent(side)

        normed_fold.begin_one(other, side + (2 - side) * (1 // (hop + 1)), produce_normed)

    def forward_blocks(hop):
        def act(other, side):
            forward_block(other)

            @pl.when(jnp.logical_not(normed_fold.fed(side)))
            def _():
                begin_normed(other, side, hop)
                normed_fold.leave(other, side, hop)

        net.sides(hop, act)

    def begin_fed(hop):
        def act(other, side):
            pl.when(normed_fold.fed(side))(lambda: begin_normed(other, side, hop))

        net.sides(hop, act)

    n2_line.here()
    for spread in (spread_g, spread_u, spread_d):
        spread.finish()
    forward_block(net.z)

    @pl.loop(1, net.n_l)
    def _(hop):
        n2_line.step(hop)
        pairs(n2_line, hop)
        pl.when(hop == 1)(lambda: normed_fold.begin_one(net.z, 2, produce_normed))
        forward_blocks(hop)
        pl.when(hop > 1)(lambda: begin_fed(hop - 1))

    begin_fed(net.n_l - 1)

    def weight_terms(task):
        at, kind = net.n_f - 1 - task // 3, task % 3
        cols = aligned(gate_sum.owner(at) * depth, depth)
        for way, (grid_sum, left, right) in enumerate(
            ((down_sum, hidden, gout), (gate_sum, dgate, rows), (up_sum, dup, rows))
        ):

            @pl.when(kind == way)
            def _():
                half = left.shape[0] // 2

                @pl.loop(0, 2)
                def _(part):
                    units = aligned(part * half, half, 16)
                    grid_sum.stage[at, units, :] = dot(left[units, :], right[:, cols]).astype(BF)

                grid_sum.first(at)

    tasks = 3 * net.n_f
    waves = max(net.n_l - 2, 1)
    each = -(-tasks // (2 * normed_fold.pieces * waves))
    for wave in range(net.n_l - waves, net.n_l):

        def between(turn, piece):
            slot = ((wave - net.n_l + waves) * 2 + turn) * normed_fold.pieces + piece

            @pl.loop(0, each)
            def _(i):
                pl.when(slot * each + i < tasks)(lambda: weight_terms(slot * each + i))

        normed_fold.passes_between(wave, True, between)
    normed_fold.finals()
    n2_line.finish()

    def beside(act):
        act(net.mate)
        for side in range(2):
            pl.when(n2_line.goes_on(side))(lambda: act(net.s + 2 - 4 * side))

    beside(lambda to: pl.semaphore_signal(free_sem, 1, device_id={"seq": to}, device_id_type=MESH))

    def write_middle(i, span, value):
        value = value + gout[aligned(net.s * chunk + i * 32, 32), :].astype(F32)
        dmid_o[span, :] = value
        low[span, :] = value.astype(BF)

    terms_o[...] = jnp.zeros(terms_o.shape, F32)
    norm_backward(chunk, mid, total, gain_two, terms_o, 2, write_middle)
    ends = (net.z + net.n_l - 1) // net.n_l + (2 * net.n_l - 2 - net.z) // net.n_l
    pl.semaphore_wait(free_sem, 1 + ends)
    dm_line.prepare()
    dm_line.start()
    normed_fold.finish()

    def produce_top(place, write):
        left = hidden[:, aligned(place * pair, pair)].T

        @pl.loop(0, width // TILE)
        def _(j):
            cols = aligned(j * TILE, TILE)
            write(cols, dot(left, wd[:, cols]))

    copies.wait(q_copy)
    datt = q

    def dm_copy(other):
        span = aligned(other * pair, pair)
        return pltpu.make_async_copy(rows.at[span], dm_o.at[span], dm_sems.at[other])

    def back_block(other, side):
        span = aligned(other * pair, pair)
        dm_copy(other).start()
        datt[span, :] = dot_nt(rows[span, :], wo[...]).astype(BF)

    dm_line.here()
    dm_line.step(1)
    top_fold.begin(produce_top)
    back_block(net.z, 0)
    top_fold.open_total()
    for at in range(1, net.n_l):
        if at + 1 < net.n_l:
            dm_line.step(at + 1)
        top_fold.wave(at)
        pairs(dm_line, at)
        net.sides(at, back_block)
    copies.start(datt, datt_o)

    @pl.loop(0, chunk // 32)
    def _(i):
        span = aligned(i * 32, 32)
        top_fold.out[net.z, span, :] = (mid[span, :] + total[span, :]).astype(BF)

    copies.start(top_fold.out.at[net.z], top_o)
    top_fold.finish()
    gout_line.finish()
    dm_line.finish()
    hands = []
    for grid_sum, out in zip(sums, (down_o, gate_o, up_o)):
        grid_sum.sum_first()
        hands.extend(grid_sum.hand_on(out))
        for copy in grid_sum.hand_on(out):
            copy.start()
    for grid_sum in sums:
        grid_sum.finish_first()
    for copy in hands:
        copy.wait()
    copies.wait()
    pl.loop(0, net.n_l)(lambda other: dm_copy(other).wait())


def layer_part(tokens, norms, wq, wo, wg, wu, wd, gout, tables):
    chunk, width = tokens.shape
    n_f, n_s = lax.axis_size("fsdp"), lax.axis_size("seq")
    length = chunk * n_s
    depth, columns = wq.shape[1:]
    units = wg.shape[0]
    shape = jax.ShapeDtypeStruct
    wide, head, turned, weight = (length, width), (length, columns), (units, length), (units, width)
    return pl.pallas_call(
        layer_kernel,
        name="layer",
        out_shape=[
            shape(head, BF),
            shape(head, BF),
            shape((columns, length), BF),
            shape(head, BF),
            shape(head, BF),
            shape((8, length), F32),
            shape(wide, BF),
            shape((SMALL, width), F32),
            shape((3, width, columns), BF),
            shape((columns, width), BF),
            shape(wide, BF),
            shape(head, BF),
            shape((chunk, width), F32),
            shape((chunk, width), BF),
            shape((SMALL, width), F32),
            *[shape((GridEnd.count(n_f), units // 2, depth), BF)] * 3,
        ],
        in_specs=[ANY, *[VMEM] * 5, *[ANY] * 6, VMEM, VMEM],
        out_specs=[*[ANY] * 5, VMEM, ANY, VMEM, *[ANY] * 4, VMEM, ANY, VMEM, *[ANY] * 3],
        scratch_shapes=[
            pltpu.VMEM(wide, BF),
            pltpu.VMEM(wide, BF),
            pltpu.VMEM((3, width, columns), BF),
            pltpu.VMEM((columns, width), BF),
            *[pltpu.VMEM(weight, BF)] * 3,
            pltpu.VMEM(head, BF),
            pltpu.VMEM(head, BF),
            pltpu.VMEM((columns, 2 * chunk), BF),
            pltpu.VMEM((2 * chunk, columns), BF),
            pltpu.VMEM((columns, length), BF),
            pltpu.VMEM((columns, 2 * chunk), F32),
            pltpu.VMEM(head, BF),
            *[pltpu.VMEM(turned, BF)] * 3,
            pltpu.VMEM((chunk, width), F32),
            pltpu.VMEM((chunk, width), BF),
            pltpu.VMEM((SMALL, 128), F32),
            pltpu.VMEM((n_s, n_f, SMALL, 128), F32),
            *Fold.shared(chunk, width),
            *Fold.buffers(n_s, chunk, width),
            *Fold.sems(n_s) * 3,
            *Line.sems(n_s) * 4,
            *[pltpu.SemaphoreType.DMA((Spread.count(n_f),))] * 5,
            *GridSum.scratch(n_f, units, depth) * 3,
            pltpu.SemaphoreType.DMA((Packets.count(n_f, n_s),)),
            pltpu.SemaphoreType.DMA((8,)),
            pltpu.SemaphoreType.DMA((4,)),
            pltpu.SemaphoreType.DMA((n_s // 2,)),
            pltpu.SemaphoreType.REGULAR,
        ],
        compiler_params=pltpu.CompilerParams(
            collective_id=1, has_side_effects=True, vmem_limit_bytes=VMEM_BYTES
        ),
        cost_estimate=pl.CostEstimate(
            flops=2 * length * width * (4 * columns + 9 * units),
            bytes_accessed=8 * length * width,
            transcendentals=length * (length * columns // HEAD + units),
        ),
    )(tokens, *norms, wq, wo, wg, wu, wd, gout, *tables)


def back_kernel(
    datt_in,
    q_in,
    k_in,
    kt_in,
    v_in,
    att_in,
    wq_in,
    n1_in,
    dm_in,
    down_in,
    gate_in,
    up_in,
    lse,
    tok,
    dmid,
    gains,
    terms_in,
    cosine,
    sine,
    gin_o,
    small_o,
    out_o,
    qkv_o,
    down_o,
    gate_o,
    up_o,
    datt,
    q,
    k,
    kt,
    v,
    att,
    wq,
    n1,
    dm,
    query,
    upstream,
    inners,
    dk,
    dv,
    dqt,
    dproj,
    terms,
    tiles,
    total,
    *rest,
):
    net = Net()
    chunk, width = tok.shape
    length, columns = q_in.shape
    heads = columns // HEAD
    pair = 2 * chunk
    depth = width // net.n_f
    block = 256
    buffers, rest = rest[:4], rest[4:]
    fold_sems, rest = rest[:4], rest[4:]
    packet_scratch, rest = rest[:5], rest[5:]
    out_sum, qkv_sum = GridSum(net, *rest[:3]), GridSum(net, *rest[3:6])
    ends = [
        GridEnd(net, rest[at], came, rest[at + 1]) for at, came in ((6, down_o), (8, gate_o), (10, up_o))
    ]
    copy_sems, column_sems = rest[12:]

    copies = Copies(copy_sems)
    loads = [
        copies.start(src, dst)
        for src, dst in (
            (datt_in, datt),
            (q_in, q),
            (k_in, k),
            (kt_in, kt),
            (v_in, v),
            (att_in, att),
            (wq_in, wq),
            (down_in, ends[0].sums),
            (gate_in, ends[1].sums),
            (up_in, ends[2].sums),
        )
    ]
    def load(at, way):
        src, dst = ((n1_in, n1), (dm_in, dm))[way]
        cols = aligned(qkv_sum.owner(at) * depth, depth)
        return pltpu.make_async_copy(src.at[:, cols], dst.at[at % 2], column_sems.at[way, at % 2])

    for at in range(net.n_f - 1, max(net.n_f - 3, -1), -1):
        for way in range(2):
            load(at, way).start()

    @pl.loop(0, length // block)
    def _(i):
        span = aligned(i * block, block)
        dk[span, :] = jnp.zeros((block, columns), F32)
        dv[span, :] = jnp.zeros((block, columns), F32)

    net.barrier()
    copies.wait(*loads[:6])

    def start_ends():
        for load_of in loads[7:]:
            load_of.wait()
        for end in ends:
            end.start()


    of_head = (
        lax.broadcasted_iota(jnp.int32, (8, columns), 1) // HEAD
        == lax.broadcasted_iota(jnp.int32, (8, columns), 0)
    ).astype(F32)

    @pl.loop(0, length // block)
    def _(i):
        span = aligned(i * block, block)
        product = datt[span, :].astype(F32) * att[span, :].astype(F32)
        inners[:, span] = lax.dot_general(
            of_head,
            product,
            (((1,), (1,)), ((), ())),
            precision=lax.Precision.HIGHEST,
            preferred_element_type=F32,
        )

    @pl.loop(0, heads, unroll=2)
    def _(head):
        lane = lax.broadcasted_iota(jnp.int32, (1, columns), 1)
        here = jnp.where(lane // HEAD == head, 1.0, 0.0).astype(BF)
        scale = HEAD**-0.5
        visible = lax.broadcasted_iota(jnp.int32, (block, block), 0) <= lax.broadcasted_iota(
            jnp.int32, (block, block), 1
        )
        head_rows = aligned(head * HEAD, HEAD)

        @pl.loop(0, length // block)
        def _(i):
            span = aligned(i * block, block)
            query[span, :] = q[span, :] * (here * scale)
            upstream[span, :] = datt[span, :] * here

        pl.when(head == min(1, heads - 1))(start_ends)

        for j in range(length // block):
            at, end = j * block, (j + 1) * block
            keys, values, turned = k[at:end, :], v[at:end, :], kt[head_rows, at:end]

            def part(lo, hi, near):
                probs = jnp.exp(dot_nt(keys, query[lo:hi, :]) - lse[pl.ds(head, 1), lo:hi])
                if near:
                    probs = jnp.where(visible, probs, 0.0)
                grads = dot_nt(values, upstream[lo:hi, :])
                scores = (probs * (grads - inners[pl.ds(head, 1), lo:hi])).astype(BF)
                out = dot(turned, scores)
                dqt[head_rows, lo:hi] = dqt[head_rows, lo:hi] + out if j else out
                return dot(probs.astype(BF), upstream[lo:hi, :]), dot(scores, query[lo:hi, :])

            value_grads, key_grads = part(at, end, True)
            if end < length:
                more_values, more_keys = part(end, length, False)
                value_grads, key_grads = value_grads + more_values, key_grads + more_keys
            dv[at:end, :] = dv[at:end, :] + value_grads
            dk[at:end, :] = dk[at:end, :] + key_grads

    terms[...] = terms_in[...]
    bias_cols = aligned(net.s * columns, columns)

    @pl.loop(0, length // block)
    def _(i):
        span = aligned(i * block, block)
        tables = cosine[span, :], -sine[span, :]
        parts = [
            rotary((dqt[:, span].T * HEAD**-0.5).astype(BF).astype(F32), *tables).astype(BF),
            rotary(dk[span, :].astype(BF).astype(F32), *tables).astype(BF),
            dv[span, :].astype(BF),
        ]
        for kind in range(3):
            dproj[kind, span, :] = parts[kind]
            row = slice(4 + kind, 5 + kind)
            terms[row, bias_cols] = terms[row, bias_cols] + jnp.sum(parts[kind].astype(F32), 0, keepdims=True)

    def weight_terms(task):
        at = net.n_f - 1 - task // 2

        def loaded(way):
            load(at, way).wait()

        def next_load(way):
            pl.when(at >= 2)(lambda: load(at - 2, way).start())

        @pl.when(task % 2 == 0)
        def _():
            loaded(0)
            left = n1[at % 2].T
            for kind in range(3):
                qkv_sum.stage[at, kind * depth : (kind + 1) * depth, :] = dot(left, dproj[kind]).astype(BF)
            next_load(0)
            qkv_sum.first(at)

        @pl.when(task % 2 == 1)
        def _():
            loaded(1)
            out_sum.stage[at] = dot_tn(att[...], dm[at % 2]).astype(BF)
            next_load(1)
            out_sum.first(at)

    def produce(place, write):
        span = aligned(place * pair, pair)

        @pl.loop(0, width // TILE)
        def _(j):
            cols = aligned(j * TILE, TILE)
            value = dot_nt(dproj[0, span, :], wq[0, cols, :])
            for kind in range(1, 3):
                value = value + dot_nt(dproj[kind, span, :], wq[kind, cols, :])
            write(cols, value)

    fold = Fold(net, tiles, total, *buffers, *fold_sems)
    copies.wait(loads[6])
    fold.begin(produce)
    fold.open_total()
    tasks = 2 * net.n_f
    waves = max(net.n_l - 2, 1)
    each = -(-tasks // (2 * fold.pieces * waves))

    def between(slot):
        @pl.loop(0, each)
        def _(i):
            pl.when(slot * each + i < tasks)(lambda: weight_terms(slot * each + i))

    for at in range(1, waves + 1):
        fold.wave(at, between=between)
    for at in range(waves + 1, net.n_l):
        fold.wave(at)

    def write_input(i, span, value):
        gin_o[span, :] = value + dmid[span, :]

    norm_backward(chunk, tok, total, gains[0:1, :], terms, 0, write_input)
    packet_sum = PacketSum(net, *packet_scratch)
    packet_sum.start(terms, width // (net.n_f * net.n_s))
    for grid_sum in (qkv_sum, out_sum):
        grid_sum.second()
    packet_sum.middle()
    packet_sum.finish(small_o)
    for end in ends:
        end.finish()
    fold.finish()
    for grid_sum, out in ((qkv_sum, qkv_o), (out_sum, out_o)):
        grid_sum.last(out)
        grid_sum.finish()


def back_part(datt, q, k, kt, v, att, wq, n1, dm, down, gate, up, lse, tokens, dmid, gains, terms, tables):
    chunk, width = tokens.shape
    n_f, n_s = lax.axis_size("fsdp"), lax.axis_size("seq")
    length, columns = q.shape
    depth = width // n_f
    units = 2 * gate.shape[1]
    shape = jax.ShapeDtypeStruct
    return pl.pallas_call(
        back_kernel,
        name="back",
        out_shape=[
            shape((chunk, width), F32),
            shape((SMALL, 128), F32),
            shape((columns, depth), F32),
            shape((3 * depth, columns), F32),
            *[shape((GridEnd.count(n_f) - 2, units // 2, depth), BF)] * 3,
        ],
        in_specs=[ANY] * 12 + [VMEM] * 7,
        out_specs=[VMEM] * 4 + [ANY] * 3,
        scratch_shapes=[
            pltpu.VMEM((length, columns), BF),
            pltpu.VMEM((length, columns), BF),
            pltpu.VMEM((length, columns), BF),
            pltpu.VMEM((columns, length), BF),
            pltpu.VMEM((length, columns), BF),
            pltpu.VMEM((length, columns), BF),
            pltpu.VMEM((3, width, columns), BF),
            pltpu.VMEM((2, length, depth), BF),
            pltpu.VMEM((2, length, depth), BF),
            pltpu.VMEM((length, columns), BF),
            pltpu.VMEM((length, columns), BF),
            pltpu.VMEM((8, length), F32),
            pltpu.VMEM((length, columns), F32),
            pltpu.VMEM((length, columns), F32),
            pltpu.VMEM((columns, length), F32),
            pltpu.VMEM((3, length, columns), BF),
            pltpu.VMEM((SMALL, width), F32),
            *Fold.shared(chunk, width),
            *Fold.buffers(n_s, chunk, width),
            *Fold.sems(n_s, 8),
            *PacketSum.scratch(n_f, n_s),
            *GridSum.scratch(n_f, columns, depth),
            *GridSum.scratch(n_f, 3 * depth, columns),
            *GridEnd.scratch(n_f, units, depth) * 3,
            pltpu.SemaphoreType.DMA((10,)),
            pltpu.SemaphoreType.DMA((2, 2)),
        ],
        compiler_params=pltpu.CompilerParams(
            collective_id=3, has_side_effects=True, vmem_limit_bytes=VMEM_BYTES
        ),
        cost_estimate=pl.CostEstimate(
            flops=2 * length * columns * (8 * width + 5 * length),
            bytes_accessed=4 * length * width,
            transcendentals=length * length * columns // HEAD,
        ),
    )(datt, q, k, kt, v, att, wq, n1, dm, down, gate, up, lse, tokens, dmid, gains, terms, *tables)


def outputs_kernel(tall, small, *refs):
    plain, sums, came, refs = refs[:4], refs[4:7], refs[7:10], refs[10:]
    results, totals, parts = refs[:4], refs[4:7], refs[7:]
    own = parts[0].shape[1]
    for src, dst in zip(plain, results):
        dst[...] = src[...]
    for so_far, last, dst in zip(sums, came, totals):
        half = so_far.shape[1]
        count = last.shape[0]
        for at, slots in enumerate((range(tall - 1), range(tall - 1, count))):
            value = so_far[at].astype(F32)
            for slot in slots:
                value = value + last[slot].astype(F32)
            dst[at * half : (at + 1) * half, :] = value
    for at in range(4):
        parts[at][...] = small[at : at + 1, 0:own]
    parts[4][...] = small[4:7, 0:own]


def outputs_part(small, own, plain, sums, came):
    shape = jax.ShapeDtypeStruct
    tall = 2 if lax.axis_size("fsdp") % 2 == 0 else 1
    return pl.pallas_call(
        functools.partial(outputs_kernel, tall),
        name="outputs",
        out_shape=[shape(v.shape, v.dtype) for v in plain]
        + [shape((2 * v.shape[1], v.shape[2]), F32) for v in sums]
        + [shape((1, own), F32)] * 4
        + [shape((3, own), F32)],
        in_specs=[VMEM] * 11,
        out_specs=[VMEM] * 12,
        compiler_params=pltpu.CompilerParams(vmem_limit_bytes=VMEM_BYTES),
    )(small, *plain, *sums, *came)


def per_device(
    tokens,
    gain_one,
    shift_one,
    w_qkv,
    b_qkv,
    w_out,
    gain_two,
    shift_two,
    w_gate,
    w_up,
    w_down,
    grad_output,
):
    length = tokens.shape[1] * lax.axis_size("seq")
    width = gain_one.shape[0]
    norms = [v[None] for v in (gain_one, shift_one, gain_two, shift_two)] + [b_qkv]
    tables = rotary_tables(length)
    q, k, kt, v, att, lse, n1, gains, wq, _, dm, datt, dmid, top, terms, gate, up, down = layer_part(
        tokens[0], norms, w_qkv.transpose(1, 0, 2), w_out, w_gate.T, w_up.T, w_down, grad_output[0], tables
    )
    grad_input, small, out, qkv, *came = back_part(
        datt, q, k, kt, v, att, wq, n1, dm, down, gate, up, lse, tokens[0], dmid, gains, terms, tables
    )

    top, grad_input, qkv, out, down, gate, up, one, shift, two, shift_to, bias = outputs_part(
        small, width, (top, grad_input, qkv, out), (down, gate, up), came
    )
    return (
        top[None],
        grad_input[None],
        one[0],
        shift[0],
        qkv.reshape(3, -1, qkv.shape[1]).transpose(1, 0, 2),
        bias,
        out,
        two[0],
        shift_to[0],
        gate.T,
        up.T,
        down,
    )


def solution(mesh):
    whole = P(("fsdp", "seq"))
    rows = P("fsdp", "seq", None)
    inner = P("seq", "fsdp")
    outer = P("fsdp", "seq")
    heads = P("fsdp", None, "seq")
    bias = P(None, ("fsdp", "seq"))
    return jax.shard_map(
        per_device,
        mesh=mesh,
        in_specs=(rows, whole, whole, heads, bias, inner, whole, whole, outer, outer, inner, rows),
        out_specs=(rows, rows, whole, whole, heads, bias, inner, whole, whole, outer, outer, inner),
        check_vma=False,
    )
```
